32 devices in a mesh: dp: 8 (over z, y), tensor: 4 (over x, core).
Axes of the slice: x: 2, y: 2, z: 4, core: 2. Of those that a mesh axis runs over, the one named last changes fastest.
Arguments:
- tokens: bfloat16 [8192, 2048], P('dp'), may hold values from -8 to 8
- positions: int32 [8192], P('dp'), may hold values from 0 to 3069, as said below
- out_grad: bfloat16 [8192, 2048], P('dp'), may hold values from -8 to 8
- qkv_weight: float32 [2048, 8, 4, 128], P('dp', 'tensor'), may hold values from -0.125 to 0.125
- qkv_first: float32 [2048, 8, 4, 128], P('dp', 'tensor'), may hold values from -40 to 40
- qkv_second: float32 [2048, 8, 4, 128], P('dp', 'tensor'), may hold values from 212.992 to 860.16
- out_weight: float32 [2048, 2048], P('dp', 'tensor'), may hold values from -1 to 1
- out_first: float32 [2048, 2048], P('dp', 'tensor'), may hold values from -10 to 10
- out_second: float32 [2048, 2048], P('dp', 'tensor'), may hold values from 9.8304 to 39.3216
- gate_up: float32 [2, 2048, 6144], P(None, 'dp', 'tensor'), may hold values from -0.125 to 0.125
- gate_up_first: float32 [2, 2048, 6144], P(None, 'dp', 'tensor'), may hold values from -32 to 32
- gate_up_second: float32 [2, 2048, 6144], P(None, 'dp', 'tensor'), may hold values from 106.496 to 434.176
- down_weight: float32 [2048, 6144], P('dp', 'tensor'), may hold values from -0.078125 to 0.078125
- down_first: float32 [2048, 6144], P('dp', 'tensor'), may hold values from -32 to 32
- down_second: float32 [2048, 6144], P('dp', 'tensor'), may hold values from 155.648 to 622.592
- gains: float32 [4352], P('dp'), may hold values from 0.5 to 1.5
- gains_first: float32 [4352], P('dp'), may hold values from -64 to 64
- gains_second: float32 [4352], P('dp'), may hold values from 434.176 to 1720.32
Outputs:
- block_out: bfloat16 [8192, 2048], P('dp')
- grad_input: float32 [8192, 2048], P('dp')
- qkv_first_new: float32 [2048, 8, 4, 128], P('dp', 'tensor')
- qkv_second_new: float32 [2048, 8, 4, 128], P('dp', 'tensor')
- qkv_new: float32 [2048, 8, 4, 128], P('dp', 'tensor')
- out_first_new: float32 [2048, 2048], P('dp', 'tensor')
- out_second_new: float32 [2048, 2048], P('dp', 'tensor')
- out_new: float32 [2048, 2048], P('dp', 'tensor')
- gate_up_first_new: float32 [2, 2048, 6144], P(None, 'dp', 'tensor')
- gate_up_second_new: float32 [2, 2048, 6144], P(None, 'dp', 'tensor')
- gate_up_new: float32 [2, 2048, 6144], P(None, 'dp', 'tensor')
- down_first_new: float32 [2048, 6144], P('dp', 'tensor')
- down_second_new: float32 [2048, 6144], P('dp', 'tensor')
- down_new: float32 [2048, 6144], P('dp', 'tensor')
- gains_first_new: float32 [4352], P('dp')
- gains_second_new: float32 [4352], P('dp')
- gains_new: float32 [4352], P('dp')
The draws below stay inside these ranges and needn't reach their ends.
Inputs may be any that keep to these rules, and one draw needn't show every extreme that they name: Within each sequence of 1024 tokens the positions start at 0 and rise by 1 to 3 from one token to the next; in one sequence, drawn from the seed, they rise by 3 at every token.
All inputs are finite; a program needn't handle non-finite values.
Results may differ from the reference program's by a relative error of at most 0.03.
Values may be sent and summed in bfloat16 or wider, within the bound.
A program may use at most 320 MiB of HBM per device.

```python
import math
import jax
import jax.numpy as jnp
from jax import lax

D = 2048
HQ = 16
HK = 8
HD = 128
FF = 6144
SEQ = 1024
STEP = 10
TOKENS = 8192
GAINS = 4352


def draw_positions(key, part):
    key = jax.random.fold_in(key, 11)
    gap_key, pick_key = jax.random.split(key)
    seq_total = TOKENS // SEQ
    gaps = jax.random.randint(gap_key, (seq_total, SEQ), 1, 4)
    chosen = jax.random.randint(pick_key, (), 0, seq_total)
    row_index = jnp.arange(seq_total, dtype=jnp.int32)[:, None]
    gaps = jnp.where(row_index == chosen, 3, gaps)
    column = jnp.arange(SEQ, dtype=jnp.int32)[None, :]
    gaps = jnp.where(column == 0, 0, gaps)
    return jnp.cumsum(gaps, axis=1).reshape(TOKENS).astype(jnp.int32)


def raised(entries, rng, source, target, blocks, factor):
    def block_of(dim):
        return (jnp.arange(entries.shape[dim]) // (entries.shape[dim] // blocks)).reshape((-1,) + (1,) * (entries.ndim - 1 - dim))

    first = jax.random.permutation(rng, blocks)[block_of(target)]
    second = (block_of(target) + blocks // 2) % blocks
    return jnp.where((block_of(source) == first) | (block_of(source) == second), factor * entries, entries)


def steps_of(rng, shape, cuts, smallest, high):
    level, own = 1.0, jax.random.fold_in(rng, 6)
    for axis_at, shards_of in cuts:
        draws = jnp.exp(jax.random.uniform(jax.random.fold_in(own, axis_at), (shards_of,), jnp.float32, smallest / len(cuts), high / len(cuts)))
        level = level * jnp.repeat(draws, shape[axis_at] // shards_of).reshape([-1 if axis == axis_at else 1 for axis in range(len(shape))])
    return level


def scatter_about(stream_key, extent, spread, bound, shards=(), kind=jnp.bfloat16):
    values = jax.random.normal(stream_key, extent, jnp.float32) * spread
    if len(shards) > 0:
        values = steps_of(stream_key, extent, shards, -0.22, 0.18) * values
    return jnp.clip(values, min=-bound, max=bound).astype(kind)


def noise_with(key, extent, spread, bound, cuts, heavy, kind=jnp.bfloat16):
    result = spread * jax.random.normal(key, extent, jnp.float32)
    if cuts:
        result = result * steps_of(key, extent, cuts, -0.22, 0.18)
    return jnp.clip(raised(result, jax.random.fold_in(key, 3), *heavy), -bound, bound).astype(kind)


def setup_inputs(seed: int = 0) -> dict:
    splits = jax.random.split(jax.random.key(seed), 19)
    return {
        "tokens": noise_with(splits[0], (TOKENS, D), 1.0, 8.0, ((0, 8),), (0, 1, 8, 2.0)),
        "positions": draw_positions(jax.random.fold_in(splits[18], 71), 0),
        "out_grad": noise_with(splits[2], (TOKENS, D), 1.0, 8.0, ((0, 8),), (0, 1, 8, 2.0)),
        "qkv_weight": scatter_about(splits[3], (D, HK, 4, HD), D ** -0.5, 0.125, ((0, 8), (1, 4)), jnp.float32),
        "qkv_first": scatter_about(splits[4], (D, HK, 4, HD), (0.08 * TOKENS ** 0.5), 40.0, ((0, 8), (1, 4)), jnp.float32),
        "qkv_second": jnp.clip(jnp.exp(math.log(860.16) - 1.3958638 * jax.random.uniform(splits[5], (D, HK, 4, HD), jnp.float32) ** steps_of(splits[5], (D, HK, 4, HD), ((0, 8), (1, 4)), -0.2, 0.2)), 212.992, 860.16),
        "out_weight": scatter_about(splits[6], (D, HQ * HD), (HQ * HD // 64) ** -0.5, 1.0, ((0, 8), (1, 4)), jnp.float32),
        "out_first": scatter_about(splits[7], (D, HQ * HD), (0.017 * TOKENS ** 0.5), 10.0, ((0, 8), (1, 4)), jnp.float32),
        "out_second": jnp.clip(jnp.exp(math.log(39.3216) - 1.3862944 * jax.random.uniform(splits[8], (D, HQ * HD), jnp.float32) ** steps_of(splits[8], (D, HQ * HD), ((0, 8), (1, 4)), -0.2, 0.2)), 9.8304, 39.3216),
        "gate_up": scatter_about(splits[9], (2, D, FF), D ** -0.5, 0.125, ((1, 8), (2, 4)), jnp.float32),
        "gate_up_first": scatter_about(splits[10], (2, D, FF), (0.055 * TOKENS ** 0.5), 32.0, ((1, 8), (2, 4)), jnp.float32),
        "gate_up_second": jnp.clip(jnp.exp(math.log(434.176) - 1.40534252 * jax.random.uniform(splits[11], (2, D, FF), jnp.float32) ** steps_of(splits[11], (2, D, FF), ((1, 8), (2, 4)), -0.2, 0.2)), 106.496, 434.176),
        "down_weight": scatter_about(splits[12], (D, FF), FF ** -0.5, 0.078125, ((0, 8), (1, 4)), jnp.float32),
        "down_first": scatter_about(splits[13], (D, FF), (0.066 * TOKENS ** 0.5), 32.0, ((0, 8), (1, 4)), jnp.float32),
        "down_second": jnp.clip(jnp.exp(math.log(622.592) - 1.3862944 * jax.random.uniform(splits[14], (D, FF), jnp.float32) ** steps_of(splits[14], (D, FF), ((0, 8), (1, 4)), -0.2, 0.2)), 155.648, 622.592),
        "gains": jnp.clip(1.0 + 0.1 * jax.random.normal(splits[15], (GAINS,), jnp.float32), 0.5, 1.5),
        "gains_first": scatter_about(splits[16], (GAINS,), (0.11 * TOKENS ** 0.5), 64.0, ((0, 8),), jnp.float32),
        "gains_second": jnp.clip(jnp.exp(math.log(1720.32) - 1.3768156 * jax.random.uniform(splits[17], (GAINS,), jnp.float32) ** steps_of(splits[17], (GAINS,), ((0, 8),), -0.2, 0.2)), 434.176, 1720.32),
    }


@jax.custom_vjp
def low(v):
    return lax.optimization_barrier(v.astype(jnp.bfloat16)).astype(jnp.float32)

@jax.custom_vjp
def low_back(v):
    return v

def low_keep(v):
    return (low(v), None)

def low_pass(kept, grad):
    return (grad,)

def back_keep(v):
    return (v, None)

def back_low(kept, grad):
    return (low(grad),)
low.defvjp(low_keep, low_pass)
low_back.defvjp(back_keep, back_low)
EPS_NORM = 1e-06
THETA = 1000000.0
BETA_ONE = 0.9
BETA_TWO = 0.95
ADAM_EPS = 1e-08
DECAY_RATE = 0.1
RATE_QKV = 0.05
RATE_OUT = 0.3
RATE_GATE = 0.05
RATE_DOWN = 0.03
RATE_GAIN = 1.0
HIGHEST = lax.Precision.HIGHEST

def matmul(left, right):
    return jnp.dot(left, right, precision=HIGHEST, preferred_element_type=jnp.float32)

def matmul_t(left, right):
    return lax.dot_general(left, right, (((1,), (1,)), ((), ())), precision=HIGHEST, preferred_element_type=jnp.float32)

def rms_scale(values, gain):
    factor = lax.rsqrt(lax.optimization_barrier(jnp.mean(values * values, -1, keepdims=True)) + EPS_NORM)
    return values * factor * gain

def rotary(positions):
    freq_index = jnp.arange(HD // 2, dtype=jnp.float32)
    inverse = jnp.exp(freq_index * (-2.0 * math.log(THETA) / HD))
    angles = positions.astype(jnp.float32)[:, None] * inverse[None, :]
    cosine = jnp.cos(angles)
    sine_table = jnp.sin(angles)
    return (jnp.concatenate([cosine, cosine], -1), jnp.concatenate([sine_table, sine_table], -1))

def rotate(values, cosine, sine_table):
    half_size = values.shape[-1] // 2
    turned = jnp.concatenate([-values[..., half_size:], values[..., :half_size]], -1)
    return values * cosine[:, None, :] + turned * sine_table[:, None, :]

def attend(parts):
    query, key_rot, values_low = parts
    seq_len = query.shape[0]
    grouped = query.reshape(seq_len, HK, HQ // HK, HD)
    causal = jnp.arange(seq_len)[:, None] >= jnp.arange(seq_len)[None, :]
    scores = jnp.einsum('qkgd,skd->kgqs', grouped, key_rot, precision=HIGHEST)
    scores = low_back(scores)
    scores = jnp.where(causal, scores, -1000000000.0)
    probs_low = low(jax.nn.softmax(scores, axis=-1))
    output = jnp.einsum('kgqs,skd->qkgd', probs_low, values_low, precision=HIGHEST)
    return output.reshape(seq_len, HQ * HD)

def layer(inputs, qkv_weight, out_weight, gate_up, down_weight, gains, cosine, sine_table):
    tok_rows = inputs.shape[0]
    gain_all = low(gains)
    gain_in = gain_all[:D]
    gain_post = gain_all[D:2 * D]
    gain_q = gain_all[2 * D:2 * D + HD]
    gain_k = gain_all[2 * D + HD:]
    normed = low(rms_scale(inputs, gain_in))
    mixed_proj = matmul(normed, low(qkv_weight).reshape(D, HK * 4 * HD))
    mixed_proj = low_back(mixed_proj).reshape(tok_rows, HK, 4, HD)
    query_raw = mixed_proj[:, :, :2].reshape(tok_rows, HQ, HD)
    key_raw = mixed_proj[:, :, 2]
    values_low = low(mixed_proj[:, :, 3])
    query = low(rotate(rms_scale(query_raw, gain_q), cosine, sine_table) * (1.0 / math.sqrt(HD)))
    key_rot = low(rotate(rms_scale(key_raw, gain_k), cosine, sine_table))
    seq_count = tok_rows // SEQ
    attended = lax.map(jax.checkpoint(attend), (query.reshape(seq_count, SEQ, HQ, HD), key_rot.reshape(seq_count, SEQ, HK, HD), values_low.reshape(seq_count, SEQ, HK, HD)))
    attended = low(low_back(attended.reshape(tok_rows, HQ * HD)))
    branch = low_back(matmul_t(attended, low(out_weight)))
    hidden = inputs + branch
    normed_post = low(rms_scale(hidden, gain_post))
    gate_low = low(gate_up)
    gate_pre = low_back(matmul(normed_post, gate_low[0]))
    up_proj = low_back(matmul(normed_post, gate_low[1]))
    active = low(jax.nn.silu(gate_pre) * up_proj)
    mlp_out = low_back(matmul_t(active, low(down_weight)))
    return hidden + mlp_out

def adamw(weight, gradient, moment, second, step_rate, decay_rate):
    moment = BETA_ONE * moment + (1.0 - BETA_ONE) * gradient
    second = BETA_TWO * second + (1.0 - BETA_TWO) * gradient * gradient
    first_hat = moment / (1.0 - BETA_ONE ** STEP)
    second_hat = second / (1.0 - BETA_TWO ** STEP)
    weight = weight - step_rate * (first_hat / (jnp.sqrt(second_hat) + ADAM_EPS) + decay_rate * weight)
    return (moment, second, weight)

def reference(tokens, positions, out_grad, qkv_weight, qkv_first, qkv_second, out_weight, out_first, out_second, gate_up, gate_up_first, gate_up_second, down_weight, down_first, down_second, gains, gains_first, gains_second):
    seq_count = TOKENS // SEQ
    group_seqs = max((group_size for group_size in range(1, seq_count + 1) if seq_count % group_size == 0 and group_size * SEQ <= max(4096, SEQ)))
    scan_steps = seq_count // group_seqs
    group_rows = group_seqs * SEQ
    input_groups = tokens.astype(jnp.float32).reshape(scan_steps, group_rows, D)
    position_groups = positions.reshape(scan_steps, group_rows)
    grad_groups = out_grad.astype(jnp.float32).reshape(scan_steps, group_rows, D)
    weights = (qkv_weight, out_weight, gate_up, down_weight, gains)

    def one_group(totals, item):
        input_part, position_part, grad_part = item
        cosine, sine_table = rotary(position_part)

        def forward(inputs, *params):
            return layer(inputs, *params, cosine, sine_table)
        output, pull_back = jax.vjp(forward, input_part, *weights)
        pulled = pull_back(grad_part)
        totals = tuple((jnp.add(left_sum, right_sum) for left_sum, right_sum in zip(totals, pulled[1:])))
        return (totals, (output.astype(jnp.bfloat16), pulled[0]))
    zeros = tuple((jnp.zeros(weight.shape, jnp.float32) for weight in weights))
    totals, (outputs, input_grads) = lax.scan(one_group, zeros, (input_groups, position_groups, grad_groups))
    block_out = outputs.reshape(TOKENS, D)
    grad_input = input_grads.reshape(TOKENS, D)
    qkv_m, qkv_v, qkv_w = adamw(qkv_weight, totals[0], qkv_first, qkv_second, RATE_QKV, DECAY_RATE)
    out_m, out_v, out_w = adamw(out_weight, totals[1], out_first, out_second, RATE_OUT, DECAY_RATE)
    gate_m, gate_v, gate_w = adamw(gate_up, totals[2], gate_up_first, gate_up_second, RATE_GATE, DECAY_RATE)
    down_m, down_v, down_w = adamw(down_weight, totals[3], down_first, down_second, RATE_DOWN, DECAY_RATE)
    gain_m, gain_v, gain_w = adamw(gains, totals[4], gains_first, gains_second, RATE_GAIN, 0.0)
    return (block_out, grad_input, qkv_m, qkv_v, qkv_w, out_m, out_v, out_w, gate_m, gate_v, gate_w, down_m, down_v, down_w, gain_m, gain_v, gain_w)
```

```python
import functools
import math

import jax
import jax.numpy as jnp
from jax import lax
from jax.sharding import PartitionSpec as P

SEQ = 1024
STEP = 10


EPS_NORM = 1e-06
THETA = 1000000.0
BETA_ONE = 0.9
BETA_TWO = 0.95
ADAM_EPS = 1e-08
DECAY_RATE = 0.1
RATE_QKV = 0.05
RATE_OUT = 0.3
RATE_GATE = 0.05
RATE_DOWN = 0.03
RATE_GAIN = 1.0


def rotary(positions, head_size):
    freq_index = jnp.arange(head_size // 2, dtype=jnp.float32)
    inverse = jnp.exp(freq_index * (-2.0 * math.log(THETA) / head_size))
    angles = positions.astype(jnp.float32)[:, None] * inverse[None, :]
    cosine = jnp.cos(angles)
    sine_table = jnp.sin(angles)
    return (jnp.concatenate([cosine, cosine], -1), jnp.concatenate([sine_table, sine_table], -1))


def rotate(values, cosine, sine_table):
    half_size = values.shape[-1] // 2
    turned = jnp.concatenate([-values[..., half_size:], values[..., :half_size]], -1)
    return values * cosine[:, None, :] + turned * sine_table[:, None, :]


def unrotate(gradient, cosine, sine_table):
    half_size = gradient.shape[-1] // 2
    turned = gradient * sine_table[:, None, :]
    rotated_back = jnp.concatenate([turned[..., half_size:], -turned[..., :half_size]], -1)
    return gradient * cosine[:, None, :] + rotated_back


def norm_back(grad_unit, unit_vals, factor):
    return factor * (grad_unit - unit_vals * jnp.mean(grad_unit * unit_vals, -1, keepdims=True))


def contract_rows(left, right):
    return lax.dot_general(
        left, right, (((0,), (0,)), ((), ())), preferred_element_type=jnp.float32
    )


def contract_cols(left, right):
    return lax.dot_general(
        left, right, (((1,), (1,)), ((), ())), preferred_element_type=jnp.float32
    )


def block_scores(query_part, key_part, first_row, block_rows, last_row):
    scores = jnp.einsum(
        "nqkgd,nskd->nkgqs", query_part, key_part, preferred_element_type=jnp.float32
    )
    causal = (first_row + jnp.arange(block_rows))[:, None] >= jnp.arange(last_row)[None, :]
    return jnp.where(causal, scores, -1000000000.0)


def attention_forward(query, key_rot, values_low, seq_len):
    block_rows = min(512, seq_len)
    outputs = []
    log_sums = []
    for first_row in range(0, seq_len, block_rows):
        last_row = first_row + block_rows
        query_part = query[:, first_row:last_row]
        scores = block_scores(query_part, key_rot[:, :last_row], first_row, block_rows, last_row)
        row_max = jnp.max(scores, -1, keepdims=True)
        exponent = jnp.exp(scores - row_max)
        row_total = jnp.sum(exponent, -1, keepdims=True)
        probs_low = (exponent / row_total).astype(jnp.bfloat16)
        outputs.append(
            jnp.einsum(
                "nkgqs,nskd->nqkgd",
                probs_low,
                values_low[:, :last_row],
                preferred_element_type=jnp.float32,
            )
        )
        log_sums.append(row_max + jnp.log(row_total))
    return (jnp.concatenate(outputs, 1), log_sums)


def attention_backward(query, key_rot, values_low, grad_att, log_sums, seq_len):
    block_rows = min(512, seq_len)
    query_grads = []
    key_grad = jnp.zeros(key_rot.shape, jnp.float32)
    value_grad = jnp.zeros(values_low.shape, jnp.float32)
    for block_index, first_row in enumerate(range(0, seq_len, block_rows)):
        last_row = first_row + block_rows
        query_part = query[:, first_row:last_row]
        grad_part = grad_att[:, first_row:last_row]
        key_part = key_rot[:, :last_row]
        value_part = values_low[:, :last_row]
        scores = block_scores(query_part, key_part, first_row, block_rows, last_row)
        probs = jnp.exp(scores - log_sums[block_index])
        probs_low = probs.astype(jnp.bfloat16)
        grad_probs = jnp.einsum(
            "nqkgd,nskd->nkgqs", grad_part, value_part, preferred_element_type=jnp.float32
        )
        grad_scores = (
            probs * (grad_probs - jnp.sum(probs * grad_probs, -1, keepdims=True))
        ).astype(jnp.bfloat16)
        query_grads.append(
            jnp.einsum(
                "nkgqs,nskd->nqkgd", grad_scores, key_part, preferred_element_type=jnp.float32
            )
        )
        padding = ((0, 0), (0, seq_len - last_row), (0, 0), (0, 0))
        key_grad = key_grad + jnp.pad(
            jnp.einsum(
                "nkgqs,nqkgd->nskd", grad_scores, query_part, preferred_element_type=jnp.float32
            ),
            padding,
        )
        value_grad = value_grad + jnp.pad(
            jnp.einsum(
                "nkgqs,nqkgd->nskd", probs_low, grad_part, preferred_element_type=jnp.float32
            ),
            padding,
        )
    return (jnp.concatenate(query_grads, 1), key_grad, value_grad)


def adamw(weight, gradient, moment, second, step_rate, decay_rate):
    moment = BETA_ONE * moment + (1.0 - BETA_ONE) * gradient
    second = BETA_TWO * second + (1.0 - BETA_TWO) * gradient * gradient
    first_hat = moment / (1.0 - BETA_ONE**STEP)
    second_hat = second / (1.0 - BETA_TWO**STEP)
    weight = weight - step_rate * (
        first_hat / (jnp.sqrt(second_hat) + ADAM_EPS) + decay_rate * weight
    )
    return (moment, second, weight)


class Plan:
    def __init__(self, mesh):
        self.total = mesh.shape["dp"]
        self.zones = self.total // 2
        self.tensor = mesh.shape["tensor"]

    def place(self):
        index = lax.axis_index("dp")
        self.zone = index // 2
        self.side = index % 2
        self.core = lax.axis_index("tensor") % 2

    def zone_shift(self, value, shift):
        pairs = [(d, ((d // 2 + shift) % self.zones) * 2 + d % 2) for d in range(self.total)]
        return lax.ppermute(value, "dp", pairs)

    def side_swap(self, value):
        return lax.ppermute(value, "dp", [(d, d ^ 1) for d in range(self.total)])

    def core_swap(self, value):
        return lax.ppermute(value, "tensor", [(t, t ^ 1) for t in range(self.tensor)])

    def row_swap(self, value):
        return lax.ppermute(value, "tensor", [(t, t ^ 2) for t in range(self.tensor)])

    def owner(self, slot):
        zone = (self.zone + slot % self.zones) % self.zones
        side = self.side if slot < self.zones else 1 - self.side
        return zone * 2 + side

    def to_local(self, value, axis):
        width = value.shape[axis] // self.total
        return jnp.concatenate(
            [
                lax.dynamic_slice_in_dim(value, self.owner(slot) * width, width, axis)
                for slot in range(self.total)
            ],
            axis,
        )

    def to_natural(self, value, axis):
        width = value.shape[axis] // self.total
        parts = []
        for block in range(self.total):
            zone_slot = (block // 2 - self.zone) % self.zones
            slot = zone_slot + jnp.where(block % 2 == self.side, 0, self.zones)
            parts.append(lax.dynamic_slice_in_dim(value, slot * width, width, axis))
        return jnp.concatenate(parts, axis)

    def gather(self, shard, axis):
        near = [shard] + [self.zone_shift(shard, -shift) for shift in range(1, self.zones)]
        far = [self.side_swap(part) for part in near]
        return jnp.concatenate(near + far, axis)

    def scatter(self, make_near, make_far, axis):
        far = make_far().astype(jnp.bfloat16)
        width = far.shape[axis] // self.zones
        got = [
            self.side_swap(lax.slice_in_dim(far, slot * width, (slot + 1) * width, axis=axis))
            for slot in range(self.zones)
        ]
        near = make_near()
        near = [
            lax.slice_in_dim(near, slot * width, (slot + 1) * width, axis=axis)
            + got[slot].astype(jnp.float32)
            for slot in range(self.zones)
        ]
        total = near[0]
        for shift in range(1, self.zones):
            total = total + self.zone_shift(near[shift].astype(jnp.bfloat16), shift).astype(
                jnp.float32
            )
        return total

    def half(self, value, which):
        rows = value.shape[0] // 2
        return lax.dynamic_slice_in_dim(value, which * rows, rows, 0)

    def tensor_sum(self, terms):
        got = self.core_swap(terms(1 - self.core).astype(jnp.bfloat16))
        chip = (terms(self.core) + got.astype(jnp.float32)).astype(jnp.bfloat16)
        return chip.astype(jnp.float32) + self.row_swap(chip).astype(jnp.float32)

    def both_cores(self, value):
        other = self.core_swap(value)
        first = self.core == 0
        return jnp.concatenate(
            [jnp.where(first, value, other), jnp.where(first, other, value)], 0
        )

    def tensor_total(self, value):
        value = value + self.core_swap(value)
        return value + self.row_swap(value)

    def gather_small(self, shard):
        index = lax.axis_index("dp")
        parts = jnp.stack(
            [shard]
            + [
                lax.ppermute(shard, "dp", [(d, (d + step) % self.total) for d in range(self.total)])
                for step in range(1, self.total)
            ]
        )
        order = (index - jnp.arange(self.total)) % self.total
        return parts[order].reshape(-1)

    def scatter_small(self, value):
        index = lax.axis_index("dp")
        parts = value.reshape(self.total, -1)
        total = parts[index]
        for step in range(1, self.total):
            total = total + lax.ppermute(
                parts[(index + step) % self.total],
                "dp",
                [(d, (d + step) % self.total) for d in range(self.total)],
            )
        return total


def shards(
    plan,
    tokens,
    positions,
    out_grad,
    qkv_weight,
    qkv_first,
    qkv_second,
    out_weight,
    out_first,
    out_second,
    gate_up,
    gate_up_first,
    gate_up_second,
    down_weight,
    down_first,
    down_second,
    gains,
    gains_first,
    gains_second,
):
    plan.place()
    tok_rows, model_width = tokens.shape
    groups = qkv_weight.shape[1]
    head_size = qkv_weight.shape[3]
    shard_rows = qkv_weight.shape[0]
    seq_count = tok_rows // SEQ
    mixed_cols = groups * 4 * head_size
    near_cols = model_width // 2
    full_gains = plan.gather_small(gains.astype(jnp.bfloat16))
    full_qkv = plan.gather(qkv_weight.reshape(shard_rows, mixed_cols).astype(jnp.bfloat16), 0)
    full_out = plan.gather(out_weight.astype(jnp.bfloat16), 0)
    full_gate = plan.gather(gate_up.astype(jnp.bfloat16), 1)
    full_down = plan.gather(down_weight.astype(jnp.bfloat16), 0)
    gain_all = full_gains.astype(jnp.float32)
    gain_in = plan.to_local(gain_all[:model_width], 0)
    gain_post = plan.to_local(gain_all[model_width : 2 * model_width], 0)
    gain_q = gain_all[2 * model_width : 2 * model_width + head_size]
    gain_k = gain_all[2 * model_width + head_size :]
    tokens = plan.to_local(tokens, 1)
    out_grad = plan.to_local(out_grad, 1)
    inputs = tokens.astype(jnp.float32)
    factor_in = lax.rsqrt(jnp.mean(inputs * inputs, -1, keepdims=True) + EPS_NORM)
    normed = (inputs * factor_in * gain_in).astype(jnp.bfloat16)
    mixed_proj = jnp.dot(normed, full_qkv, preferred_element_type=jnp.float32).reshape(
        tok_rows, groups, 4, head_size
    )
    query_raw = mixed_proj[:, :, :2].reshape(tok_rows, groups * 2, head_size)
    key_raw = mixed_proj[:, :, 2]
    values_low = mixed_proj[:, :, 3].astype(jnp.bfloat16)
    cosine, sine_table = rotary(positions, head_size)
    score_scale = 1.0 / math.sqrt(head_size)
    factor_q = lax.rsqrt(jnp.mean(query_raw * query_raw, -1, keepdims=True) + EPS_NORM)
    unit_q = query_raw * factor_q
    query = (rotate(unit_q * gain_q, cosine, sine_table) * score_scale).astype(jnp.bfloat16)
    factor_k = lax.rsqrt(jnp.mean(key_raw * key_raw, -1, keepdims=True) + EPS_NORM)
    unit_k = key_raw * factor_k
    key_rot = rotate(unit_k * gain_k, cosine, sine_table).astype(jnp.bfloat16)
    shaped_query = query.reshape(seq_count, SEQ, groups, 2, head_size)
    shaped_key = key_rot.reshape(seq_count, SEQ, groups, head_size)
    shaped_value = values_low.reshape(seq_count, SEQ, groups, head_size)
    attended, log_sums = attention_forward(shaped_query, shaped_key, shaped_value, SEQ)
    attended = attended.reshape(tok_rows, groups * 2 * head_size).astype(jnp.bfloat16)

    branch = plan.tensor_sum(lambda half: contract_cols(plan.half(attended, half), full_out))
    half_inputs = plan.half(tokens, plan.core).astype(jnp.float32)
    half_grad = plan.half(out_grad, plan.core).astype(jnp.float32)
    half_factor_in = plan.half(factor_in, plan.core)
    hidden = half_inputs + branch
    factor_post = lax.rsqrt(jnp.mean(hidden * hidden, -1, keepdims=True) + EPS_NORM)
    normed_rows = plan.both_cores((hidden * factor_post * gain_post).astype(jnp.bfloat16))
    gate_pre = jnp.dot(normed_rows, full_gate[0], preferred_element_type=jnp.float32)
    up_proj = jnp.dot(normed_rows, full_gate[1], preferred_element_type=jnp.float32)
    sigmoid_gate = jax.nn.sigmoid(gate_pre)
    silu_gate = gate_pre * sigmoid_gate
    active = (silu_gate * up_proj).astype(jnp.bfloat16)
    summed_down = plan.scatter(
        lambda: contract_rows(out_grad[:, :near_cols], active),
        lambda: contract_rows(out_grad[:, near_cols:], active),
        0,
    )
    grad_active = jnp.dot(out_grad, full_down, preferred_element_type=jnp.float32)
    grad_gate = (
        grad_active * up_proj * sigmoid_gate * (1.0 + gate_pre * (1.0 - sigmoid_gate))
    ).astype(jnp.bfloat16)
    grad_up = (grad_active * silu_gate).astype(jnp.bfloat16)

    def gate_terms(rows):
        return jnp.stack([contract_rows(rows, grad_gate), contract_rows(rows, grad_up)])

    summed_gate = plan.scatter(
        lambda: gate_terms(normed_rows[:, :near_cols]),
        lambda: gate_terms(normed_rows[:, near_cols:]),
        1,
    )
    grad_post = plan.tensor_sum(
        lambda half: contract_cols(plan.half(grad_gate, half), full_gate[0])
        + contract_cols(plan.half(grad_up, half), full_gate[1])
    )
    unit_post = hidden * factor_post
    post_gain_grad = jnp.sum(grad_post * unit_post, 0)
    grad_hidden = half_grad + norm_back(grad_post * gain_post, unit_post, factor_post)
    branch_rows = plan.both_cores(grad_hidden.astype(jnp.bfloat16))
    mlp_out = plan.tensor_sum(lambda half: contract_cols(plan.half(active, half), full_down))
    block_out = plan.to_natural(plan.both_cores((hidden + mlp_out).astype(jnp.bfloat16)), 1)
    summed_out = plan.scatter(
        lambda: contract_rows(branch_rows[:, :near_cols], attended),
        lambda: contract_rows(branch_rows[:, near_cols:], attended),
        0,
    )
    grad_att = jnp.dot(branch_rows, full_out, preferred_element_type=jnp.float32).astype(
        jnp.bfloat16
    )
    grad_att = grad_att.reshape(seq_count, SEQ, groups, 2, head_size)
    grad_query, grad_key, grad_value = attention_backward(
        shaped_query, shaped_key, shaped_value, grad_att, log_sums, SEQ
    )
    grad_query = unrotate(
        grad_query.reshape(tok_rows, groups * 2, head_size) * score_scale, cosine, sine_table
    )
    query_gain_grad = jnp.sum(grad_query * unit_q, (0, 1))
    grad_query = norm_back(grad_query * gain_q, unit_q, factor_q)
    grad_key = unrotate(grad_key.reshape(tok_rows, groups, head_size), cosine, sine_table)
    key_gain_grad = jnp.sum(grad_key * unit_k, (0, 1))
    grad_key = norm_back(grad_key * gain_k, unit_k, factor_k)
    grad_mixed = jnp.concatenate(
        [
            grad_query.reshape(tok_rows, groups, 2, head_size),
            grad_key[:, :, None],
            grad_value.reshape(tok_rows, groups, 1, head_size),
        ],
        2,
    )
    grad_mixed = grad_mixed.reshape(tok_rows, mixed_cols).astype(jnp.bfloat16)
    summed_qkv = plan.scatter(
        lambda: contract_rows(normed[:, :near_cols], grad_mixed),
        lambda: contract_rows(normed[:, near_cols:], grad_mixed),
        0,
    ).reshape(qkv_weight.shape)
    grad_normed = plan.tensor_sum(
        lambda half: contract_cols(plan.half(grad_mixed, half), full_qkv)
    )
    half_unit = half_inputs * half_factor_in
    input_gain_grad = jnp.sum(grad_normed * half_unit, 0)
    input_rows = grad_hidden + norm_back(grad_normed * gain_in, half_unit, half_factor_in)
    input_rows = plan.to_natural(plan.both_cores(input_rows), 1)
    gain_terms = jnp.concatenate(
        [
            0.5 * plan.to_natural(input_gain_grad, 0),
            0.5 * plan.to_natural(post_gain_grad, 0),
            query_gain_grad,
            key_gain_grad,
        ]
    )
    summed_gains = plan.tensor_total(plan.scatter_small(gain_terms))
    qkv_moment, qkv_square, qkv_updated = adamw(
        qkv_weight, summed_qkv, qkv_first, qkv_second, RATE_QKV, DECAY_RATE
    )
    out_moment, out_square, out_updated = adamw(
        out_weight, summed_out, out_first, out_second, RATE_OUT, DECAY_RATE
    )
    gate_moment, gate_square, gate_updated = adamw(
        gate_up, summed_gate, gate_up_first, gate_up_second, RATE_GATE, DECAY_RATE
    )
    down_moment, down_square, down_updated = adamw(
        down_weight, summed_down, down_first, down_second, RATE_DOWN, DECAY_RATE
    )
    gain_moment, gain_square, gain_updated = adamw(
        gains, summed_gains, gains_first, gains_second, RATE_GAIN, 0.0
    )
    return (
        block_out,
        input_rows,
        qkv_moment,
        qkv_square,
        qkv_updated,
        out_moment,
        out_square,
        out_updated,
        gate_moment,
        gate_square,
        gate_updated,
        down_moment,
        down_square,
        down_updated,
        gain_moment,
        gain_square,
        gain_updated,
    )


def solution(mesh):
    plan = Plan(mesh)
    placed = (
        P("dp", None),
        P("dp"),
        P("dp", None),
        P("dp", "tensor", None, None),
        P("dp", "tensor", None, None),
        P("dp", "tensor", None, None),
        P("dp", "tensor"),
        P("dp", "tensor"),
        P("dp", "tensor"),
        P(None, "dp", "tensor"),
        P(None, "dp", "tensor"),
        P(None, "dp", "tensor"),
        P("dp", "tensor"),
        P("dp", "tensor"),
        P("dp", "tensor"),
        P("dp"),
        P("dp"),
        P("dp"),
    )
    return jax.shard_map(
        functools.partial(shards, plan),
        mesh=mesh,
        in_specs=placed,
        out_specs=(
            P("dp", None),
            P("dp", None),
            P("dp", "tensor", None, None),
            P("dp", "tensor", None, None),
            P("dp", "tensor", None, None),
            P("dp", "tensor"),
            P("dp", "tensor"),
            P("dp", "tensor"),
            P(None, "dp", "tensor"),
            P(None, "dp", "tensor"),
            P(None, "dp", "tensor"),
            P("dp", "tensor"),
            P("dp", "tensor"),
            P("dp", "tensor"),
            P("dp"),
            P("dp"),
            P("dp"),
        ),
        check_vma=False,
    )
```

```python
import functools
import math

import jax
import jax.numpy as jnp
from jax import lax
from jax.sharding import PartitionSpec as P

SEQ = 1024
STEP = 10


EPS_NORM = 1e-06
THETA = 1000000.0
BETA_ONE = 0.9
BETA_TWO = 0.95
ADAM_EPS = 1e-08
DECAY_RATE = 0.1
RATE_QKV = 0.05
RATE_OUT = 0.3
RATE_GATE = 0.05
RATE_DOWN = 0.03
RATE_GAIN = 1.0


def rotary(positions, head_size):
    freq_index = jnp.arange(head_size // 2, dtype=jnp.float32)
    inverse = jnp.exp(freq_index * (-2.0 * math.log(THETA) / head_size))
    angles = positions.astype(jnp.float32)[:, None] * inverse[None, :]
    cosine = jnp.cos(angles)
    sine_table = jnp.sin(angles)
    return (jnp.concatenate([cosine, cosine], -1), jnp.concatenate([sine_table, sine_table], -1))


def rotate(values, cosine, sine_table):
    half_size = values.shape[-1] // 2
    turned = jnp.concatenate([-values[..., half_size:], values[..., :half_size]], -1)
    return values * cosine[:, None, :] + turned * sine_table[:, None, :]


def unrotate(gradient, cosine, sine_table):
    half_size = gradient.shape[-1] // 2
    turned = gradient * sine_table[:, None, :]
    rotated_back = jnp.concatenate([turned[..., half_size:], -turned[..., :half_size]], -1)
    return gradient * cosine[:, None, :] + rotated_back


def norm_back(grad_unit, unit_vals, factor):
    return factor * (grad_unit - unit_vals * jnp.mean(grad_unit * unit_vals, -1, keepdims=True))


def contract_rows(left, right):
    return lax.dot_general(
        left, right, (((0,), (0,)), ((), ())), preferred_element_type=jnp.float32
    )


def contract_cols(left, right):
    return lax.dot_general(
        left, right, (((1,), (1,)), ((), ())), preferred_element_type=jnp.float32
    )


def block_scores(query_part, key_part, first_row, block_rows, last_row):
    scores = jnp.einsum(
        "nqkgd,nskd->nkgqs", query_part, key_part, preferred_element_type=jnp.float32
    )
    causal = (first_row + jnp.arange(block_rows))[:, None] >= jnp.arange(last_row)[None, :]
    return jnp.where(causal, scores, -1000000000.0)


def attention_forward(query, key_rot, values_low, seq_len):
    block_rows = min(512, seq_len)
    outputs = []
    log_sums = []
    for first_row in range(0, seq_len, block_rows):
        last_row = first_row + block_rows
        query_part = query[:, first_row:last_row]
        scores = block_scores(query_part, key_rot[:, :last_row], first_row, block_rows, last_row)
        row_max = jnp.max(scores, -1, keepdims=True)
        exponent = jnp.exp(scores - row_max)
        row_total = jnp.sum(exponent, -1, keepdims=True)
        probs_low = (exponent / row_total).astype(jnp.bfloat16)
        outputs.append(
            jnp.einsum(
                "nkgqs,nskd->nqkgd",
                probs_low,
                values_low[:, :last_row],
                preferred_element_type=jnp.float32,
            )
        )
        log_sums.append(row_max + jnp.log(row_total))
    return (jnp.concatenate(outputs, 1), log_sums)


def attention_backward(query, key_rot, values_low, grad_att, log_sums, seq_len):
    block_rows = min(512, seq_len)
    query_grads = []
    key_grad = jnp.zeros(key_rot.shape, jnp.float32)
    value_grad = jnp.zeros(values_low.shape, jnp.float32)
    for block_index, first_row in enumerate(range(0, seq_len, block_rows)):
        last_row = first_row + block_rows
        query_part = query[:, first_row:last_row]
        grad_part = grad_att[:, first_row:last_row]
        key_part = key_rot[:, :last_row]
        value_part = values_low[:, :last_row]
        scores = block_scores(query_part, key_part, first_row, block_rows, last_row)
        probs = jnp.exp(scores - log_sums[block_index])
        probs_low = probs.astype(jnp.bfloat16)
        grad_probs = jnp.einsum(
            "nqkgd,nskd->nkgqs", grad_part, value_part, preferred_element_type=jnp.float32
        )
        grad_scores = (
            probs * (grad_probs - jnp.sum(probs * grad_probs, -1, keepdims=True))
        ).astype(jnp.bfloat16)
        query_grads.append(
            jnp.einsum(
                "nkgqs,nskd->nqkgd", grad_scores, key_part, preferred_element_type=jnp.float32
            )
        )
        padding = ((0, 0), (0, seq_len - last_row), (0, 0), (0, 0))
        key_grad = key_grad + jnp.pad(
            jnp.einsum(
                "nkgqs,nqkgd->nskd", grad_scores, query_part, preferred_element_type=jnp.float32
            ),
            padding,
        )
        value_grad = value_grad + jnp.pad(
            jnp.einsum(
                "nkgqs,nqkgd->nskd", probs_low, grad_part, preferred_element_type=jnp.float32
            ),
            padding,
        )
    return (jnp.concatenate(query_grads, 1), key_grad, value_grad)


def adamw(weight, gradient, moment, second, step_rate, decay_rate):
    moment = BETA_ONE * moment + (1.0 - BETA_ONE) * gradient
    second = BETA_TWO * second + (1.0 - BETA_TWO) * gradient * gradient
    first_hat = moment / (1.0 - BETA_ONE**STEP)
    second_hat = second / (1.0 - BETA_TWO**STEP)
    weight = weight - step_rate * (
        first_hat / (jnp.sqrt(second_hat) + ADAM_EPS) + decay_rate * weight
    )
    return (moment, second, weight)


def fence(*values):
    return lax.optimization_barrier(values)


class Plan:
    def __init__(self, mesh):
        self.total = mesh.shape["dp"]
        self.zones = self.total // 2
        self.tensor = mesh.shape["tensor"]

    def place(self):
        self.index = lax.axis_index("dp")
        self.zone = self.index // 2
        self.side = self.index % 2
        self.row = lax.axis_index("tensor") // 2
        self.core = lax.axis_index("tensor") % 2
        self.home = self.side == self.core

    def move(self, value, target):
        pairs = []
        for d in range(self.total):
            for t in range(self.tensor):
                to = target(d // 2, d % 2, t // 2, t % 2)
                if to is not None:
                    zone, side, row, core = to
                    pairs.append((d * self.tensor + t, (zone * 2 + side) * self.tensor + row * 2 + core))
        return lax.ppermute(value, ("dp", "tensor"), pairs)

    def turn(self, value):
        return self.move(value, lambda z, y, x, c: (z, c, x, y))

    def zone_shift(self, value, shift):
        return self.move(value, lambda z, y, x, c: ((z + shift) % self.zones, y, x, c))

    def zone_flip(self, value, bit):
        return self.move(value, lambda z, y, x, c: (z ^ bit, y, x, c))

    def core_swap(self, value):
        return self.move(value, lambda z, y, x, c: (z, y, x, 1 - c))

    def side_swap(self, value):
        return self.move(value, lambda z, y, x, c: (z, 1 - y, x, c))

    def row_swap(self, value):
        return self.move(value, lambda z, y, x, c: (z, y, 1 - x, c))

    def to_local(self, value, axis):
        width = value.shape[axis] // self.total
        parts = []
        for core in (self.core, 1 - self.core):
            for slot in range(self.zones):
                owner = ((self.zone + slot) % self.zones) * 2 + core
                parts.append(lax.dynamic_slice_in_dim(value, owner * width, width, axis))
        return jnp.concatenate(parts, axis)

    def to_natural(self, value, axis):
        width = value.shape[axis] // self.total
        parts = []
        for block in range(self.total):
            slot = (block // 2 - self.zone) % self.zones
            slot = slot + jnp.where(block % 2 == self.core, 0, self.zones)
            parts.append(lax.dynamic_slice_in_dim(value, slot * width, width, axis))
        return jnp.concatenate(parts, axis)

    def row_owners(self):
        own, off = (self.row, self.side), (1 - self.row, 1 - self.side)
        first = lambda x, y: x * 2 + y
        second = lambda x, y: 4 + y * 2 + x
        return [
            first(own[0], own[1]),
            first(own[0], off[1]),
            second(own[0], own[1]),
            second(off[0], own[1]),
            first(off[0], own[1]),
            first(off[0], off[1]),
            second(own[0], off[1]),
            second(off[0], off[1]),
        ]

    def rows_local(self, value, slots=range(8)):
        size = value.shape[0] // 8
        owners = self.row_owners()
        return jnp.concatenate(
            [lax.dynamic_slice_in_dim(value, owners[slot] * size, size, 0) for slot in slots], 0
        )

    def rows_natural(self, value, order=range(8)):
        size = value.shape[0] // 8
        place = [list(order).index(slot) for slot in range(8)]
        parts = []
        for piece in range(8):
            x, y = (piece // 2, piece % 2) if piece < 4 else (piece % 2, (piece - 4) // 2)
            slots = (0, 1, 4, 5) if piece < 4 else (2, 6, 3, 7)
            same_x, same_y = x == self.row, y == self.side
            slot = jnp.where(
                same_x,
                jnp.where(same_y, place[slots[0]], place[slots[1]]),
                jnp.where(same_y, place[slots[2]], place[slots[3]]),
            )
            parts.append(lax.dynamic_slice_in_dim(value, slot * size, size, 0))
        return jnp.concatenate(parts, 0)

    def from_zones(self, shard):
        return [self.zone_shift(shard, -shift) for shift in range(1, self.zones)]

    def to_zones(self, parts):
        return [self.zone_shift(parts[shift], shift) for shift in range(1, self.zones)]

    def first_swap(self, send):
        half = send.shape[0] // 2
        return self.row_swap(send[:half]), self.side_swap(send[half:])

    def second_swap(self, keep, got):
        quarter = keep.shape[0] // 4
        row_part = keep[: 2 * quarter] + got[0].astype(jnp.float32)
        side_part = keep[2 * quarter :] + got[1].astype(jnp.float32)
        own = jnp.concatenate([row_part[:quarter], side_part[:quarter]], 0)
        return own, (
            self.side_swap(row_part[quarter:].astype(jnp.bfloat16)),
            self.row_swap(side_part[quarter:].astype(jnp.bfloat16)),
        )

    def spread_first(self, own):
        half = own.shape[0] // 2
        return (self.side_swap(own[:half]), self.row_swap(own[half:]))

    def spread_second(self, own, got):
        half = own.shape[0] // 2
        row_part = jnp.concatenate([own[:half], got[0]], 0)
        side_part = jnp.concatenate([own[half:], got[1]], 0)
        return row_part, side_part, self.row_swap(row_part), self.side_swap(side_part)

    def send_home(self, own):
        to_home = lambda z, y, x, c: (z, c, x, c) if y != c else None
        return jnp.concatenate([own, self.move(own, to_home)], 0)

    def row_home(self, part):
        return self.move(part, lambda z, y, x, c: (z, y, 1 - x, c) if y == c else None)

    def share_home(self, part, other):
        full = jnp.concatenate([part, other], 0)
        full = self.to_natural(self.rows_natural(full, (0, 2, 1, 6, 4, 3, 5, 7)), 1)
        got = self.move(full, lambda z, y, x, c: (z, y, x, 1 - c) if y == c else None)
        return full, got

    def sum_everywhere(self, value):
        value = value + self.row_swap(value)
        value = value + self.side_swap(value)
        value = value + self.core_swap(value)
        bit = 1
        while bit < self.zones:
            value = value + self.zone_flip(value, bit)
            bit *= 2
        return value


def shards(
    plan,
    tokens,
    positions,
    out_grad,
    qkv_weight,
    qkv_first,
    qkv_second,
    out_weight,
    out_first,
    out_second,
    gate_up,
    gate_up_first,
    gate_up_second,
    down_weight,
    down_first,
    down_second,
    gains,
    gains_first,
    gains_second,
):
    plan.place()
    low = jnp.bfloat16
    tok_rows, model_width = tokens.shape
    groups = qkv_weight.shape[1]
    head_size = qkv_weight.shape[3]
    shard_rows = qkv_weight.shape[0]
    seq_count = tok_rows // SEQ
    mixed_cols = groups * 4 * head_size
    near_cols = model_width // 2
    kept = tok_rows // 2
    gain_count = gains.shape[0]

    gain_rows = 16
    gain_block = jnp.pad(gains.astype(low), (0, gain_rows * mixed_cols - gain_count))
    low_qkv = jnp.concatenate(
        [
            qkv_weight.reshape(shard_rows, mixed_cols).astype(low),
            gain_block.reshape(gain_rows, mixed_cols),
        ],
        0,
    )
    turned_qkv = plan.turn(low_qkv)
    tokens = plan.turn(tokens)
    positions = plan.turn(positions.astype(jnp.float32))
    turned_out = plan.turn(out_weight.astype(low))
    turned_qkv, turned_out, low_gate = fence(turned_qkv, turned_out, gate_up.astype(low))

    zone_qkv = plan.from_zones(turned_qkv)
    turned_gate = plan.turn(low_gate)
    zone_qkv, tokens, positions, turned_gate, turned_out, turned_qkv, low_down, out_grad = fence(
        zone_qkv,
        tokens,
        positions,
        turned_gate,
        turned_out,
        turned_qkv,
        down_weight.astype(low),
        out_grad,
    )

    near_qkv = jnp.stack([turned_qkv] + zone_qkv)
    far_qkv = plan.core_swap(near_qkv)
    zone_out = plan.from_zones(turned_out)
    out_grad = plan.turn(out_grad)
    tokens = plan.to_local(tokens, 1)
    inputs = tokens.astype(jnp.float32)
    factor_in = lax.rsqrt(jnp.mean(inputs * inputs, -1, keepdims=True) + EPS_NORM)
    cosine, sine_table = rotary(positions, head_size)
    near_qkv, far_qkv, zone_out, turned_out, tokens, factor_in, cosine, sine_table, turned_gate, low_down = fence(
        near_qkv,
        far_qkv,
        zone_out,
        turned_out,
        tokens,
        factor_in,
        cosine,
        sine_table,
        turned_gate,
        low_down,
    )

    near_out = jnp.concatenate([turned_out] + zone_out, 0)
    far_out = plan.core_swap(near_out)
    zone_gate = plan.from_zones(turned_gate[0])
    turned_down = plan.turn(low_down)
    both_qkv = jnp.concatenate([near_qkv, far_qkv], 0)
    full_qkv = both_qkv[:, :shard_rows].reshape(model_width, mixed_cols)
    gain_slots = both_qkv[:, shard_rows:].reshape(plan.total, gain_rows * mixed_cols)[:, :gain_count]
    gain_all = plan.to_natural(gain_slots.reshape(-1), 0).astype(jnp.float32)
    gain_in = plan.to_local(gain_all[:model_width], 0)
    gain_post = plan.to_local(gain_all[model_width : 2 * model_width], 0)
    gain_q = gain_all[2 * model_width : 2 * model_width + head_size]
    gain_k = gain_all[2 * model_width + head_size :]
    inputs = tokens.astype(jnp.float32)
    normed = (inputs * factor_in * gain_in).astype(low)
    mixed_proj = jnp.dot(normed, full_qkv, preferred_element_type=jnp.float32).reshape(
        tok_rows, groups, 4, head_size
    )
    query_raw = mixed_proj[:, :, :2].reshape(tok_rows, groups * 2, head_size)
    key_raw = mixed_proj[:, :, 2]
    values_low = mixed_proj[:, :, 3].astype(low)
    score_scale = 1.0 / math.sqrt(head_size)
    factor_q = lax.rsqrt(jnp.mean(query_raw * query_raw, -1, keepdims=True) + EPS_NORM)
    unit_q = query_raw * factor_q
    query = (rotate(unit_q * gain_q, cosine, sine_table) * score_scale).astype(low)
    factor_k = lax.rsqrt(jnp.mean(key_raw * key_raw, -1, keepdims=True) + EPS_NORM)
    unit_k = key_raw * factor_k
    key_rot = rotate(unit_k * gain_k, cosine, sine_table).astype(low)
    shaped_query = query.reshape(seq_count, SEQ, groups, 2, head_size)
    shaped_key = key_rot.reshape(seq_count, SEQ, groups, head_size)
    shaped_value = values_low.reshape(seq_count, SEQ, groups, head_size)
    attended, log_sums = attention_forward(shaped_query, shaped_key, shaped_value, SEQ)
    attended = attended.reshape(tok_rows, groups * 2 * head_size).astype(low)
    attended = plan.rows_local(attended)
    attended, near_out, far_out = fence(attended, near_out, far_out)

    full_out = jnp.concatenate([near_out, far_out], 0)
    branch_send = contract_cols(attended[kept:], full_out).astype(low)
    branch_got = plan.first_swap(branch_send)
    branch_keep = contract_cols(attended[:kept], full_out)
    branch_keep, branch_got, zone_gate, turned_gate, turned_down, out_grad, tokens = fence(
        branch_keep, branch_got, zone_gate, turned_gate, turned_down, out_grad, tokens
    )

    zone_up = plan.from_zones(turned_gate[1])
    branch_own, branch_last = plan.second_swap(branch_keep, branch_got)
    near_gate = jnp.concatenate([turned_gate[0]] + zone_gate, 0)
    own_tokens = plan.rows_local(tokens, (0, 1, 2, 3))
    eighth = tok_rows // 8
    own_pick = lambda v: jnp.concatenate([v[:eighth], v[2 * eighth : 3 * eighth]], 0)
    own_inputs = own_pick(own_tokens).astype(jnp.float32)
    out_grad = plan.to_local(plan.rows_local(out_grad), 1)
    branch_own, branch_last, near_gate, own_inputs, out_grad = fence(
        branch_own, branch_last, near_gate, own_inputs, out_grad
    )

    branch = branch_own + jnp.concatenate(branch_last, 0).astype(jnp.float32)
    hidden = own_inputs + branch
    factor_post = lax.rsqrt(jnp.mean(hidden * hidden, -1, keepdims=True) + EPS_NORM)
    normed_own = (hidden * factor_post * gain_post).astype(low)
    normed_got = plan.spread_first(normed_own)
    normed_own, normed_got, hidden, near_gate = fence(normed_own, normed_got, hidden, near_gate)

    row_part, side_part, row_got, side_got = plan.spread_second(normed_own, normed_got)
    far_gate = plan.core_swap(near_gate)
    row_part, side_part, row_got, side_got, near_gate, far_gate, zone_up, turned_gate, turned_down = fence(
        row_part, side_part, row_got, side_got, near_gate, far_gate, zone_up, turned_gate, turned_down
    )

    zone_down = plan.from_zones(turned_down)
    normed_rows = jnp.concatenate([row_part, side_part, row_got, side_got], 0)
    full_gate = jnp.concatenate([near_gate, far_gate], 0)
    near_up = jnp.concatenate([turned_gate[1]] + zone_up, 0)
    far_up = plan.core_swap(near_up)
    gate_pre = jnp.dot(normed_rows, full_gate, preferred_element_type=jnp.float32)
    gate_pre, near_up, far_up, normed_rows = fence(gate_pre, near_up, far_up, normed_rows)

    full_up = jnp.concatenate([near_up, far_up], 0)
    up_proj = jnp.dot(normed_rows, full_up, preferred_element_type=jnp.float32)
    sigmoid_gate = jax.nn.sigmoid(gate_pre)
    silu_gate = gate_pre * sigmoid_gate
    active = (silu_gate * up_proj).astype(low)
    down_far = contract_rows(out_grad[:, near_cols:], active).astype(low)
    down_far, active, up_proj, gate_pre, out_grad = fence(down_far, active, up_proj, gate_pre, out_grad)

    down_got = plan.core_swap(down_far)
    down_near = contract_rows(out_grad[:, :near_cols], active)
    down_near, down_got, zone_down, turned_down, active, up_proj, gate_pre, out_grad = fence(
        down_near, down_got, zone_down, turned_down, active, up_proj, gate_pre, out_grad
    )

    def zone_parts(near, got):
        both = (near + got.astype(jnp.float32)).astype(low)
        size = both.shape[0] // plan.zones
        return [both[slot * size : (slot + 1) * size] for slot in range(plan.zones)]

    def zone_total(parts, arrived):
        total = parts[0].astype(jnp.float32)
        for part in arrived:
            total = total + part.astype(jnp.float32)
        return total.astype(low)

    down_parts = zone_parts(down_near, down_got)
    down_sent = plan.to_zones(down_parts)
    near_down = jnp.concatenate([turned_down] + zone_down, 0)
    far_down = plan.core_swap(near_down)
    near_down, far_down, active, up_proj, gate_pre, out_grad = fence(
        near_down, far_down, active, up_proj, gate_pre, out_grad
    )

    full_down = jnp.concatenate([near_down, far_down], 0)
    grad_active = jnp.dot(out_grad, full_down, preferred_element_type=jnp.float32)
    sigmoid_gate = jax.nn.sigmoid(gate_pre)
    silu_gate = gate_pre * sigmoid_gate
    grad_gate = (
        grad_active * up_proj * sigmoid_gate * (1.0 + gate_pre * (1.0 - sigmoid_gate))
    ).astype(low)
    grad_up = (grad_active * silu_gate).astype(low)
    post_send = (
        contract_cols(grad_gate[kept:], full_gate) + contract_cols(grad_up[kept:], full_up)
    ).astype(low)
    post_send, grad_gate, grad_up, normed_rows = fence(post_send, grad_gate, grad_up, normed_rows)

    post_got = plan.first_swap(post_send)
    gate_far = contract_rows(normed_rows[:, near_cols:], grad_gate).astype(low)
    post_keep = contract_cols(grad_gate[:kept], full_gate) + contract_cols(grad_up[:kept], full_up)
    post_got, gate_far, post_keep, grad_gate, grad_up, normed_rows = fence(
        post_got, gate_far, post_keep, grad_gate, grad_up, normed_rows
    )

    post_own, post_last = plan.second_swap(post_keep, post_got)
    gate_got = plan.core_swap(gate_far)
    gate_near = contract_rows(normed_rows[:, :near_cols], grad_gate)
    post_own, post_last, gate_got, gate_near, down_sent, down_parts, grad_up, normed_rows = fence(
        post_own, post_last, gate_got, gate_near, down_sent, down_parts, grad_up, normed_rows
    )

    gate_parts = zone_parts(gate_near, gate_got)
    gate_sent = plan.to_zones(gate_parts)
    grad_post = post_own + jnp.concatenate(post_last, 0).astype(jnp.float32)
    factor_post = lax.rsqrt(jnp.mean(hidden * hidden, -1, keepdims=True) + EPS_NORM)
    unit_post = hidden * factor_post
    post_gain_grad = jnp.sum(grad_post * unit_post, 0)
    own_grad = own_pick(out_grad).astype(jnp.float32)
    grad_hidden = own_grad + norm_back(grad_post * gain_post, unit_post, factor_post)
    branch_own = grad_hidden.astype(low)
    branch_got = plan.spread_first(branch_own)
    up_far = contract_rows(normed_rows[:, near_cols:], grad_up).astype(low)
    branch_own, branch_got, up_far, grad_up, normed_rows, active, grad_hidden = fence(
        branch_own, branch_got, up_far, grad_up, normed_rows, active, grad_hidden
    )

    row_part, side_part, row_got, side_got = plan.spread_second(branch_own, branch_got)
    up_got = plan.core_swap(up_far)
    up_near = contract_rows(normed_rows[:, :near_cols], grad_up)
    mlp_send = contract_cols(active[kept:], full_down).astype(low)
    row_part, side_part, row_got, side_got, up_got, up_near, mlp_send, active = fence(
        row_part, side_part, row_got, side_got, up_got, up_near, mlp_send, active
    )

    branch_rows = jnp.concatenate([row_part, side_part, row_got, side_got], 0)
    mlp_got = plan.first_swap(mlp_send)
    out_far = contract_rows(branch_rows[:, near_cols:], attended).astype(low)
    grad_att = jnp.dot(branch_rows, full_out, preferred_element_type=jnp.float32).astype(low)
    grad_att = plan.rows_natural(grad_att)
    grad_att = grad_att.reshape(seq_count, SEQ, groups, 2, head_size)
    mlp_keep = contract_cols(active[:kept], full_down)
    up_parts = zone_parts(up_near, up_got)
    mlp_got, mlp_keep, out_far, grad_att, up_parts, gate_sent, gate_parts, branch_rows = fence(
        mlp_got, mlp_keep, out_far, grad_att, up_parts, gate_sent, gate_parts, branch_rows
    )

    up_sent = plan.to_zones(up_parts)
    mlp_own, mlp_last = plan.second_swap(mlp_keep, mlp_got)
    out_got = plan.core_swap(out_far)
    out_near = contract_rows(branch_rows[:, :near_cols], attended)
    grad_query, grad_key, grad_value = attention_backward(
        shaped_query, shaped_key, shaped_value, grad_att, log_sums, SEQ
    )
    grad_query = unrotate(
        grad_query.reshape(tok_rows, groups * 2, head_size) * score_scale, cosine, sine_table
    )
    query_gain_grad = jnp.sum(grad_query * unit_q, (0, 1))
    grad_query = norm_back(grad_query * gain_q, unit_q, factor_q)
    grad_key = unrotate(grad_key.reshape(tok_rows, groups, head_size), cosine, sine_table)
    key_gain_grad = jnp.sum(grad_key * unit_k, (0, 1))
    grad_key = norm_back(grad_key * gain_k, unit_k, factor_k)
    grad_mixed = jnp.concatenate(
        [
            grad_query.reshape(tok_rows, groups, 2, head_size),
            grad_key[:, :, None],
            grad_value.reshape(tok_rows, groups, 1, head_size),
        ],
        2,
    )
    grad_mixed = grad_mixed.reshape(tok_rows, mixed_cols).astype(low)
    qkv_far = contract_rows(normed[:, near_cols:], grad_mixed).astype(low)
    mixed_rows = plan.rows_local(grad_mixed)
    normed_send = contract_cols(mixed_rows[kept:], full_qkv).astype(low)
    gain_terms = jnp.concatenate(
        [
            plan.to_natural(post_gain_grad, 0),
            query_gain_grad,
            key_gain_grad,
        ]
    )
    out_parts = zone_parts(out_near, out_got)
    qkv_far, normed_send, mixed_rows, grad_mixed, mlp_own, mlp_last, up_sent, up_parts, out_parts, gain_terms = fence(
        qkv_far,
        normed_send,
        mixed_rows,
        grad_mixed,
        mlp_own,
        mlp_last,
        up_sent,
        up_parts,
        out_parts,
        gain_terms,
    )

    normed_got = plan.first_swap(normed_send)
    qkv_got = plan.core_swap(qkv_far)
    out_sent = plan.to_zones(out_parts)
    normed_keep = contract_cols(mixed_rows[:kept], full_qkv)
    qkv_near = contract_rows(normed[:, :near_cols], grad_mixed)
    block_own = (hidden + mlp_own + jnp.concatenate(mlp_last, 0).astype(jnp.float32)).astype(low)
    qkv_parts = zone_parts(qkv_near, qkv_got)
    normed_got, normed_keep, qkv_parts, out_sent, out_parts, block_own = fence(
        normed_got, normed_keep, qkv_parts, out_sent, out_parts, block_own
    )

    qkv_sent = plan.to_zones(qkv_parts)
    normed_own, normed_last = plan.second_swap(normed_keep, normed_got)
    normed_own, normed_last, block_own, own_inputs = fence(
        normed_own, normed_last, block_own, own_inputs
    )

    grad_normed = normed_own + jnp.concatenate(normed_last, 0).astype(jnp.float32)
    own_factor = lax.rsqrt(jnp.mean(own_inputs * own_inputs, -1, keepdims=True) + EPS_NORM)
    own_unit = own_inputs * own_factor
    input_gain_grad = plan.to_natural(jnp.sum(grad_normed * own_unit, 0), 0)
    input_own = grad_hidden + norm_back(grad_normed * gain_in, own_unit, own_factor)
    input_home = plan.send_home(input_own.astype(low))
    block_home = plan.send_home(block_own)
    gain_terms = jnp.concatenate([input_gain_grad, gain_terms])
    input_home, block_home, gain_terms, qkv_sent = fence(input_home, block_home, gain_terms, qkv_sent)

    input_row = plan.row_home(input_home)
    block_row = plan.row_home(block_home)
    summed_down = plan.turn(zone_total(down_parts, down_sent)).astype(jnp.float32)
    summed_gate = plan.turn(
        jnp.stack([zone_total(gate_parts, gate_sent), zone_total(up_parts, up_sent)])
    ).astype(jnp.float32)
    summed_out = plan.turn(zone_total(out_parts, out_sent)).astype(jnp.float32)
    summed_qkv = (
        plan.turn(zone_total(qkv_parts, qkv_sent)).astype(jnp.float32).reshape(qkv_weight.shape)
    )
    summed_gains = plan.sum_everywhere(gain_terms)
    summed_gains = lax.dynamic_slice_in_dim(summed_gains, plan.index * gain_count, gain_count, 0)
    input_full, input_got = plan.share_home(input_home, input_row)
    block_full, block_got = plan.share_home(block_home, block_row)
    block_out = jnp.where(plan.home, block_full, block_got)
    input_rows = jnp.where(plan.home, input_full, input_got).astype(jnp.float32)

    qkv_moment, qkv_square, qkv_updated = adamw(
        qkv_weight, summed_qkv, qkv_first, qkv_second, RATE_QKV, DECAY_RATE
    )
    out_moment, out_square, out_updated = adamw(
        out_weight, summed_out, out_first, out_second, RATE_OUT, DECAY_RATE
    )
    gate_moment, gate_square, gate_updated = adamw(
        gate_up, summed_gate, gate_up_first, gate_up_second, RATE_GATE, DECAY_RATE
    )
    down_moment, down_square, down_updated = adamw(
        down_weight, summed_down, down_first, down_second, RATE_DOWN, DECAY_RATE
    )
    gain_moment, gain_square, gain_updated = adamw(
        gains, summed_gains, gains_first, gains_second, RATE_GAIN, 0.0
    )
    return (
        block_out,
        input_rows,
        qkv_moment,
        qkv_square,
        qkv_updated,
        out_moment,
        out_square,
        out_updated,
        gate_moment,
        gate_square,
        gate_updated,
        down_moment,
        down_square,
        down_updated,
        gain_moment,
        gain_square,
        gain_updated,
    )


def solution(mesh):
    plan = Plan(mesh)
    placed = (
        P("dp", None),
        P("dp"),
        P("dp", None),
        P("dp", "tensor", None, None),
        P("dp", "tensor", None, None),
        P("dp", "tensor", None, None),
        P("dp", "tensor"),
        P("dp", "tensor"),
        P("dp", "tensor"),
        P(None, "dp", "tensor"),
        P(None, "dp", "tensor"),
        P(None, "dp", "tensor"),
        P("dp", "tensor"),
        P("dp", "tensor"),
        P("dp", "tensor"),
        P("dp"),
        P("dp"),
        P("dp"),
    )
    return jax.shard_map(
        functools.partial(shards, plan),
        mesh=mesh,
        in_specs=placed,
        out_specs=(
            P("dp", None),
            P("dp", None),
            P("dp", "tensor", None, None),
            P("dp", "tensor", None, None),
            P("dp", "tensor", None, None),
            P("dp", "tensor"),
            P("dp", "tensor"),
            P("dp", "tensor"),
            P(None, "dp", "tensor"),
            P(None, "dp", "tensor"),
            P(None, "dp", "tensor"),
            P("dp", "tensor"),
            P("dp", "tensor"),
            P("dp", "tensor"),
            P("dp"),
            P("dp"),
            P("dp"),
        ),
        check_vma=False,
    )
```

```python
import functools
import math

import jax
import jax.numpy as jnp
from jax import lax
from jax.experimental import pallas as pl
from jax.experimental.pallas import tpu as pltpu
from jax.sharding import PartitionSpec as P

SEQ = 1024
STEP = 10


EPS_NORM = 1e-06
THETA = 1000000.0
BETA_ONE = 0.9
BETA_TWO = 0.95
ADAM_EPS = 1e-08
DECAY_RATE = 0.1
RATE_QKV = 0.05
RATE_OUT = 0.3
RATE_GATE = 0.05
RATE_DOWN = 0.03
RATE_GAIN = 1.0


def rotary(positions, head_size):
    freq_index = jnp.arange(head_size // 2, dtype=jnp.float32)
    inverse = jnp.exp(freq_index * (-2.0 * math.log(THETA) / head_size))
    angles = positions.astype(jnp.float32)[:, None] * inverse[None, :]
    cosine = jnp.cos(angles)
    sine_table = jnp.sin(angles)
    return (jnp.concatenate([cosine, cosine], -1), jnp.concatenate([sine_table, sine_table], -1))


def rotate(values, cosine, sine_table):
    half_size = values.shape[-1] // 2
    turned = jnp.concatenate([-values[..., half_size:], values[..., :half_size]], -1)
    return values * cosine[:, None, :] + turned * sine_table[:, None, :]


def unrotate(gradient, cosine, sine_table):
    half_size = gradient.shape[-1] // 2
    turned = gradient * sine_table[:, None, :]
    rotated_back = jnp.concatenate([turned[..., half_size:], -turned[..., :half_size]], -1)
    return gradient * cosine[:, None, :] + rotated_back


def norm_back(grad_unit, unit_vals, factor):
    return factor * (grad_unit - unit_vals * jnp.mean(grad_unit * unit_vals, -1, keepdims=True))


def contract_rows(left, right):
    return lax.dot_general(
        left, right, (((0,), (0,)), ((), ())), preferred_element_type=jnp.float32
    )


def contract_cols(left, right):
    return lax.dot_general(
        left, right, (((1,), (1,)), ((), ())), preferred_element_type=jnp.float32
    )


def block_scores(query_part, key_part, first_row, block_rows, last_row):
    scores = jnp.einsum(
        "nqkgd,nskd->nkgqs", query_part, key_part, preferred_element_type=jnp.float32
    )
    causal = (first_row + jnp.arange(block_rows))[:, None] >= jnp.arange(last_row)[None, :]
    return jnp.where(causal, scores, -1000000000.0)


def attention_forward(query, key_rot, values_low, seq_len):
    block_rows = min(512, seq_len)
    outputs = []
    log_sums = []
    for first_row in range(0, seq_len, block_rows):
        last_row = first_row + block_rows
        query_part = query[:, first_row:last_row]
        scores = block_scores(query_part, key_rot[:, :last_row], first_row, block_rows, last_row)
        row_max = jnp.max(scores, -1, keepdims=True)
        exponent = jnp.exp(scores - row_max)
        row_total = jnp.sum(exponent, -1, keepdims=True)
        probs_low = (exponent / row_total).astype(jnp.bfloat16)
        outputs.append(
            jnp.einsum(
                "nkgqs,nskd->nqkgd",
                probs_low,
                values_low[:, :last_row],
                preferred_element_type=jnp.float32,
            )
        )
        log_sums.append(row_max + jnp.log(row_total))
    return (jnp.concatenate(outputs, 1), log_sums)


def attention_backward(query, key_rot, values_low, grad_att, log_sums, seq_len):
    block_rows = min(512, seq_len)
    query_grads = []
    key_grad = jnp.zeros(key_rot.shape, jnp.float32)
    value_grad = jnp.zeros(values_low.shape, jnp.float32)
    for block_index, first_row in enumerate(range(0, seq_len, block_rows)):
        last_row = first_row + block_rows
        query_part = query[:, first_row:last_row]
        grad_part = grad_att[:, first_row:last_row]
        key_part = key_rot[:, :last_row]
        value_part = values_low[:, :last_row]
        scores = block_scores(query_part, key_part, first_row, block_rows, last_row)
        probs = jnp.exp(scores - log_sums[block_index])
        probs_low = probs.astype(jnp.bfloat16)
        grad_probs = jnp.einsum(
            "nqkgd,nskd->nkgqs", grad_part, value_part, preferred_element_type=jnp.float32
        )
        grad_scores = (
            probs * (grad_probs - jnp.sum(probs * grad_probs, -1, keepdims=True))
        ).astype(jnp.bfloat16)
        query_grads.append(
            jnp.einsum(
                "nkgqs,nskd->nqkgd", grad_scores, key_part, preferred_element_type=jnp.float32
            )
        )
        padding = ((0, 0), (0, seq_len - last_row), (0, 0), (0, 0))
        key_grad = key_grad + jnp.pad(
            jnp.einsum(
                "nkgqs,nqkgd->nskd", grad_scores, query_part, preferred_element_type=jnp.float32
            ),
            padding,
        )
        value_grad = value_grad + jnp.pad(
            jnp.einsum(
                "nkgqs,nqkgd->nskd", probs_low, grad_part, preferred_element_type=jnp.float32
            ),
            padding,
        )
    return (jnp.concatenate(query_grads, 1), key_grad, value_grad)


def adamw(weight, gradient, moment, second, step_rate, decay_rate):
    moment = BETA_ONE * moment + (1.0 - BETA_ONE) * gradient
    second = BETA_TWO * second + (1.0 - BETA_TWO) * gradient * gradient
    first_hat = moment / (1.0 - BETA_ONE**STEP)
    second_hat = second / (1.0 - BETA_TWO**STEP)
    weight = weight - step_rate * (
        first_hat / (jnp.sqrt(second_hat) + ADAM_EPS) + decay_rate * weight
    )
    return (moment, second, weight)


def fence(*values):
    return lax.optimization_barrier(values)


MESH = pl.DeviceIdType.MESH


def neighbours():
    index, place = lax.axis_index("dp"), lax.axis_index("tensor")
    side, row, core = lax.rem(index, 2), lax.div(place, 2), lax.rem(place, 2)
    return (
        (index, place + 2 - 4 * row),
        (index + 1 - 2 * side, place),
        (index, place + 1 - 2 * core),
    )


def greet(devices):
    barrier = pltpu.get_barrier_semaphore()
    for device in devices:
        pl.semaphore_signal(barrier, inc=1, device_id=device, device_id_type=MESH)
    pl.semaphore_wait(barrier, len(devices))


def for_rows(count, body):
    step = 32

    def one(block, carry):
        body(pl.multiple_of(block * step, step), step)
        return carry

    lax.fori_loop(0, count // step, one, 0)


class Copies:
    def __init__(self, send_sems, recv_sems):
        self.send_sems, self.recv_sems = send_sems, recv_sems
        self.all = []

    def make(self, number, source, target, device):
        return pltpu.make_async_remote_copy(
            src_ref=source,
            dst_ref=target,
            send_sem=self.send_sems.at[number],
            recv_sem=self.recv_sems.at[number],
            device_id=device,
            device_id_type=MESH,
        )

    def start(self, number, source, target, device):
        copy = self.make(number, source, target, device)
        copy.start()
        self.all.append(copy)
        return copy


def sum_eighths(copies, row_peer, side_peer, send, keep, forward, first, second, store):
    size = send.shape[0] // 4
    part = lambda ref, slot: ref.at[pl.ds(slot * size, size)]
    arrivals = [
        copies.start(0, part(send, 1), part(first, 1), row_peer),
        copies.start(1, part(send, 3), part(first, 3), side_peer),
        copies.start(2, part(send, 0), part(first, 0), row_peer),
        copies.start(3, part(send, 2), part(first, 2), side_peer),
    ]
    passed = []
    for number, slot, peer in ((0, 1, side_peer), (1, 3, row_peer)):
        arrivals[number].wait_recv()

        def add(row, count, number=number, slot=slot):
            here = pl.ds(slot * size + row, count)
            both = keep[here, :] + first[here, :].astype(jnp.float32)
            forward[pl.ds(number * size + row, count), :] = both.astype(jnp.bfloat16)

        for_rows(size, add)
        passed.append(copies.start(4 + number, part(forward, number), part(second, number), peer))
    for number, slot in ((0, 0), (1, 2)):
        arrivals[2 + number].wait_recv()
        passed[number].wait_recv()

        def total(row, count, number=number, slot=slot):
            here = pl.ds(slot * size + row, count)
            sums = keep[here, :] + first[here, :].astype(jnp.float32)
            sums = sums + second[pl.ds(number * size + row, count), :].astype(jnp.float32)
            store(number, row, count, sums)

        for_rows(size, total)
        yield number


def spread_kernel(middle, extra_count, out_count, send, keep, *refs):
    extras, refs = refs[:extra_count], refs[extra_count:]
    full, outs, refs = refs[0], refs[1 : 1 + out_count], refs[1 + out_count :]
    forward, first, second, send_sems, recv_sems = refs
    row_peer, side_peer, _ = neighbours()
    copies = Copies(send_sems, recv_sems)
    size = send.shape[0] // 4
    part = lambda slot: full.at[pl.ds(slot * size, size)]
    for out in outs:
        if out.shape[0] == 1:
            out[...] = jnp.zeros_like(out)
    greet((row_peer, side_peer))

    def store(number, row, count, sums):
        own = pl.ds(number * size + row, count)
        full[pl.ds(2 * number * size + row, count), :] = middle(own, sums, extras, outs)

    firsts, seconds = [], []
    for number in sum_eighths(
        copies, row_peer, side_peer, send, keep, forward, first, second, store
    ):
        near, other = (side_peer, row_peer) if number == 0 else (row_peer, side_peer)
        slot = 2 * number
        firsts.append(copies.start(6 + number, part(slot), part(slot + 1), near))
        seconds.append(copies.start(8 + number, part(slot), part(4 + slot), other))
    firsts[0].wait_recv()
    seconds.append(copies.start(10, part(1), part(5), row_peer))
    firsts[1].wait_recv()
    seconds.append(copies.start(11, part(3), part(7), side_peer))
    for copy in copies.all:
        copy.wait_send()
    for copy in seconds:
        copy.wait_recv()


def home_kernel(middle, extra_count, out_count, send, keep, *refs):
    extras, refs = refs[:extra_count], refs[extra_count:]
    full, outs, refs = refs[0], refs[1 : 1 + out_count], refs[1 + out_count :]
    forward, first, second, own, send_sems, recv_sems, local_sems = refs
    row_peer, side_peer, core_peer = neighbours()
    copies = Copies(send_sems, recv_sems)
    size = send.shape[0] // 4
    index, place = lax.axis_index("dp"), lax.axis_index("tensor")
    side, row, core = lax.rem(index, 2), lax.div(place, 2), lax.rem(place, 2)
    at_home = side == core
    away = side != core
    for out in outs:
        if out.shape[0] == 1:
            out[...] = jnp.zeros_like(out)
    greet((row_peer, side_peer, core_peer))

    def store(number, start, count, sums):
        here = pl.ds(number * size + start, count)
        own[here, :] = middle(here, sums, extras, outs)

    for _ in sum_eighths(copies, row_peer, side_peer, send, keep, forward, first, second, store):
        pass
    for copy in copies.all:
        copy.wait_send()

    def piece(number, x, y):
        start = (x * 2 + y) * size if number == 0 else (4 + y * 2 + x) * size
        return full.at[pl.ds(pl.multiple_of(start, size), size)]

    mine = lambda number: own.at[pl.ds(number * size, size)]
    to_side = [copies.make(6 + k, mine(k), piece(k, row, side), side_peer) for k in (0, 1)]
    from_side = [copies.make(6 + k, mine(k), piece(k, row, 1 - side), side_peer) for k in (0, 1)]
    to_row = [copies.make(8 + k, mine(k), piece(k, row, side), row_peer) for k in (0, 1)]
    pass_row = [
        copies.make(10 + k, piece(k, row, 1 - side), piece(k, row, 1 - side), row_peer)
        for k in (0, 1)
    ]
    from_row = [
        copies.make(8 + k, mine(k), piece(k, 1 - row, side), row_peer) for k in (0, 1)
    ] + [copies.make(10 + k, mine(k), piece(k, 1 - row, 1 - side), row_peer) for k in (0, 1)]
    share = []
    for number, (x, y) in enumerate(
        ((row, side), (row, 1 - side), (1 - row, side), (1 - row, 1 - side))
    ):
        for k in (0, 1):
            source = mine(k) if number == 0 else piece(k, x, y)
            share.append(copies.make(12 + 2 * number + k, source, piece(k, x, y), core_peer))

    @pl.when(away)
    def _():
        for copy in to_side:
            copy.start()
        for copy in to_side:
            copy.wait_send()
        for copy in share:
            copy.wait_recv()

    @pl.when(at_home)
    def _():
        kept = [
            pltpu.make_async_copy(mine(k), piece(k, row, side), local_sems.at[k]) for k in (0, 1)
        ]
        for copy in to_row + kept + share[:2]:
            copy.start()
        for k in (0, 1):
            from_side[k].wait_recv()
            pass_row[k].start()
            share[2 + k].start()
        for k in range(4):
            from_row[k].wait_recv()
            share[4 + k].start()
        for copy in to_row + pass_row + share:
            copy.wait_send()
        for copy in kept:
            copy.wait()


def sum_rows(kernel, middle, send, keep, extras, outs, number):
    half, width = send.shape
    eighth = half // 4
    low = jnp.bfloat16
    vmem = pl.BlockSpec(memory_space=pltpu.VMEM)
    scratch = [
        pltpu.VMEM((2 * eighth, width), low),
        pltpu.VMEM((half, width), low),
        pltpu.VMEM((2 * eighth, width), low),
    ]
    if kernel is home_kernel:
        scratch.append(pltpu.VMEM((2 * eighth, width), low))
    copies = 12 if kernel is spread_kernel else 20
    scratch += [pltpu.SemaphoreType.DMA((copies,)), pltpu.SemaphoreType.DMA((copies,))]
    if kernel is home_kernel:
        scratch.append(pltpu.SemaphoreType.DMA((2,)))
    return pl.pallas_call(
        functools.partial(kernel, middle, len(extras), len(outs)),
        out_shape=[jax.ShapeDtypeStruct((2 * half, width), low)] + outs,
        in_specs=[vmem] * (2 + len(extras)),
        out_specs=[vmem] * (1 + len(outs)),
        scratch_shapes=scratch,
        compiler_params=pltpu.CompilerParams(
            collective_id=number, has_side_effects=True, vmem_limit_bytes=48 * 2**20
        ),
        cost_estimate=pl.CostEstimate(
            flops=4 * 10**10, bytes_accessed=10**8, transcendentals=0
        ),
        name=middle.__name__,
    )(send, keep, *extras)


def inverse_rms(values):
    return lax.rsqrt(jnp.mean(values * values, -1, keepdims=True) + EPS_NORM)


def hidden_rows(own, sums, extras, outs):
    tokens, gain = extras
    hidden = tokens[own, :].astype(jnp.float32) + sums
    outs[0][own, :] = hidden
    return (hidden * inverse_rms(hidden) * gain[...]).astype(jnp.bfloat16)


def grad_hidden_rows(own, sums, extras, outs):
    hidden, out_grad, gain = extras
    values = hidden[own, :]
    factor = inverse_rms(values)
    unit = values * factor
    outs[1][...] += jnp.sum(sums * unit, 0, keepdims=True)
    grad = out_grad[own, :].astype(jnp.float32) + norm_back(sums * gain[...], unit, factor)
    outs[0][own, :] = grad
    return grad.astype(jnp.bfloat16)


def grad_input_rows(own, sums, extras, outs):
    tokens, grad_hidden, gain = extras
    values = tokens[own, :].astype(jnp.float32)
    factor = inverse_rms(values)
    unit = values * factor
    outs[0][...] += jnp.sum(sums * unit, 0, keepdims=True)
    return (grad_hidden[own, :] + norm_back(sums * gain[...], unit, factor)).astype(jnp.bfloat16)


class Plan:
    def __init__(self, mesh):
        self.total = mesh.shape["dp"]
        self.zones = self.total // 2
        self.tensor = mesh.shape["tensor"]

    def place(self):
        self.index = lax.axis_index("dp")
        self.zone = self.index // 2
        self.side = self.index % 2
        self.row = lax.axis_index("tensor") // 2
        self.core = lax.axis_index("tensor") % 2
        self.home = self.side == self.core

    def move(self, value, target):
        pairs = []
        for d in range(self.total):
            for t in range(self.tensor):
                to = target(d // 2, d % 2, t // 2, t % 2)
                if to is not None:
                    zone, side, row, core = to
                    pairs.append((d * self.tensor + t, (zone * 2 + side) * self.tensor + row * 2 + core))
        return lax.ppermute(value, ("dp", "tensor"), pairs)

    def turn(self, value):
        got = self.move(value, lambda z, y, x, c: (z, c, x, y) if y != c else None)
        return jnp.where(self.home, value, got)

    def zone_shift(self, value, shift):
        return self.move(value, lambda z, y, x, c: ((z + shift) % self.zones, y, x, c))

    def zone_flip(self, value, bit):
        return self.move(value, lambda z, y, x, c: (z ^ bit, y, x, c))

    def core_swap(self, value):
        return self.move(value, lambda z, y, x, c: (z, y, x, 1 - c))

    def side_swap(self, value):
        return self.move(value, lambda z, y, x, c: (z, 1 - y, x, c))

    def row_swap(self, value):
        return self.move(value, lambda z, y, x, c: (z, y, 1 - x, c))

    def to_local(self, value, axis):
        width = value.shape[axis] // self.total
        parts = []
        for core in (self.core, 1 - self.core):
            for slot in range(self.zones):
                owner = ((self.zone + slot) % self.zones) * 2 + core
                parts.append(lax.dynamic_slice_in_dim(value, owner * width, width, axis))
        return jnp.concatenate(parts, axis)

    def to_natural(self, value, axis, core=None):
        core = self.core if core is None else core
        width = value.shape[axis] // self.total
        parts = []
        for block in range(self.total):
            slot = (block // 2 - self.zone) % self.zones
            slot = slot + jnp.where(block % 2 == core, 0, self.zones)
            parts.append(lax.dynamic_slice_in_dim(value, slot * width, width, axis))
        return jnp.concatenate(parts, axis)

    def row_owners(self):
        own, off = (self.row, self.side), (1 - self.row, 1 - self.side)
        first = lambda x, y: x * 2 + y
        second = lambda x, y: 4 + y * 2 + x
        return [
            first(own[0], own[1]),
            first(own[0], off[1]),
            second(own[0], own[1]),
            second(off[0], own[1]),
            first(off[0], own[1]),
            first(off[0], off[1]),
            second(own[0], off[1]),
            second(off[0], off[1]),
        ]

    def rows_local(self, value, slots=range(8)):
        size = value.shape[0] // 8
        owners = self.row_owners()
        return jnp.concatenate(
            [lax.dynamic_slice_in_dim(value, owners[slot] * size, size, 0) for slot in slots], 0
        )

    def rows_natural(self, value, order=range(8)):
        size = value.shape[0] // 8
        place = [list(order).index(slot) for slot in range(8)]
        parts = []
        for piece in range(8):
            x, y = (piece // 2, piece % 2) if piece < 4 else (piece % 2, (piece - 4) // 2)
            slots = (0, 1, 4, 5) if piece < 4 else (2, 6, 3, 7)
            same_x, same_y = x == self.row, y == self.side
            slot = jnp.where(
                same_x,
                jnp.where(same_y, place[slots[0]], place[slots[1]]),
                jnp.where(same_y, place[slots[2]], place[slots[3]]),
            )
            parts.append(lax.dynamic_slice_in_dim(value, slot * size, size, 0))
        return jnp.concatenate(parts, 0)

    def odd_shifts(self):
        return [shift for shift in range(1, self.zones) if shift % 2]

    def even_shifts(self):
        return [shift for shift in range(1, self.zones) if not shift % 2]

    def from_zones(self, shard, shifts=None):
        shifts = range(1, self.zones) if shifts is None else shifts
        return {shift: self.zone_shift(shard, -shift) for shift in shifts}

    def near(self, shard, *got, axis=0):
        parts = {0: shard}
        for group in got:
            parts.update(group)
        return jnp.concatenate([parts[slot] for slot in range(self.zones)], axis)

    def to_zones(self, parts, shifts=None):
        shifts = range(1, self.zones) if shifts is None else shifts
        return [self.zone_shift(parts[shift], shift) for shift in shifts]

    def first_swap(self, send):
        half = send.shape[0] // 2
        return self.row_swap(send[:half]), self.side_swap(send[half:])

    def second_swap(self, keep, got):
        quarter = keep.shape[0] // 4
        row_part = keep[: 2 * quarter] + got[0].astype(jnp.float32)
        side_part = keep[2 * quarter :] + got[1].astype(jnp.float32)
        own = jnp.concatenate([row_part[:quarter], side_part[:quarter]], 0)
        return own, (
            self.side_swap(row_part[quarter:].astype(jnp.bfloat16)),
            self.row_swap(side_part[quarter:].astype(jnp.bfloat16)),
        )

    def spread_first(self, own):
        half = own.shape[0] // 2
        return (self.side_swap(own[:half]), self.row_swap(own[half:]))

    def spread_second(self, own, got):
        half = own.shape[0] // 2
        row_part = jnp.concatenate([own[:half], got[0]], 0)
        side_part = jnp.concatenate([own[half:], got[1]], 0)
        return row_part, side_part, self.row_swap(row_part), self.side_swap(side_part)

    def send_home(self, own):
        to_home = lambda z, y, x, c: (z, c, x, c) if y != c else None
        return jnp.concatenate([own, self.move(own, to_home)], 0)

    def row_home(self, part):
        return self.move(part, lambda z, y, x, c: (z, y, 1 - x, c) if y == c else None)

    def share_home(self, part, other):
        full = jnp.concatenate([part, other], 0)
        full = self.to_natural(self.rows_natural(full, (0, 2, 1, 6, 4, 3, 5, 7)), 1)
        got = self.move(full, lambda z, y, x, c: (z, y, x, 1 - c) if y == c else None)
        return full, got

    def sum_everywhere(self, value):
        value = value + self.row_swap(value)
        value = value + self.side_swap(value)
        value = value + self.core_swap(value)
        bit = 1
        while bit < self.zones:
            value = value + self.zone_flip(value, bit)
            bit *= 2
        return value


def shards(
    plan,
    tokens,
    positions,
    out_grad,
    qkv_weight,
    qkv_first,
    qkv_second,
    out_weight,
    out_first,
    out_second,
    gate_up,
    gate_up_first,
    gate_up_second,
    down_weight,
    down_first,
    down_second,
    gains,
    gains_first,
    gains_second,
):
    plan.place()
    low = jnp.bfloat16
    tok_rows, model_width = tokens.shape
    groups = qkv_weight.shape[1]
    head_size = qkv_weight.shape[3]
    shard_rows = qkv_weight.shape[0]
    seq_count = tok_rows // SEQ
    mixed_cols = groups * 4 * head_size
    near_cols = model_width // 2
    kept = tok_rows // 2
    gain_count = gains.shape[0]

    gain_rows = 16
    gain_block = jnp.pad(gains.astype(low), (0, mixed_cols - gain_count))
    low_qkv = jnp.concatenate(
        [
            qkv_weight.reshape(shard_rows, mixed_cols).astype(low),
            jnp.broadcast_to(gain_block, (gain_rows, mixed_cols)),
        ],
        0,
    )
    turned_qkv = plan.turn(low_qkv)
    tokens = plan.turn(tokens)
    positions = plan.turn(positions.astype(jnp.float32))
    turned_out = plan.turn(out_weight.astype(low))
    turned_qkv, turned_out, low_gate, low_down = fence(
        turned_qkv, turned_out, gate_up.astype(low), down_weight.astype(low)
    )

    zone_qkv = plan.from_zones(turned_qkv)
    turned_gate = plan.turn(low_gate)
    zone_qkv, tokens, positions, turned_gate, turned_out, turned_qkv, low_down, out_grad = fence(
        zone_qkv, tokens, positions, turned_gate, turned_out, turned_qkv, low_down, out_grad
    )

    near_qkv = jnp.stack([turned_qkv] + [zone_qkv[shift] for shift in range(1, plan.zones)])
    far_qkv = plan.core_swap(near_qkv)
    zone_out = plan.from_zones(turned_out)
    turned_down = plan.turn(low_down)
    tokens = plan.to_local(tokens, 1)
    inputs = tokens.astype(jnp.float32)
    factor_in = lax.rsqrt(jnp.mean(inputs * inputs, -1, keepdims=True) + EPS_NORM)
    cosine, sine_table = rotary(positions, head_size)
    near_qkv, far_qkv, zone_out, turned_out, tokens, factor_in, cosine, sine_table = fence(
        near_qkv, far_qkv, zone_out, turned_out, tokens, factor_in, cosine, sine_table
    )
    turned_gate, turned_down, out_grad = fence(turned_gate, turned_down, out_grad)

    near_out = plan.near(turned_out, zone_out)
    far_out = plan.core_swap(near_out)
    odd_gate = plan.from_zones(turned_gate, plan.odd_shifts()[:1])
    out_grad = plan.turn(out_grad)
    both_qkv = jnp.concatenate([near_qkv, far_qkv], 0)
    full_qkv = both_qkv[:, :shard_rows].reshape(model_width, mixed_cols)
    gain_slots = both_qkv[:, shard_rows, :gain_count]
    gain_all = plan.to_natural(gain_slots.reshape(-1), 0).astype(jnp.float32)
    gain_in = plan.to_local(gain_all[:model_width], 0)
    gain_post = plan.to_local(gain_all[model_width : 2 * model_width], 0)
    gain_q = gain_all[2 * model_width : 2 * model_width + head_size]
    gain_k = gain_all[2 * model_width + head_size :]
    inputs = tokens.astype(jnp.float32)
    normed = (inputs * factor_in * gain_in).astype(low)
    mixed_proj = jnp.dot(normed, full_qkv, preferred_element_type=jnp.float32).reshape(
        tok_rows, groups, 4, head_size
    )
    query_raw = mixed_proj[:, :, :2].reshape(tok_rows, groups * 2, head_size)
    key_raw = mixed_proj[:, :, 2]
    values_low = mixed_proj[:, :, 3].astype(low)
    score_scale = 1.0 / math.sqrt(head_size)
    factor_q = lax.rsqrt(jnp.mean(query_raw * query_raw, -1, keepdims=True) + EPS_NORM)
    unit_q = query_raw * factor_q
    query = (rotate(unit_q * gain_q, cosine, sine_table) * score_scale).astype(low)
    factor_k = lax.rsqrt(jnp.mean(key_raw * key_raw, -1, keepdims=True) + EPS_NORM)
    unit_k = key_raw * factor_k
    key_rot = rotate(unit_k * gain_k, cosine, sine_table).astype(low)
    shaped_query = query.reshape(seq_count, SEQ, groups, 2, head_size)
    shaped_key = key_rot.reshape(seq_count, SEQ, groups, head_size)
    shaped_value = values_low.reshape(seq_count, SEQ, groups, head_size)
    attended, log_sums = attention_forward(shaped_query, shaped_key, shaped_value, SEQ)
    attended = attended.reshape(tok_rows, groups * 2 * head_size).astype(low)
    attended = plan.rows_local(attended)
    own_tokens = plan.rows_local(tokens, (0, 2))
    attended, near_out, far_out, odd_gate, turned_gate, turned_down, own_tokens, out_grad = fence(
        attended, near_out, far_out, odd_gate, turned_gate, turned_down, own_tokens, out_grad
    )

    full_out = jnp.concatenate([near_out, far_out], 0)
    rest_gate = plan.from_zones(turned_gate, plan.odd_shifts()[1:] + plan.even_shifts())
    branch_send = contract_cols(attended[kept:], full_out).astype(low)
    branch_keep = contract_cols(attended[:kept], full_out)
    normed_rows, hidden = sum_rows(
        spread_kernel,
        hidden_rows,
        branch_send,
        branch_keep,
        [own_tokens, gain_post[None]],
        [jax.ShapeDtypeStruct((tok_rows // 4, model_width), jnp.float32)],
        0,
    )
    normed_rows, hidden, odd_gate, rest_gate, turned_gate, turned_down, out_grad = fence(
        normed_rows, hidden, odd_gate, rest_gate, turned_gate, turned_down, out_grad
    )

    near_gate = plan.near(turned_gate, odd_gate, rest_gate, axis=1)
    far_gate = plan.core_swap(near_gate)
    odd_down = plan.from_zones(turned_down, plan.odd_shifts())
    out_grad = plan.to_local(plan.rows_local(out_grad), 1)
    full_gate = jnp.concatenate([near_gate, far_gate], 1)
    gate_pre = jnp.dot(normed_rows, full_gate[0], preferred_element_type=jnp.float32)
    up_proj = jnp.dot(normed_rows, full_gate[1], preferred_element_type=jnp.float32)
    sigmoid_gate = jax.nn.sigmoid(gate_pre)
    silu_gate = gate_pre * sigmoid_gate
    active = (silu_gate * up_proj).astype(low)
    down_far = contract_rows(out_grad[:, near_cols:], active).astype(low)
    down_far, active, up_proj, gate_pre, out_grad, odd_down, turned_down, normed_rows = fence(
        down_far, active, up_proj, gate_pre, out_grad, odd_down, turned_down, normed_rows
    )

    even_down = plan.from_zones(turned_down, plan.even_shifts())
    down_got = plan.core_swap(down_far)
    down_near = contract_rows(out_grad[:, :near_cols], active)

    def zone_parts(near, got, axis=0):
        both = (near + got.astype(jnp.float32)).astype(low)
        return jnp.split(both, plan.zones, axis)

    def zone_total(parts, *arrived):
        total = parts[0].astype(jnp.float32)
        for part in sum(arrived, []):
            total = total + part.astype(jnp.float32)
        return total.astype(low)

    down_parts = zone_parts(down_near, down_got)
    down_parts, odd_down, even_down, turned_down, active, up_proj, gate_pre, out_grad = fence(
        down_parts, odd_down, even_down, turned_down, active, up_proj, gate_pre, out_grad
    )

    near_down = plan.near(turned_down, odd_down, even_down)
    far_down = plan.core_swap(near_down)
    first_shift = plan.odd_shifts()[:1]
    down_sent = plan.to_zones(down_parts, plan.odd_shifts())
    full_down = jnp.concatenate([near_down, far_down], 0)
    grad_active = jnp.dot(out_grad, full_down, preferred_element_type=jnp.float32)
    sigmoid_gate = jax.nn.sigmoid(gate_pre)
    silu_gate = gate_pre * sigmoid_gate
    grad_gate = (
        grad_active * up_proj * sigmoid_gate * (1.0 + gate_pre * (1.0 - sigmoid_gate))
    ).astype(low)
    grad_up = (grad_active * silu_gate).astype(low)

    def gate_terms(rows):
        return jnp.stack([contract_rows(rows, grad_gate), contract_rows(rows, grad_up)])

    gate_far = gate_terms(normed_rows[:, near_cols:]).astype(low)
    gate_far, grad_gate, grad_up, normed_rows, down_sent, down_parts, full_down = fence(
        gate_far, grad_gate, grad_up, normed_rows, down_sent, down_parts, full_down
    )

    gate_got = plan.core_swap(gate_far)
    post_send = (
        contract_cols(grad_gate[kept:], full_gate[0]) + contract_cols(grad_up[kept:], full_gate[1])
    ).astype(low)
    post_keep = contract_cols(grad_gate[:kept], full_gate[0]) + contract_cols(
        grad_up[:kept], full_gate[1]
    )
    gate_near = gate_terms(normed_rows[:, :near_cols])
    gate_parts = zone_parts(gate_near, gate_got, 1)
    post_send, post_keep, gate_parts, down_parts, out_grad = fence(
        post_send, post_keep, gate_parts, down_parts, out_grad
    )

    down_last = plan.to_zones(down_parts, plan.even_shifts())
    gate_sent = plan.to_zones(gate_parts, first_shift)
    eighth = tok_rows // 8
    own_grad = jnp.concatenate([out_grad[:eighth], out_grad[2 * eighth : 3 * eighth]], 0)
    branch_rows, grad_hidden, post_gain_grad = sum_rows(
        spread_kernel,
        grad_hidden_rows,
        post_send,
        post_keep,
        [hidden, own_grad, gain_post[None]],
        [
            jax.ShapeDtypeStruct((tok_rows // 4, model_width), jnp.float32),
            jax.ShapeDtypeStruct((1, model_width), jnp.float32),
        ],
        1,
    )
    branch_rows, grad_hidden, post_gain_grad, down_last, gate_sent, gate_parts, active, hidden = fence(
        branch_rows, grad_hidden, post_gain_grad, down_last, gate_sent, gate_parts, active, hidden
    )

    gate_next = plan.to_zones(gate_parts, plan.odd_shifts()[1:])
    mlp_send = contract_cols(active[kept:], full_down).astype(low)
    mlp_keep = contract_cols(active[:kept], full_down)
    mlp_got = plan.first_swap(mlp_send)
    out_far = contract_rows(branch_rows[:, near_cols:], attended).astype(low)
    out_got = plan.core_swap(out_far)
    grad_att = jnp.dot(branch_rows, full_out, preferred_element_type=jnp.float32).astype(low)
    grad_att = plan.rows_natural(grad_att)
    grad_att = grad_att.reshape(seq_count, SEQ, groups, 2, head_size)
    grad_att, mlp_got, mlp_keep, gate_next, out_got, branch_rows, gate_parts = fence(
        grad_att, mlp_got, mlp_keep, gate_next, out_got, branch_rows, gate_parts
    )
    gate_last = plan.to_zones(gate_parts, plan.even_shifts())
    grad_query, grad_key, grad_value = attention_backward(
        shaped_query, shaped_key, shaped_value, grad_att, log_sums, SEQ
    )
    grad_query = unrotate(
        grad_query.reshape(tok_rows, groups * 2, head_size) * score_scale, cosine, sine_table
    )
    query_gain_grad = jnp.sum(grad_query * unit_q, (0, 1))
    grad_query = norm_back(grad_query * gain_q, unit_q, factor_q)
    grad_key = unrotate(grad_key.reshape(tok_rows, groups, head_size), cosine, sine_table)
    key_gain_grad = jnp.sum(grad_key * unit_k, (0, 1))
    grad_key = norm_back(grad_key * gain_k, unit_k, factor_k)
    grad_mixed = jnp.concatenate(
        [
            grad_query.reshape(tok_rows, groups, 2, head_size),
            grad_key[:, :, None],
            grad_value.reshape(tok_rows, groups, 1, head_size),
        ],
        2,
    )
    grad_mixed = grad_mixed.reshape(tok_rows, mixed_cols).astype(low)
    out_parts = zone_parts(contract_rows(branch_rows[:, :near_cols], attended), out_got)
    gain_terms = jnp.concatenate(
        [plan.to_natural(post_gain_grad[0], 0), query_gain_grad, key_gain_grad]
    )
    grad_mixed, mlp_got, mlp_keep, gate_last, out_parts, gain_terms, normed = fence(
        grad_mixed, mlp_got, mlp_keep, gate_last, out_parts, gain_terms, normed
    )

    mlp_own, mlp_last = plan.second_swap(mlp_keep, mlp_got)
    out_sent = plan.to_zones(out_parts)
    qkv_far = contract_rows(normed[:, near_cols:], grad_mixed).astype(low)
    qkv_got = plan.core_swap(qkv_far)
    mixed_rows = plan.rows_local(grad_mixed)
    normed_send = contract_cols(mixed_rows[kept:], full_qkv).astype(low)
    normed_keep = contract_cols(mixed_rows[:kept], full_qkv)
    qkv_parts = zone_parts(contract_rows(normed[:, :near_cols], grad_mixed), qkv_got)
    block_own = (hidden + mlp_own + jnp.concatenate(mlp_last, 0).astype(jnp.float32)).astype(low)
    block_own, qkv_parts, normed_send, normed_keep, out_sent, out_parts = fence(
        block_own, qkv_parts, normed_send, normed_keep, out_sent, out_parts
    )

    qkv_sent = plan.to_zones(qkv_parts)
    block_home = plan.send_home(block_own)
    input_full, input_gain_grad = sum_rows(
        home_kernel,
        grad_input_rows,
        normed_send,
        normed_keep,
        [own_tokens, grad_hidden, gain_in[None]],
        [jax.ShapeDtypeStruct((1, model_width), jnp.float32)],
        2,
    )
    summed_down = plan.turn(zone_total(down_parts, down_sent, down_last)).astype(jnp.float32)
    gain_terms = jnp.concatenate([plan.to_natural(input_gain_grad[0], 0), gain_terms])
    input_full, gain_terms, qkv_sent, qkv_parts, block_home, summed_down = fence(
        input_full, gain_terms, qkv_sent, qkv_parts, block_home, summed_down
    )

    block_row = plan.row_home(block_home)
    summed_gate = plan.turn(zone_total(gate_parts, gate_sent, gate_next, gate_last)).astype(jnp.float32)
    summed_out = plan.turn(zone_total(out_parts, out_sent)).astype(jnp.float32)
    summed_qkv = (
        plan.turn(zone_total(qkv_parts, qkv_sent)).astype(jnp.float32).reshape(qkv_weight.shape)
    )
    summed_gains = plan.sum_everywhere(gain_terms)
    summed_gains = lax.dynamic_slice_in_dim(summed_gains, plan.index * gain_count, gain_count, 0)
    block_full, block_got = plan.share_home(block_home, block_row)
    block_out = jnp.where(plan.home, block_full, block_got)
    input_rows = plan.to_natural(input_full, 1, plan.side).astype(jnp.float32)

    qkv_moment, qkv_square, qkv_updated = adamw(
        qkv_weight, summed_qkv, qkv_first, qkv_second, RATE_QKV, DECAY_RATE
    )
    out_moment, out_square, out_updated = adamw(
        out_weight, summed_out, out_first, out_second, RATE_OUT, DECAY_RATE
    )
    gate_moment, gate_square, gate_updated = adamw(
        gate_up, summed_gate, gate_up_first, gate_up_second, RATE_GATE, DECAY_RATE
    )
    down_moment, down_square, down_updated = adamw(
        down_weight, summed_down, down_first, down_second, RATE_DOWN, DECAY_RATE
    )
    gain_moment, gain_square, gain_updated = adamw(
        gains, summed_gains, gains_first, gains_second, RATE_GAIN, 0.0
    )
    return (
        block_out,
        input_rows,
        qkv_moment,
        qkv_square,
        qkv_updated,
        out_moment,
        out_square,
        out_updated,
        gate_moment,
        gate_square,
        gate_updated,
        down_moment,
        down_square,
        down_updated,
        gain_moment,
        gain_square,
        gain_updated,
    )


def solution(mesh):
    plan = Plan(mesh)
    placed = (
        P("dp", None),
        P("dp"),
        P("dp", None),
        P("dp", "tensor", None, None),
        P("dp", "tensor", None, None),
        P("dp", "tensor", None, None),
        P("dp", "tensor"),
        P("dp", "tensor"),
        P("dp", "tensor"),
        P(None, "dp", "tensor"),
        P(None, "dp", "tensor"),
        P(None, "dp", "tensor"),
        P("dp", "tensor"),
        P("dp", "tensor"),
        P("dp", "tensor"),
        P("dp"),
        P("dp"),
        P("dp"),
    )
    return jax.shard_map(
        functools.partial(shards, plan),
        mesh=mesh,
        in_specs=placed,
        out_specs=(
            P("dp", None),
            P("dp", None),
            P("dp", "tensor", None, None),
            P("dp", "tensor", None, None),
            P("dp", "tensor", None, None),
            P("dp", "tensor"),
            P("dp", "tensor"),
            P("dp", "tensor"),
            P(None, "dp", "tensor"),
            P(None, "dp", "tensor"),
            P(None, "dp", "tensor"),
            P("dp", "tensor"),
            P("dp", "tensor"),
            P("dp", "tensor"),
            P("dp"),
            P("dp"),
            P("dp"),
        ),
        check_vma=False,
    )
```

```python
import functools
import math

import jax
import jax.numpy as jnp
from jax import lax
from jax.experimental import pallas as pl
from jax.experimental.pallas import tpu as pltpu
from jax.sharding import PartitionSpec as P

SEQ = 1024
STEP = 10


EPS_NORM = 1e-06
THETA = 1000000.0
BETA_ONE = 0.9
BETA_TWO = 0.95
ADAM_EPS = 1e-08
DECAY_RATE = 0.1
RATE_QKV = 0.05
RATE_OUT = 0.3
RATE_GATE = 0.05
RATE_DOWN = 0.03
RATE_GAIN = 1.0


def rotary(positions, head_size):
    freq_index = jnp.arange(head_size // 2, dtype=jnp.float32)
    inverse = jnp.exp(freq_index * (-2.0 * math.log(THETA) / head_size))
    angles = positions.astype(jnp.float32)[:, None] * inverse[None, :]
    cosine = jnp.cos(angles)
    sine_table = jnp.sin(angles)
    return (jnp.concatenate([cosine, cosine], -1), jnp.concatenate([sine_table, sine_table], -1))


def rotate(values, cosine, sine_table):
    half_size = values.shape[-1] // 2
    turned = jnp.concatenate([-values[..., half_size:], values[..., :half_size]], -1)
    return values * cosine[:, None, :] + turned * sine_table[:, None, :]


def unrotate(gradient, cosine, sine_table):
    half_size = gradient.shape[-1] // 2
    turned = gradient * sine_table[:, None, :]
    rotated_back = jnp.concatenate([turned[..., half_size:], -turned[..., :half_size]], -1)
    return gradient * cosine[:, None, :] + rotated_back


def norm_back(grad_unit, unit_vals, factor):
    return factor * (grad_unit - unit_vals * jnp.mean(grad_unit * unit_vals, -1, keepdims=True))


def contract_rows(left, right):
    return lax.dot_general(
        left, right, (((0,), (0,)), ((), ())), preferred_element_type=jnp.float32
    )


def contract_cols(left, right):
    return lax.dot_general(
        left, right, (((1,), (1,)), ((), ())), preferred_element_type=jnp.float32
    )


def block_scores(query_part, key_part, first_row, block_rows, last_row):
    scores = jnp.einsum(
        "nqkgd,nskd->nkgqs", query_part, key_part, preferred_element_type=jnp.float32
    )
    causal = (first_row + jnp.arange(block_rows))[:, None] >= jnp.arange(last_row)[None, :]
    return jnp.where(causal, scores, -1000000000.0)


def attention_forward(query, key_rot, values_low, seq_len):
    block_rows = min(512, seq_len)
    outputs = []
    log_sums = []
    for first_row in range(0, seq_len, block_rows):
        last_row = first_row + block_rows
        query_part = query[:, first_row:last_row]
        scores = block_scores(query_part, key_rot[:, :last_row], first_row, block_rows, last_row)
        row_max = jnp.max(scores, -1, keepdims=True)
        exponent = jnp.exp(scores - row_max)
        row_total = jnp.sum(exponent, -1, keepdims=True)
        probs_low = (exponent / row_total).astype(jnp.bfloat16)
        outputs.append(
            jnp.einsum(
                "nkgqs,nskd->nqkgd",
                probs_low,
                values_low[:, :last_row],
                preferred_element_type=jnp.float32,
            )
        )
        log_sums.append(row_max + jnp.log(row_total))
    return (jnp.concatenate(outputs, 1), log_sums)


def attention_backward(query, key_rot, values_low, grad_att, log_sums, seq_len):
    block_rows = min(512, seq_len)
    query_grads = []
    key_grad = jnp.zeros(key_rot.shape, jnp.float32)
    value_grad = jnp.zeros(values_low.shape, jnp.float32)
    for block_index, first_row in enumerate(range(0, seq_len, block_rows)):
        last_row = first_row + block_rows
        query_part = query[:, first_row:last_row]
        grad_part = grad_att[:, first_row:last_row]
        key_part = key_rot[:, :last_row]
        value_part = values_low[:, :last_row]
        scores = block_scores(query_part, key_part, first_row, block_rows, last_row)
        probs = jnp.exp(scores - log_sums[block_index])
        probs_low = probs.astype(jnp.bfloat16)
        grad_probs = jnp.einsum(
            "nqkgd,nskd->nkgqs", grad_part, value_part, preferred_element_type=jnp.float32
        )
        grad_scores = (
            probs * (grad_probs - jnp.sum(probs * grad_probs, -1, keepdims=True))
        ).astype(jnp.bfloat16)
        query_grads.append(
            jnp.einsum(
                "nkgqs,nskd->nqkgd", grad_scores, key_part, preferred_element_type=jnp.float32
            )
        )
        padding = ((0, 0), (0, seq_len - last_row), (0, 0), (0, 0))
        key_grad = key_grad + jnp.pad(
            jnp.einsum(
                "nkgqs,nqkgd->nskd", grad_scores, query_part, preferred_element_type=jnp.float32
            ),
            padding,
        )
        value_grad = value_grad + jnp.pad(
            jnp.einsum(
                "nkgqs,nqkgd->nskd", probs_low, grad_part, preferred_element_type=jnp.float32
            ),
            padding,
        )
    return (jnp.concatenate(query_grads, 1), key_grad, value_grad)


def adamw(weight, gradient, moment, second, step_rate, decay_rate):
    moment = BETA_ONE * moment + (1.0 - BETA_ONE) * gradient
    second = BETA_TWO * second + (1.0 - BETA_TWO) * gradient * gradient
    first_hat = moment / (1.0 - BETA_ONE**STEP)
    second_hat = second / (1.0 - BETA_TWO**STEP)
    weight = weight - step_rate * (
        first_hat / (jnp.sqrt(second_hat) + ADAM_EPS) + decay_rate * weight
    )
    return (moment, second, weight)


def fence(*values):
    return lax.optimization_barrier(values)


MESH = pl.DeviceIdType.MESH
HEAD = 128


def place_here():
    index, place = lax.axis_index("dp"), lax.axis_index("tensor")
    return lax.div(index, 2), lax.rem(index, 2), lax.div(place, 2), lax.rem(place, 2)


def device(zone, side, row, core):
    return (zone * 2 + side, row * 2 + core)


def flipped(zone, flip):
    bit = 1
    while bit <= flip:
        if flip & bit:
            zone = zone + bit - 2 * bit * lax.rem(lax.div(zone, bit), 2)
        bit *= 2
    return zone


def greet(devices, amount=None):
    barrier = pltpu.get_barrier_semaphore()
    for peer in devices:
        pl.semaphore_signal(barrier, inc=1, device_id=peer, device_id_type=MESH)
    pl.semaphore_wait(barrier, len(devices) if amount is None else amount)


def for_rows(count, body):
    step = 32

    def one(block, carry):
        body(pl.multiple_of(block * step, step), step)
        return carry

    lax.fori_loop(0, count // step, one, 0)


class Copies:
    def __init__(self, send_sems, recv_sems):
        self.send_sems, self.recv_sems = send_sems, recv_sems
        self.number = 0

    def make(self, source, target, peer):
        number, self.number = self.number, self.number + 1
        return pltpu.make_async_remote_copy(
            src_ref=source,
            dst_ref=target,
            send_sem=self.send_sems.at[number],
            recv_sem=self.recv_sems.at[number],
            device_id=peer,
            device_id_type=MESH,
        )

    def start(self, source, target, peer):
        copy = self.make(source, target, peer)
        copy.start()
        return copy


class GainSum:
    def __init__(self, plan, rest, width):
        self.plan, self.width = plan, width
        self.total = width + rest
        self.scratch = [
            pltpu.VMEM((8, 1, self.total), jnp.float32),
            pltpu.VMEM((plan.zones, 1, self.total), jnp.float32),
        ]
        self.output = jax.ShapeDtypeStruct((1, self.total), jnp.float32)
        self.count = 7 + plan.zones - 1

    def plane_peers(self, zone, side, row, core):
        steps = [(s, r, c) for s in range(2) for r in range(2) for c in range(2)][1:]
        turn = lambda value, step: 1 - value if step else value
        return [device(zone, turn(side, s), turn(row, r), turn(core, c)) for s, r, c in steps]

    def zone_peers(self, zone, side, row, core):
        return {flip: device(flipped(zone, flip), side, row, core) for flip in self.plan.flips[1:]}

    def start(self, copies, rest, blocks, plane_sums, zone_sums):
        zone, side, row, core = place_here()
        plan = self.plan
        size = self.width // plan.total
        self.copies, self.plane_sums, self.zone_sums, self.zone = copies, plane_sums, zone_sums, zone
        here = side * 4 + row * 2 + core
        plane_sums[here, :, pl.ds(self.width, self.total - self.width)] = rest[...]
        for slot in range(plan.total):
            owner = flipped(zone, plan.flips[slot % plan.zones]) * 2
            owner = owner + (core if slot < plan.zones else 1 - core)
            spot = pl.ds(pl.multiple_of(owner * size, size), size)
            plane_sums[here, :, spot] = blocks[:, pl.ds(slot * size, size)]
        self.plane = [
            copies.start(plane_sums.at[here], plane_sums.at[here], peer)
            for peer in self.plane_peers(zone, side, row, core)
        ]

    def middle(self):
        for copy in self.plane:
            copy.wait_recv()
        total = self.plane_sums[0]
        for place in range(1, 8):
            total = total + self.plane_sums[place]
        self.zone_sums[self.zone] = total
        zone, side, row, core = place_here()
        self.across = [
            self.copies.start(self.zone_sums.at[self.zone], self.zone_sums.at[self.zone], peer)
            for peer in self.zone_peers(zone, side, row, core).values()
        ]

    def finish(self, out):
        for copy in self.across:
            copy.wait_recv()
        total = self.zone_sums[0]
        for place in range(1, self.plan.zones):
            total = total + self.zone_sums[place]
        out[...] = total
        for copy in self.plane + self.across:
            copy.wait_send()


class ZoneBlocks:
    count_local = 0

    def __init__(self, plan, source, slots):
        self.flips, self.slots, self.sources = plan.flips, list(slots), [source]
        self.outputs = [
            jax.ShapeDtypeStruct((len(self.slots),) + source.shape[1:], source.dtype)
        ]
        self.count = len(self.slots)

    def peers(self, zone, side, row, core):
        return {self.flips[slot]: device(flipped(zone, self.flips[slot]), side, row, core) for slot in self.slots}

    def start(self, copies, local_sems, sources, targets):
        zone, side, row, core = place_here()
        self.started = [
            copies.start(
                sources[0].at[slot],
                targets[0].at[number],
                device(flipped(zone, self.flips[slot]), side, row, core),
            )
            for number, slot in enumerate(self.slots)
        ]

    def pump(self, steps):
        pass

    def finish(self):
        for copy in self.started:
            copy.wait_send()
        for copy in self.started:
            copy.wait_recv()


class PairTree:
    def __init__(self, pairs, pieces):
        self.sources = [shard for pair in pairs for shard in pair]
        self.pieces = pieces
        self.outputs = [
            jax.ShapeDtypeStruct((8,) + own.shape, own.dtype) for own, _ in pairs
        ]
        self.count = 6 * sum(pieces) + 2 * len(pairs)
        self.count_local = 2 * len(pairs)

    def peers(self, zone, side, row, core):
        return {
            1: device(flipped(zone, 1), side, row, core),
            3: device(flipped(zone, 3), side, row, core),
            "core": device(zone, side, row, 1 - core),
        }

    def start(self, copies, local_sems, sources, targets):
        zone, side, row, core = place_here()
        inner_peer = device(flipped(zone, 3), side, row, core)
        outer_peer = device(flipped(zone, 1), side, row, core)
        core_peer = device(zone, side, row, 1 - core)
        self.inner = lax.rem(lax.div(zone + 1, 2), 2) == 1
        self.outer = lax.rem(lax.div(zone + 1, 2), 2) == 0
        self.across, self.onward, self.shared, self.late, self.kept = [], [], [], [], []
        for weight, full in enumerate(targets):
            pair = sources[2 * weight : 2 * weight + 2]
            size = pair[0].shape[0] // self.pieces[weight]
            for piece in range(self.pieces[weight]):
                rows = pl.ds(piece * size, size)
                for slot in (0, 1):
                    self.across.append(
                        copies.make(pair[slot].at[rows], full.at[2 + slot, rows], inner_peer)
                    )
                    self.onward.append(
                        copies.make(full.at[2 + slot, rows], full.at[3 - slot, rows], outer_peer)
                    )
                    self.late.append(
                        copies.make(full.at[2 + slot, rows], full.at[6 + slot, rows], core_peer)
                    )
            for slot in (0, 1):
                self.shared.append(copies.make(pair[slot], full.at[4 + slot], core_peer))
                self.kept.append(
                    pltpu.make_async_copy(
                        pair[slot], full.at[slot], local_sems.at[2 * weight + slot]
                    )
                )

        @pl.when(self.inner)
        def _():
            for copy in self.across:
                copy.start()

        for copy in self.shared + self.kept:
            copy.start()

    def pump(self, steps):
        steps = [step for step in steps if step < len(self.across)]

        @pl.when(self.inner)
        def _():
            for step in steps:
                self.across[step].wait_recv()
                self.onward[step].start()
                self.late[step].start()

    def finish(self):
        @pl.when(self.inner)
        def _():
            for copy in self.across + self.onward:
                copy.wait_send()

        @pl.when(self.outer)
        def _():
            for number, copy in enumerate(self.onward):
                copy.wait_recv()
                self.late[number + 1 - 2 * (number % 2)].start()

        for copy in self.kept:
            copy.wait()
        for copy in self.shared + self.late:
            copy.wait_send()
        for copy in self.shared + self.late:
            copy.wait_recv()


def sum_eighths(copies, row_peer, side_peer, send, keep, forward, first, second, store, pump):
    size = send.shape[0] // 4
    part = lambda ref, slot: ref.at[pl.ds(slot * size, size)]
    arrivals = [
        copies.start(part(send, 1), part(first, 1), row_peer),
        copies.start(part(send, 3), part(first, 3), side_peer),
        copies.start(part(send, 0), part(first, 0), row_peer),
        copies.start(part(send, 2), part(first, 2), side_peer),
    ]
    passed = []
    for number, slot, peer in ((0, 1, side_peer), (1, 3, row_peer)):
        arrivals[number].wait_recv()

        def add(row, count, number=number, slot=slot):
            here = pl.ds(slot * size + row, count)
            both = keep[here, :] + first[here, :].astype(jnp.float32)
            forward[pl.ds(number * size + row, count), :] = both.astype(jnp.bfloat16)

        for_rows(size, add)
        passed.append(copies.start(part(forward, number), part(second, number), peer))
    pump([0, 1, 2])
    for number, slot in ((0, 0), (1, 2)):
        arrivals[2 + number].wait_recv()
        passed[number].wait_recv()

        def total(row, count, number=number, slot=slot):
            here = pl.ds(slot * size + row, count)
            sums = keep[here, :] + first[here, :].astype(jnp.float32)
            sums = sums + second[pl.ds(number * size + row, count), :].astype(jnp.float32)
            store(number, row, count, sums)

        for_rows(size, total)
        yield number
    for copy in arrivals + passed:
        copy.wait_send()


def split_refs(refs, jobs, extra_count, out_count):
    refs = list(refs)
    take = lambda count: [refs.pop(0) for _ in range(count)]
    extras = take(extra_count)
    sources = [take(len(job.sources)) for job in jobs]
    full = take(1)[0]
    outs = take(out_count)
    targets = [take(len(job.outputs)) for job in jobs]
    return extras, sources, full, outs, targets, refs


def spread_kernel(middle, jobs, extra_count, out_count, gain_sum, send, keep, *refs):
    extras, sources, full, outs, targets, scratch = split_refs(refs, jobs, extra_count, out_count)
    forward, first, second, send_sems, recv_sems, local_sems = scratch
    zone, side, row, core = place_here()
    row_peer, side_peer = device(zone, side, 1 - row, core), device(zone, 1 - side, row, core)
    copies = Copies(send_sems, recv_sems)
    size = send.shape[0] // 4
    part = lambda slot: full.at[pl.ds(slot * size, size)]
    for out in outs:
        if out.shape[0] == 1:
            out[...] = jnp.zeros_like(out)
    peers = {}
    for job in jobs:
        peers.update(job.peers(zone, side, row, core))
    greet([row_peer, side_peer] + list(peers.values()))
    for job, source, target in zip(jobs, sources, targets):
        job.start(copies, local_sems, source, target)

    def pump(steps):
        for job in jobs:
            job.pump(steps)

    def store(number, row, count, sums):
        own = pl.ds(number * size + row, count)
        full[pl.ds(2 * number * size + row, count), :] = middle(own, sums, extras, outs)

    firsts, seconds = [], []
    for number in sum_eighths(
        copies, row_peer, side_peer, send, keep, forward, first, second, store, pump
    ):
        near, other = (side_peer, row_peer) if number == 0 else (row_peer, side_peer)
        slot = 2 * number
        firsts.append(copies.start(part(slot), part(slot + 1), near))
        seconds.append(copies.start(part(slot), part(4 + slot), other))
    pump([3])
    firsts[0].wait_recv()
    seconds.append(copies.start(part(1), part(5), row_peer))
    firsts[1].wait_recv()
    seconds.append(copies.start(part(3), part(7), side_peer))
    pump(range(4, 64))
    for copy in seconds:
        copy.wait_recv()
    for copy in firsts + seconds:
        copy.wait_send()
    for job in jobs:
        job.finish()


def home_kernel(middle, jobs, extra_count, out_count, gain_sum, send, keep, *refs):
    extras, sources, full, outs, targets, scratch = split_refs(refs, jobs, extra_count, out_count)
    forward, first, second, own, send_sems, recv_sems, local_sems, *gain_scratch = scratch
    zone, side, row, core = place_here()
    row_peer, side_peer = device(zone, side, 1 - row, core), device(zone, 1 - side, row, core)
    core_peer = device(zone, side, row, 1 - core)
    copies = Copies(send_sems, recv_sems)
    size = send.shape[0] // 4
    at_home = side == core
    away = side != core
    for out in outs:
        if out.shape[0] == 1:
            out[...] = jnp.zeros_like(out)
    peers = {}
    for job in jobs:
        peers.update(job.peers(zone, side, row, core))
    plane = [row_peer, side_peer, core_peer]
    if gain_sum is not None:
        plane = gain_sum.plane_peers(zone, side, row, core)
        peers.update(gain_sum.zone_peers(zone, side, row, core))
    greet(plane + list(peers.values()))
    for job, source, target in zip(jobs, sources, targets):
        job.start(copies, local_sems, source, target)

    def store(number, start, count, sums):
        here = pl.ds(number * size + start, count)
        own[here, :] = middle(here, sums, extras, outs)

    for _ in sum_eighths(
        copies, row_peer, side_peer, send, keep, forward, first, second, store, lambda steps: None
    ):
        pass

    def piece(number, x, y):
        start = (x * 2 + y) * size if number == 0 else (4 + y * 2 + x) * size
        return full.at[pl.ds(pl.multiple_of(start, size), size)]

    mine = lambda number: own.at[pl.ds(number * size, size)]
    both = (0, 1)
    to_side = [copies.make(mine(k), piece(k, row, side), side_peer) for k in both]
    to_row = [copies.make(mine(k), piece(k, row, side), row_peer) for k in both]
    pass_row = [
        copies.make(piece(k, row, 1 - side), piece(k, row, 1 - side), row_peer) for k in both
    ]
    share = []
    for number, (x, y) in enumerate(
        ((row, side), (row, 1 - side), (1 - row, side), (1 - row, 1 - side))
    ):
        for k in both:
            source = mine(k) if number == 0 else piece(k, x, y)
            share.append(copies.make(source, piece(k, x, y), core_peer))

    kept = [pltpu.make_async_copy(mine(k), piece(k, row, side), local_sems.at[k]) for k in both]
    if gain_sum is not None:
        gain_sum.start(copies, extras[-1], outs[0], *gain_scratch)

    @pl.when(away)
    def _():
        for copy in to_side:
            copy.start()

    @pl.when(at_home)
    def _():
        for copy in to_row + kept + share[:2]:
            copy.start()

    if gain_sum is not None:
        gain_sum.middle()

    @pl.when(away)
    def _():
        for copy in to_side:
            copy.wait_send()
        for copy in share:
            copy.wait_recv()

    @pl.when(at_home)
    def _():
        for k in both:
            to_side[k].wait_recv()
            pass_row[k].start()
            share[2 + k].start()
        for k, copy in enumerate(to_row + pass_row):
            copy.wait_recv()
            share[4 + k].start()
        for copy in to_row + pass_row + share:
            copy.wait_send()
        for copy in kept:
            copy.wait()

    if gain_sum is not None:
        gain_sum.finish(outs[-1])
    for job in jobs:
        job.finish()


def sum_rows(kernel, middle, send, keep, extras, outs, number, jobs=(), gain_sum=None):
    half, width = send.shape
    eighth = half // 4
    low = jnp.bfloat16
    vmem, hbm = pl.BlockSpec(memory_space=pltpu.VMEM), pl.BlockSpec(memory_space=pl.ANY)
    scratch = [
        pltpu.VMEM((2 * eighth, width), low),
        pltpu.VMEM((half, width), low),
        pltpu.VMEM((2 * eighth, width), low),
    ]
    if kernel is home_kernel:
        scratch.append(pltpu.VMEM((2 * eighth, width), low))
    copies = (12 if kernel is spread_kernel else 20) + sum(job.count for job in jobs)
    local = max([2] + [job.count_local for job in jobs])
    if gain_sum is not None:
        copies += gain_sum.count
        outs = outs + [gain_sum.output]
    scratch += [pltpu.SemaphoreType.DMA((count,)) for count in (copies, copies, local)]
    if gain_sum is not None:
        scratch += gain_sum.scratch
    sources = [source for job in jobs for source in job.sources]
    targets = [target for job in jobs for target in job.outputs]
    return pl.pallas_call(
        functools.partial(kernel, middle, jobs, len(extras), len(outs), gain_sum),
        out_shape=[jax.ShapeDtypeStruct((2 * half, width), low)] + outs + targets,
        in_specs=[vmem] * (2 + len(extras)) + [hbm] * len(sources),
        out_specs=[vmem] * (1 + len(outs)) + [hbm] * len(targets),
        scratch_shapes=scratch,
        compiler_params=pltpu.CompilerParams(
            collective_id=number, has_side_effects=True, vmem_limit_bytes=48 * 2**20
        ),
        cost_estimate=pl.CostEstimate(flops=4 * 10**10, bytes_accessed=10**8, transcendentals=0),
        name=middle.__name__,
    )(send, keep, *extras, *sources)


def opening_kernel(plan, ordered, qkv, gains, gate, out, down, tokens, angles, *refs):
    qkv_full, gains_full, turned_gate, turned_out, turned_down, turned_tokens, turned_angles = refs[:7]
    partner_gate, send_sems, recv_sems, local_sems = refs[7:]
    zone, side, row, core = place_here()
    partner = device(zone, core, row, side)
    row_peer, core_peer = device(zone, side, 1 - row, core), device(zone, side, row, 1 - core)
    zone_peers = [device(flipped(zone, flip), side, row, core) for flip in plan.flips[1:]]
    at_home, away = side == core, side != core
    always = [row_peer, core_peer] + zone_peers

    @pl.when(at_home)
    def _():
        greet(always)

    @pl.when(away)
    def _():
        greet(always + [partner])

    copies = Copies(send_sems, recv_sems)
    zones = plan.zones
    turn = [
        copies.make(source, target, partner)
        for source, target in (
            (gains, gains_full.at[0]),
            (qkv, qkv_full.at[0]),
            (angles, turned_angles),
            (gate, turned_gate),
            (out, turned_out),
            (down, turned_down),
        )
    ]
    half = tokens.shape[0] // 2
    rows = pl.ds(pl.multiple_of(row * half, half), half)
    if ordered:
        width = tokens.shape[1] // plan.total

        def columns(of_core):
            owners = [
                flipped(zone, plan.flips[slot % zones]) * 2
                + (of_core if slot < zones else 1 - of_core)
                for slot in range(plan.total)
            ]
            return [pl.ds(pl.multiple_of(owner * width, width), width) for owner in owners]

        theirs, ours = columns(side), columns(core)
        into = [pl.ds(slot * width, width) for slot in range(plan.total)]
        turn_tokens = [
            copies.make(tokens.at[rows, source], turned_tokens.at[rows, target], partner)
            for source, target in zip(theirs, into)
        ]
        pass_tokens = [
            copies.make(turned_tokens.at[rows, target], turned_tokens.at[rows, target], row_peer)
            for target in into
        ]
        kept_tokens = [
            (tokens.at[:, source], turned_tokens.at[:, target])
            for source, target in zip(ours, into)
        ]
    else:
        turn_tokens = [copies.make(tokens.at[rows], turned_tokens.at[rows], partner)]
        pass_tokens = [copies.make(turned_tokens.at[rows], turned_tokens.at[rows], row_peer)]
        kept_tokens = [(tokens, turned_tokens)]
    kept = [
        pltpu.make_async_copy(source, target, local_sems.at[number])
        for number, (source, target) in enumerate(
            kept_tokens
            + [
                (qkv, qkv_full.at[0]),
                (gains, gains_full.at[0]),
                (angles, turned_angles),
                (gate, turned_gate),
                (out, turned_out),
                (down, turned_down),
            ]
        )
    ]
    slots = list(range(1, zones))
    weights = ((gains, gains_full), (qkv, qkv_full))
    from_own = [
        [copies.make(source, full.at[slot], zone_peers[slot - 1]) for slot in slots]
        + [copies.make(source, full.at[zones], core_peer)]
        for source, full in weights
    ] + [[copies.make(gate, partner_gate, zone_peers[0])]]
    copies.number -= 2 * zones + 1
    from_turned = [
        [copies.make(full.at[0], full.at[slot], zone_peers[slot - 1]) for slot in slots]
        + [copies.make(full.at[0], full.at[zones], core_peer)]
        for _, full in weights
    ] + [[copies.make(turned_gate, partner_gate, zone_peers[0])]]
    cross = [
        [copies.make(full.at[slot], full.at[zones + slot], core_peer) for slot in slots]
        for _, full in weights
    ]

    @pl.when(away)
    def _():
        for copy in turn[:4] + turn_tokens + turn[4:]:
            copy.start()
        for which in (0, 1):
            turn[which].wait_recv()
            for copy in from_turned[which]:
                copy.start()
        turn[3].wait_recv()
        from_turned[2][0].start()
        for first, second in zip(turn_tokens, pass_tokens):
            first.wait_recv()
            second.start()

    @pl.when(at_home)
    def _():
        for copy in from_own[0] + from_own[1] + from_own[2] + kept:
            copy.start()

    for k in range(zones - 1):
        for which in (0, 1):
            from_turned[which][k].wait_recv()
            cross[which][k].start()
    for which in (0, 1):
        from_turned[which][zones - 1].wait_recv()
        for copy in from_turned[which]:
            copy.wait_send()
        for copy in cross[which]:
            copy.wait_recv()
            copy.wait_send()
    from_turned[2][0].wait_recv()
    from_turned[2][0].wait_send()

    @pl.when(away)
    def _():
        for copy in pass_tokens + turn[2:3] + turn[4:]:
            copy.wait_recv()
        for copy in turn + turn_tokens + pass_tokens:
            copy.wait_send()

    @pl.when(at_home)
    def _():
        for copy in kept:
            copy.wait()


def opening(plan, qkv, gains, gate, out, down, tokens, angles, number):
    hbm = pl.BlockSpec(memory_space=pl.ANY)
    like = lambda v: jax.ShapeDtypeStruct(v.shape, v.dtype)
    whole = lambda v: jax.ShapeDtypeStruct((2 * plan.zones,) + v.shape, v.dtype)
    operands = (qkv, gains, gate, out, down, tokens, angles)
    ordered = plan.ordered
    blocks = plan.total if ordered else 1
    copies = 6 + 2 * blocks + 2 * plan.zones + 1 + 2 * (plan.zones - 1)
    return pl.pallas_call(
        functools.partial(opening_kernel, plan, ordered),
        out_shape=[whole(qkv), whole(gains)] + [like(v) for v in operands[2:]] + [like(gate)],
        in_specs=[hbm] * 7,
        out_specs=[hbm] * 8,
        scratch_shapes=[
            pltpu.SemaphoreType.DMA((count,)) for count in (copies, copies, blocks + 6)
        ],
        compiler_params=pltpu.CompilerParams(collective_id=number, has_side_effects=True),
        cost_estimate=pl.CostEstimate(flops=4 * 10**10, bytes_accessed=10**8, transcendentals=0),
        name="opening",
    )(*operands)


def inverse_rms(values):
    return lax.rsqrt(jnp.mean(values * values, -1, keepdims=True) + EPS_NORM)


def hidden_rows(own, sums, extras, outs):
    tokens, gain = extras
    hidden = tokens[own, :].astype(jnp.float32) + sums
    outs[0][own, :] = hidden
    return (hidden * inverse_rms(hidden) * gain[...]).astype(jnp.bfloat16)


def grad_hidden_rows(own, sums, extras, outs):
    hidden, out_grad, gain = extras
    values = hidden[own, :]
    factor = inverse_rms(values)
    unit = values * factor
    outs[1][...] += jnp.sum(sums * unit, 0, keepdims=True)
    grad = out_grad[own, :].astype(jnp.float32) + norm_back(sums * gain[...], unit, factor)
    outs[0][own, :] = grad
    return grad.astype(jnp.bfloat16)


def grad_input_rows(own, sums, extras, outs):
    tokens, grad_hidden, gain = extras[:3]
    values = tokens[own, :].astype(jnp.float32)
    factor = inverse_rms(values)
    unit = values * factor
    outs[0][...] += jnp.sum(sums * unit, 0, keepdims=True)
    return (grad_hidden[own, :] + norm_back(sums * gain[...], unit, factor)).astype(jnp.bfloat16)


def dot(left, right, left_dim=1, right_dim=0):
    return lax.dot_general(
        left, right, (((left_dim,), (right_dim,)), ((), ())), preferred_element_type=jnp.float32
    )


def turn_head(values, cosine, signed_sine):
    return values * cosine + pltpu.roll(values, HEAD // 2, 1) * signed_sine


def turn_back(gradient, cosine, signed_sine):
    return gradient * cosine + pltpu.roll(gradient * signed_sine, HEAD // 2, 1)


def softmax_block(query, key, first_row):
    rows, keys = query.shape[0], key.shape[0]
    scores = dot(query, key, 1, 1)
    row_at = lax.broadcasted_iota(jnp.int32, (rows, keys), 0) + first_row
    key_at = lax.broadcasted_iota(jnp.int32, (rows, keys), 1)
    scores = jnp.where(key_at <= row_at, scores, -1000000000.0)
    exponent = jnp.exp(scores - jnp.max(scores, -1, keepdims=True))
    return exponent / jnp.sum(exponent, -1, keepdims=True)


def eighth_owners():
    _, side, row, _ = place_here()
    own, off = (row, side), (1 - row, 1 - side)
    first = lambda x, y: x * 2 + y
    second = lambda x, y: 4 + y * 2 + x
    return [
        first(own[0], own[1]),
        first(own[0], off[1]),
        second(own[0], own[1]),
        second(off[0], own[1]),
        first(off[0], own[1]),
        first(off[0], off[1]),
        second(own[0], off[1]),
        second(off[0], off[1]),
    ]


def reorder_rows(source, target, into_local):
    size = source.shape[0] // 8
    for slot, owner in enumerate(eighth_owners()):
        natural = pl.ds(pl.multiple_of(owner * size, size), size)
        local = pl.ds(slot * size, size)
        if into_local:
            target[local, :] = source[natural, :]
        else:
            target[natural, :] = source[local, :]


def forward_kernel(
    tokens, weights, gain_in, gain_q, gain_k, cosine, sine,
    normed, raw, query, key, value, local, attended,
):
    low = jnp.bfloat16
    total, heads = tokens.shape[0], query.shape[1] // HEAD
    block = 256

    def project(step, carry):
        rows = pl.ds(pl.multiple_of(step * block, block), block)
        values = tokens[rows, :].astype(jnp.float32)
        normed[rows, :] = (values * inverse_rms(values) * gain_in[...]).astype(low)
        raw[rows, :] = dot(normed[rows, :], weights[...])
        turns = (cosine[rows, :], sine[rows, :])
        for head in range(heads):
            column = (head // 2) * 4 * HEAD + (head % 2) * HEAD
            values = raw[rows, pl.ds(column, HEAD)]
            values = turn_head(values * inverse_rms(values) * gain_q[...], *turns)
            query[rows, pl.ds(head * HEAD, HEAD)] = (values * (1.0 / math.sqrt(HEAD))).astype(low)
        for group in range(heads // 2):
            column = group * 4 * HEAD + 2 * HEAD
            here = pl.ds(group * HEAD, HEAD)
            values = raw[rows, pl.ds(column, HEAD)]
            values = turn_head(values * inverse_rms(values) * gain_k[...], *turns)
            key[rows, here] = values.astype(low)
            value[rows, here] = raw[rows, pl.ds(column + HEAD, HEAD)].astype(low)
        return carry

    lax.fori_loop(0, total // block, project, 0)

    def attend(head, carry):
        mine = pl.ds(pl.multiple_of(head * HEAD, HEAD), HEAD)
        shared = pl.ds(pl.multiple_of(lax.div(head, 2) * HEAD, HEAD), HEAD)
        for start in range(0, total, SEQ):
            for first in range(0, SEQ, block):
                rows, keys = pl.ds(start + first, block), pl.ds(start, first + block)
                probs = softmax_block(query[rows, mine], key[keys, shared], first)
                attended[rows, mine] = dot(probs.astype(low), value[keys, shared]).astype(low)
        return carry

    lax.fori_loop(0, heads, attend, 0)
    reorder_rows(attended, local, True)


def attention(tokens, weights, gain_in, gain_q, gain_k, cosine, sine):
    total = tokens.shape[0]
    columns = weights.shape[1]
    low = jnp.bfloat16
    shape = lambda width, kind=low: jax.ShapeDtypeStruct((total, width), kind)
    vmem = pl.BlockSpec(memory_space=pltpu.VMEM)
    return pl.pallas_call(
        forward_kernel,
        out_shape=[
            shape(tokens.shape[1]),
            shape(columns, jnp.float32),
            shape(columns // 2),
            shape(columns // 4),
            shape(columns // 4),
            shape(columns // 2),
        ],
        in_specs=[vmem] * 7,
        out_specs=[vmem] * 6,
        scratch_shapes=[pltpu.VMEM((total, columns // 2), low)],
        compiler_params=pltpu.CompilerParams(vmem_limit_bytes=48 * 2**20),
        cost_estimate=pl.CostEstimate(flops=10**10, bytes_accessed=2 * 10**7, transcendentals=0),
        name="attention",
    )(tokens, weights, gain_in, gain_q, gain_k, cosine, sine)


def backward_kernel(
    query, key, value, raw, grad_rows, gain_q, gain_k, cosine, sine,
    mixed, mixed_local, query_gain, key_gain, grad, key_sum, value_sum,
):
    low = jnp.bfloat16
    total, heads = query.shape[0], query.shape[1] // HEAD
    block = 256
    reorder_rows(grad_rows, grad, False)
    query_gain[...] = jnp.zeros_like(query_gain)
    key_gain[...] = jnp.zeros_like(key_gain)

    def head_norm_back(rows, column, gradient, gain, gain_grad):
        values = raw[rows, column]
        factor = inverse_rms(values)
        unit = values * factor
        turned = turn_back(gradient, cosine[rows, :], sine[rows, :])
        gain_grad[...] += jnp.sum(turned * unit, 0, keepdims=True)
        mixed[rows, column] = norm_back(turned * gain[...], unit, factor).astype(low)

    def one_group(group, carry):
        at = lambda offset: pl.ds(pl.multiple_of(group * 4 * HEAD + offset * HEAD, HEAD), HEAD)
        shared = pl.ds(pl.multiple_of(group * HEAD, HEAD), HEAD)
        key_sum[...] = jnp.zeros_like(key_sum)
        value_sum[...] = jnp.zeros_like(value_sum)
        for head in (0, 1):
            mine = pl.ds(pl.multiple_of((group * 2 + head) * HEAD, HEAD), HEAD)
            for start in range(0, total, SEQ):
                for first in range(0, SEQ, block):
                    rows, keys = pl.ds(start + first, block), pl.ds(start, first + block)
                    query_part, grad_part = query[rows, mine], grad[rows, mine]
                    probs = softmax_block(query_part, key[keys, shared], first)
                    weighed = probs * dot(grad_part, value[keys, shared], 1, 1)
                    scores = weighed - probs * jnp.sum(weighed, -1, keepdims=True)
                    scores = scores.astype(low)
                    grad_query = dot(scores, key[keys, shared]) * (1.0 / math.sqrt(HEAD))
                    head_norm_back(rows, at(head), grad_query, gain_q, query_gain)
                    key_sum[keys, :] += dot(scores, query_part, 0, 0)
                    value_sum[keys, :] += dot(probs.astype(low), grad_part, 0, 0)
        for first in range(0, total, block):
            rows = pl.ds(first, block)
            head_norm_back(rows, at(2), key_sum[rows, :], gain_k, key_gain)
            mixed[rows, at(3)] = value_sum[rows, :].astype(low)
        return carry

    lax.fori_loop(0, heads // 2, one_group, 0)
    reorder_rows(mixed, mixed_local, True)


def attention_back(query, key, value, raw, grad_rows, gain_q, gain_k, cosine, sine):
    total, columns = raw.shape
    low = jnp.bfloat16
    vmem = pl.BlockSpec(memory_space=pltpu.VMEM)
    return pl.pallas_call(
        backward_kernel,
        out_shape=[
            jax.ShapeDtypeStruct((total, columns), low),
            jax.ShapeDtypeStruct((total, columns), low),
            jax.ShapeDtypeStruct((1, HEAD), jnp.float32),
            jax.ShapeDtypeStruct((1, HEAD), jnp.float32),
        ],
        in_specs=[vmem] * 9,
        out_specs=[vmem] * 4,
        scratch_shapes=[
            pltpu.VMEM(grad_rows.shape, low),
            pltpu.VMEM((total, HEAD), jnp.float32),
            pltpu.VMEM((total, HEAD), jnp.float32),
        ],
        compiler_params=pltpu.CompilerParams(vmem_limit_bytes=48 * 2**20),
        cost_estimate=pl.CostEstimate(flops=10**10, bytes_accessed=2 * 10**7, transcendentals=0),
        name="attention_back",
    )(query, key, value, raw, grad_rows, gain_q, gain_k, cosine, sine)


class Plan:
    def __init__(self, mesh):
        self.total = mesh.shape["dp"]
        self.zones = self.total // 2
        self.tensor = mesh.shape["tensor"]
        self.flips = [k ^ (k >> 1) for k in range(self.zones)]

    def place(self):
        self.index = lax.axis_index("dp")
        self.zone = self.index // 2
        self.side = self.index % 2
        self.row = lax.axis_index("tensor") // 2
        self.core = lax.axis_index("tensor") % 2
        self.home = self.side == self.core

    def move(self, value, target):
        pairs = []
        for d in range(self.total):
            for t in range(self.tensor):
                to = target(d // 2, d % 2, t // 2, t % 2)
                if to is not None:
                    zone, side, row, core = to
                    pairs.append((d * self.tensor + t, (zone * 2 + side) * self.tensor + row * 2 + core))
        return lax.ppermute(value, ("dp", "tensor"), pairs)

    def turn(self, value):
        got = self.move(value, lambda z, y, x, c: (z, c, x, y) if y != c else None)
        return jnp.where(self.home, value, got)

    def zone_flip(self, value, bit):
        return self.move(value, lambda z, y, x, c: (z ^ bit, y, x, c))

    def core_swap(self, value):
        return self.move(value, lambda z, y, x, c: (z, y, x, 1 - c))

    def side_swap(self, value):
        return self.move(value, lambda z, y, x, c: (z, 1 - y, x, c))

    def row_swap(self, value):
        return self.move(value, lambda z, y, x, c: (z, y, 1 - x, c))

    def to_local(self, value, axis):
        width = value.shape[axis] // self.total
        parts = []
        for core in (self.core, 1 - self.core):
            for slot in range(self.zones):
                owner = (self.zone ^ self.flips[slot]) * 2 + core
                parts.append(lax.dynamic_slice_in_dim(value, owner * width, width, axis))
        return jnp.concatenate(parts, axis)

    def to_natural(self, value, axis, core=None):
        core = self.core if core is None else core
        width = value.shape[axis] // self.total
        parts = []
        for block in range(self.total):
            slot = flip = (block // 2) ^ self.zone
            for bits in range(1, self.zones.bit_length()):
                slot = slot ^ (flip >> bits)
            slot = slot + jnp.where(block % 2 == core, 0, self.zones)
            parts.append(lax.dynamic_slice_in_dim(value, slot * width, width, axis))
        return jnp.concatenate(parts, axis)

    def row_owners(self):
        own, off = (self.row, self.side), (1 - self.row, 1 - self.side)
        first = lambda x, y: x * 2 + y
        second = lambda x, y: 4 + y * 2 + x
        return [
            first(own[0], own[1]),
            first(own[0], off[1]),
            second(own[0], own[1]),
            second(off[0], own[1]),
            first(off[0], own[1]),
            first(off[0], off[1]),
            second(own[0], off[1]),
            second(off[0], off[1]),
        ]

    def rows_local(self, value, slots=range(8)):
        size = value.shape[0] // 8
        owners = self.row_owners()
        return jnp.concatenate(
            [lax.dynamic_slice_in_dim(value, owners[slot] * size, size, 0) for slot in slots], 0
        )

    def rows_natural(self, value, order=range(8)):
        size = value.shape[0] // 8
        place = [list(order).index(slot) for slot in range(8)]
        parts = []
        for piece in range(8):
            x, y = (piece // 2, piece % 2) if piece < 4 else (piece % 2, (piece - 4) // 2)
            slots = (0, 1, 4, 5) if piece < 4 else (2, 6, 3, 7)
            same_x, same_y = x == self.row, y == self.side
            slot = jnp.where(
                same_x,
                jnp.where(same_y, place[slots[0]], place[slots[1]]),
                jnp.where(same_y, place[slots[2]], place[slots[3]]),
            )
            parts.append(lax.dynamic_slice_in_dim(value, slot * size, size, 0))
        return jnp.concatenate(parts, 0)

    def from_zones(self, shard):
        return [self.zone_flip(shard, flip) for flip in self.flips[1:]]

    def to_zones(self, parts, slots):
        return [self.zone_flip(parts[slot], self.flips[slot]) for slot in slots]

    def middle_swap(self, pair):
        return self.move(pair, lambda z, y, x, c: (z ^ 3, y, x, c) if z in (1, 2) else None)

    def pass_outward(self, pair):
        return self.move(pair, lambda z, y, x, c: (z ^ 1, y, x, c) if z in (1, 2) else None)

    def far_pair(self, middle, passed):
        inner = (self.zone == 1) | (self.zone == 2)
        return jnp.where(inner, middle, passed[::-1])

    def first_swap(self, send):
        half = send.shape[0] // 2
        return self.row_swap(send[:half]), self.side_swap(send[half:])

    def second_swap(self, keep, got):
        quarter = keep.shape[0] // 4
        row_part = keep[: 2 * quarter] + got[0].astype(jnp.float32)
        side_part = keep[2 * quarter :] + got[1].astype(jnp.float32)
        own = jnp.concatenate([row_part[:quarter], side_part[:quarter]], 0)
        return own, (
            self.side_swap(row_part[quarter:].astype(jnp.bfloat16)),
            self.row_swap(side_part[quarter:].astype(jnp.bfloat16)),
        )

    def spread_first(self, own):
        half = own.shape[0] // 2
        return (self.side_swap(own[:half]), self.row_swap(own[half:]))

    def spread_second(self, own, got):
        half = own.shape[0] // 2
        row_part = jnp.concatenate([own[:half], got[0]], 0)
        side_part = jnp.concatenate([own[half:], got[1]], 0)
        return row_part, side_part, self.row_swap(row_part), self.side_swap(side_part)

    def send_home(self, own):
        to_home = lambda z, y, x, c: (z, c, x, c) if y != c else None
        return jnp.concatenate([own, self.move(own, to_home)], 0)

    def row_home(self, part):
        return self.move(part, lambda z, y, x, c: (z, y, 1 - x, c) if y == c else None)

    def share_home(self, part, other):
        full = jnp.concatenate([part, other], 0)
        full = self.to_natural(self.rows_natural(full, (0, 2, 1, 6, 4, 3, 5, 7)), 1)
        got = self.move(full, lambda z, y, x, c: (z, y, x, 1 - c) if y == c else None)
        return full, got

    def turned(self, own, got):
        return jnp.where(self.home, own, got)

    def sum_everywhere(self, value):
        value = value + self.row_swap(value)
        value = value + self.side_swap(value)
        value = value + self.core_swap(value)
        bit = 1
        while bit < self.zones:
            value = value + self.zone_flip(value, bit)
            bit *= 2
        return value


def shards(
    plan,
    tokens,
    positions,
    out_grad,
    qkv_weight,
    qkv_first,
    qkv_second,
    out_weight,
    out_first,
    out_second,
    gate_up,
    gate_up_first,
    gate_up_second,
    down_weight,
    down_first,
    down_second,
    gains,
    gains_first,
    gains_second,
):
    plan.place()
    low = jnp.bfloat16
    tok_rows, model_width = tokens.shape
    groups = qkv_weight.shape[1]
    head_size = qkv_weight.shape[3]
    shard_rows = qkv_weight.shape[0]
    seq_count = tok_rows // SEQ
    mixed_cols = groups * 4 * head_size
    near_cols = model_width // 2
    kept = tok_rows // 2
    gain_count = gains.shape[0]

    tree = plan.zones == 4
    slots = range(1, plan.zones)

    def column_parts(value):
        return value.reshape((plan.zones, -1) + value.shape[1:])

    units = gate_up.shape[2]
    plan.ordered = (model_width // plan.total) % 128 == 0
    gain_rows = 16
    gain_block = jnp.pad(gains.astype(low), (0, gain_rows * 128 - gain_count)).reshape(gain_rows, 128)
    low_qkv = qkv_weight.reshape(shard_rows, mixed_cols).astype(low)
    low_gate = jnp.concatenate([gate_up[0].astype(low), gate_up[1].astype(low)], 1)
    angle_at = positions.astype(jnp.float32).reshape(-1, 128)
    both_qkv, both_gains, turned_gate, turned_out, turned_down, tokens, angle_at, partner_gate = opening(
        plan,
        low_qkv,
        gain_block,
        low_gate,
        out_weight.astype(low),
        down_weight.astype(low),
        tokens,
        angle_at,
        3,
    )
    positions = angle_at.reshape(-1)
    turned_out, turned_gate, turned_down, tokens, positions, both_qkv, both_gains, out_grad = fence(
        turned_out, turned_gate, turned_down, tokens, positions, both_qkv, both_gains, out_grad
    )

    zone_out = plan.from_zones(turned_out)
    if tree:
        partner_down = plan.zone_flip(turned_down, 1)
    else:
        partner_down = plan.from_zones(turned_down)
        partner_gate = plan.from_zones(turned_gate)
    out_grad = plan.turn(out_grad)
    if not plan.ordered:
        tokens = plan.to_local(tokens, 1)
    cosine, sine_table = rotary(positions, head_size)
    signed_sine = jnp.concatenate(
        [-sine_table[:, : head_size // 2], sine_table[:, head_size // 2 :]], 1
    )
    full_qkv = both_qkv.reshape(model_width, mixed_cols)
    gain_slots = both_gains.reshape(plan.total, -1)[:, :gain_count]
    gain_all = plan.to_natural(gain_slots.reshape(-1), 0).astype(jnp.float32)
    gain_in = plan.to_local(gain_all[:model_width], 0)[None]
    gain_post = plan.to_local(gain_all[model_width : 2 * model_width], 0)[None]
    gain_q = gain_all[2 * model_width : 2 * model_width + head_size][None]
    gain_k = gain_all[2 * model_width + head_size :][None]
    normed, raw, query, key_rot, values_low, attended = attention(
        tokens, full_qkv, gain_in, gain_q, gain_k, cosine, signed_sine
    )
    attended, zone_out, turned_out, partner_down, turned_down, turned_gate, partner_gate = fence(
        attended, zone_out, turned_out, partner_down, turned_down, turned_gate, partner_gate
    )

    near_out = jnp.concatenate([turned_out] + zone_out, 0)
    far_out = plan.core_swap(near_out)
    own_tokens = plan.rows_local(tokens, (0, 2))
    near_out, far_out, own_tokens, out_grad = fence(near_out, far_out, own_tokens, out_grad)

    full_out = jnp.concatenate([near_out, far_out], 0)
    branch_send = contract_cols(attended[kept:], full_out).astype(low)
    branch_keep = contract_cols(attended[:kept], full_out)
    pairs = [(turned_gate, partner_gate), (turned_down, partner_down)]
    normed_rows, hidden, *gathered = sum_rows(
        spread_kernel,
        hidden_rows,
        branch_send,
        branch_keep,
        [own_tokens, gain_post],
        [jax.ShapeDtypeStruct((tok_rows // 4, model_width), jnp.float32)],
        0,
        [PairTree(pairs, (4, 2))] if tree else [],
    )
    if not tree:
        near = [jnp.concatenate([own] + rest, 0) for own, rest in pairs]
        gathered = [jnp.concatenate([part, plan.core_swap(part)], 0) for part in near]
    full_gate = gathered[0].reshape(model_width, 2 * units)
    full_down = gathered[1].reshape(model_width, units)
    normed_rows, hidden, full_gate, full_down, out_grad = fence(
        normed_rows, hidden, full_gate, full_down, out_grad
    )

    out_grad = plan.to_local(plan.rows_local(out_grad), 1)
    gate_pre = jnp.dot(normed_rows, full_gate[:, :units], preferred_element_type=jnp.float32)
    up_proj = jnp.dot(normed_rows, full_gate[:, units:], preferred_element_type=jnp.float32)
    sigmoid_gate = jax.nn.sigmoid(gate_pre)
    silu_gate = gate_pre * sigmoid_gate
    active = (silu_gate * up_proj).astype(low)
    down_far = contract_rows(out_grad[:, near_cols:], active).astype(low)
    down_far, active, up_proj, gate_pre, out_grad, normed_rows = fence(
        down_far, active, up_proj, gate_pre, out_grad, normed_rows
    )

    def zone_parts(near, got):
        both = (near + got.astype(jnp.float32)).astype(low)
        return both.reshape((plan.zones, -1) + both.shape[1:])

    def zone_total(parts, *arrived):
        total = parts[0].astype(jnp.float32)
        for part in sum([list(group) for group in arrived], []):
            total = total + part.astype(jnp.float32)
        return total.astype(low)

    down_got = plan.core_swap(down_far)
    grad_active = jnp.dot(out_grad, full_down, preferred_element_type=jnp.float32)
    sigmoid_gate = jax.nn.sigmoid(gate_pre)
    silu_gate = gate_pre * sigmoid_gate
    grad_gate = (
        grad_active * up_proj * sigmoid_gate * (1.0 + gate_pre * (1.0 - sigmoid_gate))
    ).astype(low)
    grad_up = (grad_active * silu_gate).astype(low)
    grad_both = jnp.concatenate([grad_gate, grad_up], 1)
    down_parts = zone_parts(contract_rows(out_grad[:, :near_cols], active), down_got)
    down_parts, grad_both, normed_rows = fence(down_parts, grad_both, normed_rows)

    down_sent = plan.to_zones(down_parts, [2])
    gate_far = contract_rows(normed_rows[:, near_cols:], grad_both).astype(low)
    post_send = contract_cols(grad_both[kept:], full_gate).astype(low)
    gate_far, post_send, grad_both, normed_rows, down_sent, down_parts = fence(
        gate_far, post_send, grad_both, normed_rows, down_sent, down_parts
    )

    gate_got = plan.core_swap(gate_far)
    down_last = plan.to_zones(down_parts, [slot for slot in slots if slot != 2])
    post_keep = contract_cols(grad_both[:kept], full_gate)
    gate_parts = zone_parts(contract_rows(normed_rows[:, :near_cols], grad_both), gate_got)
    post_send, post_keep, gate_parts, down_parts, out_grad, down_last = fence(
        post_send, post_keep, gate_parts, down_parts, out_grad, down_last
    )

    eighth = tok_rows // 8
    own_grad = jnp.concatenate([out_grad[:eighth], out_grad[2 * eighth : 3 * eighth]], 0)
    early = [slot for slot in slots if slot != 3]
    branch_rows, grad_hidden, post_gain_grad, gate_sent = sum_rows(
        spread_kernel,
        grad_hidden_rows,
        post_send,
        post_keep,
        [hidden, own_grad, gain_post],
        [
            jax.ShapeDtypeStruct((tok_rows // 4, model_width), jnp.float32),
            jax.ShapeDtypeStruct((1, model_width), jnp.float32),
        ],
        1,
        [ZoneBlocks(plan, gate_parts, early)],
    )
    branch_rows, grad_hidden, post_gain_grad, gate_sent, gate_parts, active, hidden = fence(
        branch_rows, grad_hidden, post_gain_grad, gate_sent, gate_parts, active, hidden
    )

    gate_last = plan.to_zones(gate_parts[:, :, :units], [3])
    mlp_send = contract_cols(active[kept:], full_down).astype(low)
    mlp_got = plan.first_swap(mlp_send)
    mlp_keep = contract_cols(active[:kept], full_down)
    out_far = contract_rows(branch_rows[:, near_cols:], attended).astype(low)
    out_got = plan.core_swap(out_far)
    grad_att = jnp.dot(branch_rows, full_out, preferred_element_type=jnp.float32).astype(low)
    out_parts = zone_parts(contract_rows(branch_rows[:, :near_cols], attended), out_got)
    grad_att, mlp_got, mlp_keep, gate_last, out_parts, gate_parts = fence(
        grad_att, mlp_got, mlp_keep, gate_last, out_parts, gate_parts
    )

    up_last = plan.to_zones(gate_parts[:, :, units:], [3])
    mlp_own, mlp_last = plan.second_swap(mlp_keep, mlp_got)
    grad_mixed, mixed_rows, query_gain_grad, key_gain_grad = attention_back(
        query, key_rot, values_low, raw, grad_att, gain_q, gain_k, cosine, signed_sine
    )
    gain_terms = jnp.concatenate(
        [plan.to_natural(post_gain_grad, 1), query_gain_grad, key_gain_grad], 1
    )
    summed_down = plan.turn(zone_total(down_parts, down_sent, down_last))
    grad_mixed, mixed_rows, mlp_own, mlp_last, gain_terms, normed, up_last, summed_down = fence(
        grad_mixed, mixed_rows, mlp_own, mlp_last, gain_terms, normed, up_last, summed_down
    )

    block_own = (hidden + mlp_own + jnp.concatenate(mlp_last, 0).astype(jnp.float32)).astype(low)
    block_home = plan.send_home(block_own)
    qkv_far = contract_rows(normed[:, near_cols:], grad_mixed).astype(low)
    qkv_got = plan.core_swap(qkv_far)
    gate_rest = jnp.concatenate([gate_last[0], up_last[0]], 1)
    summed_gate = plan.turn(zone_total(gate_parts, gate_sent, [gate_rest]))
    normed_send = contract_cols(mixed_rows[kept:], full_qkv).astype(low)
    normed_keep = contract_cols(mixed_rows[:kept], full_qkv)
    qkv_parts = zone_parts(contract_rows(normed[:, :near_cols], grad_mixed), qkv_got)
    block_home, qkv_parts, normed_send, normed_keep, gain_terms = fence(
        block_home, qkv_parts, normed_send, normed_keep, gain_terms
    )

    block_row = plan.row_home(block_home)
    gain_sum = GainSum(plan, gain_terms.shape[1], model_width) if plan.ordered else None
    input_full, input_gain_grad, *rest = sum_rows(
        home_kernel,
        grad_input_rows,
        normed_send,
        normed_keep,
        [own_tokens, grad_hidden, gain_in] + ([gain_terms] if plan.ordered else []),
        [jax.ShapeDtypeStruct((1, model_width), jnp.float32)],
        2,
        [ZoneBlocks(plan, qkv_parts, slots), ZoneBlocks(plan, out_parts, slots)],
        gain_sum,
    )
    if plan.ordered:
        summed_gains, qkv_sent, out_sent = rest
    else:
        qkv_sent, out_sent = rest
        summed_gains = plan.sum_everywhere(
            jnp.concatenate([plan.to_natural(input_gain_grad, 1), gain_terms], 1)
        )
    input_full, summed_gains, qkv_sent, out_sent, block_home, block_row, summed_gate = fence(
        input_full, summed_gains, qkv_sent, out_sent, block_home, block_row, summed_gate
    )

    block_full, block_got = plan.share_home(block_home, block_row)
    summed_both = plan.turn(
        jnp.concatenate([zone_total(qkv_parts, qkv_sent), zone_total(out_parts, out_sent)], 1)
    ).astype(jnp.float32)
    summed_qkv = summed_both[:, :mixed_cols].reshape(qkv_weight.shape)
    summed_out = summed_both[:, mixed_cols:]
    summed_gate = summed_gate.astype(jnp.float32)
    summed_gate = jnp.stack([summed_gate[:, :units], summed_gate[:, units:]])
    summed_down = summed_down.astype(jnp.float32)
    summed_gains = lax.dynamic_slice_in_dim(summed_gains[0], plan.index * gain_count, gain_count, 0)
    block_out = jnp.where(plan.home, block_full, block_got)
    input_rows = plan.to_natural(input_full, 1, plan.side).astype(jnp.float32)

    qkv_moment, qkv_square, qkv_updated = adamw(
        qkv_weight, summed_qkv, qkv_first, qkv_second, RATE_QKV, DECAY_RATE
    )
    out_moment, out_square, out_updated = adamw(
        out_weight, summed_out, out_first, out_second, RATE_OUT, DECAY_RATE
    )
    gate_moment, gate_square, gate_updated = adamw(
        gate_up, summed_gate, gate_up_first, gate_up_second, RATE_GATE, DECAY_RATE
    )
    down_moment, down_square, down_updated = adamw(
        down_weight, summed_down, down_first, down_second, RATE_DOWN, DECAY_RATE
    )
    gain_moment, gain_square, gain_updated = adamw(
        gains, summed_gains, gains_first, gains_second, RATE_GAIN, 0.0
    )
    return (
        block_out,
        input_rows,
        qkv_moment,
        qkv_square,
        qkv_updated,
        out_moment,
        out_square,
        out_updated,
        gate_moment,
        gate_square,
        gate_updated,
        down_moment,
        down_square,
        down_updated,
        gain_moment,
        gain_square,
        gain_updated,
    )


def solution(mesh):
    plan = Plan(mesh)
    placed = (
        P("dp", None),
        P("dp"),
        P("dp", None),
        P("dp", "tensor", None, None),
        P("dp", "tensor", None, None),
        P("dp", "tensor", None, None),
        P("dp", "tensor"),
        P("dp", "tensor"),
        P("dp", "tensor"),
        P(None, "dp", "tensor"),
        P(None, "dp", "tensor"),
        P(None, "dp", "tensor"),
        P("dp", "tensor"),
        P("dp", "tensor"),
        P("dp", "tensor"),
        P("dp"),
        P("dp"),
        P("dp"),
    )
    return jax.shard_map(
        functools.partial(shards, plan),
        mesh=mesh,
        in_specs=placed,
        out_specs=(
            P("dp", None),
            P("dp", None),
            P("dp", "tensor", None, None),
            P("dp", "tensor", None, None),
            P("dp", "tensor", None, None),
            P("dp", "tensor"),
            P("dp", "tensor"),
            P("dp", "tensor"),
            P(None, "dp", "tensor"),
            P(None, "dp", "tensor"),
            P(None, "dp", "tensor"),
            P("dp", "tensor"),
            P("dp", "tensor"),
            P("dp", "tensor"),
            P("dp"),
            P("dp"),
            P("dp"),
        ),
        check_vma=False,
    )
```

```python
import functools
import math

import jax
import jax.numpy as jnp
from jax import lax
from jax.experimental import pallas as pl
from jax.experimental.pallas import tpu as pltpu
from jax.sharding import PartitionSpec as P

SEQ = 1024
STEP = 10


EPS_NORM = 1e-06
THETA = 1000000.0
BETA_ONE = 0.9
BETA_TWO = 0.95
ADAM_EPS = 1e-08
DECAY_RATE = 0.1
RATE_QKV = 0.05
RATE_OUT = 0.3
RATE_GATE = 0.05
RATE_DOWN = 0.03
RATE_GAIN = 1.0


def rotary(positions, head_size):
    freq_index = jnp.arange(head_size // 2, dtype=jnp.float32)
    inverse = jnp.exp(freq_index * (-2.0 * math.log(THETA) / head_size))
    angles = positions.astype(jnp.float32)[:, None] * inverse[None, :]
    cosine = jnp.cos(angles)
    sine_table = jnp.sin(angles)
    return (jnp.concatenate([cosine, cosine], -1), jnp.concatenate([sine_table, sine_table], -1))


def rotate(values, cosine, sine_table):
    half_size = values.shape[-1] // 2
    turned = jnp.concatenate([-values[..., half_size:], values[..., :half_size]], -1)
    return values * cosine[:, None, :] + turned * sine_table[:, None, :]


def unrotate(gradient, cosine, sine_table):
    half_size = gradient.shape[-1] // 2
    turned = gradient * sine_table[:, None, :]
    rotated_back = jnp.concatenate([turned[..., half_size:], -turned[..., :half_size]], -1)
    return gradient * cosine[:, None, :] + rotated_back


def norm_back(grad_unit, unit_vals, factor):
    return factor * (grad_unit - unit_vals * jnp.mean(grad_unit * unit_vals, -1, keepdims=True))


def contract_rows(left, right):
    return lax.dot_general(
        left, right, (((0,), (0,)), ((), ())), preferred_element_type=jnp.float32
    )


def contract_cols(left, right):
    return lax.dot_general(
        left, right, (((1,), (1,)), ((), ())), preferred_element_type=jnp.float32
    )


def block_scores(query_part, key_part, first_row, block_rows, last_row):
    scores = jnp.einsum(
        "nqkgd,nskd->nkgqs", query_part, key_part, preferred_element_type=jnp.float32
    )
    causal = (first_row + jnp.arange(block_rows))[:, None] >= jnp.arange(last_row)[None, :]
    return jnp.where(causal, scores, -1000000000.0)


def attention_forward(query, key_rot, values_low, seq_len):
    block_rows = min(512, seq_len)
    outputs = []
    log_sums = []
    for first_row in range(0, seq_len, block_rows):
        last_row = first_row + block_rows
        query_part = query[:, first_row:last_row]
        scores = block_scores(query_part, key_rot[:, :last_row], first_row, block_rows, last_row)
        row_max = jnp.max(scores, -1, keepdims=True)
        exponent = jnp.exp(scores - row_max)
        row_total = jnp.sum(exponent, -1, keepdims=True)
        probs_low = (exponent / row_total).astype(jnp.bfloat16)
        outputs.append(
            jnp.einsum(
                "nkgqs,nskd->nqkgd",
                probs_low,
                values_low[:, :last_row],
                preferred_element_type=jnp.float32,
            )
        )
        log_sums.append(row_max + jnp.log(row_total))
    return (jnp.concatenate(outputs, 1), log_sums)


def attention_backward(query, key_rot, values_low, grad_att, log_sums, seq_len):
    block_rows = min(512, seq_len)
    query_grads = []
    key_grad = jnp.zeros(key_rot.shape, jnp.float32)
    value_grad = jnp.zeros(values_low.shape, jnp.float32)
    for block_index, first_row in enumerate(range(0, seq_len, block_rows)):
        last_row = first_row + block_rows
        query_part = query[:, first_row:last_row]
        grad_part = grad_att[:, first_row:last_row]
        key_part = key_rot[:, :last_row]
        value_part = values_low[:, :last_row]
        scores = block_scores(query_part, key_part, first_row, block_rows, last_row)
        probs = jnp.exp(scores - log_sums[block_index])
        probs_low = probs.astype(jnp.bfloat16)
        grad_probs = jnp.einsum(
            "nqkgd,nskd->nkgqs", grad_part, value_part, preferred_element_type=jnp.float32
        )
        grad_scores = (
            probs * (grad_probs - jnp.sum(probs * grad_probs, -1, keepdims=True))
        ).astype(jnp.bfloat16)
        query_grads.append(
            jnp.einsum(
                "nkgqs,nskd->nqkgd", grad_scores, key_part, preferred_element_type=jnp.float32
            )
        )
        padding = ((0, 0), (0, seq_len - last_row), (0, 0), (0, 0))
        key_grad = key_grad + jnp.pad(
            jnp.einsum(
                "nkgqs,nqkgd->nskd", grad_scores, query_part, preferred_element_type=jnp.float32
            ),
            padding,
        )
        value_grad = value_grad + jnp.pad(
            jnp.einsum(
                "nkgqs,nqkgd->nskd", probs_low, grad_part, preferred_element_type=jnp.float32
            ),
            padding,
        )
    return (jnp.concatenate(query_grads, 1), key_grad, value_grad)


def adamw(weight, gradient, moment, second, step_rate, decay_rate):
    moment = BETA_ONE * moment + (1.0 - BETA_ONE) * gradient
    second = BETA_TWO * second + (1.0 - BETA_TWO) * gradient * gradient
    first_hat = moment / (1.0 - BETA_ONE**STEP)
    second_hat = second / (1.0 - BETA_TWO**STEP)
    weight = weight - step_rate * (
        first_hat / (jnp.sqrt(second_hat) + ADAM_EPS) + decay_rate * weight
    )
    return (moment, second, weight)


def fence(*values):
    return lax.optimization_barrier(values)


MESH = pl.DeviceIdType.MESH
HEAD = 128


def place_here():
    index, place = lax.axis_index("dp"), lax.axis_index("tensor")
    return lax.div(index, 2), lax.rem(index, 2), lax.div(place, 2), lax.rem(place, 2)


def device(zone, side, row, core):
    return (zone * 2 + side, row * 2 + core)


def flipped(zone, flip):
    bit = 1
    while bit <= flip:
        if flip & bit:
            zone = zone + bit - 2 * bit * lax.rem(lax.div(zone, bit), 2)
        bit *= 2
    return zone


def greet(devices, amount=None):
    barrier = pltpu.get_barrier_semaphore()
    for peer in devices:
        pl.semaphore_signal(barrier, inc=1, device_id=peer, device_id_type=MESH)
    pl.semaphore_wait(barrier, len(devices) if amount is None else amount)


def for_rows(count, body):
    step = 32

    def one(block, carry):
        body(pl.multiple_of(block * step, step), step)
        return carry

    lax.fori_loop(0, count // step, one, 0)


class Copies:
    def __init__(self, send_sems, recv_sems):
        self.send_sems, self.recv_sems = send_sems, recv_sems
        self.number = 0

    def make(self, source, target, peer):
        number, self.number = self.number, self.number + 1
        return pltpu.make_async_remote_copy(
            src_ref=source,
            dst_ref=target,
            send_sem=self.send_sems.at[number],
            recv_sem=self.recv_sems.at[number],
            device_id=peer,
            device_id_type=MESH,
        )

    def start(self, source, target, peer):
        copy = self.make(source, target, peer)
        copy.start()
        return copy


class GainSum:
    def __init__(self, plan, rest, width):
        self.plan, self.width = plan, width
        self.total = width + rest
        self.scratch = [
            pltpu.VMEM((8, 1, self.total), jnp.float32),
            pltpu.VMEM((plan.zones, 1, self.total), jnp.float32),
        ]
        self.output = jax.ShapeDtypeStruct((1, self.total), jnp.float32)
        self.count = 7 + plan.zones - 1

    def plane_peers(self, zone, side, row, core):
        steps = [(s, r, c) for s in range(2) for r in range(2) for c in range(2)][1:]
        turn = lambda value, step: 1 - value if step else value
        return [device(zone, turn(side, s), turn(row, r), turn(core, c)) for s, r, c in steps]

    def zone_peers(self, zone, side, row, core):
        return {flip: device(flipped(zone, flip), side, row, core) for flip in self.plan.flips[1:]}

    def start(self, copies, rest, blocks, plane_sums, zone_sums):
        zone, side, row, core = place_here()
        plan = self.plan
        size = self.width // plan.total
        self.copies, self.plane_sums, self.zone_sums, self.zone = copies, plane_sums, zone_sums, zone
        here = side * 4 + row * 2 + core
        plane_sums[here, :, pl.ds(self.width, self.total - self.width)] = rest[...]
        for slot in range(plan.total):
            owner = flipped(zone, plan.flips[slot % plan.zones]) * 2
            owner = owner + (core if slot < plan.zones else 1 - core)
            spot = pl.ds(pl.multiple_of(owner * size, size), size)
            plane_sums[here, :, spot] = blocks[:, pl.ds(slot * size, size)]
        self.plane = [
            copies.start(plane_sums.at[here], plane_sums.at[here], peer)
            for peer in self.plane_peers(zone, side, row, core)
        ]

    def middle(self):
        for copy in self.plane:
            copy.wait_recv()
        total = self.plane_sums[0]
        for place in range(1, 8):
            total = total + self.plane_sums[place]
        self.zone_sums[self.zone] = total
        zone, side, row, core = place_here()
        self.across = [
            self.copies.start(self.zone_sums.at[self.zone], self.zone_sums.at[self.zone], peer)
            for peer in self.zone_peers(zone, side, row, core).values()
        ]

    def finish(self, out):
        for copy in self.across:
            copy.wait_recv()
        total = self.zone_sums[0]
        for place in range(1, self.plan.zones):
            total = total + self.zone_sums[place]
        out[...] = total
        for copy in self.plane + self.across:
            copy.wait_send()


class ZoneBlocks:
    count_local, scratch = 0, []

    def __init__(self, plan, source, slots):
        self.flips, self.slots, self.sources = plan.flips, list(slots), [source]
        self.outputs = [
            jax.ShapeDtypeStruct((len(self.slots),) + source.shape[1:], source.dtype)
        ]
        self.count = len(self.slots)

    def peers(self, zone, side, row, core):
        return {self.flips[slot]: device(flipped(zone, self.flips[slot]), side, row, core) for slot in self.slots}

    def start(self, copies, local_sems, sources, targets, stages):
        zone, side, row, core = place_here()
        self.started = [
            copies.start(
                sources[0].at[slot],
                targets[0].at[number],
                device(flipped(zone, self.flips[slot]), side, row, core),
            )
            for number, slot in enumerate(self.slots)
        ]

    def pump(self, steps):
        pass

    def finish(self):
        for copy in self.started:
            copy.wait_send()
        for copy in self.started:
            copy.wait_recv()


class PairTree:
    def __init__(self, pairs, pieces):
        self.sources = [shard for pair in pairs for shard in pair]
        self.pieces = pieces
        self.outputs = [
            jax.ShapeDtypeStruct((8,) + own.shape, own.dtype) for own, _ in pairs
        ]
        self.count = 6 * sum(pieces) + 2 * len(pairs)
        self.count_local = 4 * len(pairs)
        self.scratch = [pltpu.VMEM(shard.shape, shard.dtype) for shard in self.sources]

    def peers(self, zone, side, row, core):
        return {
            1: device(flipped(zone, 1), side, row, core),
            3: device(flipped(zone, 3), side, row, core),
            "core": device(zone, side, row, 1 - core),
        }

    def start(self, copies, local_sems, sources, targets, stages):
        zone, side, row, core = place_here()
        inner_peer = device(flipped(zone, 3), side, row, core)
        outer_peer = device(flipped(zone, 1), side, row, core)
        core_peer = device(zone, side, row, 1 - core)
        self.inner = lax.rem(lax.div(zone + 1, 2), 2) == 1
        self.outer = lax.rem(lax.div(zone + 1, 2), 2) == 0
        self.across, self.onward, self.shared, self.late = [], [], [], []
        self.fetch, self.place = [], []
        for weight, full in enumerate(targets):
            pair = sources[2 * weight : 2 * weight + 2]
            size = pair[0].shape[0] // self.pieces[weight]
            for piece in range(self.pieces[weight]):
                rows = pl.ds(piece * size, size)
                for slot in (0, 1):
                    self.across.append(
                        copies.make(pair[slot].at[rows], full.at[2 + slot, rows], inner_peer)
                    )
                    self.onward.append(
                        copies.make(full.at[2 + slot, rows], full.at[3 - slot, rows], outer_peer)
                    )
                    self.late.append(
                        copies.make(full.at[2 + slot, rows], full.at[6 + slot, rows], core_peer)
                    )
            for slot in (0, 1):
                self.shared.append(copies.make(pair[slot], full.at[4 + slot], core_peer))
                spot = 2 * weight + slot
                stage, sem = stages[spot], local_sems.at[2 * spot]
                self.fetch.append(pltpu.make_async_copy(pair[slot], stage, sem))
                sem = local_sems.at[2 * spot + 1]
                self.place.append(pltpu.make_async_copy(stage, full.at[slot], sem))

        @pl.when(self.inner)
        def _():
            for copy in self.across:
                copy.start()

        for copy in self.shared + self.fetch:
            copy.start()

    def pump(self, steps):
        steps = [step for step in steps if step < len(self.across)]
        for copy in self.fetch if 0 in steps else []:
            copy.wait()
        for copy in self.place if 0 in steps else []:
            copy.start()

        @pl.when(self.inner)
        def _():
            for step in steps:
                self.across[step].wait_recv()
                self.onward[step].start()
                self.late[step].start()

    def finish(self):
        @pl.when(self.inner)
        def _():
            for copy in self.across + self.onward:
                copy.wait_send()

        @pl.when(self.outer)
        def _():
            for number, copy in enumerate(self.onward):
                copy.wait_recv()
                self.late[number + 1 - 2 * (number % 2)].start()

        for copy in self.place:
            copy.wait()
        for copy in self.shared + self.late:
            copy.wait_send()
        for copy in self.shared + self.late:
            copy.wait_recv()


def sum_eighths(copies, row_peer, side_peer, send, keep, forward, first, second, store, pump):
    size = send.shape[0] // 4
    part = lambda ref, slot: ref.at[pl.ds(slot * size, size)]
    arrivals = [
        copies.start(part(send, 1), part(first, 1), row_peer),
        copies.start(part(send, 3), part(first, 3), side_peer),
        copies.start(part(send, 0), part(first, 0), row_peer),
        copies.start(part(send, 2), part(first, 2), side_peer),
    ]
    passed = []
    for number, slot, peer in ((0, 1, side_peer), (1, 3, row_peer)):
        arrivals[number].wait_recv()

        def add(row, count, number=number, slot=slot):
            here = pl.ds(slot * size + row, count)
            both = keep[here, :].astype(jnp.float32) + first[here, :].astype(jnp.float32)
            forward[pl.ds(number * size + row, count), :] = both.astype(jnp.bfloat16)

        for_rows(size, add)
        passed.append(copies.start(part(forward, number), part(second, number), peer))
    pump([0, 1, 2])
    for number, slot in ((0, 0), (1, 2)):
        arrivals[2 + number].wait_recv()
        passed[number].wait_recv()

        def total(row, count, number=number, slot=slot):
            here = pl.ds(slot * size + row, count)
            sums = keep[here, :].astype(jnp.float32) + first[here, :].astype(jnp.float32)
            sums = sums + second[pl.ds(number * size + row, count), :].astype(jnp.float32)
            store(number, row, count, sums)

        for_rows(size, total)
        yield number
    for copy in arrivals + passed:
        copy.wait_send()


def halves(terms):
    rows = terms.shape[0] // 2
    return terms.at[pl.ds(0, rows)], terms.at[pl.ds(rows, rows)]


def split_refs(refs, jobs, extra_count, out_count):
    refs = list(refs)
    take = lambda count: [refs.pop(0) for _ in range(count)]
    extras = take(extra_count)
    sources = [take(len(job.sources)) for job in jobs]
    full = take(1)[0]
    outs = take(out_count)
    targets = [take(len(job.outputs)) for job in jobs]
    return extras, sources, full, outs, targets, refs


def spread_kernel(middle, jobs, extra_count, out_count, gain_sum, terms, *refs):
    keep, send = halves(terms)
    extras, sources, full, outs, targets, scratch = split_refs(refs, jobs, extra_count, out_count)
    forward, first, second, send_sems, recv_sems, local_sems, *stages = scratch
    zone, side, row, core = place_here()
    row_peer, side_peer = device(zone, side, 1 - row, core), device(zone, 1 - side, row, core)
    copies = Copies(send_sems, recv_sems)
    size = send.shape[0] // 4
    part = lambda slot: full.at[pl.ds(slot * size, size)]
    for out in outs:
        if out.shape[0] == 1:
            out[...] = jnp.zeros_like(out)
    peers = {}
    for job in jobs:
        peers.update(job.peers(zone, side, row, core))
    greet([row_peer, side_peer] + list(peers.values()))
    for job, source, target in zip(jobs, sources, targets):
        job.start(copies, local_sems, source, target, stages)

    def pump(steps):
        for job in jobs:
            job.pump(steps)

    def store(number, row, count, sums):
        own = pl.ds(number * size + row, count)
        full[pl.ds(2 * number * size + row, count), :] = middle(own, sums, extras, outs)

    firsts, seconds = [], []
    for number in sum_eighths(
        copies, row_peer, side_peer, send, keep, forward, first, second, store, pump
    ):
        near, other = (side_peer, row_peer) if number == 0 else (row_peer, side_peer)
        slot = 2 * number
        firsts.append(copies.start(part(slot), part(slot + 1), near))
        seconds.append(copies.start(part(slot), part(4 + slot), other))
    pump([3])
    firsts[0].wait_recv()
    seconds.append(copies.start(part(1), part(5), row_peer))
    firsts[1].wait_recv()
    seconds.append(copies.start(part(3), part(7), side_peer))
    pump(range(4, 64))
    for copy in seconds:
        copy.wait_recv()
    for copy in firsts + seconds:
        copy.wait_send()
    for job in jobs:
        job.finish()


def home_kernel(middle, jobs, extra_count, out_count, gain_sum, terms, *refs):
    keep, send = halves(terms)
    extras, sources, full, outs, targets, scratch = split_refs(refs, jobs, extra_count, out_count)
    forward, first, second, own, send_sems, recv_sems, local_sems, *gain_scratch = scratch
    zone, side, row, core = place_here()
    row_peer, side_peer = device(zone, side, 1 - row, core), device(zone, 1 - side, row, core)
    core_peer = device(zone, side, row, 1 - core)
    copies = Copies(send_sems, recv_sems)
    size = send.shape[0] // 4
    at_home = side == core
    away = side != core
    for out in outs:
        if out.shape[0] == 1:
            out[...] = jnp.zeros_like(out)
    peers = {}
    for job in jobs:
        peers.update(job.peers(zone, side, row, core))
    plane = [row_peer, side_peer, core_peer]
    if gain_sum is not None:
        plane = gain_sum.plane_peers(zone, side, row, core)
        peers.update(gain_sum.zone_peers(zone, side, row, core))
    greet(plane + list(peers.values()))
    for job, source, target in zip(jobs, sources, targets):
        job.start(copies, local_sems, source, target, [])

    def store(number, start, count, sums):
        here = pl.ds(number * size + start, count)
        values = middle(here, sums, extras, outs)
        own[here, :] = values
        eighth = row * 2 + side if number == 0 else 4 + side * 2 + row

        @pl.when(at_home)
        def _():
            full[pl.ds(pl.multiple_of(eighth * size + start, 32), count), :] = values

    for _ in sum_eighths(
        copies, row_peer, side_peer, send, keep, forward, first, second, store, lambda steps: None
    ):
        pass

    def piece(number, x, y):
        start = (x * 2 + y) * size if number == 0 else (4 + y * 2 + x) * size
        return full.at[pl.ds(pl.multiple_of(start, size), size)]

    mine = lambda number: own.at[pl.ds(number * size, size)]
    both = (0, 1)
    to_side = [copies.make(mine(k), piece(k, row, side), side_peer) for k in both]
    to_row = [copies.make(mine(k), piece(k, row, side), row_peer) for k in both]
    pass_row = [
        copies.make(piece(k, row, 1 - side), piece(k, row, 1 - side), row_peer) for k in both
    ]
    share = []
    for number, (x, y) in enumerate(
        ((row, side), (row, 1 - side), (1 - row, side), (1 - row, 1 - side))
    ):
        for k in both:
            source = mine(k) if number == 0 else piece(k, x, y)
            share.append(copies.make(source, piece(k, x, y), core_peer))

    if gain_sum is not None:
        gain_sum.start(copies, extras[-1], outs[0], *gain_scratch)

    @pl.when(away)
    def _():
        for copy in to_side:
            copy.start()

    @pl.when(at_home)
    def _():
        for copy in to_row + share[:2]:
            copy.start()

    if gain_sum is not None:
        gain_sum.middle()

    @pl.when(away)
    def _():
        for copy in to_side:
            copy.wait_send()
        for copy in share:
            copy.wait_recv()

    @pl.when(at_home)
    def _():
        for k in both:
            to_side[k].wait_recv()
            pass_row[k].start()
            share[2 + k].start()
        for k, copy in enumerate(to_row + pass_row):
            copy.wait_recv()
            share[4 + k].start()
        for copy in to_row + pass_row + share:
            copy.wait_send()

    if gain_sum is not None:
        gain_sum.finish(outs[-1])
    for job in jobs:
        job.finish()


def sum_rows(kernel, middle, terms, extras, outs, number, jobs=(), gain_sum=None):
    half, width = terms.shape[0] // 2, terms.shape[1]
    eighth = half // 4
    low = jnp.bfloat16
    vmem, hbm = pl.BlockSpec(memory_space=pltpu.VMEM), pl.BlockSpec(memory_space=pl.ANY)
    scratch = [
        pltpu.VMEM((2 * eighth, width), low),
        pltpu.VMEM((half, width), low),
        pltpu.VMEM((2 * eighth, width), low),
    ]
    if kernel is home_kernel:
        scratch.append(pltpu.VMEM((2 * eighth, width), low))
    copies = (12 if kernel is spread_kernel else 20) + sum(job.count for job in jobs)
    local = max([2] + [job.count_local for job in jobs])
    if gain_sum is not None:
        copies += gain_sum.count
        outs = outs + [gain_sum.output]
    scratch += [pltpu.SemaphoreType.DMA((count,)) for count in (copies, copies, local)]
    if gain_sum is not None:
        scratch += gain_sum.scratch
    scratch += [stage for job in jobs for stage in job.scratch]
    sources = [source for job in jobs for source in job.sources]
    targets = [target for job in jobs for target in job.outputs]
    return pl.pallas_call(
        functools.partial(kernel, middle, jobs, len(extras), len(outs), gain_sum),
        out_shape=[jax.ShapeDtypeStruct((2 * half, width), low)] + outs + targets,
        in_specs=[vmem] * (1 + len(extras)) + [hbm] * len(sources),
        out_specs=[vmem] * (1 + len(outs)) + [hbm] * len(targets),
        scratch_shapes=scratch,
        compiler_params=pltpu.CompilerParams(
            collective_id=number, has_side_effects=True, vmem_limit_bytes=48 * 2**20
        ),
        cost_estimate=pl.CostEstimate(flops=4 * 10**10, bytes_accessed=10**8, transcendentals=0),
        name=middle.__name__,
    )(terms, *extras, *sources)


def opening_kernel(plan, ordered, qkv, gains, gate, out, down, tokens, angles, *refs):
    qkv_full, gains_full, turned_gate, turned_out, turned_down, turned_tokens, turned_angles = refs[:7]
    partner_gate, send_sems, recv_sems, local_sems, *stages = refs[7:]
    zone, side, row, core = place_here()
    partner = device(zone, core, row, side)
    row_peer, core_peer = device(zone, side, 1 - row, core), device(zone, side, row, 1 - core)
    zone_peers = [device(flipped(zone, flip), side, row, core) for flip in plan.flips[1:]]
    at_home, away = side == core, side != core
    always = [row_peer, core_peer] + zone_peers

    @pl.when(at_home)
    def _():
        greet(always)

    @pl.when(away)
    def _():
        greet(always + [partner])

    copies = Copies(send_sems, recv_sems)
    zones = plan.zones
    turn = [
        copies.make(source, target, partner)
        for source, target in (
            (gains, gains_full.at[0]),
            (qkv, qkv_full.at[0]),
            (angles, turned_angles),
            (gate, turned_gate),
            (out, turned_out),
            (down, turned_down),
        )
    ]
    half = tokens.shape[0] // 2
    rows = pl.ds(pl.multiple_of(row * half, half), half)
    if ordered:
        width = tokens.shape[1] // plan.total

        def columns(of_core):
            owners = [
                flipped(zone, plan.flips[slot % zones]) * 2
                + (of_core if slot < zones else 1 - of_core)
                for slot in range(plan.total)
            ]
            return [pl.ds(pl.multiple_of(owner * width, width), width) for owner in owners]

        theirs, ours = columns(side), columns(core)
        into = [pl.ds(slot * width, width) for slot in range(plan.total)]
        turn_tokens = [
            copies.make(tokens.at[rows, source], turned_tokens.at[rows, target], partner)
            for source, target in zip(theirs, into)
        ]
        pass_tokens = [
            copies.make(turned_tokens.at[rows, target], turned_tokens.at[rows, target], row_peer)
            for target in into
        ]
        fetch_tokens = [
            (tokens.at[:, source], stages[0].at[:, target]) for source, target in zip(ours, into)
        ]
    else:
        turn_tokens = [copies.make(tokens.at[rows], turned_tokens.at[rows], partner)]
        pass_tokens = [copies.make(turned_tokens.at[rows], turned_tokens.at[rows], row_peer)]
        fetch_tokens = [(tokens, stages[0])]
    own = (qkv, gains, angles, gate, out, down)
    ends = (qkv_full.at[0], gains_full.at[0], turned_angles, turned_gate, turned_out, turned_down)
    fetch = [
        pltpu.make_async_copy(source, target, local_sems.at[number])
        for number, (source, target) in enumerate(fetch_tokens + list(zip(own, stages[1:])))
    ]
    place = [
        pltpu.make_async_copy(source, target, local_sems.at[len(fetch) + number])
        for number, (source, target) in enumerate(zip(stages, (turned_tokens,) + ends))
    ]
    slots = list(range(1, zones))
    weights = ((gains, gains_full), (qkv, qkv_full))
    from_own = [
        [copies.make(source, full.at[slot], zone_peers[slot - 1]) for slot in slots]
        + [copies.make(source, full.at[zones], core_peer)]
        for source, full in weights
    ] + [[copies.make(gate, partner_gate, zone_peers[0])]]
    copies.number -= 2 * zones + 1
    from_turned = [
        [copies.make(full.at[0], full.at[slot], zone_peers[slot - 1]) for slot in slots]
        + [copies.make(full.at[0], full.at[zones], core_peer)]
        for _, full in weights
    ] + [[copies.make(turned_gate, partner_gate, zone_peers[0])]]
    cross = [
        [copies.make(full.at[slot], full.at[zones + slot], core_peer) for slot in slots]
        for _, full in weights
    ]

    @pl.when(away)
    def _():
        for copy in turn[:4] + turn_tokens + turn[4:]:
            copy.start()
        for which in (0, 1):
            turn[which].wait_recv()
            for copy in from_turned[which]:
                copy.start()
        turn[3].wait_recv()
        from_turned[2][0].start()
        for first, second in zip(turn_tokens, pass_tokens):
            first.wait_recv()
            second.start()

    @pl.when(at_home)
    def _():
        for copy in from_own[0] + from_own[1] + from_own[2] + fetch:
            copy.start()
        for copy in fetch:
            copy.wait()
        for copy in place:
            copy.start()

    for k in range(zones - 1):
        for which in (0, 1):
            from_turned[which][k].wait_recv()
            cross[which][k].start()
    for which in (0, 1):
        from_turned[which][zones - 1].wait_recv()
        for copy in from_turned[which]:
            copy.wait_send()
        for copy in cross[which]:
            copy.wait_recv()
            copy.wait_send()
    from_turned[2][0].wait_recv()
    from_turned[2][0].wait_send()

    @pl.when(away)
    def _():
        for copy in pass_tokens + turn[2:3] + turn[4:]:
            copy.wait_recv()
        for copy in turn + turn_tokens + pass_tokens:
            copy.wait_send()

    @pl.when(at_home)
    def _():
        for copy in place:
            copy.wait()


def opening(plan, qkv, gains, gate, out, down, tokens, angles, number):
    hbm = pl.BlockSpec(memory_space=pl.ANY)
    like = lambda v: jax.ShapeDtypeStruct(v.shape, v.dtype)
    whole = lambda v: jax.ShapeDtypeStruct((2 * plan.zones,) + v.shape, v.dtype)
    operands = (qkv, gains, gate, out, down, tokens, angles)
    ordered = plan.ordered
    blocks = plan.total if ordered else 1
    copies = 6 + 2 * blocks + 2 * plan.zones + 1 + 2 * (plan.zones - 1)
    return pl.pallas_call(
        functools.partial(opening_kernel, plan, ordered),
        out_shape=[whole(qkv), whole(gains)] + [like(v) for v in operands[2:]] + [like(gate)],
        in_specs=[hbm] * 7,
        out_specs=[hbm] * 8,
        scratch_shapes=[
            pltpu.SemaphoreType.DMA((count,)) for count in (copies, copies, blocks + 13)
        ]
        + [pltpu.VMEM(v.shape, v.dtype) for v in (tokens, qkv, gains, angles, gate, out, down)],
        compiler_params=pltpu.CompilerParams(
            collective_id=number, has_side_effects=True, vmem_limit_bytes=32 * 2**20
        ),
        cost_estimate=pl.CostEstimate(flops=4 * 10**10, bytes_accessed=10**8, transcendentals=0),
        name="opening",
    )(*operands)


def inverse_rms(values):
    return lax.rsqrt(jnp.mean(values * values, -1, keepdims=True) + EPS_NORM)


def hidden_rows(own, sums, extras, outs):
    tokens, gain = extras
    hidden = tokens[own, :].astype(jnp.float32) + sums
    outs[0][own, :] = hidden
    return (hidden * inverse_rms(hidden) * gain[...]).astype(jnp.bfloat16)


def grad_hidden_rows(own, sums, extras, outs):
    hidden, out_grad, gain = extras
    values = hidden[own, :]
    factor = inverse_rms(values)
    unit = values * factor
    outs[1][...] += jnp.sum(sums * unit, 0, keepdims=True)
    grad = out_grad[own, :].astype(jnp.float32) + norm_back(sums * gain[...], unit, factor)
    outs[0][own, :] = grad
    return grad.astype(jnp.bfloat16)


def grad_input_rows(own, sums, extras, outs):
    tokens, grad_hidden, gain = extras[:3]
    values = tokens[own, :].astype(jnp.float32)
    factor = inverse_rms(values)
    unit = values * factor
    outs[0][...] += jnp.sum(sums * unit, 0, keepdims=True)
    return (grad_hidden[own, :] + norm_back(sums * gain[...], unit, factor)).astype(jnp.bfloat16)


def dot(left, right, left_dim=1, right_dim=0):
    return lax.dot_general(
        left, right, (((left_dim,), (right_dim,)), ((), ())), preferred_element_type=jnp.float32
    )


def turn_head(values, cosine, signed_sine):
    return values * cosine + pltpu.roll(values, HEAD // 2, 1) * signed_sine


def turn_back(gradient, cosine, signed_sine):
    return gradient * cosine + pltpu.roll(gradient * signed_sine, HEAD // 2, 1)


def softmax_block(query, key, first_row):
    rows, keys = query.shape[0], key.shape[0]
    scores = dot(query, key, 1, 1)
    row_at = lax.broadcasted_iota(jnp.int32, (rows, keys), 0) + first_row
    key_at = lax.broadcasted_iota(jnp.int32, (rows, keys), 1)
    scores = jnp.where(key_at <= row_at, scores, -1000000000.0)
    exponent = jnp.exp(scores - jnp.max(scores, -1, keepdims=True))
    return exponent / jnp.sum(exponent, -1, keepdims=True)


def eighth_owners():
    _, side, row, _ = place_here()
    own, off = (row, side), (1 - row, 1 - side)
    first = lambda x, y: x * 2 + y
    second = lambda x, y: 4 + y * 2 + x
    return [
        first(own[0], own[1]),
        first(own[0], off[1]),
        second(own[0], own[1]),
        second(off[0], own[1]),
        first(off[0], own[1]),
        first(off[0], off[1]),
        second(own[0], off[1]),
        second(off[0], off[1]),
    ]


def reorder_rows(source, target, into_local):
    size = source.shape[0] // 8
    for slot, owner in enumerate(eighth_owners()):
        natural = pl.ds(pl.multiple_of(owner * size, size), size)
        local = pl.ds(slot * size, size)
        if into_local:
            target[local, :] = source[natural, :]
        else:
            target[natural, :] = source[local, :]


def forward_kernel(
    tokens, weights, gain_in, gain_q, gain_k, cosine, sine,
    normed, raw, query, key, value, local, attended,
):
    low = jnp.bfloat16
    total, heads = tokens.shape[0], query.shape[1] // HEAD
    block = 256

    def project(step, carry):
        rows = pl.ds(pl.multiple_of(step * block, block), block)
        values = tokens[rows, :].astype(jnp.float32)
        normed[rows, :] = (values * inverse_rms(values) * gain_in[...]).astype(low)
        raw[rows, :] = dot(normed[rows, :], weights[...])
        turns = (cosine[rows, :], sine[rows, :])
        for head in range(heads):
            column = (head // 2) * 4 * HEAD + (head % 2) * HEAD
            values = raw[rows, pl.ds(column, HEAD)]
            values = turn_head(values * inverse_rms(values) * gain_q[...], *turns)
            query[rows, pl.ds(head * HEAD, HEAD)] = (values * (1.0 / math.sqrt(HEAD))).astype(low)
        for group in range(heads // 2):
            column = group * 4 * HEAD + 2 * HEAD
            here = pl.ds(group * HEAD, HEAD)
            values = raw[rows, pl.ds(column, HEAD)]
            values = turn_head(values * inverse_rms(values) * gain_k[...], *turns)
            key[rows, here] = values.astype(low)
            value[rows, here] = raw[rows, pl.ds(column + HEAD, HEAD)].astype(low)
        return carry

    lax.fori_loop(0, total // block, project, 0)

    def attend(head, carry):
        mine = pl.ds(pl.multiple_of(head * HEAD, HEAD), HEAD)
        shared = pl.ds(pl.multiple_of(lax.div(head, 2) * HEAD, HEAD), HEAD)
        for start in range(0, total, SEQ):
            for first in range(0, SEQ, block):
                rows, keys = pl.ds(start + first, block), pl.ds(start, first + block)
                probs = softmax_block(query[rows, mine], key[keys, shared], first)
                attended[rows, mine] = dot(probs.astype(low), value[keys, shared]).astype(low)
        return carry

    lax.fori_loop(0, heads, attend, 0)
    reorder_rows(attended, local, True)


def attention(tokens, weights, gain_in, gain_q, gain_k, cosine, sine):
    total = tokens.shape[0]
    columns = weights.shape[1]
    low = jnp.bfloat16
    shape = lambda width, kind=low: jax.ShapeDtypeStruct((total, width), kind)
    vmem = pl.BlockSpec(memory_space=pltpu.VMEM)
    return pl.pallas_call(
        forward_kernel,
        out_shape=[
            shape(tokens.shape[1]),
            shape(columns, jnp.float32),
            shape(columns // 2),
            shape(columns // 4),
            shape(columns // 4),
            shape(columns // 2),
        ],
        in_specs=[vmem] * 7,
        out_specs=[vmem] * 6,
        scratch_shapes=[pltpu.VMEM((total, columns // 2), low)],
        compiler_params=pltpu.CompilerParams(vmem_limit_bytes=48 * 2**20),
        cost_estimate=pl.CostEstimate(flops=10**10, bytes_accessed=2 * 10**7, transcendentals=0),
        name="attention",
    )(tokens, weights, gain_in, gain_q, gain_k, cosine, sine)


def backward_kernel(
    query, key, value, raw, grad_rows, gain_q, gain_k, cosine, sine,
    mixed, mixed_local, query_gain, key_gain, grad, key_sum, value_sum,
):
    low = jnp.bfloat16
    total, heads = query.shape[0], query.shape[1] // HEAD
    block = 256
    reorder_rows(grad_rows, grad, False)
    query_gain[...] = jnp.zeros_like(query_gain)
    key_gain[...] = jnp.zeros_like(key_gain)

    def head_norm_back(rows, column, gradient, gain, gain_grad):
        values = raw[rows, column]
        factor = inverse_rms(values)
        unit = values * factor
        turned = turn_back(gradient, cosine[rows, :], sine[rows, :])
        gain_grad[...] += jnp.sum(turned * unit, 0, keepdims=True)
        mixed[rows, column] = norm_back(turned * gain[...], unit, factor).astype(low)

    def one_group(group, carry):
        at = lambda offset: pl.ds(pl.multiple_of(group * 4 * HEAD + offset * HEAD, HEAD), HEAD)
        shared = pl.ds(pl.multiple_of(group * HEAD, HEAD), HEAD)
        key_sum[...] = jnp.zeros_like(key_sum)
        value_sum[...] = jnp.zeros_like(value_sum)
        for head in (0, 1):
            mine = pl.ds(pl.multiple_of((group * 2 + head) * HEAD, HEAD), HEAD)
            for start in range(0, total, SEQ):
                for first in range(0, SEQ, block):
                    rows, keys = pl.ds(start + first, block), pl.ds(start, first + block)
                    query_part, grad_part = query[rows, mine], grad[rows, mine]
                    probs = softmax_block(query_part, key[keys, shared], first)
                    weighed = probs * dot(grad_part, value[keys, shared], 1, 1)
                    scores = weighed - probs * jnp.sum(weighed, -1, keepdims=True)
                    scores = scores.astype(low)
                    grad_query = dot(scores, key[keys, shared]) * (1.0 / math.sqrt(HEAD))
                    head_norm_back(rows, at(head), grad_query, gain_q, query_gain)
                    key_sum[keys, :] += dot(scores, query_part, 0, 0)
                    value_sum[keys, :] += dot(probs.astype(low), grad_part, 0, 0)
        for first in range(0, total, block):
            rows = pl.ds(first, block)
            head_norm_back(rows, at(2), key_sum[rows, :], gain_k, key_gain)
            mixed[rows, at(3)] = value_sum[rows, :].astype(low)
        return carry

    lax.fori_loop(0, heads // 2, one_group, 0)
    reorder_rows(mixed, mixed_local, True)


def attention_back(query, key, value, raw, grad_rows, gain_q, gain_k, cosine, sine):
    total, columns = raw.shape
    low = jnp.bfloat16
    vmem = pl.BlockSpec(memory_space=pltpu.VMEM)
    return pl.pallas_call(
        backward_kernel,
        out_shape=[
            jax.ShapeDtypeStruct((total, columns), low),
            jax.ShapeDtypeStruct((total, columns), low),
            jax.ShapeDtypeStruct((1, HEAD), jnp.float32),
            jax.ShapeDtypeStruct((1, HEAD), jnp.float32),
        ],
        in_specs=[vmem] * 9,
        out_specs=[vmem] * 4,
        scratch_shapes=[
            pltpu.VMEM(grad_rows.shape, low),
            pltpu.VMEM((total, HEAD), jnp.float32),
            pltpu.VMEM((total, HEAD), jnp.float32),
        ],
        compiler_params=pltpu.CompilerParams(vmem_limit_bytes=48 * 2**20),
        cost_estimate=pl.CostEstimate(flops=10**10, bytes_accessed=2 * 10**7, transcendentals=0),
        name="attention_back",
    )(query, key, value, raw, grad_rows, gain_q, gain_k, cosine, sine)


def feed_kernel(rows, out_grad, gate_up, down, active, grads):
    low = jnp.bfloat16
    block = 256
    units = down.shape[1]

    def one(step, carry):
        here = pl.ds(pl.multiple_of(step * block, block), block)
        both = dot(rows[here, :], gate_up[...])
        grad = dot(out_grad[here, :], down[...])
        gate, up = both[:, :units], both[:, units:]
        sigmoid = jax.nn.sigmoid(gate)
        silu = gate * sigmoid
        active[here, :] = (silu * up).astype(low)
        grads[here, :units] = (grad * up * sigmoid * (1.0 + gate * (1.0 - sigmoid))).astype(low)
        grads[here, units:] = (grad * silu).astype(low)
        return carry

    lax.fori_loop(0, rows.shape[0] // block, one, 0)


def feed_forward(rows, out_grad, gate_up, down, tile):
    total, width = rows.shape
    units = down.shape[1]
    low = jnp.bfloat16
    whole = pl.BlockSpec((total, width), lambda step: (0, 0))
    return pl.pallas_call(
        feed_kernel,
        grid=(units // tile,),
        out_shape=[
            jax.ShapeDtypeStruct((total, units), low),
            jax.ShapeDtypeStruct((total, 2 * units), low),
        ],
        in_specs=[
            whole,
            whole,
            pl.BlockSpec((width, 2 * tile), lambda step: (0, step)),
            pl.BlockSpec((width, tile), lambda step: (0, step)),
        ],
        out_specs=[
            pl.BlockSpec((total, tile), lambda step: (0, step)),
            pl.BlockSpec((total, 2 * tile), lambda step: (0, step)),
        ],
        compiler_params=pltpu.CompilerParams(vmem_limit_bytes=48 * 2**20),
        cost_estimate=pl.CostEstimate(
            flops=6 * total * width * units, bytes_accessed=4 * 10**7, transcendentals=total * units
        ),
        name="feed_forward",
    )(rows, out_grad, gate_up, down)


class Plan:
    def __init__(self, mesh):
        self.total = mesh.shape["dp"]
        self.zones = self.total // 2
        self.tensor = mesh.shape["tensor"]
        self.flips = [k ^ (k >> 1) for k in range(self.zones)]

    def place(self):
        self.index = lax.axis_index("dp")
        self.zone = self.index // 2
        self.side = self.index % 2
        self.row = lax.axis_index("tensor") // 2
        self.core = lax.axis_index("tensor") % 2
        self.home = self.side == self.core

    def move(self, value, target):
        pairs = []
        for d in range(self.total):
            for t in range(self.tensor):
                to = target(d // 2, d % 2, t // 2, t % 2)
                if to is not None:
                    zone, side, row, core = to
                    pairs.append((d * self.tensor + t, (zone * 2 + side) * self.tensor + row * 2 + core))
        return lax.ppermute(value, ("dp", "tensor"), pairs)

    def turn(self, value):
        got = self.move(value, lambda z, y, x, c: (z, c, x, y) if y != c else None)
        return jnp.where(self.home, value, got)

    def zone_flip(self, value, bit):
        return self.move(value, lambda z, y, x, c: (z ^ bit, y, x, c))

    def core_swap(self, value):
        return self.move(value, lambda z, y, x, c: (z, y, x, 1 - c))

    def side_swap(self, value):
        return self.move(value, lambda z, y, x, c: (z, 1 - y, x, c))

    def row_swap(self, value):
        return self.move(value, lambda z, y, x, c: (z, y, 1 - x, c))

    def to_local(self, value, axis):
        width = value.shape[axis] // self.total
        parts = []
        for core in (self.core, 1 - self.core):
            for slot in range(self.zones):
                owner = (self.zone ^ self.flips[slot]) * 2 + core
                parts.append(lax.dynamic_slice_in_dim(value, owner * width, width, axis))
        return jnp.concatenate(parts, axis)

    def to_natural(self, value, axis, core=None):
        core = self.core if core is None else core
        width = value.shape[axis] // self.total
        parts = []
        for block in range(self.total):
            slot = flip = (block // 2) ^ self.zone
            for bits in range(1, self.zones.bit_length()):
                slot = slot ^ (flip >> bits)
            slot = slot + jnp.where(block % 2 == core, 0, self.zones)
            parts.append(lax.dynamic_slice_in_dim(value, slot * width, width, axis))
        return jnp.concatenate(parts, axis)

    def row_owners(self):
        own, off = (self.row, self.side), (1 - self.row, 1 - self.side)
        first = lambda x, y: x * 2 + y
        second = lambda x, y: 4 + y * 2 + x
        return [
            first(own[0], own[1]),
            first(own[0], off[1]),
            second(own[0], own[1]),
            second(off[0], own[1]),
            first(off[0], own[1]),
            first(off[0], off[1]),
            second(own[0], off[1]),
            second(off[0], off[1]),
        ]

    def rows_local(self, value, slots=range(8)):
        size = value.shape[0] // 8
        owners = self.row_owners()
        return jnp.concatenate(
            [lax.dynamic_slice_in_dim(value, owners[slot] * size, size, 0) for slot in slots], 0
        )

    def rows_natural(self, value, order=range(8)):
        size = value.shape[0] // 8
        place = [list(order).index(slot) for slot in range(8)]
        parts = []
        for piece in range(8):
            x, y = (piece // 2, piece % 2) if piece < 4 else (piece % 2, (piece - 4) // 2)
            slots = (0, 1, 4, 5) if piece < 4 else (2, 6, 3, 7)
            same_x, same_y = x == self.row, y == self.side
            slot = jnp.where(
                same_x,
                jnp.where(same_y, place[slots[0]], place[slots[1]]),
                jnp.where(same_y, place[slots[2]], place[slots[3]]),
            )
            parts.append(lax.dynamic_slice_in_dim(value, slot * size, size, 0))
        return jnp.concatenate(parts, 0)

    def from_zones(self, shard):
        return [self.zone_flip(shard, flip) for flip in self.flips[1:]]

    def to_zones(self, parts, slots):
        return [self.zone_flip(parts[slot], self.flips[slot]) for slot in slots]

    def middle_swap(self, pair):
        return self.move(pair, lambda z, y, x, c: (z ^ 3, y, x, c) if z in (1, 2) else None)

    def pass_outward(self, pair):
        return self.move(pair, lambda z, y, x, c: (z ^ 1, y, x, c) if z in (1, 2) else None)

    def far_pair(self, middle, passed):
        inner = (self.zone == 1) | (self.zone == 2)
        return jnp.where(inner, middle, passed[::-1])

    def first_swap(self, send):
        half = send.shape[0] // 2
        return self.row_swap(send[:half]), self.side_swap(send[half:])

    def second_swap(self, keep, got):
        quarter = keep.shape[0] // 4
        row_part = keep[: 2 * quarter] + got[0].astype(jnp.float32)
        side_part = keep[2 * quarter :] + got[1].astype(jnp.float32)
        own = jnp.concatenate([row_part[:quarter], side_part[:quarter]], 0)
        return own, (
            self.side_swap(row_part[quarter:].astype(jnp.bfloat16)),
            self.row_swap(side_part[quarter:].astype(jnp.bfloat16)),
        )

    def spread_first(self, own):
        half = own.shape[0] // 2
        return (self.side_swap(own[:half]), self.row_swap(own[half:]))

    def spread_second(self, own, got):
        half = own.shape[0] // 2
        row_part = jnp.concatenate([own[:half], got[0]], 0)
        side_part = jnp.concatenate([own[half:], got[1]], 0)
        return row_part, side_part, self.row_swap(row_part), self.side_swap(side_part)

    def send_home(self, own):
        to_home = lambda z, y, x, c: (z, c, x, c) if y != c else None
        return jnp.concatenate([own, self.move(own, to_home)], 0)

    def row_home(self, part):
        return self.move(part, lambda z, y, x, c: (z, y, 1 - x, c) if y == c else None)

    def share_home(self, part, other):
        full = jnp.concatenate([part, other], 0)
        full = self.to_natural(self.rows_natural(full, (0, 2, 1, 6, 4, 3, 5, 7)), 1)
        got = self.move(full, lambda z, y, x, c: (z, y, x, 1 - c) if y == c else None)
        return full, got

    def turned(self, own, got):
        return jnp.where(self.home, own, got)

    def sum_everywhere(self, value):
        value = value + self.row_swap(value)
        value = value + self.side_swap(value)
        value = value + self.core_swap(value)
        bit = 1
        while bit < self.zones:
            value = value + self.zone_flip(value, bit)
            bit *= 2
        return value


def shards(
    plan,
    tokens,
    positions,
    out_grad,
    qkv_weight,
    qkv_first,
    qkv_second,
    out_weight,
    out_first,
    out_second,
    gate_up,
    gate_up_first,
    gate_up_second,
    down_weight,
    down_first,
    down_second,
    gains,
    gains_first,
    gains_second,
):
    plan.place()
    low = jnp.bfloat16
    tok_rows, model_width = tokens.shape
    groups = qkv_weight.shape[1]
    head_size = qkv_weight.shape[3]
    shard_rows = qkv_weight.shape[0]
    seq_count = tok_rows // SEQ
    mixed_cols = groups * 4 * head_size
    near_cols = model_width // 2
    kept = tok_rows // 2
    gain_count = gains.shape[0]

    tree = plan.zones == 4
    slots = range(1, plan.zones)

    def column_parts(value):
        return value.reshape((plan.zones, -1) + value.shape[1:])

    units = gate_up.shape[2]
    plan.ordered = (model_width // plan.total) % 128 == 0
    gain_rows = 16
    gain_block = jnp.pad(gains.astype(low), (0, gain_rows * 128 - gain_count)).reshape(gain_rows, 128)
    low_qkv = qkv_weight.reshape(shard_rows, mixed_cols).astype(low)
    tile = min(units, 256)
    low_gate = gate_up.astype(low).reshape(2, shard_rows, units // tile, tile)
    low_gate = low_gate.transpose(1, 2, 0, 3).reshape(shard_rows, 2 * units)
    angle_at = positions.astype(jnp.float32).reshape(-1, 128)
    both_qkv, both_gains, turned_gate, turned_out, turned_down, tokens, angle_at, partner_gate = opening(
        plan,
        low_qkv,
        gain_block,
        low_gate,
        out_weight.astype(low),
        down_weight.astype(low),
        tokens,
        angle_at,
        3,
    )
    positions = angle_at.reshape(-1)
    turned_out, turned_gate, turned_down, tokens, positions, both_qkv, both_gains, out_grad = fence(
        turned_out, turned_gate, turned_down, tokens, positions, both_qkv, both_gains, out_grad
    )

    zone_out = plan.from_zones(turned_out)
    if tree:
        partner_down = plan.zone_flip(turned_down, 1)
    else:
        partner_down = plan.from_zones(turned_down)
        partner_gate = plan.from_zones(turned_gate)
    out_grad = plan.turn(out_grad)
    if not plan.ordered:
        tokens = plan.to_local(tokens, 1)
    cosine, sine_table = rotary(positions, head_size)
    signed_sine = jnp.concatenate(
        [-sine_table[:, : head_size // 2], sine_table[:, head_size // 2 :]], 1
    )
    full_qkv = both_qkv.reshape(model_width, mixed_cols)
    gain_slots = both_gains.reshape(plan.total, -1)[:, :gain_count]
    gain_all = plan.to_natural(gain_slots.reshape(-1), 0).astype(jnp.float32)
    gain_in = plan.to_local(gain_all[:model_width], 0)[None]
    gain_post = plan.to_local(gain_all[model_width : 2 * model_width], 0)[None]
    gain_q = gain_all[2 * model_width : 2 * model_width + head_size][None]
    gain_k = gain_all[2 * model_width + head_size :][None]
    normed, raw, query, key_rot, values_low, attended = attention(
        tokens, full_qkv, gain_in, gain_q, gain_k, cosine, signed_sine
    )
    attended, zone_out, turned_out, partner_down, turned_down, turned_gate, partner_gate = fence(
        attended, zone_out, turned_out, partner_down, turned_down, turned_gate, partner_gate
    )

    near_out = jnp.concatenate([turned_out] + zone_out, 0)
    far_out = plan.core_swap(near_out)
    own_tokens = plan.rows_local(tokens, (0, 2))
    out_grad = plan.to_local(plan.rows_local(out_grad), 1)
    near_out, far_out, own_tokens, out_grad = fence(near_out, far_out, own_tokens, out_grad)

    full_out = jnp.concatenate([near_out, far_out], 0)
    branch_terms = contract_cols(attended, full_out).astype(low)
    pairs = [(turned_gate, partner_gate), (turned_down, partner_down)]
    normed_rows, hidden, *gathered = sum_rows(
        spread_kernel,
        hidden_rows,
        branch_terms,
        [own_tokens, gain_post],
        [jax.ShapeDtypeStruct((tok_rows // 4, model_width), jnp.float32)],
        0,
        [PairTree(pairs, (4, 2))] if tree else [],
    )
    if not tree:
        near = [jnp.concatenate([own] + rest, 0) for own, rest in pairs]
        gathered = [jnp.concatenate([part, plan.core_swap(part)], 0) for part in near]
    full_gate = gathered[0].reshape(model_width, 2 * units)
    full_down = gathered[1].reshape(model_width, units)
    normed_rows, hidden, full_gate, full_down, out_grad = fence(
        normed_rows, hidden, full_gate, full_down, out_grad
    )

    def zone_parts(near, got):
        both = (near + got.astype(jnp.float32)).astype(low)
        return both.reshape((plan.zones, -1) + both.shape[1:])

    def zone_total(parts, *arrived):
        total = parts[0].astype(jnp.float32)
        for part in sum([list(group) for group in arrived], []):
            total = total + part.astype(jnp.float32)
        return total.astype(low)

    active, grad_both = feed_forward(normed_rows, out_grad, full_gate, full_down, tile)
    down_far = contract_rows(out_grad[:, near_cols:], active).astype(low)
    down_far, active, grad_both = fence(down_far, active, grad_both)

    down_got = plan.core_swap(down_far)
    gate_far = contract_rows(normed_rows[:, near_cols:], grad_both).astype(low)
    down_parts = zone_parts(contract_rows(out_grad[:, :near_cols], active), down_got)
    down_parts, gate_far, grad_both = fence(down_parts, gate_far, grad_both)

    gate_got = plan.core_swap(gate_far)
    down_sent = plan.to_zones(down_parts, [slot for slot in slots if slot != 3])
    post_terms = contract_cols(grad_both, full_gate).astype(low)
    gate_parts = zone_parts(contract_rows(normed_rows[:, :near_cols], grad_both), gate_got)
    post_terms, gate_parts, down_parts, down_sent = fence(
        post_terms, gate_parts, down_parts, down_sent
    )

    eighth = tok_rows // 8
    own_grad = jnp.concatenate([out_grad[:eighth], out_grad[2 * eighth : 3 * eighth]], 0)
    branch_rows, grad_hidden, post_gain_grad, down_last, gate_first, gate_next = sum_rows(
        spread_kernel,
        grad_hidden_rows,
        post_terms,
        [hidden, own_grad, gain_post],
        [
            jax.ShapeDtypeStruct((tok_rows // 4, model_width), jnp.float32),
            jax.ShapeDtypeStruct((1, model_width), jnp.float32),
        ],
        1,
        [
            ZoneBlocks(plan, down_parts, [3]),
            ZoneBlocks(plan, gate_parts, [slot for slot in slots if slot not in (2, 3)]),
            ZoneBlocks(plan, gate_parts[:, :, :units], [2]),
        ],
    )
    branch_rows, grad_hidden, post_gain_grad, down_last, gate_first, gate_next, gate_parts, active, hidden = fence(
        branch_rows, grad_hidden, post_gain_grad, down_last, gate_first, gate_next, gate_parts, active, hidden
    )

    gate_more = plan.to_zones(gate_parts[:, :, units:], [2])
    grad_att = jnp.dot(branch_rows, full_out, preferred_element_type=jnp.float32).astype(low)
    grad_mixed, mixed_rows, query_gain_grad, key_gain_grad = attention_back(
        query, key_rot, values_low, raw, grad_att, gain_q, gain_k, cosine, signed_sine
    )
    gain_terms = jnp.concatenate(
        [plan.to_natural(post_gain_grad, 1), query_gain_grad, key_gain_grad], 1
    )
    summed_down = plan.turn(zone_total(down_parts, down_sent, down_last))
    grad_mixed, mixed_rows, gain_terms, normed, gate_more, summed_down, gate_parts, branch_rows = fence(
        grad_mixed, mixed_rows, gain_terms, normed, gate_more, summed_down, gate_parts, branch_rows
    )

    gate_last = plan.to_zones(gate_parts[:, :, :units], [3])
    mlp_terms = contract_cols(active, full_down).astype(low)
    mlp_got = plan.first_swap(mlp_terms[kept:])
    out_far = contract_rows(branch_rows[:, near_cols:], attended).astype(low)
    out_got = plan.core_swap(out_far)
    qkv_far = contract_rows(normed[:, near_cols:], grad_mixed).astype(low)
    out_parts = zone_parts(contract_rows(branch_rows[:, :near_cols], attended), out_got)
    mlp_got, mlp_terms, gate_last, out_parts, qkv_far, grad_mixed, mixed_rows, gate_parts = fence(
        mlp_got, mlp_terms, gate_last, out_parts, qkv_far, grad_mixed, mixed_rows, gate_parts
    )

    up_last = plan.to_zones(gate_parts[:, :, units:], [3])
    qkv_got = plan.core_swap(qkv_far)
    mlp_own, mlp_last = plan.second_swap(mlp_terms[:kept].astype(jnp.float32), mlp_got)
    normed_terms = contract_cols(mixed_rows, full_qkv).astype(low)
    qkv_parts = zone_parts(contract_rows(normed[:, :near_cols], grad_mixed), qkv_got)
    mlp_own, mlp_last, qkv_parts, normed_terms, up_last = fence(
        mlp_own, mlp_last, qkv_parts, normed_terms, up_last
    )

    block_own = (hidden + mlp_own + jnp.concatenate(mlp_last, 0).astype(jnp.float32)).astype(low)
    block_home = plan.send_home(block_own)
    gate_half = [gate_next[0].astype(jnp.float32) + gate_last[0], gate_more[0].astype(jnp.float32) + up_last[0]]
    summed_gate = plan.turn(zone_total(gate_parts, gate_first, [jnp.concatenate(gate_half, 1)]))
    gain_sum = GainSum(plan, gain_terms.shape[1], model_width) if plan.ordered else None
    input_full, input_gain_grad, *rest = sum_rows(
        home_kernel,
        grad_input_rows,
        normed_terms,
        [own_tokens, grad_hidden, gain_in] + ([gain_terms] if plan.ordered else []),
        [jax.ShapeDtypeStruct((1, model_width), jnp.float32)],
        2,
        [ZoneBlocks(plan, qkv_parts, slots), ZoneBlocks(plan, out_parts, slots)],
        gain_sum,
    )
    if plan.ordered:
        summed_gains, qkv_sent, out_sent = rest
    else:
        qkv_sent, out_sent = rest
        summed_gains = plan.sum_everywhere(
            jnp.concatenate([plan.to_natural(input_gain_grad, 1), gain_terms], 1)
        )
    input_full, summed_gains, qkv_sent, out_sent, block_home, summed_gate = fence(
        input_full, summed_gains, qkv_sent, out_sent, block_home, summed_gate
    )

    block_row = plan.row_home(block_home)
    block_full, block_got = plan.share_home(block_home, block_row)
    summed_both = plan.turn(
        jnp.concatenate([zone_total(qkv_parts, qkv_sent), zone_total(out_parts, out_sent)], 1)
    ).astype(jnp.float32)
    summed_qkv = summed_both[:, :mixed_cols].reshape(qkv_weight.shape)
    summed_out = summed_both[:, mixed_cols:]
    summed_gate = summed_gate.astype(jnp.float32)
    summed_gate = summed_gate.reshape(shard_rows, units // tile, 2, tile)
    summed_gate = summed_gate.transpose(2, 0, 1, 3).reshape(gate_up.shape)
    summed_down = summed_down.astype(jnp.float32)
    summed_gains = lax.dynamic_slice_in_dim(summed_gains[0], plan.index * gain_count, gain_count, 0)
    block_out = jnp.where(plan.home, block_full, block_got)
    input_rows = plan.to_natural(input_full, 1, plan.side).astype(jnp.float32)

    qkv_moment, qkv_square, qkv_updated = adamw(
        qkv_weight, summed_qkv, qkv_first, qkv_second, RATE_QKV, DECAY_RATE
    )
    out_moment, out_square, out_updated = adamw(
        out_weight, summed_out, out_first, out_second, RATE_OUT, DECAY_RATE
    )
    gate_moment, gate_square, gate_updated = adamw(
        gate_up, summed_gate, gate_up_first, gate_up_second, RATE_GATE, DECAY_RATE
    )
    down_moment, down_square, down_updated = adamw(
        down_weight, summed_down, down_first, down_second, RATE_DOWN, DECAY_RATE
    )
    gain_moment, gain_square, gain_updated = adamw(
        gains, summed_gains, gains_first, gains_second, RATE_GAIN, 0.0
    )
    return (
        block_out,
        input_rows,
        qkv_moment,
        qkv_square,
        qkv_updated,
        out_moment,
        out_square,
        out_updated,
        gate_moment,
        gate_square,
        gate_updated,
        down_moment,
        down_square,
        down_updated,
        gain_moment,
        gain_square,
        gain_updated,
    )


def solution(mesh):
    plan = Plan(mesh)
    placed = (
        P("dp", None),
        P("dp"),
        P("dp", None),
        P("dp", "tensor", None, None),
        P("dp", "tensor", None, None),
        P("dp", "tensor", None, None),
        P("dp", "tensor"),
        P("dp", "tensor"),
        P("dp", "tensor"),
        P(None, "dp", "tensor"),
        P(None, "dp", "tensor"),
        P(None, "dp", "tensor"),
        P("dp", "tensor"),
        P("dp", "tensor"),
        P("dp", "tensor"),
        P("dp"),
        P("dp"),
        P("dp"),
    )
    return jax.shard_map(
        functools.partial(shards, plan),
        mesh=mesh,
        in_specs=placed,
        out_specs=(
            P("dp", None),
            P("dp", None),
            P("dp", "tensor", None, None),
            P("dp", "tensor", None, None),
            P("dp", "tensor", None, None),
            P("dp", "tensor"),
            P("dp", "tensor"),
            P("dp", "tensor"),
            P(None, "dp", "tensor"),
            P(None, "dp", "tensor"),
            P(None, "dp", "tensor"),
            P("dp", "tensor"),
            P("dp", "tensor"),
            P("dp", "tensor"),
            P("dp"),
            P("dp"),
            P("dp"),
        ),
        check_vma=False,
    )
```

```python
import functools
import math

import jax
import jax.numpy as jnp
from jax import lax
from jax.experimental import pallas as pl
from jax.experimental.pallas import tpu as pltpu
from jax.sharding import PartitionSpec as P

SEQ = 1024
STEP = 10


EPS_NORM = 1e-06
THETA = 1000000.0
BETA_ONE = 0.9
BETA_TWO = 0.95
ADAM_EPS = 1e-08
DECAY_RATE = 0.1
RATE_QKV = 0.05
RATE_OUT = 0.3
RATE_GATE = 0.05
RATE_DOWN = 0.03
RATE_GAIN = 1.0


def rotary(positions, head_size):
    freq_index = jnp.arange(head_size // 2, dtype=jnp.float32)
    inverse = jnp.exp(freq_index * (-2.0 * math.log(THETA) / head_size))
    angles = positions.astype(jnp.float32)[:, None] * inverse[None, :]
    cosine = jnp.cos(angles)
    sine_table = jnp.sin(angles)
    return (jnp.concatenate([cosine, cosine], -1), jnp.concatenate([sine_table, sine_table], -1))


def rotate(values, cosine, sine_table):
    half_size = values.shape[-1] // 2
    turned = jnp.concatenate([-values[..., half_size:], values[..., :half_size]], -1)
    return values * cosine[:, None, :] + turned * sine_table[:, None, :]


def unrotate(gradient, cosine, sine_table):
    half_size = gradient.shape[-1] // 2
    turned = gradient * sine_table[:, None, :]
    rotated_back = jnp.concatenate([turned[..., half_size:], -turned[..., :half_size]], -1)
    return gradient * cosine[:, None, :] + rotated_back


def norm_back(grad_unit, unit_vals, factor):
    return factor * (grad_unit - unit_vals * jnp.mean(grad_unit * unit_vals, -1, keepdims=True))


def contract_rows(left, right):
    return lax.dot_general(
        left, right, (((0,), (0,)), ((), ())), preferred_element_type=jnp.float32
    )


def contract_cols(left, right):
    return lax.dot_general(
        left, right, (((1,), (1,)), ((), ())), preferred_element_type=jnp.float32
    )


def block_scores(query_part, key_part, first_row, block_rows, last_row):
    scores = jnp.einsum(
        "nqkgd,nskd->nkgqs", query_part, key_part, preferred_element_type=jnp.float32
    )
    causal = (first_row + jnp.arange(block_rows))[:, None] >= jnp.arange(last_row)[None, :]
    return jnp.where(causal, scores, -1000000000.0)


def attention_forward(query, key_rot, values_low, seq_len):
    block_rows = min(512, seq_len)
    outputs = []
    log_sums = []
    for first_row in range(0, seq_len, block_rows):
        last_row = first_row + block_rows
        query_part = query[:, first_row:last_row]
        scores = block_scores(query_part, key_rot[:, :last_row], first_row, block_rows, last_row)
        row_max = jnp.max(scores, -1, keepdims=True)
        exponent = jnp.exp(scores - row_max)
        row_total = jnp.sum(exponent, -1, keepdims=True)
        probs_low = (exponent / row_total).astype(jnp.bfloat16)
        outputs.append(
            jnp.einsum(
                "nkgqs,nskd->nqkgd",
                probs_low,
                values_low[:, :last_row],
                preferred_element_type=jnp.float32,
            )
        )
        log_sums.append(row_max + jnp.log(row_total))
    return (jnp.concatenate(outputs, 1), log_sums)


def attention_backward(query, key_rot, values_low, grad_att, log_sums, seq_len):
    block_rows = min(512, seq_len)
    query_grads = []
    key_grad = jnp.zeros(key_rot.shape, jnp.float32)
    value_grad = jnp.zeros(values_low.shape, jnp.float32)
    for block_index, first_row in enumerate(range(0, seq_len, block_rows)):
        last_row = first_row + block_rows
        query_part = query[:, first_row:last_row]
        grad_part = grad_att[:, first_row:last_row]
        key_part = key_rot[:, :last_row]
        value_part = values_low[:, :last_row]
        scores = block_scores(query_part, key_part, first_row, block_rows, last_row)
        probs = jnp.exp(scores - log_sums[block_index])
        probs_low = probs.astype(jnp.bfloat16)
        grad_probs = jnp.einsum(
            "nqkgd,nskd->nkgqs", grad_part, value_part, preferred_element_type=jnp.float32
        )
        grad_scores = (
            probs * (grad_probs - jnp.sum(probs * grad_probs, -1, keepdims=True))
        ).astype(jnp.bfloat16)
        query_grads.append(
            jnp.einsum(
                "nkgqs,nskd->nqkgd", grad_scores, key_part, preferred_element_type=jnp.float32
            )
        )
        padding = ((0, 0), (0, seq_len - last_row), (0, 0), (0, 0))
        key_grad = key_grad + jnp.pad(
            jnp.einsum(
                "nkgqs,nqkgd->nskd", grad_scores, query_part, preferred_element_type=jnp.float32
            ),
            padding,
        )
        value_grad = value_grad + jnp.pad(
            jnp.einsum(
                "nkgqs,nqkgd->nskd", probs_low, grad_part, preferred_element_type=jnp.float32
            ),
            padding,
        )
    return (jnp.concatenate(query_grads, 1), key_grad, value_grad)


def adamw(weight, gradient, moment, second, step_rate, decay_rate):
    moment = BETA_ONE * moment + (1.0 - BETA_ONE) * gradient
    second = BETA_TWO * second + (1.0 - BETA_TWO) * gradient * gradient
    first_hat = moment / (1.0 - BETA_ONE**STEP)
    second_hat = second / (1.0 - BETA_TWO**STEP)
    weight = weight - step_rate * (
        first_hat / (jnp.sqrt(second_hat) + ADAM_EPS) + decay_rate * weight
    )
    return (moment, second, weight)


def fence(*values):
    return lax.optimization_barrier(values)


MESH = pl.DeviceIdType.MESH
HEAD = 128


def place_here():
    index, place = lax.axis_index("dp"), lax.axis_index("tensor")
    return lax.div(index, 2), lax.rem(index, 2), lax.div(place, 2), lax.rem(place, 2)


def device(zone, side, row, core):
    return (zone * 2 + side, row * 2 + core)


def flipped(zone, flip):
    bit = 1
    while bit <= flip:
        if flip & bit:
            zone = zone + bit - 2 * bit * lax.rem(lax.div(zone, bit), 2)
        bit *= 2
    return zone


def greet(devices, amount=None):
    barrier = pltpu.get_barrier_semaphore()
    for peer in devices:
        pl.semaphore_signal(barrier, inc=1, device_id=peer, device_id_type=MESH)
    pl.semaphore_wait(barrier, len(devices) if amount is None else amount)


def for_rows(count, body):
    step = 32

    def one(block, carry):
        body(pl.multiple_of(block * step, step), step)
        return carry

    lax.fori_loop(0, count // step, one, 0)


class Copies:
    def __init__(self, send_sems, recv_sems):
        self.send_sems, self.recv_sems = send_sems, recv_sems
        self.number = 0

    def make(self, source, target, peer):
        number, self.number = self.number, self.number + 1
        return pltpu.make_async_remote_copy(
            src_ref=source,
            dst_ref=target,
            send_sem=self.send_sems.at[number],
            recv_sem=self.recv_sems.at[number],
            device_id=peer,
            device_id_type=MESH,
        )

    def start(self, source, target, peer):
        copy = self.make(source, target, peer)
        copy.start()
        return copy


class GainSum:
    def __init__(self, plan, rest, width):
        self.plan, self.width = plan, width
        self.total = width + rest
        self.scratch = [
            pltpu.VMEM((8, 1, self.total), jnp.float32),
            pltpu.VMEM((plan.zones, 1, self.total), jnp.float32),
        ]
        self.output = jax.ShapeDtypeStruct((1, self.total), jnp.float32)
        self.count = 7 + plan.zones - 1

    def plane_peers(self, zone, side, row, core):
        steps = [(s, r, c) for s in range(2) for r in range(2) for c in range(2)][1:]
        turn = lambda value, step: 1 - value if step else value
        return [device(zone, turn(side, s), turn(row, r), turn(core, c)) for s, r, c in steps]

    def zone_peers(self, zone, side, row, core):
        return {flip: device(flipped(zone, flip), side, row, core) for flip in self.plan.flips[1:]}

    def start(self, copies, rest, blocks, plane_sums, zone_sums):
        zone, side, row, core = place_here()
        plan = self.plan
        size = self.width // plan.total
        self.copies, self.plane_sums, self.zone_sums, self.zone = copies, plane_sums, zone_sums, zone
        here = side * 4 + row * 2 + core
        plane_sums[here, :, pl.ds(self.width, self.total - self.width)] = rest[...]
        for slot in range(plan.total):
            owner = flipped(zone, plan.flips[slot % plan.zones]) * 2
            owner = owner + (core if slot < plan.zones else 1 - core)
            spot = pl.ds(pl.multiple_of(owner * size, size), size)
            plane_sums[here, :, spot] = blocks[:, pl.ds(slot * size, size)]
        self.plane = [
            copies.start(plane_sums.at[here], plane_sums.at[here], peer)
            for peer in self.plane_peers(zone, side, row, core)
        ]

    def middle(self):
        for copy in self.plane:
            copy.wait_recv()
        total = self.plane_sums[0]
        for place in range(1, 8):
            total = total + self.plane_sums[place]
        self.zone_sums[self.zone] = total
        zone, side, row, core = place_here()
        self.across = [
            self.copies.start(self.zone_sums.at[self.zone], self.zone_sums.at[self.zone], peer)
            for peer in self.zone_peers(zone, side, row, core).values()
        ]

    def finish(self, out):
        for copy in self.across:
            copy.wait_recv()
        total = self.zone_sums[0]
        for place in range(1, self.plan.zones):
            total = total + self.zone_sums[place]
        out[...] = total
        for copy in self.plane + self.across:
            copy.wait_send()


class ZoneBlocks:
    scratch = []

    def __init__(self, plan, source, slots):
        self.flips, self.slots, self.sources = plan.flips, list(slots), [source]
        self.outputs = [
            jax.ShapeDtypeStruct((len(self.slots),) + source.shape[1:], source.dtype)
        ]
        self.count, self.count_local = len(self.slots), 0
        self.in_hbm = False

    def peers(self, zone, side, row, core):
        return {
            self.flips[slot]: device(flipped(zone, self.flips[slot]), side, row, core)
            for slot in self.slots
        }

    def start(self, copies, local_sems, sources, targets, stages):
        zone, side, row, core = place_here()
        self.started = [
            copies.start(
                sources[0].at[slot],
                targets[0].at[number],
                device(flipped(zone, self.flips[slot]), side, row, core),
            )
            for number, slot in enumerate(self.slots)
        ]

    def pump(self, steps):
        pass

    def finish(self):
        for copy in self.started:
            copy.wait_send()
        for copy in self.started:
            copy.wait_recv()


def inner_zone(zone):
    return lax.rem(lax.div(zone + 1, 2), 2)


class PairScatter:
    def __init__(self, parts, pieces):
        self.sources, self.pieces = [parts], pieces
        _, rows, columns = parts.shape
        self.size = rows // pieces
        self.outputs = [jax.ShapeDtypeStruct((2, rows, columns), parts.dtype)]
        self.scratch = [pltpu.VMEM((2, rows, columns), parts.dtype)] * 2
        self.count, self.count_local = 4 * pieces, 0
        self.in_hbm = False

    def peers(self, zone, side, row, core):
        return {
            1: device(flipped(zone, 1), side, row, core),
            3: device(flipped(zone, 3), side, row, core),
        }

    def start(self, copies, local_sems, sources, targets, stages):
        zone, side, row, core = place_here()
        self.parts, self.out = sources[0], targets[0]
        self.inward, self.crossed = stages
        inner_peer = device(flipped(zone, 3), side, row, core)
        outer_peer = device(flipped(zone, 1), side, row, core)
        self.inner = inner_zone(zone) == 1
        self.outer = inner_zone(zone) == 0
        self.steps = [
            (slot, pl.ds(piece * self.size, self.size))
            for piece in range(self.pieces)
            for slot in (0, 1)
        ]
        self.to_inner = [
            copies.make(self.parts.at[3 - slot, rows], self.inward.at[slot, rows], outer_peer)
            for slot, rows in self.steps
        ]
        self.across = [
            copies.make(self.inward.at[slot, rows], self.crossed.at[slot, rows], inner_peer)
            for slot, rows in self.steps
        ]

        @pl.when(self.outer)
        def _():
            for copy in self.to_inner:
                copy.start()

    def add(self, target, slot, rows, left, right):
        def some(row, count):
            here = pl.ds(rows.start + row, count)
            both = left[here, :].astype(jnp.float32) + right[here, :].astype(jnp.float32)
            target.at[slot][here, :] = both.astype(jnp.bfloat16)

        for_rows(self.size, some)

    def pump(self, steps):
        steps = [step for step in steps if step < len(self.steps)]

        @pl.when(self.inner)
        def _():
            for step in steps:
                slot, rows = self.steps[step]
                self.to_inner[step].wait_recv()
                self.add(self.inward, slot, rows, self.parts.at[2 + slot], self.inward.at[slot])
                self.across[step].start()

    def finish(self):
        @pl.when(self.inner)
        def _():
            for step, (slot, rows) in enumerate(self.steps):
                self.across[step].wait_recv()
                self.add(self.out, slot, rows, self.parts.at[slot], self.crossed.at[slot])
            for copy in self.across:
                copy.wait_send()

        @pl.when(self.outer)
        def _():
            for slot in (0, 1):

                def some(row, count, slot=slot):
                    here = pl.ds(row, count)
                    self.out.at[slot][here, :] = self.parts.at[slot][here, :]

                for_rows(self.parts.shape[1], some)
            for copy in self.to_inner:
                copy.wait_send()


class PairTree:
    def __init__(self, pairs, pieces):
        self.sources = [shard for pair in pairs for shard in pair]
        self.pieces = pieces
        self.outputs = [
            jax.ShapeDtypeStruct((8,) + own.shape, own.dtype) for own, _ in pairs
        ]
        self.count = 6 * sum(pieces) + 2 * len(pairs)
        self.count_local = 2 * len(pairs) + 2 * sum(pieces)
        self.scratch = [pltpu.VMEM((2,) + own.shape, own.dtype) for own, _ in pairs]
        self.in_hbm = True

    def peers(self, zone, side, row, core):
        return {
            1: device(flipped(zone, 1), side, row, core),
            3: device(flipped(zone, 3), side, row, core),
            "core": device(zone, side, row, 1 - core),
        }

    def start(self, copies, local_sems, sources, targets, stages):
        zone, side, row, core = place_here()
        inner_peer = device(flipped(zone, 3), side, row, core)
        outer_peer = device(flipped(zone, 1), side, row, core)
        core_peer = device(zone, side, row, 1 - core)
        self.inner = inner_zone(zone) == 1
        self.outer = inner_zone(zone) == 0
        self.across, self.onward, self.late, self.place = [], [], [], []
        self.shared, self.kept = [], []
        sem = 0
        for weight, full in enumerate(targets):
            pair, landing = sources[2 * weight : 2 * weight + 2], stages[weight]
            size = pair[0].shape[0] // self.pieces[weight]
            for piece in range(self.pieces[weight]):
                rows = pl.ds(piece * size, size)
                for slot in (0, 1):
                    here = landing.at[slot, rows]
                    self.across.append(copies.make(pair[slot].at[rows], here, inner_peer))
                    self.onward.append(copies.make(here, landing.at[1 - slot, rows], outer_peer))
                    self.late.append(copies.make(here, full.at[6 + slot, rows], core_peer))
                    self.place.append(
                        pltpu.make_async_copy(here, full.at[2 + slot, rows], local_sems.at[sem])
                    )
                    sem += 1
            for slot in (0, 1):
                self.shared.append(copies.make(pair[slot], full.at[4 + slot], core_peer))
                self.kept.append(
                    pltpu.make_async_copy(pair[slot], full.at[slot], local_sems.at[sem])
                )
                sem += 1

        @pl.when(self.inner)
        def _():
            for copy in self.across:
                copy.start()

        for copy in self.shared + self.kept:
            copy.start()

    def pump(self, steps):
        steps = [step for step in steps if step < len(self.across)]

        @pl.when(self.inner)
        def _():
            for step in steps:
                self.across[step].wait_recv()
                self.onward[step].start()
                self.late[step].start()
                self.place[step].start()

    def finish(self):
        @pl.when(self.inner)
        def _():
            for copy in self.across + self.onward:
                copy.wait_send()

        @pl.when(self.outer)
        def _():
            for number, copy in enumerate(self.onward):
                copy.wait_recv()
                arrived = number + 1 - 2 * (number % 2)
                self.late[arrived].start()
                self.place[arrived].start()

        for copy in self.kept + self.place:
            copy.wait()
        for copy in self.shared + self.late:
            copy.wait_send()
        for copy in self.shared + self.late:
            copy.wait_recv()


def sum_eighths(copies, row_peer, side_peer, send, keep, forward, first, second, store, pump):
    size = send.shape[0] // 4
    part = lambda ref, slot: ref.at[pl.ds(slot * size, size)]
    arrivals = [
        copies.start(part(send, 1), part(first, 1), row_peer),
        copies.start(part(send, 3), part(first, 3), side_peer),
        copies.start(part(send, 0), part(first, 0), row_peer),
        copies.start(part(send, 2), part(first, 2), side_peer),
    ]
    passed = []
    for number, slot, peer in ((0, 1, side_peer), (1, 3, row_peer)):
        arrivals[number].wait_recv()

        def add(row, count, number=number, slot=slot):
            here = pl.ds(slot * size + row, count)
            both = keep[here, :].astype(jnp.float32) + first[here, :].astype(jnp.float32)
            forward[pl.ds(number * size + row, count), :] = both.astype(jnp.bfloat16)

        for_rows(size, add)
        passed.append(copies.start(part(forward, number), part(second, number), peer))
    pump([0, 1, 2])
    for number, slot in ((0, 0), (1, 2)):
        arrivals[2 + number].wait_recv()
        passed[number].wait_recv()

        def total(row, count, number=number, slot=slot):
            here = pl.ds(slot * size + row, count)
            sums = keep[here, :].astype(jnp.float32) + first[here, :].astype(jnp.float32)
            sums = sums + second[pl.ds(number * size + row, count), :].astype(jnp.float32)
            store(number, row, count, sums)

        for_rows(size, total)
        yield number
    for copy in arrivals + passed:
        copy.wait_send()


def halves(terms):
    rows = terms.shape[0] // 2
    return terms.at[pl.ds(0, rows)], terms.at[pl.ds(rows, rows)]


def split_refs(refs, jobs, extra_count, out_count):
    refs = list(refs)
    take = lambda count: [refs.pop(0) for _ in range(count)]
    extras = take(extra_count)
    sources = [take(len(job.sources)) for job in jobs]
    full = take(1)[0]
    outs = take(out_count)
    targets = [take(len(job.outputs)) for job in jobs]
    return extras, sources, full, outs, targets, refs


def spread_kernel(middle, jobs, extra_count, out_count, gain_sum, terms, *refs):
    keep, send = halves(terms)
    extras, sources, full, outs, targets, scratch = split_refs(refs, jobs, extra_count, out_count)
    forward, first, second, send_sems, recv_sems, local_sems, *stages = scratch
    zone, side, row, core = place_here()
    row_peer, side_peer = device(zone, side, 1 - row, core), device(zone, 1 - side, row, core)
    copies = Copies(send_sems, recv_sems)
    size = send.shape[0] // 4
    part = lambda slot: full.at[pl.ds(slot * size, size)]
    for out in outs:
        if out.shape[0] == 1:
            out[...] = jnp.zeros_like(out)
    peers = {}
    for job in jobs:
        peers.update(job.peers(zone, side, row, core))
    greet([row_peer, side_peer] + list(peers.values()))
    for job, source, target in zip(jobs, sources, targets):
        job.start(copies, local_sems, source, target, stages[: len(job.scratch)])
        stages = stages[len(job.scratch) :]

    def pump(steps):
        for job in jobs:
            job.pump(steps)

    def store(number, row, count, sums):
        own = pl.ds(number * size + row, count)
        full[pl.ds(2 * number * size + row, count), :] = middle(own, sums, extras, outs)

    firsts, seconds = [], []
    for number in sum_eighths(
        copies, row_peer, side_peer, send, keep, forward, first, second, store, pump
    ):
        near, other = (side_peer, row_peer) if number == 0 else (row_peer, side_peer)
        slot = 2 * number
        firsts.append(copies.start(part(slot), part(slot + 1), near))
        seconds.append(copies.start(part(slot), part(4 + slot), other))
    pump([3])
    firsts[0].wait_recv()
    seconds.append(copies.start(part(1), part(5), row_peer))
    firsts[1].wait_recv()
    seconds.append(copies.start(part(3), part(7), side_peer))
    pump(range(4, 64))
    for copy in seconds:
        copy.wait_recv()
    for copy in firsts + seconds:
        copy.wait_send()
    for job in jobs:
        job.finish()


def home_kernel(middle, jobs, extra_count, out_count, gain_sum, terms, *refs):
    keep, send = halves(terms)
    extras, sources, full, outs, targets, scratch = split_refs(refs, jobs, extra_count, out_count)
    forward, first, second, own, send_sems, recv_sems, local_sems, *gain_scratch = scratch
    zone, side, row, core = place_here()
    row_peer, side_peer = device(zone, side, 1 - row, core), device(zone, 1 - side, row, core)
    core_peer = device(zone, side, row, 1 - core)
    copies = Copies(send_sems, recv_sems)
    size = send.shape[0] // 4
    at_home = side == core
    away = side != core
    for out in outs:
        if out.shape[0] == 1:
            out[...] = jnp.zeros_like(out)
    peers = {}
    for job in jobs:
        peers.update(job.peers(zone, side, row, core))
    plane = [row_peer, side_peer, core_peer]
    if gain_sum is not None:
        plane = gain_sum.plane_peers(zone, side, row, core)
        peers.update(gain_sum.zone_peers(zone, side, row, core))
    greet(plane + list(peers.values()))
    for job, source, target in zip(jobs, sources, targets):
        job.start(copies, local_sems, source, target, [])

    def store(number, start, count, sums):
        here = pl.ds(number * size + start, count)
        values = middle(here, sums, extras, outs)
        own[here, :] = values
        eighth = row * 2 + side if number == 0 else 4 + side * 2 + row

        @pl.when(at_home)
        def _():
            full[pl.ds(pl.multiple_of(eighth * size + start, 32), count), :] = values

    for _ in sum_eighths(
        copies, row_peer, side_peer, send, keep, forward, first, second, store, lambda steps: None
    ):
        pass

    def piece(number, x, y):
        start = (x * 2 + y) * size if number == 0 else (4 + y * 2 + x) * size
        return full.at[pl.ds(pl.multiple_of(start, size), size)]

    mine = lambda number: own.at[pl.ds(number * size, size)]
    both = (0, 1)
    to_side = [copies.make(mine(k), piece(k, row, side), side_peer) for k in both]
    to_row = [copies.make(mine(k), piece(k, row, side), row_peer) for k in both]
    pass_row = [
        copies.make(piece(k, row, 1 - side), piece(k, row, 1 - side), row_peer) for k in both
    ]
    share = []
    for number, (x, y) in enumerate(
        ((row, side), (row, 1 - side), (1 - row, side), (1 - row, 1 - side))
    ):
        for k in both:
            source = mine(k) if number == 0 else piece(k, x, y)
            share.append(copies.make(source, piece(k, x, y), core_peer))

    if gain_sum is not None:
        gain_sum.start(copies, extras[-1], outs[0], *gain_scratch)

    @pl.when(away)
    def _():
        for copy in to_side:
            copy.start()

    @pl.when(at_home)
    def _():
        for copy in to_row + share[:2]:
            copy.start()

    if gain_sum is not None:
        gain_sum.middle()

    @pl.when(away)
    def _():
        for copy in to_side:
            copy.wait_send()
        for copy in share:
            copy.wait_recv()

    @pl.when(at_home)
    def _():
        for k in both:
            to_side[k].wait_recv()
            pass_row[k].start()
            share[2 + k].start()
        for k, copy in enumerate(to_row + pass_row):
            copy.wait_recv()
            share[4 + k].start()
        for copy in to_row + pass_row + share:
            copy.wait_send()

    if gain_sum is not None:
        gain_sum.finish(outs[-1])
    for job in jobs:
        job.finish()


def sum_rows(kernel, middle, terms, extras, outs, number, jobs=(), gain_sum=None):
    half, width = terms.shape[0] // 2, terms.shape[1]
    eighth = half // 4
    low = jnp.bfloat16
    vmem, hbm = pl.BlockSpec(memory_space=pltpu.VMEM), pl.BlockSpec(memory_space=pl.ANY)
    scratch = [
        pltpu.VMEM((2 * eighth, width), low),
        pltpu.VMEM((half, width), low),
        pltpu.VMEM((2 * eighth, width), low),
    ]
    if kernel is home_kernel:
        scratch.append(pltpu.VMEM((2 * eighth, width), low))
    copies = (12 if kernel is spread_kernel else 20) + sum(job.count for job in jobs)
    local = max([2] + [job.count_local for job in jobs])
    if gain_sum is not None:
        copies += gain_sum.count
        outs = outs + [gain_sum.output]
    scratch += [pltpu.SemaphoreType.DMA((count,)) for count in (copies, copies, local)]
    if gain_sum is not None:
        scratch += gain_sum.scratch
    scratch += [stage for job in jobs for stage in job.scratch]
    sources = [source for job in jobs for source in job.sources]
    targets = [target for job in jobs for target in job.outputs]
    return pl.pallas_call(
        functools.partial(kernel, middle, jobs, len(extras), len(outs), gain_sum),
        out_shape=[jax.ShapeDtypeStruct((2 * half, width), low)] + outs + targets,
        in_specs=[vmem] * (1 + len(extras) + len(sources)),
        out_specs=[vmem] * (1 + len(outs))
        + [hbm if job.in_hbm else vmem for job in jobs for _ in job.outputs],
        scratch_shapes=scratch,
        compiler_params=pltpu.CompilerParams(
            collective_id=number, has_side_effects=True, vmem_limit_bytes=56 * 2**20
        ),
        cost_estimate=pl.CostEstimate(flops=4 * 10**10, bytes_accessed=10**8, transcendentals=0),
        name=middle.__name__,
    )(terms, *extras, *sources)


def copy_rows(source, target):
    def some(row, count):
        target[pl.ds(row, count), :] = source[pl.ds(row, count), :]

    if source.shape[0] % 32:
        target[...] = source[...]
    else:
        for_rows(source.shape[0], some)


def opening_kernel(plan, qkv, gains, gate, out, down, tokens, out_grad, angles, *refs):
    qkv_full, gains_full, turned_gate, turned_out, turned_down, turned_tokens, turned_angles = refs[:7]
    rows_grad, partner_gate, send_sems, recv_sems, turned_grad = refs[7:]
    zone, side, row, core = place_here()
    partner = device(zone, core, row, side)
    row_peer, core_peer = device(zone, side, 1 - row, core), device(zone, side, row, 1 - core)
    zone_peers = [device(flipped(zone, flip), side, row, core) for flip in plan.flips[1:]]
    at_home, away = side == core, side != core
    always = [row_peer, core_peer] + zone_peers

    @pl.when(at_home)
    def _():
        greet(always)

    @pl.when(away)
    def _():
        greet(always + [partner])

    copies = Copies(send_sems, recv_sems)
    zones = plan.zones
    own = (gains, qkv, angles, gate, out, down)
    ends = (gains_full.at[0], qkv_full.at[0], turned_angles, turned_gate, turned_out, turned_down)
    turn = [copies.make(source, target, partner) for source, target in zip(own, ends)]
    half = tokens.shape[0] // 2
    rows = pl.ds(pl.multiple_of(row * half, half), half)
    width = tokens.shape[1] // plan.total if plan.ordered else tokens.shape[1]

    def columns(of_core):
        if not plan.ordered:
            return [pl.ds(0, width)]
        owners = [
            flipped(zone, plan.flips[slot % zones]) * 2 + (of_core if slot < zones else 1 - of_core)
            for slot in range(plan.total)
        ]
        return [pl.ds(pl.multiple_of(owner * width, width), width) for owner in owners]

    theirs, ours = columns(side), columns(core)
    into = [pl.ds(slot * width, width) for slot in range(len(ours))]
    moved = ((tokens, turned_tokens), (out_grad, turned_grad))
    turn_halves = [
        [copies.make(full.at[rows, a], target.at[rows, b], partner) for a, b in zip(theirs, into)]
        for full, target in moved
    ]
    pass_halves = [
        [copies.make(target.at[rows, b], target.at[rows, b], row_peer) for b in into]
        for _, target in moved
    ]
    slots = list(range(1, zones))
    weights = ((gains, gains_full), (qkv, qkv_full))
    from_own = [
        [copies.make(source, full.at[slot], zone_peers[slot - 1]) for slot in slots]
        + [copies.make(source, full.at[zones], core_peer)]
        for source, full in weights
    ] + [[copies.make(gate, partner_gate, zone_peers[0])]]
    copies.number -= 2 * zones + 1
    from_turned = [
        [copies.make(full.at[0], full.at[slot], zone_peers[slot - 1]) for slot in slots]
        + [copies.make(full.at[0], full.at[zones], core_peer)]
        for _, full in weights
    ] + [[copies.make(turned_gate, partner_gate, zone_peers[0])]]
    cross = [
        [copies.make(full.at[slot], full.at[zones + slot], core_peer) for slot in slots]
        for _, full in weights
    ]

    @pl.when(away)
    def _():
        for copy in turn[:4] + turn_halves[0] + turn[4:] + turn_halves[1]:
            copy.start()
        for which in (0, 1):
            turn[which].wait_recv()
            for copy in from_turned[which]:
                copy.start()
        turn[3].wait_recv()
        from_turned[2][0].start()
        for first, second in zip(turn_halves[0], pass_halves[0]):
            first.wait_recv()
            second.start()

    @pl.when(at_home)
    def _():
        for copy in from_own[0] + from_own[1] + from_own[2]:
            copy.start()
        for source, target in zip(own, ends):
            copy_rows(source, target)
        for full, target in moved:

            def some(start, count, full=full, target=target):
                here = pl.ds(start, count)
                for a, b in zip(ours, into):
                    target[here, b] = full[here, a]

            for_rows(full.shape[0], some)

    for k in range(zones - 1):
        for which in (0, 1):
            from_turned[which][k].wait_recv()
            cross[which][k].start()

    @pl.when(away)
    def _():
        for first, second in zip(turn_halves[1], pass_halves[1]):
            first.wait_recv()
            second.start()

    for which in (0, 1):
        from_turned[which][zones - 1].wait_recv()
        for copy in from_turned[which]:
            copy.wait_send()
        for copy in cross[which]:
            copy.wait_recv()
            copy.wait_send()
    from_turned[2][0].wait_recv()
    from_turned[2][0].wait_send()

    @pl.when(away)
    def _():
        passed = pass_halves[0] + pass_halves[1]
        for copy in passed + turn[2:3] + turn[4:]:
            copy.wait_recv()
        for copy in turn + turn_halves[0] + turn_halves[1] + passed:
            copy.wait_send()

    reorder_rows(turned_grad, rows_grad, True)


def opening(plan, qkv, gains, gate, out, down, tokens, out_grad, angles, number):
    vmem = pl.BlockSpec(memory_space=pltpu.VMEM)
    like = lambda v: jax.ShapeDtypeStruct(v.shape, v.dtype)
    whole = lambda v: jax.ShapeDtypeStruct((2 * plan.zones,) + v.shape, v.dtype)
    operands = (qkv, gains, gate, out, down, tokens, out_grad, angles)
    outputs = [whole(qkv), whole(gains)] + [like(v) for v in (gate, out, down, tokens, angles)]
    outputs += [like(out_grad), like(gate)]
    blocks = plan.total if plan.ordered else 1
    copies = 6 + 4 * blocks + 2 * plan.zones + 1 + 2 * (plan.zones - 1)
    return pl.pallas_call(
        functools.partial(opening_kernel, plan),
        out_shape=outputs,
        in_specs=[vmem] * len(operands),
        out_specs=[vmem] * len(outputs),
        scratch_shapes=[
            pltpu.SemaphoreType.DMA((copies,)),
            pltpu.SemaphoreType.DMA((copies,)),
            pltpu.VMEM(out_grad.shape, out_grad.dtype),
        ],
        compiler_params=pltpu.CompilerParams(
            collective_id=number, has_side_effects=True, vmem_limit_bytes=56 * 2**20
        ),
        cost_estimate=pl.CostEstimate(flops=4 * 10**10, bytes_accessed=10**8, transcendentals=0),
        name="opening",
    )(*operands)


def inverse_rms(values):
    return lax.rsqrt(jnp.mean(values * values, -1, keepdims=True) + EPS_NORM)


def hidden_rows(own, sums, extras, outs):
    tokens, gain = extras
    hidden = tokens[own, :].astype(jnp.float32) + sums
    outs[0][own, :] = hidden
    return (hidden * inverse_rms(hidden) * gain[...]).astype(jnp.bfloat16)


def grad_hidden_rows(own, sums, extras, outs):
    hidden, out_grad, gain = extras
    values = hidden[own, :]
    factor = inverse_rms(values)
    unit = values * factor
    outs[1][...] += jnp.sum(sums * unit, 0, keepdims=True)
    grad = out_grad[own, :].astype(jnp.float32) + norm_back(sums * gain[...], unit, factor)
    outs[0][own, :] = grad
    return grad.astype(jnp.bfloat16)


def grad_input_rows(own, sums, extras, outs):
    tokens, grad_hidden, gain = extras[:3]
    values = tokens[own, :].astype(jnp.float32)
    factor = inverse_rms(values)
    unit = values * factor
    outs[0][...] += jnp.sum(sums * unit, 0, keepdims=True)
    return (grad_hidden[own, :] + norm_back(sums * gain[...], unit, factor)).astype(jnp.bfloat16)


def dot(left, right, left_dim=1, right_dim=0):
    return lax.dot_general(
        left, right, (((left_dim,), (right_dim,)), ((), ())), preferred_element_type=jnp.float32
    )


def turn_head(values, cosine, signed_sine):
    return values * cosine + pltpu.roll(values, HEAD // 2, 1) * signed_sine


def turn_back(gradient, cosine, signed_sine):
    return gradient * cosine + pltpu.roll(gradient * signed_sine, HEAD // 2, 1)


def softmax_block(query, key, first_row):
    rows, keys = query.shape[0], key.shape[0]
    scores = dot(query, key, 1, 1)
    row_at = lax.broadcasted_iota(jnp.int32, (rows, keys), 0) + first_row
    key_at = lax.broadcasted_iota(jnp.int32, (rows, keys), 1)
    scores = jnp.where(key_at <= row_at, scores, -1000000000.0)
    exponent = jnp.exp(scores - jnp.max(scores, -1, keepdims=True))
    return exponent / jnp.sum(exponent, -1, keepdims=True)


def eighth_owners():
    _, side, row, _ = place_here()
    own, off = (row, side), (1 - row, 1 - side)
    first = lambda x, y: x * 2 + y
    second = lambda x, y: 4 + y * 2 + x
    return [
        first(own[0], own[1]),
        first(own[0], off[1]),
        second(own[0], own[1]),
        second(off[0], own[1]),
        first(off[0], own[1]),
        first(off[0], off[1]),
        second(own[0], off[1]),
        second(off[0], off[1]),
    ]


def reorder_rows(source, target, into_local):
    size = source.shape[0] // 8
    for slot, owner in enumerate(eighth_owners()):
        natural = pl.ds(pl.multiple_of(owner * size, size), size)
        local = pl.ds(slot * size, size)
        if into_local:
            target[local, :] = source[natural, :]
        else:
            target[natural, :] = source[local, :]


def forward_kernel(
    tokens, weights, gain_in, gain_q, gain_k, cosine, sine,
    normed, raw, query, key, value, local, attended,
):
    low = jnp.bfloat16
    total, heads = tokens.shape[0], query.shape[1] // HEAD
    block = 256

    def project(step, carry):
        rows = pl.ds(pl.multiple_of(step * block, block), block)
        values = tokens[rows, :].astype(jnp.float32)
        normed[rows, :] = (values * inverse_rms(values) * gain_in[...]).astype(low)
        raw[rows, :] = dot(normed[rows, :], weights[...])
        turns = (cosine[rows, :], sine[rows, :])
        for head in range(heads):
            column = (head // 2) * 4 * HEAD + (head % 2) * HEAD
            values = raw[rows, pl.ds(column, HEAD)]
            values = turn_head(values * inverse_rms(values) * gain_q[...], *turns)
            query[rows, pl.ds(head * HEAD, HEAD)] = (values * (1.0 / math.sqrt(HEAD))).astype(low)
        for group in range(heads // 2):
            column = group * 4 * HEAD + 2 * HEAD
            here = pl.ds(group * HEAD, HEAD)
            values = raw[rows, pl.ds(column, HEAD)]
            values = turn_head(values * inverse_rms(values) * gain_k[...], *turns)
            key[rows, here] = values.astype(low)
            value[rows, here] = raw[rows, pl.ds(column + HEAD, HEAD)].astype(low)
        return carry

    lax.fori_loop(0, total // block, project, 0)

    def attend(head, carry):
        mine = pl.ds(pl.multiple_of(head * HEAD, HEAD), HEAD)
        shared = pl.ds(pl.multiple_of(lax.div(head, 2) * HEAD, HEAD), HEAD)
        for start in range(0, total, SEQ):
            for first in range(0, SEQ, block):
                rows, keys = pl.ds(start + first, block), pl.ds(start, first + block)
                probs = softmax_block(query[rows, mine], key[keys, shared], first)
                attended[rows, mine] = dot(probs.astype(low), value[keys, shared]).astype(low)
        return carry

    lax.fori_loop(0, heads, attend, 0)
    reorder_rows(attended, local, True)


def attention(tokens, weights, gain_in, gain_q, gain_k, cosine, sine):
    total = tokens.shape[0]
    columns = weights.shape[1]
    low = jnp.bfloat16
    shape = lambda width, kind=low: jax.ShapeDtypeStruct((total, width), kind)
    vmem = pl.BlockSpec(memory_space=pltpu.VMEM)
    return pl.pallas_call(
        forward_kernel,
        out_shape=[
            shape(tokens.shape[1]),
            shape(columns, jnp.float32),
            shape(columns // 2),
            shape(columns // 4),
            shape(columns // 4),
            shape(columns // 2),
        ],
        in_specs=[vmem] * 7,
        out_specs=[vmem] * 6,
        scratch_shapes=[pltpu.VMEM((total, columns // 2), low)],
        compiler_params=pltpu.CompilerParams(vmem_limit_bytes=48 * 2**20),
        cost_estimate=pl.CostEstimate(flops=10**10, bytes_accessed=2 * 10**7, transcendentals=0),
        name="attention",
    )(tokens, weights, gain_in, gain_q, gain_k, cosine, sine)


def backward_kernel(
    query, key, value, raw, grad_rows, gain_q, gain_k, cosine, sine,
    mixed, mixed_local, query_gain, key_gain, grad, key_sum, value_sum,
):
    low = jnp.bfloat16
    total, heads = query.shape[0], query.shape[1] // HEAD
    block = 256
    reorder_rows(grad_rows, grad, False)
    query_gain[...] = jnp.zeros_like(query_gain)
    key_gain[...] = jnp.zeros_like(key_gain)

    def head_norm_back(rows, column, gradient, gain, gain_grad):
        values = raw[rows, column]
        factor = inverse_rms(values)
        unit = values * factor
        turned = turn_back(gradient, cosine[rows, :], sine[rows, :])
        gain_grad[...] += jnp.sum(turned * unit, 0, keepdims=True)
        mixed[rows, column] = norm_back(turned * gain[...], unit, factor).astype(low)

    def one_group(group, carry):
        at = lambda offset: pl.ds(pl.multiple_of(group * 4 * HEAD + offset * HEAD, HEAD), HEAD)
        shared = pl.ds(pl.multiple_of(group * HEAD, HEAD), HEAD)
        key_sum[...] = jnp.zeros_like(key_sum)
        value_sum[...] = jnp.zeros_like(value_sum)
        for head in (0, 1):
            mine = pl.ds(pl.multiple_of((group * 2 + head) * HEAD, HEAD), HEAD)
            for start in range(0, total, SEQ):
                for first in range(0, SEQ, block):
                    rows, keys = pl.ds(start + first, block), pl.ds(start, first + block)
                    query_part, grad_part = query[rows, mine], grad[rows, mine]
                    probs = softmax_block(query_part, key[keys, shared], first)
                    weighed = probs * dot(grad_part, value[keys, shared], 1, 1)
                    scores = weighed - probs * jnp.sum(weighed, -1, keepdims=True)
                    scores = scores.astype(low)
                    grad_query = dot(scores, key[keys, shared]) * (1.0 / math.sqrt(HEAD))
                    head_norm_back(rows, at(head), grad_query, gain_q, query_gain)
                    key_sum[keys, :] += dot(scores, query_part, 0, 0)
                    value_sum[keys, :] += dot(probs.astype(low), grad_part, 0, 0)
        for first in range(0, total, block):
            rows = pl.ds(first, block)
            head_norm_back(rows, at(2), key_sum[rows, :], gain_k, key_gain)
            mixed[rows, at(3)] = value_sum[rows, :].astype(low)
        return carry

    lax.fori_loop(0, heads // 2, one_group, 0)
    reorder_rows(mixed, mixed_local, True)


def attention_back(query, key, value, raw, grad_rows, gain_q, gain_k, cosine, sine):
    total, columns = raw.shape
    low = jnp.bfloat16
    vmem = pl.BlockSpec(memory_space=pltpu.VMEM)
    return pl.pallas_call(
        backward_kernel,
        out_shape=[
            jax.ShapeDtypeStruct((total, columns), low),
            jax.ShapeDtypeStruct((total, columns), low),
            jax.ShapeDtypeStruct((1, HEAD), jnp.float32),
            jax.ShapeDtypeStruct((1, HEAD), jnp.float32),
        ],
        in_specs=[vmem] * 9,
        out_specs=[vmem] * 4,
        scratch_shapes=[
            pltpu.VMEM(grad_rows.shape, low),
            pltpu.VMEM((total, HEAD), jnp.float32),
            pltpu.VMEM((total, HEAD), jnp.float32),
        ],
        compiler_params=pltpu.CompilerParams(vmem_limit_bytes=48 * 2**20),
        cost_estimate=pl.CostEstimate(flops=10**10, bytes_accessed=2 * 10**7, transcendentals=0),
        name="attention_back",
    )(query, key, value, raw, grad_rows, gain_q, gain_k, cosine, sine)


def feed_kernel(rows, out_grad, gate_up, up_part, down, active, grads):
    low = jnp.bfloat16
    block = 256
    tile = down.shape[1]
    step = pl.program_id(0)
    gate_at = pl.ds(pl.multiple_of(step * tile, tile), tile)
    up_at = pl.ds(pl.multiple_of(grads.shape[1] // 2 + step * tile, tile), tile)

    def one(block_at, carry):
        here = pl.ds(pl.multiple_of(block_at * block, block), block)
        gate = dot(rows[here, :], gate_up[...])
        up = dot(rows[here, :], up_part[...])
        grad = dot(out_grad[here, :], down[...])
        sigmoid = jax.nn.sigmoid(gate)
        silu = gate * sigmoid
        active[here, :] = (silu * up).astype(low)
        grads[here, gate_at] = (grad * up * sigmoid * (1.0 + gate * (1.0 - sigmoid))).astype(low)
        grads[here, up_at] = (grad * silu).astype(low)
        return carry

    lax.fori_loop(0, rows.shape[0] // block, one, 0)


def feed_forward(rows, out_grad, gate_up, down, tile):
    total, width = rows.shape
    units = down.shape[1]
    low = jnp.bfloat16
    tiles = units // tile
    whole = pl.BlockSpec((total, width), lambda step: (0, 0))
    return pl.pallas_call(
        feed_kernel,
        grid=(tiles,),
        out_shape=[
            jax.ShapeDtypeStruct((total, units), low),
            jax.ShapeDtypeStruct((total, 2 * units), low),
        ],
        in_specs=[
            whole,
            whole,
            pl.BlockSpec((width, tile), lambda step: (0, step)),
            pl.BlockSpec((width, tile), lambda step: (0, step + tiles)),
            pl.BlockSpec((width, tile), lambda step: (0, step)),
        ],
        out_specs=[
            pl.BlockSpec((total, tile), lambda step: (0, step)),
            pl.BlockSpec((total, 2 * units), lambda step: (0, 0)),
        ],
        compiler_params=pltpu.CompilerParams(vmem_limit_bytes=56 * 2**20),
        cost_estimate=pl.CostEstimate(
            flops=6 * total * width * units, bytes_accessed=4 * 10**7, transcendentals=total * units
        ),
        name="feed_forward",
    )(rows, out_grad, gate_up, gate_up, down)


class Plan:
    def __init__(self, mesh):
        self.total = mesh.shape["dp"]
        self.zones = self.total // 2
        self.tensor = mesh.shape["tensor"]
        self.flips = [k ^ (k >> 1) for k in range(self.zones)]

    def place(self):
        self.index = lax.axis_index("dp")
        self.zone = self.index // 2
        self.side = self.index % 2
        self.row = lax.axis_index("tensor") // 2
        self.core = lax.axis_index("tensor") % 2
        self.home = self.side == self.core

    def move(self, value, target):
        pairs = []
        for d in range(self.total):
            for t in range(self.tensor):
                to = target(d // 2, d % 2, t // 2, t % 2)
                if to is not None:
                    zone, side, row, core = to
                    pairs.append((d * self.tensor + t, (zone * 2 + side) * self.tensor + row * 2 + core))
        return lax.ppermute(value, ("dp", "tensor"), pairs)

    def turn(self, value):
        got = self.move(value, lambda z, y, x, c: (z, c, x, y) if y != c else None)
        return jnp.where(self.home, value, got)

    def zone_flip(self, value, bit):
        return self.move(value, lambda z, y, x, c: (z ^ bit, y, x, c))

    def core_swap(self, value):
        return self.move(value, lambda z, y, x, c: (z, y, x, 1 - c))

    def side_swap(self, value):
        return self.move(value, lambda z, y, x, c: (z, 1 - y, x, c))

    def row_swap(self, value):
        return self.move(value, lambda z, y, x, c: (z, y, 1 - x, c))

    def to_local(self, value, axis):
        width = value.shape[axis] // self.total
        parts = []
        for core in (self.core, 1 - self.core):
            for slot in range(self.zones):
                owner = (self.zone ^ self.flips[slot]) * 2 + core
                parts.append(lax.dynamic_slice_in_dim(value, owner * width, width, axis))
        return jnp.concatenate(parts, axis)

    def to_natural(self, value, axis, core=None):
        core = self.core if core is None else core
        width = value.shape[axis] // self.total
        parts = []
        for block in range(self.total):
            slot = flip = (block // 2) ^ self.zone
            for bits in range(1, self.zones.bit_length()):
                slot = slot ^ (flip >> bits)
            slot = slot + jnp.where(block % 2 == core, 0, self.zones)
            parts.append(lax.dynamic_slice_in_dim(value, slot * width, width, axis))
        return jnp.concatenate(parts, axis)

    def row_owners(self):
        own, off = (self.row, self.side), (1 - self.row, 1 - self.side)
        first = lambda x, y: x * 2 + y
        second = lambda x, y: 4 + y * 2 + x
        return [
            first(own[0], own[1]),
            first(own[0], off[1]),
            second(own[0], own[1]),
            second(off[0], own[1]),
            first(off[0], own[1]),
            first(off[0], off[1]),
            second(own[0], off[1]),
            second(off[0], off[1]),
        ]

    def rows_local(self, value, slots=range(8)):
        size = value.shape[0] // 8
        owners = self.row_owners()
        return jnp.concatenate(
            [lax.dynamic_slice_in_dim(value, owners[slot] * size, size, 0) for slot in slots], 0
        )

    def rows_natural(self, value, order=range(8)):
        size = value.shape[0] // 8
        place = [list(order).index(slot) for slot in range(8)]
        parts = []
        for piece in range(8):
            x, y = (piece // 2, piece % 2) if piece < 4 else (piece % 2, (piece - 4) // 2)
            slots = (0, 1, 4, 5) if piece < 4 else (2, 6, 3, 7)
            same_x, same_y = x == self.row, y == self.side
            slot = jnp.where(
                same_x,
                jnp.where(same_y, place[slots[0]], place[slots[1]]),
                jnp.where(same_y, place[slots[2]], place[slots[3]]),
            )
            parts.append(lax.dynamic_slice_in_dim(value, slot * size, size, 0))
        return jnp.concatenate(parts, 0)

    def from_zones(self, shard):
        return [self.zone_flip(shard, flip) for flip in self.flips[1:]]

    def to_zones(self, parts, slots):
        return [self.zone_flip(parts[slot], self.flips[slot]) for slot in slots]

    def middle_swap(self, pair):
        return self.move(pair, lambda z, y, x, c: (z ^ 3, y, x, c) if z in (1, 2) else None)

    def pass_outward(self, pair):
        return self.move(pair, lambda z, y, x, c: (z ^ 1, y, x, c) if z in (1, 2) else None)

    def far_pair(self, middle, passed):
        inner = (self.zone == 1) | (self.zone == 2)
        return jnp.where(inner, middle, passed[::-1])

    def first_swap(self, send):
        half = send.shape[0] // 2
        return self.row_swap(send[:half]), self.side_swap(send[half:])

    def second_swap(self, keep, got):
        quarter = keep.shape[0] // 4
        row_part = keep[: 2 * quarter] + got[0].astype(jnp.float32)
        side_part = keep[2 * quarter :] + got[1].astype(jnp.float32)
        own = jnp.concatenate([row_part[:quarter], side_part[:quarter]], 0)
        return own, (
            self.side_swap(row_part[quarter:].astype(jnp.bfloat16)),
            self.row_swap(side_part[quarter:].astype(jnp.bfloat16)),
        )

    def spread_first(self, own):
        half = own.shape[0] // 2
        return (self.side_swap(own[:half]), self.row_swap(own[half:]))

    def spread_second(self, own, got):
        half = own.shape[0] // 2
        row_part = jnp.concatenate([own[:half], got[0]], 0)
        side_part = jnp.concatenate([own[half:], got[1]], 0)
        return row_part, side_part, self.row_swap(row_part), self.side_swap(side_part)

    def send_home(self, own):
        to_home = lambda z, y, x, c: (z, c, x, c) if y != c else None
        return jnp.concatenate([own, self.move(own, to_home)], 0)

    def row_home(self, part):
        return self.move(part, lambda z, y, x, c: (z, y, 1 - x, c) if y == c else None)

    def share_home(self, part, other):
        full = jnp.concatenate([part, other], 0)
        full = self.to_natural(self.rows_natural(full, (0, 2, 1, 6, 4, 3, 5, 7)), 1)
        got = self.move(full, lambda z, y, x, c: (z, y, x, 1 - c) if y == c else None)
        return full, got

    def turned(self, own, got):
        return jnp.where(self.home, own, got)

    def sum_everywhere(self, value):
        value = value + self.row_swap(value)
        value = value + self.side_swap(value)
        value = value + self.core_swap(value)
        bit = 1
        while bit < self.zones:
            value = value + self.zone_flip(value, bit)
            bit *= 2
        return value


def shards(
    plan,
    tokens,
    positions,
    out_grad,
    qkv_weight,
    qkv_first,
    qkv_second,
    out_weight,
    out_first,
    out_second,
    gate_up,
    gate_up_first,
    gate_up_second,
    down_weight,
    down_first,
    down_second,
    gains,
    gains_first,
    gains_second,
):
    plan.place()
    low = jnp.bfloat16
    tok_rows, model_width = tokens.shape
    groups = qkv_weight.shape[1]
    head_size = qkv_weight.shape[3]
    shard_rows = qkv_weight.shape[0]
    seq_count = tok_rows // SEQ
    mixed_cols = groups * 4 * head_size
    near_cols = model_width // 2
    kept = tok_rows // 2
    gain_count = gains.shape[0]

    tree = plan.zones == 4
    slots = range(1, plan.zones)

    def column_parts(value):
        return value.reshape((plan.zones, -1) + value.shape[1:])

    units = gate_up.shape[2]
    plan.ordered = (model_width // plan.total) % 128 == 0
    gain_rows = 16
    gain_block = jnp.pad(gains.astype(low), (0, gain_rows * 128 - gain_count)).reshape(gain_rows, 128)
    low_qkv = qkv_weight.reshape(shard_rows, mixed_cols).astype(low)
    tile = min(units, 256)
    low_gate = jnp.concatenate([gate_up[0].astype(low), gate_up[1].astype(low)], 1)
    angle_at = positions.astype(jnp.float32).reshape(-1, 128)
    (
        both_qkv,
        both_gains,
        turned_gate,
        turned_out,
        turned_down,
        tokens,
        angle_at,
        out_grad,
        partner_gate,
    ) = opening(
        plan,
        low_qkv,
        gain_block,
        low_gate,
        out_weight.astype(low),
        down_weight.astype(low),
        tokens,
        out_grad,
        angle_at,
        3,
    )
    positions = angle_at.reshape(-1)
    turned_out, turned_gate, turned_down, tokens, positions, both_qkv, both_gains, out_grad = fence(
        turned_out, turned_gate, turned_down, tokens, positions, both_qkv, both_gains, out_grad
    )

    zone_out = plan.from_zones(turned_out)
    if tree:
        partner_down = plan.zone_flip(turned_down, 1)
    else:
        partner_down = plan.from_zones(turned_down)
        partner_gate = plan.from_zones(turned_gate)
    if not plan.ordered:
        tokens = plan.to_local(tokens, 1)
        out_grad = plan.to_local(out_grad, 1)
    cosine, sine_table = rotary(positions, head_size)
    signed_sine = jnp.concatenate(
        [-sine_table[:, : head_size // 2], sine_table[:, head_size // 2 :]], 1
    )
    full_qkv = both_qkv.reshape(model_width, mixed_cols)
    gain_slots = both_gains.reshape(plan.total, -1)[:, :gain_count]
    gain_all = plan.to_natural(gain_slots.reshape(-1), 0).astype(jnp.float32)
    gain_in = plan.to_local(gain_all[:model_width], 0)[None]
    gain_post = plan.to_local(gain_all[model_width : 2 * model_width], 0)[None]
    gain_q = gain_all[2 * model_width : 2 * model_width + head_size][None]
    gain_k = gain_all[2 * model_width + head_size :][None]
    normed, raw, query, key_rot, values_low, attended = attention(
        tokens, full_qkv, gain_in, gain_q, gain_k, cosine, signed_sine
    )
    attended, zone_out, turned_out, partner_down, turned_down, turned_gate, partner_gate = fence(
        attended, zone_out, turned_out, partner_down, turned_down, turned_gate, partner_gate
    )

    near_out = jnp.concatenate([turned_out] + zone_out, 0)
    far_out = plan.core_swap(near_out)
    own_tokens = plan.rows_local(tokens, (0, 2))
    near_out, far_out, own_tokens, out_grad = fence(near_out, far_out, own_tokens, out_grad)

    full_out = jnp.concatenate([near_out, far_out], 0)
    branch_terms = contract_cols(attended, full_out).astype(low)
    pairs = [(turned_gate, partner_gate), (turned_down, partner_down)]
    normed_rows, hidden, *gathered = sum_rows(
        spread_kernel,
        hidden_rows,
        branch_terms,
        [own_tokens, gain_post],
        [jax.ShapeDtypeStruct((tok_rows // 4, model_width), jnp.float32)],
        0,
        [PairTree(pairs, (4, 2))] if tree else [],
    )
    if not tree:
        near = [jnp.concatenate([own] + rest, 0) for own, rest in pairs]
        gathered = [jnp.concatenate([part, plan.core_swap(part)], 0) for part in near]
    full_gate = gathered[0].reshape(model_width, 2 * units)
    full_down = gathered[1].reshape(model_width, units)
    normed_rows, hidden, full_gate, full_down, out_grad = fence(
        normed_rows, hidden, full_gate, full_down, out_grad
    )

    def zone_parts(near, got):
        both = (near + got.astype(jnp.float32)).astype(low)
        return both.reshape((plan.zones, -1) + both.shape[1:])

    def zone_total(parts, *arrived):
        total = parts[0].astype(jnp.float32)
        for part in sum([list(group) for group in arrived], []):
            total = total + part.astype(jnp.float32)
        return total.astype(low)

    active, grad_both = feed_forward(normed_rows, out_grad, full_gate, full_down, tile)
    down_far = contract_rows(out_grad[:, near_cols:], active).astype(low)
    down_far, active, grad_both = fence(down_far, active, grad_both)

    down_got = plan.core_swap(down_far)
    gate_far = contract_rows(normed_rows[:, near_cols:], grad_both).astype(low)
    down_parts = zone_parts(contract_rows(out_grad[:, :near_cols], active), down_got)
    down_parts, gate_far, grad_both = fence(down_parts, gate_far, grad_both)

    gate_got = plan.core_swap(gate_far)
    down_sent = plan.to_zones(down_parts, [slot for slot in slots if slot != 3])
    post_terms = contract_cols(grad_both, full_gate).astype(low)
    gate_parts = zone_parts(contract_rows(normed_rows[:, :near_cols], grad_both), gate_got)
    post_terms, gate_parts, down_parts, down_sent = fence(
        post_terms, gate_parts, down_parts, down_sent
    )

    eighth = tok_rows // 8
    own_grad = jnp.concatenate([out_grad[:eighth], out_grad[2 * eighth : 3 * eighth]], 0)
    branch_rows, grad_hidden, post_gain_grad, gate_sums = sum_rows(
        spread_kernel,
        grad_hidden_rows,
        post_terms,
        [hidden, own_grad, gain_post],
        [
            jax.ShapeDtypeStruct((tok_rows // 4, model_width), jnp.float32),
            jax.ShapeDtypeStruct((1, model_width), jnp.float32),
        ],
        1,
        [PairScatter(gate_parts, 4) if tree else ZoneBlocks(plan, gate_parts, slots)],
    )
    branch_rows, grad_hidden, post_gain_grad, gate_sums, active, hidden, down_parts, down_sent = fence(
        branch_rows, grad_hidden, post_gain_grad, gate_sums, active, hidden, down_parts, down_sent
    )

    if tree:
        gate_last = [plan.zone_flip(gate_sums[1], 1)]
        gate_own = gate_sums
    else:
        gate_last, gate_own = gate_sums, gate_parts
    mlp_terms = contract_cols(active, full_down).astype(low)
    mlp_got = plan.first_swap(mlp_terms[kept:])
    grad_att = jnp.dot(branch_rows, full_out, preferred_element_type=jnp.float32).astype(low)
    grad_mixed, mixed_rows, query_gain_grad, key_gain_grad = attention_back(
        query, key_rot, values_low, raw, grad_att, gain_q, gain_k, cosine, signed_sine
    )
    gain_terms = jnp.concatenate(
        [plan.to_natural(post_gain_grad, 1), query_gain_grad, key_gain_grad], 1
    )
    grad_mixed, mixed_rows, gain_terms, normed, gate_last, branch_rows, mlp_got, mlp_terms, down_parts = fence(
        grad_mixed, mixed_rows, gain_terms, normed, gate_last, branch_rows, mlp_got, mlp_terms, down_parts
    )

    down_last = plan.to_zones(down_parts, [3])
    mlp_own, mlp_last = plan.second_swap(mlp_terms[:kept].astype(jnp.float32), mlp_got)
    total_gate = zone_total(gate_own, gate_last)
    summed_gate = plan.turn(jnp.stack([total_gate[:, :units], total_gate[:, units:]]))
    out_far = contract_rows(branch_rows[:, near_cols:], attended).astype(low)
    out_got = plan.core_swap(out_far)
    qkv_far = contract_rows(normed[:, near_cols:], grad_mixed).astype(low)
    out_parts = zone_parts(contract_rows(branch_rows[:, :near_cols], attended), out_got)
    mlp_own, mlp_last, out_parts, qkv_far, grad_mixed, mixed_rows, summed_gate, down_last = fence(
        mlp_own, mlp_last, out_parts, qkv_far, grad_mixed, mixed_rows, summed_gate, down_last
    )

    block_own = (hidden + mlp_own + jnp.concatenate(mlp_last, 0).astype(jnp.float32)).astype(low)
    block_home = plan.send_home(block_own)
    qkv_got = plan.core_swap(qkv_far)
    summed_down = plan.turn(zone_total(down_parts, down_sent, down_last))
    normed_terms = contract_cols(mixed_rows, full_qkv).astype(low)
    block_home, qkv_got, normed_terms, summed_down = fence(
        block_home, qkv_got, normed_terms, summed_down
    )
    block_row = plan.row_home(block_home)
    qkv_parts = zone_parts(contract_rows(normed[:, :near_cols], grad_mixed), qkv_got)
    block_home, block_row, qkv_parts, normed_terms = fence(
        block_home, block_row, qkv_parts, normed_terms
    )

    gain_sum = GainSum(plan, gain_terms.shape[1], model_width) if plan.ordered else None
    input_full, input_gain_grad, *rest = sum_rows(
        home_kernel,
        grad_input_rows,
        normed_terms,
        [own_tokens, grad_hidden, gain_in] + ([gain_terms] if plan.ordered else []),
        [jax.ShapeDtypeStruct((1, model_width), jnp.float32)],
        2,
        [ZoneBlocks(plan, qkv_parts, slots), ZoneBlocks(plan, out_parts, slots)],
        gain_sum,
    )
    if plan.ordered:
        summed_gains, qkv_sent, out_sent = rest
    else:
        qkv_sent, out_sent = rest
        summed_gains = plan.sum_everywhere(
            jnp.concatenate([plan.to_natural(input_gain_grad, 1), gain_terms], 1)
        )
    input_full, summed_gains, qkv_sent, out_sent, block_home, block_row = fence(
        input_full, summed_gains, qkv_sent, out_sent, block_home, block_row
    )

    block_full, block_got = plan.share_home(block_home, block_row)
    summed_both = plan.turn(
        jnp.concatenate([zone_total(qkv_parts, qkv_sent), zone_total(out_parts, out_sent)], 1)
    ).astype(jnp.float32)
    summed_qkv = summed_both[:, :mixed_cols].reshape(qkv_weight.shape)
    summed_out = summed_both[:, mixed_cols:]
    summed_gate = summed_gate.astype(jnp.float32)
    summed_down = summed_down.astype(jnp.float32)
    summed_gains = lax.dynamic_slice_in_dim(summed_gains[0], plan.index * gain_count, gain_count, 0)
    block_out = jnp.where(plan.home, block_full, block_got)
    input_rows = plan.to_natural(input_full, 1, plan.side).astype(jnp.float32)

    qkv_moment, qkv_square, qkv_updated = adamw(
        qkv_weight, summed_qkv, qkv_first, qkv_second, RATE_QKV, DECAY_RATE
    )
    out_moment, out_square, out_updated = adamw(
        out_weight, summed_out, out_first, out_second, RATE_OUT, DECAY_RATE
    )
    gate_moment, gate_square, gate_updated = adamw(
        gate_up, summed_gate, gate_up_first, gate_up_second, RATE_GATE, DECAY_RATE
    )
    down_moment, down_square, down_updated = adamw(
        down_weight, summed_down, down_first, down_second, RATE_DOWN, DECAY_RATE
    )
    gain_moment, gain_square, gain_updated = adamw(
        gains, summed_gains, gains_first, gains_second, RATE_GAIN, 0.0
    )
    return (
        block_out,
        input_rows,
        qkv_moment,
        qkv_square,
        qkv_updated,
        out_moment,
        out_square,
        out_updated,
        gate_moment,
        gate_square,
        gate_updated,
        down_moment,
        down_square,
        down_updated,
        gain_moment,
        gain_square,
        gain_updated,
    )


def solution(mesh):
    plan = Plan(mesh)
    placed = (
        P("dp", None),
        P("dp"),
        P("dp", None),
        P("dp", "tensor", None, None),
        P("dp", "tensor", None, None),
        P("dp", "tensor", None, None),
        P("dp", "tensor"),
        P("dp", "tensor"),
        P("dp", "tensor"),
        P(None, "dp", "tensor"),
        P(None, "dp", "tensor"),
        P(None, "dp", "tensor"),
        P("dp", "tensor"),
        P("dp", "tensor"),
        P("dp", "tensor"),
        P("dp"),
        P("dp"),
        P("dp"),
    )
    return jax.shard_map(
        functools.partial(shards, plan),
        mesh=mesh,
        in_specs=placed,
        out_specs=(
            P("dp", None),
            P("dp", None),
            P("dp", "tensor", None, None),
            P("dp", "tensor", None, None),
            P("dp", "tensor", None, None),
            P("dp", "tensor"),
            P("dp", "tensor"),
            P("dp", "tensor"),
            P(None, "dp", "tensor"),
            P(None, "dp", "tensor"),
            P(None, "dp", "tensor"),
            P("dp", "tensor"),
            P("dp", "tensor"),
            P("dp", "tensor"),
            P("dp"),
            P("dp"),
            P("dp"),
        ),
        check_vma=False,
    )
```

```python
import functools
import math

import jax
import jax.numpy as jnp
from jax import lax
from jax.experimental import pallas as pl
from jax.experimental.pallas import tpu as pltpu
from jax.sharding import PartitionSpec as P

SEQ = 1024
STEP = 10


EPS_NORM = 1e-06
THETA = 1000000.0
BETA_ONE = 0.9
BETA_TWO = 0.95
ADAM_EPS = 1e-08
DECAY_RATE = 0.1
RATE_QKV = 0.05
RATE_OUT = 0.3
RATE_GATE = 0.05
RATE_DOWN = 0.03
RATE_GAIN = 1.0


def rotary(positions, head_size):
    freq_index = jnp.arange(head_size // 2, dtype=jnp.float32)
    inverse = jnp.exp(freq_index * (-2.0 * math.log(THETA) / head_size))
    angles = positions.astype(jnp.float32)[:, None] * inverse[None, :]
    cosine = jnp.cos(angles)
    sine_table = jnp.sin(angles)
    return (jnp.concatenate([cosine, cosine], -1), jnp.concatenate([sine_table, sine_table], -1))


def rotate(values, cosine, sine_table):
    half_size = values.shape[-1] // 2
    turned = jnp.concatenate([-values[..., half_size:], values[..., :half_size]], -1)
    return values * cosine[:, None, :] + turned * sine_table[:, None, :]


def unrotate(gradient, cosine, sine_table):
    half_size = gradient.shape[-1] // 2
    turned = gradient * sine_table[:, None, :]
    rotated_back = jnp.concatenate([turned[..., half_size:], -turned[..., :half_size]], -1)
    return gradient * cosine[:, None, :] + rotated_back


def norm_back(grad_unit, unit_vals, factor):
    return factor * (grad_unit - unit_vals * jnp.mean(grad_unit * unit_vals, -1, keepdims=True))


def contract_rows(left, right):
    return lax.dot_general(
        left, right, (((0,), (0,)), ((), ())), preferred_element_type=jnp.float32
    )


def contract_cols(left, right):
    return lax.dot_general(
        left, right, (((1,), (1,)), ((), ())), preferred_element_type=jnp.float32
    )


def block_scores(query_part, key_part, first_row, block_rows, last_row):
    scores = jnp.einsum(
        "nqkgd,nskd->nkgqs", query_part, key_part, preferred_element_type=jnp.float32
    )
    causal = (first_row + jnp.arange(block_rows))[:, None] >= jnp.arange(last_row)[None, :]
    return jnp.where(causal, scores, -1000000000.0)


def attention_forward(query, key_rot, values_low, seq_len):
    block_rows = min(512, seq_len)
    outputs = []
    log_sums = []
    for first_row in range(0, seq_len, block_rows):
        last_row = first_row + block_rows
        query_part = query[:, first_row:last_row]
        scores = block_scores(query_part, key_rot[:, :last_row], first_row, block_rows, last_row)
        row_max = jnp.max(scores, -1, keepdims=True)
        exponent = jnp.exp(scores - row_max)
        row_total = jnp.sum(exponent, -1, keepdims=True)
        probs_low = (exponent / row_total).astype(jnp.bfloat16)
        outputs.append(
            jnp.einsum(
                "nkgqs,nskd->nqkgd",
                probs_low,
                values_low[:, :last_row],
                preferred_element_type=jnp.float32,
            )
        )
        log_sums.append(row_max + jnp.log(row_total))
    return (jnp.concatenate(outputs, 1), log_sums)


def attention_backward(query, key_rot, values_low, grad_att, log_sums, seq_len):
    block_rows = min(512, seq_len)
    query_grads = []
    key_grad = jnp.zeros(key_rot.shape, jnp.float32)
    value_grad = jnp.zeros(values_low.shape, jnp.float32)
    for block_index, first_row in enumerate(range(0, seq_len, block_rows)):
        last_row = first_row + block_rows
        query_part = query[:, first_row:last_row]
        grad_part = grad_att[:, first_row:last_row]
        key_part = key_rot[:, :last_row]
        value_part = values_low[:, :last_row]
        scores = block_scores(query_part, key_part, first_row, block_rows, last_row)
        probs = jnp.exp(scores - log_sums[block_index])
        probs_low = probs.astype(jnp.bfloat16)
        grad_probs = jnp.einsum(
            "nqkgd,nskd->nkgqs", grad_part, value_part, preferred_element_type=jnp.float32
        )
        grad_scores = (
            probs * (grad_probs - jnp.sum(probs * grad_probs, -1, keepdims=True))
        ).astype(jnp.bfloat16)
        query_grads.append(
            jnp.einsum(
                "nkgqs,nskd->nqkgd", grad_scores, key_part, preferred_element_type=jnp.float32
            )
        )
        padding = ((0, 0), (0, seq_len - last_row), (0, 0), (0, 0))
        key_grad = key_grad + jnp.pad(
            jnp.einsum(
                "nkgqs,nqkgd->nskd", grad_scores, query_part, preferred_element_type=jnp.float32
            ),
            padding,
        )
        value_grad = value_grad + jnp.pad(
            jnp.einsum(
                "nkgqs,nqkgd->nskd", probs_low, grad_part, preferred_element_type=jnp.float32
            ),
            padding,
        )
    return (jnp.concatenate(query_grads, 1), key_grad, value_grad)


def adamw(weight, gradient, moment, second, step_rate, decay_rate):
    moment = BETA_ONE * moment + (1.0 - BETA_ONE) * gradient
    second = BETA_TWO * second + (1.0 - BETA_TWO) * gradient * gradient
    first_hat = moment / (1.0 - BETA_ONE**STEP)
    second_hat = second / (1.0 - BETA_TWO**STEP)
    weight = weight - step_rate * (
        first_hat / (jnp.sqrt(second_hat) + ADAM_EPS) + decay_rate * weight
    )
    return (moment, second, weight)


def fence(*values):
    return lax.optimization_barrier(values)


MESH = pl.DeviceIdType.MESH
HEAD = 128
AHEAD = 3


def place_here():
    index, place = lax.axis_index("dp"), lax.axis_index("tensor")
    return lax.div(index, 2), lax.rem(index, 2), lax.div(place, 2), lax.rem(place, 2)


def device(zone, side, row, core):
    return (zone * 2 + side, row * 2 + core)


def flipped(zone, flip):
    bit = 1
    while bit <= flip:
        if flip & bit:
            zone = zone + bit - 2 * bit * lax.rem(lax.div(zone, bit), 2)
        bit *= 2
    return zone


def greet(devices, amount=None):
    barrier = pltpu.get_barrier_semaphore()
    for peer in devices:
        pl.semaphore_signal(barrier, inc=1, device_id=peer, device_id_type=MESH)
    pl.semaphore_wait(barrier, len(devices) if amount is None else amount)


def for_rows(count, body):
    step = 32

    def one(block, carry):
        body(pl.multiple_of(block * step, step), step)
        return carry

    lax.fori_loop(0, count // step, one, 0)


class Copies:
    def __init__(self, send_sems, recv_sems):
        self.send_sems, self.recv_sems = send_sems, recv_sems
        self.number = 0

    def make(self, source, target, peer):
        number, self.number = self.number, self.number + 1
        return pltpu.make_async_remote_copy(
            src_ref=source,
            dst_ref=target,
            send_sem=self.send_sems.at[number],
            recv_sem=self.recv_sems.at[number],
            device_id=peer,
            device_id_type=MESH,
        )

    def start(self, source, target, peer):
        copy = self.make(source, target, peer)
        copy.start()
        return copy


class GainSum:
    def __init__(self, plan, rest, width):
        self.plan, self.width = plan, width
        self.total = width + rest
        self.scratch = [
            pltpu.VMEM((8, 1, self.total), jnp.float32),
            pltpu.VMEM((plan.zones, 1, self.total), jnp.float32),
        ]
        self.output = jax.ShapeDtypeStruct((1, self.total), jnp.float32)
        self.count = 7 + plan.zones - 1

    def plane_peers(self, zone, side, row, core):
        steps = [(s, r, c) for s in range(2) for r in range(2) for c in range(2)][1:]
        turn = lambda value, step: 1 - value if step else value
        return [device(zone, turn(side, s), turn(row, r), turn(core, c)) for s, r, c in steps]

    def zone_peers(self, zone, side, row, core):
        return {flip: device(flipped(zone, flip), side, row, core) for flip in self.plan.flips[1:]}

    def start(self, copies, rest, blocks, plane_sums, zone_sums):
        zone, side, row, core = place_here()
        plan = self.plan
        size = self.width // plan.total
        self.copies, self.plane_sums, self.zone_sums, self.zone = copies, plane_sums, zone_sums, zone
        here = side * 4 + row * 2 + core
        plane_sums[here, :, pl.ds(self.width, self.total - self.width)] = rest[...]
        for slot in range(plan.total):
            owner = flipped(zone, plan.flips[slot % plan.zones]) * 2
            owner = owner + (core if slot < plan.zones else 1 - core)
            spot = pl.ds(pl.multiple_of(owner * size, size), size)
            plane_sums[here, :, spot] = blocks[:, pl.ds(slot * size, size)]
        self.plane = [
            copies.start(plane_sums.at[here], plane_sums.at[here], peer)
            for peer in self.plane_peers(zone, side, row, core)
        ]

    def middle(self):
        for copy in self.plane:
            copy.wait_recv()
        total = self.plane_sums[0]
        for place in range(1, 8):
            total = total + self.plane_sums[place]
        self.zone_sums[self.zone] = total
        zone, side, row, core = place_here()
        self.across = [
            self.copies.start(self.zone_sums.at[self.zone], self.zone_sums.at[self.zone], peer)
            for peer in self.zone_peers(zone, side, row, core).values()
        ]

    def finish(self, out):
        for copy in self.across:
            copy.wait_recv()
        total = self.zone_sums[0]
        for place in range(1, self.plan.zones):
            total = total + self.zone_sums[place]
        out[...] = total
        for copy in self.plane + self.across:
            copy.wait_send()


class ZoneBlocks:
    scratch = []

    def __init__(self, plan, source, slots, begin=0):
        self.flips, self.slots, self.sources, self.begin = plan.flips, list(slots), [source], begin
        self.outputs = [
            jax.ShapeDtypeStruct((len(self.slots),) + source.shape[1:], source.dtype)
        ]
        self.count, self.count_local = len(self.slots), 0
        self.in_hbm = False

    def peers(self, zone, side, row, core):
        return {
            self.flips[slot]: device(flipped(zone, self.flips[slot]), side, row, core)
            for slot in self.slots
        }

    def start(self, copies, local_sems, sources, targets, stages):
        zone, side, row, core = place_here()
        self.started = [
            copies.make(
                sources[0].at[slot],
                targets[0].at[number],
                device(flipped(zone, self.flips[slot]), side, row, core),
            )
            for number, slot in enumerate(self.slots)
        ]
        self.waiting = True
        if self.begin == 0:
            self.pump([0])

    def pump(self, steps):
        if self.waiting and self.begin in steps:
            self.waiting = False
            for copy in self.started:
                copy.start()

    def finish(self):
        for copy in self.started:
            copy.wait_send()
        for copy in self.started:
            copy.wait_recv()


def inner_zone(zone):
    return lax.rem(lax.div(zone + 1, 2), 2)


class PairScatter:
    def __init__(self, parts, pieces):
        self.sources, self.pieces = [parts], pieces
        _, rows, columns = parts.shape
        self.size = rows // pieces
        self.outputs = [jax.ShapeDtypeStruct((2, rows, columns), parts.dtype)]
        self.scratch = [pltpu.VMEM((2, rows, columns), parts.dtype)] * 2
        self.count, self.count_local = 4 * pieces, 0
        self.in_hbm = False

    def peers(self, zone, side, row, core):
        return {
            1: device(flipped(zone, 1), side, row, core),
            3: device(flipped(zone, 3), side, row, core),
        }

    def start(self, copies, local_sems, sources, targets, stages):
        zone, side, row, core = place_here()
        self.parts, self.out = sources[0], targets[0]
        self.inward, self.crossed = stages
        inner_peer = device(flipped(zone, 3), side, row, core)
        outer_peer = device(flipped(zone, 1), side, row, core)
        self.inner = inner_zone(zone) == 1
        self.outer = inner_zone(zone) == 0
        self.steps = [
            (slot, pl.ds(piece * self.size, self.size))
            for piece in range(self.pieces)
            for slot in (0, 1)
        ]
        self.to_inner = [
            copies.make(self.parts.at[3 - slot, rows], self.inward.at[slot, rows], outer_peer)
            for slot, rows in self.steps
        ]
        self.across = [
            copies.make(self.inward.at[slot, rows], self.crossed.at[slot, rows], inner_peer)
            for slot, rows in self.steps
        ]

        @pl.when(self.outer)
        def _():
            for copy in self.to_inner[:AHEAD]:
                copy.start()

    def add(self, target, slot, rows, left, right):
        def some(row, count):
            here = pl.ds(rows.start + row, count)
            both = left[here, :].astype(jnp.float32) + right[here, :].astype(jnp.float32)
            target.at[slot][here, :] = both.astype(jnp.bfloat16)

        for_rows(self.size, some)

    def pump(self, steps):
        steps = [step for step in steps if step < len(self.steps)]

        @pl.when(self.inner)
        def _():
            for step in steps:
                slot, rows = self.steps[step]
                self.to_inner[step].wait_recv()
                self.add(self.inward, slot, rows, self.parts.at[2 + slot], self.inward.at[slot])
                self.across[step].start()

        @pl.when(self.outer)
        def _():
            for step in steps:
                self.to_inner[step].wait_send()
                for copy in self.to_inner[step + AHEAD : step + AHEAD + 1]:
                    copy.start()

    def finish(self):
        @pl.when(self.inner)
        def _():
            for step, (slot, rows) in enumerate(self.steps):
                self.across[step].wait_recv()
                self.add(self.out, slot, rows, self.parts.at[slot], self.crossed.at[slot])
            for copy in self.across:
                copy.wait_send()

        @pl.when(self.outer)
        def _():
            for slot in (0, 1):

                def some(row, count, slot=slot):
                    here = pl.ds(row, count)
                    self.out.at[slot][here, :] = self.parts.at[slot][here, :]

                for_rows(self.parts.shape[1], some)


class PairTree:
    def __init__(self, pairs, pieces):
        self.sources = [shard for pair in pairs for shard in pair]
        self.pieces = pieces
        self.outputs = [
            jax.ShapeDtypeStruct((8,) + own.shape, own.dtype) for own, _ in pairs
        ]
        self.count = 6 * sum(pieces) + 2 * len(pairs)
        self.count_local = 2 * len(pairs) + 2 * sum(pieces)
        self.scratch = [pltpu.VMEM((2,) + own.shape, own.dtype) for own, _ in pairs]
        self.in_hbm = True

    def peers(self, zone, side, row, core):
        return {
            1: device(flipped(zone, 1), side, row, core),
            3: device(flipped(zone, 3), side, row, core),
            "core": device(zone, side, row, 1 - core),
        }

    def start(self, copies, local_sems, sources, targets, stages):
        zone, side, row, core = place_here()
        inner_peer = device(flipped(zone, 3), side, row, core)
        outer_peer = device(flipped(zone, 1), side, row, core)
        core_peer = device(zone, side, row, 1 - core)
        self.inner = inner_zone(zone) == 1
        self.outer = inner_zone(zone) == 0
        self.across, self.onward, self.late, self.place = [], [], [], []
        self.shared, self.kept = [], []
        sem = 0
        for weight, full in enumerate(targets):
            pair, landing = sources[2 * weight : 2 * weight + 2], stages[weight]
            size = pair[0].shape[0] // self.pieces[weight]
            for piece in range(self.pieces[weight]):
                rows = pl.ds(piece * size, size)
                for slot in (0, 1):
                    here = landing.at[slot, rows]
                    self.across.append(copies.make(pair[slot].at[rows], here, inner_peer))
                    self.onward.append(copies.make(here, landing.at[1 - slot, rows], outer_peer))
                    self.late.append(copies.make(here, full.at[6 + slot, rows], core_peer))
                    self.place.append(
                        pltpu.make_async_copy(here, full.at[2 + slot, rows], local_sems.at[sem])
                    )
                    sem += 1
            for slot in (0, 1):
                self.shared.append(copies.make(pair[slot], full.at[4 + slot], core_peer))
                self.kept.append(
                    pltpu.make_async_copy(pair[slot], full.at[slot], local_sems.at[sem])
                )
                sem += 1

        @pl.when(self.inner)
        def _():
            for copy in self.across[:AHEAD]:
                copy.start()

    def pump(self, steps):
        steps = [step for step in steps if step < len(self.across)]

        @pl.when(self.inner)
        def _():
            for step in steps:
                self.across[step].wait_recv()
                for copy in self.across[step + AHEAD : step + AHEAD + 1]:
                    copy.start()
                self.onward[step].start()
                self.late[step].start()
                self.place[step].start()

        for copy in self.shared + self.kept if 3 in steps else []:
            copy.start()

    def finish(self):
        @pl.when(self.inner)
        def _():
            for copy in self.across + self.onward:
                copy.wait_send()

        @pl.when(self.outer)
        def _():
            for number, copy in enumerate(self.onward):
                copy.wait_recv()
                arrived = number + 1 - 2 * (number % 2)
                self.late[arrived].start()
                self.place[arrived].start()

        for copy in self.kept + self.place:
            copy.wait()
        for copy in self.shared + self.late:
            copy.wait_send()
        for copy in self.shared + self.late:
            copy.wait_recv()


def sum_eighths(
    copies, row_peer, side_peer, send, keep, forward, first, second, store, begin, pump
):
    size = send.shape[0] // 4
    part = lambda ref, slot: ref.at[pl.ds(slot * size, size)]
    arrivals = [
        copies.start(part(send, 1), part(first, 1), row_peer),
        copies.start(part(send, 3), part(first, 3), side_peer),
        copies.start(part(send, 0), part(first, 0), row_peer),
        copies.start(part(send, 2), part(first, 2), side_peer),
    ]
    begin()
    passed = []
    for number, slot, peer in ((0, 1, side_peer), (1, 3, row_peer)):
        arrivals[number].wait_recv()

        def add(row, count, number=number, slot=slot):
            here = pl.ds(slot * size + row, count)
            both = keep[here, :].astype(jnp.float32) + first[here, :].astype(jnp.float32)
            forward[pl.ds(number * size + row, count), :] = both.astype(jnp.bfloat16)

        for_rows(size, add)
        passed.append(copies.start(part(forward, number), part(second, number), peer))
    pump([0, 1, 2])
    for number, slot in ((0, 0), (1, 2)):
        arrivals[2 + number].wait_recv()
        passed[number].wait_recv()

        def total(row, count, number=number, slot=slot):
            here = pl.ds(slot * size + row, count)
            sums = keep[here, :].astype(jnp.float32) + first[here, :].astype(jnp.float32)
            sums = sums + second[pl.ds(number * size + row, count), :].astype(jnp.float32)
            store(number, row, count, sums)

        for_rows(size, total)
        yield number
    for copy in arrivals + passed:
        copy.wait_send()


def halves(terms):
    rows = terms.shape[0] // 2
    return terms.at[pl.ds(0, rows)], terms.at[pl.ds(rows, rows)]


def split_refs(refs, jobs, extra_count, out_count):
    refs = list(refs)
    take = lambda count: [refs.pop(0) for _ in range(count)]
    extras = take(extra_count)
    sources = [take(len(job.sources)) for job in jobs]
    full = take(1)[0]
    outs = take(out_count)
    targets = [take(len(job.outputs)) for job in jobs]
    return extras, sources, full, outs, targets, refs


def spread_kernel(middle, jobs, extra_count, out_count, gain_sum, terms, *refs):
    keep, send = halves(terms)
    extras, sources, full, outs, targets, scratch = split_refs(refs, jobs, extra_count, out_count)
    forward, first, second, send_sems, recv_sems, local_sems, *stages = scratch
    zone, side, row, core = place_here()
    row_peer, side_peer = device(zone, side, 1 - row, core), device(zone, 1 - side, row, core)
    copies = Copies(send_sems, recv_sems)
    size = send.shape[0] // 4
    part = lambda slot: full.at[pl.ds(slot * size, size)]
    for out in outs:
        if out.shape[0] == 1:
            out[...] = jnp.zeros_like(out)
    peers = {}
    for job in jobs:
        peers.update(job.peers(zone, side, row, core))
    greet([row_peer, side_peer] + list(peers.values()))

    def begin():
        spot = 0
        for job, source, target in zip(jobs, sources, targets):
            own_stages = stages[spot : spot + len(job.scratch)]
            job.start(copies, local_sems, source, target, own_stages)
            spot += len(job.scratch)

    def pump(steps):
        for job in jobs:
            job.pump(steps)

    def store(number, row, count, sums):
        own = pl.ds(number * size + row, count)
        full[pl.ds(2 * number * size + row, count), :] = middle(own, sums, extras, outs)

    firsts, seconds = [], []
    for number in sum_eighths(
        copies, row_peer, side_peer, send, keep, forward, first, second, store, begin, pump
    ):
        near, other = (side_peer, row_peer) if number == 0 else (row_peer, side_peer)
        slot = 2 * number
        firsts.append(copies.start(part(slot), part(slot + 1), near))
        seconds.append(copies.start(part(slot), part(4 + slot), other))
    pump([3])
    firsts[0].wait_recv()
    seconds.append(copies.start(part(1), part(5), row_peer))
    firsts[1].wait_recv()
    seconds.append(copies.start(part(3), part(7), side_peer))
    pump(range(4, 64))
    for copy in seconds:
        copy.wait_recv()
    for copy in firsts + seconds:
        copy.wait_send()
    for job in jobs:
        job.finish()


def home_kernel(middle, jobs, extra_count, out_count, gain_sum, terms, *refs):
    keep, send = halves(terms)
    extras, sources, full, outs, targets, scratch = split_refs(refs, jobs, extra_count, out_count)
    forward, first, second, own, send_sems, recv_sems, local_sems, *gain_scratch = scratch
    zone, side, row, core = place_here()
    row_peer, side_peer = device(zone, side, 1 - row, core), device(zone, 1 - side, row, core)
    core_peer = device(zone, side, row, 1 - core)
    copies = Copies(send_sems, recv_sems)
    size = send.shape[0] // 4
    at_home = side == core
    away = side != core
    for out in outs:
        if out.shape[0] == 1:
            out[...] = jnp.zeros_like(out)
    peers = {}
    for job in jobs:
        peers.update(job.peers(zone, side, row, core))
    plane = [row_peer, side_peer, core_peer]
    if gain_sum is not None:
        plane = gain_sum.plane_peers(zone, side, row, core)
        peers.update(gain_sum.zone_peers(zone, side, row, core))
    greet(plane + list(peers.values()))

    def begin():
        for job, source, target in zip(jobs, sources, targets):
            job.start(copies, local_sems, source, target, [])

    def pump(steps):
        for job in jobs:
            job.pump(steps)

    def store(number, start, count, sums):
        here = pl.ds(number * size + start, count)
        values = middle(here, sums, extras, outs)
        own[here, :] = values
        eighth = row * 2 + side if number == 0 else 4 + side * 2 + row

        @pl.when(at_home)
        def _():
            full[pl.ds(pl.multiple_of(eighth * size + start, 32), count), :] = values

    for _ in sum_eighths(
        copies, row_peer, side_peer, send, keep, forward, first, second, store, begin, pump
    ):
        pass
    pump([3])

    def piece(number, x, y):
        start = (x * 2 + y) * size if number == 0 else (4 + y * 2 + x) * size
        return full.at[pl.ds(pl.multiple_of(start, size), size)]

    mine = lambda number: own.at[pl.ds(number * size, size)]
    both = (0, 1)
    to_side = [copies.make(mine(k), piece(k, row, side), side_peer) for k in both]
    to_row = [copies.make(mine(k), piece(k, row, side), row_peer) for k in both]
    pass_row = [
        copies.make(piece(k, row, 1 - side), piece(k, row, 1 - side), row_peer) for k in both
    ]
    share = []
    for number, (x, y) in enumerate(
        ((row, side), (row, 1 - side), (1 - row, side), (1 - row, 1 - side))
    ):
        for k in both:
            source = mine(k) if number == 0 else piece(k, x, y)
            share.append(copies.make(source, piece(k, x, y), core_peer))

    if gain_sum is not None:
        gain_sum.start(copies, extras[-1], outs[0], *gain_scratch)

    @pl.when(away)
    def _():
        for copy in to_side:
            copy.start()

    @pl.when(at_home)
    def _():
        for copy in to_row + share[:2]:
            copy.start()

    if gain_sum is not None:
        gain_sum.middle()

    @pl.when(away)
    def _():
        for copy in to_side:
            copy.wait_send()
        for copy in share:
            copy.wait_recv()

    @pl.when(at_home)
    def _():
        for k in both:
            to_side[k].wait_recv()
            pass_row[k].start()
            share[2 + k].start()
        for k, copy in enumerate(to_row + pass_row):
            copy.wait_recv()
            share[4 + k].start()
        for copy in to_row + pass_row + share:
            copy.wait_send()

    if gain_sum is not None:
        gain_sum.finish(outs[-1])
    for job in jobs:
        job.finish()


def sum_rows(kernel, middle, terms, extras, outs, number, jobs=(), gain_sum=None):
    half, width = terms.shape[0] // 2, terms.shape[1]
    eighth = half // 4
    low = jnp.bfloat16
    vmem, hbm = pl.BlockSpec(memory_space=pltpu.VMEM), pl.BlockSpec(memory_space=pl.ANY)
    scratch = [
        pltpu.VMEM((2 * eighth, width), low),
        pltpu.VMEM((half, width), low),
        pltpu.VMEM((2 * eighth, width), low),
    ]
    if kernel is home_kernel:
        scratch.append(pltpu.VMEM((2 * eighth, width), low))
    copies = (12 if kernel is spread_kernel else 20) + sum(job.count for job in jobs)
    local = max([2] + [job.count_local for job in jobs])
    if gain_sum is not None:
        copies += gain_sum.count
        outs = outs + [gain_sum.output]
    scratch += [pltpu.SemaphoreType.DMA((count,)) for count in (copies, copies, local)]
    if gain_sum is not None:
        scratch += gain_sum.scratch
    scratch += [stage for job in jobs for stage in job.scratch]
    sources = [source for job in jobs for source in job.sources]
    targets = [target for job in jobs for target in job.outputs]
    return pl.pallas_call(
        functools.partial(kernel, middle, jobs, len(extras), len(outs), gain_sum),
        out_shape=[jax.ShapeDtypeStruct((2 * half, width), low)] + outs + targets,
        in_specs=[vmem] * (1 + len(extras) + len(sources)),
        out_specs=[vmem] * (1 + len(outs))
        + [hbm if job.in_hbm else vmem for job in jobs for _ in job.outputs],
        scratch_shapes=scratch,
        compiler_params=pltpu.CompilerParams(
            collective_id=number, has_side_effects=True, vmem_limit_bytes=56 * 2**20
        ),
        cost_estimate=pl.CostEstimate(flops=4 * 10**10, bytes_accessed=10**8, transcendentals=0),
        name=middle.__name__,
    )(terms, *extras, *sources)


def copy_rows(source, target):
    def some(row, count):
        target[pl.ds(row, count), :] = source[pl.ds(row, count), :]

    if source.shape[0] % 32:
        target[...] = source[...]
    else:
        for_rows(source.shape[0], some)


def opening_kernel(plan, qkv, gains, gate, out, down, tokens, out_grad, angles, *refs):
    qkv_full, gains_full, turned_gate, turned_out, turned_down, turned_tokens, turned_angles = refs[:7]
    rows_grad, partner_gate, send_sems, recv_sems, tokens_stage, grad_stage = refs[7:]
    zone, side, row, core = place_here()
    partner = device(zone, core, row, side)
    row_peer, core_peer = device(zone, side, 1 - row, core), device(zone, side, row, 1 - core)
    zone_peers = [device(flipped(zone, flip), side, row, core) for flip in plan.flips[1:]]
    at_home, away = side == core, side != core
    always = [row_peer, core_peer] + zone_peers

    @pl.when(at_home)
    def _():
        greet(always)

    @pl.when(away)
    def _():
        greet(always + [partner])

    copies = Copies(send_sems, recv_sems)
    zones = plan.zones
    own = (gains, qkv, angles, gate, out, down)
    ends = (gains_full.at[0], qkv_full.at[0], turned_angles, turned_gate, turned_out, turned_down)
    turn = [copies.make(source, target, partner) for source, target in zip(own, ends)]
    size = tokens.shape[0] // 4
    moved = [
        (source, stage, pl.ds(pl.multiple_of((row * 2 + piece) * size, size), size))
        for source, stage in ((out_grad, grad_stage), (tokens, tokens_stage))
        for piece in (0, 1)
    ]
    turn_rows = [copies.make(a.at[spot], b.at[spot], partner) for a, b, spot in moved]
    pass_rows = [copies.make(b.at[spot], b.at[spot], row_peer) for _, b, spot in moved]
    width = tokens.shape[1] // plan.total if plan.ordered else tokens.shape[1]
    natural = [pl.ds(0, width)]
    if plan.ordered:
        owners = [
            flipped(zone, plan.flips[slot % zones]) * 2 + (core if slot < zones else 1 - core)
            for slot in range(plan.total)
        ]
        natural = [pl.ds(pl.multiple_of(owner * width, width), width) for owner in owners]
    local = [pl.ds(slot * width, width) for slot in range(len(natural))]

    def lay_down(all_tokens, all_grad):
        def some(start, count):
            here = pl.ds(start, count)
            for a, b in zip(natural, local):
                turned_tokens[here, b] = all_tokens[here, a]

        for_rows(all_tokens.shape[0], some)
        eighth = all_grad.shape[0] // 8
        for slot, owner in enumerate(eighth_owners()):

            def some(start, count, slot=slot, owner=owner):
                here = pl.ds(pl.multiple_of(owner * eighth + start, 32), count)
                there = pl.ds(slot * eighth + start, count)
                for a, b in zip(natural, local):
                    rows_grad[there, b] = all_grad[here, a]

            for_rows(eighth, some)

    slots = list(range(1, zones))
    weights = ((gains, gains_full), (qkv, qkv_full))
    from_own = [
        [copies.make(source, full.at[slot], zone_peers[slot - 1]) for slot in slots]
        + [copies.make(source, full.at[zones], core_peer)]
        for source, full in weights
    ] + [[copies.make(gate, partner_gate, zone_peers[0])]]
    copies.number -= 2 * zones + 1
    from_turned = [
        [copies.make(full.at[0], full.at[slot], zone_peers[slot - 1]) for slot in slots]
        + [copies.make(full.at[0], full.at[zones], core_peer)]
        for _, full in weights
    ] + [[copies.make(turned_gate, partner_gate, zone_peers[0])]]
    cross = [
        [copies.make(full.at[slot], full.at[zones + slot], core_peer) for slot in slots]
        for _, full in weights
    ]

    def cross_over(k):
        for which in (0, 1):
            from_turned[which][k].wait_recv()
            cross[which][k].start()

    @pl.when(away)
    def _():
        for copy in turn[:3]:
            copy.start()
        for which in (0, 1):
            turn[which].wait_recv()
            for copy in from_turned[which]:
                copy.start()
        turn[3].start()
        turn_rows[0].start()
        turn[3].wait_recv()
        from_turned[2][0].start()
        turn_rows[1].start()
        cross_over(0)
        for k in range(4):
            turn_rows[k].wait_recv()
            pass_rows[k].start()
            for copy in turn_rows[k + 2 : k + 3] + (turn[4:] if k == 2 else []):
                copy.start()

    @pl.when(at_home)
    def _():
        for copy in from_own[0] + from_own[1] + from_own[2]:
            copy.start()
        for source, target in zip(own, ends):
            copy_rows(source, target)
        lay_down(tokens, out_grad)
        cross_over(0)

    for k in range(1, zones - 1):
        cross_over(k)
    for which in (0, 1):
        from_turned[which][zones - 1].wait_recv()
        for copy in from_turned[which]:
            copy.wait_send()
        for copy in cross[which]:
            copy.wait_recv()
            copy.wait_send()
    from_turned[2][0].wait_recv()
    from_turned[2][0].wait_send()

    @pl.when(away)
    def _():
        for copy in pass_rows + turn[2:3] + turn[4:]:
            copy.wait_recv()
        lay_down(tokens_stage, grad_stage)
        for copy in turn + turn_rows + pass_rows:
            copy.wait_send()


def opening(plan, qkv, gains, gate, out, down, tokens, out_grad, angles, number):
    vmem = pl.BlockSpec(memory_space=pltpu.VMEM)
    like = lambda v: jax.ShapeDtypeStruct(v.shape, v.dtype)
    whole = lambda v: jax.ShapeDtypeStruct((2 * plan.zones,) + v.shape, v.dtype)
    operands = (qkv, gains, gate, out, down, tokens, out_grad, angles)
    outputs = [whole(qkv), whole(gains)] + [like(v) for v in (gate, out, down, tokens, angles)]
    outputs += [like(out_grad), like(gate)]
    copies = 6 + 8 + 2 * plan.zones + 1 + 2 * (plan.zones - 1)
    return pl.pallas_call(
        functools.partial(opening_kernel, plan),
        out_shape=outputs,
        in_specs=[vmem] * len(operands),
        out_specs=[vmem] * len(outputs),
        scratch_shapes=[
            pltpu.SemaphoreType.DMA((copies,)),
            pltpu.SemaphoreType.DMA((copies,)),
            pltpu.VMEM(tokens.shape, tokens.dtype),
            pltpu.VMEM(out_grad.shape, out_grad.dtype),
        ],
        compiler_params=pltpu.CompilerParams(
            collective_id=number, has_side_effects=True, vmem_limit_bytes=56 * 2**20
        ),
        cost_estimate=pl.CostEstimate(flops=4 * 10**10, bytes_accessed=10**8, transcendentals=0),
        name="opening",
    )(*operands)


def inverse_rms(values):
    return lax.rsqrt(jnp.mean(values * values, -1, keepdims=True) + EPS_NORM)


def hidden_rows(own, sums, extras, outs):
    tokens, gain = extras
    hidden = tokens[own, :].astype(jnp.float32) + sums
    outs[0][own, :] = hidden
    return (hidden * inverse_rms(hidden) * gain[...]).astype(jnp.bfloat16)


def grad_hidden_rows(own, sums, extras, outs):
    hidden, out_grad, gain = extras
    values = hidden[own, :]
    factor = inverse_rms(values)
    unit = values * factor
    outs[1][...] += jnp.sum(sums * unit, 0, keepdims=True)
    grad = out_grad[own, :].astype(jnp.float32) + norm_back(sums * gain[...], unit, factor)
    outs[0][own, :] = grad
    return grad.astype(jnp.bfloat16)


def grad_input_rows(own, sums, extras, outs):
    tokens, grad_hidden, gain = extras[:3]
    values = tokens[own, :].astype(jnp.float32)
    factor = inverse_rms(values)
    unit = values * factor
    outs[0][...] += jnp.sum(sums * unit, 0, keepdims=True)
    return (grad_hidden[own, :] + norm_back(sums * gain[...], unit, factor)).astype(jnp.bfloat16)


def dot(left, right, left_dim=1, right_dim=0):
    return lax.dot_general(
        left, right, (((left_dim,), (right_dim,)), ((), ())), preferred_element_type=jnp.float32
    )


def turn_head(values, cosine, signed_sine):
    return values * cosine + pltpu.roll(values, HEAD // 2, 1) * signed_sine


def turn_back(gradient, cosine, signed_sine):
    return gradient * cosine + pltpu.roll(gradient * signed_sine, HEAD // 2, 1)


def softmax_block(query, key, first_row):
    rows, keys = query.shape[0], key.shape[0]
    scores = dot(query, key, 1, 1)
    row_at = lax.broadcasted_iota(jnp.int32, (rows, keys), 0) + first_row
    key_at = lax.broadcasted_iota(jnp.int32, (rows, keys), 1)
    scores = jnp.where(key_at <= row_at, scores, -1000000000.0)
    exponent = jnp.exp(scores - jnp.max(scores, -1, keepdims=True))
    return exponent / jnp.sum(exponent, -1, keepdims=True)


def eighth_owners():
    _, side, row, _ = place_here()
    own, off = (row, side), (1 - row, 1 - side)
    first = lambda x, y: x * 2 + y
    second = lambda x, y: 4 + y * 2 + x
    return [
        first(own[0], own[1]),
        first(own[0], off[1]),
        second(own[0], own[1]),
        second(off[0], own[1]),
        first(off[0], own[1]),
        first(off[0], off[1]),
        second(own[0], off[1]),
        second(off[0], off[1]),
    ]


def reorder_rows(source, target, into_local):
    size = source.shape[0] // 8
    for slot, owner in enumerate(eighth_owners()):
        natural = pl.ds(pl.multiple_of(owner * size, size), size)
        local = pl.ds(slot * size, size)
        if into_local:
            target[local, :] = source[natural, :]
        else:
            target[natural, :] = source[local, :]


def forward_kernel(
    tokens, weights, gain_in, gain_q, gain_k, cosine, sine,
    normed, raw, query, key, value, local, attended,
):
    low = jnp.bfloat16
    total, heads = tokens.shape[0], query.shape[1] // HEAD
    block, wide = 256, 512

    def project(step, carry):
        rows = pl.ds(pl.multiple_of(step * wide, wide), wide)
        values = tokens[rows, :].astype(jnp.float32)
        normed[rows, :] = (values * inverse_rms(values) * gain_in[...]).astype(low)
        raw[rows, :] = dot(normed[rows, :], weights[...])
        turns = (cosine[rows, :], sine[rows, :])
        for head in range(heads):
            column = (head // 2) * 4 * HEAD + (head % 2) * HEAD
            values = raw[rows, pl.ds(column, HEAD)]
            values = turn_head(values * inverse_rms(values) * gain_q[...], *turns)
            query[rows, pl.ds(head * HEAD, HEAD)] = (values * (1.0 / math.sqrt(HEAD))).astype(low)
        for group in range(heads // 2):
            column = group * 4 * HEAD + 2 * HEAD
            here = pl.ds(group * HEAD, HEAD)
            values = raw[rows, pl.ds(column, HEAD)]
            values = turn_head(values * inverse_rms(values) * gain_k[...], *turns)
            key[rows, here] = values.astype(low)
            value[rows, here] = raw[rows, pl.ds(column + HEAD, HEAD)].astype(low)
        return carry

    lax.fori_loop(0, total // wide, project, 0)

    def attend(head, carry):
        mine = pl.ds(pl.multiple_of(head * HEAD, HEAD), HEAD)
        shared = pl.ds(pl.multiple_of(lax.div(head, 2) * HEAD, HEAD), HEAD)
        for start in range(0, total, SEQ):
            for first in range(0, SEQ, block):
                rows, keys = pl.ds(start + first, block), pl.ds(start, first + block)
                probs = softmax_block(query[rows, mine], key[keys, shared], first)
                attended[rows, mine] = dot(probs.astype(low), value[keys, shared]).astype(low)
        return carry

    lax.fori_loop(0, heads, attend, 0)
    reorder_rows(attended, local, True)


def attention(tokens, weights, gain_in, gain_q, gain_k, cosine, sine):
    total = tokens.shape[0]
    columns = weights.shape[1]
    low = jnp.bfloat16
    shape = lambda width, kind=low: jax.ShapeDtypeStruct((total, width), kind)
    vmem = pl.BlockSpec(memory_space=pltpu.VMEM)
    return pl.pallas_call(
        forward_kernel,
        out_shape=[
            shape(tokens.shape[1]),
            shape(columns, jnp.float32),
            shape(columns // 2),
            shape(columns // 4),
            shape(columns // 4),
            shape(columns // 2),
        ],
        in_specs=[vmem] * 7,
        out_specs=[vmem] * 6,
        scratch_shapes=[pltpu.VMEM((total, columns // 2), low)],
        compiler_params=pltpu.CompilerParams(vmem_limit_bytes=48 * 2**20),
        cost_estimate=pl.CostEstimate(flops=10**10, bytes_accessed=2 * 10**7, transcendentals=0),
        name="attention",
    )(tokens, weights, gain_in, gain_q, gain_k, cosine, sine)


def backward_kernel(
    query, key, value, raw, grad_rows, gain_q, gain_k, cosine, sine,
    mixed, mixed_local, query_gain, key_gain, grad, key_sum, value_sum,
):
    low = jnp.bfloat16
    total, heads = query.shape[0], query.shape[1] // HEAD
    block = 256
    reorder_rows(grad_rows, grad, False)
    query_gain[...] = jnp.zeros_like(query_gain)
    key_gain[...] = jnp.zeros_like(key_gain)

    def head_norm_back(rows, column, gradient, gain, gain_grad):
        values = raw[rows, column]
        factor = inverse_rms(values)
        unit = values * factor
        turned = turn_back(gradient, cosine[rows, :], sine[rows, :])
        gain_grad[...] += jnp.sum(turned * unit, 0, keepdims=True)
        mixed[rows, column] = norm_back(turned * gain[...], unit, factor).astype(low)

    def one_group(group, carry):
        at = lambda offset: pl.ds(pl.multiple_of(group * 4 * HEAD + offset * HEAD, HEAD), HEAD)
        shared = pl.ds(pl.multiple_of(group * HEAD, HEAD), HEAD)
        key_sum[...] = jnp.zeros_like(key_sum)
        value_sum[...] = jnp.zeros_like(value_sum)
        for head in (0, 1):
            mine = pl.ds(pl.multiple_of((group * 2 + head) * HEAD, HEAD), HEAD)
            for start in range(0, total, SEQ):
                for first in range(0, SEQ, block):
                    rows, keys = pl.ds(start + first, block), pl.ds(start, first + block)
                    query_part, grad_part = query[rows, mine], grad[rows, mine]
                    probs = softmax_block(query_part, key[keys, shared], first)
                    weighed = probs * dot(grad_part, value[keys, shared], 1, 1)
                    scores = weighed - probs * jnp.sum(weighed, -1, keepdims=True)
                    scores = scores.astype(low)
                    grad_query = dot(scores, key[keys, shared]) * (1.0 / math.sqrt(HEAD))
                    head_norm_back(rows, at(head), grad_query, gain_q, query_gain)
                    key_sum[keys, :] += dot(scores, query_part, 0, 0)
                    value_sum[keys, :] += dot(probs.astype(low), grad_part, 0, 0)
        for first in range(0, total, block):
            rows = pl.ds(first, block)
            head_norm_back(rows, at(2), key_sum[rows, :], gain_k, key_gain)
            mixed[rows, at(3)] = value_sum[rows, :].astype(low)
        return carry

    lax.fori_loop(0, heads // 2, one_group, 0)
    reorder_rows(mixed, mixed_local, True)


def attention_back(query, key, value, raw, grad_rows, gain_q, gain_k, cosine, sine):
    total, columns = raw.shape
    low = jnp.bfloat16
    vmem = pl.BlockSpec(memory_space=pltpu.VMEM)
    return pl.pallas_call(
        backward_kernel,
        out_shape=[
            jax.ShapeDtypeStruct((total, columns), low),
            jax.ShapeDtypeStruct((total, columns), low),
            jax.ShapeDtypeStruct((1, HEAD), jnp.float32),
            jax.ShapeDtypeStruct((1, HEAD), jnp.float32),
        ],
        in_specs=[vmem] * 9,
        out_specs=[vmem] * 4,
        scratch_shapes=[
            pltpu.VMEM(grad_rows.shape, low),
            pltpu.VMEM((total, HEAD), jnp.float32),
            pltpu.VMEM((total, HEAD), jnp.float32),
        ],
        compiler_params=pltpu.CompilerParams(vmem_limit_bytes=48 * 2**20),
        cost_estimate=pl.CostEstimate(flops=10**10, bytes_accessed=2 * 10**7, transcendentals=0),
        name="attention_back",
    )(query, key, value, raw, grad_rows, gain_q, gain_k, cosine, sine)


def feed_kernel(rows, out_grad, gate_up, up_part, down, active, grads):
    low = jnp.bfloat16
    block = 512
    tile = down.shape[1]
    step = pl.program_id(0)
    gate_at = pl.ds(pl.multiple_of(step * tile, tile), tile)
    up_at = pl.ds(pl.multiple_of(grads.shape[1] // 2 + step * tile, tile), tile)

    def one(block_at, carry):
        here = pl.ds(pl.multiple_of(block_at * block, block), block)
        gate = dot(rows[here, :], gate_up[...])
        up = dot(rows[here, :], up_part[...])
        grad = dot(out_grad[here, :], down[...])
        sigmoid = jax.nn.sigmoid(gate)
        silu = gate * sigmoid
        active[here, :] = (silu * up).astype(low)
        grads[here, gate_at] = (grad * up * sigmoid * (1.0 + gate * (1.0 - sigmoid))).astype(low)
        grads[here, up_at] = (grad * silu).astype(low)
        return carry

    lax.fori_loop(0, rows.shape[0] // block, one, 0)


def feed_forward(rows, out_grad, gate_up, down, tile):
    total, width = rows.shape
    units = down.shape[1]
    low = jnp.bfloat16
    tiles = units // tile
    whole = pl.BlockSpec((total, width), lambda step: (0, 0))
    return pl.pallas_call(
        feed_kernel,
        grid=(tiles,),
        out_shape=[
            jax.ShapeDtypeStruct((total, units), low),
            jax.ShapeDtypeStruct((total, 2 * units), low),
        ],
        in_specs=[
            whole,
            whole,
            pl.BlockSpec((width, tile), lambda step: (0, step)),
            pl.BlockSpec((width, tile), lambda step: (0, step + tiles)),
            pl.BlockSpec((width, tile), lambda step: (0, step)),
        ],
        out_specs=[
            pl.BlockSpec((total, tile), lambda step: (0, step)),
            pl.BlockSpec((total, 2 * units), lambda step: (0, 0)),
        ],
        compiler_params=pltpu.CompilerParams(vmem_limit_bytes=56 * 2**20),
        cost_estimate=pl.CostEstimate(
            flops=6 * total * width * units, bytes_accessed=4 * 10**7, transcendentals=total * units
        ),
        name="feed_forward",
    )(rows, out_grad, gate_up, gate_up, down)


class Plan:
    def __init__(self, mesh):
        self.total = mesh.shape["dp"]
        self.zones = self.total // 2
        self.tensor = mesh.shape["tensor"]
        self.flips = [k ^ (k >> 1) for k in range(self.zones)]

    def place(self):
        self.index = lax.axis_index("dp")
        self.zone = self.index // 2
        self.side = self.index % 2
        self.row = lax.axis_index("tensor") // 2
        self.core = lax.axis_index("tensor") % 2
        self.home = self.side == self.core

    def move(self, value, target):
        pairs = []
        for d in range(self.total):
            for t in range(self.tensor):
                to = target(d // 2, d % 2, t // 2, t % 2)
                if to is not None:
                    zone, side, row, core = to
                    pairs.append((d * self.tensor + t, (zone * 2 + side) * self.tensor + row * 2 + core))
        return lax.ppermute(value, ("dp", "tensor"), pairs)

    def turn(self, value):
        got = self.move(value, lambda z, y, x, c: (z, c, x, y) if y != c else None)
        return jnp.where(self.home, value, got)

    def zone_flip(self, value, bit):
        return self.move(value, lambda z, y, x, c: (z ^ bit, y, x, c))

    def core_swap(self, value):
        return self.move(value, lambda z, y, x, c: (z, y, x, 1 - c))

    def side_swap(self, value):
        return self.move(value, lambda z, y, x, c: (z, 1 - y, x, c))

    def row_swap(self, value):
        return self.move(value, lambda z, y, x, c: (z, y, 1 - x, c))

    def to_local(self, value, axis):
        width = value.shape[axis] // self.total
        parts = []
        for core in (self.core, 1 - self.core):
            for slot in range(self.zones):
                owner = (self.zone ^ self.flips[slot]) * 2 + core
                parts.append(lax.dynamic_slice_in_dim(value, owner * width, width, axis))
        return jnp.concatenate(parts, axis)

    def to_natural(self, value, axis, core=None):
        core = self.core if core is None else core
        width = value.shape[axis] // self.total
        parts = []
        for block in range(self.total):
            slot = flip = (block // 2) ^ self.zone
            for bits in range(1, self.zones.bit_length()):
                slot = slot ^ (flip >> bits)
            slot = slot + jnp.where(block % 2 == core, 0, self.zones)
            parts.append(lax.dynamic_slice_in_dim(value, slot * width, width, axis))
        return jnp.concatenate(parts, axis)

    def row_owners(self):
        own, off = (self.row, self.side), (1 - self.row, 1 - self.side)
        first = lambda x, y: x * 2 + y
        second = lambda x, y: 4 + y * 2 + x
        return [
            first(own[0], own[1]),
            first(own[0], off[1]),
            second(own[0], own[1]),
            second(off[0], own[1]),
            first(off[0], own[1]),
            first(off[0], off[1]),
            second(own[0], off[1]),
            second(off[0], off[1]),
        ]

    def rows_local(self, value, slots=range(8)):
        size = value.shape[0] // 8
        owners = self.row_owners()
        return jnp.concatenate(
            [lax.dynamic_slice_in_dim(value, owners[slot] * size, size, 0) for slot in slots], 0
        )

    def rows_natural(self, value, order=range(8)):
        size = value.shape[0] // 8
        place = [list(order).index(slot) for slot in range(8)]
        parts = []
        for piece in range(8):
            x, y = (piece // 2, piece % 2) if piece < 4 else (piece % 2, (piece - 4) // 2)
            slots = (0, 1, 4, 5) if piece < 4 else (2, 6, 3, 7)
            same_x, same_y = x == self.row, y == self.side
            slot = jnp.where(
                same_x,
                jnp.where(same_y, place[slots[0]], place[slots[1]]),
                jnp.where(same_y, place[slots[2]], place[slots[3]]),
            )
            parts.append(lax.dynamic_slice_in_dim(value, slot * size, size, 0))
        return jnp.concatenate(parts, 0)

    def from_zones(self, shard):
        return [self.zone_flip(shard, flip) for flip in self.flips[1:]]

    def to_zones(self, parts, slots):
        return [self.zone_flip(parts[slot], self.flips[slot]) for slot in slots]

    def middle_swap(self, pair):
        return self.move(pair, lambda z, y, x, c: (z ^ 3, y, x, c) if z in (1, 2) else None)

    def inward(self, parts):
        send = jnp.concatenate([parts[3:4], parts[2:3]], 0)
        return self.move(send, lambda z, y, x, c: (z ^ 1, y, x, c) if z in (0, 3) else None)

    def pass_outward(self, pair):
        return self.move(pair, lambda z, y, x, c: (z ^ 1, y, x, c) if z in (1, 2) else None)

    def far_pair(self, middle, passed):
        inner = (self.zone == 1) | (self.zone == 2)
        return jnp.where(inner, middle, passed[::-1])

    def first_swap(self, send):
        half = send.shape[0] // 2
        return self.row_swap(send[:half]), self.side_swap(send[half:])

    def second_swap(self, keep, got):
        quarter = keep.shape[0] // 4
        row_part = keep[: 2 * quarter] + got[0].astype(jnp.float32)
        side_part = keep[2 * quarter :] + got[1].astype(jnp.float32)
        own = jnp.concatenate([row_part[:quarter], side_part[:quarter]], 0)
        return own, (
            self.side_swap(row_part[quarter:].astype(jnp.bfloat16)),
            self.row_swap(side_part[quarter:].astype(jnp.bfloat16)),
        )

    def spread_first(self, own):
        half = own.shape[0] // 2
        return (self.side_swap(own[:half]), self.row_swap(own[half:]))

    def spread_second(self, own, got):
        half = own.shape[0] // 2
        row_part = jnp.concatenate([own[:half], got[0]], 0)
        side_part = jnp.concatenate([own[half:], got[1]], 0)
        return row_part, side_part, self.row_swap(row_part), self.side_swap(side_part)

    def send_home(self, own):
        to_home = lambda z, y, x, c: (z, c, x, c) if y != c else None
        return jnp.concatenate([own, self.move(own, to_home)], 0)

    def row_home(self, part):
        return self.move(part, lambda z, y, x, c: (z, y, 1 - x, c) if y == c else None)

    def share_home(self, part, other):
        full = jnp.concatenate([part, other], 0)
        full = self.to_natural(self.rows_natural(full, (0, 2, 1, 6, 4, 3, 5, 7)), 1)
        got = self.move(full, lambda z, y, x, c: (z, y, x, 1 - c) if y == c else None)
        return full, got

    def turned(self, own, got):
        return jnp.where(self.home, own, got)

    def sum_everywhere(self, value):
        value = value + self.row_swap(value)
        value = value + self.side_swap(value)
        value = value + self.core_swap(value)
        bit = 1
        while bit < self.zones:
            value = value + self.zone_flip(value, bit)
            bit *= 2
        return value


def shards(
    plan,
    tokens,
    positions,
    out_grad,
    qkv_weight,
    qkv_first,
    qkv_second,
    out_weight,
    out_first,
    out_second,
    gate_up,
    gate_up_first,
    gate_up_second,
    down_weight,
    down_first,
    down_second,
    gains,
    gains_first,
    gains_second,
):
    plan.place()
    low = jnp.bfloat16
    tok_rows, model_width = tokens.shape
    groups = qkv_weight.shape[1]
    head_size = qkv_weight.shape[3]
    shard_rows = qkv_weight.shape[0]
    seq_count = tok_rows // SEQ
    mixed_cols = groups * 4 * head_size
    near_cols = model_width // 2
    kept = tok_rows // 2
    gain_count = gains.shape[0]

    tree = plan.zones == 4
    slots = range(1, plan.zones)

    def column_parts(value):
        return value.reshape((plan.zones, -1) + value.shape[1:])

    units = gate_up.shape[2]
    plan.ordered = (model_width // plan.total) % 128 == 0
    gain_rows = 16
    gain_block = jnp.pad(gains.astype(low), (0, gain_rows * 128 - gain_count)).reshape(gain_rows, 128)
    low_qkv = qkv_weight.reshape(shard_rows, mixed_cols).astype(low)
    tile = min(units, 256)
    low_gate = jnp.concatenate([gate_up[0].astype(low), gate_up[1].astype(low)], 1)
    angle_at = positions.astype(jnp.float32).reshape(-1, 128)
    (
        both_qkv,
        both_gains,
        turned_gate,
        turned_out,
        turned_down,
        tokens,
        angle_at,
        out_grad,
        partner_gate,
    ) = opening(
        plan,
        low_qkv,
        gain_block,
        low_gate,
        out_weight.astype(low),
        down_weight.astype(low),
        tokens,
        out_grad,
        angle_at,
        3,
    )
    positions = angle_at.reshape(-1)
    turned_out, turned_gate, turned_down, tokens, positions, both_qkv, both_gains, out_grad = fence(
        turned_out, turned_gate, turned_down, tokens, positions, both_qkv, both_gains, out_grad
    )

    zone_out = plan.from_zones(turned_out)
    if tree:
        partner_down = plan.zone_flip(turned_down, 1)
    else:
        partner_down = plan.from_zones(turned_down)
        partner_gate = plan.from_zones(turned_gate)
    if not plan.ordered:
        tokens = plan.to_local(tokens, 1)
        out_grad = plan.to_local(out_grad, 1)
    cosine, sine_table = rotary(positions, head_size)
    signed_sine = jnp.concatenate(
        [-sine_table[:, : head_size // 2], sine_table[:, head_size // 2 :]], 1
    )
    full_qkv = both_qkv.reshape(model_width, mixed_cols)
    gain_slots = both_gains.reshape(plan.total, -1)[:, :gain_count]
    gain_all = plan.to_natural(gain_slots.reshape(-1), 0).astype(jnp.float32)
    gain_in = plan.to_local(gain_all[:model_width], 0)[None]
    gain_post = plan.to_local(gain_all[model_width : 2 * model_width], 0)[None]
    gain_q = gain_all[2 * model_width : 2 * model_width + head_size][None]
    gain_k = gain_all[2 * model_width + head_size :][None]
    normed, raw, query, key_rot, values_low, attended = attention(
        tokens, full_qkv, gain_in, gain_q, gain_k, cosine, signed_sine
    )
    attended, zone_out, turned_out, partner_down, turned_down, turned_gate, partner_gate = fence(
        attended, zone_out, turned_out, partner_down, turned_down, turned_gate, partner_gate
    )

    near_out = jnp.concatenate([turned_out] + zone_out, 0)
    far_out = plan.core_swap(near_out)
    own_tokens = plan.rows_local(tokens, (0, 2))
    near_out, far_out, own_tokens, out_grad = fence(near_out, far_out, own_tokens, out_grad)

    full_out = jnp.concatenate([near_out, far_out], 0)
    branch_terms = contract_cols(attended, full_out).astype(low)
    pairs = [(turned_gate, partner_gate), (turned_down, partner_down)]
    normed_rows, hidden, *gathered = sum_rows(
        spread_kernel,
        hidden_rows,
        branch_terms,
        [own_tokens, gain_post],
        [jax.ShapeDtypeStruct((tok_rows // 4, model_width), jnp.float32)],
        0,
        [PairTree(pairs, (4, 2))] if tree else [],
    )
    if not tree:
        near = [jnp.concatenate([own] + rest, 0) for own, rest in pairs]
        gathered = [jnp.concatenate([part, plan.core_swap(part)], 0) for part in near]
    full_gate = gathered[0].reshape(model_width, 2 * units)
    full_down = gathered[1].reshape(model_width, units)
    normed_rows, hidden, full_gate, full_down, out_grad = fence(
        normed_rows, hidden, full_gate, full_down, out_grad
    )

    def zone_parts(near, got):
        both = (near + got.astype(jnp.float32)).astype(low)
        return both.reshape((plan.zones, -1) + both.shape[1:])

    def zone_total(parts, *arrived):
        total = parts[0].astype(jnp.float32)
        for part in sum([list(group) for group in arrived], []):
            total = total + part.astype(jnp.float32)
        return total.astype(low)

    active, grad_both = feed_forward(normed_rows, out_grad, full_gate, full_down, tile)
    mlp_terms = contract_cols(active, full_down).astype(low)
    mlp_terms, active, grad_both = fence(mlp_terms, active, grad_both)

    mlp_got = plan.first_swap(mlp_terms[kept:])
    down_far = contract_rows(out_grad[:, near_cols:], active).astype(low)
    down_got = plan.core_swap(down_far)
    gate_far = contract_rows(normed_rows[:, near_cols:], grad_both).astype(low)
    down_parts = zone_parts(contract_rows(out_grad[:, :near_cols], active), down_got)
    down_parts, gate_far, grad_both, mlp_got, mlp_terms = fence(
        down_parts, gate_far, grad_both, mlp_got, mlp_terms
    )

    gate_got = plan.core_swap(gate_far)
    if tree:
        down_sums = plan.inward(down_parts)
    else:
        down_sums = plan.to_zones(down_parts, slots)
    mlp_own, mlp_last = plan.second_swap(mlp_terms[:kept].astype(jnp.float32), mlp_got)
    post_terms = contract_cols(grad_both, full_gate).astype(low)
    mlp_own, mlp_last, post_terms, gate_got = fence(mlp_own, mlp_last, post_terms, gate_got)

    block_own = (hidden + mlp_own + jnp.concatenate(mlp_last, 0).astype(jnp.float32)).astype(low)
    block_home = plan.send_home(block_own)
    gate_parts = zone_parts(contract_rows(normed_rows[:, :near_cols], grad_both), gate_got)
    post_terms, gate_parts, down_parts, down_sums, block_home = fence(
        post_terms, gate_parts, down_parts, down_sums, block_home
    )

    eighth = tok_rows // 8
    own_grad = jnp.concatenate([out_grad[:eighth], out_grad[2 * eighth : 3 * eighth]], 0)
    branch_rows, grad_hidden, post_gain_grad, gate_sums = sum_rows(
        spread_kernel,
        grad_hidden_rows,
        post_terms,
        [hidden, own_grad, gain_post],
        [
            jax.ShapeDtypeStruct((tok_rows // 4, model_width), jnp.float32),
            jax.ShapeDtypeStruct((1, model_width), jnp.float32),
        ],
        1,
        [PairScatter(gate_parts, 4) if tree else ZoneBlocks(plan, gate_parts, slots)],
    )
    if tree:
        down_pair = (down_parts[2:].astype(jnp.float32) + down_sums.astype(jnp.float32)).astype(low)
    else:
        down_pair = down_parts
    branch_rows, grad_hidden, post_gain_grad, gate_sums, block_home, down_parts, down_pair = fence(
        branch_rows, grad_hidden, post_gain_grad, gate_sums, block_home, down_parts, down_pair
    )

    block_row = plan.row_home(block_home)
    if tree:
        gate_last = [plan.zone_flip(gate_sums[1], 1)]
        gate_own = gate_sums
        down_sums = plan.middle_swap(down_pair)
    else:
        gate_last, gate_own = gate_sums, gate_parts
    grad_att = jnp.dot(branch_rows, full_out, preferred_element_type=jnp.float32).astype(low)
    grad_mixed, mixed_rows, query_gain_grad, key_gain_grad = attention_back(
        query, key_rot, values_low, raw, grad_att, gain_q, gain_k, cosine, signed_sine
    )
    gain_terms = jnp.concatenate(
        [plan.to_natural(post_gain_grad, 1), query_gain_grad, key_gain_grad], 1
    )
    if tree:
        down_own = (down_parts[:2].astype(jnp.float32) + down_sums.astype(jnp.float32)).astype(low)
    grad_mixed, mixed_rows, gain_terms, normed, gate_last, branch_rows, block_row, down_sums = fence(
        grad_mixed, mixed_rows, gain_terms, normed, gate_last, branch_rows, block_row, down_sums
    )

    if tree:
        total_down = zone_total(down_own, [plan.zone_flip(down_own[1], 1)])
    else:
        total_down = zone_total(down_parts, down_sums)
    total_gate = zone_total(gate_own, gate_last)
    summed_gate = plan.turn(jnp.stack([total_gate[:, :units], total_gate[:, units:]]))
    out_far = contract_rows(branch_rows[:, near_cols:], attended).astype(low)
    out_got = plan.core_swap(out_far)
    qkv_far = contract_rows(normed[:, near_cols:], grad_mixed).astype(low)
    qkv_got = plan.core_swap(qkv_far)
    normed_terms = contract_cols(mixed_rows, full_qkv).astype(low)
    block_full, block_got = plan.share_home(block_home, block_row)
    out_parts = zone_parts(contract_rows(branch_rows[:, :near_cols], attended), out_got)
    qkv_parts = zone_parts(contract_rows(normed[:, :near_cols], grad_mixed), qkv_got)
    block_full, block_got, out_parts, qkv_parts, normed_terms, summed_gate, total_down = fence(
        block_full, block_got, out_parts, qkv_parts, normed_terms, summed_gate, total_down
    )
    block_out = jnp.where(plan.home, block_full, block_got)

    gain_sum = GainSum(plan, gain_terms.shape[1], model_width) if plan.ordered else None
    input_full, input_gain_grad, *rest = sum_rows(
        home_kernel,
        grad_input_rows,
        normed_terms,
        [own_tokens, grad_hidden, gain_in] + ([gain_terms] if plan.ordered else []),
        [jax.ShapeDtypeStruct((1, model_width), jnp.float32)],
        2,
        [ZoneBlocks(plan, qkv_parts, slots), ZoneBlocks(plan, out_parts, slots, 3)],
        gain_sum,
    )
    if plan.ordered:
        summed_gains, qkv_sent, out_sent = rest
    else:
        qkv_sent, out_sent = rest
        summed_gains = plan.sum_everywhere(
            jnp.concatenate([plan.to_natural(input_gain_grad, 1), gain_terms], 1)
        )
    summed_down = plan.turn(total_down)
    input_full, summed_gains, qkv_sent, out_sent, summed_down = fence(
        input_full, summed_gains, qkv_sent, out_sent, summed_down
    )

    summed_both = plan.turn(
        jnp.concatenate([zone_total(qkv_parts, qkv_sent), zone_total(out_parts, out_sent)], 1)
    ).astype(jnp.float32)
    summed_qkv = summed_both[:, :mixed_cols].reshape(qkv_weight.shape)
    summed_out = summed_both[:, mixed_cols:]
    summed_gate = summed_gate.astype(jnp.float32)
    summed_down = summed_down.astype(jnp.float32)
    summed_gains = lax.dynamic_slice_in_dim(summed_gains[0], plan.index * gain_count, gain_count, 0)
    input_rows = plan.to_natural(input_full, 1, plan.side).astype(jnp.float32)

    qkv_moment, qkv_square, qkv_updated = adamw(
        qkv_weight, summed_qkv, qkv_first, qkv_second, RATE_QKV, DECAY_RATE
    )
    out_moment, out_square, out_updated = adamw(
        out_weight, summed_out, out_first, out_second, RATE_OUT, DECAY_RATE
    )
    gate_moment, gate_square, gate_updated = adamw(
        gate_up, summed_gate, gate_up_first, gate_up_second, RATE_GATE, DECAY_RATE
    )
    down_moment, down_square, down_updated = adamw(
        down_weight, summed_down, down_first, down_second, RATE_DOWN, DECAY_RATE
    )
    gain_moment, gain_square, gain_updated = adamw(
        gains, summed_gains, gains_first, gains_second, RATE_GAIN, 0.0
    )
    return (
        block_out,
        input_rows,
        qkv_moment,
        qkv_square,
        qkv_updated,
        out_moment,
        out_square,
        out_updated,
        gate_moment,
        gate_square,
        gate_updated,
        down_moment,
        down_square,
        down_updated,
        gain_moment,
        gain_square,
        gain_updated,
    )


def solution(mesh):
    plan = Plan(mesh)
    placed = (
        P("dp", None),
        P("dp"),
        P("dp", None),
        P("dp", "tensor", None, None),
        P("dp", "tensor", None, None),
        P("dp", "tensor", None, None),
        P("dp", "tensor"),
        P("dp", "tensor"),
        P("dp", "tensor"),
        P(None, "dp", "tensor"),
        P(None, "dp", "tensor"),
        P(None, "dp", "tensor"),
        P("dp", "tensor"),
        P("dp", "tensor"),
        P("dp", "tensor"),
        P("dp"),
        P("dp"),
        P("dp"),
    )
    return jax.shard_map(
        functools.partial(shards, plan),
        mesh=mesh,
        in_specs=placed,
        out_specs=(
            P("dp", None),
            P("dp", None),
            P("dp", "tensor", None, None),
            P("dp", "tensor", None, None),
            P("dp", "tensor", None, None),
            P("dp", "tensor"),
            P("dp", "tensor"),
            P("dp", "tensor"),
            P(None, "dp", "tensor"),
            P(None, "dp", "tensor"),
            P(None, "dp", "tensor"),
            P("dp", "tensor"),
            P("dp", "tensor"),
            P("dp", "tensor"),
            P("dp"),
            P("dp"),
            P("dp"),
        ),
        check_vma=False,
    )
```

```python
import functools
import math

import jax
import jax.numpy as jnp
from jax import lax
from jax.experimental import pallas as pl
from jax.experimental.pallas import tpu as pltpu
from jax.sharding import PartitionSpec as P

SEQ = 1024
STEP = 10


EPS_NORM = 1e-06
THETA = 1000000.0
BETA_ONE = 0.9
BETA_TWO = 0.95
ADAM_EPS = 1e-08
DECAY_RATE = 0.1
RATE_QKV = 0.05
RATE_OUT = 0.3
RATE_GATE = 0.05
RATE_DOWN = 0.03
RATE_GAIN = 1.0


def rotary(positions, head_size):
    freq_index = jnp.arange(head_size // 2, dtype=jnp.float32)
    inverse = jnp.exp(freq_index * (-2.0 * math.log(THETA) / head_size))
    angles = positions.astype(jnp.float32)[:, None] * inverse[None, :]
    cosine = jnp.cos(angles)
    sine_table = jnp.sin(angles)
    return (jnp.concatenate([cosine, cosine], -1), jnp.concatenate([sine_table, sine_table], -1))


def rotate(values, cosine, sine_table):
    half_size = values.shape[-1] // 2
    turned = jnp.concatenate([-values[..., half_size:], values[..., :half_size]], -1)
    return values * cosine[:, None, :] + turned * sine_table[:, None, :]


def unrotate(gradient, cosine, sine_table):
    half_size = gradient.shape[-1] // 2
    turned = gradient * sine_table[:, None, :]
    rotated_back = jnp.concatenate([turned[..., half_size:], -turned[..., :half_size]], -1)
    return gradient * cosine[:, None, :] + rotated_back


def norm_back(grad_unit, unit_vals, factor):
    return factor * (grad_unit - unit_vals * jnp.mean(grad_unit * unit_vals, -1, keepdims=True))


def contract_rows(left, right):
    return lax.dot_general(
        left, right, (((0,), (0,)), ((), ())), preferred_element_type=jnp.float32
    )


def contract_cols(left, right):
    return lax.dot_general(
        left, right, (((1,), (1,)), ((), ())), preferred_element_type=jnp.float32
    )


def block_scores(query_part, key_part, first_row, block_rows, last_row):
    scores = jnp.einsum(
        "nqkgd,nskd->nkgqs", query_part, key_part, preferred_element_type=jnp.float32
    )
    causal = (first_row + jnp.arange(block_rows))[:, None] >= jnp.arange(last_row)[None, :]
    return jnp.where(causal, scores, -1000000000.0)


def attention_forward(query, key_rot, values_low, seq_len):
    block_rows = min(512, seq_len)
    outputs = []
    log_sums = []
    for first_row in range(0, seq_len, block_rows):
        last_row = first_row + block_rows
        query_part = query[:, first_row:last_row]
        scores = block_scores(query_part, key_rot[:, :last_row], first_row, block_rows, last_row)
        row_max = jnp.max(scores, -1, keepdims=True)
        exponent = jnp.exp(scores - row_max)
        row_total = jnp.sum(exponent, -1, keepdims=True)
        probs_low = (exponent / row_total).astype(jnp.bfloat16)
        outputs.append(
            jnp.einsum(
                "nkgqs,nskd->nqkgd",
                probs_low,
                values_low[:, :last_row],
                preferred_element_type=jnp.float32,
            )
        )
        log_sums.append(row_max + jnp.log(row_total))
    return (jnp.concatenate(outputs, 1), log_sums)


def attention_backward(query, key_rot, values_low, grad_att, log_sums, seq_len):
    block_rows = min(512, seq_len)
    query_grads = []
    key_grad = jnp.zeros(key_rot.shape, jnp.float32)
    value_grad = jnp.zeros(values_low.shape, jnp.float32)
    for block_index, first_row in enumerate(range(0, seq_len, block_rows)):
        last_row = first_row + block_rows
        query_part = query[:, first_row:last_row]
        grad_part = grad_att[:, first_row:last_row]
        key_part = key_rot[:, :last_row]
        value_part = values_low[:, :last_row]
        scores = block_scores(query_part, key_part, first_row, block_rows, last_row)
        probs = jnp.exp(scores - log_sums[block_index])
        probs_low = probs.astype(jnp.bfloat16)
        grad_probs = jnp.einsum(
            "nqkgd,nskd->nkgqs", grad_part, value_part, preferred_element_type=jnp.float32
        )
        grad_scores = (
            probs * (grad_probs - jnp.sum(probs * grad_probs, -1, keepdims=True))
        ).astype(jnp.bfloat16)
        query_grads.append(
            jnp.einsum(
                "nkgqs,nskd->nqkgd", grad_scores, key_part, preferred_element_type=jnp.float32
            )
        )
        padding = ((0, 0), (0, seq_len - last_row), (0, 0), (0, 0))
        key_grad = key_grad + jnp.pad(
            jnp.einsum(
                "nkgqs,nqkgd->nskd", grad_scores, query_part, preferred_element_type=jnp.float32
            ),
            padding,
        )
        value_grad = value_grad + jnp.pad(
            jnp.einsum(
                "nkgqs,nqkgd->nskd", probs_low, grad_part, preferred_element_type=jnp.float32
            ),
            padding,
        )
    return (jnp.concatenate(query_grads, 1), key_grad, value_grad)


def adamw(weight, gradient, moment, second, step_rate, decay_rate):
    moment = BETA_ONE * moment + (1.0 - BETA_ONE) * gradient
    second = BETA_TWO * second + (1.0 - BETA_TWO) * gradient * gradient
    first_hat = moment / (1.0 - BETA_ONE**STEP)
    second_hat = second / (1.0 - BETA_TWO**STEP)
    weight = weight - step_rate * (
        first_hat / (jnp.sqrt(second_hat) + ADAM_EPS) + decay_rate * weight
    )
    return (moment, second, weight)


def fence(*values):
    return lax.optimization_barrier(values)


MESH = pl.DeviceIdType.MESH
HEAD = 128
AHEAD = 3


def place_here():
    index, place = lax.axis_index("dp"), lax.axis_index("tensor")
    return lax.div(index, 2), lax.rem(index, 2), lax.div(place, 2), lax.rem(place, 2)


def device(zone, side, row, core):
    return (zone * 2 + side, row * 2 + core)


def flipped(zone, flip):
    bit = 1
    while bit <= flip:
        if flip & bit:
            zone = zone + bit - 2 * bit * lax.rem(lax.div(zone, bit), 2)
        bit *= 2
    return zone


def greet(devices, amount=None):
    barrier = pltpu.get_barrier_semaphore()
    for peer in devices:
        pl.semaphore_signal(barrier, inc=1, device_id=peer, device_id_type=MESH)
    pl.semaphore_wait(barrier, len(devices) if amount is None else amount)


def for_rows(count, body):
    step = 32

    def one(block, carry):
        body(pl.multiple_of(block * step, step), step)
        return carry

    lax.fori_loop(0, count // step, one, 0)


class Copies:
    def __init__(self, send_sems, recv_sems):
        self.send_sems, self.recv_sems = send_sems, recv_sems
        self.number = 0

    def make(self, source, target, peer):
        number, self.number = self.number, self.number + 1
        return pltpu.make_async_remote_copy(
            src_ref=source,
            dst_ref=target,
            send_sem=self.send_sems.at[number],
            recv_sem=self.recv_sems.at[number],
            device_id=peer,
            device_id_type=MESH,
        )

    def start(self, source, target, peer):
        copy = self.make(source, target, peer)
        copy.start()
        return copy


class GainSum:
    def __init__(self, plan, rest, width):
        self.plan, self.width = plan, width
        self.total = width + rest
        self.scratch = [
            pltpu.VMEM((8, 1, self.total), jnp.float32),
            pltpu.VMEM((plan.zones, 1, self.total), jnp.float32),
        ]
        self.output = jax.ShapeDtypeStruct((1, self.total), jnp.float32)
        self.count = 7 + plan.zones - 1

    def plane_peers(self, zone, side, row, core):
        steps = [(s, r, c) for s in range(2) for r in range(2) for c in range(2)][1:]
        turn = lambda value, step: 1 - value if step else value
        return [device(zone, turn(side, s), turn(row, r), turn(core, c)) for s, r, c in steps]

    def zone_peers(self, zone, side, row, core):
        return {flip: device(flipped(zone, flip), side, row, core) for flip in self.plan.flips[1:]}

    def start(self, copies, rest, blocks, plane_sums, zone_sums):
        zone, side, row, core = place_here()
        plan = self.plan
        size = self.width // plan.total
        self.copies, self.plane_sums, self.zone_sums, self.zone = copies, plane_sums, zone_sums, zone
        here = side * 4 + row * 2 + core
        plane_sums[here, :, pl.ds(self.width, self.total - self.width)] = rest[...]
        for slot in range(plan.total):
            owner = flipped(zone, plan.flips[slot % plan.zones]) * 2
            owner = owner + (core if slot < plan.zones else 1 - core)
            spot = pl.ds(pl.multiple_of(owner * size, size), size)
            plane_sums[here, :, spot] = blocks[:, pl.ds(slot * size, size)]
        self.plane = [
            copies.start(plane_sums.at[here], plane_sums.at[here], peer)
            for peer in self.plane_peers(zone, side, row, core)
        ]

    def middle(self):
        for copy in self.plane:
            copy.wait_recv()
        total = self.plane_sums[0]
        for place in range(1, 8):
            total = total + self.plane_sums[place]
        self.zone_sums[self.zone] = total
        zone, side, row, core = place_here()
        self.across = [
            self.copies.start(self.zone_sums.at[self.zone], self.zone_sums.at[self.zone], peer)
            for peer in self.zone_peers(zone, side, row, core).values()
        ]

    def finish(self, out):
        for copy in self.across:
            copy.wait_recv()
        total = self.zone_sums[0]
        for place in range(1, self.plan.zones):
            total = total + self.zone_sums[place]
        out[...] = total
        for copy in self.plane + self.across:
            copy.wait_send()


class ZoneBlocks:
    scratch = []

    def __init__(self, plan, source, slots, begin=0):
        self.flips, self.slots, self.sources, self.begin = plan.flips, list(slots), [source], begin
        self.outputs = [
            jax.ShapeDtypeStruct((len(self.slots),) + source.shape[1:], source.dtype)
        ]
        self.count, self.count_local = len(self.slots), 0
        self.in_hbm = False

    def peers(self, zone, side, row, core):
        return {
            self.flips[slot]: device(flipped(zone, self.flips[slot]), side, row, core)
            for slot in self.slots
        }

    def start(self, copies, local_sems, sources, targets, stages):
        zone, side, row, core = place_here()
        self.started = [
            copies.make(
                sources[0].at[slot],
                targets[0].at[number],
                device(flipped(zone, self.flips[slot]), side, row, core),
            )
            for number, slot in enumerate(self.slots)
        ]
        self.waiting = True
        if self.begin == 0:
            self.pump([0])

    def pump(self, steps):
        if self.waiting and self.begin in steps:
            self.waiting = False
            for copy in self.started:
                copy.start()

    def finish(self):
        for copy in self.started:
            copy.wait_send()
        for copy in self.started:
            copy.wait_recv()


def inner_zone(zone):
    return lax.rem(lax.div(zone + 1, 2), 2)


class PairScatter:
    def __init__(self, parts, pieces):
        self.sources, self.pieces = [parts], pieces
        _, rows, columns = parts.shape
        self.size = rows // pieces
        self.outputs = [jax.ShapeDtypeStruct((2, rows, columns), parts.dtype)]
        self.scratch = [pltpu.VMEM((2, rows, columns), parts.dtype)] * 2
        self.count, self.count_local = 4 * pieces, 0
        self.in_hbm = False

    def peers(self, zone, side, row, core):
        return {
            1: device(flipped(zone, 1), side, row, core),
            3: device(flipped(zone, 3), side, row, core),
        }

    def start(self, copies, local_sems, sources, targets, stages):
        zone, side, row, core = place_here()
        self.parts, self.out = sources[0], targets[0]
        self.inward, self.crossed = stages
        inner_peer = device(flipped(zone, 3), side, row, core)
        outer_peer = device(flipped(zone, 1), side, row, core)
        self.inner = inner_zone(zone) == 1
        self.outer = inner_zone(zone) == 0
        self.steps = [
            (slot, pl.ds(piece * self.size, self.size))
            for piece in range(self.pieces)
            for slot in (0, 1)
        ]
        self.to_inner = [
            copies.make(self.parts.at[3 - slot, rows], self.inward.at[slot, rows], outer_peer)
            for slot, rows in self.steps
        ]
        self.across = [
            copies.make(self.inward.at[slot, rows], self.crossed.at[slot, rows], inner_peer)
            for slot, rows in self.steps
        ]

        @pl.when(self.outer)
        def _():
            for copy in self.to_inner[:AHEAD]:
                copy.start()

    def add(self, target, slot, rows, left, right):
        def some(row, count):
            here = pl.ds(rows.start + row, count)
            both = left[here, :].astype(jnp.float32) + right[here, :].astype(jnp.float32)
            target.at[slot][here, :] = both.astype(jnp.bfloat16)

        for_rows(self.size, some)

    def pump(self, steps):
        steps = [step for step in steps if step < len(self.steps)]

        @pl.when(self.inner)
        def _():
            for step in steps:
                slot, rows = self.steps[step]
                self.to_inner[step].wait_recv()
                self.add(self.inward, slot, rows, self.parts.at[2 + slot], self.inward.at[slot])
                self.across[step].start()
                if step >= AHEAD:
                    self.settle(step - AHEAD)

        @pl.when(self.outer)
        def _():
            for step in steps:
                self.to_inner[step].wait_send()
                for copy in self.to_inner[step + AHEAD : step + AHEAD + 1]:
                    copy.start()

    def settle(self, step):
        slot, rows = self.steps[step]
        self.across[step].wait_recv()
        self.add(self.out, slot, rows, self.parts.at[slot], self.crossed.at[slot])

    def finish(self):
        @pl.when(self.inner)
        def _():
            for step in range(len(self.steps) - AHEAD, len(self.steps)):
                self.settle(step)
            for copy in self.across:
                copy.wait_send()

        @pl.when(self.outer)
        def _():
            for slot in (0, 1):

                def some(row, count, slot=slot):
                    here = pl.ds(row, count)
                    self.out.at[slot][here, :] = self.parts.at[slot][here, :]

                for_rows(self.parts.shape[1], some)


class PairTree:
    def __init__(self, pairs, pieces):
        self.sources = [shard for pair in pairs for shard in pair]
        self.pieces = pieces
        self.outputs = [
            jax.ShapeDtypeStruct((8,) + own.shape, own.dtype) for own, *_ in pairs
        ]
        self.count = 6 * sum(pieces)
        self.count_local = 4 * len(pairs) + 2 * sum(pieces)
        self.scratch = [pltpu.VMEM((2,) + own.shape, own.dtype) for own, *_ in pairs]
        self.in_hbm = True

    def peers(self, zone, side, row, core):
        return {
            1: device(flipped(zone, 1), side, row, core),
            3: device(flipped(zone, 3), side, row, core),
            "core": device(zone, side, row, 1 - core),
        }

    def start(self, copies, local_sems, sources, targets, stages):
        zone, side, row, core = place_here()
        inner_peer = device(flipped(zone, 3), side, row, core)
        outer_peer = device(flipped(zone, 1), side, row, core)
        core_peer = device(zone, side, row, 1 - core)
        self.inner = inner_zone(zone) == 1
        self.outer = inner_zone(zone) == 0
        self.across, self.onward, self.late, self.place = [], [], [], []
        self.kept = []
        sem = 0
        for weight, full in enumerate(targets):
            pair, landing = sources[4 * weight : 4 * weight + 4], stages[weight]
            size = pair[0].shape[0] // self.pieces[weight]
            for piece in range(self.pieces[weight]):
                rows = pl.ds(piece * size, size)
                for slot in (0, 1):
                    here = landing.at[slot, rows]
                    self.across.append(copies.make(pair[slot].at[rows], here, inner_peer))
                    self.onward.append(copies.make(here, landing.at[1 - slot, rows], outer_peer))
                    self.late.append(copies.make(here, full.at[6 + slot, rows], core_peer))
                    self.place.append(
                        pltpu.make_async_copy(here, full.at[2 + slot, rows], local_sems.at[sem])
                    )
                    sem += 1
            for place, slot in enumerate((0, 1, 4, 5)):
                self.kept.append(
                    pltpu.make_async_copy(pair[place], full.at[slot], local_sems.at[sem])
                )
                sem += 1

        @pl.when(self.inner)
        def _():
            for copy in self.across[:AHEAD]:
                copy.start()

    def pump(self, steps):
        steps = [step for step in steps if step < len(self.across)]

        @pl.when(self.inner)
        def _():
            for step in steps:
                self.across[step].wait_recv()
                for copy in self.across[step + AHEAD : step + AHEAD + 1]:
                    copy.start()
                self.onward[step].start()
                self.late[step].start()
                self.place[step].start()

        for copy in self.kept if 3 in steps else []:
            copy.start()

    def finish(self):
        @pl.when(self.inner)
        def _():
            for copy in self.across + self.onward:
                copy.wait_send()

        @pl.when(self.outer)
        def _():
            for number, copy in enumerate(self.onward):
                copy.wait_recv()
                arrived = number + 1 - 2 * (number % 2)
                self.late[arrived].start()
                self.place[arrived].start()

        for copy in self.kept + self.place:
            copy.wait()
        for copy in self.late:
            copy.wait_send()
        for copy in self.late:
            copy.wait_recv()


def sum_eighths(
    copies, row_peer, side_peer, send, keep, forward, first, second, store, begin, pump
):
    size = send.shape[0] // 4
    part = lambda ref, slot: ref.at[pl.ds(slot * size, size)]
    arrivals = [
        copies.start(part(send, 1), part(first, 1), row_peer),
        copies.start(part(send, 3), part(first, 3), side_peer),
        copies.start(part(send, 0), part(first, 0), row_peer),
        copies.start(part(send, 2), part(first, 2), side_peer),
    ]
    begin()
    passed = []
    for number, slot, peer in ((0, 1, side_peer), (1, 3, row_peer)):
        arrivals[number].wait_recv()

        def add(row, count, number=number, slot=slot):
            here = pl.ds(slot * size + row, count)
            both = keep[here, :].astype(jnp.float32) + first[here, :].astype(jnp.float32)
            forward[pl.ds(number * size + row, count), :] = both.astype(jnp.bfloat16)

        for_rows(size, add)
        passed.append(copies.start(part(forward, number), part(second, number), peer))
    pump([0, 1, 2])
    for number, slot in ((0, 0), (1, 2)):
        arrivals[2 + number].wait_recv()
        passed[number].wait_recv()

        def total(row, count, number=number, slot=slot):
            here = pl.ds(slot * size + row, count)
            sums = keep[here, :].astype(jnp.float32) + first[here, :].astype(jnp.float32)
            sums = sums + second[pl.ds(number * size + row, count), :].astype(jnp.float32)
            store(number, row, count, sums)

        for_rows(size, total)
        yield number
    for copy in arrivals + passed:
        copy.wait_send()


def halves(terms):
    rows = terms.shape[0] // 2
    return terms.at[pl.ds(0, rows)], terms.at[pl.ds(rows, rows)]


def split_refs(refs, jobs, extra_count, out_count):
    refs = list(refs)
    take = lambda count: [refs.pop(0) for _ in range(count)]
    extras = take(extra_count)
    sources = [take(len(job.sources)) for job in jobs]
    full = take(1)[0]
    outs = take(out_count)
    targets = [take(len(job.outputs)) for job in jobs]
    return extras, sources, full, outs, targets, refs


def spread_kernel(middle, jobs, extra_count, out_count, gain_sum, terms, *refs):
    keep, send = halves(terms)
    extras, sources, full, outs, targets, scratch = split_refs(refs, jobs, extra_count, out_count)
    forward, first, second, send_sems, recv_sems, local_sems, *stages = scratch
    zone, side, row, core = place_here()
    row_peer, side_peer = device(zone, side, 1 - row, core), device(zone, 1 - side, row, core)
    copies = Copies(send_sems, recv_sems)
    size = send.shape[0] // 4
    part = lambda slot: full.at[pl.ds(slot * size, size)]
    for out in outs:
        if out.shape[0] == 1:
            out[...] = jnp.zeros_like(out)
    peers = {}
    for job in jobs:
        peers.update(job.peers(zone, side, row, core))
    greet([row_peer, side_peer] + list(peers.values()))

    def begin():
        spot = 0
        for job, source, target in zip(jobs, sources, targets):
            own_stages = stages[spot : spot + len(job.scratch)]
            job.start(copies, local_sems, source, target, own_stages)
            spot += len(job.scratch)

    def pump(steps):
        for job in jobs:
            job.pump(steps)

    def store(number, row, count, sums):
        own = pl.ds(number * size + row, count)
        full[pl.ds(2 * number * size + row, count), :] = middle(own, sums, extras, outs)

    firsts, seconds = [], []
    for number in sum_eighths(
        copies, row_peer, side_peer, send, keep, forward, first, second, store, begin, pump
    ):
        near, other = (side_peer, row_peer) if number == 0 else (row_peer, side_peer)
        slot = 2 * number
        firsts.append(copies.start(part(slot), part(slot + 1), near))
        seconds.append(copies.start(part(slot), part(4 + slot), other))
    pump([3])
    firsts[0].wait_recv()
    seconds.append(copies.start(part(1), part(5), row_peer))
    firsts[1].wait_recv()
    seconds.append(copies.start(part(3), part(7), side_peer))
    pump(range(4, 64))
    for copy in seconds:
        copy.wait_recv()
    for copy in firsts + seconds:
        copy.wait_send()
    for job in jobs:
        job.finish()


def home_kernel(middle, jobs, extra_count, out_count, gain_sum, terms, *refs):
    keep, send = halves(terms)
    extras, sources, full, outs, targets, scratch = split_refs(refs, jobs, extra_count, out_count)
    forward, first, second, own, send_sems, recv_sems, local_sems, *gain_scratch = scratch
    zone, side, row, core = place_here()
    row_peer, side_peer = device(zone, side, 1 - row, core), device(zone, 1 - side, row, core)
    copies = Copies(send_sems, recv_sems)
    size = send.shape[0] // 4
    at_home = side == core
    away = side != core
    for out in outs:
        if out.shape[0] == 1:
            out[...] = jnp.zeros_like(out)
    peers = {}
    for job in jobs:
        peers.update(job.peers(zone, side, row, core))
    plane = [row_peer, side_peer]
    if gain_sum is not None:
        plane = gain_sum.plane_peers(zone, side, row, core)
        peers.update(gain_sum.zone_peers(zone, side, row, core))
    greet(plane + list(peers.values()))

    def begin():
        for job, source, target in zip(jobs, sources, targets):
            job.start(copies, local_sems, source, target, [])

    def pump(steps):
        for job in jobs:
            job.pump(steps)

    def store(number, start, count, sums):
        here = pl.ds(number * size + start, count)
        values = middle(here, sums, extras, outs)
        own[here, :] = values
        eighth = row * 2 + side if number == 0 else 4 + side * 2 + row

        @pl.when(at_home)
        def _():
            full[pl.ds(pl.multiple_of(eighth * size + start, 32), count), :] = values

    for _ in sum_eighths(
        copies, row_peer, side_peer, send, keep, forward, first, second, store, begin, pump
    ):
        pass
    pump([3])

    def piece(number, x, y):
        start = (x * 2 + y) * size if number == 0 else (4 + y * 2 + x) * size
        return full.at[pl.ds(pl.multiple_of(start, size), size)]

    mine = lambda number: own.at[pl.ds(number * size, size)]
    both = (0, 1)
    to_side = [copies.make(mine(k), piece(k, row, side), side_peer) for k in both]
    to_row = [copies.make(mine(k), piece(k, row, side), row_peer) for k in both]
    pass_row = [
        copies.make(piece(k, row, 1 - side), piece(k, row, 1 - side), row_peer) for k in both
    ]
    if gain_sum is not None:
        gain_sum.start(copies, extras[-1], outs[0], *gain_scratch)

    @pl.when(away)
    def _():
        for copy in to_side:
            copy.start()

    @pl.when(at_home)
    def _():
        for copy in to_row:
            copy.start()

    if gain_sum is not None:
        gain_sum.middle()

    @pl.when(away)
    def _():
        for copy in to_side:
            copy.wait_send()

    @pl.when(at_home)
    def _():
        for k in both:
            to_side[k].wait_recv()
            pass_row[k].start()
        for copy in to_row + pass_row:
            copy.wait_recv()
            copy.wait_send()

    if gain_sum is not None:
        gain_sum.finish(outs[-1])
    for job in jobs:
        job.finish()


def sum_rows(kernel, middle, terms, extras, outs, number, jobs=(), gain_sum=None):
    half, width = terms.shape[0] // 2, terms.shape[1]
    eighth = half // 4
    low = jnp.bfloat16
    vmem, hbm = pl.BlockSpec(memory_space=pltpu.VMEM), pl.BlockSpec(memory_space=pl.ANY)
    scratch = [
        pltpu.VMEM((2 * eighth, width), low),
        pltpu.VMEM((half, width), low),
        pltpu.VMEM((2 * eighth, width), low),
    ]
    if kernel is home_kernel:
        scratch.append(pltpu.VMEM((2 * eighth, width), low))
    copies = 12 + sum(job.count for job in jobs)
    local = max([2] + [job.count_local for job in jobs])
    if gain_sum is not None:
        copies += gain_sum.count
        outs = outs + [gain_sum.output]
    scratch += [pltpu.SemaphoreType.DMA((count,)) for count in (copies, copies, local)]
    if gain_sum is not None:
        scratch += gain_sum.scratch
    scratch += [stage for job in jobs for stage in job.scratch]
    sources = [source for job in jobs for source in job.sources]
    targets = [target for job in jobs for target in job.outputs]
    return pl.pallas_call(
        functools.partial(kernel, middle, jobs, len(extras), len(outs), gain_sum),
        out_shape=[jax.ShapeDtypeStruct((2 * half, width), low)] + outs + targets,
        in_specs=[vmem] * (1 + len(extras) + len(sources)),
        out_specs=[vmem] * (1 + len(outs))
        + [hbm if job.in_hbm else vmem for job in jobs for _ in job.outputs],
        scratch_shapes=scratch,
        compiler_params=pltpu.CompilerParams(
            collective_id=number, has_side_effects=True, vmem_limit_bytes=56 * 2**20
        ),
        cost_estimate=pl.CostEstimate(flops=4 * 10**10, bytes_accessed=10**8, transcendentals=0),
        name=middle.__name__,
    )(terms, *extras, *sources)


def exchange_rows(copies, source, stage, partner, row_peer, pieces):
    _, _, row, _ = place_here()
    size = source.shape[0] // (2 * pieces)
    spots = [
        pl.ds(pl.multiple_of((row * pieces + piece) * size, size), size) for piece in range(pieces)
    ]
    turn = [copies.make(source.at[spot], stage.at[spot], partner) for spot in spots]
    onward = [copies.make(stage.at[spot], stage.at[spot], row_peer) for spot in spots]
    return turn, onward


def block_columns(plan, width):
    if not plan.ordered:
        return [pl.ds(0, width)], [pl.ds(0, width)]
    zone, _, _, core = place_here()
    size, zones = width // plan.total, plan.zones
    owners = [
        flipped(zone, plan.flips[slot % zones]) * 2 + (core if slot < zones else 1 - core)
        for slot in range(plan.total)
    ]
    natural = [pl.ds(pl.multiple_of(owner * size, size), size) for owner in owners]
    return natural, [pl.ds(slot * size, size) for slot in range(plan.total)]


def copy_rows(source, target):
    def some(row, count):
        target[pl.ds(row, count), :] = source[pl.ds(row, count), :]

    if source.shape[0] % 32:
        target[...] = source[...]
    else:
        for_rows(source.shape[0], some)


def opening_kernel(plan, qkv, gains, gate, out, down, tokens, angles, *refs):
    qkv_full, gains_full, turned_gate, turned_out, turned_down, turned_tokens, turned_angles = refs[:7]
    partner_gate, send_sems, recv_sems, tokens_stage = refs[7:]
    zone, side, row, core = place_here()
    partner = device(zone, core, row, side)
    row_peer, core_peer = device(zone, side, 1 - row, core), device(zone, side, row, 1 - core)
    zone_peers = [device(flipped(zone, flip), side, row, core) for flip in plan.flips[1:]]
    at_home, away = side == core, side != core
    always = [row_peer, core_peer] + zone_peers

    @pl.when(at_home)
    def _():
        greet(always)

    @pl.when(away)
    def _():
        greet(always + [partner])

    copies = Copies(send_sems, recv_sems)
    zones = plan.zones
    own = (gains, qkv, angles, gate, out, down)
    ends = (gains_full.at[0], qkv_full.at[0], turned_angles, turned_gate, turned_out, turned_down)
    turn = [copies.make(source, target, partner) for source, target in zip(own, ends)]
    turn_rows, pass_rows = exchange_rows(copies, tokens, tokens_stage, partner, row_peer, 4)
    natural, local = block_columns(plan, tokens.shape[1])

    def lay_down(all_tokens):
        def some(start, count):
            here = pl.ds(start, count)
            for a, b in zip(natural, local):
                turned_tokens[here, b] = all_tokens[here, a]

        for_rows(all_tokens.shape[0], some)

    slots = list(range(1, zones))
    weights = ((gains, gains_full), (qkv, qkv_full))
    from_own = [
        [copies.make(source, full.at[slot], zone_peers[slot - 1]) for slot in slots]
        + [copies.make(source, full.at[zones], core_peer)]
        for source, full in weights
    ] + [[copies.make(gate, partner_gate, zone_peers[0])]]
    copies.number -= 2 * zones + 1
    from_turned = [
        [copies.make(full.at[0], full.at[slot], zone_peers[slot - 1]) for slot in slots]
        + [copies.make(full.at[0], full.at[zones], core_peer)]
        for _, full in weights
    ] + [[copies.make(turned_gate, partner_gate, zone_peers[0])]]
    cross = [
        [copies.make(full.at[slot], full.at[zones + slot], core_peer) for slot in slots]
        for _, full in weights
    ]

    def cross_over(k):
        for which in (0, 1):
            from_turned[which][k].wait_recv()
            cross[which][k].start()

    @pl.when(away)
    def _():
        for copy in turn[:3]:
            copy.start()
        for which in (0, 1):
            turn[which].wait_recv()
            for copy in from_turned[which]:
                copy.start()
        turn[3].start()
        turn_rows[0].start()
        turn[3].wait_recv()
        from_turned[2][0].start()
        turn_rows[1].start()
        cross_over(0)
        for k in range(4):
            turn_rows[k].wait_recv()
            pass_rows[k].start()
            for copy in turn_rows[k + 2 : k + 3] + (turn[4:] if k == 1 else []):
                copy.start()

    @pl.when(at_home)
    def _():
        for copy in from_own[0] + from_own[1] + from_own[2]:
            copy.start()
        for source, target in zip(own, ends):
            copy_rows(source, target)
        lay_down(tokens)
        cross_over(0)

    for k in range(1, zones - 1):
        cross_over(k)
    for which in (0, 1):
        from_turned[which][zones - 1].wait_recv()
        for copy in from_turned[which]:
            copy.wait_send()
        for copy in cross[which]:
            copy.wait_recv()
            copy.wait_send()
    from_turned[2][0].wait_recv()
    from_turned[2][0].wait_send()

    @pl.when(away)
    def _():
        for copy in pass_rows + turn[2:3] + turn[4:]:
            copy.wait_recv()
        lay_down(tokens_stage)
        for copy in turn + turn_rows + pass_rows:
            copy.wait_send()


def opening(plan, qkv, gains, gate, out, down, tokens, angles, number):
    vmem = pl.BlockSpec(memory_space=pltpu.VMEM)
    like = lambda v: jax.ShapeDtypeStruct(v.shape, v.dtype)
    whole = lambda v: jax.ShapeDtypeStruct((2 * plan.zones,) + v.shape, v.dtype)
    operands = (qkv, gains, gate, out, down, tokens, angles)
    outputs = [whole(qkv), whole(gains)] + [like(v) for v in (gate, out, down, tokens, angles)]
    outputs += [like(gate)]
    copies = 6 + 8 + 2 * plan.zones + 1 + 2 * (plan.zones - 1)
    return pl.pallas_call(
        functools.partial(opening_kernel, plan),
        out_shape=outputs,
        in_specs=[vmem] * len(operands),
        out_specs=[vmem] * len(outputs),
        scratch_shapes=[
            pltpu.SemaphoreType.DMA((copies,)),
            pltpu.SemaphoreType.DMA((copies,)),
            pltpu.VMEM(tokens.shape, tokens.dtype),
        ],
        compiler_params=pltpu.CompilerParams(
            collective_id=number, has_side_effects=True, vmem_limit_bytes=56 * 2**20
        ),
        cost_estimate=pl.CostEstimate(flops=4 * 10**10, bytes_accessed=10**8, transcendentals=0),
        name="opening",
    )(*operands)


def inverse_rms(values):
    return lax.rsqrt(jnp.mean(values * values, -1, keepdims=True) + EPS_NORM)


def hidden_rows(own, sums, extras, outs):
    tokens, gain = extras
    hidden = tokens[own, :].astype(jnp.float32) + sums
    outs[0][own, :] = hidden
    return (hidden * inverse_rms(hidden) * gain[...]).astype(jnp.bfloat16)


def grad_hidden_rows(own, sums, extras, outs):
    hidden, out_grad, gain = extras
    values = hidden[own, :]
    factor = inverse_rms(values)
    unit = values * factor
    outs[1][...] += jnp.sum(sums * unit, 0, keepdims=True)
    grad = out_grad[own, :].astype(jnp.float32) + norm_back(sums * gain[...], unit, factor)
    outs[0][own, :] = grad
    return grad.astype(jnp.bfloat16)


def grad_input_rows(own, sums, extras, outs):
    tokens, grad_hidden, gain = extras[:3]
    values = tokens[own, :].astype(jnp.float32)
    factor = inverse_rms(values)
    unit = values * factor
    outs[0][...] += jnp.sum(sums * unit, 0, keepdims=True)
    return (grad_hidden[own, :] + norm_back(sums * gain[...], unit, factor)).astype(jnp.bfloat16)


def dot(left, right, left_dim=1, right_dim=0):
    return lax.dot_general(
        left, right, (((left_dim,), (right_dim,)), ((), ())), preferred_element_type=jnp.float32
    )


def turn_head(values, cosine, signed_sine):
    return values * cosine + pltpu.roll(values, HEAD // 2, 1) * signed_sine


def turn_back(gradient, cosine, signed_sine):
    return gradient * cosine + pltpu.roll(gradient * signed_sine, HEAD // 2, 1)


def softmax_block(query, key, first_row):
    rows, keys = query.shape[0], key.shape[0]
    scores = dot(query, key, 1, 1)
    row_at = lax.broadcasted_iota(jnp.int32, (rows, keys), 0) + first_row
    key_at = lax.broadcasted_iota(jnp.int32, (rows, keys), 1)
    scores = jnp.where(key_at <= row_at, scores, -1000000000.0)
    exponent = jnp.exp(scores - jnp.max(scores, -1, keepdims=True))
    return exponent / jnp.sum(exponent, -1, keepdims=True)


def eighth_owners():
    _, side, row, _ = place_here()
    own, off = (row, side), (1 - row, 1 - side)
    first = lambda x, y: x * 2 + y
    second = lambda x, y: 4 + y * 2 + x
    return [
        first(own[0], own[1]),
        first(own[0], off[1]),
        second(own[0], own[1]),
        second(off[0], own[1]),
        first(off[0], own[1]),
        first(off[0], off[1]),
        second(own[0], off[1]),
        second(off[0], off[1]),
    ]


def reorder_rows(source, target, into_local):
    size = source.shape[0] // 8
    for slot, owner in enumerate(eighth_owners()):
        natural = pl.ds(pl.multiple_of(owner * size, size), size)
        local = pl.ds(slot * size, size)
        if into_local:
            target[local, :] = source[natural, :]
        else:
            target[natural, :] = source[local, :]


def forward_kernel(
    plan, tokens, weights, gain_in, gain_q, gain_k, cosine, sine, out_grad,
    normed, raw, query, key, value, local, rows_grad, attended, grad_stage, send_sems, recv_sems,
):
    low = jnp.bfloat16
    zone, side, row, core = place_here()
    partner, row_peer = device(zone, core, row, side), device(zone, side, 1 - row, core)
    at_home, away = side == core, side != core
    copies = Copies(send_sems, recv_sems)
    turn, onward = exchange_rows(copies, out_grad, grad_stage, partner, row_peer, 4)

    @pl.when(away)
    def _():
        greet([partner, row_peer])
        for copy in turn:
            copy.start()

    def lay_down(source):
        natural, blocks = block_columns(plan, source.shape[1])
        eighth = source.shape[0] // 8
        for slot, owner in enumerate(eighth_owners()):

            def some(start, count, slot=slot, owner=owner):
                here = pl.ds(pl.multiple_of(owner * eighth + start, 32), count)
                there = pl.ds(slot * eighth + start, count)
                for a, b in zip(natural, blocks):
                    rows_grad[there, b] = source[here, a]

            for_rows(eighth, some)

    total, heads = tokens.shape[0], query.shape[1] // HEAD
    block, wide = 256, 512

    def project(step, carry):
        rows = pl.ds(pl.multiple_of(step * wide, wide), wide)
        values = tokens[rows, :].astype(jnp.float32)
        normed[rows, :] = (values * inverse_rms(values) * gain_in[...]).astype(low)
        raw[rows, :] = dot(normed[rows, :], weights[...])
        turns = (cosine[rows, :], sine[rows, :])
        for head in range(heads):
            column = (head // 2) * 4 * HEAD + (head % 2) * HEAD
            values = raw[rows, pl.ds(column, HEAD)]
            values = turn_head(values * inverse_rms(values) * gain_q[...], *turns)
            query[rows, pl.ds(head * HEAD, HEAD)] = (values * (1.0 / math.sqrt(HEAD))).astype(low)
        for group in range(heads // 2):
            column = group * 4 * HEAD + 2 * HEAD
            here = pl.ds(group * HEAD, HEAD)
            values = raw[rows, pl.ds(column, HEAD)]
            values = turn_head(values * inverse_rms(values) * gain_k[...], *turns)
            key[rows, here] = values.astype(low)
            value[rows, here] = raw[rows, pl.ds(column + HEAD, HEAD)].astype(low)
        return carry

    lax.fori_loop(0, total // wide, project, 0)

    @pl.when(away)
    def _():
        for first, second in zip(turn[:2], onward[:2]):
            first.wait_recv()
            second.start()


    def attend(head, carry):
        mine = pl.ds(pl.multiple_of(head * HEAD, HEAD), HEAD)
        shared = pl.ds(pl.multiple_of(lax.div(head, 2) * HEAD, HEAD), HEAD)
        for start in range(0, total, SEQ):
            for first in range(0, SEQ, block):
                rows, keys = pl.ds(start + first, block), pl.ds(start, first + block)
                probs = softmax_block(query[rows, mine], key[keys, shared], first)
                attended[rows, mine] = dot(probs.astype(low), value[keys, shared]).astype(low)
        return carry

    lax.fori_loop(0, heads, attend, 0)
    reorder_rows(attended, local, True)

    @pl.when(away)
    def _():
        for first, second in zip(turn[2:], onward[2:]):
            first.wait_recv()
            second.start()
        for copy in onward:
            copy.wait_recv()
        lay_down(grad_stage)
        for copy in turn + onward:
            copy.wait_send()

    @pl.when(at_home)
    def _():
        lay_down(out_grad)


def attention(plan, tokens, weights, gain_in, gain_q, gain_k, cosine, sine, out_grad, number):
    total = tokens.shape[0]
    columns = weights.shape[1]
    low = jnp.bfloat16
    shape = lambda width, kind=low: jax.ShapeDtypeStruct((total, width), kind)
    vmem = pl.BlockSpec(memory_space=pltpu.VMEM)
    return pl.pallas_call(
        functools.partial(forward_kernel, plan),
        out_shape=[
            shape(tokens.shape[1]),
            shape(columns, jnp.float32),
            shape(columns // 2),
            shape(columns // 4),
            shape(columns // 4),
            shape(columns // 2),
            shape(out_grad.shape[1]),
        ],
        in_specs=[vmem] * 8,
        out_specs=[vmem] * 7,
        scratch_shapes=[
            pltpu.VMEM((total, columns // 2), low),
            pltpu.VMEM(out_grad.shape, low),
            pltpu.SemaphoreType.DMA((8,)),
            pltpu.SemaphoreType.DMA((8,)),
        ],
        compiler_params=pltpu.CompilerParams(
            collective_id=number, has_side_effects=True, vmem_limit_bytes=56 * 2**20
        ),
        cost_estimate=pl.CostEstimate(flops=10**10, bytes_accessed=2 * 10**7, transcendentals=0),
        name="attention",
    )(tokens, weights, gain_in, gain_q, gain_k, cosine, sine, out_grad)


def backward_kernel(
    query, key, value, raw, grad_rows, gain_q, gain_k, cosine, sine,
    mixed, mixed_local, query_gain, key_gain, grad, key_sum, value_sum,
):
    low = jnp.bfloat16
    total, heads = query.shape[0], query.shape[1] // HEAD
    block = 256
    reorder_rows(grad_rows, grad, False)
    query_gain[...] = jnp.zeros_like(query_gain)
    key_gain[...] = jnp.zeros_like(key_gain)

    def head_norm_back(rows, column, gradient, gain, gain_grad):
        values = raw[rows, column]
        factor = inverse_rms(values)
        unit = values * factor
        turned = turn_back(gradient, cosine[rows, :], sine[rows, :])
        gain_grad[...] += jnp.sum(turned * unit, 0, keepdims=True)
        mixed[rows, column] = norm_back(turned * gain[...], unit, factor).astype(low)

    def one_group(group, carry):
        at = lambda offset: pl.ds(pl.multiple_of(group * 4 * HEAD + offset * HEAD, HEAD), HEAD)
        shared = pl.ds(pl.multiple_of(group * HEAD, HEAD), HEAD)
        key_sum[...] = jnp.zeros_like(key_sum)
        value_sum[...] = jnp.zeros_like(value_sum)
        for head in (0, 1):
            mine = pl.ds(pl.multiple_of((group * 2 + head) * HEAD, HEAD), HEAD)
            for start in range(0, total, SEQ):
                for first in range(0, SEQ, block):
                    rows, keys = pl.ds(start + first, block), pl.ds(start, first + block)
                    query_part, grad_part = query[rows, mine], grad[rows, mine]
                    probs = softmax_block(query_part, key[keys, shared], first)
                    weighed = probs * dot(grad_part, value[keys, shared], 1, 1)
                    scores = weighed - probs * jnp.sum(weighed, -1, keepdims=True)
                    scores = scores.astype(low)
                    grad_query = dot(scores, key[keys, shared]) * (1.0 / math.sqrt(HEAD))
                    head_norm_back(rows, at(head), grad_query, gain_q, query_gain)
                    key_sum[keys, :] += dot(scores, query_part, 0, 0)
                    value_sum[keys, :] += dot(probs.astype(low), grad_part, 0, 0)
        for first in range(0, total, block):
            rows = pl.ds(first, block)
            head_norm_back(rows, at(2), key_sum[rows, :], gain_k, key_gain)
            mixed[rows, at(3)] = value_sum[rows, :].astype(low)
        return carry

    lax.fori_loop(0, heads // 2, one_group, 0)
    reorder_rows(mixed, mixed_local, True)


def attention_back(query, key, value, raw, grad_rows, gain_q, gain_k, cosine, sine):
    total, columns = raw.shape
    low = jnp.bfloat16
    vmem = pl.BlockSpec(memory_space=pltpu.VMEM)
    return pl.pallas_call(
        backward_kernel,
        out_shape=[
            jax.ShapeDtypeStruct((total, columns), low),
            jax.ShapeDtypeStruct((total, columns), low),
            jax.ShapeDtypeStruct((1, HEAD), jnp.float32),
            jax.ShapeDtypeStruct((1, HEAD), jnp.float32),
        ],
        in_specs=[vmem] * 9,
        out_specs=[vmem] * 4,
        scratch_shapes=[
            pltpu.VMEM(grad_rows.shape, low),
            pltpu.VMEM((total, HEAD), jnp.float32),
            pltpu.VMEM((total, HEAD), jnp.float32),
        ],
        compiler_params=pltpu.CompilerParams(vmem_limit_bytes=48 * 2**20),
        cost_estimate=pl.CostEstimate(flops=10**10, bytes_accessed=2 * 10**7, transcendentals=0),
        name="attention_back",
    )(query, key, value, raw, grad_rows, gain_q, gain_k, cosine, sine)


def feed_kernel(rows, out_grad, gate_up, up_part, down, active, grads):
    low = jnp.bfloat16
    block = 512
    tile = down.shape[1]
    step = pl.program_id(0)
    gate_at = pl.ds(pl.multiple_of(step * tile, tile), tile)
    up_at = pl.ds(pl.multiple_of(grads.shape[1] // 2 + step * tile, tile), tile)

    def one(block_at, carry):
        here = pl.ds(pl.multiple_of(block_at * block, block), block)
        gate = dot(rows[here, :], gate_up[...])
        up = dot(rows[here, :], up_part[...])
        grad = dot(out_grad[here, :], down[...])
        sigmoid = jax.nn.sigmoid(gate)
        silu = gate * sigmoid
        active[here, :] = (silu * up).astype(low)
        grads[here, gate_at] = (grad * up * sigmoid * (1.0 + gate * (1.0 - sigmoid))).astype(low)
        grads[here, up_at] = (grad * silu).astype(low)
        return carry

    lax.fori_loop(0, rows.shape[0] // block, one, 0)


def feed_forward(rows, out_grad, gate_up, down, tile):
    total, width = rows.shape
    units = down.shape[1]
    low = jnp.bfloat16
    tiles = units // tile
    whole = pl.BlockSpec((total, width), lambda step: (0, 0))
    return pl.pallas_call(
        feed_kernel,
        grid=(tiles,),
        out_shape=[
            jax.ShapeDtypeStruct((total, units), low),
            jax.ShapeDtypeStruct((total, 2 * units), low),
        ],
        in_specs=[
            whole,
            whole,
            pl.BlockSpec((width, tile), lambda step: (0, step)),
            pl.BlockSpec((width, tile), lambda step: (0, step + tiles)),
            pl.BlockSpec((width, tile), lambda step: (0, step)),
        ],
        out_specs=[
            pl.BlockSpec((total, tile), lambda step: (0, step)),
            pl.BlockSpec((total, 2 * units), lambda step: (0, 0)),
        ],
        compiler_params=pltpu.CompilerParams(vmem_limit_bytes=56 * 2**20),
        cost_estimate=pl.CostEstimate(
            flops=6 * total * width * units, bytes_accessed=4 * 10**7, transcendentals=total * units
        ),
        name="feed_forward",
    )(rows, out_grad, gate_up, gate_up, down)


class Plan:
    def __init__(self, mesh):
        self.total = mesh.shape["dp"]
        self.zones = self.total // 2
        self.tensor = mesh.shape["tensor"]
        self.flips = [k ^ (k >> 1) for k in range(self.zones)]

    def place(self):
        self.index = lax.axis_index("dp")
        self.zone = self.index // 2
        self.side = self.index % 2
        self.row = lax.axis_index("tensor") // 2
        self.core = lax.axis_index("tensor") % 2
        self.home = self.side == self.core

    def move(self, value, target):
        pairs = []
        for d in range(self.total):
            for t in range(self.tensor):
                to = target(d // 2, d % 2, t // 2, t % 2)
                if to is not None:
                    zone, side, row, core = to
                    pairs.append((d * self.tensor + t, (zone * 2 + side) * self.tensor + row * 2 + core))
        return lax.ppermute(value, ("dp", "tensor"), pairs)

    def turn(self, value):
        got = self.move(value, lambda z, y, x, c: (z, c, x, y) if y != c else None)
        return jnp.where(self.home, value, got)

    def zone_flip(self, value, bit):
        return self.move(value, lambda z, y, x, c: (z ^ bit, y, x, c))

    def core_swap(self, value):
        return self.move(value, lambda z, y, x, c: (z, y, x, 1 - c))

    def side_swap(self, value):
        return self.move(value, lambda z, y, x, c: (z, 1 - y, x, c))

    def row_swap(self, value):
        return self.move(value, lambda z, y, x, c: (z, y, 1 - x, c))

    def to_local(self, value, axis):
        width = value.shape[axis] // self.total
        parts = []
        for core in (self.core, 1 - self.core):
            for slot in range(self.zones):
                owner = (self.zone ^ self.flips[slot]) * 2 + core
                parts.append(lax.dynamic_slice_in_dim(value, owner * width, width, axis))
        return jnp.concatenate(parts, axis)

    def to_natural(self, value, axis, core=None):
        core = self.core if core is None else core
        width = value.shape[axis] // self.total
        parts = []
        for block in range(self.total):
            slot = flip = (block // 2) ^ self.zone
            for bits in range(1, self.zones.bit_length()):
                slot = slot ^ (flip >> bits)
            slot = slot + jnp.where(block % 2 == core, 0, self.zones)
            parts.append(lax.dynamic_slice_in_dim(value, slot * width, width, axis))
        return jnp.concatenate(parts, axis)

    def row_owners(self):
        own, off = (self.row, self.side), (1 - self.row, 1 - self.side)
        first = lambda x, y: x * 2 + y
        second = lambda x, y: 4 + y * 2 + x
        return [
            first(own[0], own[1]),
            first(own[0], off[1]),
            second(own[0], own[1]),
            second(off[0], own[1]),
            first(off[0], own[1]),
            first(off[0], off[1]),
            second(own[0], off[1]),
            second(off[0], off[1]),
        ]

    def rows_local(self, value, slots=range(8)):
        size = value.shape[0] // 8
        owners = self.row_owners()
        return jnp.concatenate(
            [lax.dynamic_slice_in_dim(value, owners[slot] * size, size, 0) for slot in slots], 0
        )

    def rows_natural(self, value, order=range(8)):
        size = value.shape[0] // 8
        place = [list(order).index(slot) for slot in range(8)]
        parts = []
        for piece in range(8):
            x, y = (piece // 2, piece % 2) if piece < 4 else (piece % 2, (piece - 4) // 2)
            slots = (0, 1, 4, 5) if piece < 4 else (2, 6, 3, 7)
            same_x, same_y = x == self.row, y == self.side
            slot = jnp.where(
                same_x,
                jnp.where(same_y, place[slots[0]], place[slots[1]]),
                jnp.where(same_y, place[slots[2]], place[slots[3]]),
            )
            parts.append(lax.dynamic_slice_in_dim(value, slot * size, size, 0))
        return jnp.concatenate(parts, 0)

    def from_zones(self, shard):
        return [self.zone_flip(shard, flip) for flip in self.flips[1:]]

    def to_zones(self, parts, slots):
        return [self.zone_flip(parts[slot], self.flips[slot]) for slot in slots]

    def middle_swap(self, pair):
        return self.move(pair, lambda z, y, x, c: (z ^ 3, y, x, c) if z in (1, 2) else None)

    def inward(self, parts):
        send = jnp.concatenate([parts[3:4], parts[2:3]], 0)
        return self.move(send, lambda z, y, x, c: (z ^ 1, y, x, c) if z in (0, 3) else None)

    def pass_outward(self, pair):
        return self.move(pair, lambda z, y, x, c: (z ^ 1, y, x, c) if z in (1, 2) else None)

    def far_pair(self, middle, passed):
        inner = (self.zone == 1) | (self.zone == 2)
        return jnp.where(inner, middle, passed[::-1])

    def first_swap(self, send):
        half = send.shape[0] // 2
        return self.row_swap(send[:half]), self.side_swap(send[half:])

    def second_swap(self, keep, got):
        quarter = keep.shape[0] // 4
        row_part = keep[: 2 * quarter] + got[0].astype(jnp.float32)
        side_part = keep[2 * quarter :] + got[1].astype(jnp.float32)
        own = jnp.concatenate([row_part[:quarter], side_part[:quarter]], 0)
        return own, (
            self.side_swap(row_part[quarter:].astype(jnp.bfloat16)),
            self.row_swap(side_part[quarter:].astype(jnp.bfloat16)),
        )

    def spread_first(self, own):
        half = own.shape[0] // 2
        return (self.side_swap(own[:half]), self.row_swap(own[half:]))

    def spread_second(self, own, got):
        half = own.shape[0] // 2
        row_part = jnp.concatenate([own[:half], got[0]], 0)
        side_part = jnp.concatenate([own[half:], got[1]], 0)
        return row_part, side_part, self.row_swap(row_part), self.side_swap(side_part)

    def send_home(self, own):
        to_home = lambda z, y, x, c: (z, c, x, c) if y != c else None
        return jnp.concatenate([own, self.move(own, to_home)], 0)

    def row_home(self, part):
        return self.move(part, lambda z, y, x, c: (z, y, 1 - x, c) if y == c else None)

    def share_home(self, part, other):
        full = jnp.concatenate([part, other], 0)
        full = self.to_natural(self.rows_natural(full, (0, 2, 1, 6, 4, 3, 5, 7)), 1)
        got = self.move(full, lambda z, y, x, c: (z, y, x, 1 - c) if y == c else None)
        return full, got

    def turned(self, own, got):
        return jnp.where(self.home, own, got)

    def sum_everywhere(self, value):
        value = value + self.row_swap(value)
        value = value + self.side_swap(value)
        value = value + self.core_swap(value)
        bit = 1
        while bit < self.zones:
            value = value + self.zone_flip(value, bit)
            bit *= 2
        return value


def shards(
    plan,
    tokens,
    positions,
    out_grad,
    qkv_weight,
    qkv_first,
    qkv_second,
    out_weight,
    out_first,
    out_second,
    gate_up,
    gate_up_first,
    gate_up_second,
    down_weight,
    down_first,
    down_second,
    gains,
    gains_first,
    gains_second,
):
    plan.place()
    low = jnp.bfloat16
    tok_rows, model_width = tokens.shape
    groups = qkv_weight.shape[1]
    head_size = qkv_weight.shape[3]
    shard_rows = qkv_weight.shape[0]
    seq_count = tok_rows // SEQ
    mixed_cols = groups * 4 * head_size
    near_cols = model_width // 2
    kept = tok_rows // 2
    gain_count = gains.shape[0]

    tree = plan.zones == 4
    slots = range(1, plan.zones)

    def column_parts(value):
        return value.reshape((plan.zones, -1) + value.shape[1:])

    units = gate_up.shape[2]
    plan.ordered = (model_width // plan.total) % 128 == 0
    gain_rows = 16
    gain_block = jnp.pad(gains.astype(low), (0, gain_rows * 128 - gain_count)).reshape(gain_rows, 128)
    low_qkv = qkv_weight.reshape(shard_rows, mixed_cols).astype(low)
    tile = min(units, 256)
    low_gate = jnp.concatenate([gate_up[0].astype(low), gate_up[1].astype(low)], 1)
    angle_at = positions.astype(jnp.float32).reshape(-1, 128)
    (
        both_qkv,
        both_gains,
        turned_gate,
        turned_out,
        turned_down,
        tokens,
        angle_at,
        partner_gate,
    ) = opening(
        plan,
        low_qkv,
        gain_block,
        low_gate,
        out_weight.astype(low),
        down_weight.astype(low),
        tokens,
        angle_at,
        3,
    )
    positions = angle_at.reshape(-1)
    turned_out, turned_gate, turned_down, tokens, positions, both_qkv, both_gains, partner_gate = fence(
        turned_out, turned_gate, turned_down, tokens, positions, both_qkv, both_gains, partner_gate
    )

    zone_out = plan.from_zones(turned_out)
    if tree:
        partner_down = plan.zone_flip(turned_down, 1)
        far_gate = plan.core_swap(jnp.stack([turned_gate, partner_gate]))
    else:
        far_gate = turned_gate
        partner_down = plan.from_zones(turned_down)
        partner_gate = plan.from_zones(turned_gate)
    if not plan.ordered:
        tokens = plan.to_local(tokens, 1)
    cosine, sine_table = rotary(positions, head_size)
    signed_sine = jnp.concatenate(
        [-sine_table[:, : head_size // 2], sine_table[:, head_size // 2 :]], 1
    )
    full_qkv = both_qkv.reshape(model_width, mixed_cols)
    gain_slots = both_gains.reshape(plan.total, -1)[:, :gain_count]
    gain_all = plan.to_natural(gain_slots.reshape(-1), 0).astype(jnp.float32)
    gain_in = plan.to_local(gain_all[:model_width], 0)[None]
    gain_post = plan.to_local(gain_all[model_width : 2 * model_width], 0)[None]
    gain_q = gain_all[2 * model_width : 2 * model_width + head_size][None]
    gain_k = gain_all[2 * model_width + head_size :][None]
    normed, raw, query, key_rot, values_low, attended, out_grad = attention(
        plan, tokens, full_qkv, gain_in, gain_q, gain_k, cosine, signed_sine, out_grad, 4
    )
    if not plan.ordered:
        out_grad = plan.to_local(out_grad, 1)
    attended, zone_out, turned_out, partner_down, turned_down, turned_gate, partner_gate, far_gate = fence(
        attended, zone_out, turned_out, partner_down, turned_down, turned_gate, partner_gate, far_gate
    )

    near_out = jnp.concatenate([turned_out] + zone_out, 0)
    far_out = plan.core_swap(near_out)
    if tree:
        far_down = plan.core_swap(jnp.stack([turned_down, partner_down]))
        pairs = [
            (turned_gate, partner_gate, far_gate[0], far_gate[1]),
            (turned_down, partner_down, far_down[0], far_down[1]),
        ]
    else:
        pairs = [(turned_gate, partner_gate), (turned_down, partner_down)]
    own_tokens = plan.rows_local(tokens, (0, 2))
    near_out, far_out, own_tokens, out_grad, pairs = fence(
        near_out, far_out, own_tokens, out_grad, pairs
    )

    full_out = jnp.concatenate([near_out, far_out], 0)
    branch_terms = contract_cols(attended, full_out).astype(low)
    normed_rows, hidden, *gathered = sum_rows(
        spread_kernel,
        hidden_rows,
        branch_terms,
        [own_tokens, gain_post],
        [jax.ShapeDtypeStruct((tok_rows // 4, model_width), jnp.float32)],
        0,
        [PairTree(pairs, (4, 2))] if tree else [],
    )
    if not tree:
        near = [jnp.concatenate([own] + rest, 0) for own, rest in pairs]
        gathered = [jnp.concatenate([part, plan.core_swap(part)], 0) for part in near]
    full_gate = gathered[0].reshape(model_width, 2 * units)
    full_down = gathered[1].reshape(model_width, units)
    normed_rows, hidden, full_gate, full_down, out_grad = fence(
        normed_rows, hidden, full_gate, full_down, out_grad
    )

    def zone_parts(near, got):
        both = (near + got.astype(jnp.float32)).astype(low)
        return both.reshape((plan.zones, -1) + both.shape[1:])

    def zone_total(parts, *arrived):
        total = parts[0].astype(jnp.float32)
        for part in sum([list(group) for group in arrived], []):
            total = total + part.astype(jnp.float32)
        return total.astype(low)

    active, grad_both = feed_forward(normed_rows, out_grad, full_gate, full_down, tile)
    mlp_terms = contract_cols(active, full_down).astype(low)
    mlp_terms, active, grad_both = fence(mlp_terms, active, grad_both)

    mlp_got = plan.first_swap(mlp_terms[kept:])
    down_far = contract_rows(out_grad[:, near_cols:], active).astype(low)
    down_got = plan.core_swap(down_far)
    gate_far = contract_rows(normed_rows[:, near_cols:], grad_both).astype(low)
    down_parts = zone_parts(contract_rows(out_grad[:, :near_cols], active), down_got)
    down_parts, gate_far, grad_both, mlp_got, mlp_terms = fence(
        down_parts, gate_far, grad_both, mlp_got, mlp_terms
    )

    gate_got = plan.core_swap(gate_far)
    if tree:
        down_sums = plan.inward(down_parts)
    else:
        down_sums = plan.to_zones(down_parts, slots)
    mlp_own, mlp_last = plan.second_swap(mlp_terms[:kept].astype(jnp.float32), mlp_got)
    post_terms = contract_cols(grad_both, full_gate).astype(low)
    mlp_own, mlp_last, post_terms, gate_got = fence(mlp_own, mlp_last, post_terms, gate_got)

    block_own = (hidden + mlp_own + jnp.concatenate(mlp_last, 0).astype(jnp.float32)).astype(low)
    block_home = plan.send_home(block_own)
    gate_parts = zone_parts(contract_rows(normed_rows[:, :near_cols], grad_both), gate_got)
    post_terms, gate_parts, down_parts, down_sums, block_home = fence(
        post_terms, gate_parts, down_parts, down_sums, block_home
    )

    eighth = tok_rows // 8
    own_grad = jnp.concatenate([out_grad[:eighth], out_grad[2 * eighth : 3 * eighth]], 0)
    branch_rows, grad_hidden, post_gain_grad, gate_sums = sum_rows(
        spread_kernel,
        grad_hidden_rows,
        post_terms,
        [hidden, own_grad, gain_post],
        [
            jax.ShapeDtypeStruct((tok_rows // 4, model_width), jnp.float32),
            jax.ShapeDtypeStruct((1, model_width), jnp.float32),
        ],
        1,
        [PairScatter(gate_parts, 4) if tree else ZoneBlocks(plan, gate_parts, slots)],
    )
    if tree:
        down_pair = (down_parts[2:].astype(jnp.float32) + down_sums.astype(jnp.float32)).astype(low)
    else:
        down_pair = down_parts
    branch_rows, grad_hidden, post_gain_grad, gate_sums, block_home, down_parts, down_pair = fence(
        branch_rows, grad_hidden, post_gain_grad, gate_sums, block_home, down_parts, down_pair
    )

    block_row = plan.row_home(block_home)
    if tree:
        gate_last = [plan.zone_flip(gate_sums[1], 1)]
        gate_own = gate_sums
        down_sums = plan.middle_swap(down_pair)
    else:
        gate_last, gate_own = gate_sums, gate_parts
    grad_att = jnp.dot(branch_rows, full_out, preferred_element_type=jnp.float32).astype(low)
    grad_mixed, mixed_rows, query_gain_grad, key_gain_grad = attention_back(
        query, key_rot, values_low, raw, grad_att, gain_q, gain_k, cosine, signed_sine
    )
    gain_terms = jnp.concatenate(
        [plan.to_natural(post_gain_grad, 1), query_gain_grad, key_gain_grad], 1
    )
    if tree:
        down_own = (down_parts[:2].astype(jnp.float32) + down_sums.astype(jnp.float32)).astype(low)
    grad_mixed, mixed_rows, gain_terms, normed, gate_last, branch_rows, block_row, down_sums = fence(
        grad_mixed, mixed_rows, gain_terms, normed, gate_last, branch_rows, block_row, down_sums
    )

    if tree:
        total_down = zone_total(down_own, [plan.zone_flip(down_own[1], 1)])
    else:
        total_down = zone_total(down_parts, down_sums)
    total_gate = zone_total(gate_own, gate_last)
    summed_gate = plan.turn(jnp.stack([total_gate[:, :units], total_gate[:, units:]]))
    out_far = contract_rows(branch_rows[:, near_cols:], attended).astype(low)
    out_got = plan.core_swap(out_far)
    qkv_far = contract_rows(normed[:, near_cols:], grad_mixed).astype(low)
    qkv_got = plan.core_swap(qkv_far)
    normed_terms = contract_cols(mixed_rows, full_qkv).astype(low)
    block_full, block_got = plan.share_home(block_home, block_row)
    out_parts = zone_parts(contract_rows(branch_rows[:, :near_cols], attended), out_got)
    qkv_parts = zone_parts(contract_rows(normed[:, :near_cols], grad_mixed), qkv_got)
    block_full, block_got, out_parts, qkv_parts, normed_terms, summed_gate, total_down = fence(
        block_full, block_got, out_parts, qkv_parts, normed_terms, summed_gate, total_down
    )
    block_out = jnp.where(plan.home, block_full, block_got)

    gain_sum = GainSum(plan, gain_terms.shape[1], model_width) if plan.ordered else None
    input_full, input_gain_grad, *rest = sum_rows(
        home_kernel,
        grad_input_rows,
        normed_terms,
        [own_tokens, grad_hidden, gain_in] + ([gain_terms] if plan.ordered else []),
        [jax.ShapeDtypeStruct((1, model_width), jnp.float32)],
        2,
        [ZoneBlocks(plan, qkv_parts, slots), ZoneBlocks(plan, out_parts, slots, 3)],
        gain_sum,
    )
    if plan.ordered:
        summed_gains, qkv_sent, out_sent = rest
    else:
        qkv_sent, out_sent = rest
        summed_gains = plan.sum_everywhere(
            jnp.concatenate([plan.to_natural(input_gain_grad, 1), gain_terms], 1)
        )
    summed_down = plan.turn(total_down)
    input_full, summed_gains, qkv_sent, out_sent, summed_down = fence(
        input_full, summed_gains, qkv_sent, out_sent, summed_down
    )

    input_full = jnp.where(
        plan.home,
        input_full,
        plan.move(input_full, lambda z, y, x, c: (z, y, x, 1 - c) if y == c else None),
    )
    summed_both = plan.turn(
        jnp.concatenate([zone_total(qkv_parts, qkv_sent), zone_total(out_parts, out_sent)], 1)
    ).astype(jnp.float32)
    summed_qkv = summed_both[:, :mixed_cols].reshape(qkv_weight.shape)
    summed_out = summed_both[:, mixed_cols:]
    summed_gate = summed_gate.astype(jnp.float32)
    summed_down = summed_down.astype(jnp.float32)
    summed_gains = lax.dynamic_slice_in_dim(summed_gains[0], plan.index * gain_count, gain_count, 0)
    input_rows = plan.to_natural(input_full, 1, plan.side).astype(jnp.float32)

    qkv_moment, qkv_square, qkv_updated = adamw(
        qkv_weight, summed_qkv, qkv_first, qkv_second, RATE_QKV, DECAY_RATE
    )
    out_moment, out_square, out_updated = adamw(
        out_weight, summed_out, out_first, out_second, RATE_OUT, DECAY_RATE
    )
    gate_moment, gate_square, gate_updated = adamw(
        gate_up, summed_gate, gate_up_first, gate_up_second, RATE_GATE, DECAY_RATE
    )
    down_moment, down_square, down_updated = adamw(
        down_weight, summed_down, down_first, down_second, RATE_DOWN, DECAY_RATE
    )
    gain_moment, gain_square, gain_updated = adamw(
        gains, summed_gains, gains_first, gains_second, RATE_GAIN, 0.0
    )
    return (
        block_out,
        input_rows,
        qkv_moment,
        qkv_square,
        qkv_updated,
        out_moment,
        out_square,
        out_updated,
        gate_moment,
        gate_square,
        gate_updated,
        down_moment,
        down_square,
        down_updated,
        gain_moment,
        gain_square,
        gain_updated,
    )


def solution(mesh):
    plan = Plan(mesh)
    placed = (
        P("dp", None),
        P("dp"),
        P("dp", None),
        P("dp", "tensor", None, None),
        P("dp", "tensor", None, None),
        P("dp", "tensor", None, None),
        P("dp", "tensor"),
        P("dp", "tensor"),
        P("dp", "tensor"),
        P(None, "dp", "tensor"),
        P(None, "dp", "tensor"),
        P(None, "dp", "tensor"),
        P("dp", "tensor"),
        P("dp", "tensor"),
        P("dp", "tensor"),
        P("dp"),
        P("dp"),
        P("dp"),
    )
    return jax.shard_map(
        functools.partial(shards, plan),
        mesh=mesh,
        in_specs=placed,
        out_specs=(
            P("dp", None),
            P("dp", None),
            P("dp", "tensor", None, None),
            P("dp", "tensor", None, None),
            P("dp", "tensor", None, None),
            P("dp", "tensor"),
            P("dp", "tensor"),
            P("dp", "tensor"),
            P(None, "dp", "tensor"),
            P(None, "dp", "tensor"),
            P(None, "dp", "tensor"),
            P("dp", "tensor"),
            P("dp", "tensor"),
            P("dp", "tensor"),
            P("dp"),
            P("dp"),
            P("dp"),
        ),
        check_vma=False,
    )
```

```python
import functools
import math

import jax
import jax.numpy as jnp
from jax import lax
from jax.experimental import pallas as pl
from jax.experimental.pallas import tpu as pltpu
from jax.sharding import PartitionSpec as P

SEQ = 1024
STEP = 10


EPS_NORM = 1e-06
THETA = 1000000.0
BETA_ONE = 0.9
BETA_TWO = 0.95
ADAM_EPS = 1e-08
DECAY_RATE = 0.1
RATE_QKV = 0.05
RATE_OUT = 0.3
RATE_GATE = 0.05
RATE_DOWN = 0.03
RATE_GAIN = 1.0


def rotary(positions, head_size):
    freq_index = jnp.arange(head_size // 2, dtype=jnp.float32)
    inverse = jnp.exp(freq_index * (-2.0 * math.log(THETA) / head_size))
    angles = positions.astype(jnp.float32)[:, None] * inverse[None, :]
    cosine = jnp.cos(angles)
    sine_table = jnp.sin(angles)
    return (jnp.concatenate([cosine, cosine], -1), jnp.concatenate([sine_table, sine_table], -1))


def rotate(values, cosine, sine_table):
    half_size = values.shape[-1] // 2
    turned = jnp.concatenate([-values[..., half_size:], values[..., :half_size]], -1)
    return values * cosine[:, None, :] + turned * sine_table[:, None, :]


def unrotate(gradient, cosine, sine_table):
    half_size = gradient.shape[-1] // 2
    turned = gradient * sine_table[:, None, :]
    rotated_back = jnp.concatenate([turned[..., half_size:], -turned[..., :half_size]], -1)
    return gradient * cosine[:, None, :] + rotated_back


def norm_back(grad_unit, unit_vals, factor):
    return factor * (grad_unit - unit_vals * jnp.mean(grad_unit * unit_vals, -1, keepdims=True))


def contract_rows(left, right):
    return lax.dot_general(
        left, right, (((0,), (0,)), ((), ())), preferred_element_type=jnp.float32
    )


def contract_cols(left, right):
    return lax.dot_general(
        left, right, (((1,), (1,)), ((), ())), preferred_element_type=jnp.float32
    )


def block_scores(query_part, key_part, first_row, block_rows, last_row):
    scores = jnp.einsum(
        "nqkgd,nskd->nkgqs", query_part, key_part, preferred_element_type=jnp.float32
    )
    causal = (first_row + jnp.arange(block_rows))[:, None] >= jnp.arange(last_row)[None, :]
    return jnp.where(causal, scores, -1000000000.0)


def attention_forward(query, key_rot, values_low, seq_len):
    block_rows = min(512, seq_len)
    outputs = []
    log_sums = []
    for first_row in range(0, seq_len, block_rows):
        last_row = first_row + block_rows
        query_part = query[:, first_row:last_row]
        scores = block_scores(query_part, key_rot[:, :last_row], first_row, block_rows, last_row)
        row_max = jnp.max(scores, -1, keepdims=True)
        exponent = jnp.exp(scores - row_max)
        row_total = jnp.sum(exponent, -1, keepdims=True)
        probs_low = (exponent / row_total).astype(jnp.bfloat16)
        outputs.append(
            jnp.einsum(
                "nkgqs,nskd->nqkgd",
                probs_low,
                values_low[:, :last_row],
                preferred_element_type=jnp.float32,
            )
        )
        log_sums.append(row_max + jnp.log(row_total))
    return (jnp.concatenate(outputs, 1), log_sums)


def attention_backward(query, key_rot, values_low, grad_att, log_sums, seq_len):
    block_rows = min(512, seq_len)
    query_grads = []
    key_grad = jnp.zeros(key_rot.shape, jnp.float32)
    value_grad = jnp.zeros(values_low.shape, jnp.float32)
    for block_index, first_row in enumerate(range(0, seq_len, block_rows)):
        last_row = first_row + block_rows
        query_part = query[:, first_row:last_row]
        grad_part = grad_att[:, first_row:last_row]
        key_part = key_rot[:, :last_row]
        value_part = values_low[:, :last_row]
        scores = block_scores(query_part, key_part, first_row, block_rows, last_row)
        probs = jnp.exp(scores - log_sums[block_index])
        probs_low = probs.astype(jnp.bfloat16)
        grad_probs = jnp.einsum(
            "nqkgd,nskd->nkgqs", grad_part, value_part, preferred_element_type=jnp.float32
        )
        grad_scores = (
            probs * (grad_probs - jnp.sum(probs * grad_probs, -1, keepdims=True))
        ).astype(jnp.bfloat16)
        query_grads.append(
            jnp.einsum(
                "nkgqs,nskd->nqkgd", grad_scores, key_part, preferred_element_type=jnp.float32
            )
        )
        padding = ((0, 0), (0, seq_len - last_row), (0, 0), (0, 0))
        key_grad = key_grad + jnp.pad(
            jnp.einsum(
                "nkgqs,nqkgd->nskd", grad_scores, query_part, preferred_element_type=jnp.float32
            ),
            padding,
        )
        value_grad = value_grad + jnp.pad(
            jnp.einsum(
                "nkgqs,nqkgd->nskd", probs_low, grad_part, preferred_element_type=jnp.float32
            ),
            padding,
        )
    return (jnp.concatenate(query_grads, 1), key_grad, value_grad)


def adamw(weight, gradient, moment, second, step_rate, decay_rate):
    moment = BETA_ONE * moment + (1.0 - BETA_ONE) * gradient
    second = BETA_TWO * second + (1.0 - BETA_TWO) * gradient * gradient
    first_hat = moment / (1.0 - BETA_ONE**STEP)
    second_hat = second / (1.0 - BETA_TWO**STEP)
    weight = weight - step_rate * (
        first_hat / (jnp.sqrt(second_hat) + ADAM_EPS) + decay_rate * weight
    )
    return (moment, second, weight)


def fence(*values):
    return lax.optimization_barrier(values)


MESH = pl.DeviceIdType.MESH
HEAD = 128
AHEAD = 2


def place_here():
    index, place = lax.axis_index("dp"), lax.axis_index("tensor")
    return lax.div(index, 2), lax.rem(index, 2), lax.div(place, 2), lax.rem(place, 2)


def device(zone, side, row, core):
    return (zone * 2 + side, row * 2 + core)


def flipped(zone, flip):
    bit = 1
    while bit <= flip:
        if flip & bit:
            zone = zone + bit - 2 * bit * lax.rem(lax.div(zone, bit), 2)
        bit *= 2
    return zone


def greet(devices, amount=None):
    barrier = pltpu.get_barrier_semaphore()
    for peer in devices:
        pl.semaphore_signal(barrier, inc=1, device_id=peer, device_id_type=MESH)
    pl.semaphore_wait(barrier, len(devices) if amount is None else amount)


def for_rows(count, body):
    step = 32

    def one(block, carry):
        body(pl.multiple_of(block * step, step), step)
        return carry

    lax.fori_loop(0, count // step, one, 0)


class Copies:
    def __init__(self, send_sems, recv_sems):
        self.send_sems, self.recv_sems = send_sems, recv_sems
        self.number = 0

    def make(self, source, target, peer):
        number, self.number = self.number, self.number + 1
        return pltpu.make_async_remote_copy(
            src_ref=source,
            dst_ref=target,
            send_sem=self.send_sems.at[number],
            recv_sem=self.recv_sems.at[number],
            device_id=peer,
            device_id_type=MESH,
        )

    def start(self, source, target, peer):
        copy = self.make(source, target, peer)
        copy.start()
        return copy


class GainSum:
    def __init__(self, plan, rest, width):
        self.plan, self.width = plan, width
        self.total = width + rest
        self.scratch = [
            pltpu.VMEM((8, 1, self.total), jnp.float32),
            pltpu.VMEM((plan.zones, 1, self.total), jnp.float32),
        ]
        self.output = jax.ShapeDtypeStruct((1, self.total), jnp.float32)
        self.count = 7 + plan.zones - 1

    def plane_peers(self, zone, side, row, core):
        steps = [(s, r, c) for s in range(2) for r in range(2) for c in range(2)][1:]
        turn = lambda value, step: 1 - value if step else value
        return [device(zone, turn(side, s), turn(row, r), turn(core, c)) for s, r, c in steps]

    def zone_peers(self, zone, side, row, core):
        return {flip: device(flipped(zone, flip), side, row, core) for flip in self.plan.flips[1:]}

    def start(self, copies, rest, blocks, plane_sums, zone_sums):
        zone, side, row, core = place_here()
        plan = self.plan
        size = self.width // plan.total
        self.copies, self.plane_sums, self.zone_sums, self.zone = copies, plane_sums, zone_sums, zone
        here = side * 4 + row * 2 + core
        plane_sums[here, :, pl.ds(self.width, self.total - self.width)] = rest[...]
        for slot in range(plan.total):
            owner = flipped(zone, plan.flips[slot % plan.zones]) * 2
            owner = owner + (core if slot < plan.zones else 1 - core)
            spot = pl.ds(pl.multiple_of(owner * size, size), size)
            plane_sums[here, :, spot] = blocks[:, pl.ds(slot * size, size)]
        self.plane = [
            copies.start(plane_sums.at[here], plane_sums.at[here], peer)
            for peer in self.plane_peers(zone, side, row, core)
        ]

    def middle(self):
        for copy in self.plane:
            copy.wait_recv()
        total = self.plane_sums[0]
        for place in range(1, 8):
            total = total + self.plane_sums[place]
        self.zone_sums[self.zone] = total
        zone, side, row, core = place_here()
        self.across = [
            self.copies.start(self.zone_sums.at[self.zone], self.zone_sums.at[self.zone], peer)
            for peer in self.zone_peers(zone, side, row, core).values()
        ]

    def finish(self, out):
        for copy in self.across:
            copy.wait_recv()
        total = self.zone_sums[0]
        for place in range(1, self.plan.zones):
            total = total + self.zone_sums[place]
        out[...] = total
        for copy in self.plane + self.across:
            copy.wait_send()


class ZoneBlocks:
    scratch = []

    def __init__(self, plan, source, slots, begin=0):
        self.flips, self.slots, self.sources, self.begin = plan.flips, list(slots), [source], begin
        self.outputs = [
            jax.ShapeDtypeStruct((len(self.slots),) + source.shape[1:], source.dtype)
        ]
        self.count, self.count_local = len(self.slots), 0
        self.in_hbm = False

    def peers(self, zone, side, row, core):
        return {
            self.flips[slot]: device(flipped(zone, self.flips[slot]), side, row, core)
            for slot in self.slots
        }

    def start(self, copies, local_sems, sources, targets, stages):
        zone, side, row, core = place_here()
        self.started = [
            copies.make(
                sources[0].at[slot],
                targets[0].at[number],
                device(flipped(zone, self.flips[slot]), side, row, core),
            )
            for number, slot in enumerate(self.slots)
        ]
        self.waiting = True
        if self.begin == 0:
            self.pump([0])

    def pump(self, steps):
        if self.waiting and self.begin in steps:
            self.waiting = False
            for copy in self.started:
                copy.start()

    def finish(self):
        for copy in self.started:
            copy.wait_send()
        for copy in self.started:
            copy.wait_recv()


def inner_zone(zone):
    return lax.rem(lax.div(zone + 1, 2), 2)


class PairScatter:
    def __init__(self, parts, pieces):
        self.sources, self.pieces = [parts], pieces
        _, rows, columns = parts.shape
        self.size = rows // pieces
        self.outputs = [jax.ShapeDtypeStruct((2, rows, columns), parts.dtype)]
        self.scratch = [pltpu.VMEM((2, rows, columns), parts.dtype)] * 2
        self.count, self.count_local = 4 * pieces, 0
        self.in_hbm = False

    def peers(self, zone, side, row, core):
        return {
            1: device(flipped(zone, 1), side, row, core),
            3: device(flipped(zone, 3), side, row, core),
        }

    def start(self, copies, local_sems, sources, targets, stages):
        zone, side, row, core = place_here()
        self.parts, self.out = sources[0], targets[0]
        self.inward, self.crossed = stages
        inner_peer = device(flipped(zone, 3), side, row, core)
        outer_peer = device(flipped(zone, 1), side, row, core)
        self.inner = inner_zone(zone) == 1
        self.outer = inner_zone(zone) == 0
        self.steps = [
            (slot, pl.ds(piece * self.size, self.size))
            for piece in range(self.pieces)
            for slot in (0, 1)
        ]
        self.to_inner = [
            copies.make(self.parts.at[3 - slot, rows], self.inward.at[slot, rows], outer_peer)
            for slot, rows in self.steps
        ]
        self.across = [
            copies.make(self.inward.at[slot, rows], self.crossed.at[slot, rows], inner_peer)
            for slot, rows in self.steps
        ]

        @pl.when(self.outer)
        def _():
            for copy in self.to_inner[:AHEAD]:
                copy.start()

    def add(self, target, slot, rows, left, right):
        def some(row, count):
            here = pl.ds(rows.start + row, count)
            both = left[here, :].astype(jnp.float32) + right[here, :].astype(jnp.float32)
            target.at[slot][here, :] = both.astype(jnp.bfloat16)

        for_rows(self.size, some)

    def pump(self, steps):
        steps = [step for step in steps if step < len(self.steps)]

        @pl.when(self.inner)
        def _():
            for step in steps:
                slot, rows = self.steps[step]
                self.to_inner[step].wait_recv()
                self.add(self.inward, slot, rows, self.parts.at[2 + slot], self.inward.at[slot])
                self.across[step].start()
                if step >= AHEAD:
                    self.settle(step - AHEAD)

        @pl.when(self.outer)
        def _():
            for step in steps:
                self.to_inner[step].wait_send()
                for copy in self.to_inner[step + AHEAD : step + AHEAD + 1]:
                    copy.start()

    def settle(self, step):
        slot, rows = self.steps[step]
        self.across[step].wait_recv()
        self.add(self.out, slot, rows, self.parts.at[slot], self.crossed.at[slot])

    def finish(self):
        @pl.when(self.inner)
        def _():
            for step in range(len(self.steps) - AHEAD, len(self.steps)):
                self.settle(step)
            for copy in self.across:
                copy.wait_send()

        @pl.when(self.outer)
        def _():
            for slot in (0, 1):

                def some(row, count, slot=slot):
                    here = pl.ds(row, count)
                    self.out.at[slot][here, :] = self.parts.at[slot][here, :]

                for_rows(self.parts.shape[1], some)


class PairTree:
    def __init__(self, pairs, pieces):
        self.sources = [shard for pair in pairs for shard in pair]
        self.pieces = pieces
        self.outputs = [
            jax.ShapeDtypeStruct((8,) + own.shape, own.dtype) for own, _ in pairs
        ]
        self.count = 6 * sum(pieces) + 2 * len(pairs)
        self.count_local = 2 * len(pairs) + 2 * sum(pieces)
        self.scratch = [pltpu.VMEM((2,) + own.shape, own.dtype) for own, _ in pairs]
        self.in_hbm = True

    def peers(self, zone, side, row, core):
        return {
            1: device(flipped(zone, 1), side, row, core),
            3: device(flipped(zone, 3), side, row, core),
            "core": device(zone, side, row, 1 - core),
        }

    def start(self, copies, local_sems, sources, targets, stages):
        zone, side, row, core = place_here()
        inner_peer = device(flipped(zone, 3), side, row, core)
        outer_peer = device(flipped(zone, 1), side, row, core)
        core_peer = device(zone, side, row, 1 - core)
        self.inner = inner_zone(zone) == 1
        self.outer = inner_zone(zone) == 0
        self.across, self.onward, self.late, self.place = [], [], [], []
        self.shared, self.kept = [], []
        sem = 0
        for weight, full in enumerate(targets):
            pair, landing = sources[2 * weight : 2 * weight + 2], stages[weight]
            size = pair[0].shape[0] // self.pieces[weight]
            for piece in range(self.pieces[weight]):
                rows = pl.ds(piece * size, size)
                for slot in (0, 1):
                    here = landing.at[slot, rows]
                    self.across.append(copies.make(pair[slot].at[rows], here, inner_peer))
                    self.onward.append(copies.make(here, landing.at[1 - slot, rows], outer_peer))
                    self.late.append(copies.make(here, full.at[6 + slot, rows], core_peer))
                    self.place.append(
                        pltpu.make_async_copy(here, full.at[2 + slot, rows], local_sems.at[sem])
                    )
                    sem += 1
            for slot in (0, 1):
                self.shared.append(copies.make(pair[slot], full.at[4 + slot], core_peer))
                self.kept.append(
                    pltpu.make_async_copy(pair[slot], full.at[slot], local_sems.at[sem])
                )
                sem += 1

        @pl.when(self.inner)
        def _():
            for copy in self.across[:AHEAD]:
                copy.start()

    def pump(self, steps):
        steps = [step for step in steps if step < len(self.across)]

        @pl.when(self.inner)
        def _():
            for step in steps:
                self.across[step].wait_recv()
                for copy in self.across[step + AHEAD : step + AHEAD + 1]:
                    copy.start()
                self.onward[step].start()
                self.late[step].start()
                self.place[step].start()

        for copy in self.shared + self.kept if 1 in steps else []:
            copy.start()

    def finish(self):
        @pl.when(self.inner)
        def _():
            for copy in self.across + self.onward:
                copy.wait_send()

        @pl.when(self.outer)
        def _():
            for number, copy in enumerate(self.onward):
                copy.wait_recv()
                arrived = number + 1 - 2 * (number % 2)
                self.late[arrived].start()
                self.place[arrived].start()

        for copy in self.kept + self.place:
            copy.wait()
        for copy in self.shared + self.late:
            copy.wait_send()
        for copy in self.shared + self.late:
            copy.wait_recv()


def sum_eighths(
    copies, row_peer, side_peer, send, keep, forward, first, second, store, begin, pump
):
    size = send.shape[0] // 4
    part = lambda ref, slot: ref.at[pl.ds(slot * size, size)]
    arrivals = [
        copies.start(part(send, 1), part(first, 1), row_peer),
        copies.start(part(send, 3), part(first, 3), side_peer),
        copies.start(part(send, 0), part(first, 0), row_peer),
        copies.start(part(send, 2), part(first, 2), side_peer),
    ]
    begin()
    passed = []
    for number, slot, peer in ((0, 1, side_peer), (1, 3, row_peer)):
        arrivals[number].wait_recv()

        def add(row, count, number=number, slot=slot):
            here = pl.ds(slot * size + row, count)
            both = keep[here, :].astype(jnp.float32) + first[here, :].astype(jnp.float32)
            forward[pl.ds(number * size + row, count), :] = both.astype(jnp.bfloat16)

        for_rows(size, add)
        passed.append(copies.start(part(forward, number), part(second, number), peer))
    pump([0])
    for number, slot in ((0, 0), (1, 2)):
        arrivals[2 + number].wait_recv()
        passed[number].wait_recv()

        def total(row, count, number=number, slot=slot):
            here = pl.ds(slot * size + row, count)
            sums = keep[here, :].astype(jnp.float32) + first[here, :].astype(jnp.float32)
            sums = sums + second[pl.ds(number * size + row, count), :].astype(jnp.float32)
            store(number, row, count, sums)

        for_rows(size, total)
        yield number
    for copy in arrivals + passed:
        copy.wait_send()


def halves(terms):
    rows = terms.shape[0] // 2
    return terms.at[pl.ds(0, rows)], terms.at[pl.ds(rows, rows)]


def split_refs(refs, jobs, extra_count, out_count):
    refs = list(refs)
    take = lambda count: [refs.pop(0) for _ in range(count)]
    extras = take(extra_count)
    sources = [take(len(job.sources)) for job in jobs]
    full = take(1)[0]
    outs = take(out_count)
    targets = [take(len(job.outputs)) for job in jobs]
    return extras, sources, full, outs, targets, refs


def spread_kernel(middle, jobs, extra_count, out_count, gain_sum, terms, *refs):
    keep, send = halves(terms)
    extras, sources, full, outs, targets, scratch = split_refs(refs, jobs, extra_count, out_count)
    forward, first, second, send_sems, recv_sems, local_sems, *stages = scratch
    zone, side, row, core = place_here()
    row_peer, side_peer = device(zone, side, 1 - row, core), device(zone, 1 - side, row, core)
    copies = Copies(send_sems, recv_sems)
    size = send.shape[0] // 4
    part = lambda slot: full.at[pl.ds(slot * size, size)]
    for out in outs:
        if out.shape[0] == 1:
            out[...] = jnp.zeros_like(out)
    peers = {}
    for job in jobs:
        peers.update(job.peers(zone, side, row, core))
    greet([row_peer, side_peer] + list(peers.values()))

    def begin():
        spot = 0
        for job, source, target in zip(jobs, sources, targets):
            own_stages = stages[spot : spot + len(job.scratch)]
            job.start(copies, local_sems, source, target, own_stages)
            spot += len(job.scratch)

    def pump(steps):
        for job in jobs:
            job.pump(steps)

    def store(number, row, count, sums):
        own = pl.ds(number * size + row, count)
        full[pl.ds(2 * number * size + row, count), :] = middle(own, sums, extras, outs)

    firsts, seconds = [], []
    for number in sum_eighths(
        copies, row_peer, side_peer, send, keep, forward, first, second, store, begin, pump
    ):
        near, other = (side_peer, row_peer) if number == 0 else (row_peer, side_peer)
        slot = 2 * number
        firsts.append(copies.start(part(slot), part(slot + 1), near))
        seconds.append(copies.start(part(slot), part(4 + slot), other))
    pump([1])
    firsts[0].wait_recv()
    seconds.append(copies.start(part(1), part(5), row_peer))
    firsts[1].wait_recv()
    seconds.append(copies.start(part(3), part(7), side_peer))
    pump(range(2, 64))
    for copy in seconds:
        copy.wait_recv()
    for copy in firsts + seconds:
        copy.wait_send()
    for job in jobs:
        job.finish()


def home_kernel(middle, jobs, extra_count, out_count, gain_sum, terms, *refs):
    keep, send = halves(terms)
    extras, sources, full, outs, targets, scratch = split_refs(refs, jobs, extra_count, out_count)
    forward, first, second, own, send_sems, recv_sems, local_sems, *gain_scratch = scratch
    zone, side, row, core = place_here()
    row_peer, side_peer = device(zone, side, 1 - row, core), device(zone, 1 - side, row, core)
    core_peer = device(zone, side, row, 1 - core)
    copies = Copies(send_sems, recv_sems)
    size = send.shape[0] // 4
    at_home = side == core
    away = side != core
    for out in outs:
        if out.shape[0] == 1:
            out[...] = jnp.zeros_like(out)
    peers = {}
    for job in jobs:
        peers.update(job.peers(zone, side, row, core))
    plane = [row_peer, side_peer, core_peer]
    if gain_sum is not None:
        plane = gain_sum.plane_peers(zone, side, row, core)
        peers.update(gain_sum.zone_peers(zone, side, row, core))
    greet(plane + list(peers.values()))

    def begin():
        for job, source, target in zip(jobs, sources, targets):
            job.start(copies, local_sems, source, target, [])

    def pump(steps):
        for job in jobs:
            job.pump(steps)

    def store(number, start, count, sums):
        here = pl.ds(number * size + start, count)
        values = middle(here, sums, extras, outs)
        own[here, :] = values
        eighth = row * 2 + side if number == 0 else 4 + side * 2 + row

        @pl.when(at_home)
        def _():
            full[pl.ds(pl.multiple_of(eighth * size + start, 32), count), :] = values

    for _ in sum_eighths(
        copies, row_peer, side_peer, send, keep, forward, first, second, store, begin, pump
    ):
        pass
    pump([1])

    def piece(number, x, y):
        start = (x * 2 + y) * size if number == 0 else (4 + y * 2 + x) * size
        return full.at[pl.ds(pl.multiple_of(start, size), size)]

    mine = lambda number: own.at[pl.ds(number * size, size)]
    both = (0, 1)
    to_side = [copies.make(mine(k), piece(k, row, side), side_peer) for k in both]
    to_row = [copies.make(mine(k), piece(k, row, side), row_peer) for k in both]
    pass_row = [
        copies.make(piece(k, row, 1 - side), piece(k, row, 1 - side), row_peer) for k in both
    ]
    share = []
    for number, (x, y) in enumerate(
        ((row, side), (row, 1 - side), (1 - row, side), (1 - row, 1 - side))
    ):
        for k in both:
            source = mine(k) if number == 0 else piece(k, x, y)
            share.append(copies.make(source, piece(k, x, y), core_peer))

    if gain_sum is not None:
        gain_sum.start(copies, extras[-1], outs[0], *gain_scratch)

    @pl.when(away)
    def _():
        for copy in to_side:
            copy.start()

    @pl.when(at_home)
    def _():
        for copy in to_row + share[:2]:
            copy.start()

    if gain_sum is not None:
        gain_sum.middle()

    @pl.when(away)
    def _():
        for copy in to_side:
            copy.wait_send()
        for copy in share:
            copy.wait_recv()

    @pl.when(at_home)
    def _():
        for k in both:
            to_side[k].wait_recv()
            pass_row[k].start()
            share[2 + k].start()
        for k, copy in enumerate(to_row + pass_row):
            copy.wait_recv()
            share[4 + k].start()
        for copy in to_row + pass_row + share:
            copy.wait_send()

    if gain_sum is not None:
        gain_sum.finish(outs[-1])
    for job in jobs:
        job.finish()


def sum_rows(kernel, middle, terms, extras, outs, number, jobs=(), gain_sum=None):
    half, width = terms.shape[0] // 2, terms.shape[1]
    eighth = half // 4
    low = jnp.bfloat16
    vmem, hbm = pl.BlockSpec(memory_space=pltpu.VMEM), pl.BlockSpec(memory_space=pl.ANY)
    scratch = [
        pltpu.VMEM((2 * eighth, width), low),
        pltpu.VMEM((half, width), low),
        pltpu.VMEM((2 * eighth, width), low),
    ]
    if kernel is home_kernel:
        scratch.append(pltpu.VMEM((2 * eighth, width), low))
    copies = (12 if kernel is spread_kernel else 20) + sum(job.count for job in jobs)
    local = max([2] + [job.count_local for job in jobs])
    if gain_sum is not None:
        copies += gain_sum.count
        outs = outs + [gain_sum.output]
    scratch += [pltpu.SemaphoreType.DMA((count,)) for count in (copies, copies, local)]
    if gain_sum is not None:
        scratch += gain_sum.scratch
    scratch += [stage for job in jobs for stage in job.scratch]
    sources = [source for job in jobs for source in job.sources]
    targets = [target for job in jobs for target in job.outputs]
    return pl.pallas_call(
        functools.partial(kernel, middle, jobs, len(extras), len(outs), gain_sum),
        out_shape=[jax.ShapeDtypeStruct((2 * half, width), low)] + outs + targets,
        in_specs=[vmem] * (1 + len(extras) + len(sources)),
        out_specs=[vmem] * (1 + len(outs))
        + [hbm if job.in_hbm else vmem for job in jobs for _ in job.outputs],
        scratch_shapes=scratch,
        compiler_params=pltpu.CompilerParams(
            collective_id=number, has_side_effects=True, vmem_limit_bytes=56 * 2**20
        ),
        cost_estimate=pl.CostEstimate(flops=4 * 10**10, bytes_accessed=10**8, transcendentals=0),
        name=middle.__name__,
    )(terms, *extras, *sources)


def block_columns(plan, width):
    if not plan.ordered:
        return [pl.ds(0, width)], [pl.ds(0, width)]
    zone, _, _, core = place_here()
    size, zones = width // plan.total, plan.zones
    owners = [
        flipped(zone, plan.flips[slot % zones]) * 2 + (core if slot < zones else 1 - core)
        for slot in range(plan.total)
    ]
    natural = [pl.ds(pl.multiple_of(owner * size, size), size) for owner in owners]
    return natural, [pl.ds(slot * size, size) for slot in range(plan.total)]


def copy_rows(source, target):
    def some(row, count):
        target[pl.ds(row, count), :] = source[pl.ds(row, count), :]

    if source.shape[0] % 32:
        target[...] = source[...]
    else:
        for_rows(source.shape[0], some)


def opening_kernel(plan, qkv, gains, gate, out, down, tokens, angles, *refs):
    qkv_full, gains_full, turned_gate, turned_out, turned_down, turned_tokens, turned_angles = refs[:7]
    partner_gate, send_sems, recv_sems, tokens_stage = refs[7:]
    zone, side, row, core = place_here()
    partner = device(zone, core, row, side)
    row_peer, core_peer = device(zone, side, 1 - row, core), device(zone, side, row, 1 - core)
    zone_peers = [device(flipped(zone, flip), side, row, core) for flip in plan.flips[1:]]
    at_home, away = side == core, side != core
    always = [row_peer, core_peer] + zone_peers

    @pl.when(at_home)
    def _():
        greet(always)

    @pl.when(away)
    def _():
        greet(always + [partner])

    copies = Copies(send_sems, recv_sems)
    zones = plan.zones
    own = (gains, qkv, angles, gate, out, down)
    ends = (gains_full.at[0], qkv_full.at[0], turned_angles, turned_gate, turned_out, turned_down)
    turn = [copies.make(source, target, partner) for source, target in zip(own, ends)]
    pieces = 2
    size = tokens.shape[0] // (2 * pieces)
    spots = [
        pl.ds(pl.multiple_of((row * pieces + piece) * size, size), size) for piece in range(pieces)
    ]
    turn_rows = [copies.make(tokens.at[s], tokens_stage.at[s], partner) for s in spots]
    pass_rows = [copies.make(tokens_stage.at[s], tokens_stage.at[s], row_peer) for s in spots]
    natural, local = block_columns(plan, tokens.shape[1])

    def lay_down(all_tokens):
        def some(start, count):
            here = pl.ds(start, count)
            for a, b in zip(natural, local):
                turned_tokens[here, b] = all_tokens[here, a]

        for_rows(all_tokens.shape[0], some)

    slots = list(range(1, zones))
    weights = ((gains, gains_full), (qkv, qkv_full))
    from_own = [
        [copies.make(source, full.at[slot], zone_peers[slot - 1]) for slot in slots]
        + [copies.make(source, full.at[zones], core_peer)]
        for source, full in weights
    ] + [[copies.make(gate, partner_gate, zone_peers[0])]]
    copies.number -= 2 * zones + 1
    from_turned = [
        [copies.make(full.at[0], full.at[slot], zone_peers[slot - 1]) for slot in slots]
        + [copies.make(full.at[0], full.at[zones], core_peer)]
        for _, full in weights
    ] + [[copies.make(turned_gate, partner_gate, zone_peers[0])]]
    cross = [
        [copies.make(full.at[slot], full.at[zones + slot], core_peer) for slot in slots]
        for _, full in weights
    ]

    def cross_over(k):
        for which in (0, 1):
            from_turned[which][k].wait_recv()
            cross[which][k].start()

    @pl.when(away)
    def _():
        for copy in turn[:3]:
            copy.start()
        for which in (0, 1):
            turn[which].wait_recv()
            for copy in from_turned[which]:
                copy.start()
        turn[3].start()
        turn_rows[0].start()
        turn[3].wait_recv()
        from_turned[2][0].start()
        turn_rows[1].start()
        cross_over(0)
        turn_rows[0].wait_recv()
        pass_rows[0].start()
        for copy in turn[4:]:
            copy.start()
        turn_rows[1].wait_recv()
        pass_rows[1].start()

    @pl.when(at_home)
    def _():
        for copy in from_own[0] + from_own[1] + from_own[2]:
            copy.start()
        for source, target in zip(own, ends):
            copy_rows(source, target)
        lay_down(tokens)
        cross_over(0)

    for k in range(1, zones - 1):
        cross_over(k)
    for which in (0, 1):
        from_turned[which][zones - 1].wait_recv()
        for copy in from_turned[which]:
            copy.wait_send()
        for copy in cross[which]:
            copy.wait_recv()
            copy.wait_send()
    from_turned[2][0].wait_recv()
    from_turned[2][0].wait_send()

    @pl.when(away)
    def _():
        for copy in pass_rows + turn[2:3] + turn[4:]:
            copy.wait_recv()
        lay_down(tokens_stage)
        for copy in turn + turn_rows + pass_rows:
            copy.wait_send()


def opening(plan, qkv, gains, gate, out, down, tokens, angles, number):
    vmem = pl.BlockSpec(memory_space=pltpu.VMEM)
    like = lambda v: jax.ShapeDtypeStruct(v.shape, v.dtype)
    whole = lambda v: jax.ShapeDtypeStruct((2 * plan.zones,) + v.shape, v.dtype)
    operands = (qkv, gains, gate, out, down, tokens, angles)
    outputs = [whole(qkv), whole(gains)] + [like(v) for v in (gate, out, down, tokens, angles)]
    outputs += [like(gate)]
    copies = 6 + 4 + 2 * plan.zones + 1 + 2 * (plan.zones - 1)
    return pl.pallas_call(
        functools.partial(opening_kernel, plan),
        out_shape=outputs,
        in_specs=[vmem] * len(operands),
        out_specs=[vmem] * len(outputs),
        scratch_shapes=[
            pltpu.SemaphoreType.DMA((copies,)),
            pltpu.SemaphoreType.DMA((copies,)),
            pltpu.VMEM(tokens.shape, tokens.dtype),
        ],
        compiler_params=pltpu.CompilerParams(
            collective_id=number, has_side_effects=True, vmem_limit_bytes=56 * 2**20
        ),
        cost_estimate=pl.CostEstimate(flops=4 * 10**10, bytes_accessed=10**8, transcendentals=0),
        name="opening",
    )(*operands)


def inverse_rms(values):
    return lax.rsqrt(jnp.mean(values * values, -1, keepdims=True) + EPS_NORM)


def hidden_rows(own, sums, extras, outs):
    tokens, gain = extras
    hidden = tokens[own, :].astype(jnp.float32) + sums
    outs[0][own, :] = hidden
    return (hidden * inverse_rms(hidden) * gain[...]).astype(jnp.bfloat16)


def grad_hidden_rows(own, sums, extras, outs):
    hidden, out_grad, gain = extras
    values = hidden[own, :]
    factor = inverse_rms(values)
    unit = values * factor
    outs[1][...] += jnp.sum(sums * unit, 0, keepdims=True)
    grad = out_grad[own, :].astype(jnp.float32) + norm_back(sums * gain[...], unit, factor)
    outs[0][own, :] = grad
    return grad.astype(jnp.bfloat16)


def grad_input_rows(own, sums, extras, outs):
    tokens, grad_hidden, gain = extras[:3]
    values = tokens[own, :].astype(jnp.float32)
    factor = inverse_rms(values)
    unit = values * factor
    outs[0][...] += jnp.sum(sums * unit, 0, keepdims=True)
    return (grad_hidden[own, :] + norm_back(sums * gain[...], unit, factor)).astype(jnp.bfloat16)


def dot(left, right, left_dim=1, right_dim=0):
    return lax.dot_general(
        left, right, (((left_dim,), (right_dim,)), ((), ())), preferred_element_type=jnp.float32
    )


def turn_head(values, cosine, signed_sine):
    return values * cosine + pltpu.roll(values, HEAD // 2, 1) * signed_sine


def turn_back(gradient, cosine, signed_sine):
    return gradient * cosine + pltpu.roll(gradient * signed_sine, HEAD // 2, 1)


def softmax_block(query, key, first_row):
    rows, keys = query.shape[0], key.shape[0]
    scores = dot(query, key, 1, 1)
    row_at = lax.broadcasted_iota(jnp.int32, (rows, keys), 0) + first_row
    key_at = lax.broadcasted_iota(jnp.int32, (rows, keys), 1)
    scores = jnp.where(key_at <= row_at, scores, -1000000000.0)
    exponent = jnp.exp(scores - jnp.max(scores, -1, keepdims=True))
    return exponent / jnp.sum(exponent, -1, keepdims=True)


def eighth_owners():
    _, side, row, _ = place_here()
    own, off = (row, side), (1 - row, 1 - side)
    first = lambda x, y: x * 2 + y
    second = lambda x, y: 4 + y * 2 + x
    return [
        first(own[0], own[1]),
        first(own[0], off[1]),
        second(own[0], own[1]),
        second(off[0], own[1]),
        first(off[0], own[1]),
        first(off[0], off[1]),
        second(own[0], off[1]),
        second(off[0], off[1]),
    ]


def reorder_rows(source, target, into_local):
    size = source.shape[0] // 8
    for slot, owner in enumerate(eighth_owners()):
        natural = pl.ds(pl.multiple_of(owner * size, size), size)
        local = pl.ds(slot * size, size)
        if into_local:
            target[local, :] = source[natural, :]
        else:
            target[natural, :] = source[local, :]


def forward_kernel(
    tokens, weights, gain_in, gain_q, gain_k, cosine, sine,
    normed, raw, query, key, value, local, attended,
):
    low = jnp.bfloat16
    total, heads = tokens.shape[0], query.shape[1] // HEAD
    block, wide = 256, 512

    def project(step, carry):
        rows = pl.ds(pl.multiple_of(step * wide, wide), wide)
        values = tokens[rows, :].astype(jnp.float32)
        normed[rows, :] = (values * inverse_rms(values) * gain_in[...]).astype(low)
        raw[rows, :] = dot(normed[rows, :], weights[...])
        turns = (cosine[rows, :], sine[rows, :])
        for head in range(heads):
            column = (head // 2) * 4 * HEAD + (head % 2) * HEAD
            values = raw[rows, pl.ds(column, HEAD)]
            values = turn_head(values * inverse_rms(values) * gain_q[...], *turns)
            query[rows, pl.ds(head * HEAD, HEAD)] = (values * (1.0 / math.sqrt(HEAD))).astype(low)
        for group in range(heads // 2):
            column = group * 4 * HEAD + 2 * HEAD
            here = pl.ds(group * HEAD, HEAD)
            values = raw[rows, pl.ds(column, HEAD)]
            values = turn_head(values * inverse_rms(values) * gain_k[...], *turns)
            key[rows, here] = values.astype(low)
            value[rows, here] = raw[rows, pl.ds(column + HEAD, HEAD)].astype(low)
        return carry

    lax.fori_loop(0, total // wide, project, 0)

    def attend(head, carry):
        mine = pl.ds(pl.multiple_of(head * HEAD, HEAD), HEAD)
        shared = pl.ds(pl.multiple_of(lax.div(head, 2) * HEAD, HEAD), HEAD)
        for start in range(0, total, SEQ):
            for first in range(0, SEQ, block):
                rows, keys = pl.ds(start + first, block), pl.ds(start, first + block)
                probs = softmax_block(query[rows, mine], key[keys, shared], first)
                attended[rows, mine] = dot(probs.astype(low), value[keys, shared]).astype(low)
        return carry

    lax.fori_loop(0, heads, attend, 0)
    reorder_rows(attended, local, True)


def attention(tokens, weights, gain_in, gain_q, gain_k, cosine, sine):
    total = tokens.shape[0]
    columns = weights.shape[1]
    low = jnp.bfloat16
    shape = lambda width, kind=low: jax.ShapeDtypeStruct((total, width), kind)
    vmem = pl.BlockSpec(memory_space=pltpu.VMEM)
    return pl.pallas_call(
        forward_kernel,
        out_shape=[
            shape(tokens.shape[1]),
            shape(columns, jnp.float32),
            shape(columns // 2),
            shape(columns // 4),
            shape(columns // 4),
            shape(columns // 2),
        ],
        in_specs=[vmem] * 7,
        out_specs=[vmem] * 6,
        scratch_shapes=[pltpu.VMEM((total, columns // 2), low)],
        compiler_params=pltpu.CompilerParams(vmem_limit_bytes=48 * 2**20),
        cost_estimate=pl.CostEstimate(flops=10**10, bytes_accessed=2 * 10**7, transcendentals=0),
        name="attention",
    )(tokens, weights, gain_in, gain_q, gain_k, cosine, sine)


def backward_kernel(
    query, key, value, raw, grad_rows, gain_q, gain_k, cosine, sine,
    mixed, mixed_local, query_gain, key_gain, grad, key_sum, value_sum,
):
    low = jnp.bfloat16
    total, heads = query.shape[0], query.shape[1] // HEAD
    block = 256
    reorder_rows(grad_rows, grad, False)
    query_gain[...] = jnp.zeros_like(query_gain)
    key_gain[...] = jnp.zeros_like(key_gain)

    def head_norm_back(rows, column, gradient, gain, gain_grad):
        values = raw[rows, column]
        factor = inverse_rms(values)
        unit = values * factor
        turned = turn_back(gradient, cosine[rows, :], sine[rows, :])
        gain_grad[...] += jnp.sum(turned * unit, 0, keepdims=True)
        mixed[rows, column] = norm_back(turned * gain[...], unit, factor).astype(low)

    def one_group(group, carry):
        at = lambda offset: pl.ds(pl.multiple_of(group * 4 * HEAD + offset * HEAD, HEAD), HEAD)
        shared = pl.ds(pl.multiple_of(group * HEAD, HEAD), HEAD)
        key_sum[...] = jnp.zeros_like(key_sum)
        value_sum[...] = jnp.zeros_like(value_sum)
        for head in (0, 1):
            mine = pl.ds(pl.multiple_of((group * 2 + head) * HEAD, HEAD), HEAD)
            for start in range(0, total, SEQ):
                for first in range(0, SEQ, block):
                    rows, keys = pl.ds(start + first, block), pl.ds(start, first + block)
                    query_part, grad_part = query[rows, mine], grad[rows, mine]
                    probs = softmax_block(query_part, key[keys, shared], first)
                    weighed = probs * dot(grad_part, value[keys, shared], 1, 1)
                    scores = weighed - probs * jnp.sum(weighed, -1, keepdims=True)
                    scores = scores.astype(low)
                    grad_query = dot(scores, key[keys, shared]) * (1.0 / math.sqrt(HEAD))
                    head_norm_back(rows, at(head), grad_query, gain_q, query_gain)
                    key_sum[keys, :] += dot(scores, query_part, 0, 0)
                    value_sum[keys, :] += dot(probs.astype(low), grad_part, 0, 0)
        for first in range(0, total, block):
            rows = pl.ds(first, block)
            head_norm_back(rows, at(2), key_sum[rows, :], gain_k, key_gain)
            mixed[rows, at(3)] = value_sum[rows, :].astype(low)
        return carry

    lax.fori_loop(0, heads // 2, one_group, 0)
    reorder_rows(mixed, mixed_local, True)


def attention_back(query, key, value, raw, grad_rows, gain_q, gain_k, cosine, sine):
    total, columns = raw.shape
    low = jnp.bfloat16
    vmem = pl.BlockSpec(memory_space=pltpu.VMEM)
    return pl.pallas_call(
        backward_kernel,
        out_shape=[
            jax.ShapeDtypeStruct((total, columns), low),
            jax.ShapeDtypeStruct((total, columns), low),
            jax.ShapeDtypeStruct((1, HEAD), jnp.float32),
            jax.ShapeDtypeStruct((1, HEAD), jnp.float32),
        ],
        in_specs=[vmem] * 9,
        out_specs=[vmem] * 4,
        scratch_shapes=[
            pltpu.VMEM(grad_rows.shape, low),
            pltpu.VMEM((total, HEAD), jnp.float32),
            pltpu.VMEM((total, HEAD), jnp.float32),
        ],
        compiler_params=pltpu.CompilerParams(vmem_limit_bytes=48 * 2**20),
        cost_estimate=pl.CostEstimate(flops=10**10, bytes_accessed=2 * 10**7, transcendentals=0),
        name="attention_back",
    )(query, key, value, raw, grad_rows, gain_q, gain_k, cosine, sine)


def feed_kernel(plan, rows, own_grad, got_grad, gate_up, up_part, down, active, grads, out_grad):
    low = jnp.bfloat16
    block = 512
    tile = down.shape[1]
    step = pl.program_id(0)
    gate_at = pl.ds(pl.multiple_of(step * tile, tile), tile)
    up_at = pl.ds(pl.multiple_of(grads.shape[1] // 2 + step * tile, tile), tile)
    _, side, _, core = place_here()

    def lay_down(source):
        natural, blocks = block_columns(plan, source.shape[1])
        eighth = source.shape[0] // 8
        for slot, owner in enumerate(eighth_owners()):

            def some(start, count, slot=slot, owner=owner):
                here = pl.ds(pl.multiple_of(owner * eighth + start, 32), count)
                there = pl.ds(slot * eighth + start, count)
                for a, b in zip(natural, blocks):
                    out_grad[there, b] = source[here, a]

            for_rows(eighth, some)

    @pl.when((step == 0) & (side == core))
    def _():
        lay_down(own_grad)

    @pl.when((step == 0) & (side != core))
    def _():
        lay_down(got_grad)

    def one(block_at, carry):
        here = pl.ds(pl.multiple_of(block_at * block, block), block)
        gate = dot(rows[here, :], gate_up[...])
        up = dot(rows[here, :], up_part[...])
        grad = dot(out_grad[here, :], down[...])
        sigmoid = jax.nn.sigmoid(gate)
        silu = gate * sigmoid
        active[here, :] = (silu * up).astype(low)
        grads[here, gate_at] = (grad * up * sigmoid * (1.0 + gate * (1.0 - sigmoid))).astype(low)
        grads[here, up_at] = (grad * silu).astype(low)
        return carry

    lax.fori_loop(0, rows.shape[0] // block, one, 0)


def feed_forward(plan, rows, own_grad, got_grad, gate_up, down, tile):
    total, width = rows.shape
    units = down.shape[1]
    low = jnp.bfloat16
    tiles = units // tile
    whole = pl.BlockSpec(memory_space=pltpu.VMEM)
    return pl.pallas_call(
        functools.partial(feed_kernel, plan),
        grid=(tiles,),
        out_shape=[
            jax.ShapeDtypeStruct((total, units), low),
            jax.ShapeDtypeStruct((total, 2 * units), low),
            jax.ShapeDtypeStruct((total, width), low),
        ],
        in_specs=[
            whole,
            whole,
            whole,
            pl.BlockSpec((width, tile), lambda step: (0, step)),
            pl.BlockSpec((width, tile), lambda step: (0, step + tiles)),
            pl.BlockSpec((width, tile), lambda step: (0, step)),
        ],
        out_specs=[
            pl.BlockSpec((total, tile), lambda step: (0, step)),
            whole,
            whole,
        ],
        compiler_params=pltpu.CompilerParams(vmem_limit_bytes=56 * 2**20),
        cost_estimate=pl.CostEstimate(
            flops=6 * total * width * units, bytes_accessed=4 * 10**7, transcendentals=total * units
        ),
        name="feed_forward",
    )(rows, own_grad, got_grad, gate_up, gate_up, down)


class Plan:
    def __init__(self, mesh):
        self.total = mesh.shape["dp"]
        self.zones = self.total // 2
        self.tensor = mesh.shape["tensor"]
        self.flips = [k ^ (k >> 1) for k in range(self.zones)]

    def place(self):
        self.index = lax.axis_index("dp")
        self.zone = self.index // 2
        self.side = self.index % 2
        self.row = lax.axis_index("tensor") // 2
        self.core = lax.axis_index("tensor") % 2
        self.home = self.side == self.core

    def move(self, value, target):
        pairs = []
        for d in range(self.total):
            for t in range(self.tensor):
                to = target(d // 2, d % 2, t // 2, t % 2)
                if to is not None:
                    zone, side, row, core = to
                    pairs.append((d * self.tensor + t, (zone * 2 + side) * self.tensor + row * 2 + core))
        return lax.ppermute(value, ("dp", "tensor"), pairs)

    def turn(self, value):
        got = self.move(value, lambda z, y, x, c: (z, c, x, y) if y != c else None)
        return jnp.where(self.home, value, got)

    def zone_flip(self, value, bit):
        return self.move(value, lambda z, y, x, c: (z ^ bit, y, x, c))

    def core_swap(self, value):
        return self.move(value, lambda z, y, x, c: (z, y, x, 1 - c))

    def side_swap(self, value):
        return self.move(value, lambda z, y, x, c: (z, 1 - y, x, c))

    def row_swap(self, value):
        return self.move(value, lambda z, y, x, c: (z, y, 1 - x, c))

    def to_local(self, value, axis):
        width = value.shape[axis] // self.total
        parts = []
        for core in (self.core, 1 - self.core):
            for slot in range(self.zones):
                owner = (self.zone ^ self.flips[slot]) * 2 + core
                parts.append(lax.dynamic_slice_in_dim(value, owner * width, width, axis))
        return jnp.concatenate(parts, axis)

    def to_natural(self, value, axis, core=None):
        core = self.core if core is None else core
        width = value.shape[axis] // self.total
        parts = []
        for block in range(self.total):
            slot = flip = (block // 2) ^ self.zone
            for bits in range(1, self.zones.bit_length()):
                slot = slot ^ (flip >> bits)
            slot = slot + jnp.where(block % 2 == core, 0, self.zones)
            parts.append(lax.dynamic_slice_in_dim(value, slot * width, width, axis))
        return jnp.concatenate(parts, axis)

    def row_owners(self):
        own, off = (self.row, self.side), (1 - self.row, 1 - self.side)
        first = lambda x, y: x * 2 + y
        second = lambda x, y: 4 + y * 2 + x
        return [
            first(own[0], own[1]),
            first(own[0], off[1]),
            second(own[0], own[1]),
            second(off[0], own[1]),
            first(off[0], own[1]),
            first(off[0], off[1]),
            second(own[0], off[1]),
            second(off[0], off[1]),
        ]

    def rows_local(self, value, slots=range(8)):
        size = value.shape[0] // 8
        owners = self.row_owners()
        return jnp.concatenate(
            [lax.dynamic_slice_in_dim(value, owners[slot] * size, size, 0) for slot in slots], 0
        )

    def rows_natural(self, value, order=range(8)):
        size = value.shape[0] // 8
        place = [list(order).index(slot) for slot in range(8)]
        parts = []
        for piece in range(8):
            x, y = (piece // 2, piece % 2) if piece < 4 else (piece % 2, (piece - 4) // 2)
            slots = (0, 1, 4, 5) if piece < 4 else (2, 6, 3, 7)
            same_x, same_y = x == self.row, y == self.side
            slot = jnp.where(
                same_x,
                jnp.where(same_y, place[slots[0]], place[slots[1]]),
                jnp.where(same_y, place[slots[2]], place[slots[3]]),
            )
            parts.append(lax.dynamic_slice_in_dim(value, slot * size, size, 0))
        return jnp.concatenate(parts, 0)

    def from_zones(self, shard):
        return [self.zone_flip(shard, flip) for flip in self.flips[1:]]

    def to_zones(self, parts, slots):
        return [self.zone_flip(parts[slot], self.flips[slot]) for slot in slots]

    def middle_swap(self, pair):
        return self.move(pair, lambda z, y, x, c: (z ^ 3, y, x, c) if z in (1, 2) else None)

    def inward(self, part):
        return self.move(part, lambda z, y, x, c: (z ^ 1, y, x, c) if z in (0, 3) else None)

    def pass_outward(self, pair):
        return self.move(pair, lambda z, y, x, c: (z ^ 1, y, x, c) if z in (1, 2) else None)

    def far_pair(self, middle, passed):
        inner = (self.zone == 1) | (self.zone == 2)
        return jnp.where(inner, middle, passed[::-1])

    def first_swap(self, send):
        half = send.shape[0] // 2
        return self.row_swap(send[:half]), self.side_swap(send[half:])

    def second_swap(self, keep, got):
        quarter = keep.shape[0] // 4
        row_part = keep[: 2 * quarter] + got[0].astype(jnp.float32)
        side_part = keep[2 * quarter :] + got[1].astype(jnp.float32)
        own = jnp.concatenate([row_part[:quarter], side_part[:quarter]], 0)
        return own, (
            self.side_swap(row_part[quarter:].astype(jnp.bfloat16)),
            self.row_swap(side_part[quarter:].astype(jnp.bfloat16)),
        )

    def spread_first(self, own):
        half = own.shape[0] // 2
        return (self.side_swap(own[:half]), self.row_swap(own[half:]))

    def spread_second(self, own, got):
        half = own.shape[0] // 2
        row_part = jnp.concatenate([own[:half], got[0]], 0)
        side_part = jnp.concatenate([own[half:], got[1]], 0)
        return row_part, side_part, self.row_swap(row_part), self.side_swap(side_part)

    def send_home(self, own):
        to_home = lambda z, y, x, c: (z, c, x, c) if y != c else None
        return jnp.concatenate([own, self.move(own, to_home)], 0)

    def row_home(self, part):
        return self.move(part, lambda z, y, x, c: (z, y, 1 - x, c) if y == c else None)

    def share_home(self, part, other):
        full = jnp.concatenate([part, other], 0)
        full = self.to_natural(self.rows_natural(full, (0, 2, 1, 6, 4, 3, 5, 7)), 1)
        got = self.move(full, lambda z, y, x, c: (z, y, x, 1 - c) if y == c else None)
        return full, got

    def turned(self, own, got):
        return jnp.where(self.home, own, got)

    def sum_everywhere(self, value):
        value = value + self.row_swap(value)
        value = value + self.side_swap(value)
        value = value + self.core_swap(value)
        bit = 1
        while bit < self.zones:
            value = value + self.zone_flip(value, bit)
            bit *= 2
        return value


def shards(
    plan,
    tokens,
    positions,
    out_grad,
    qkv_weight,
    qkv_first,
    qkv_second,
    out_weight,
    out_first,
    out_second,
    gate_up,
    gate_up_first,
    gate_up_second,
    down_weight,
    down_first,
    down_second,
    gains,
    gains_first,
    gains_second,
):
    plan.place()
    low = jnp.bfloat16
    tok_rows, model_width = tokens.shape
    groups = qkv_weight.shape[1]
    head_size = qkv_weight.shape[3]
    shard_rows = qkv_weight.shape[0]
    seq_count = tok_rows // SEQ
    mixed_cols = groups * 4 * head_size
    near_cols = model_width // 2
    kept = tok_rows // 2
    gain_count = gains.shape[0]

    tree = plan.zones == 4
    slots = range(1, plan.zones)

    def column_parts(value):
        return value.reshape((plan.zones, -1) + value.shape[1:])

    units = gate_up.shape[2]
    plan.ordered = (model_width // plan.total) % 128 == 0
    gain_rows = 16
    gain_block = jnp.pad(gains.astype(low), (0, gain_rows * 128 - gain_count)).reshape(gain_rows, 128)
    low_qkv = qkv_weight.reshape(shard_rows, mixed_cols).astype(low)
    tile = min(units, 256)
    low_gate = jnp.concatenate([gate_up[0].astype(low), gate_up[1].astype(low)], 1)
    angle_at = positions.astype(jnp.float32).reshape(-1, 128)
    (
        both_qkv,
        both_gains,
        turned_gate,
        turned_out,
        turned_down,
        tokens,
        angle_at,
        partner_gate,
    ) = opening(
        plan,
        low_qkv,
        gain_block,
        low_gate,
        out_weight.astype(low),
        down_weight.astype(low),
        tokens,
        angle_at,
        3,
    )
    positions = angle_at.reshape(-1)
    turned_out, turned_gate, turned_down, tokens, positions, both_qkv, both_gains, out_grad = fence(
        turned_out, turned_gate, turned_down, tokens, positions, both_qkv, both_gains, out_grad
    )

    got_grad = plan.move(out_grad, lambda z, y, x, c: (z, c, x, y) if y != c else None)
    zone_out = plan.from_zones(turned_out)
    if tree:
        partner_down = plan.zone_flip(turned_down, 1)
    else:
        partner_down = plan.from_zones(turned_down)
        partner_gate = plan.from_zones(turned_gate)
    if not plan.ordered:
        tokens = plan.to_local(tokens, 1)
    cosine, sine_table = rotary(positions, head_size)
    signed_sine = jnp.concatenate(
        [-sine_table[:, : head_size // 2], sine_table[:, head_size // 2 :]], 1
    )
    full_qkv = both_qkv.reshape(model_width, mixed_cols)
    gain_slots = both_gains.reshape(plan.total, -1)[:, :gain_count]
    gain_all = plan.to_natural(gain_slots.reshape(-1), 0).astype(jnp.float32)
    gain_in = plan.to_local(gain_all[:model_width], 0)[None]
    gain_post = plan.to_local(gain_all[model_width : 2 * model_width], 0)[None]
    gain_q = gain_all[2 * model_width : 2 * model_width + head_size][None]
    gain_k = gain_all[2 * model_width + head_size :][None]
    normed, raw, query, key_rot, values_low, attended = attention(
        tokens, full_qkv, gain_in, gain_q, gain_k, cosine, signed_sine
    )
    attended, zone_out, turned_out, partner_down, turned_down, turned_gate, partner_gate = fence(
        attended, zone_out, turned_out, partner_down, turned_down, turned_gate, partner_gate
    )

    near_out = jnp.concatenate([turned_out] + zone_out, 0)
    far_out = plan.core_swap(near_out)
    own_tokens = plan.rows_local(tokens, (0, 2))
    near_out, far_out, own_tokens = fence(near_out, far_out, own_tokens)

    full_out = jnp.concatenate([near_out, far_out], 0)
    branch_terms = contract_cols(attended, full_out).astype(low)
    pairs = [(turned_gate, partner_gate), (turned_down, partner_down)]
    normed_rows, hidden, *gathered = sum_rows(
        spread_kernel,
        hidden_rows,
        branch_terms,
        [own_tokens, gain_post],
        [jax.ShapeDtypeStruct((tok_rows // 4, model_width), jnp.float32)],
        0,
        [PairTree(pairs, (2, 1))] if tree else [],
    )
    if not tree:
        near = [jnp.concatenate([own] + rest, 0) for own, rest in pairs]
        gathered = [jnp.concatenate([part, plan.core_swap(part)], 0) for part in near]
    full_gate = gathered[0].reshape(model_width, 2 * units)
    full_down = gathered[1].reshape(model_width, units)
    normed_rows, hidden, full_gate, full_down, got_grad = fence(
        normed_rows, hidden, full_gate, full_down, got_grad
    )

    def zone_parts(near, got):
        both = (near + got.astype(jnp.float32)).astype(low)
        return both.reshape((plan.zones, -1) + both.shape[1:])

    def zone_total(parts, *arrived):
        total = parts[0].astype(jnp.float32)
        for part in sum([list(group) for group in arrived], []):
            total = total + part.astype(jnp.float32)
        return total.astype(low)

    active, grad_both, out_grad = feed_forward(
        plan, normed_rows, out_grad, got_grad, full_gate, full_down, tile
    )
    if not plan.ordered:
        out_grad = plan.to_local(out_grad, 1)
    mlp_terms = contract_cols(active, full_down).astype(low)
    mlp_terms, active, grad_both, out_grad = fence(mlp_terms, active, grad_both, out_grad)

    mlp_got = plan.first_swap(mlp_terms[kept:])
    down_far = contract_rows(out_grad[:, near_cols:], active).astype(low)
    down_got = plan.core_swap(down_far)
    gate_far = contract_rows(normed_rows[:, near_cols:], grad_both).astype(low)
    down_parts = zone_parts(contract_rows(out_grad[:, :near_cols], active), down_got)
    down_parts, gate_far, grad_both, mlp_got, mlp_terms = fence(
        down_parts, gate_far, grad_both, mlp_got, mlp_terms
    )

    gate_got = plan.core_swap(gate_far)
    if tree:
        inner_terms = plan.inward(down_parts[3])
    else:
        inner_terms = plan.to_zones(down_parts, slots)
    mlp_own, mlp_last = plan.second_swap(mlp_terms[:kept].astype(jnp.float32), mlp_got)
    post_terms = contract_cols(grad_both, full_gate).astype(low)
    mlp_own, mlp_last, post_terms, gate_got, inner_terms, down_parts = fence(
        mlp_own, mlp_last, post_terms, gate_got, inner_terms, down_parts
    )

    block_own = (hidden + mlp_own + jnp.concatenate(mlp_last, 0).astype(jnp.float32)).astype(low)
    block_home = plan.send_home(block_own)
    down_sums = jnp.stack([inner_terms, plan.inward(down_parts[2])]) if tree else inner_terms
    gate_parts = zone_parts(contract_rows(normed_rows[:, :near_cols], grad_both), gate_got)
    post_terms, gate_parts, down_parts, down_sums, block_home = fence(
        post_terms, gate_parts, down_parts, down_sums, block_home
    )

    eighth = tok_rows // 8
    own_grad = jnp.concatenate([out_grad[:eighth], out_grad[2 * eighth : 3 * eighth]], 0)
    branch_rows, grad_hidden, post_gain_grad, gate_sums = sum_rows(
        spread_kernel,
        grad_hidden_rows,
        post_terms,
        [hidden, own_grad, gain_post],
        [
            jax.ShapeDtypeStruct((tok_rows // 4, model_width), jnp.float32),
            jax.ShapeDtypeStruct((1, model_width), jnp.float32),
        ],
        1,
        [PairScatter(gate_parts, 2) if tree else ZoneBlocks(plan, gate_parts, slots)],
    )
    if tree:
        down_pair = (down_parts[2:].astype(jnp.float32) + down_sums.astype(jnp.float32)).astype(low)
    else:
        down_pair = down_parts
    branch_rows, grad_hidden, post_gain_grad, gate_sums, block_home, down_parts, down_pair = fence(
        branch_rows, grad_hidden, post_gain_grad, gate_sums, block_home, down_parts, down_pair
    )

    block_row = plan.row_home(block_home)
    if tree:
        gate_last = [plan.zone_flip(gate_sums[1], 1)]
        gate_own = gate_sums
        down_sums = plan.middle_swap(down_pair)
    else:
        gate_last, gate_own = gate_sums, gate_parts
    grad_att = jnp.dot(branch_rows, full_out, preferred_element_type=jnp.float32).astype(low)
    grad_mixed, mixed_rows, query_gain_grad, key_gain_grad = attention_back(
        query, key_rot, values_low, raw, grad_att, gain_q, gain_k, cosine, signed_sine
    )
    gain_terms = jnp.concatenate(
        [plan.to_natural(post_gain_grad, 1), query_gain_grad, key_gain_grad], 1
    )
    if tree:
        down_own = (down_parts[:2].astype(jnp.float32) + down_sums.astype(jnp.float32)).astype(low)
    grad_mixed, mixed_rows, gain_terms, normed, gate_last, branch_rows, block_row, down_sums = fence(
        grad_mixed, mixed_rows, gain_terms, normed, gate_last, branch_rows, block_row, down_sums
    )

    if tree:
        total_down = zone_total(down_own, [plan.zone_flip(down_own[1], 1)])
    else:
        total_down = zone_total(down_parts, down_sums)
    total_gate = zone_total(gate_own, gate_last)
    summed_gate = plan.turn(jnp.stack([total_gate[:, :units], total_gate[:, units:]]))
    out_far = contract_rows(branch_rows[:, near_cols:], attended).astype(low)
    out_got = plan.core_swap(out_far)
    qkv_far = contract_rows(normed[:, near_cols:], grad_mixed).astype(low)
    qkv_got = plan.core_swap(qkv_far)
    normed_terms = contract_cols(mixed_rows, full_qkv).astype(low)
    block_full, block_got = plan.share_home(block_home, block_row)
    out_parts = zone_parts(contract_rows(branch_rows[:, :near_cols], attended), out_got)
    qkv_parts = zone_parts(contract_rows(normed[:, :near_cols], grad_mixed), qkv_got)
    block_full, block_got, out_parts, qkv_parts, normed_terms, summed_gate, total_down = fence(
        block_full, block_got, out_parts, qkv_parts, normed_terms, summed_gate, total_down
    )
    block_out = jnp.where(plan.home, block_full, block_got)

    gain_sum = GainSum(plan, gain_terms.shape[1], model_width) if plan.ordered else None
    input_full, input_gain_grad, *rest = sum_rows(
        home_kernel,
        grad_input_rows,
        normed_terms,
        [own_tokens, grad_hidden, gain_in] + ([gain_terms] if plan.ordered else []),
        [jax.ShapeDtypeStruct((1, model_width), jnp.float32)],
        2,
        [ZoneBlocks(plan, qkv_parts, slots), ZoneBlocks(plan, out_parts, slots, 1)],
        gain_sum,
    )
    if plan.ordered:
        summed_gains, qkv_sent, out_sent = rest
    else:
        qkv_sent, out_sent = rest
        summed_gains = plan.sum_everywhere(
            jnp.concatenate([plan.to_natural(input_gain_grad, 1), gain_terms], 1)
        )
    summed_down = plan.turn(total_down)
    input_full, summed_gains, qkv_sent, out_sent, summed_down = fence(
        input_full, summed_gains, qkv_sent, out_sent, summed_down
    )

    summed_both = plan.turn(
        jnp.concatenate([zone_total(qkv_parts, qkv_sent), zone_total(out_parts, out_sent)], 1)
    ).astype(jnp.float32)
    summed_qkv = summed_both[:, :mixed_cols].reshape(qkv_weight.shape)
    summed_out = summed_both[:, mixed_cols:]
    summed_gate = summed_gate.astype(jnp.float32)
    summed_down = summed_down.astype(jnp.float32)
    summed_gains = lax.dynamic_slice_in_dim(summed_gains[0], plan.index * gain_count, gain_count, 0)
    input_rows = plan.to_natural(input_full, 1, plan.side).astype(jnp.float32)

    qkv_moment, qkv_square, qkv_updated = adamw(
        qkv_weight, summed_qkv, qkv_first, qkv_second, RATE_QKV, DECAY_RATE
    )
    out_moment, out_square, out_updated = adamw(
        out_weight, summed_out, out_first, out_second, RATE_OUT, DECAY_RATE
    )
    gate_moment, gate_square, gate_updated = adamw(
        gate_up, summed_gate, gate_up_first, gate_up_second, RATE_GATE, DECAY_RATE
    )
    down_moment, down_square, down_updated = adamw(
        down_weight, summed_down, down_first, down_second, RATE_DOWN, DECAY_RATE
    )
    gain_moment, gain_square, gain_updated = adamw(
        gains, summed_gains, gains_first, gains_second, RATE_GAIN, 0.0
    )
    return (
        block_out,
        input_rows,
        qkv_moment,
        qkv_square,
        qkv_updated,
        out_moment,
        out_square,
        out_updated,
        gate_moment,
        gate_square,
        gate_updated,
        down_moment,
        down_square,
        down_updated,
        gain_moment,
        gain_square,
        gain_updated,
    )


def solution(mesh):
    plan = Plan(mesh)
    placed = (
        P("dp", None),
        P("dp"),
        P("dp", None),
        P("dp", "tensor", None, None),
        P("dp", "tensor", None, None),
        P("dp", "tensor", None, None),
        P("dp", "tensor"),
        P("dp", "tensor"),
        P("dp", "tensor"),
        P(None, "dp", "tensor"),
        P(None, "dp", "tensor"),
        P(None, "dp", "tensor"),
        P("dp", "tensor"),
        P("dp", "tensor"),
        P("dp", "tensor"),
        P("dp"),
        P("dp"),
        P("dp"),
    )
    return jax.shard_map(
        functools.partial(shards, plan),
        mesh=mesh,
        in_specs=placed,
        out_specs=(
            P("dp", None),
            P("dp", None),
            P("dp", "tensor", None, None),
            P("dp", "tensor", None, None),
            P("dp", "tensor", None, None),
            P("dp", "tensor"),
            P("dp", "tensor"),
            P("dp", "tensor"),
            P(None, "dp", "tensor"),
            P(None, "dp", "tensor"),
            P(None, "dp", "tensor"),
            P("dp", "tensor"),
            P("dp", "tensor"),
            P("dp", "tensor"),
            P("dp"),
            P("dp"),
            P("dp"),
        ),
        check_vma=False,
    )
```

```python
import functools
import math

import jax
import jax.numpy as jnp
from jax import lax
from jax.experimental import pallas as pl
from jax.experimental.pallas import tpu as pltpu
from jax.sharding import PartitionSpec as P

SEQ = 1024
STEP = 10


EPS_NORM = 1e-06
THETA = 1000000.0
BETA_ONE = 0.9
BETA_TWO = 0.95
ADAM_EPS = 1e-08
DECAY_RATE = 0.1
RATE_QKV = 0.05
RATE_OUT = 0.3
RATE_GATE = 0.05
RATE_DOWN = 0.03
RATE_GAIN = 1.0


def rotary(positions, head_size):
    freq_index = jnp.arange(head_size // 2, dtype=jnp.float32)
    inverse = jnp.exp(freq_index * (-2.0 * math.log(THETA) / head_size))
    angles = positions.astype(jnp.float32)[:, None] * inverse[None, :]
    cosine = jnp.cos(angles)
    sine_table = jnp.sin(angles)
    return (jnp.concatenate([cosine, cosine], -1), jnp.concatenate([sine_table, sine_table], -1))


def rotate(values, cosine, sine_table):
    half_size = values.shape[-1] // 2
    turned = jnp.concatenate([-values[..., half_size:], values[..., :half_size]], -1)
    return values * cosine[:, None, :] + turned * sine_table[:, None, :]


def unrotate(gradient, cosine, sine_table):
    half_size = gradient.shape[-1] // 2
    turned = gradient * sine_table[:, None, :]
    rotated_back = jnp.concatenate([turned[..., half_size:], -turned[..., :half_size]], -1)
    return gradient * cosine[:, None, :] + rotated_back


def norm_back(grad_unit, unit_vals, factor):
    return factor * (grad_unit - unit_vals * jnp.mean(grad_unit * unit_vals, -1, keepdims=True))


def contract_rows(left, right):
    return lax.dot_general(
        left, right, (((0,), (0,)), ((), ())), preferred_element_type=jnp.float32
    )


def contract_cols(left, right):
    return lax.dot_general(
        left, right, (((1,), (1,)), ((), ())), preferred_element_type=jnp.float32
    )


def block_scores(query_part, key_part, first_row, block_rows, last_row):
    scores = jnp.einsum(
        "nqkgd,nskd->nkgqs", query_part, key_part, preferred_element_type=jnp.float32
    )
    causal = (first_row + jnp.arange(block_rows))[:, None] >= jnp.arange(last_row)[None, :]
    return jnp.where(causal, scores, -1000000000.0)


def attention_forward(query, key_rot, values_low, seq_len):
    block_rows = min(512, seq_len)
    outputs = []
    log_sums = []
    for first_row in range(0, seq_len, block_rows):
        last_row = first_row + block_rows
        query_part = query[:, first_row:last_row]
        scores = block_scores(query_part, key_rot[:, :last_row], first_row, block_rows, last_row)
        row_max = jnp.max(scores, -1, keepdims=True)
        exponent = jnp.exp(scores - row_max)
        row_total = jnp.sum(exponent, -1, keepdims=True)
        probs_low = (exponent / row_total).astype(jnp.bfloat16)
        outputs.append(
            jnp.einsum(
                "nkgqs,nskd->nqkgd",
                probs_low,
                values_low[:, :last_row],
                preferred_element_type=jnp.float32,
            )
        )
        log_sums.append(row_max + jnp.log(row_total))
    return (jnp.concatenate(outputs, 1), log_sums)


def attention_backward(query, key_rot, values_low, grad_att, log_sums, seq_len):
    block_rows = min(512, seq_len)
    query_grads = []
    key_grad = jnp.zeros(key_rot.shape, jnp.float32)
    value_grad = jnp.zeros(values_low.shape, jnp.float32)
    for block_index, first_row in enumerate(range(0, seq_len, block_rows)):
        last_row = first_row + block_rows
        query_part = query[:, first_row:last_row]
        grad_part = grad_att[:, first_row:last_row]
        key_part = key_rot[:, :last_row]
        value_part = values_low[:, :last_row]
        scores = block_scores(query_part, key_part, first_row, block_rows, last_row)
        probs = jnp.exp(scores - log_sums[block_index])
        probs_low = probs.astype(jnp.bfloat16)
        grad_probs = jnp.einsum(
            "nqkgd,nskd->nkgqs", grad_part, value_part, preferred_element_type=jnp.float32
        )
        grad_scores = (
            probs * (grad_probs - jnp.sum(probs * grad_probs, -1, keepdims=True))
        ).astype(jnp.bfloat16)
        query_grads.append(
            jnp.einsum(
                "nkgqs,nskd->nqkgd", grad_scores, key_part, preferred_element_type=jnp.float32
            )
        )
        padding = ((0, 0), (0, seq_len - last_row), (0, 0), (0, 0))
        key_grad = key_grad + jnp.pad(
            jnp.einsum(
                "nkgqs,nqkgd->nskd", grad_scores, query_part, preferred_element_type=jnp.float32
            ),
            padding,
        )
        value_grad = value_grad + jnp.pad(
            jnp.einsum(
                "nkgqs,nqkgd->nskd", probs_low, grad_part, preferred_element_type=jnp.float32
            ),
            padding,
        )
    return (jnp.concatenate(query_grads, 1), key_grad, value_grad)


def adamw(weight, gradient, moment, second, step_rate, decay_rate):
    moment = BETA_ONE * moment + (1.0 - BETA_ONE) * gradient
    second = BETA_TWO * second + (1.0 - BETA_TWO) * gradient * gradient
    first_hat = moment / (1.0 - BETA_ONE**STEP)
    second_hat = second / (1.0 - BETA_TWO**STEP)
    weight = weight - step_rate * (
        first_hat / (jnp.sqrt(second_hat) + ADAM_EPS) + decay_rate * weight
    )
    return (moment, second, weight)


def fence(*values):
    return lax.optimization_barrier(values)


MESH = pl.DeviceIdType.MESH
HEAD = 128
AHEAD = 2


def place_here():
    index, place = lax.axis_index("dp"), lax.axis_index("tensor")
    return lax.div(index, 2), lax.rem(index, 2), lax.div(place, 2), lax.rem(place, 2)


def device(zone, side, row, core):
    return (zone * 2 + side, row * 2 + core)


def flipped(zone, flip):
    bit = 1
    while bit <= flip:
        if flip & bit:
            zone = zone + bit - 2 * bit * lax.rem(lax.div(zone, bit), 2)
        bit *= 2
    return zone


def greet(devices, amount=None):
    barrier = pltpu.get_barrier_semaphore()
    for peer in devices:
        pl.semaphore_signal(barrier, inc=1, device_id=peer, device_id_type=MESH)
    pl.semaphore_wait(barrier, len(devices) if amount is None else amount)


def for_rows(count, body):
    step = 32

    def one(block, carry):
        body(pl.multiple_of(block * step, step), step)
        return carry

    lax.fori_loop(0, count // step, one, 0)


class Copies:
    def __init__(self, send_sems, recv_sems):
        self.send_sems, self.recv_sems = send_sems, recv_sems
        self.number = 0

    def make(self, source, target, peer):
        number, self.number = self.number, self.number + 1
        return pltpu.make_async_remote_copy(
            src_ref=source,
            dst_ref=target,
            send_sem=self.send_sems.at[number],
            recv_sem=self.recv_sems.at[number],
            device_id=peer,
            device_id_type=MESH,
        )

    def start(self, source, target, peer):
        copy = self.make(source, target, peer)
        copy.start()
        return copy


class GainSum:
    def __init__(self, plan, rest, width):
        self.plan, self.width = plan, width
        self.total = width + rest
        self.scratch = [
            pltpu.VMEM((8, 1, self.total), jnp.float32),
            pltpu.VMEM((plan.zones, 1, self.total), jnp.float32),
        ]
        self.output = jax.ShapeDtypeStruct((1, self.total), jnp.float32)
        self.count = 7 + plan.zones - 1

    def plane_peers(self, zone, side, row, core):
        steps = [(s, r, c) for s in range(2) for r in range(2) for c in range(2)][1:]
        turn = lambda value, step: 1 - value if step else value
        return [device(zone, turn(side, s), turn(row, r), turn(core, c)) for s, r, c in steps]

    def zone_peers(self, zone, side, row, core):
        return {flip: device(flipped(zone, flip), side, row, core) for flip in self.plan.flips[1:]}

    def start(self, copies, rest, blocks, plane_sums, zone_sums):
        zone, side, row, core = place_here()
        plan = self.plan
        size = self.width // plan.total
        self.copies, self.plane_sums, self.zone_sums, self.zone = copies, plane_sums, zone_sums, zone
        here = side * 4 + row * 2 + core
        plane_sums[here, :, pl.ds(self.width, self.total - self.width)] = rest[...]
        for slot in range(plan.total):
            owner = flipped(zone, plan.flips[slot % plan.zones]) * 2
            owner = owner + (core if slot < plan.zones else 1 - core)
            spot = pl.ds(pl.multiple_of(owner * size, size), size)
            plane_sums[here, :, spot] = blocks[:, pl.ds(slot * size, size)]
        self.plane = [
            copies.start(plane_sums.at[here], plane_sums.at[here], peer)
            for peer in self.plane_peers(zone, side, row, core)
        ]

    def middle(self):
        for copy in self.plane:
            copy.wait_recv()
        total = self.plane_sums[0]
        for place in range(1, 8):
            total = total + self.plane_sums[place]
        self.zone_sums[self.zone] = total
        zone, side, row, core = place_here()
        self.across = [
            self.copies.start(self.zone_sums.at[self.zone], self.zone_sums.at[self.zone], peer)
            for peer in self.zone_peers(zone, side, row, core).values()
        ]

    def finish(self, out):
        for copy in self.across:
            copy.wait_recv()
        total = self.zone_sums[0]
        for place in range(1, self.plan.zones):
            total = total + self.zone_sums[place]
        out[...] = total
        for copy in self.plane + self.across:
            copy.wait_send()


class ZoneBlocks:
    scratch = []

    def __init__(self, plan, source, slots, begin=0):
        self.flips, self.slots, self.sources, self.begin = plan.flips, list(slots), [source], begin
        self.outputs = [
            jax.ShapeDtypeStruct((len(self.slots),) + source.shape[1:], source.dtype)
        ]
        self.count, self.count_local = len(self.slots), 0
        self.in_hbm = False

    def peers(self, zone, side, row, core):
        return {
            self.flips[slot]: device(flipped(zone, self.flips[slot]), side, row, core)
            for slot in self.slots
        }

    def start(self, copies, local_sems, sources, targets, stages):
        zone, side, row, core = place_here()
        self.started = [
            copies.make(
                sources[0].at[slot],
                targets[0].at[number],
                device(flipped(zone, self.flips[slot]), side, row, core),
            )
            for number, slot in enumerate(self.slots)
        ]
        self.waiting = True
        if self.begin == 0:
            self.pump([0])

    def pump(self, steps):
        if self.waiting and self.begin in steps:
            self.waiting = False
            for copy in self.started:
                copy.start()

    def finish(self):
        for copy in self.started:
            copy.wait_send()
        for copy in self.started:
            copy.wait_recv()


def inner_zone(zone):
    return lax.rem(lax.div(zone + 1, 2), 2)


class SideDot:
    count, count_local, scratch, in_hbm = 0, 0, [], False

    def __init__(self, left, right):
        self.sources = [left, right]
        self.outputs = [jax.ShapeDtypeStruct((left.shape[0], right.shape[0]), jnp.bfloat16)]

    def peers(self, zone, side, row, core):
        return {}

    def some(self, first, last):
        left, right = self.refs
        size = 256

        def one(step, carry):
            here = pl.ds(pl.multiple_of(step * size, size), size)
            self.out[:, here] = dot(left[...], right[here, :], 1, 1).astype(jnp.bfloat16)
            return carry

        lax.fori_loop(first, last, one, 0)

    def start(self, copies, local_sems, sources, targets, stages):
        self.refs, self.out = sources, targets[0]
        self.steps = self.out.shape[1] // 256
        self.some(0, self.steps // 2)

    def pump(self, steps):
        if 0 in steps:
            self.some(self.steps // 2, self.steps)

    def finish(self):
        pass


class PairTree:
    def __init__(self, pairs, pieces):
        self.pairs = [len(pair) for pair in pairs]
        self.sources = [shard for pair in pairs for shard in pair]
        self.pieces = pieces
        self.outputs = [
            jax.ShapeDtypeStruct((8,) + own.shape, own.dtype) for own, *_ in pairs
        ]
        self.count = 6 * sum(pieces) + 2 * len(pairs) + self.pairs.count(1)
        self.count_local = 2 * len(pairs) + 2 * sum(pieces)
        self.scratch = [pltpu.VMEM((2,) + own.shape, own.dtype) for own, *_ in pairs]
        self.scratch += [pltpu.VMEM(p[0].shape, p[0].dtype) for p in pairs if len(p) == 1]
        self.in_hbm = True

    def peers(self, zone, side, row, core):
        return {
            1: device(flipped(zone, 1), side, row, core),
            3: device(flipped(zone, 3), side, row, core),
            "core": device(zone, side, row, 1 - core),
        }

    def start(self, copies, local_sems, sources, targets, stages):
        zone, side, row, core = place_here()
        inner_peer = device(flipped(zone, 3), side, row, core)
        outer_peer = device(flipped(zone, 1), side, row, core)
        core_peer = device(zone, side, row, 1 - core)
        self.inner = inner_zone(zone) == 1
        self.outer = inner_zone(zone) == 0
        self.across, self.onward, self.late, self.place = [], [], [], []
        self.shared, self.kept, self.partners = [], [], []
        sem = 0
        sources, late_stages = list(sources), list(stages[len(targets) :])
        for weight, full in enumerate(targets):
            landing = stages[weight]
            pair = [sources.pop(0) for _ in range(self.pairs[weight])]
            if len(pair) == 1:
                pair.append(late_stages.pop(0))
                self.partners.append(copies.start(pair[0], pair[1], outer_peer))
            size = pair[0].shape[0] // self.pieces[weight]
            for piece in range(self.pieces[weight]):
                rows = pl.ds(piece * size, size)
                for slot in (0, 1):
                    here = landing.at[slot, rows]
                    self.across.append(copies.make(pair[slot].at[rows], here, inner_peer))
                    self.onward.append(copies.make(here, landing.at[1 - slot, rows], outer_peer))
                    self.late.append(copies.make(here, full.at[6 + slot, rows], core_peer))
                    self.place.append(
                        pltpu.make_async_copy(here, full.at[2 + slot, rows], local_sems.at[sem])
                    )
                    sem += 1
            for slot in (0, 1):
                self.shared.append(copies.make(pair[slot], full.at[4 + slot], core_peer))
                self.kept.append(
                    pltpu.make_async_copy(pair[slot], full.at[slot], local_sems.at[sem])
                )
                sem += 1

        @pl.when(self.inner)
        def _():
            for copy in self.across[:AHEAD]:
                copy.start()

    def pump(self, steps):
        steps = [step for step in steps if step < len(self.across)]

        @pl.when(self.inner)
        def _():
            for step in steps:
                self.across[step].wait_recv()
                for copy in self.across[step + AHEAD : step + AHEAD + 1]:
                    copy.start()
                self.onward[step].start()
                self.late[step].start()
                self.place[step].start()

        for copy in self.partners if 1 in steps else []:
            copy.wait_recv()
            copy.wait_send()
        for copy in self.shared + self.kept if 1 in steps else []:
            copy.start()

    def finish(self):
        @pl.when(self.inner)
        def _():
            for copy in self.across + self.onward:
                copy.wait_send()

        @pl.when(self.outer)
        def _():
            for number, copy in enumerate(self.onward):
                copy.wait_recv()
                arrived = number + 1 - 2 * (number % 2)
                self.late[arrived].start()
                self.place[arrived].start()

        for copy in self.kept + self.place:
            copy.wait()
        for copy in self.shared + self.late:
            copy.wait_send()
        for copy in self.shared + self.late:
            copy.wait_recv()


def sum_eighths(
    copies, row_peer, side_peer, send, keep, forward, first, second, store, begin, pump
):
    size = send.shape[0] // 4
    part = lambda ref, slot: ref.at[pl.ds(slot * size, size)]
    arrivals = [
        copies.start(part(send, 1), part(first, 1), row_peer),
        copies.start(part(send, 3), part(first, 3), side_peer),
        copies.start(part(send, 0), part(first, 0), row_peer),
        copies.start(part(send, 2), part(first, 2), side_peer),
    ]
    begin()
    passed = []
    for number, slot, peer in ((0, 1, side_peer), (1, 3, row_peer)):
        arrivals[number].wait_recv()

        def add(row, count, number=number, slot=slot):
            here = pl.ds(slot * size + row, count)
            both = keep[here, :].astype(jnp.float32) + first[here, :].astype(jnp.float32)
            forward[pl.ds(number * size + row, count), :] = both.astype(jnp.bfloat16)

        for_rows(size, add)
        passed.append(copies.start(part(forward, number), part(second, number), peer))
    pump([0])
    for number, slot in ((0, 0), (1, 2)):
        arrivals[2 + number].wait_recv()
        passed[number].wait_recv()

        def total(row, count, number=number, slot=slot):
            here = pl.ds(slot * size + row, count)
            sums = keep[here, :].astype(jnp.float32) + first[here, :].astype(jnp.float32)
            sums = sums + second[pl.ds(number * size + row, count), :].astype(jnp.float32)
            store(number, row, count, sums)

        for_rows(size, total)
        yield number
    for copy in arrivals + passed:
        copy.wait_send()


def halves(terms):
    rows = terms.shape[0] // 2
    return terms.at[pl.ds(0, rows)], terms.at[pl.ds(rows, rows)]


def split_refs(refs, jobs, extra_count, out_count):
    refs = list(refs)
    take = lambda count: [refs.pop(0) for _ in range(count)]
    extras = take(extra_count)
    sources = [take(len(job.sources)) for job in jobs]
    full = take(1)[0]
    outs = take(out_count)
    targets = [take(len(job.outputs)) for job in jobs]
    return extras, sources, full, outs, targets, refs


def spread_kernel(middle, jobs, extra_count, out_count, gain_sum, terms, *refs):
    keep, send = halves(terms)
    extras, sources, full, outs, targets, scratch = split_refs(refs, jobs, extra_count, out_count)
    forward, first, second, send_sems, recv_sems, local_sems, *stages = scratch
    zone, side, row, core = place_here()
    row_peer, side_peer = device(zone, side, 1 - row, core), device(zone, 1 - side, row, core)
    copies = Copies(send_sems, recv_sems)
    size = send.shape[0] // 4
    part = lambda slot: full.at[pl.ds(slot * size, size)]
    for out in outs:
        if out.shape[0] == 1:
            out[...] = jnp.zeros_like(out)
    peers = {}
    for job in jobs:
        peers.update(job.peers(zone, side, row, core))
    greet([row_peer, side_peer] + list(peers.values()))

    def begin():
        spot = 0
        for job, source, target in zip(jobs, sources, targets):
            own_stages = stages[spot : spot + len(job.scratch)]
            job.start(copies, local_sems, source, target, own_stages)
            spot += len(job.scratch)

    def pump(steps):
        for job in jobs:
            job.pump(steps)

    def store(number, row, count, sums):
        own = pl.ds(number * size + row, count)
        full[pl.ds(2 * number * size + row, count), :] = middle(own, sums, extras, outs)

    firsts, seconds = [], []
    for number in sum_eighths(
        copies, row_peer, side_peer, send, keep, forward, first, second, store, begin, pump
    ):
        near, other = (side_peer, row_peer) if number == 0 else (row_peer, side_peer)
        slot = 2 * number
        firsts.append(copies.start(part(slot), part(slot + 1), near))
        seconds.append(copies.start(part(slot), part(4 + slot), other))
    pump([1])
    firsts[0].wait_recv()
    seconds.append(copies.start(part(1), part(5), row_peer))
    firsts[1].wait_recv()
    seconds.append(copies.start(part(3), part(7), side_peer))
    pump(range(2, 64))
    for copy in seconds:
        copy.wait_recv()
    for copy in firsts + seconds:
        copy.wait_send()
    for job in jobs:
        job.finish()


def home_kernel(middle, jobs, extra_count, out_count, gain_sum, terms, *refs):
    keep, send = halves(terms)
    extras, sources, full, outs, targets, scratch = split_refs(refs, jobs, extra_count, out_count)
    forward, first, second, own, send_sems, recv_sems, local_sems, *gain_scratch = scratch
    zone, side, row, core = place_here()
    row_peer, side_peer = device(zone, side, 1 - row, core), device(zone, 1 - side, row, core)
    core_peer = device(zone, side, row, 1 - core)
    copies = Copies(send_sems, recv_sems)
    size = send.shape[0] // 4
    at_home = side == core
    away = side != core
    for out in outs:
        if out.shape[0] == 1:
            out[...] = jnp.zeros_like(out)
    peers = {}
    for job in jobs:
        peers.update(job.peers(zone, side, row, core))
    plane = [row_peer, side_peer, core_peer]
    if gain_sum is not None:
        plane = gain_sum.plane_peers(zone, side, row, core)
        peers.update(gain_sum.zone_peers(zone, side, row, core))
    greet(plane + list(peers.values()))

    def begin():
        for job, source, target in zip(jobs, sources, targets):
            job.start(copies, local_sems, source, target, [])

    def pump(steps):
        for job in jobs:
            job.pump(steps)

    def store(number, start, count, sums):
        here = pl.ds(number * size + start, count)
        values = middle(here, sums, extras, outs)
        own[here, :] = values
        eighth = row * 2 + side if number == 0 else 4 + side * 2 + row

        @pl.when(at_home)
        def _():
            full[pl.ds(pl.multiple_of(eighth * size + start, 32), count), :] = values

    for _ in sum_eighths(
        copies, row_peer, side_peer, send, keep, forward, first, second, store, begin, pump
    ):
        pass
    pump([1])

    def piece(number, x, y):
        start = (x * 2 + y) * size if number == 0 else (4 + y * 2 + x) * size
        return full.at[pl.ds(pl.multiple_of(start, size), size)]

    mine = lambda number: own.at[pl.ds(number * size, size)]
    both = (0, 1)
    to_side = [copies.make(mine(k), piece(k, row, side), side_peer) for k in both]
    to_row = [copies.make(mine(k), piece(k, row, side), row_peer) for k in both]
    pass_row = [
        copies.make(piece(k, row, 1 - side), piece(k, row, 1 - side), row_peer) for k in both
    ]
    share = []
    for number, (x, y) in enumerate(
        ((row, side), (row, 1 - side), (1 - row, side), (1 - row, 1 - side))
    ):
        for k in both:
            source = mine(k) if number == 0 else piece(k, x, y)
            share.append(copies.make(source, piece(k, x, y), core_peer))

    if gain_sum is not None:
        gain_sum.start(copies, extras[-1], outs[0], *gain_scratch)

    @pl.when(away)
    def _():
        for copy in to_side:
            copy.start()

    @pl.when(at_home)
    def _():
        for copy in to_row + share[:2]:
            copy.start()

    if gain_sum is not None:
        gain_sum.middle()

    @pl.when(away)
    def _():
        for copy in to_side:
            copy.wait_send()
        for copy in share:
            copy.wait_recv()

    @pl.when(at_home)
    def _():
        for k in both:
            to_side[k].wait_recv()
            pass_row[k].start()
            share[2 + k].start()
        for k, copy in enumerate(to_row + pass_row):
            copy.wait_recv()
            share[4 + k].start()
        for copy in to_row + pass_row + share:
            copy.wait_send()

    if gain_sum is not None:
        gain_sum.finish(outs[-1])
    for job in jobs:
        job.finish()


def sum_rows(kernel, middle, terms, extras, outs, number, jobs=(), gain_sum=None):
    half, width = terms.shape[0] // 2, terms.shape[1]
    eighth = half // 4
    low = jnp.bfloat16
    vmem, hbm = pl.BlockSpec(memory_space=pltpu.VMEM), pl.BlockSpec(memory_space=pl.ANY)
    scratch = [
        pltpu.VMEM((2 * eighth, width), low),
        pltpu.VMEM((half, width), low),
        pltpu.VMEM((2 * eighth, width), low),
    ]
    if kernel is home_kernel:
        scratch.append(pltpu.VMEM((2 * eighth, width), low))
    copies = (12 if kernel is spread_kernel else 20) + sum(job.count for job in jobs)
    local = max([2] + [job.count_local for job in jobs])
    if gain_sum is not None:
        copies += gain_sum.count
        outs = outs + [gain_sum.output]
    scratch += [pltpu.SemaphoreType.DMA((count,)) for count in (copies, copies, local)]
    if gain_sum is not None:
        scratch += gain_sum.scratch
    scratch += [stage for job in jobs for stage in job.scratch]
    sources = [source for job in jobs for source in job.sources]
    targets = [target for job in jobs for target in job.outputs]
    return pl.pallas_call(
        functools.partial(kernel, middle, jobs, len(extras), len(outs), gain_sum),
        out_shape=[jax.ShapeDtypeStruct((2 * half, width), low)] + outs + targets,
        in_specs=[vmem] * (1 + len(extras) + len(sources)),
        out_specs=[vmem] * (1 + len(outs))
        + [hbm if job.in_hbm else vmem for job in jobs for _ in job.outputs],
        scratch_shapes=scratch,
        compiler_params=pltpu.CompilerParams(
            collective_id=number, has_side_effects=True, vmem_limit_bytes=56 * 2**20
        ),
        cost_estimate=pl.CostEstimate(flops=4 * 10**10, bytes_accessed=10**8, transcendentals=0),
        name=middle.__name__,
    )(terms, *extras, *sources)


def block_columns(plan, width):
    if not plan.ordered:
        return [pl.ds(0, width)], [pl.ds(0, width)]
    zone, _, _, core = place_here()
    size, zones = width // plan.total, plan.zones
    owners = [
        flipped(zone, plan.flips[slot % zones]) * 2 + (core if slot < zones else 1 - core)
        for slot in range(plan.total)
    ]
    natural = [pl.ds(pl.multiple_of(owner * size, size), size) for owner in owners]
    return natural, [pl.ds(slot * size, size) for slot in range(plan.total)]


def copy_rows(source, target):
    def some(row, count):
        target[pl.ds(row, count), :] = source[pl.ds(row, count), :]

    if source.shape[0] % 32:
        target[...] = source[...]
    else:
        for_rows(source.shape[0], some)


def cast_rows(source, target):
    def some(row, count):
        here = pl.ds(row, count)
        target[here, :] = source[here, :].astype(target.dtype)

    for_rows(source.shape[0], some)


def opening_kernel(plan, wide_qkv, gains, wide_gate, wide_out, tokens, angles, *refs):
    qkv_full, gains_full, turned_gate, turned_out, turned_tokens, turned_angles = refs[:6]
    partner_gate, send_sems, recv_sems, tokens_stage, qkv, gate, out = refs[6:]
    cast_rows(wide_qkv, qkv)
    zone, side, row, core = place_here()
    partner = device(zone, core, row, side)
    row_peer, core_peer = device(zone, side, 1 - row, core), device(zone, side, row, 1 - core)
    zone_peers = [device(flipped(zone, flip), side, row, core) for flip in plan.flips[1:]]
    at_home, away = side == core, side != core
    always = [row_peer, core_peer] + zone_peers

    @pl.when(at_home)
    def _():
        greet(always)

    @pl.when(away)
    def _():
        greet(always + [partner])

    copies = Copies(send_sems, recv_sems)
    zones = plan.zones
    own = (gains, qkv, angles, gate, out)
    ends = (gains_full.at[0], qkv_full.at[0], turned_angles, turned_gate, turned_out)
    units = wide_gate.shape[2]

    def cast_rest():
        for half in (0, 1):
            cast_rows(wide_gate.at[half], gate.at[:, pl.ds(half * units, units)])
        cast_rows(wide_out, out)

    turn = [copies.make(source, target, partner) for source, target in zip(own, ends)]
    pieces = 2
    size = tokens.shape[0] // (2 * pieces)
    spots = [
        pl.ds(pl.multiple_of((row * pieces + piece) * size, size), size) for piece in range(pieces)
    ]
    turn_rows = [copies.make(tokens.at[s], tokens_stage.at[s], partner) for s in spots]
    pass_rows = [copies.make(tokens_stage.at[s], tokens_stage.at[s], row_peer) for s in spots]
    natural, local = block_columns(plan, tokens.shape[1])

    def lay_down(all_tokens):
        def some(start, count):
            here = pl.ds(start, count)
            for a, b in zip(natural, local):
                turned_tokens[here, b] = all_tokens[here, a]

        for_rows(all_tokens.shape[0], some)

    slots = list(range(1, zones))
    weights = ((gains, gains_full), (qkv, qkv_full))
    from_own = [
        [copies.make(source, full.at[slot], zone_peers[slot - 1]) for slot in slots]
        + [copies.make(source, full.at[zones], core_peer)]
        for source, full in weights
    ] + [[copies.make(gate, partner_gate, zone_peers[0])]]
    copies.number -= 2 * zones + 1
    from_turned = [
        [copies.make(full.at[0], full.at[slot], zone_peers[slot - 1]) for slot in slots]
        + [copies.make(full.at[0], full.at[zones], core_peer)]
        for _, full in weights
    ] + [[copies.make(turned_gate, partner_gate, zone_peers[0])]]
    cross = [
        [copies.make(full.at[slot], full.at[zones + slot], core_peer) for slot in slots]
        for _, full in weights
    ]

    def cross_over(k):
        for which in (0, 1):
            from_turned[which][k].wait_recv()
            cross[which][k].start()

    @pl.when(away)
    def _():
        for copy in turn[:3]:
            copy.start()
        cast_rest()
        for which in (0, 1):
            turn[which].wait_recv()
            for copy in from_turned[which]:
                copy.start()
        turn[3].start()
        turn_rows[0].start()
        turn[3].wait_recv()
        from_turned[2][0].start()
        turn_rows[1].start()
        cross_over(0)
        turn_rows[0].wait_recv()
        pass_rows[0].start()
        for copy in turn[4:]:
            copy.start()
        turn_rows[1].wait_recv()
        pass_rows[1].start()

    @pl.when(at_home)
    def _():
        for copy in from_own[0] + from_own[1]:
            copy.start()
        cast_rest()
        for copy in from_own[2]:
            copy.start()
        for source, target in zip(own, ends):
            copy_rows(source, target)
        lay_down(tokens)
        cross_over(0)

    for k in range(1, zones - 1):
        cross_over(k)
    for which in (0, 1):
        from_turned[which][zones - 1].wait_recv()
        for copy in from_turned[which]:
            copy.wait_send()
        for copy in cross[which]:
            copy.wait_recv()
            copy.wait_send()
    from_turned[2][0].wait_recv()
    from_turned[2][0].wait_send()

    @pl.when(away)
    def _():
        for copy in pass_rows + turn[2:3] + turn[4:]:
            copy.wait_recv()
        lay_down(tokens_stage)
        for copy in turn + turn_rows + pass_rows:
            copy.wait_send()


def opening(plan, qkv, gains, gate, out, tokens, angles, number):
    low = jnp.bfloat16
    vmem = pl.BlockSpec(memory_space=pltpu.VMEM)
    like = lambda v: jax.ShapeDtypeStruct(v.shape, v.dtype)
    whole = lambda v: jax.ShapeDtypeStruct((2 * plan.zones,) + v.shape, low)
    operands = (qkv, gains, gate, out, tokens, angles)
    low_gate = jax.ShapeDtypeStruct((gate.shape[1], 2 * gate.shape[2]), low)
    low_out = jax.ShapeDtypeStruct(out.shape, low)
    outputs = [whole(qkv), whole(gains), low_gate, low_out, like(tokens), like(angles), low_gate]
    copies = 5 + 4 + 2 * plan.zones + 1 + 2 * (plan.zones - 1)
    return pl.pallas_call(
        functools.partial(opening_kernel, plan),
        out_shape=outputs,
        in_specs=[vmem] * len(operands),
        out_specs=[vmem] * len(outputs),
        scratch_shapes=[
            pltpu.SemaphoreType.DMA((copies,)),
            pltpu.SemaphoreType.DMA((copies,)),
            pltpu.VMEM(tokens.shape, tokens.dtype),
            pltpu.VMEM(qkv.shape, low),
            pltpu.VMEM(low_gate.shape, low),
            pltpu.VMEM(out.shape, low),
        ],
        compiler_params=pltpu.CompilerParams(
            collective_id=number, has_side_effects=True, vmem_limit_bytes=56 * 2**20
        ),
        cost_estimate=pl.CostEstimate(flops=4 * 10**10, bytes_accessed=10**8, transcendentals=0),
        name="opening",
    )(*operands)


def inverse_rms(values):
    return lax.rsqrt(jnp.mean(values * values, -1, keepdims=True) + EPS_NORM)


def hidden_rows(own, sums, extras, outs):
    tokens, gain = extras
    hidden = tokens[own, :].astype(jnp.float32) + sums
    outs[0][own, :] = hidden
    return (hidden * inverse_rms(hidden) * gain[...]).astype(jnp.bfloat16)


def grad_hidden_rows(own, sums, extras, outs):
    hidden, out_grad, gain = extras
    values = hidden[own, :]
    factor = inverse_rms(values)
    unit = values * factor
    outs[1][...] += jnp.sum(sums * unit, 0, keepdims=True)
    grad = out_grad[own, :].astype(jnp.float32) + norm_back(sums * gain[...], unit, factor)
    outs[0][own, :] = grad
    return grad.astype(jnp.bfloat16)


def grad_input_rows(own, sums, extras, outs):
    tokens, grad_hidden, gain = extras[:3]
    values = tokens[own, :].astype(jnp.float32)
    factor = inverse_rms(values)
    unit = values * factor
    outs[0][...] += jnp.sum(sums * unit, 0, keepdims=True)
    return (grad_hidden[own, :] + norm_back(sums * gain[...], unit, factor)).astype(jnp.bfloat16)


def dot(left, right, left_dim=1, right_dim=0):
    return lax.dot_general(
        left, right, (((left_dim,), (right_dim,)), ((), ())), preferred_element_type=jnp.float32
    )


def turn_head(values, cosine, signed_sine):
    return values * cosine + pltpu.roll(values, HEAD // 2, 1) * signed_sine


def turn_back(gradient, cosine, signed_sine):
    return gradient * cosine + pltpu.roll(gradient * signed_sine, HEAD // 2, 1)


def softmax_block(query, key, first_row):
    rows, keys = query.shape[0], key.shape[0]
    scores = dot(query, key, 1, 1)
    row_at = lax.broadcasted_iota(jnp.int32, (rows, keys), 0) + first_row
    key_at = lax.broadcasted_iota(jnp.int32, (rows, keys), 1)
    scores = jnp.where(key_at <= row_at, scores, -1000000000.0)
    exponent = jnp.exp(scores - jnp.max(scores, -1, keepdims=True))
    return exponent / jnp.sum(exponent, -1, keepdims=True)


def eighth_owners():
    _, side, row, _ = place_here()
    own, off = (row, side), (1 - row, 1 - side)
    first = lambda x, y: x * 2 + y
    second = lambda x, y: 4 + y * 2 + x
    return [
        first(own[0], own[1]),
        first(own[0], off[1]),
        second(own[0], own[1]),
        second(off[0], own[1]),
        first(off[0], own[1]),
        first(off[0], off[1]),
        second(own[0], off[1]),
        second(off[0], off[1]),
    ]


def reorder_rows(source, target, into_local):
    size = source.shape[0] // 8
    for slot, owner in enumerate(eighth_owners()):
        natural = pl.ds(pl.multiple_of(owner * size, size), size)
        local = pl.ds(slot * size, size)
        if into_local:
            target[local, :] = source[natural, :]
        else:
            target[natural, :] = source[local, :]


def forward_kernel(
    tokens, weights, gain_in, gain_q, gain_k, cosine, sine,
    normed, raw, query, key, value, local, attended,
):
    low = jnp.bfloat16
    total, heads = tokens.shape[0], query.shape[1] // HEAD
    block, wide = 256, 512

    def project(step, carry):
        rows = pl.ds(pl.multiple_of(step * wide, wide), wide)
        values = tokens[rows, :].astype(jnp.float32)
        normed[rows, :] = (values * inverse_rms(values) * gain_in[...]).astype(low)
        raw[rows, :] = dot(normed[rows, :], weights[...])
        turns = (cosine[rows, :], sine[rows, :])
        for head in range(heads):
            column = (head // 2) * 4 * HEAD + (head % 2) * HEAD
            values = raw[rows, pl.ds(column, HEAD)]
            values = turn_head(values * inverse_rms(values) * gain_q[...], *turns)
            query[rows, pl.ds(head * HEAD, HEAD)] = (values * (1.0 / math.sqrt(HEAD))).astype(low)
        for group in range(heads // 2):
            column = group * 4 * HEAD + 2 * HEAD
            here = pl.ds(group * HEAD, HEAD)
            values = raw[rows, pl.ds(column, HEAD)]
            values = turn_head(values * inverse_rms(values) * gain_k[...], *turns)
            key[rows, here] = values.astype(low)
            value[rows, here] = raw[rows, pl.ds(column + HEAD, HEAD)].astype(low)
        return carry

    lax.fori_loop(0, total // wide, project, 0)

    def attend(head, carry):
        mine = pl.ds(pl.multiple_of(head * HEAD, HEAD), HEAD)
        shared = pl.ds(pl.multiple_of(lax.div(head, 2) * HEAD, HEAD), HEAD)
        for start in range(0, total, SEQ):
            for first in range(0, SEQ, block):
                rows, keys = pl.ds(start + first, block), pl.ds(start, first + block)
                probs = softmax_block(query[rows, mine], key[keys, shared], first)
                attended[rows, mine] = dot(probs.astype(low), value[keys, shared]).astype(low)
        return carry

    lax.fori_loop(0, heads, attend, 0)
    reorder_rows(attended, local, True)


def attention(tokens, weights, gain_in, gain_q, gain_k, cosine, sine):
    total = tokens.shape[0]
    columns = weights.shape[1]
    low = jnp.bfloat16
    shape = lambda width, kind=low: jax.ShapeDtypeStruct((total, width), kind)
    vmem = pl.BlockSpec(memory_space=pltpu.VMEM)
    return pl.pallas_call(
        forward_kernel,
        out_shape=[
            shape(tokens.shape[1]),
            shape(columns, jnp.float32),
            shape(columns // 2),
            shape(columns // 4),
            shape(columns // 4),
            shape(columns // 2),
        ],
        in_specs=[vmem] * 7,
        out_specs=[vmem] * 6,
        scratch_shapes=[pltpu.VMEM((total, columns // 2), low)],
        compiler_params=pltpu.CompilerParams(vmem_limit_bytes=48 * 2**20),
        cost_estimate=pl.CostEstimate(flops=10**10, bytes_accessed=2 * 10**7, transcendentals=0),
        name="attention",
    )(tokens, weights, gain_in, gain_q, gain_k, cosine, sine)


def backward_kernel(
    query, key, value, raw, grad_rows, gain_q, gain_k, cosine, sine,
    mixed, mixed_local, query_gain, key_gain, grad, key_sum, value_sum,
):
    low = jnp.bfloat16
    total, heads = query.shape[0], query.shape[1] // HEAD
    block = 256
    reorder_rows(grad_rows, grad, False)
    query_gain[...] = jnp.zeros_like(query_gain)
    key_gain[...] = jnp.zeros_like(key_gain)

    def head_norm_back(rows, column, gradient, gain, gain_grad):
        values = raw[rows, column]
        factor = inverse_rms(values)
        unit = values * factor
        turned = turn_back(gradient, cosine[rows, :], sine[rows, :])
        gain_grad[...] += jnp.sum(turned * unit, 0, keepdims=True)
        mixed[rows, column] = norm_back(turned * gain[...], unit, factor).astype(low)

    def one_group(group, carry):
        at = lambda offset: pl.ds(pl.multiple_of(group * 4 * HEAD + offset * HEAD, HEAD), HEAD)
        shared = pl.ds(pl.multiple_of(group * HEAD, HEAD), HEAD)
        key_sum[...] = jnp.zeros_like(key_sum)
        value_sum[...] = jnp.zeros_like(value_sum)
        for head in (0, 1):
            mine = pl.ds(pl.multiple_of((group * 2 + head) * HEAD, HEAD), HEAD)
            for start in range(0, total, SEQ):
                for first in range(0, SEQ, block):
                    rows, keys = pl.ds(start + first, block), pl.ds(start, first + block)
                    query_part, grad_part = query[rows, mine], grad[rows, mine]
                    probs = softmax_block(query_part, key[keys, shared], first)
                    weighed = probs * dot(grad_part, value[keys, shared], 1, 1)
                    scores = weighed - probs * jnp.sum(weighed, -1, keepdims=True)
                    scores = scores.astype(low)
                    grad_query = dot(scores, key[keys, shared]) * (1.0 / math.sqrt(HEAD))
                    head_norm_back(rows, at(head), grad_query, gain_q, query_gain)
                    key_sum[keys, :] += dot(scores, query_part, 0, 0)
                    value_sum[keys, :] += dot(probs.astype(low), grad_part, 0, 0)
        for first in range(0, total, block):
            rows = pl.ds(first, block)
            head_norm_back(rows, at(2), key_sum[rows, :], gain_k, key_gain)
            mixed[rows, at(3)] = value_sum[rows, :].astype(low)
        return carry

    lax.fori_loop(0, heads // 2, one_group, 0)
    reorder_rows(mixed, mixed_local, True)


def attention_back(query, key, value, raw, grad_rows, gain_q, gain_k, cosine, sine):
    total, columns = raw.shape
    low = jnp.bfloat16
    vmem = pl.BlockSpec(memory_space=pltpu.VMEM)
    return pl.pallas_call(
        backward_kernel,
        out_shape=[
            jax.ShapeDtypeStruct((total, columns), low),
            jax.ShapeDtypeStruct((total, columns), low),
            jax.ShapeDtypeStruct((1, HEAD), jnp.float32),
            jax.ShapeDtypeStruct((1, HEAD), jnp.float32),
        ],
        in_specs=[vmem] * 9,
        out_specs=[vmem] * 4,
        scratch_shapes=[
            pltpu.VMEM(grad_rows.shape, low),
            pltpu.VMEM((total, HEAD), jnp.float32),
            pltpu.VMEM((total, HEAD), jnp.float32),
        ],
        compiler_params=pltpu.CompilerParams(vmem_limit_bytes=48 * 2**20),
        cost_estimate=pl.CostEstimate(flops=10**10, bytes_accessed=2 * 10**7, transcendentals=0),
        name="attention_back",
    )(query, key, value, raw, grad_rows, gain_q, gain_k, cosine, sine)


def feed_kernel(plan, rows, own_grad, got_grad, gate_up, up_part, down, active, grads, out_grad):
    low = jnp.bfloat16
    block = 512
    tile = down.shape[1]
    step = pl.program_id(0)
    gate_at = pl.ds(pl.multiple_of(step * tile, tile), tile)
    up_at = pl.ds(pl.multiple_of(grads.shape[1] // 2 + step * tile, tile), tile)
    _, side, _, core = place_here()

    def lay_down(source):
        natural, blocks = block_columns(plan, source.shape[1])
        eighth = source.shape[0] // 8
        for slot, owner in enumerate(eighth_owners()):

            def some(start, count, slot=slot, owner=owner):
                here = pl.ds(pl.multiple_of(owner * eighth + start, 32), count)
                there = pl.ds(slot * eighth + start, count)
                for a, b in zip(natural, blocks):
                    out_grad[there, b] = source[here, a]

            for_rows(eighth, some)

    @pl.when((step == 0) & (side == core))
    def _():
        lay_down(own_grad)

    @pl.when((step == 0) & (side != core))
    def _():
        lay_down(got_grad)

    def one(block_at, carry):
        here = pl.ds(pl.multiple_of(block_at * block, block), block)
        gate = dot(rows[here, :], gate_up[...])
        up = dot(rows[here, :], up_part[...])
        grad = dot(out_grad[here, :], down[...])
        sigmoid = jax.nn.sigmoid(gate)
        silu = gate * sigmoid
        active[here, :] = (silu * up).astype(low)
        grads[here, gate_at] = (grad * up * sigmoid * (1.0 + gate * (1.0 - sigmoid))).astype(low)
        grads[here, up_at] = (grad * silu).astype(low)
        return carry

    lax.fori_loop(0, rows.shape[0] // block, one, 0)


def feed_forward(plan, rows, own_grad, got_grad, gate_up, down, tile):
    total, width = rows.shape
    units = down.shape[1]
    low = jnp.bfloat16
    tiles = units // tile
    whole = pl.BlockSpec(memory_space=pltpu.VMEM)
    return pl.pallas_call(
        functools.partial(feed_kernel, plan),
        grid=(tiles,),
        out_shape=[
            jax.ShapeDtypeStruct((total, units), low),
            jax.ShapeDtypeStruct((total, 2 * units), low),
            jax.ShapeDtypeStruct((total, width), low),
        ],
        in_specs=[
            whole,
            whole,
            whole,
            pl.BlockSpec((width, tile), lambda step: (0, step)),
            pl.BlockSpec((width, tile), lambda step: (0, step + tiles)),
            pl.BlockSpec((width, tile), lambda step: (0, step)),
        ],
        out_specs=[
            pl.BlockSpec((total, tile), lambda step: (0, step)),
            whole,
            whole,
        ],
        compiler_params=pltpu.CompilerParams(vmem_limit_bytes=56 * 2**20),
        cost_estimate=pl.CostEstimate(
            flops=6 * total * width * units, bytes_accessed=4 * 10**7, transcendentals=total * units
        ),
        name="feed_forward",
    )(rows, own_grad, got_grad, gate_up, gate_up, down)


class Plan:
    def __init__(self, mesh):
        self.total = mesh.shape["dp"]
        self.zones = self.total // 2
        self.tensor = mesh.shape["tensor"]
        self.flips = [k ^ (k >> 1) for k in range(self.zones)]

    def place(self):
        self.index = lax.axis_index("dp")
        self.zone = self.index // 2
        self.side = self.index % 2
        self.row = lax.axis_index("tensor") // 2
        self.core = lax.axis_index("tensor") % 2
        self.home = self.side == self.core

    def move(self, value, target):
        pairs = []
        for d in range(self.total):
            for t in range(self.tensor):
                to = target(d // 2, d % 2, t // 2, t % 2)
                if to is not None:
                    zone, side, row, core = to
                    pairs.append((d * self.tensor + t, (zone * 2 + side) * self.tensor + row * 2 + core))
        return lax.ppermute(value, ("dp", "tensor"), pairs)

    def turn(self, value):
        got = self.move(value, lambda z, y, x, c: (z, c, x, y) if y != c else None)
        return jnp.where(self.home, value, got)

    def zone_flip(self, value, bit):
        return self.move(value, lambda z, y, x, c: (z ^ bit, y, x, c))

    def core_swap(self, value):
        return self.move(value, lambda z, y, x, c: (z, y, x, 1 - c))

    def side_swap(self, value):
        return self.move(value, lambda z, y, x, c: (z, 1 - y, x, c))

    def row_swap(self, value):
        return self.move(value, lambda z, y, x, c: (z, y, 1 - x, c))

    def to_local(self, value, axis):
        width = value.shape[axis] // self.total
        parts = []
        for core in (self.core, 1 - self.core):
            for slot in range(self.zones):
                owner = (self.zone ^ self.flips[slot]) * 2 + core
                parts.append(lax.dynamic_slice_in_dim(value, owner * width, width, axis))
        return jnp.concatenate(parts, axis)

    def to_natural(self, value, axis, core=None):
        core = self.core if core is None else core
        width = value.shape[axis] // self.total
        parts = []
        for block in range(self.total):
            slot = flip = (block // 2) ^ self.zone
            for bits in range(1, self.zones.bit_length()):
                slot = slot ^ (flip >> bits)
            slot = slot + jnp.where(block % 2 == core, 0, self.zones)
            parts.append(lax.dynamic_slice_in_dim(value, slot * width, width, axis))
        return jnp.concatenate(parts, axis)

    def row_owners(self):
        own, off = (self.row, self.side), (1 - self.row, 1 - self.side)
        first = lambda x, y: x * 2 + y
        second = lambda x, y: 4 + y * 2 + x
        return [
            first(own[0], own[1]),
            first(own[0], off[1]),
            second(own[0], own[1]),
            second(off[0], own[1]),
            first(off[0], own[1]),
            first(off[0], off[1]),
            second(own[0], off[1]),
            second(off[0], off[1]),
        ]

    def rows_local(self, value, slots=range(8)):
        size = value.shape[0] // 8
        owners = self.row_owners()
        return jnp.concatenate(
            [lax.dynamic_slice_in_dim(value, owners[slot] * size, size, 0) for slot in slots], 0
        )

    def rows_natural(self, value, order=range(8)):
        size = value.shape[0] // 8
        place = [list(order).index(slot) for slot in range(8)]
        parts = []
        for piece in range(8):
            x, y = (piece // 2, piece % 2) if piece < 4 else (piece % 2, (piece - 4) // 2)
            slots = (0, 1, 4, 5) if piece < 4 else (2, 6, 3, 7)
            same_x, same_y = x == self.row, y == self.side
            slot = jnp.where(
                same_x,
                jnp.where(same_y, place[slots[0]], place[slots[1]]),
                jnp.where(same_y, place[slots[2]], place[slots[3]]),
            )
            parts.append(lax.dynamic_slice_in_dim(value, slot * size, size, 0))
        return jnp.concatenate(parts, 0)

    def from_zones(self, shard):
        return [self.zone_flip(shard, flip) for flip in self.flips[1:]]

    def to_zones(self, parts, slots):
        return [self.zone_flip(parts[slot], self.flips[slot]) for slot in slots]

    def middle_swap(self, pair):
        return self.move(pair, lambda z, y, x, c: (z ^ 3, y, x, c) if z in (1, 2) else None)

    def inward(self, part):
        return self.move(part, lambda z, y, x, c: (z ^ 1, y, x, c) if z in (0, 3) else None)

    def pass_outward(self, pair):
        return self.move(pair, lambda z, y, x, c: (z ^ 1, y, x, c) if z in (1, 2) else None)

    def far_pair(self, middle, passed):
        inner = (self.zone == 1) | (self.zone == 2)
        return jnp.where(inner, middle, passed[::-1])

    def first_swap(self, send):
        half = send.shape[0] // 2
        return self.row_swap(send[:half]), self.side_swap(send[half:])

    def second_swap(self, keep, got):
        quarter = keep.shape[0] // 4
        row_part = keep[: 2 * quarter] + got[0].astype(jnp.float32)
        side_part = keep[2 * quarter :] + got[1].astype(jnp.float32)
        own = jnp.concatenate([row_part[:quarter], side_part[:quarter]], 0)
        return own, (
            self.side_swap(row_part[quarter:].astype(jnp.bfloat16)),
            self.row_swap(side_part[quarter:].astype(jnp.bfloat16)),
        )

    def spread_first(self, own):
        half = own.shape[0] // 2
        return (self.side_swap(own[:half]), self.row_swap(own[half:]))

    def spread_second(self, own, got):
        half = own.shape[0] // 2
        row_part = jnp.concatenate([own[:half], got[0]], 0)
        side_part = jnp.concatenate([own[half:], got[1]], 0)
        return row_part, side_part, self.row_swap(row_part), self.side_swap(side_part)

    def send_home(self, own):
        to_home = lambda z, y, x, c: (z, c, x, c) if y != c else None
        return jnp.concatenate([own, self.move(own, to_home)], 0)

    def row_home(self, part):
        return self.move(part, lambda z, y, x, c: (z, y, 1 - x, c) if y == c else None)

    def share_home(self, part, other):
        full = jnp.concatenate([part, other], 0)
        full = self.to_natural(self.rows_natural(full, (0, 2, 1, 6, 4, 3, 5, 7)), 1)
        got = self.move(full, lambda z, y, x, c: (z, y, x, 1 - c) if y == c else None)
        return full, got

    def turned(self, own, got):
        return jnp.where(self.home, own, got)

    def sum_everywhere(self, value):
        value = value + self.row_swap(value)
        value = value + self.side_swap(value)
        value = value + self.core_swap(value)
        bit = 1
        while bit < self.zones:
            value = value + self.zone_flip(value, bit)
            bit *= 2
        return value


def shards(
    plan,
    tokens,
    positions,
    out_grad,
    qkv_weight,
    qkv_first,
    qkv_second,
    out_weight,
    out_first,
    out_second,
    gate_up,
    gate_up_first,
    gate_up_second,
    down_weight,
    down_first,
    down_second,
    gains,
    gains_first,
    gains_second,
):
    plan.place()
    low = jnp.bfloat16
    tok_rows, model_width = tokens.shape
    groups = qkv_weight.shape[1]
    head_size = qkv_weight.shape[3]
    shard_rows = qkv_weight.shape[0]
    seq_count = tok_rows // SEQ
    mixed_cols = groups * 4 * head_size
    near_cols = model_width // 2
    kept = tok_rows // 2
    gain_count = gains.shape[0]

    tree = plan.zones == 4
    slots = range(1, plan.zones)

    def column_parts(value):
        return value.reshape((plan.zones, -1) + value.shape[1:])

    units = gate_up.shape[2]
    plan.ordered = (model_width // plan.total) % 128 == 0
    gain_rows = 16
    gain_block = jnp.pad(gains.astype(low), (0, gain_rows * 128 - gain_count)).reshape(gain_rows, 128)
    tile = min(units, 256)
    angle_at = positions.astype(jnp.float32).reshape(-1, 128)
    both_qkv, both_gains, turned_gate, turned_out, tokens, angle_at, partner_gate = opening(
        plan,
        qkv_weight.reshape(shard_rows, mixed_cols),
        gain_block,
        gate_up,
        out_weight,
        tokens,
        angle_at,
        3,
    )
    positions = angle_at.reshape(-1)
    turned_out, turned_gate, tokens, positions, both_qkv, both_gains, out_grad, low_down = fence(
        turned_out,
        turned_gate,
        tokens,
        positions,
        both_qkv,
        both_gains,
        out_grad,
        down_weight.astype(low),
    )

    got_grad = plan.move(out_grad, lambda z, y, x, c: (z, c, x, y) if y != c else None)
    zone_out = plan.from_zones(turned_out)
    got_down = plan.move(low_down, lambda z, y, x, c: (z, c, x, y) if y != c else None)
    if not tree:
        partner_gate = plan.from_zones(turned_gate)
    if not plan.ordered:
        tokens = plan.to_local(tokens, 1)
    cosine, sine_table = rotary(positions, head_size)
    signed_sine = jnp.concatenate(
        [-sine_table[:, : head_size // 2], sine_table[:, head_size // 2 :]], 1
    )
    full_qkv = both_qkv.reshape(model_width, mixed_cols)
    gain_slots = both_gains.reshape(plan.total, -1)[:, :gain_count]
    gain_all = plan.to_natural(gain_slots.reshape(-1), 0).astype(jnp.float32)
    gain_in = plan.to_local(gain_all[:model_width], 0)[None]
    gain_post = plan.to_local(gain_all[model_width : 2 * model_width], 0)[None]
    gain_q = gain_all[2 * model_width : 2 * model_width + head_size][None]
    gain_k = gain_all[2 * model_width + head_size :][None]
    normed, raw, query, key_rot, values_low, attended = attention(
        tokens, full_qkv, gain_in, gain_q, gain_k, cosine, signed_sine
    )
    attended, zone_out, turned_out, low_down, got_down, turned_gate, partner_gate = fence(
        attended, zone_out, turned_out, low_down, got_down, turned_gate, partner_gate
    )

    near_out = jnp.concatenate([turned_out] + zone_out, 0)
    far_out = plan.core_swap(near_out)
    own_tokens = plan.rows_local(tokens, (0, 2))
    turned_down = plan.turned(low_down, got_down)
    near_out, far_out, own_tokens, turned_down = fence(near_out, far_out, own_tokens, turned_down)

    full_out = jnp.concatenate([near_out, far_out], 0)
    branch_terms = contract_cols(attended, full_out).astype(low)
    if tree:
        pairs = [(turned_gate, partner_gate), (turned_down,)]
    else:
        pairs = [(turned_gate, partner_gate), (turned_down, plan.from_zones(turned_down))]
    normed_rows, hidden, *gathered = sum_rows(
        spread_kernel,
        hidden_rows,
        branch_terms,
        [own_tokens, gain_post],
        [jax.ShapeDtypeStruct((tok_rows // 4, model_width), jnp.float32)],
        0,
        [PairTree(pairs, (2, 2))] if tree else [],
    )
    if not tree:
        near = [jnp.concatenate([own] + rest, 0) for own, rest in pairs]
        gathered = [jnp.concatenate([part, plan.core_swap(part)], 0) for part in near]
    full_gate = gathered[0].reshape(model_width, 2 * units)
    full_down = gathered[1].reshape(model_width, units)
    normed_rows, hidden, full_gate, full_down, got_grad = fence(
        normed_rows, hidden, full_gate, full_down, got_grad
    )

    def zone_parts(near, got):
        both = (near + got.astype(jnp.float32)).astype(low)
        return both.reshape((plan.zones, -1) + both.shape[1:])

    def zone_total(parts, *arrived):
        total = parts[0].astype(jnp.float32)
        for part in sum([list(group) for group in arrived], []):
            total = total + part.astype(jnp.float32)
        return total.astype(low)

    active, grad_both, out_grad = feed_forward(
        plan, normed_rows, out_grad, got_grad, full_gate, full_down, tile
    )
    if not plan.ordered:
        out_grad = plan.to_local(out_grad, 1)
    down_far = contract_rows(out_grad[:, near_cols:], active).astype(low)
    down_far, active, grad_both, out_grad = fence(down_far, active, grad_both, out_grad)

    down_got = plan.core_swap(down_far)
    gate_far = contract_rows(normed_rows[:, near_cols:], grad_both).astype(low)
    down_parts = zone_parts(contract_rows(out_grad[:, :near_cols], active), down_got)
    down_parts, gate_far, grad_both = fence(down_parts, gate_far, grad_both)

    gate_got = plan.core_swap(gate_far)
    if tree:
        inner_terms = plan.inward(down_parts[3])
    else:
        inner_terms = plan.to_zones(down_parts, slots)
    post_terms = contract_cols(grad_both, full_gate).astype(low)
    post_terms, gate_got, inner_terms, down_parts = fence(
        post_terms, gate_got, inner_terms, down_parts
    )

    down_sums = jnp.stack([inner_terms, plan.inward(down_parts[2])]) if tree else inner_terms
    gate_parts = zone_parts(contract_rows(normed_rows[:, :near_cols], grad_both), gate_got)
    if tree:
        down_pair = (down_parts[2:].astype(jnp.float32) + down_sums.astype(jnp.float32)).astype(low)
    else:
        down_pair = down_parts
    post_terms, gate_parts, down_parts, down_pair = fence(
        post_terms, gate_parts, down_parts, down_pair
    )

    if tree:
        down_sums = plan.middle_swap(down_pair)
        gate_sums = [plan.inward(gate_parts[3]), plan.inward(gate_parts[2])]
    else:
        gate_sums = plan.to_zones(gate_parts, slots)
    eighth = tok_rows // 8
    own_grad = jnp.concatenate([out_grad[:eighth], out_grad[2 * eighth : 3 * eighth]], 0)
    branch_rows, grad_hidden, post_gain_grad, mlp_terms = sum_rows(
        spread_kernel,
        grad_hidden_rows,
        post_terms,
        [hidden, own_grad, gain_post],
        [
            jax.ShapeDtypeStruct((tok_rows // 4, model_width), jnp.float32),
            jax.ShapeDtypeStruct((1, model_width), jnp.float32),
        ],
        1,
        [SideDot(active, full_down)],
    )
    branch_rows, grad_hidden, post_gain_grad, mlp_terms, down_sums, gate_sums, down_parts, gate_parts = fence(
        branch_rows,
        grad_hidden,
        post_gain_grad,
        mlp_terms,
        down_sums,
        gate_sums,
        down_parts,
        gate_parts,
    )

    def plus(left, right):
        return (left.astype(jnp.float32) + right.astype(jnp.float32)).astype(low)

    mlp_got = plan.first_swap(mlp_terms[kept:])
    if tree:
        gate_first = plan.middle_swap(plus(gate_parts[2], gate_sums[0]))
        down_own = [plus(down_parts[0], down_sums[0]), plus(down_parts[1], down_sums[1])]
        down_last = [plan.zone_flip(down_own[1], 1)]
    else:
        gate_first = gate_parts[0]
        down_own, down_last = down_parts, down_sums
    grad_att = jnp.dot(branch_rows, full_out, preferred_element_type=jnp.float32).astype(low)
    grad_mixed, mixed_rows, query_gain_grad, key_gain_grad = attention_back(
        query, key_rot, values_low, raw, grad_att, gain_q, gain_k, cosine, signed_sine
    )
    gain_terms = jnp.concatenate(
        [plan.to_natural(post_gain_grad, 1), query_gain_grad, key_gain_grad], 1
    )
    grad_mixed, mixed_rows, gain_terms, normed, branch_rows, mlp_got, gate_first, gate_parts, gate_sums = fence(
        grad_mixed, mixed_rows, gain_terms, normed, branch_rows, mlp_got, gate_first, gate_parts, gate_sums
    )

    mlp_own, mlp_last = plan.second_swap(mlp_terms[:kept].astype(jnp.float32), mlp_got)
    if tree:
        gate_second = plan.middle_swap(plus(gate_parts[3], gate_sums[1]))
    else:
        gate_second = gate_parts[1]
    out_far = contract_rows(branch_rows[:, near_cols:], attended).astype(low)
    out_got = plan.core_swap(out_far)
    qkv_far = contract_rows(normed[:, near_cols:], grad_mixed).astype(low)
    qkv_got = plan.core_swap(qkv_far)
    total_down = zone_total(down_own, down_last)
    summed_down = plan.turn(total_down)
    normed_terms = contract_cols(mixed_rows, full_qkv).astype(low)
    out_parts = zone_parts(contract_rows(branch_rows[:, :near_cols], attended), out_got)
    qkv_parts = zone_parts(contract_rows(normed[:, :near_cols], grad_mixed), qkv_got)
    block_own = (hidden + mlp_own + jnp.concatenate(mlp_last, 0).astype(jnp.float32)).astype(low)
    block_own, out_parts, qkv_parts, normed_terms, gate_second, summed_down = fence(
        block_own, out_parts, qkv_parts, normed_terms, gate_second, summed_down
    )

    gain_sum = GainSum(plan, gain_terms.shape[1], model_width) if plan.ordered else None
    input_full, input_gain_grad, *rest = sum_rows(
        home_kernel,
        grad_input_rows,
        normed_terms,
        [own_tokens, grad_hidden, gain_in] + ([gain_terms] if plan.ordered else []),
        [jax.ShapeDtypeStruct((1, model_width), jnp.float32)],
        2,
        [ZoneBlocks(plan, qkv_parts, slots), ZoneBlocks(plan, out_parts, slots, 1)],
        gain_sum,
    )
    if plan.ordered:
        summed_gains, qkv_sent, out_sent = rest
    else:
        qkv_sent, out_sent = rest
        summed_gains = plan.sum_everywhere(
            jnp.concatenate([plan.to_natural(input_gain_grad, 1), gain_terms], 1)
        )
    if tree:
        gate_own = [plus(gate_parts[0], gate_first), plus(gate_parts[1], gate_second)]
        gate_last = [plan.zone_flip(gate_own[1], 1)]
    else:
        gate_own, gate_last = gate_parts, gate_sums
    block_home = plan.send_home(block_own)
    input_full, summed_gains, qkv_sent, out_sent, gate_own, gate_last, block_home = fence(
        input_full, summed_gains, qkv_sent, out_sent, gate_own, gate_last, block_home
    )

    block_row = plan.row_home(block_home)
    summed_both = plan.turn(
        jnp.concatenate([zone_total(qkv_parts, qkv_sent), zone_total(out_parts, out_sent)], 1)
    ).astype(jnp.float32)
    total_gate = zone_total(gate_own, gate_last)
    summed_gate = plan.turn(jnp.stack([total_gate[:, :units], total_gate[:, units:]]))
    block_full, block_got = plan.share_home(block_home, block_row)
    block_out = jnp.where(plan.home, block_full, block_got)
    summed_qkv = summed_both[:, :mixed_cols].reshape(qkv_weight.shape)
    summed_out = summed_both[:, mixed_cols:]
    summed_gate = summed_gate.astype(jnp.float32)
    summed_down = summed_down.astype(jnp.float32)
    summed_gains = lax.dynamic_slice_in_dim(summed_gains[0], plan.index * gain_count, gain_count, 0)
    input_rows = plan.to_natural(input_full, 1, plan.side).astype(jnp.float32)

    qkv_moment, qkv_square, qkv_updated = adamw(
        qkv_weight, summed_qkv, qkv_first, qkv_second, RATE_QKV, DECAY_RATE
    )
    out_moment, out_square, out_updated = adamw(
        out_weight, summed_out, out_first, out_second, RATE_OUT, DECAY_RATE
    )
    gate_moment, gate_square, gate_updated = adamw(
        gate_up, summed_gate, gate_up_first, gate_up_second, RATE_GATE, DECAY_RATE
    )
    down_moment, down_square, down_updated = adamw(
        down_weight, summed_down, down_first, down_second, RATE_DOWN, DECAY_RATE
    )
    gain_moment, gain_square, gain_updated = adamw(
        gains, summed_gains, gains_first, gains_second, RATE_GAIN, 0.0
    )
    return (
        block_out,
        input_rows,
        qkv_moment,
        qkv_square,
        qkv_updated,
        out_moment,
        out_square,
        out_updated,
        gate_moment,
        gate_square,
        gate_updated,
        down_moment,
        down_square,
        down_updated,
        gain_moment,
        gain_square,
        gain_updated,
    )


def solution(mesh):
    plan = Plan(mesh)
    placed = (
        P("dp", None),
        P("dp"),
        P("dp", None),
        P("dp", "tensor", None, None),
        P("dp", "tensor", None, None),
        P("dp", "tensor", None, None),
        P("dp", "tensor"),
        P("dp", "tensor"),
        P("dp", "tensor"),
        P(None, "dp", "tensor"),
        P(None, "dp", "tensor"),
        P(None, "dp", "tensor"),
        P("dp", "tensor"),
        P("dp", "tensor"),
        P("dp", "tensor"),
        P("dp"),
        P("dp"),
        P("dp"),
    )
    return jax.shard_map(
        functools.partial(shards, plan),
        mesh=mesh,
        in_specs=placed,
        out_specs=(
            P("dp", None),
            P("dp", None),
            P("dp", "tensor", None, None),
            P("dp", "tensor", None, None),
            P("dp", "tensor", None, None),
            P("dp", "tensor"),
            P("dp", "tensor"),
            P("dp", "tensor"),
            P(None, "dp", "tensor"),
            P(None, "dp", "tensor"),
            P(None, "dp", "tensor"),
            P("dp", "tensor"),
            P("dp", "tensor"),
            P("dp", "tensor"),
            P("dp"),
            P("dp"),
            P("dp"),
        ),
        check_vma=False,
    )
```

```python
import functools
import math

import jax
import jax.numpy as jnp
from jax import lax
from jax.experimental import pallas as pl
from jax.experimental.pallas import tpu as pltpu
from jax.sharding import PartitionSpec as P

SEQ = 1024
STEP = 10


EPS_NORM = 1e-06
THETA = 1000000.0
BETA_ONE = 0.9
BETA_TWO = 0.95
ADAM_EPS = 1e-08
DECAY_RATE = 0.1
RATE_QKV = 0.05
RATE_OUT = 0.3
RATE_GATE = 0.05
RATE_DOWN = 0.03
RATE_GAIN = 1.0


def rotary(positions, head_size):
    freq_index = jnp.arange(head_size // 2, dtype=jnp.float32)
    inverse = jnp.exp(freq_index * (-2.0 * math.log(THETA) / head_size))
    angles = positions.astype(jnp.float32)[:, None] * inverse[None, :]
    cosine = jnp.cos(angles)
    sine_table = jnp.sin(angles)
    return (jnp.concatenate([cosine, cosine], -1), jnp.concatenate([sine_table, sine_table], -1))


def rotate(values, cosine, sine_table):
    half_size = values.shape[-1] // 2
    turned = jnp.concatenate([-values[..., half_size:], values[..., :half_size]], -1)
    return values * cosine[:, None, :] + turned * sine_table[:, None, :]


def unrotate(gradient, cosine, sine_table):
    half_size = gradient.shape[-1] // 2
    turned = gradient * sine_table[:, None, :]
    rotated_back = jnp.concatenate([turned[..., half_size:], -turned[..., :half_size]], -1)
    return gradient * cosine[:, None, :] + rotated_back


def norm_back(grad_unit, unit_vals, factor):
    return factor * (grad_unit - unit_vals * jnp.mean(grad_unit * unit_vals, -1, keepdims=True))


def contract_rows(left, right):
    return lax.dot_general(
        left, right, (((0,), (0,)), ((), ())), preferred_element_type=jnp.float32
    )


def contract_cols(left, right):
    return lax.dot_general(
        left, right, (((1,), (1,)), ((), ())), preferred_element_type=jnp.float32
    )


def block_scores(query_part, key_part, first_row, block_rows, last_row):
    scores = jnp.einsum(
        "nqkgd,nskd->nkgqs", query_part, key_part, preferred_element_type=jnp.float32
    )
    causal = (first_row + jnp.arange(block_rows))[:, None] >= jnp.arange(last_row)[None, :]
    return jnp.where(causal, scores, -1000000000.0)


def attention_forward(query, key_rot, values_low, seq_len):
    block_rows = min(512, seq_len)
    outputs = []
    log_sums = []
    for first_row in range(0, seq_len, block_rows):
        last_row = first_row + block_rows
        query_part = query[:, first_row:last_row]
        scores = block_scores(query_part, key_rot[:, :last_row], first_row, block_rows, last_row)
        row_max = jnp.max(scores, -1, keepdims=True)
        exponent = jnp.exp(scores - row_max)
        row_total = jnp.sum(exponent, -1, keepdims=True)
        probs_low = (exponent / row_total).astype(jnp.bfloat16)
        outputs.append(
            jnp.einsum(
                "nkgqs,nskd->nqkgd",
                probs_low,
                values_low[:, :last_row],
                preferred_element_type=jnp.float32,
            )
        )
        log_sums.append(row_max + jnp.log(row_total))
    return (jnp.concatenate(outputs, 1), log_sums)


def attention_backward(query, key_rot, values_low, grad_att, log_sums, seq_len):
    block_rows = min(512, seq_len)
    query_grads = []
    key_grad = jnp.zeros(key_rot.shape, jnp.float32)
    value_grad = jnp.zeros(values_low.shape, jnp.float32)
    for block_index, first_row in enumerate(range(0, seq_len, block_rows)):
        last_row = first_row + block_rows
        query_part = query[:, first_row:last_row]
        grad_part = grad_att[:, first_row:last_row]
        key_part = key_rot[:, :last_row]
        value_part = values_low[:, :last_row]
        scores = block_scores(query_part, key_part, first_row, block_rows, last_row)
        probs = jnp.exp(scores - log_sums[block_index])
        probs_low = probs.astype(jnp.bfloat16)
        grad_probs = jnp.einsum(
            "nqkgd,nskd->nkgqs", grad_part, value_part, preferred_element_type=jnp.float32
        )
        grad_scores = (
            probs * (grad_probs - jnp.sum(probs * grad_probs, -1, keepdims=True))
        ).astype(jnp.bfloat16)
        query_grads.append(
            jnp.einsum(
                "nkgqs,nskd->nqkgd", grad_scores, key_part, preferred_element_type=jnp.float32
            )
        )
        padding = ((0, 0), (0, seq_len - last_row), (0, 0), (0, 0))
        key_grad = key_grad + jnp.pad(
            jnp.einsum(
                "nkgqs,nqkgd->nskd", grad_scores, query_part, preferred_element_type=jnp.float32
            ),
            padding,
        )
        value_grad = value_grad + jnp.pad(
            jnp.einsum(
                "nkgqs,nqkgd->nskd", probs_low, grad_part, preferred_element_type=jnp.float32
            ),
            padding,
        )
    return (jnp.concatenate(query_grads, 1), key_grad, value_grad)


def adamw(weight, gradient, moment, second, step_rate, decay_rate):
    moment = BETA_ONE * moment + (1.0 - BETA_ONE) * gradient
    second = BETA_TWO * second + (1.0 - BETA_TWO) * gradient * gradient
    first_hat = moment / (1.0 - BETA_ONE**STEP)
    second_hat = second / (1.0 - BETA_TWO**STEP)
    weight = weight - step_rate * (
        first_hat / (jnp.sqrt(second_hat) + ADAM_EPS) + decay_rate * weight
    )
    return (moment, second, weight)


def fence(*values):
    return lax.optimization_barrier(values)


MESH = pl.DeviceIdType.MESH
HEAD = 128
AHEAD = 2


def place_here():
    index, place = lax.axis_index("dp"), lax.axis_index("tensor")
    return lax.div(index, 2), lax.rem(index, 2), lax.div(place, 2), lax.rem(place, 2)


def device(zone, side, row, core):
    return (zone * 2 + side, row * 2 + core)


def flipped(zone, flip):
    bit = 1
    while bit <= flip:
        if flip & bit:
            zone = zone + bit - 2 * bit * lax.rem(lax.div(zone, bit), 2)
        bit *= 2
    return zone


def greet(devices, amount=None):
    barrier = pltpu.get_barrier_semaphore()
    for peer in devices:
        pl.semaphore_signal(barrier, inc=1, device_id=peer, device_id_type=MESH)
    pl.semaphore_wait(barrier, len(devices) if amount is None else amount)


def for_rows(count, body):
    step = 32

    def one(block, carry):
        body(pl.multiple_of(block * step, step), step)
        return carry

    lax.fori_loop(0, count // step, one, 0)


class Copies:
    def __init__(self, send_sems, recv_sems):
        self.send_sems, self.recv_sems = send_sems, recv_sems
        self.number = 0

    def make(self, source, target, peer):
        number, self.number = self.number, self.number + 1
        return pltpu.make_async_remote_copy(
            src_ref=source,
            dst_ref=target,
            send_sem=self.send_sems.at[number],
            recv_sem=self.recv_sems.at[number],
            device_id=peer,
            device_id_type=MESH,
        )

    def start(self, source, target, peer):
        copy = self.make(source, target, peer)
        copy.start()
        return copy


class GainSum:
    def __init__(self, plan, rest, width):
        self.plan, self.width = plan, width
        self.total = width + rest
        self.scratch = [
            pltpu.VMEM((8, 1, self.total), jnp.float32),
            pltpu.VMEM((plan.zones, 1, self.total), jnp.float32),
        ]
        self.output = jax.ShapeDtypeStruct((1, self.total), jnp.float32)
        self.count = 7 + plan.zones - 1

    def plane_peers(self, zone, side, row, core):
        steps = [(s, r, c) for s in range(2) for r in range(2) for c in range(2)][1:]
        turn = lambda value, step: 1 - value if step else value
        return [device(zone, turn(side, s), turn(row, r), turn(core, c)) for s, r, c in steps]

    def zone_peers(self, zone, side, row, core):
        return {flip: device(flipped(zone, flip), side, row, core) for flip in self.plan.flips[1:]}

    def start(self, copies, rest, blocks, plane_sums, zone_sums):
        zone, side, row, core = place_here()
        plan = self.plan
        size = self.width // plan.total
        self.copies, self.plane_sums, self.zone_sums, self.zone = copies, plane_sums, zone_sums, zone
        here = side * 4 + row * 2 + core
        plane_sums[here, :, pl.ds(self.width, self.total - self.width)] = rest[...]
        for slot in range(plan.total):
            owner = flipped(zone, plan.flips[slot % plan.zones]) * 2
            owner = owner + (core if slot < plan.zones else 1 - core)
            spot = pl.ds(pl.multiple_of(owner * size, size), size)
            plane_sums[here, :, spot] = blocks[:, pl.ds(slot * size, size)]
        self.plane = [
            copies.start(plane_sums.at[here], plane_sums.at[here], peer)
            for peer in self.plane_peers(zone, side, row, core)
        ]

    def middle(self):
        for copy in self.plane:
            copy.wait_recv()
        total = self.plane_sums[0]
        for place in range(1, 8):
            total = total + self.plane_sums[place]
        self.zone_sums[self.zone] = total
        zone, side, row, core = place_here()
        self.across = [
            self.copies.start(self.zone_sums.at[self.zone], self.zone_sums.at[self.zone], peer)
            for peer in self.zone_peers(zone, side, row, core).values()
        ]

    def finish(self, out):
        for copy in self.across:
            copy.wait_recv()
        total = self.zone_sums[0]
        for place in range(1, self.plan.zones):
            total = total + self.zone_sums[place]
        out[...] = total
        for copy in self.plane + self.across:
            copy.wait_send()


class ZoneBlocks:
    scratch = []

    def __init__(self, plan, source, slots, begin=0):
        self.flips, self.slots, self.sources, self.begin = plan.flips, list(slots), [source], begin
        self.outputs = [
            jax.ShapeDtypeStruct((len(self.slots),) + source.shape[1:], source.dtype)
        ]
        self.count, self.count_local = len(self.slots), 0
        self.in_hbm = False

    def peers(self, zone, side, row, core):
        return {
            self.flips[slot]: device(flipped(zone, self.flips[slot]), side, row, core)
            for slot in self.slots
        }

    def start(self, copies, local_sems, sources, targets, stages):
        zone, side, row, core = place_here()
        self.started = [
            copies.make(
                sources[0].at[slot],
                targets[0].at[number],
                device(flipped(zone, self.flips[slot]), side, row, core),
            )
            for number, slot in enumerate(self.slots)
        ]
        self.waiting = True
        if self.begin == 0:
            self.pump([0])

    def pump(self, steps):
        if self.waiting and self.begin in steps:
            self.waiting = False
            for copy in self.started:
                copy.start()

    def finish(self):
        for copy in self.started:
            copy.wait_send()
        for copy in self.started:
            copy.wait_recv()


def inner_zone(zone):
    return lax.rem(lax.div(zone + 1, 2), 2)


class SideDot:
    count, count_local, scratch, in_hbm = 0, 0, [], False

    def __init__(self, left, right):
        self.sources = [left, right]
        self.outputs = [jax.ShapeDtypeStruct((left.shape[0], right.shape[0]), jnp.bfloat16)]

    def peers(self, zone, side, row, core):
        return {}

    def some(self, first, last):
        left, right = self.refs
        size = 256

        def one(step, carry):
            here = pl.ds(pl.multiple_of(step * size, size), size)
            self.out[:, here] = dot(left[...], right[here, :], 1, 1).astype(jnp.bfloat16)
            return carry

        lax.fori_loop(first, last, one, 0)

    def start(self, copies, local_sems, sources, targets, stages):
        self.refs, self.out = sources, targets[0]
        self.steps = self.out.shape[1] // 256
        self.some(0, self.steps // 2)

    def pump(self, steps):
        if 0 in steps:
            self.some(self.steps // 2, self.steps)

    def finish(self):
        pass


class PairScatter:
    def __init__(self, parts, pieces):
        self.sources, self.pieces = [parts], pieces
        _, rows, columns = parts.shape
        self.size = rows // pieces
        self.outputs = [jax.ShapeDtypeStruct((2, rows, columns), parts.dtype)]
        self.scratch = [pltpu.VMEM((2, rows, columns), parts.dtype)] * 2
        self.count, self.count_local = 4 * pieces, 0
        self.in_hbm = False

    def peers(self, zone, side, row, core):
        return {
            1: device(flipped(zone, 1), side, row, core),
            3: device(flipped(zone, 3), side, row, core),
        }

    def start(self, copies, local_sems, sources, targets, stages):
        zone, side, row, core = place_here()
        self.parts, self.out = sources[0], targets[0]
        self.inward, self.crossed = stages
        inner_peer = device(flipped(zone, 3), side, row, core)
        outer_peer = device(flipped(zone, 1), side, row, core)
        self.inner = inner_zone(zone) == 1
        self.outer = inner_zone(zone) == 0
        self.steps = [
            (slot, pl.ds(piece * self.size, self.size))
            for piece in range(self.pieces)
            for slot in (0, 1)
        ]
        self.to_inner = [
            copies.make(self.parts.at[3 - slot, rows], self.inward.at[slot, rows], outer_peer)
            for slot, rows in self.steps
        ]
        self.across = [
            copies.make(self.inward.at[slot, rows], self.crossed.at[slot, rows], inner_peer)
            for slot, rows in self.steps
        ]

        @pl.when(self.outer)
        def _():
            for copy in self.to_inner[:AHEAD]:
                copy.start()

    def add(self, target, slot, rows, left, right):
        def some(row, count):
            here = pl.ds(rows.start + row, count)
            both = left[here, :].astype(jnp.float32) + right[here, :].astype(jnp.float32)
            target.at[slot][here, :] = both.astype(jnp.bfloat16)

        for_rows(self.size, some)

    def pump(self, steps):
        steps = [step for step in steps if step < len(self.steps)]

        @pl.when(self.inner)
        def _():
            for step in steps:
                slot, rows = self.steps[step]
                self.to_inner[step].wait_recv()
                self.add(self.inward, slot, rows, self.parts.at[2 + slot], self.inward.at[slot])
                self.across[step].start()
                if step >= AHEAD:
                    self.settle(step - AHEAD)

        @pl.when(self.outer)
        def _():
            for step in steps:
                self.to_inner[step].wait_send()
                for copy in self.to_inner[step + AHEAD : step + AHEAD + 1]:
                    copy.start()

    def settle(self, step):
        slot, rows = self.steps[step]
        self.across[step].wait_recv()
        self.add(self.out, slot, rows, self.parts.at[slot], self.crossed.at[slot])

    def finish(self):
        @pl.when(self.inner)
        def _():
            for step in range(len(self.steps) - AHEAD, len(self.steps)):
                self.settle(step)
            for copy in self.across:
                copy.wait_send()

        @pl.when(self.outer)
        def _():
            for slot in (0, 1):

                def some(row, count, slot=slot):
                    here = pl.ds(row, count)
                    self.out.at[slot][here, :] = self.parts.at[slot][here, :]

                for_rows(self.parts.shape[1], some)


class PairTree:
    def __init__(self, pairs, pieces, landed):
        self.pairs = [len(pair) for pair in pairs]
        self.sources = [shard for pair in pairs for shard in pair] + [landed]
        self.pieces = pieces
        self.outputs = [
            jax.ShapeDtypeStruct((8,) + own.shape, own.dtype) for own, *_ in pairs
        ]
        self.count = 6 * sum(pieces) + 2 * len(pairs) + self.pairs.count(1)
        self.count_local = 2 * len(pairs) + 2 * sum(pieces)
        self.scratch = [pltpu.VMEM((2,) + own.shape, own.dtype) for own, *_ in pairs]
        self.scratch += [pltpu.VMEM(p[0].shape, p[0].dtype) for p in pairs if len(p) == 1]
        self.in_hbm = True

    def peers(self, zone, side, row, core):
        return {
            1: device(flipped(zone, 1), side, row, core),
            3: device(flipped(zone, 3), side, row, core),
            "core": device(zone, side, row, 1 - core),
        }

    def start(self, copies, local_sems, sources, targets, stages):
        zone, side, row, core = place_here()
        inner_peer = device(flipped(zone, 3), side, row, core)
        outer_peer = device(flipped(zone, 1), side, row, core)
        core_peer = device(zone, side, row, 1 - core)
        self.inner = inner_zone(zone) == 1
        self.outer = inner_zone(zone) == 0
        self.across, self.onward, self.late, self.place = [], [], [], []
        self.shared, self.kept, self.partners = [], [], []
        sem = 0
        sources, late_stages = list(sources), list(stages[len(targets) :])
        for weight, full in enumerate(targets):
            landing = stages[weight]
            pair = [sources.pop(0) for _ in range(self.pairs[weight])]
            if len(pair) == 1:
                pair.append(late_stages.pop(0))
                self.partners.append(copies.start(pair[0], pair[1], outer_peer))
            size = pair[0].shape[0] // self.pieces[weight]
            for piece in range(self.pieces[weight]):
                rows = pl.ds(piece * size, size)
                for slot in (0, 1):
                    here = landing.at[slot, rows]
                    first = weight == 0 and piece == 0 and slot == 0
                    self.across.append(
                        None if first else copies.make(pair[slot].at[rows], here, inner_peer)
                    )
                    self.onward.append(copies.make(here, landing.at[1 - slot, rows], outer_peer))
                    self.late.append(copies.make(here, full.at[6 + slot, rows], core_peer))
                    self.place.append(
                        pltpu.make_async_copy(here, full.at[2 + slot, rows], local_sems.at[sem])
                    )
                    sem += 1
            for slot in (0, 1):
                self.shared.append(copies.make(pair[slot], full.at[4 + slot], core_peer))
                self.kept.append(
                    pltpu.make_async_copy(pair[slot], full.at[slot], local_sems.at[sem])
                )
                sem += 1

        landed = sources[-1]
        landed_rows = pl.ds(0, landed.shape[0])

        @pl.when(self.inner)
        def _():
            for copy in self.across[1 : 1 + AHEAD]:
                copy.start()
            copy_rows(landed, stages[0].at[0, landed_rows])
            self.onward[0].start()
            self.late[0].start()
            self.place[0].start()

    def pump(self, steps):
        steps = [step for step in steps if step + 1 < len(self.across)]

        @pl.when(self.inner)
        def _():
            for step in steps:
                here = step + 1
                self.across[here].wait_recv()
                for copy in self.across[here + AHEAD : here + AHEAD + 1]:
                    copy.start()
                self.onward[here].start()
                self.late[here].start()
                self.place[here].start()

        for copy in self.partners if 1 in steps else []:
            copy.wait_recv()
            copy.wait_send()
        for copy in self.shared + self.kept if 1 in steps else []:
            copy.start()

    def finish(self):
        @pl.when(self.inner)
        def _():
            for copy in self.across[1:] + self.onward:
                copy.wait_send()

        @pl.when(self.outer)
        def _():
            for number, copy in enumerate(self.onward):
                copy.wait_recv()
                arrived = number + 1 - 2 * (number % 2)
                self.late[arrived].start()
                self.place[arrived].start()

        for copy in self.kept + self.place:
            copy.wait()
        for copy in self.shared + self.late:
            copy.wait_send()
        for copy in self.shared + self.late:
            copy.wait_recv()


def sum_eighths(
    copies, row_peer, side_peer, send, keep, forward, first, second, store, begin, pump
):
    size = send.shape[0] // 4
    part = lambda ref, slot: ref.at[pl.ds(slot * size, size)]
    arrivals = [
        copies.start(part(send, 1), part(first, 1), row_peer),
        copies.start(part(send, 3), part(first, 3), side_peer),
        copies.start(part(send, 0), part(first, 0), row_peer),
        copies.start(part(send, 2), part(first, 2), side_peer),
    ]
    begin()
    passed = []
    for number, slot, peer in ((0, 1, side_peer), (1, 3, row_peer)):
        arrivals[number].wait_recv()

        def add(row, count, number=number, slot=slot):
            here = pl.ds(slot * size + row, count)
            both = keep[here, :].astype(jnp.float32) + first[here, :].astype(jnp.float32)
            forward[pl.ds(number * size + row, count), :] = both.astype(jnp.bfloat16)

        for_rows(size, add)
        passed.append(copies.start(part(forward, number), part(second, number), peer))
    pump([0])
    for number, slot in ((0, 0), (1, 2)):
        arrivals[2 + number].wait_recv()
        passed[number].wait_recv()

        def total(row, count, number=number, slot=slot):
            here = pl.ds(slot * size + row, count)
            sums = keep[here, :].astype(jnp.float32) + first[here, :].astype(jnp.float32)
            sums = sums + second[pl.ds(number * size + row, count), :].astype(jnp.float32)
            store(number, row, count, sums)

        for_rows(size, total)
        yield number
    for copy in arrivals + passed:
        copy.wait_send()


def halves(terms):
    rows = terms.shape[0] // 2
    return terms.at[pl.ds(0, rows)], terms.at[pl.ds(rows, rows)]


def split_refs(refs, jobs, extra_count, out_count):
    refs = list(refs)
    take = lambda count: [refs.pop(0) for _ in range(count)]
    extras = take(extra_count)
    sources = [take(len(job.sources)) for job in jobs]
    full = take(1)[0]
    outs = take(out_count)
    targets = [take(len(job.outputs)) for job in jobs]
    return extras, sources, full, outs, targets, refs


def spread_kernel(middle, jobs, extra_count, out_count, gain_sum, terms, *refs):
    keep, send = halves(terms)
    extras, sources, full, outs, targets, scratch = split_refs(refs, jobs, extra_count, out_count)
    forward, first, second, send_sems, recv_sems, local_sems, *stages = scratch
    zone, side, row, core = place_here()
    row_peer, side_peer = device(zone, side, 1 - row, core), device(zone, 1 - side, row, core)
    copies = Copies(send_sems, recv_sems)
    size = send.shape[0] // 4
    part = lambda slot: full.at[pl.ds(slot * size, size)]
    for out in outs:
        if out.shape[0] == 1:
            out[...] = jnp.zeros_like(out)
    peers = {}
    for job in jobs:
        peers.update(job.peers(zone, side, row, core))
    greet([row_peer, side_peer] + list(peers.values()))

    def begin():
        spot = 0
        for job, source, target in zip(jobs, sources, targets):
            own_stages = stages[spot : spot + len(job.scratch)]
            job.start(copies, local_sems, source, target, own_stages)
            spot += len(job.scratch)

    def pump(steps):
        for job in jobs:
            job.pump(steps)

    def store(number, row, count, sums):
        own = pl.ds(number * size + row, count)
        full[pl.ds(2 * number * size + row, count), :] = middle(own, sums, extras, outs)

    firsts, seconds = [], []
    for number in sum_eighths(
        copies, row_peer, side_peer, send, keep, forward, first, second, store, begin, pump
    ):
        near, other = (side_peer, row_peer) if number == 0 else (row_peer, side_peer)
        slot = 2 * number
        firsts.append(copies.start(part(slot), part(slot + 1), near))
        seconds.append(copies.start(part(slot), part(4 + slot), other))
    pump([1])
    firsts[0].wait_recv()
    seconds.append(copies.start(part(1), part(5), row_peer))
    firsts[1].wait_recv()
    seconds.append(copies.start(part(3), part(7), side_peer))
    pump(range(2, 64))
    for copy in seconds:
        copy.wait_recv()
    for copy in firsts + seconds:
        copy.wait_send()
    for job in jobs:
        job.finish()


def home_kernel(middle, jobs, extra_count, out_count, gain_sum, terms, *refs):
    keep, send = halves(terms)
    extras, sources, full, outs, targets, scratch = split_refs(refs, jobs, extra_count, out_count)
    forward, first, second, own, send_sems, recv_sems, local_sems, *gain_scratch = scratch
    zone, side, row, core = place_here()
    row_peer, side_peer = device(zone, side, 1 - row, core), device(zone, 1 - side, row, core)
    core_peer = device(zone, side, row, 1 - core)
    copies = Copies(send_sems, recv_sems)
    size = send.shape[0] // 4
    at_home = side == core
    away = side != core
    for out in outs:
        if out.shape[0] == 1:
            out[...] = jnp.zeros_like(out)
    peers = {}
    for job in jobs:
        peers.update(job.peers(zone, side, row, core))
    plane = [row_peer, side_peer, core_peer]
    if gain_sum is not None:
        plane = gain_sum.plane_peers(zone, side, row, core)
        peers.update(gain_sum.zone_peers(zone, side, row, core))
    greet(plane + list(peers.values()))

    def begin():
        for job, source, target in zip(jobs, sources, targets):
            job.start(copies, local_sems, source, target, [])

    def pump(steps):
        for job in jobs:
            job.pump(steps)

    def store(number, start, count, sums):
        here = pl.ds(number * size + start, count)
        values = middle(here, sums, extras, outs)
        own[here, :] = values
        eighth = row * 2 + side if number == 0 else 4 + side * 2 + row

        @pl.when(at_home)
        def _():
            full[pl.ds(pl.multiple_of(eighth * size + start, 32), count), :] = values

    for _ in sum_eighths(
        copies, row_peer, side_peer, send, keep, forward, first, second, store, begin, pump
    ):
        pass
    pump([1])

    def piece(number, x, y):
        start = (x * 2 + y) * size if number == 0 else (4 + y * 2 + x) * size
        return full.at[pl.ds(pl.multiple_of(start, size), size)]

    mine = lambda number: own.at[pl.ds(number * size, size)]
    both = (0, 1)
    to_side = [copies.make(mine(k), piece(k, row, side), side_peer) for k in both]
    to_row = [copies.make(mine(k), piece(k, row, side), row_peer) for k in both]
    pass_row = [
        copies.make(piece(k, row, 1 - side), piece(k, row, 1 - side), row_peer) for k in both
    ]
    share = []
    for number, (x, y) in enumerate(
        ((row, side), (row, 1 - side), (1 - row, side), (1 - row, 1 - side))
    ):
        for k in both:
            source = mine(k) if number == 0 else piece(k, x, y)
            share.append(copies.make(source, piece(k, x, y), core_peer))

    if gain_sum is not None:
        gain_sum.start(copies, extras[-1], outs[0], *gain_scratch)

    @pl.when(away)
    def _():
        for copy in to_side:
            copy.start()

    @pl.when(at_home)
    def _():
        for copy in to_row + share[:2]:
            copy.start()

    if gain_sum is not None:
        gain_sum.middle()

    @pl.when(away)
    def _():
        for copy in to_side:
            copy.wait_send()
        for copy in share:
            copy.wait_recv()

    @pl.when(at_home)
    def _():
        for k in both:
            to_side[k].wait_recv()
            pass_row[k].start()
            share[2 + k].start()
        for k, copy in enumerate(to_row + pass_row):
            copy.wait_recv()
            share[4 + k].start()
        for copy in to_row + pass_row + share:
            copy.wait_send()

    if gain_sum is not None:
        gain_sum.finish(outs[-1])
    for job in jobs:
        job.finish()


def sum_rows(kernel, middle, terms, extras, outs, number, jobs=(), gain_sum=None):
    half, width = terms.shape[0] // 2, terms.shape[1]
    eighth = half // 4
    low = jnp.bfloat16
    vmem, hbm = pl.BlockSpec(memory_space=pltpu.VMEM), pl.BlockSpec(memory_space=pl.ANY)
    scratch = [
        pltpu.VMEM((2 * eighth, width), low),
        pltpu.VMEM((half, width), low),
        pltpu.VMEM((2 * eighth, width), low),
    ]
    if kernel is home_kernel:
        scratch.append(pltpu.VMEM((2 * eighth, width), low))
    copies = (12 if kernel is spread_kernel else 20) + sum(job.count for job in jobs)
    local = max([2] + [job.count_local for job in jobs])
    if gain_sum is not None:
        copies += gain_sum.count
        outs = outs + [gain_sum.output]
    scratch += [pltpu.SemaphoreType.DMA((count,)) for count in (copies, copies, local)]
    if gain_sum is not None:
        scratch += gain_sum.scratch
    scratch += [stage for job in jobs for stage in job.scratch]
    sources = [source for job in jobs for source in job.sources]
    targets = [target for job in jobs for target in job.outputs]
    return pl.pallas_call(
        functools.partial(kernel, middle, jobs, len(extras), len(outs), gain_sum),
        out_shape=[jax.ShapeDtypeStruct((2 * half, width), low)] + outs + targets,
        in_specs=[vmem] * (1 + len(extras) + len(sources)),
        out_specs=[vmem] * (1 + len(outs))
        + [hbm if job.in_hbm else vmem for job in jobs for _ in job.outputs],
        scratch_shapes=scratch,
        compiler_params=pltpu.CompilerParams(
            collective_id=number, has_side_effects=True, vmem_limit_bytes=56 * 2**20
        ),
        cost_estimate=pl.CostEstimate(flops=4 * 10**10, bytes_accessed=10**8, transcendentals=0),
        name=middle.__name__,
    )(terms, *extras, *sources)


def block_columns(plan, width):
    if not plan.ordered:
        return [pl.ds(0, width)], [pl.ds(0, width)]
    zone, _, _, core = place_here()
    size, zones = width // plan.total, plan.zones
    owners = [
        flipped(zone, plan.flips[slot % zones]) * 2 + (core if slot < zones else 1 - core)
        for slot in range(plan.total)
    ]
    natural = [pl.ds(pl.multiple_of(owner * size, size), size) for owner in owners]
    return natural, [pl.ds(slot * size, size) for slot in range(plan.total)]


def copy_rows(source, target):
    def some(row, count):
        target[pl.ds(row, count), :] = source[pl.ds(row, count), :]

    if source.shape[0] % 32:
        target[...] = source[...]
    else:
        for_rows(source.shape[0], some)


def cast_rows(source, target):
    def some(row, count):
        here = pl.ds(row, count)
        target[here, :] = source[here, :].astype(target.dtype)

    for_rows(source.shape[0], some)


def opening_kernel(plan, wide_qkv, gains, wide_gate, wide_out, tokens, angles, *refs):
    qkv_full, gains_full, turned_gate, turned_out, turned_tokens, turned_angles = refs[:6]
    partner_gate, send_sems, recv_sems, tokens_stage, qkv, gate, out = refs[6:]
    cast_rows(wide_qkv, qkv)
    zone, side, row, core = place_here()
    partner = device(zone, core, row, side)
    row_peer, core_peer = device(zone, side, 1 - row, core), device(zone, side, row, 1 - core)
    zone_peers = [device(flipped(zone, flip), side, row, core) for flip in plan.flips[1:]]
    at_home, away = side == core, side != core
    always = [row_peer, core_peer] + zone_peers

    @pl.when(at_home)
    def _():
        greet(always)

    @pl.when(away)
    def _():
        greet(always + [partner])

    copies = Copies(send_sems, recv_sems)
    zones = plan.zones
    own = (gains, qkv, angles, gate, out)
    ends = (gains_full.at[0], qkv_full.at[0], turned_angles, turned_gate, turned_out)
    units = wide_gate.shape[2]

    def cast_rest():
        for half in (0, 1):
            cast_rows(wide_gate.at[half], gate.at[:, pl.ds(half * units, units)])
        cast_rows(wide_out, out)

    turn = [copies.make(source, target, partner) for source, target in zip(own, ends)]
    pieces = 2
    size = tokens.shape[0] // (2 * pieces)
    spots = [
        pl.ds(pl.multiple_of((row * pieces + piece) * size, size), size) for piece in range(pieces)
    ]
    turn_rows = [copies.make(tokens.at[s], tokens_stage.at[s], partner) for s in spots]
    pass_rows = [copies.make(tokens_stage.at[s], tokens_stage.at[s], row_peer) for s in spots]
    natural, local = block_columns(plan, tokens.shape[1])

    def lay_down(all_tokens):
        def some(start, count):
            here = pl.ds(start, count)
            for a, b in zip(natural, local):
                turned_tokens[here, b] = all_tokens[here, a]

        for_rows(all_tokens.shape[0], some)

    slots = list(range(1, zones))
    weights = ((gains, gains_full), (qkv, qkv_full))
    swapped = pl.ds(0, gate.shape[0] // 2)
    from_own = [
        [copies.make(source, full.at[slot], zone_peers[slot - 1]) for slot in slots]
        + [copies.make(source, full.at[zones], core_peer)]
        for source, full in weights
    ] + [[copies.make(gate.at[swapped], partner_gate, zone_peers[0])]]
    copies.number -= 2 * zones + 1
    from_turned = [
        [copies.make(full.at[0], full.at[slot], zone_peers[slot - 1]) for slot in slots]
        + [copies.make(full.at[0], full.at[zones], core_peer)]
        for _, full in weights
    ] + [[copies.make(turned_gate.at[swapped], partner_gate, zone_peers[0])]]
    cross = [
        [copies.make(full.at[slot], full.at[zones + slot], core_peer) for slot in slots]
        for _, full in weights
    ]

    def cross_over(k):
        for which in (0, 1):
            from_turned[which][k].wait_recv()
            cross[which][k].start()

    @pl.when(away)
    def _():
        for copy in turn[:3]:
            copy.start()
        cast_rest()
        for which in (0, 1):
            turn[which].wait_recv()
            for copy in from_turned[which]:
                copy.start()
        turn[3].start()
        turn_rows[0].start()
        turn[3].wait_recv()
        from_turned[2][0].start()
        turn_rows[1].start()
        cross_over(0)
        turn_rows[0].wait_recv()
        pass_rows[0].start()
        for copy in turn[4:]:
            copy.start()
        turn_rows[1].wait_recv()
        pass_rows[1].start()

    @pl.when(at_home)
    def _():
        for copy in from_own[0] + from_own[1]:
            copy.start()
        cast_rest()
        for copy in from_own[2]:
            copy.start()
        for source, target in zip(own, ends):
            copy_rows(source, target)
        lay_down(tokens)
        cross_over(0)

    for k in range(1, zones - 1):
        cross_over(k)
    for which in (0, 1):
        from_turned[which][zones - 1].wait_recv()
        for copy in from_turned[which]:
            copy.wait_send()
        for copy in cross[which]:
            copy.wait_recv()
            copy.wait_send()
    from_turned[2][0].wait_recv()
    from_turned[2][0].wait_send()

    @pl.when(away)
    def _():
        for copy in pass_rows + turn[2:3] + turn[4:]:
            copy.wait_recv()
        lay_down(tokens_stage)
        for copy in turn + turn_rows + pass_rows:
            copy.wait_send()


def opening(plan, qkv, gains, gate, out, tokens, angles, number):
    low = jnp.bfloat16
    vmem = pl.BlockSpec(memory_space=pltpu.VMEM)
    like = lambda v: jax.ShapeDtypeStruct(v.shape, v.dtype)
    whole = lambda v: jax.ShapeDtypeStruct((2 * plan.zones,) + v.shape, low)
    operands = (qkv, gains, gate, out, tokens, angles)
    low_gate = jax.ShapeDtypeStruct((gate.shape[1], 2 * gate.shape[2]), low)
    low_out = jax.ShapeDtypeStruct(out.shape, low)
    outputs = [whole(qkv), whole(gains), low_gate, low_out, like(tokens), like(angles)]
    outputs += [jax.ShapeDtypeStruct((gate.shape[1] // 2, 2 * gate.shape[2]), low)]
    copies = 5 + 4 + 2 * plan.zones + 1 + 2 * (plan.zones - 1)
    return pl.pallas_call(
        functools.partial(opening_kernel, plan),
        out_shape=outputs,
        in_specs=[vmem] * len(operands),
        out_specs=[vmem] * len(outputs),
        scratch_shapes=[
            pltpu.SemaphoreType.DMA((copies,)),
            pltpu.SemaphoreType.DMA((copies,)),
            pltpu.VMEM(tokens.shape, tokens.dtype),
            pltpu.VMEM(qkv.shape, low),
            pltpu.VMEM(low_gate.shape, low),
            pltpu.VMEM(out.shape, low),
        ],
        compiler_params=pltpu.CompilerParams(
            collective_id=number, has_side_effects=True, vmem_limit_bytes=56 * 2**20
        ),
        cost_estimate=pl.CostEstimate(flops=4 * 10**10, bytes_accessed=10**8, transcendentals=0),
        name="opening",
    )(*operands)


def inverse_rms(values):
    return lax.rsqrt(jnp.mean(values * values, -1, keepdims=True) + EPS_NORM)


def hidden_rows(own, sums, extras, outs):
    tokens, gain = extras
    hidden = tokens[own, :].astype(jnp.float32) + sums
    outs[0][own, :] = hidden
    return (hidden * inverse_rms(hidden) * gain[...]).astype(jnp.bfloat16)


def grad_hidden_rows(own, sums, extras, outs):
    hidden, out_grad, gain = extras
    values = hidden[own, :]
    factor = inverse_rms(values)
    unit = values * factor
    outs[1][...] += jnp.sum(sums * unit, 0, keepdims=True)
    grad = out_grad[own, :].astype(jnp.float32) + norm_back(sums * gain[...], unit, factor)
    outs[0][own, :] = grad
    return grad.astype(jnp.bfloat16)


def grad_input_rows(own, sums, extras, outs):
    tokens, grad_hidden, gain = extras[:3]
    values = tokens[own, :].astype(jnp.float32)
    factor = inverse_rms(values)
    unit = values * factor
    outs[0][...] += jnp.sum(sums * unit, 0, keepdims=True)
    return (grad_hidden[own, :] + norm_back(sums * gain[...], unit, factor)).astype(jnp.bfloat16)


def dot(left, right, left_dim=1, right_dim=0):
    return lax.dot_general(
        left, right, (((left_dim,), (right_dim,)), ((), ())), preferred_element_type=jnp.float32
    )


def turn_head(values, cosine, signed_sine):
    return values * cosine + pltpu.roll(values, HEAD // 2, 1) * signed_sine


def turn_back(gradient, cosine, signed_sine):
    return gradient * cosine + pltpu.roll(gradient * signed_sine, HEAD // 2, 1)


def softmax_block(query, key, first_row):
    rows, keys = query.shape[0], key.shape[0]
    scores = dot(query, key, 1, 1)
    row_at = lax.broadcasted_iota(jnp.int32, (rows, keys), 0) + first_row
    key_at = lax.broadcasted_iota(jnp.int32, (rows, keys), 1)
    scores = jnp.where(key_at <= row_at, scores, -1000000000.0)
    exponent = jnp.exp(scores - jnp.max(scores, -1, keepdims=True))
    return exponent / jnp.sum(exponent, -1, keepdims=True)


def eighth_owners():
    _, side, row, _ = place_here()
    own, off = (row, side), (1 - row, 1 - side)
    first = lambda x, y: x * 2 + y
    second = lambda x, y: 4 + y * 2 + x
    return [
        first(own[0], own[1]),
        first(own[0], off[1]),
        second(own[0], own[1]),
        second(off[0], own[1]),
        first(off[0], own[1]),
        first(off[0], off[1]),
        second(own[0], off[1]),
        second(off[0], off[1]),
    ]


def reorder_rows(source, target, into_local):
    size = source.shape[0] // 8
    for slot, owner in enumerate(eighth_owners()):
        natural = pl.ds(pl.multiple_of(owner * size, size), size)
        local = pl.ds(slot * size, size)
        if into_local:
            target[local, :] = source[natural, :]
        else:
            target[natural, :] = source[local, :]


def forward_kernel(
    tokens, weights, gain_in, gain_q, gain_k, cosine, sine, wide_down,
    normed, raw, query, key, value, local, turned_down, attended, low_down, send_sem, recv_sem,
):
    low = jnp.bfloat16
    zone, side, row, core = place_here()
    at_home, away = side == core, side != core
    turn = Copies(send_sem, recv_sem).make(low_down, turned_down, device(zone, core, row, side))

    @pl.when(away)
    def _():
        cast_rows(wide_down, low_down)
        greet([device(zone, core, row, side)])
        turn.start()

    @pl.when(at_home)
    def _():
        cast_rows(wide_down, turned_down)

    total, heads = tokens.shape[0], query.shape[1] // HEAD
    block, wide = 256, 512

    def project(step, carry):
        rows = pl.ds(pl.multiple_of(step * wide, wide), wide)
        values = tokens[rows, :].astype(jnp.float32)
        normed[rows, :] = (values * inverse_rms(values) * gain_in[...]).astype(low)
        raw[rows, :] = dot(normed[rows, :], weights[...])
        turns = (cosine[rows, :], sine[rows, :])
        for head in range(heads):
            column = (head // 2) * 4 * HEAD + (head % 2) * HEAD
            values = raw[rows, pl.ds(column, HEAD)]
            values = turn_head(values * inverse_rms(values) * gain_q[...], *turns)
            query[rows, pl.ds(head * HEAD, HEAD)] = (values * (1.0 / math.sqrt(HEAD))).astype(low)
        for group in range(heads // 2):
            column = group * 4 * HEAD + 2 * HEAD
            here = pl.ds(group * HEAD, HEAD)
            values = raw[rows, pl.ds(column, HEAD)]
            values = turn_head(values * inverse_rms(values) * gain_k[...], *turns)
            key[rows, here] = values.astype(low)
            value[rows, here] = raw[rows, pl.ds(column + HEAD, HEAD)].astype(low)
        return carry

    lax.fori_loop(0, total // wide, project, 0)

    def attend(head, carry):
        mine = pl.ds(pl.multiple_of(head * HEAD, HEAD), HEAD)
        shared = pl.ds(pl.multiple_of(lax.div(head, 2) * HEAD, HEAD), HEAD)
        for start in range(0, total, SEQ):
            for first in range(0, SEQ, block):
                rows, keys = pl.ds(start + first, block), pl.ds(start, first + block)
                probs = softmax_block(query[rows, mine], key[keys, shared], first)
                attended[rows, mine] = dot(probs.astype(low), value[keys, shared]).astype(low)
        return carry

    lax.fori_loop(0, heads, attend, 0)
    reorder_rows(attended, local, True)

    @pl.when(away)
    def _():
        turn.wait_recv()
        turn.wait_send()


def attention(tokens, weights, gain_in, gain_q, gain_k, cosine, sine, down, number):
    total = tokens.shape[0]
    columns = weights.shape[1]
    low = jnp.bfloat16
    shape = lambda width, kind=low: jax.ShapeDtypeStruct((total, width), kind)
    vmem = pl.BlockSpec(memory_space=pltpu.VMEM)
    return pl.pallas_call(
        forward_kernel,
        out_shape=[
            shape(tokens.shape[1]),
            shape(columns, jnp.float32),
            shape(columns // 2),
            shape(columns // 4),
            shape(columns // 4),
            shape(columns // 2),
            jax.ShapeDtypeStruct(down.shape, low),
        ],
        in_specs=[vmem] * 8,
        out_specs=[vmem] * 7,
        scratch_shapes=[
            pltpu.VMEM((total, columns // 2), low),
            pltpu.VMEM(down.shape, low),
            pltpu.SemaphoreType.DMA((1,)),
            pltpu.SemaphoreType.DMA((1,)),
        ],
        compiler_params=pltpu.CompilerParams(
            collective_id=number, has_side_effects=True, vmem_limit_bytes=48 * 2**20
        ),
        cost_estimate=pl.CostEstimate(flops=10**10, bytes_accessed=2 * 10**7, transcendentals=0),
        name="attention",
    )(tokens, weights, gain_in, gain_q, gain_k, cosine, sine, down)


def backward_kernel(
    query, key, value, raw, grad_rows, gain_q, gain_k, cosine, sine,
    mixed, mixed_local, query_gain, key_gain, grad, key_sum, value_sum,
):
    low = jnp.bfloat16
    total, heads = query.shape[0], query.shape[1] // HEAD
    block = 256
    reorder_rows(grad_rows, grad, False)
    query_gain[...] = jnp.zeros_like(query_gain)
    key_gain[...] = jnp.zeros_like(key_gain)

    def head_norm_back(rows, column, gradient, gain, gain_grad):
        values = raw[rows, column]
        factor = inverse_rms(values)
        unit = values * factor
        turned = turn_back(gradient, cosine[rows, :], sine[rows, :])
        gain_grad[...] += jnp.sum(turned * unit, 0, keepdims=True)
        mixed[rows, column] = norm_back(turned * gain[...], unit, factor).astype(low)

    def one_group(group, carry):
        at = lambda offset: pl.ds(pl.multiple_of(group * 4 * HEAD + offset * HEAD, HEAD), HEAD)
        shared = pl.ds(pl.multiple_of(group * HEAD, HEAD), HEAD)
        key_sum[...] = jnp.zeros_like(key_sum)
        value_sum[...] = jnp.zeros_like(value_sum)
        for head in (0, 1):
            mine = pl.ds(pl.multiple_of((group * 2 + head) * HEAD, HEAD), HEAD)
            for start in range(0, total, SEQ):
                for first in range(0, SEQ, block):
                    rows, keys = pl.ds(start + first, block), pl.ds(start, first + block)
                    query_part, grad_part = query[rows, mine], grad[rows, mine]
                    probs = softmax_block(query_part, key[keys, shared], first)
                    weighed = probs * dot(grad_part, value[keys, shared], 1, 1)
                    scores = weighed - probs * jnp.sum(weighed, -1, keepdims=True)
                    scores = scores.astype(low)
                    grad_query = dot(scores, key[keys, shared]) * (1.0 / math.sqrt(HEAD))
                    head_norm_back(rows, at(head), grad_query, gain_q, query_gain)
                    key_sum[keys, :] += dot(scores, query_part, 0, 0)
                    value_sum[keys, :] += dot(probs.astype(low), grad_part, 0, 0)
        for first in range(0, total, block):
            rows = pl.ds(first, block)
            head_norm_back(rows, at(2), key_sum[rows, :], gain_k, key_gain)
            mixed[rows, at(3)] = value_sum[rows, :].astype(low)
        return carry

    lax.fori_loop(0, heads // 2, one_group, 0)
    reorder_rows(mixed, mixed_local, True)


def attention_back(query, key, value, raw, grad_rows, gain_q, gain_k, cosine, sine):
    total, columns = raw.shape
    low = jnp.bfloat16
    vmem = pl.BlockSpec(memory_space=pltpu.VMEM)
    return pl.pallas_call(
        backward_kernel,
        out_shape=[
            jax.ShapeDtypeStruct((total, columns), low),
            jax.ShapeDtypeStruct((total, columns), low),
            jax.ShapeDtypeStruct((1, HEAD), jnp.float32),
            jax.ShapeDtypeStruct((1, HEAD), jnp.float32),
        ],
        in_specs=[vmem] * 9,
        out_specs=[vmem] * 4,
        scratch_shapes=[
            pltpu.VMEM(grad_rows.shape, low),
            pltpu.VMEM((total, HEAD), jnp.float32),
            pltpu.VMEM((total, HEAD), jnp.float32),
        ],
        compiler_params=pltpu.CompilerParams(vmem_limit_bytes=48 * 2**20),
        cost_estimate=pl.CostEstimate(flops=10**10, bytes_accessed=2 * 10**7, transcendentals=0),
        name="attention_back",
    )(query, key, value, raw, grad_rows, gain_q, gain_k, cosine, sine)


def feed_kernel(plan, rows, own_grad, got_grad, gate_up, up_part, down, active, grads, out_grad):
    low = jnp.bfloat16
    block = 512
    tile = down.shape[1]
    step = pl.program_id(0)
    gate_at = pl.ds(pl.multiple_of(step * tile, tile), tile)
    up_at = pl.ds(pl.multiple_of(grads.shape[1] // 2 + step * tile, tile), tile)
    _, side, _, core = place_here()

    def lay_down(source):
        natural, blocks = block_columns(plan, source.shape[1])
        eighth = source.shape[0] // 8
        for slot, owner in enumerate(eighth_owners()):

            def some(start, count, slot=slot, owner=owner):
                here = pl.ds(pl.multiple_of(owner * eighth + start, 32), count)
                there = pl.ds(slot * eighth + start, count)
                for a, b in zip(natural, blocks):
                    out_grad[there, b] = source[here, a]

            for_rows(eighth, some)

    @pl.when((step == 0) & (side == core))
    def _():
        lay_down(own_grad)

    @pl.when((step == 0) & (side != core))
    def _():
        lay_down(got_grad)

    def one(block_at, carry):
        here = pl.ds(pl.multiple_of(block_at * block, block), block)
        gate = dot(rows[here, :], gate_up[...])
        up = dot(rows[here, :], up_part[...])
        grad = dot(out_grad[here, :], down[...])
        sigmoid = jax.nn.sigmoid(gate)
        silu = gate * sigmoid
        active[here, :] = (silu * up).astype(low)
        grads[here, gate_at] = (grad * up * sigmoid * (1.0 + gate * (1.0 - sigmoid))).astype(low)
        grads[here, up_at] = (grad * silu).astype(low)
        return carry

    lax.fori_loop(0, rows.shape[0] // block, one, 0)


def feed_forward(plan, rows, own_grad, got_grad, gate_up, down, tile):
    total, width = rows.shape
    units = down.shape[1]
    low = jnp.bfloat16
    tiles = units // tile
    whole = pl.BlockSpec(memory_space=pltpu.VMEM)
    return pl.pallas_call(
        functools.partial(feed_kernel, plan),
        grid=(tiles,),
        out_shape=[
            jax.ShapeDtypeStruct((total, units), low),
            jax.ShapeDtypeStruct((total, 2 * units), low),
            jax.ShapeDtypeStruct((total, width), low),
        ],
        in_specs=[
            whole,
            whole,
            whole,
            pl.BlockSpec((width, tile), lambda step: (0, step)),
            pl.BlockSpec((width, tile), lambda step: (0, step + tiles)),
            pl.BlockSpec((width, tile), lambda step: (0, step)),
        ],
        out_specs=[
            pl.BlockSpec((total, tile), lambda step: (0, step)),
            whole,
            whole,
        ],
        compiler_params=pltpu.CompilerParams(vmem_limit_bytes=56 * 2**20),
        cost_estimate=pl.CostEstimate(
            flops=6 * total * width * units, bytes_accessed=4 * 10**7, transcendentals=total * units
        ),
        name="feed_forward",
    )(rows, own_grad, got_grad, gate_up, gate_up, down)


class Plan:
    def __init__(self, mesh):
        self.total = mesh.shape["dp"]
        self.zones = self.total // 2
        self.tensor = mesh.shape["tensor"]
        self.flips = [k ^ (k >> 1) for k in range(self.zones)]

    def place(self):
        self.index = lax.axis_index("dp")
        self.zone = self.index // 2
        self.side = self.index % 2
        self.row = lax.axis_index("tensor") // 2
        self.core = lax.axis_index("tensor") % 2
        self.home = self.side == self.core

    def move(self, value, target):
        pairs = []
        for d in range(self.total):
            for t in range(self.tensor):
                to = target(d // 2, d % 2, t // 2, t % 2)
                if to is not None:
                    zone, side, row, core = to
                    pairs.append((d * self.tensor + t, (zone * 2 + side) * self.tensor + row * 2 + core))
        return lax.ppermute(value, ("dp", "tensor"), pairs)

    def turn(self, value):
        got = self.move(value, lambda z, y, x, c: (z, c, x, y) if y != c else None)
        return jnp.where(self.home, value, got)

    def zone_flip(self, value, bit):
        return self.move(value, lambda z, y, x, c: (z ^ bit, y, x, c))

    def core_swap(self, value):
        return self.move(value, lambda z, y, x, c: (z, y, x, 1 - c))

    def side_swap(self, value):
        return self.move(value, lambda z, y, x, c: (z, 1 - y, x, c))

    def row_swap(self, value):
        return self.move(value, lambda z, y, x, c: (z, y, 1 - x, c))

    def to_local(self, value, axis):
        width = value.shape[axis] // self.total
        parts = []
        for core in (self.core, 1 - self.core):
            for slot in range(self.zones):
                owner = (self.zone ^ self.flips[slot]) * 2 + core
                parts.append(lax.dynamic_slice_in_dim(value, owner * width, width, axis))
        return jnp.concatenate(parts, axis)

    def to_natural(self, value, axis, core=None):
        core = self.core if core is None else core
        width = value.shape[axis] // self.total
        parts = []
        for block in range(self.total):
            slot = flip = (block // 2) ^ self.zone
            for bits in range(1, self.zones.bit_length()):
                slot = slot ^ (flip >> bits)
            slot = slot + jnp.where(block % 2 == core, 0, self.zones)
            parts.append(lax.dynamic_slice_in_dim(value, slot * width, width, axis))
        return jnp.concatenate(parts, axis)

    def row_owners(self):
        own, off = (self.row, self.side), (1 - self.row, 1 - self.side)
        first = lambda x, y: x * 2 + y
        second = lambda x, y: 4 + y * 2 + x
        return [
            first(own[0], own[1]),
            first(own[0], off[1]),
            second(own[0], own[1]),
            second(off[0], own[1]),
            first(off[0], own[1]),
            first(off[0], off[1]),
            second(own[0], off[1]),
            second(off[0], off[1]),
        ]

    def rows_local(self, value, slots=range(8)):
        size = value.shape[0] // 8
        owners = self.row_owners()
        return jnp.concatenate(
            [lax.dynamic_slice_in_dim(value, owners[slot] * size, size, 0) for slot in slots], 0
        )

    def rows_natural(self, value, order=range(8)):
        size = value.shape[0] // 8
        place = [list(order).index(slot) for slot in range(8)]
        parts = []
        for piece in range(8):
            x, y = (piece // 2, piece % 2) if piece < 4 else (piece % 2, (piece - 4) // 2)
            slots = (0, 1, 4, 5) if piece < 4 else (2, 6, 3, 7)
            same_x, same_y = x == self.row, y == self.side
            slot = jnp.where(
                same_x,
                jnp.where(same_y, place[slots[0]], place[slots[1]]),
                jnp.where(same_y, place[slots[2]], place[slots[3]]),
            )
            parts.append(lax.dynamic_slice_in_dim(value, slot * size, size, 0))
        return jnp.concatenate(parts, 0)

    def from_zones(self, shard):
        return [self.zone_flip(shard, flip) for flip in self.flips[1:]]

    def to_zones(self, parts, slots):
        return [self.zone_flip(parts[slot], self.flips[slot]) for slot in slots]

    def middle_swap(self, pair):
        return self.move(pair, lambda z, y, x, c: (z ^ 3, y, x, c) if z in (1, 2) else None)

    def inward(self, part):
        return self.move(part, lambda z, y, x, c: (z ^ 1, y, x, c) if z in (0, 3) else None)

    def pass_outward(self, pair):
        return self.move(pair, lambda z, y, x, c: (z ^ 1, y, x, c) if z in (1, 2) else None)

    def far_pair(self, middle, passed):
        inner = (self.zone == 1) | (self.zone == 2)
        return jnp.where(inner, middle, passed[::-1])

    def first_swap(self, send):
        half = send.shape[0] // 2
        return self.row_swap(send[:half]), self.side_swap(send[half:])

    def second_swap(self, keep, got):
        quarter = keep.shape[0] // 4
        row_part = keep[: 2 * quarter] + got[0].astype(jnp.float32)
        side_part = keep[2 * quarter :] + got[1].astype(jnp.float32)
        own = jnp.concatenate([row_part[:quarter], side_part[:quarter]], 0)
        return own, (
            self.side_swap(row_part[quarter:].astype(jnp.bfloat16)),
            self.row_swap(side_part[quarter:].astype(jnp.bfloat16)),
        )

    def spread_first(self, own):
        half = own.shape[0] // 2
        return (self.side_swap(own[:half]), self.row_swap(own[half:]))

    def spread_second(self, own, got):
        half = own.shape[0] // 2
        row_part = jnp.concatenate([own[:half], got[0]], 0)
        side_part = jnp.concatenate([own[half:], got[1]], 0)
        return row_part, side_part, self.row_swap(row_part), self.side_swap(side_part)

    def send_home(self, own):
        to_home = lambda z, y, x, c: (z, c, x, c) if y != c else None
        return jnp.concatenate([own, self.move(own, to_home)], 0)

    def row_home(self, part):
        return self.move(part, lambda z, y, x, c: (z, y, 1 - x, c) if y == c else None)

    def share_home(self, part, other):
        full = jnp.concatenate([part, other], 0)
        full = self.to_natural(self.rows_natural(full, (0, 2, 1, 6, 4, 3, 5, 7)), 1)
        got = self.move(full, lambda z, y, x, c: (z, y, x, 1 - c) if y == c else None)
        return full, got

    def turned(self, own, got):
        return jnp.where(self.home, own, got)

    def sum_everywhere(self, value):
        value = value + self.row_swap(value)
        value = value + self.side_swap(value)
        value = value + self.core_swap(value)
        bit = 1
        while bit < self.zones:
            value = value + self.zone_flip(value, bit)
            bit *= 2
        return value


def shards(
    plan,
    tokens,
    positions,
    out_grad,
    qkv_weight,
    qkv_first,
    qkv_second,
    out_weight,
    out_first,
    out_second,
    gate_up,
    gate_up_first,
    gate_up_second,
    down_weight,
    down_first,
    down_second,
    gains,
    gains_first,
    gains_second,
):
    plan.place()
    low = jnp.bfloat16
    tok_rows, model_width = tokens.shape
    groups = qkv_weight.shape[1]
    head_size = qkv_weight.shape[3]
    shard_rows = qkv_weight.shape[0]
    seq_count = tok_rows // SEQ
    mixed_cols = groups * 4 * head_size
    near_cols = model_width // 2
    kept = tok_rows // 2
    gain_count = gains.shape[0]

    tree = plan.zones == 4
    slots = range(1, plan.zones)

    def column_parts(value):
        return value.reshape((plan.zones, -1) + value.shape[1:])

    units = gate_up.shape[2]
    plan.ordered = (model_width // plan.total) % 128 == 0
    gain_rows = 16
    gain_block = jnp.pad(gains.astype(low), (0, gain_rows * 128 - gain_count)).reshape(gain_rows, 128)
    tile = min(units, 256)
    angle_at = positions.astype(jnp.float32).reshape(-1, 128)
    both_qkv, both_gains, turned_gate, turned_out, tokens, angle_at, partner_gate = opening(
        plan,
        qkv_weight.reshape(shard_rows, mixed_cols),
        gain_block,
        gate_up,
        out_weight,
        tokens,
        angle_at,
        3,
    )
    positions = angle_at.reshape(-1)
    turned_out, turned_gate, tokens, positions, both_qkv, both_gains, out_grad = fence(
        turned_out, turned_gate, tokens, positions, both_qkv, both_gains, out_grad
    )

    got_grad = plan.move(out_grad, lambda z, y, x, c: (z, c, x, y) if y != c else None)
    half_rows = shard_rows // 2
    if tree:
        out_at = turned_out.size // half_rows
        both = [turned_out.reshape(half_rows, out_at), turned_gate[half_rows:]]
        both = plan.zone_flip(jnp.concatenate(both, 1), 1)
        zone_out = [both[:, :out_at].reshape(turned_out.shape)]
        zone_out += [plan.zone_flip(turned_out, flip) for flip in plan.flips[2:]]
        partner_rest = both[:, out_at:]
        landed = plan.middle_swap(turned_gate[:half_rows])
    else:
        zone_out = plan.from_zones(turned_out)
        partner_rest = landed = partner_gate
        partner_gate = plan.from_zones(turned_gate)
    if not plan.ordered:
        tokens = plan.to_local(tokens, 1)
    cosine, sine_table = rotary(positions, head_size)
    signed_sine = jnp.concatenate(
        [-sine_table[:, : head_size // 2], sine_table[:, head_size // 2 :]], 1
    )
    full_qkv = both_qkv.reshape(model_width, mixed_cols)
    gain_slots = both_gains.reshape(plan.total, -1)[:, :gain_count]
    gain_all = plan.to_natural(gain_slots.reshape(-1), 0).astype(jnp.float32)
    gain_in = plan.to_local(gain_all[:model_width], 0)[None]
    gain_post = plan.to_local(gain_all[model_width : 2 * model_width], 0)[None]
    gain_q = gain_all[2 * model_width : 2 * model_width + head_size][None]
    gain_k = gain_all[2 * model_width + head_size :][None]
    normed, raw, query, key_rot, values_low, attended, turned_down = attention(
        tokens, full_qkv, gain_in, gain_q, gain_k, cosine, signed_sine, down_weight, 4
    )
    attended, zone_out, turned_out, turned_down, turned_gate, partner_gate, partner_rest, landed = fence(
        attended, zone_out, turned_out, turned_down, turned_gate, partner_gate, partner_rest, landed
    )

    near_out = jnp.concatenate([turned_out] + zone_out, 0)
    far_out = plan.core_swap(near_out)
    own_tokens = plan.rows_local(tokens, (0, 2))
    near_out, far_out, own_tokens = fence(near_out, far_out, own_tokens)

    full_out = jnp.concatenate([near_out, far_out], 0)
    branch_terms = contract_cols(attended, full_out).astype(low)
    if tree:
        pairs = [(turned_gate, jnp.concatenate([partner_gate, partner_rest], 0)), (turned_down,)]
    else:
        pairs = [(turned_gate, partner_gate), (turned_down, plan.from_zones(turned_down))]
    normed_rows, hidden, *gathered = sum_rows(
        spread_kernel,
        hidden_rows,
        branch_terms,
        [own_tokens, gain_post],
        [jax.ShapeDtypeStruct((tok_rows // 4, model_width), jnp.float32)],
        0,
        [PairTree(pairs, (2, 2), landed)] if tree else [],
    )
    if not tree:
        near = [jnp.concatenate([own] + rest, 0) for own, rest in pairs]
        gathered = [jnp.concatenate([part, plan.core_swap(part)], 0) for part in near]
    full_gate = gathered[0].reshape(model_width, 2 * units)
    full_down = gathered[1].reshape(model_width, units)
    normed_rows, hidden, full_gate, full_down, got_grad = fence(
        normed_rows, hidden, full_gate, full_down, got_grad
    )

    def zone_parts(near, got):
        both = (near + got.astype(jnp.float32)).astype(low)
        return both.reshape((plan.zones, -1) + both.shape[1:])

    def zone_total(parts, *arrived):
        total = parts[0].astype(jnp.float32)
        for part in sum([list(group) for group in arrived], []):
            total = total + part.astype(jnp.float32)
        return total.astype(low)

    active, grad_both, out_grad = feed_forward(
        plan, normed_rows, out_grad, got_grad, full_gate, full_down, tile
    )
    if not plan.ordered:
        out_grad = plan.to_local(out_grad, 1)
    down_far = contract_rows(out_grad[:, near_cols:], active).astype(low)
    down_far, active, grad_both, out_grad = fence(down_far, active, grad_both, out_grad)

    down_got = plan.core_swap(down_far)
    gate_far = contract_rows(normed_rows[:, near_cols:], grad_both).astype(low)
    down_parts = zone_parts(contract_rows(out_grad[:, :near_cols], active), down_got)
    down_parts, gate_far, grad_both = fence(down_parts, gate_far, grad_both)

    gate_got = plan.core_swap(gate_far)
    if tree:
        inner_terms = plan.inward(down_parts[3])
    else:
        inner_terms = plan.to_zones(down_parts, slots)
    post_terms = contract_cols(grad_both, full_gate).astype(low)
    post_terms, gate_got, inner_terms, down_parts = fence(
        post_terms, gate_got, inner_terms, down_parts
    )

    down_sums = jnp.stack([inner_terms, plan.inward(down_parts[2])]) if tree else inner_terms
    gate_parts = zone_parts(contract_rows(normed_rows[:, :near_cols], grad_both), gate_got)
    if tree:
        down_pair = (down_parts[2:].astype(jnp.float32) + down_sums.astype(jnp.float32)).astype(low)
    else:
        down_pair = down_parts
    post_terms, gate_parts, down_parts, down_pair = fence(
        post_terms, gate_parts, down_parts, down_pair
    )

    if tree:
        down_sums = plan.middle_swap(down_pair)
        up_parts = gate_parts[:, :, units:]
        up_sums = [plan.inward(up_parts[3]), plan.inward(up_parts[2])]
    else:
        up_parts, up_sums = gate_parts, plan.to_zones(gate_parts, slots)
    eighth = tok_rows // 8
    own_grad = jnp.concatenate([out_grad[:eighth], out_grad[2 * eighth : 3 * eighth]], 0)
    branch_rows, grad_hidden, post_gain_grad, mlp_terms, *gate_own = sum_rows(
        spread_kernel,
        grad_hidden_rows,
        post_terms,
        [hidden, own_grad, gain_post],
        [
            jax.ShapeDtypeStruct((tok_rows // 4, model_width), jnp.float32),
            jax.ShapeDtypeStruct((1, model_width), jnp.float32),
        ],
        1,
        [SideDot(active, full_down)] + ([PairScatter(gate_parts[:, :, :units], 4)] if tree else []),
    )
    branch_rows, grad_hidden, post_gain_grad, mlp_terms, down_sums, up_sums, down_parts, up_parts, gate_own = fence(
        branch_rows,
        grad_hidden,
        post_gain_grad,
        mlp_terms,
        down_sums,
        up_sums,
        down_parts,
        up_parts,
        gate_own,
    )

    def plus(left, right):
        return (left.astype(jnp.float32) + right.astype(jnp.float32)).astype(low)

    mlp_got = plan.first_swap(mlp_terms[kept:])
    if tree:
        up_first = [plan.middle_swap(plus(up_parts[2 + slot], up_sums[slot])) for slot in (0, 1)]
        down_own = [plus(down_parts[0], down_sums[0]), plus(down_parts[1], down_sums[1])]
        both = plan.zone_flip(jnp.stack([gate_own[0][1], down_own[1]]), 1)
        gate_last, down_last = both[0], [both[1]]
    else:
        up_first = gate_last = up_sums
        down_own, down_last = down_parts, down_sums
    grad_att = jnp.dot(branch_rows, full_out, preferred_element_type=jnp.float32).astype(low)
    grad_mixed, mixed_rows, query_gain_grad, key_gain_grad = attention_back(
        query, key_rot, values_low, raw, grad_att, gain_q, gain_k, cosine, signed_sine
    )
    gain_terms = jnp.concatenate(
        [plan.to_natural(post_gain_grad, 1), query_gain_grad, key_gain_grad], 1
    )
    grad_mixed, mixed_rows, gain_terms, normed, branch_rows, mlp_got, up_first, gate_last, down_last = fence(
        grad_mixed, mixed_rows, gain_terms, normed, branch_rows, mlp_got, up_first, gate_last, down_last
    )

    mlp_own, mlp_last = plan.second_swap(mlp_terms[:kept].astype(jnp.float32), mlp_got)
    if tree:
        up_own = [plus(up_parts[slot], up_first[slot]) for slot in (0, 1)]
        up_last = plan.zone_flip(up_own[1], 1)
    out_far = contract_rows(branch_rows[:, near_cols:], attended).astype(low)
    out_got = plan.core_swap(out_far)
    qkv_far = contract_rows(normed[:, near_cols:], grad_mixed).astype(low)
    qkv_got = plan.core_swap(qkv_far)
    normed_terms = contract_cols(mixed_rows, full_qkv).astype(low)
    if tree:
        total_gate = [zone_total(gate_own[0], [gate_last]), zone_total(up_own, [up_last])]
    else:
        total_gate = zone_total(up_parts, up_sums)
        total_gate = [total_gate[:, :units], total_gate[:, units:]]
    total_down = zone_total(down_own, down_last)
    mlp_own, mlp_last, out_got, qkv_got, normed_terms, total_gate, total_down, grad_mixed = fence(
        mlp_own, mlp_last, out_got, qkv_got, normed_terms, total_gate, total_down, grad_mixed
    )

    block_own = (hidden + mlp_own + jnp.concatenate(mlp_last, 0).astype(jnp.float32)).astype(low)
    block_home = plan.send_home(block_own)
    out_parts = zone_parts(contract_rows(branch_rows[:, :near_cols], attended), out_got)
    qkv_parts = zone_parts(contract_rows(normed[:, :near_cols], grad_mixed), qkv_got)
    block_home, out_parts, qkv_parts, normed_terms = fence(
        block_home, out_parts, qkv_parts, normed_terms
    )

    gain_sum = GainSum(plan, gain_terms.shape[1], model_width) if plan.ordered else None
    input_full, input_gain_grad, *rest = sum_rows(
        home_kernel,
        grad_input_rows,
        normed_terms,
        [own_tokens, grad_hidden, gain_in] + ([gain_terms] if plan.ordered else []),
        [jax.ShapeDtypeStruct((1, model_width), jnp.float32)],
        2,
        [ZoneBlocks(plan, qkv_parts, slots), ZoneBlocks(plan, out_parts, slots, 1)],
        gain_sum,
    )
    if plan.ordered:
        summed_gains, qkv_sent, out_sent = rest
    else:
        qkv_sent, out_sent = rest
        summed_gains = plan.sum_everywhere(
            jnp.concatenate([plan.to_natural(input_gain_grad, 1), gain_terms], 1)
        )
    input_full, summed_gains, qkv_sent, out_sent, total_gate, total_down = fence(
        input_full, summed_gains, qkv_sent, out_sent, total_gate, total_down
    )

    block_row = plan.row_home(block_home)
    summed_both = plan.turn(
        jnp.concatenate([zone_total(qkv_parts, qkv_sent), zone_total(out_parts, out_sent)], 1)
    ).astype(jnp.float32)
    summed_gate = plan.turn(jnp.stack(total_gate))
    summed_down = plan.turn(total_down)
    block_full, block_got = plan.share_home(block_home, block_row)
    block_out = jnp.where(plan.home, block_full, block_got)
    summed_qkv = summed_both[:, :mixed_cols].reshape(qkv_weight.shape)
    summed_out = summed_both[:, mixed_cols:]
    summed_gate = summed_gate.astype(jnp.float32)
    summed_down = summed_down.astype(jnp.float32)
    summed_gains = lax.dynamic_slice_in_dim(summed_gains[0], plan.index * gain_count, gain_count, 0)
    input_rows = plan.to_natural(input_full, 1, plan.side).astype(jnp.float32)

    qkv_moment, qkv_square, qkv_updated = adamw(
        qkv_weight, summed_qkv, qkv_first, qkv_second, RATE_QKV, DECAY_RATE
    )
    out_moment, out_square, out_updated = adamw(
        out_weight, summed_out, out_first, out_second, RATE_OUT, DECAY_RATE
    )
    gate_moment, gate_square, gate_updated = adamw(
        gate_up, summed_gate, gate_up_first, gate_up_second, RATE_GATE, DECAY_RATE
    )
    down_moment, down_square, down_updated = adamw(
        down_weight, summed_down, down_first, down_second, RATE_DOWN, DECAY_RATE
    )
    gain_moment, gain_square, gain_updated = adamw(
        gains, summed_gains, gains_first, gains_second, RATE_GAIN, 0.0
    )
    return (
        block_out,
        input_rows,
        qkv_moment,
        qkv_square,
        qkv_updated,
        out_moment,
        out_square,
        out_updated,
        gate_moment,
        gate_square,
        gate_updated,
        down_moment,
        down_square,
        down_updated,
        gain_moment,
        gain_square,
        gain_updated,
    )


def solution(mesh):
    plan = Plan(mesh)
    placed = (
        P("dp", None),
        P("dp"),
        P("dp", None),
        P("dp", "tensor", None, None),
        P("dp", "tensor", None, None),
        P("dp", "tensor", None, None),
        P("dp", "tensor"),
        P("dp", "tensor"),
        P("dp", "tensor"),
        P(None, "dp", "tensor"),
        P(None, "dp", "tensor"),
        P(None, "dp", "tensor"),
        P("dp", "tensor"),
        P("dp", "tensor"),
        P("dp", "tensor"),
        P("dp"),
        P("dp"),
        P("dp"),
    )
    return jax.shard_map(
        functools.partial(shards, plan),
        mesh=mesh,
        in_specs=placed,
        out_specs=(
            P("dp", None),
            P("dp", None),
            P("dp", "tensor", None, None),
            P("dp", "tensor", None, None),
            P("dp", "tensor", None, None),
            P("dp", "tensor"),
            P("dp", "tensor"),
            P("dp", "tensor"),
            P(None, "dp", "tensor"),
            P(None, "dp", "tensor"),
            P(None, "dp", "tensor"),
            P("dp", "tensor"),
            P("dp", "tensor"),
            P("dp", "tensor"),
            P("dp"),
            P("dp"),
            P("dp"),
        ),
        check_vma=False,
    )
```

```python
import functools
import math

import jax
import jax.numpy as jnp
from jax import lax
from jax.experimental import pallas as pl
from jax.experimental.pallas import tpu as pltpu
from jax.sharding import PartitionSpec as P

SEQ = 1024
STEP = 10


EPS_NORM = 1e-06
THETA = 1000000.0
BETA_ONE = 0.9
BETA_TWO = 0.95
ADAM_EPS = 1e-08
DECAY_RATE = 0.1
RATE_QKV = 0.05
RATE_OUT = 0.3
RATE_GATE = 0.05
RATE_DOWN = 0.03
RATE_GAIN = 1.0


def rotary(positions, head_size):
    freq_index = jnp.arange(head_size // 2, dtype=jnp.float32)
    inverse = jnp.exp(freq_index * (-2.0 * math.log(THETA) / head_size))
    angles = positions.astype(jnp.float32)[:, None] * inverse[None, :]
    cosine = jnp.cos(angles)
    sine_table = jnp.sin(angles)
    return (jnp.concatenate([cosine, cosine], -1), jnp.concatenate([sine_table, sine_table], -1))


def rotate(values, cosine, sine_table):
    half_size = values.shape[-1] // 2
    turned = jnp.concatenate([-values[..., half_size:], values[..., :half_size]], -1)
    return values * cosine[:, None, :] + turned * sine_table[:, None, :]


def unrotate(gradient, cosine, sine_table):
    half_size = gradient.shape[-1] // 2
    turned = gradient * sine_table[:, None, :]
    rotated_back = jnp.concatenate([turned[..., half_size:], -turned[..., :half_size]], -1)
    return gradient * cosine[:, None, :] + rotated_back


def norm_back(grad_unit, unit_vals, factor):
    return factor * (grad_unit - unit_vals * jnp.mean(grad_unit * unit_vals, -1, keepdims=True))


def contract_rows(left, right):
    return lax.dot_general(
        left, right, (((0,), (0,)), ((), ())), preferred_element_type=jnp.float32
    )


def contract_cols(left, right):
    return lax.dot_general(
        left, right, (((1,), (1,)), ((), ())), preferred_element_type=jnp.float32
    )


def block_scores(query_part, key_part, first_row, block_rows, last_row):
    scores = jnp.einsum(
        "nqkgd,nskd->nkgqs", query_part, key_part, preferred_element_type=jnp.float32
    )
    causal = (first_row + jnp.arange(block_rows))[:, None] >= jnp.arange(last_row)[None, :]
    return jnp.where(causal, scores, -1000000000.0)


def attention_forward(query, key_rot, values_low, seq_len):
    block_rows = min(512, seq_len)
    outputs = []
    log_sums = []
    for first_row in range(0, seq_len, block_rows):
        last_row = first_row + block_rows
        query_part = query[:, first_row:last_row]
        scores = block_scores(query_part, key_rot[:, :last_row], first_row, block_rows, last_row)
        row_max = jnp.max(scores, -1, keepdims=True)
        exponent = jnp.exp(scores - row_max)
        row_total = jnp.sum(exponent, -1, keepdims=True)
        probs_low = (exponent / row_total).astype(jnp.bfloat16)
        outputs.append(
            jnp.einsum(
                "nkgqs,nskd->nqkgd",
                probs_low,
                values_low[:, :last_row],
                preferred_element_type=jnp.float32,
            )
        )
        log_sums.append(row_max + jnp.log(row_total))
    return (jnp.concatenate(outputs, 1), log_sums)


def attention_backward(query, key_rot, values_low, grad_att, log_sums, seq_len):
    block_rows = min(512, seq_len)
    query_grads = []
    key_grad = jnp.zeros(key_rot.shape, jnp.float32)
    value_grad = jnp.zeros(values_low.shape, jnp.float32)
    for block_index, first_row in enumerate(range(0, seq_len, block_rows)):
        last_row = first_row + block_rows
        query_part = query[:, first_row:last_row]
        grad_part = grad_att[:, first_row:last_row]
        key_part = key_rot[:, :last_row]
        value_part = values_low[:, :last_row]
        scores = block_scores(query_part, key_part, first_row, block_rows, last_row)
        probs = jnp.exp(scores - log_sums[block_index])
        probs_low = probs.astype(jnp.bfloat16)
        grad_probs = jnp.einsum(
            "nqkgd,nskd->nkgqs", grad_part, value_part, preferred_element_type=jnp.float32
        )
        grad_scores = (
            probs * (grad_probs - jnp.sum(probs * grad_probs, -1, keepdims=True))
        ).astype(jnp.bfloat16)
        query_grads.append(
            jnp.einsum(
                "nkgqs,nskd->nqkgd", grad_scores, key_part, preferred_element_type=jnp.float32
            )
        )
        padding = ((0, 0), (0, seq_len - last_row), (0, 0), (0, 0))
        key_grad = key_grad + jnp.pad(
            jnp.einsum(
                "nkgqs,nqkgd->nskd", grad_scores, query_part, preferred_element_type=jnp.float32
            ),
            padding,
        )
        value_grad = value_grad + jnp.pad(
            jnp.einsum(
                "nkgqs,nqkgd->nskd", probs_low, grad_part, preferred_element_type=jnp.float32
            ),
            padding,
        )
    return (jnp.concatenate(query_grads, 1), key_grad, value_grad)


def adamw(weight, gradient, moment, second, step_rate, decay_rate):
    moment = BETA_ONE * moment + (1.0 - BETA_ONE) * gradient
    second = BETA_TWO * second + (1.0 - BETA_TWO) * gradient * gradient
    first_hat = moment / (1.0 - BETA_ONE**STEP)
    second_hat = second / (1.0 - BETA_TWO**STEP)
    weight = weight - step_rate * (
        first_hat / (jnp.sqrt(second_hat) + ADAM_EPS) + decay_rate * weight
    )
    return (moment, second, weight)


def fence(*values):
    return lax.optimization_barrier(values)


MESH = pl.DeviceIdType.MESH
HEAD = 128
AHEAD = 2


def place_here():
    index, place = lax.axis_index("dp"), lax.axis_index("tensor")
    return lax.div(index, 2), lax.rem(index, 2), lax.div(place, 2), lax.rem(place, 2)


def device(zone, side, row, core):
    return (zone * 2 + side, row * 2 + core)


def flipped(zone, flip):
    bit = 1
    while bit <= flip:
        if flip & bit:
            zone = zone + bit - 2 * bit * lax.rem(lax.div(zone, bit), 2)
        bit *= 2
    return zone


def greet(devices, amount=None):
    barrier = pltpu.get_barrier_semaphore()
    for peer in devices:
        pl.semaphore_signal(barrier, inc=1, device_id=peer, device_id_type=MESH)
    pl.semaphore_wait(barrier, len(devices) if amount is None else amount)


def for_rows(count, body):
    step = 32

    def one(block, carry):
        body(pl.multiple_of(block * step, step), step)
        return carry

    lax.fori_loop(0, count // step, one, 0)


class Copies:
    def __init__(self, send_sems, recv_sems):
        self.send_sems, self.recv_sems = send_sems, recv_sems
        self.number = 0

    def make(self, source, target, peer):
        number, self.number = self.number, self.number + 1
        return pltpu.make_async_remote_copy(
            src_ref=source,
            dst_ref=target,
            send_sem=self.send_sems.at[number],
            recv_sem=self.recv_sems.at[number],
            device_id=peer,
            device_id_type=MESH,
        )

    def start(self, source, target, peer):
        copy = self.make(source, target, peer)
        copy.start()
        return copy


class GainSum:
    def __init__(self, plan, rest, width):
        self.plan, self.width = plan, width
        self.total = width + rest
        self.scratch = [
            pltpu.VMEM((8, 1, self.total), jnp.float32),
            pltpu.VMEM((plan.zones, 1, self.total), jnp.float32),
        ]
        self.output = jax.ShapeDtypeStruct((1, self.total), jnp.float32)
        self.count = 7 + plan.zones - 1

    def plane_peers(self, zone, side, row, core):
        steps = [(s, r, c) for s in range(2) for r in range(2) for c in range(2)][1:]
        turn = lambda value, step: 1 - value if step else value
        return [device(zone, turn(side, s), turn(row, r), turn(core, c)) for s, r, c in steps]

    def zone_peers(self, zone, side, row, core):
        return {flip: device(flipped(zone, flip), side, row, core) for flip in self.plan.flips[1:]}

    def start(self, copies, rest, blocks, plane_sums, zone_sums):
        zone, side, row, core = place_here()
        plan = self.plan
        size = self.width // plan.total
        self.copies, self.plane_sums, self.zone_sums, self.zone = copies, plane_sums, zone_sums, zone
        here = side * 4 + row * 2 + core
        plane_sums[here, :, pl.ds(self.width, self.total - self.width)] = rest[...]
        for slot in range(plan.total):
            owner = flipped(zone, plan.flips[slot % plan.zones]) * 2
            owner = owner + (core if slot < plan.zones else 1 - core)
            spot = pl.ds(pl.multiple_of(owner * size, size), size)
            plane_sums[here, :, spot] = blocks[:, pl.ds(slot * size, size)]
        self.plane = [
            copies.start(plane_sums.at[here], plane_sums.at[here], peer)
            for peer in self.plane_peers(zone, side, row, core)
        ]

    def middle(self):
        for copy in self.plane:
            copy.wait_recv()
        total = self.plane_sums[0]
        for place in range(1, 8):
            total = total + self.plane_sums[place]
        self.zone_sums[self.zone] = total
        zone, side, row, core = place_here()
        self.across = [
            self.copies.start(self.zone_sums.at[self.zone], self.zone_sums.at[self.zone], peer)
            for peer in self.zone_peers(zone, side, row, core).values()
        ]

    def finish(self, out):
        for copy in self.across:
            copy.wait_recv()
        total = self.zone_sums[0]
        for place in range(1, self.plan.zones):
            total = total + self.zone_sums[place]
        out[...] = total
        for copy in self.plane + self.across:
            copy.wait_send()


class ZoneBlocks:
    scratch = []

    def __init__(self, plan, source, slots, begin=0):
        self.flips, self.slots, self.sources, self.begin = plan.flips, list(slots), [source], begin
        self.outputs = [
            jax.ShapeDtypeStruct((len(self.slots),) + source.shape[1:], source.dtype)
        ]
        self.count, self.count_local = len(self.slots), 0
        self.in_hbm = False

    def peers(self, zone, side, row, core):
        return {
            self.flips[slot]: device(flipped(zone, self.flips[slot]), side, row, core)
            for slot in self.slots
        }

    def start(self, copies, local_sems, sources, targets, stages):
        zone, side, row, core = place_here()
        self.started = [
            copies.make(
                sources[0].at[slot],
                targets[0].at[number],
                device(flipped(zone, self.flips[slot]), side, row, core),
            )
            for number, slot in enumerate(self.slots)
        ]
        self.waiting = True
        if self.begin == 0:
            self.pump([0])

    def pump(self, steps):
        if self.waiting and self.begin in steps:
            self.waiting = False
            for copy in self.started:
                copy.start()

    def finish(self):
        for copy in self.started:
            copy.wait_send()
        for copy in self.started:
            copy.wait_recv()


def inner_zone(zone):
    return lax.rem(lax.div(zone + 1, 2), 2)


class SideDot:
    count, count_local, scratch, in_hbm = 0, 0, [], False

    def __init__(self, left, right):
        self.sources = [left, right]
        self.outputs = [jax.ShapeDtypeStruct((left.shape[0], right.shape[0]), jnp.bfloat16)]

    def peers(self, zone, side, row, core):
        return {}

    def some(self, first, last):
        left, right = self.refs
        size = 256

        def one(step, carry):
            here = pl.ds(pl.multiple_of(step * size, size), size)
            self.out[:, here] = dot(left[...], right[here, :], 1, 1).astype(jnp.bfloat16)
            return carry

        lax.fori_loop(first, last, one, 0)

    def start(self, copies, local_sems, sources, targets, stages):
        self.refs, self.out = sources, targets[0]
        self.steps = self.out.shape[1] // 256
        self.some(0, self.steps // 2)

    def pump(self, steps):
        if 0 in steps:
            self.some(self.steps // 2, self.steps)

    def finish(self):
        pass


class TurnRows:
    count, count_local, scratch, in_hbm = 4, 0, [], False

    def __init__(self, values):
        self.sources = [values]
        self.outputs = [jax.ShapeDtypeStruct(values.shape, values.dtype)]

    def peers(self, zone, side, row, core):
        return {}

    def start(self, copies, local_sems, sources, targets, stages):
        zone, side, row, core = place_here()
        values, target = sources[0], targets[0]
        partner, row_peer = device(zone, core, row, side), device(zone, side, 1 - row, core)
        size = values.shape[0] // 4
        spots = [pl.ds(pl.multiple_of((row * 2 + k) * size, size), size) for k in (0, 1)]
        self.away = side != core
        self.turn = [copies.make(values.at[spot], target.at[spot], partner) for spot in spots]
        self.onward = [copies.make(target.at[spot], target.at[spot], row_peer) for spot in spots]

    def pump(self, steps):
        pass

    def begin(self):
        @pl.when(self.away)
        def _():
            for copy in self.turn:
                copy.start()

    def pass_on(self, piece):
        @pl.when(self.away)
        def _():
            self.turn[piece].wait_recv()
            self.onward[piece].start()

    def finish(self):
        @pl.when(self.away)
        def _():
            for copy in self.onward:
                copy.wait_recv()
            for copy in self.turn + self.onward:
                copy.wait_send()


class PairTree:
    def __init__(self, pairs, pieces, landed):
        self.pairs = [len(pair) for pair in pairs]
        self.sources = [shard for pair in pairs for shard in pair] + [landed]
        self.pieces = pieces
        self.outputs = [
            jax.ShapeDtypeStruct((8,) + own.shape, own.dtype) for own, *_ in pairs
        ]
        self.count = 6 * sum(pieces) + 2 * len(pairs) + self.pairs.count(1)
        self.count_local = 2 * len(pairs) + 2 * sum(pieces)
        self.scratch = [pltpu.VMEM((2,) + own.shape, own.dtype) for own, *_ in pairs]
        self.scratch += [pltpu.VMEM(p[0].shape, p[0].dtype) for p in pairs if len(p) == 1]
        self.in_hbm = True

    def peers(self, zone, side, row, core):
        return {
            1: device(flipped(zone, 1), side, row, core),
            3: device(flipped(zone, 3), side, row, core),
            "core": device(zone, side, row, 1 - core),
        }

    def start(self, copies, local_sems, sources, targets, stages):
        zone, side, row, core = place_here()
        inner_peer = device(flipped(zone, 3), side, row, core)
        outer_peer = device(flipped(zone, 1), side, row, core)
        core_peer = device(zone, side, row, 1 - core)
        self.inner = inner_zone(zone) == 1
        self.outer = inner_zone(zone) == 0
        self.across, self.onward, self.late, self.place = [], [], [], []
        self.shared, self.kept, self.partners, self.later = [], [], [], []
        sem = 0
        sources, late_stages = list(sources), list(stages[len(targets) :])
        for weight, full in enumerate(targets):
            landing = stages[weight]
            pair = [sources.pop(0) for _ in range(self.pairs[weight])]
            if len(pair) == 1:
                pair.append(late_stages.pop(0))
                self.partners.append(copies.start(pair[0], pair[1], outer_peer))
            size = pair[0].shape[0] // self.pieces[weight]
            for piece in range(self.pieces[weight]):
                rows = pl.ds(piece * size, size)
                for slot in (0, 1):
                    here = landing.at[slot, rows]
                    first = weight == 0 and piece == 0 and slot == 0
                    self.across.append(
                        None if first else copies.make(pair[slot].at[rows], here, inner_peer)
                    )
                    self.onward.append(copies.make(here, landing.at[1 - slot, rows], outer_peer))
                    self.late.append(copies.make(here, full.at[6 + slot, rows], core_peer))
                    self.place.append(
                        pltpu.make_async_copy(here, full.at[2 + slot, rows], local_sems.at[sem])
                    )
                    sem += 1
            for slot in (0, 1):
                self.shared.append(copies.make(pair[slot], full.at[4 + slot], core_peer))
                self.kept.append(
                    pltpu.make_async_copy(pair[slot], full.at[slot], local_sems.at[sem])
                )
                sem += 1
                if slot >= self.pairs[weight]:
                    self.later += [self.shared[-1], self.kept[-1]]
                else:
                    self.shared[-1].start()
                    self.kept[-1].start()

        landed = sources[-1]
        landed_rows = pl.ds(0, landed.shape[0])

        @pl.when(self.inner)
        def _():
            for copy in self.across[1 : 1 + AHEAD]:
                copy.start()
            copy_rows(landed, stages[0].at[0, landed_rows])
            self.onward[0].start()
            self.late[0].start()
            self.place[0].start()

    def arrive(self, number):
        self.onward[number].wait_recv()
        swapped = number + 1 - 2 * (number % 2)
        self.late[swapped].start()
        self.place[swapped].start()

    def pump(self, steps):
        steps = [step for step in steps if step + 1 < len(self.across)]

        @pl.when(self.inner)
        def _():
            for step in steps:
                here = step + 1
                self.across[here].wait_recv()
                for copy in self.across[here + AHEAD : here + AHEAD + 1]:
                    copy.start()
                self.onward[here].start()
                self.late[here].start()
                self.place[here].start()

        @pl.when(self.outer)
        def _():
            for step in steps:
                self.arrive(step)

        for copy in self.partners if 1 in steps else []:
            copy.wait_recv()
            copy.wait_send()
        for copy in self.later if 1 in steps else []:
            copy.start()

    def finish(self):
        @pl.when(self.inner)
        def _():
            for copy in self.across[1:] + self.onward:
                copy.wait_send()

        @pl.when(self.outer)
        def _():
            self.arrive(len(self.onward) - 1)

        for copy in self.kept + self.place:
            copy.wait()
        for copy in self.shared + self.late:
            copy.wait_send()
        for copy in self.shared + self.late:
            copy.wait_recv()


def sum_eighths(
    copies, row_peer, side_peer, send, keep, forward, first, second, store, begin, pump
):
    size = send.shape[0] // 4
    part = lambda ref, slot: ref.at[pl.ds(slot * size, size)]
    arrivals = [
        copies.start(part(send, 1), part(first, 1), row_peer),
        copies.start(part(send, 3), part(first, 3), side_peer),
        copies.start(part(send, 0), part(first, 0), row_peer),
        copies.start(part(send, 2), part(first, 2), side_peer),
    ]
    begin()
    passed = []
    for number, slot, peer in ((0, 1, side_peer), (1, 3, row_peer)):
        arrivals[number].wait_recv()

        def add(row, count, number=number, slot=slot):
            here = pl.ds(slot * size + row, count)
            both = keep[here, :].astype(jnp.float32) + first[here, :].astype(jnp.float32)
            forward[pl.ds(number * size + row, count), :] = both.astype(jnp.bfloat16)

        for_rows(size, add)
        passed.append(copies.start(part(forward, number), part(second, number), peer))
    pump([0])
    for number, slot in ((0, 0), (1, 2)):
        arrivals[2 + number].wait_recv()
        passed[number].wait_recv()

        def total(row, count, number=number, slot=slot):
            here = pl.ds(slot * size + row, count)
            sums = keep[here, :].astype(jnp.float32) + first[here, :].astype(jnp.float32)
            sums = sums + second[pl.ds(number * size + row, count), :].astype(jnp.float32)
            store(number, row, count, sums)

        for_rows(size, total)
        yield number
    for copy in arrivals + passed:
        copy.wait_send()


def halves(terms):
    rows = terms.shape[0] // 2
    return terms.at[pl.ds(0, rows)], terms.at[pl.ds(rows, rows)]


def split_refs(refs, jobs, extra_count, out_count):
    refs = list(refs)
    take = lambda count: [refs.pop(0) for _ in range(count)]
    extras = take(extra_count)
    sources = [take(len(job.sources)) for job in jobs]
    full = take(1)[0]
    outs = take(out_count)
    targets = [take(len(job.outputs)) for job in jobs]
    return extras, sources, full, outs, targets, refs


def spread_kernel(middle, jobs, extra_count, out_count, gain_sum, terms, *refs):
    keep, send = halves(terms)
    extras, sources, full, outs, targets, scratch = split_refs(refs, jobs, extra_count, out_count)
    forward, first, second, send_sems, recv_sems, local_sems, *stages = scratch
    zone, side, row, core = place_here()
    row_peer, side_peer = device(zone, side, 1 - row, core), device(zone, 1 - side, row, core)
    copies = Copies(send_sems, recv_sems)
    size = send.shape[0] // 4
    part = lambda slot: full.at[pl.ds(slot * size, size)]
    for out in outs:
        if out.shape[0] == 1:
            out[...] = jnp.zeros_like(out)
    peers = {}
    for job in jobs:
        peers.update(job.peers(zone, side, row, core))
    always = [row_peer, side_peer] + list(peers.values())
    turns = [job for job in jobs if isinstance(job, TurnRows)]
    if turns:

        @pl.when(side == core)
        def _():
            greet(always)

        @pl.when(side != core)
        def _():
            greet(always + [device(zone, core, row, side)])

    else:
        greet(always)

    def begin():
        spot = 0
        for job, source, target in zip(jobs, sources, targets):
            own_stages = stages[spot : spot + len(job.scratch)]
            job.start(copies, local_sems, source, target, own_stages)
            spot += len(job.scratch)

    def pump(steps):
        for job in jobs:
            job.pump(steps)

    def store(number, row, count, sums):
        own = pl.ds(number * size + row, count)
        full[pl.ds(2 * number * size + row, count), :] = middle(own, sums, extras, outs)

    firsts, seconds = [], []
    for number in sum_eighths(
        copies, row_peer, side_peer, send, keep, forward, first, second, store, begin, pump
    ):
        near, other = (side_peer, row_peer) if number == 0 else (row_peer, side_peer)
        slot = 2 * number
        firsts.append(copies.start(part(slot), part(slot + 1), near))
        seconds.append(copies.start(part(slot), part(4 + slot), other))
    pump([1])
    firsts[0].wait_recv()
    seconds.append(copies.start(part(1), part(5), row_peer))
    firsts[1].wait_recv()
    seconds.append(copies.start(part(3), part(7), side_peer))
    for job in turns:
        job.begin()
    pump(range(2, 6))
    for job in turns:
        job.pass_on(0)
    pump(range(6, 64))
    for job in turns:
        job.pass_on(1)
    for copy in seconds:
        copy.wait_recv()
    for copy in firsts + seconds:
        copy.wait_send()
    for job in jobs:
        job.finish()


def home_kernel(middle, jobs, extra_count, out_count, gain_sum, terms, *refs):
    keep, send = halves(terms)
    extras, sources, full, outs, targets, scratch = split_refs(refs, jobs, extra_count, out_count)
    forward, first, second, own, send_sems, recv_sems, local_sems, *gain_scratch = scratch
    zone, side, row, core = place_here()
    row_peer, side_peer = device(zone, side, 1 - row, core), device(zone, 1 - side, row, core)
    core_peer = device(zone, side, row, 1 - core)
    copies = Copies(send_sems, recv_sems)
    size = send.shape[0] // 4
    at_home = side == core
    away = side != core
    for out in outs:
        if out.shape[0] == 1:
            out[...] = jnp.zeros_like(out)
    peers = {}
    for job in jobs:
        peers.update(job.peers(zone, side, row, core))
    plane = [row_peer, side_peer, core_peer]
    if gain_sum is not None:
        plane = gain_sum.plane_peers(zone, side, row, core)
        peers.update(gain_sum.zone_peers(zone, side, row, core))
    greet(plane + list(peers.values()))

    def begin():
        for job, source, target in zip(jobs, sources, targets):
            job.start(copies, local_sems, source, target, [])

    def pump(steps):
        for job in jobs:
            job.pump(steps)

    def store(number, start, count, sums):
        here = pl.ds(number * size + start, count)
        values = middle(here, sums, extras, outs)
        own[here, :] = values
        eighth = row * 2 + side if number == 0 else 4 + side * 2 + row

        @pl.when(at_home)
        def _():
            full[pl.ds(pl.multiple_of(eighth * size + start, 32), count), :] = values

    for _ in sum_eighths(
        copies, row_peer, side_peer, send, keep, forward, first, second, store, begin, pump
    ):
        pass
    pump([1])

    def piece(number, x, y):
        start = (x * 2 + y) * size if number == 0 else (4 + y * 2 + x) * size
        return full.at[pl.ds(pl.multiple_of(start, size), size)]

    mine = lambda number: own.at[pl.ds(number * size, size)]
    both = (0, 1)
    block_send = copies.make(extras[3], outs[1], side_peer)
    to_side = [copies.make(mine(k), piece(k, row, side), side_peer) for k in both]
    to_row = [copies.make(mine(k), piece(k, row, side), row_peer) for k in both]
    pass_row = [
        copies.make(piece(k, row, 1 - side), piece(k, row, 1 - side), row_peer) for k in both
    ]
    share = []
    for number, (x, y) in enumerate(
        ((row, side), (row, 1 - side), (1 - row, side), (1 - row, 1 - side))
    ):
        for k in both:
            source = mine(k) if number == 0 else piece(k, x, y)
            share.append(copies.make(source, piece(k, x, y), core_peer))

    if gain_sum is not None:
        gain_sum.start(copies, extras[-1], outs[0], *gain_scratch)

    @pl.when(away)
    def _():
        for copy in to_side + [block_send]:
            copy.start()

    @pl.when(at_home)
    def _():
        for copy in to_row + share[:2]:
            copy.start()

    if gain_sum is not None:
        gain_sum.middle()

    @pl.when(away)
    def _():
        for copy in to_side + [block_send]:
            copy.wait_send()
        for copy in share:
            copy.wait_recv()

    @pl.when(at_home)
    def _():
        for k in both:
            to_side[k].wait_recv()
            pass_row[k].start()
            share[2 + k].start()
        for k, copy in enumerate(to_row + pass_row):
            copy.wait_recv()
            share[4 + k].start()
        for copy in to_row + pass_row + share:
            copy.wait_send()
        block_send.wait_recv()

    if gain_sum is not None:
        gain_sum.finish(outs[-1])
    for job in jobs:
        job.finish()


def sum_rows(kernel, middle, terms, extras, outs, number, jobs=(), gain_sum=None):
    half, width = terms.shape[0] // 2, terms.shape[1]
    eighth = half // 4
    low = jnp.bfloat16
    vmem, hbm = pl.BlockSpec(memory_space=pltpu.VMEM), pl.BlockSpec(memory_space=pl.ANY)
    scratch = [
        pltpu.VMEM((2 * eighth, width), low),
        pltpu.VMEM((half, width), low),
        pltpu.VMEM((2 * eighth, width), low),
    ]
    if kernel is home_kernel:
        scratch.append(pltpu.VMEM((2 * eighth, width), low))
    copies = (12 if kernel is spread_kernel else 21) + sum(job.count for job in jobs)
    local = max([2] + [job.count_local for job in jobs])
    if gain_sum is not None:
        copies += gain_sum.count
        outs = outs + [gain_sum.output]
    scratch += [pltpu.SemaphoreType.DMA((count,)) for count in (copies, copies, local)]
    if gain_sum is not None:
        scratch += gain_sum.scratch
    scratch += [stage for job in jobs for stage in job.scratch]
    sources = [source for job in jobs for source in job.sources]
    targets = [target for job in jobs for target in job.outputs]
    return pl.pallas_call(
        functools.partial(kernel, middle, jobs, len(extras), len(outs), gain_sum),
        out_shape=[jax.ShapeDtypeStruct((2 * half, width), low)] + outs + targets,
        in_specs=[vmem] * (1 + len(extras) + len(sources)),
        out_specs=[vmem] * (1 + len(outs))
        + [hbm if job.in_hbm else vmem for job in jobs for _ in job.outputs],
        scratch_shapes=scratch,
        compiler_params=pltpu.CompilerParams(
            collective_id=number, has_side_effects=True, vmem_limit_bytes=56 * 2**20
        ),
        cost_estimate=pl.CostEstimate(flops=4 * 10**10, bytes_accessed=10**8, transcendentals=0),
        name=middle.__name__,
    )(terms, *extras, *sources)


def block_columns(plan, width):
    if not plan.ordered:
        return [pl.ds(0, width)], [pl.ds(0, width)]
    zone, _, _, core = place_here()
    size, zones = width // plan.total, plan.zones
    owners = [
        flipped(zone, plan.flips[slot % zones]) * 2 + (core if slot < zones else 1 - core)
        for slot in range(plan.total)
    ]
    natural = [pl.ds(pl.multiple_of(owner * size, size), size) for owner in owners]
    return natural, [pl.ds(slot * size, size) for slot in range(plan.total)]


def copy_rows(source, target):
    def some(row, count):
        target[pl.ds(row, count), :] = source[pl.ds(row, count), :]

    if source.shape[0] % 32:
        target[...] = source[...]
    else:
        for_rows(source.shape[0], some)


def cast_rows(source, target):
    def some(row, count):
        here = pl.ds(row, count)
        target[here, :] = source[here, :].astype(target.dtype)

    for_rows(source.shape[0], some)


def opening_kernel(plan, wide_qkv, gains, wide_gate, wide_out, tokens, angles, *refs):
    qkv_full, gains_full, turned_gate, turned_out, turned_tokens, turned_angles = refs[:6]
    partner_gate, send_sems, recv_sems, tokens_stage, qkv, gate, out = refs[6:]
    cast_rows(wide_qkv, qkv)
    zone, side, row, core = place_here()
    partner = device(zone, core, row, side)
    row_peer, core_peer = device(zone, side, 1 - row, core), device(zone, side, row, 1 - core)
    zone_peers = [device(flipped(zone, flip), side, row, core) for flip in plan.flips[1:]]
    at_home, away = side == core, side != core
    always = [row_peer, core_peer] + zone_peers

    @pl.when(at_home)
    def _():
        greet(always)

    @pl.when(away)
    def _():
        greet(always + [partner])

    copies = Copies(send_sems, recv_sems)
    zones = plan.zones
    own = (gains, qkv, angles, gate, out)
    ends = (gains_full.at[0], qkv_full.at[0], turned_angles, turned_gate, turned_out)
    units = wide_gate.shape[2]

    def cast_rest():
        for half in (0, 1):
            cast_rows(wide_gate.at[half], gate.at[:, pl.ds(half * units, units)])
        cast_rows(wide_out, out)

    turn = [copies.make(source, target, partner) for source, target in zip(own, ends)]
    pieces = 2
    size = tokens.shape[0] // (2 * pieces)
    spots = [
        pl.ds(pl.multiple_of((row * pieces + piece) * size, size), size) for piece in range(pieces)
    ]
    turn_rows = [copies.make(tokens.at[s], tokens_stage.at[s], partner) for s in spots]
    pass_rows = [copies.make(tokens_stage.at[s], tokens_stage.at[s], row_peer) for s in spots]
    natural, local = block_columns(plan, tokens.shape[1])

    def lay_down(all_tokens):
        def some(start, count):
            here = pl.ds(start, count)
            for a, b in zip(natural, local):
                turned_tokens[here, b] = all_tokens[here, a]

        for_rows(all_tokens.shape[0], some)

    slots = list(range(1, zones))
    weights = ((gains, gains_full), (qkv, qkv_full))
    swapped = pl.ds(0, gate.shape[0] // 2)
    from_own = [
        [copies.make(source, full.at[slot], zone_peers[slot - 1]) for slot in slots]
        + [copies.make(source, full.at[zones], core_peer)]
        for source, full in weights
    ] + [[copies.make(gate.at[swapped], partner_gate, zone_peers[0])]]
    copies.number -= 2 * zones + 1
    from_turned = [
        [copies.make(full.at[0], full.at[slot], zone_peers[slot - 1]) for slot in slots]
        + [copies.make(full.at[0], full.at[zones], core_peer)]
        for _, full in weights
    ] + [[copies.make(turned_gate.at[swapped], partner_gate, zone_peers[0])]]
    cross = [
        [copies.make(full.at[slot], full.at[zones + slot], core_peer) for slot in slots]
        for _, full in weights
    ]

    def cross_over(k):
        for which in (0, 1):
            from_turned[which][k].wait_recv()
            cross[which][k].start()

    @pl.when(away)
    def _():
        for copy in turn[:3]:
            copy.start()
        cast_rest()
        for which in (0, 1):
            turn[which].wait_recv()
            for copy in from_turned[which]:
                copy.start()
        turn[3].start()
        turn_rows[0].start()
        turn[3].wait_recv()
        from_turned[2][0].start()
        turn_rows[1].start()
        cross_over(0)
        turn_rows[0].wait_recv()
        pass_rows[0].start()
        for copy in turn[4:]:
            copy.start()
        turn_rows[1].wait_recv()
        pass_rows[1].start()

    @pl.when(at_home)
    def _():
        for copy in from_own[0] + from_own[1]:
            copy.start()
        cast_rest()
        for copy in from_own[2]:
            copy.start()
        for source, target in zip(own, ends):
            copy_rows(source, target)
        lay_down(tokens)
        cross_over(0)

    for k in range(1, zones - 1):
        cross_over(k)
    for which in (0, 1):
        from_turned[which][zones - 1].wait_recv()
        for copy in from_turned[which]:
            copy.wait_send()
        for copy in cross[which]:
            copy.wait_recv()
            copy.wait_send()
    from_turned[2][0].wait_recv()
    from_turned[2][0].wait_send()

    @pl.when(away)
    def _():
        for copy in pass_rows + turn[2:3] + turn[4:]:
            copy.wait_recv()
        lay_down(tokens_stage)
        for copy in turn + turn_rows + pass_rows:
            copy.wait_send()


def opening(plan, qkv, gains, gate, out, tokens, angles, number):
    low = jnp.bfloat16
    vmem = pl.BlockSpec(memory_space=pltpu.VMEM)
    like = lambda v: jax.ShapeDtypeStruct(v.shape, v.dtype)
    whole = lambda v: jax.ShapeDtypeStruct((2 * plan.zones,) + v.shape, low)
    operands = (qkv, gains, gate, out, tokens, angles)
    low_gate = jax.ShapeDtypeStruct((gate.shape[1], 2 * gate.shape[2]), low)
    low_out = jax.ShapeDtypeStruct(out.shape, low)
    outputs = [whole(qkv), whole(gains), low_gate, low_out, like(tokens), like(angles)]
    outputs += [jax.ShapeDtypeStruct((gate.shape[1] // 2, 2 * gate.shape[2]), low)]
    copies = 5 + 4 + 2 * plan.zones + 1 + 2 * (plan.zones - 1)
    return pl.pallas_call(
        functools.partial(opening_kernel, plan),
        out_shape=outputs,
        in_specs=[vmem] * len(operands),
        out_specs=[vmem] * len(outputs),
        scratch_shapes=[
            pltpu.SemaphoreType.DMA((copies,)),
            pltpu.SemaphoreType.DMA((copies,)),
            pltpu.VMEM(tokens.shape, tokens.dtype),
            pltpu.VMEM(qkv.shape, low),
            pltpu.VMEM(low_gate.shape, low),
            pltpu.VMEM(out.shape, low),
        ],
        compiler_params=pltpu.CompilerParams(
            collective_id=number, has_side_effects=True, vmem_limit_bytes=56 * 2**20
        ),
        cost_estimate=pl.CostEstimate(flops=4 * 10**10, bytes_accessed=10**8, transcendentals=0),
        name="opening",
    )(*operands)


def inverse_rms(values):
    return lax.rsqrt(jnp.mean(values * values, -1, keepdims=True) + EPS_NORM)


def hidden_rows(own, sums, extras, outs):
    tokens, gain = extras
    hidden = tokens[own, :].astype(jnp.float32) + sums
    outs[0][own, :] = hidden
    return (hidden * inverse_rms(hidden) * gain[...]).astype(jnp.bfloat16)


def grad_hidden_rows(own, sums, extras, outs):
    hidden, out_grad, gain = extras
    values = hidden[own, :]
    factor = inverse_rms(values)
    unit = values * factor
    outs[1][...] += jnp.sum(sums * unit, 0, keepdims=True)
    grad = out_grad[own, :].astype(jnp.float32) + norm_back(sums * gain[...], unit, factor)
    outs[0][own, :] = grad
    return grad.astype(jnp.bfloat16)


def grad_input_rows(own, sums, extras, outs):
    tokens, grad_hidden, gain = extras[:3]
    values = tokens[own, :].astype(jnp.float32)
    factor = inverse_rms(values)
    unit = values * factor
    outs[0][...] += jnp.sum(sums * unit, 0, keepdims=True)
    return (grad_hidden[own, :] + norm_back(sums * gain[...], unit, factor)).astype(jnp.bfloat16)


def dot(left, right, left_dim=1, right_dim=0):
    return lax.dot_general(
        left, right, (((left_dim,), (right_dim,)), ((), ())), preferred_element_type=jnp.float32
    )


def turn_head(values, cosine, signed_sine):
    return values * cosine + pltpu.roll(values, HEAD // 2, 1) * signed_sine


def turn_back(gradient, cosine, signed_sine):
    return gradient * cosine + pltpu.roll(gradient * signed_sine, HEAD // 2, 1)


def softmax_block(query, key, first_row):
    rows, keys = query.shape[0], key.shape[0]
    scores = dot(query, key, 1, 1)
    row_at = lax.broadcasted_iota(jnp.int32, (rows, keys), 0) + first_row
    key_at = lax.broadcasted_iota(jnp.int32, (rows, keys), 1)
    scores = jnp.where(key_at <= row_at, scores, -1000000000.0)
    exponent = jnp.exp(scores - jnp.max(scores, -1, keepdims=True))
    return exponent / jnp.sum(exponent, -1, keepdims=True)


def eighth_owners():
    _, side, row, _ = place_here()
    own, off = (row, side), (1 - row, 1 - side)
    first = lambda x, y: x * 2 + y
    second = lambda x, y: 4 + y * 2 + x
    return [
        first(own[0], own[1]),
        first(own[0], off[1]),
        second(own[0], own[1]),
        second(off[0], own[1]),
        first(off[0], own[1]),
        first(off[0], off[1]),
        second(own[0], off[1]),
        second(off[0], off[1]),
    ]


def reorder_rows(source, target, into_local):
    size = source.shape[0] // 8
    for slot, owner in enumerate(eighth_owners()):
        natural = pl.ds(pl.multiple_of(owner * size, size), size)
        local = pl.ds(slot * size, size)
        if into_local:
            target[local, :] = source[natural, :]
        else:
            target[natural, :] = source[local, :]


def forward_kernel(
    tokens, weights, gain_in, gain_q, gain_k, cosine, sine,
    normed, raw, query, key, value, local, attended,
):
    low = jnp.bfloat16
    total, heads = tokens.shape[0], query.shape[1] // HEAD
    block, wide = 256, 512

    def project(step, carry):
        rows = pl.ds(pl.multiple_of(step * wide, wide), wide)
        values = tokens[rows, :].astype(jnp.float32)
        normed[rows, :] = (values * inverse_rms(values) * gain_in[...]).astype(low)
        raw[rows, :] = dot(normed[rows, :], weights[...])
        turns = (cosine[rows, :], sine[rows, :])
        for head in range(heads):
            column = (head // 2) * 4 * HEAD + (head % 2) * HEAD
            values = raw[rows, pl.ds(column, HEAD)]
            values = turn_head(values * inverse_rms(values) * gain_q[...], *turns)
            query[rows, pl.ds(head * HEAD, HEAD)] = (values * (1.0 / math.sqrt(HEAD))).astype(low)
        for group in range(heads // 2):
            column = group * 4 * HEAD + 2 * HEAD
            here = pl.ds(group * HEAD, HEAD)
            values = raw[rows, pl.ds(column, HEAD)]
            values = turn_head(values * inverse_rms(values) * gain_k[...], *turns)
            key[rows, here] = values.astype(low)
            value[rows, here] = raw[rows, pl.ds(column + HEAD, HEAD)].astype(low)
        return carry

    lax.fori_loop(0, total // wide, project, 0)

    def attend(head, carry):
        mine = pl.ds(pl.multiple_of(head * HEAD, HEAD), HEAD)
        shared = pl.ds(pl.multiple_of(lax.div(head, 2) * HEAD, HEAD), HEAD)
        for start in range(0, total, SEQ):
            for first in range(0, SEQ, block):
                rows, keys = pl.ds(start + first, block), pl.ds(start, first + block)
                probs = softmax_block(query[rows, mine], key[keys, shared], first)
                attended[rows, mine] = dot(probs.astype(low), value[keys, shared]).astype(low)
        return carry

    lax.fori_loop(0, heads, attend, 0)
    reorder_rows(attended, local, True)


def attention(tokens, weights, gain_in, gain_q, gain_k, cosine, sine):
    total = tokens.shape[0]
    columns = weights.shape[1]
    low = jnp.bfloat16
    shape = lambda width, kind=low: jax.ShapeDtypeStruct((total, width), kind)
    vmem = pl.BlockSpec(memory_space=pltpu.VMEM)
    return pl.pallas_call(
        forward_kernel,
        out_shape=[
            shape(tokens.shape[1]),
            shape(columns, jnp.float32),
            shape(columns // 2),
            shape(columns // 4),
            shape(columns // 4),
            shape(columns // 2),
        ],
        in_specs=[vmem] * 7,
        out_specs=[vmem] * 6,
        scratch_shapes=[pltpu.VMEM((total, columns // 2), low)],
        compiler_params=pltpu.CompilerParams(vmem_limit_bytes=48 * 2**20),
        cost_estimate=pl.CostEstimate(flops=10**10, bytes_accessed=2 * 10**7, transcendentals=0),
        name="attention",
    )(tokens, weights, gain_in, gain_q, gain_k, cosine, sine)


def backward_kernel(
    query, key, value, raw, grad_rows, gain_q, gain_k, cosine, sine,
    mixed, mixed_local, query_gain, key_gain, grad, key_sum, value_sum,
):
    low = jnp.bfloat16
    total, heads = query.shape[0], query.shape[1] // HEAD
    block = 256
    reorder_rows(grad_rows, grad, False)
    query_gain[...] = jnp.zeros_like(query_gain)
    key_gain[...] = jnp.zeros_like(key_gain)

    def head_norm_back(rows, column, gradient, gain, gain_grad):
        values = raw[rows, column]
        factor = inverse_rms(values)
        unit = values * factor
        turned = turn_back(gradient, cosine[rows, :], sine[rows, :])
        gain_grad[...] += jnp.sum(turned * unit, 0, keepdims=True)
        mixed[rows, column] = norm_back(turned * gain[...], unit, factor).astype(low)

    def one_group(group, carry):
        at = lambda offset: pl.ds(pl.multiple_of(group * 4 * HEAD + offset * HEAD, HEAD), HEAD)
        shared = pl.ds(pl.multiple_of(group * HEAD, HEAD), HEAD)
        key_sum[...] = jnp.zeros_like(key_sum)
        value_sum[...] = jnp.zeros_like(value_sum)
        for head in (0, 1):
            mine = pl.ds(pl.multiple_of((group * 2 + head) * HEAD, HEAD), HEAD)
            for start in range(0, total, SEQ):
                for first in range(0, SEQ, block):
                    rows, keys = pl.ds(start + first, block), pl.ds(start, first + block)
                    query_part, grad_part = query[rows, mine], grad[rows, mine]
                    probs = softmax_block(query_part, key[keys, shared], first)
                    weighed = probs * dot(grad_part, value[keys, shared], 1, 1)
                    scores = weighed - probs * jnp.sum(weighed, -1, keepdims=True)
                    scores = scores.astype(low)
                    grad_query = dot(scores, key[keys, shared]) * (1.0 / math.sqrt(HEAD))
                    head_norm_back(rows, at(head), grad_query, gain_q, query_gain)
                    key_sum[keys, :] += dot(scores, query_part, 0, 0)
                    value_sum[keys, :] += dot(probs.astype(low), grad_part, 0, 0)
        for first in range(0, total, block):
            rows = pl.ds(first, block)
            head_norm_back(rows, at(2), key_sum[rows, :], gain_k, key_gain)
            mixed[rows, at(3)] = value_sum[rows, :].astype(low)
        return carry

    lax.fori_loop(0, heads // 2, one_group, 0)
    reorder_rows(mixed, mixed_local, True)


def attention_back(query, key, value, raw, grad_rows, gain_q, gain_k, cosine, sine):
    total, columns = raw.shape
    low = jnp.bfloat16
    vmem = pl.BlockSpec(memory_space=pltpu.VMEM)
    return pl.pallas_call(
        backward_kernel,
        out_shape=[
            jax.ShapeDtypeStruct((total, columns), low),
            jax.ShapeDtypeStruct((total, columns), low),
            jax.ShapeDtypeStruct((1, HEAD), jnp.float32),
            jax.ShapeDtypeStruct((1, HEAD), jnp.float32),
        ],
        in_specs=[vmem] * 9,
        out_specs=[vmem] * 4,
        scratch_shapes=[
            pltpu.VMEM(grad_rows.shape, low),
            pltpu.VMEM((total, HEAD), jnp.float32),
            pltpu.VMEM((total, HEAD), jnp.float32),
        ],
        compiler_params=pltpu.CompilerParams(vmem_limit_bytes=48 * 2**20),
        cost_estimate=pl.CostEstimate(flops=10**10, bytes_accessed=2 * 10**7, transcendentals=0),
        name="attention_back",
    )(query, key, value, raw, grad_rows, gain_q, gain_k, cosine, sine)


def feed_kernel(plan, rows, own_grad, got_grad, gate_up, up_part, down, active, grads, out_grad):
    low = jnp.bfloat16
    block = 512
    tile = down.shape[1]
    step = pl.program_id(0)
    gate_at = pl.ds(pl.multiple_of(step * tile, tile), tile)
    up_at = pl.ds(pl.multiple_of(grads.shape[1] // 2 + step * tile, tile), tile)
    _, side, _, core = place_here()

    def lay_down(source):
        natural, blocks = block_columns(plan, source.shape[1])
        eighth = source.shape[0] // 8
        for slot, owner in enumerate(eighth_owners()):

            def some(start, count, slot=slot, owner=owner):
                here = pl.ds(pl.multiple_of(owner * eighth + start, 32), count)
                there = pl.ds(slot * eighth + start, count)
                for a, b in zip(natural, blocks):
                    out_grad[there, b] = source[here, a]

            for_rows(eighth, some)

    @pl.when((step == 0) & (side == core))
    def _():
        lay_down(own_grad)

    @pl.when((step == 0) & (side != core))
    def _():
        lay_down(got_grad)

    def one(block_at, carry):
        here = pl.ds(pl.multiple_of(block_at * block, block), block)
        gate = dot(rows[here, :], gate_up[...])
        up = dot(rows[here, :], up_part[...])
        grad = dot(out_grad[here, :], down[...])
        sigmoid = jax.nn.sigmoid(gate)
        silu = gate * sigmoid
        active[here, :] = (silu * up).astype(low)
        grads[here, gate_at] = (grad * up * sigmoid * (1.0 + gate * (1.0 - sigmoid))).astype(low)
        grads[here, up_at] = (grad * silu).astype(low)
        return carry

    lax.fori_loop(0, rows.shape[0] // block, one, 0)


def feed_forward(plan, rows, own_grad, got_grad, gate_up, down, tile):
    total, width = rows.shape
    units = down.shape[1]
    low = jnp.bfloat16
    tiles = units // tile
    whole = pl.BlockSpec(memory_space=pltpu.VMEM)
    return pl.pallas_call(
        functools.partial(feed_kernel, plan),
        grid=(tiles,),
        out_shape=[
            jax.ShapeDtypeStruct((total, units), low),
            jax.ShapeDtypeStruct((total, 2 * units), low),
            jax.ShapeDtypeStruct((total, width), low),
        ],
        in_specs=[
            whole,
            whole,
            whole,
            pl.BlockSpec((width, tile), lambda step: (0, step)),
            pl.BlockSpec((width, tile), lambda step: (0, step + tiles)),
            pl.BlockSpec((width, tile), lambda step: (0, step)),
        ],
        out_specs=[
            pl.BlockSpec((total, tile), lambda step: (0, step)),
            whole,
            whole,
        ],
        compiler_params=pltpu.CompilerParams(vmem_limit_bytes=56 * 2**20),
        cost_estimate=pl.CostEstimate(
            flops=6 * total * width * units, bytes_accessed=4 * 10**7, transcendentals=total * units
        ),
        name="feed_forward",
    )(rows, own_grad, got_grad, gate_up, gate_up, down)


class Plan:
    def __init__(self, mesh):
        self.total = mesh.shape["dp"]
        self.zones = self.total // 2
        self.tensor = mesh.shape["tensor"]
        self.flips = [k ^ (k >> 1) for k in range(self.zones)]

    def place(self):
        self.index = lax.axis_index("dp")
        self.zone = self.index // 2
        self.side = self.index % 2
        self.row = lax.axis_index("tensor") // 2
        self.core = lax.axis_index("tensor") % 2
        self.home = self.side == self.core

    def move(self, value, target):
        pairs = []
        for d in range(self.total):
            for t in range(self.tensor):
                to = target(d // 2, d % 2, t // 2, t % 2)
                if to is not None:
                    zone, side, row, core = to
                    pairs.append((d * self.tensor + t, (zone * 2 + side) * self.tensor + row * 2 + core))
        return lax.ppermute(value, ("dp", "tensor"), pairs)

    def turn(self, value):
        got = self.move(value, lambda z, y, x, c: (z, c, x, y) if y != c else None)
        return jnp.where(self.home, value, got)

    def zone_flip(self, value, bit):
        return self.move(value, lambda z, y, x, c: (z ^ bit, y, x, c))

    def core_swap(self, value):
        return self.move(value, lambda z, y, x, c: (z, y, x, 1 - c))

    def side_swap(self, value):
        return self.move(value, lambda z, y, x, c: (z, 1 - y, x, c))

    def row_swap(self, value):
        return self.move(value, lambda z, y, x, c: (z, y, 1 - x, c))

    def to_local(self, value, axis):
        width = value.shape[axis] // self.total
        parts = []
        for core in (self.core, 1 - self.core):
            for slot in range(self.zones):
                owner = (self.zone ^ self.flips[slot]) * 2 + core
                parts.append(lax.dynamic_slice_in_dim(value, owner * width, width, axis))
        return jnp.concatenate(parts, axis)

    def to_natural(self, value, axis, core=None):
        core = self.core if core is None else core
        width = value.shape[axis] // self.total
        parts = []
        for block in range(self.total):
            slot = flip = (block // 2) ^ self.zone
            for bits in range(1, self.zones.bit_length()):
                slot = slot ^ (flip >> bits)
            slot = slot + jnp.where(block % 2 == core, 0, self.zones)
            parts.append(lax.dynamic_slice_in_dim(value, slot * width, width, axis))
        return jnp.concatenate(parts, axis)

    def row_owners(self):
        own, off = (self.row, self.side), (1 - self.row, 1 - self.side)
        first = lambda x, y: x * 2 + y
        second = lambda x, y: 4 + y * 2 + x
        return [
            first(own[0], own[1]),
            first(own[0], off[1]),
            second(own[0], own[1]),
            second(off[0], own[1]),
            first(off[0], own[1]),
            first(off[0], off[1]),
            second(own[0], off[1]),
            second(off[0], off[1]),
        ]

    def rows_local(self, value, slots=range(8)):
        size = value.shape[0] // 8
        owners = self.row_owners()
        return jnp.concatenate(
            [lax.dynamic_slice_in_dim(value, owners[slot] * size, size, 0) for slot in slots], 0
        )

    def rows_natural(self, value, order=range(8)):
        size = value.shape[0] // 8
        place = [list(order).index(slot) for slot in range(8)]
        parts = []
        for piece in range(8):
            x, y = (piece // 2, piece % 2) if piece < 4 else (piece % 2, (piece - 4) // 2)
            slots = (0, 1, 4, 5) if piece < 4 else (2, 6, 3, 7)
            same_x, same_y = x == self.row, y == self.side
            slot = jnp.where(
                same_x,
                jnp.where(same_y, place[slots[0]], place[slots[1]]),
                jnp.where(same_y, place[slots[2]], place[slots[3]]),
            )
            parts.append(lax.dynamic_slice_in_dim(value, slot * size, size, 0))
        return jnp.concatenate(parts, 0)

    def from_zones(self, shard):
        return [self.zone_flip(shard, flip) for flip in self.flips[1:]]

    def to_zones(self, parts, slots):
        return [self.zone_flip(parts[slot], self.flips[slot]) for slot in slots]

    def middle_swap(self, pair):
        return self.move(pair, lambda z, y, x, c: (z ^ 3, y, x, c) if z in (1, 2) else None)

    def inward(self, part):
        return self.move(part, lambda z, y, x, c: (z ^ 1, y, x, c) if z in (0, 3) else None)

    def pass_outward(self, pair):
        return self.move(pair, lambda z, y, x, c: (z ^ 1, y, x, c) if z in (1, 2) else None)

    def far_pair(self, middle, passed):
        inner = (self.zone == 1) | (self.zone == 2)
        return jnp.where(inner, middle, passed[::-1])

    def first_swap(self, send):
        half = send.shape[0] // 2
        return self.row_swap(send[:half]), self.side_swap(send[half:])

    def second_swap(self, keep, got):
        quarter = keep.shape[0] // 4
        row_part = keep[: 2 * quarter] + got[0].astype(jnp.float32)
        side_part = keep[2 * quarter :] + got[1].astype(jnp.float32)
        own = jnp.concatenate([row_part[:quarter], side_part[:quarter]], 0)
        return own, (
            self.side_swap(row_part[quarter:].astype(jnp.bfloat16)),
            self.row_swap(side_part[quarter:].astype(jnp.bfloat16)),
        )

    def spread_first(self, own):
        half = own.shape[0] // 2
        return (self.side_swap(own[:half]), self.row_swap(own[half:]))

    def spread_second(self, own, got):
        half = own.shape[0] // 2
        row_part = jnp.concatenate([own[:half], got[0]], 0)
        side_part = jnp.concatenate([own[half:], got[1]], 0)
        return row_part, side_part, self.row_swap(row_part), self.side_swap(side_part)

    def send_home(self, own):
        to_home = lambda z, y, x, c: (z, c, x, c) if y != c else None
        return jnp.concatenate([own, self.move(own, to_home)], 0)

    def row_home(self, part):
        return self.move(part, lambda z, y, x, c: (z, y, 1 - x, c) if y == c else None)

    def share_home(self, part, other):
        full = jnp.concatenate([part, other], 0)
        full = self.to_natural(self.rows_natural(full, (0, 2, 1, 6, 4, 3, 5, 7)), 1)
        got = self.move(full, lambda z, y, x, c: (z, y, x, 1 - c) if y == c else None)
        return full, got

    def turned(self, own, got):
        return jnp.where(self.home, own, got)

    def sum_everywhere(self, value):
        value = value + self.row_swap(value)
        value = value + self.side_swap(value)
        value = value + self.core_swap(value)
        bit = 1
        while bit < self.zones:
            value = value + self.zone_flip(value, bit)
            bit *= 2
        return value


def shards(
    plan,
    tokens,
    positions,
    out_grad,
    qkv_weight,
    qkv_first,
    qkv_second,
    out_weight,
    out_first,
    out_second,
    gate_up,
    gate_up_first,
    gate_up_second,
    down_weight,
    down_first,
    down_second,
    gains,
    gains_first,
    gains_second,
):
    plan.place()
    low = jnp.bfloat16
    tok_rows, model_width = tokens.shape
    groups = qkv_weight.shape[1]
    head_size = qkv_weight.shape[3]
    shard_rows = qkv_weight.shape[0]
    seq_count = tok_rows // SEQ
    mixed_cols = groups * 4 * head_size
    near_cols = model_width // 2
    kept = tok_rows // 2
    gain_count = gains.shape[0]

    tree = plan.zones == 4
    slots = range(1, plan.zones)

    def column_parts(value):
        return value.reshape((plan.zones, -1) + value.shape[1:])

    units = gate_up.shape[2]
    plan.ordered = (model_width // plan.total) % 128 == 0
    gain_rows = 16
    gain_block = jnp.pad(gains.astype(low), (0, gain_rows * 128 - gain_count)).reshape(gain_rows, 128)
    tile = min(units, 256)
    angle_at = positions.astype(jnp.float32).reshape(-1, 128)
    both_qkv, both_gains, turned_gate, turned_out, tokens, angle_at, partner_gate = opening(
        plan,
        qkv_weight.reshape(shard_rows, mixed_cols),
        gain_block,
        gate_up,
        out_weight,
        tokens,
        angle_at,
        3,
    )
    positions = angle_at.reshape(-1)
    turned_out, turned_gate, tokens, positions, both_qkv, both_gains, low_down = fence(
        turned_out,
        turned_gate,
        tokens,
        positions,
        both_qkv,
        both_gains,
        down_weight.astype(low),
    )

    got_down = plan.move(low_down, lambda z, y, x, c: (z, c, x, y) if y != c else None)
    half_rows = shard_rows // 2
    if tree:
        out_at = turned_out.size // half_rows
        both = [turned_out.reshape(half_rows, out_at), turned_gate[half_rows:]]
        both = plan.zone_flip(jnp.concatenate(both, 1), 1)
        zone_out = [both[:, :out_at].reshape(turned_out.shape)]
        zone_out += [plan.zone_flip(turned_out, flip) for flip in plan.flips[2:]]
        partner_rest = both[:, out_at:]
        landed = plan.middle_swap(turned_gate[:half_rows])
    else:
        zone_out = plan.from_zones(turned_out)
        partner_rest = landed = partner_gate
        partner_gate = plan.from_zones(turned_gate)
    if not plan.ordered:
        tokens = plan.to_local(tokens, 1)
    cosine, sine_table = rotary(positions, head_size)
    signed_sine = jnp.concatenate(
        [-sine_table[:, : head_size // 2], sine_table[:, head_size // 2 :]], 1
    )
    full_qkv = both_qkv.reshape(model_width, mixed_cols)
    gain_slots = both_gains.reshape(plan.total, -1)[:, :gain_count]
    gain_all = plan.to_natural(gain_slots.reshape(-1), 0).astype(jnp.float32)
    gain_in = plan.to_local(gain_all[:model_width], 0)[None]
    gain_post = plan.to_local(gain_all[model_width : 2 * model_width], 0)[None]
    gain_q = gain_all[2 * model_width : 2 * model_width + head_size][None]
    gain_k = gain_all[2 * model_width + head_size :][None]
    normed, raw, query, key_rot, values_low, attended = attention(
        tokens, full_qkv, gain_in, gain_q, gain_k, cosine, signed_sine
    )
    turned_down = plan.turned(low_down, got_down)
    attended, zone_out, turned_out, turned_down, turned_gate, partner_gate, partner_rest, landed = fence(
        attended, zone_out, turned_out, turned_down, turned_gate, partner_gate, partner_rest, landed
    )

    near_out = jnp.concatenate([turned_out] + zone_out, 0)
    far_out = plan.core_swap(near_out)
    own_tokens = plan.rows_local(tokens, (0, 2))
    near_out, far_out, own_tokens = fence(near_out, far_out, own_tokens)

    full_out = jnp.concatenate([near_out, far_out], 0)
    branch_terms = contract_cols(attended, full_out).astype(low)
    if tree:
        pairs = [(turned_gate, jnp.concatenate([partner_gate, partner_rest], 0)), (turned_down,)]
    else:
        pairs = [(turned_gate, partner_gate), (turned_down, plan.from_zones(turned_down))]
    jobs = [TurnRows(out_grad)] + ([PairTree(pairs, (2, 2), landed)] if tree else [])
    normed_rows, hidden, got_grad, *gathered = sum_rows(
        spread_kernel,
        hidden_rows,
        branch_terms,
        [own_tokens, gain_post],
        [jax.ShapeDtypeStruct((tok_rows // 4, model_width), jnp.float32)],
        0,
        jobs,
    )
    if not tree:
        near = [jnp.concatenate([own] + rest, 0) for own, rest in pairs]
        gathered = [jnp.concatenate([part, plan.core_swap(part)], 0) for part in near]
    full_gate = gathered[0].reshape(model_width, 2 * units)
    full_down = gathered[1].reshape(model_width, units)
    normed_rows, hidden, full_gate, full_down, got_grad = fence(
        normed_rows, hidden, full_gate, full_down, got_grad
    )

    def zone_parts(near, got):
        both = (near + got.astype(jnp.float32)).astype(low)
        return both.reshape((plan.zones, -1) + both.shape[1:])

    def zone_total(parts, *arrived):
        total = parts[0].astype(jnp.float32)
        for part in sum([list(group) for group in arrived], []):
            total = total + part.astype(jnp.float32)
        return total.astype(low)

    active, grad_both, out_grad = feed_forward(
        plan, normed_rows, out_grad, got_grad, full_gate, full_down, tile
    )
    if not plan.ordered:
        out_grad = plan.to_local(out_grad, 1)
    down_far = contract_rows(out_grad[:, near_cols:], active).astype(low)
    down_far, active, grad_both, out_grad = fence(down_far, active, grad_both, out_grad)

    down_got = plan.core_swap(down_far)
    gate_far = contract_rows(normed_rows[:, near_cols:], grad_both).astype(low)
    down_parts = zone_parts(contract_rows(out_grad[:, :near_cols], active), down_got)
    down_parts, gate_far, grad_both = fence(down_parts, gate_far, grad_both)

    gate_got = plan.core_swap(gate_far)
    if tree:
        inner_terms = plan.inward(down_parts[3])
    else:
        inner_terms = plan.to_zones(down_parts, slots)
    post_terms = contract_cols(grad_both, full_gate).astype(low)
    post_terms, gate_got, inner_terms, down_parts = fence(
        post_terms, gate_got, inner_terms, down_parts
    )

    down_sums = jnp.stack([inner_terms, plan.inward(down_parts[2])]) if tree else inner_terms
    gate_parts = zone_parts(contract_rows(normed_rows[:, :near_cols], grad_both), gate_got)
    if tree:
        down_pair = (down_parts[2:].astype(jnp.float32) + down_sums.astype(jnp.float32)).astype(low)
    else:
        down_pair = down_parts
    post_terms, gate_parts, down_parts, down_pair = fence(
        post_terms, gate_parts, down_parts, down_pair
    )

    if tree:
        down_sums = plan.middle_swap(down_pair)
        gate_sums = [plan.inward(gate_parts[3]), plan.inward(gate_parts[2])]
    else:
        gate_sums = plan.to_zones(gate_parts, slots)
    eighth = tok_rows // 8
    own_grad = jnp.concatenate([out_grad[:eighth], out_grad[2 * eighth : 3 * eighth]], 0)
    branch_rows, grad_hidden, post_gain_grad, mlp_terms = sum_rows(
        spread_kernel,
        grad_hidden_rows,
        post_terms,
        [hidden, own_grad, gain_post],
        [
            jax.ShapeDtypeStruct((tok_rows // 4, model_width), jnp.float32),
            jax.ShapeDtypeStruct((1, model_width), jnp.float32),
        ],
        1,
        [SideDot(active, full_down)],
    )
    branch_rows, grad_hidden, post_gain_grad, mlp_terms, down_sums, gate_sums, down_parts, gate_parts = fence(
        branch_rows,
        grad_hidden,
        post_gain_grad,
        mlp_terms,
        down_sums,
        gate_sums,
        down_parts,
        gate_parts,
    )

    def plus(left, right):
        return (left.astype(jnp.float32) + right.astype(jnp.float32)).astype(low)

    mlp_got = plan.first_swap(mlp_terms[kept:])
    if tree:
        gate_first = plan.middle_swap(plus(gate_parts[3], gate_sums[1]))
        down_own = [plus(down_parts[0], down_sums[0]), plus(down_parts[1], down_sums[1])]
        down_last = [plan.zone_flip(down_own[1], 1)]
    else:
        gate_first = gate_parts[0]
        down_own, down_last = down_parts, down_sums
    grad_att = jnp.dot(branch_rows, full_out, preferred_element_type=jnp.float32).astype(low)
    grad_mixed, mixed_rows, query_gain_grad, key_gain_grad = attention_back(
        query, key_rot, values_low, raw, grad_att, gain_q, gain_k, cosine, signed_sine
    )
    gain_terms = jnp.concatenate(
        [plan.to_natural(post_gain_grad, 1), query_gain_grad, key_gain_grad], 1
    )
    grad_mixed, mixed_rows, gain_terms, normed, branch_rows, mlp_got, gate_first, down_last, gate_parts, gate_sums = fence(
        grad_mixed,
        mixed_rows,
        gain_terms,
        normed,
        branch_rows,
        mlp_got,
        gate_first,
        down_last,
        gate_parts,
        gate_sums,
    )

    if tree:
        gate_second = plan.middle_swap(plus(gate_parts[2], gate_sums[0]))
        gate_last = plan.zone_flip(plus(gate_parts[1], gate_first), 1)
        gate_sums = [gate_second, gate_last]
    mlp_own, mlp_last = plan.second_swap(mlp_terms[:kept].astype(jnp.float32), mlp_got)
    out_far = contract_rows(branch_rows[:, near_cols:], attended).astype(low)
    out_got = plan.core_swap(out_far)
    qkv_far = contract_rows(normed[:, near_cols:], grad_mixed).astype(low)
    qkv_got = plan.core_swap(qkv_far)
    normed_terms = contract_cols(mixed_rows, full_qkv).astype(low)
    out_parts = zone_parts(contract_rows(branch_rows[:, :near_cols], attended), out_got)
    qkv_parts = zone_parts(contract_rows(normed[:, :near_cols], grad_mixed), qkv_got)
    total_down = zone_total(down_own, down_last)
    block_own = (hidden + mlp_own + jnp.concatenate(mlp_last, 0).astype(jnp.float32)).astype(low)
    block_own, out_parts, qkv_parts, normed_terms, gate_sums, gate_parts, total_down = fence(
        block_own, out_parts, qkv_parts, normed_terms, gate_sums, gate_parts, total_down
    )

    gain_sum = GainSum(plan, gain_terms.shape[1], model_width) if plan.ordered else None
    input_full, input_gain_grad, block_side, *rest = sum_rows(
        home_kernel,
        grad_input_rows,
        normed_terms,
        [own_tokens, grad_hidden, gain_in, block_own] + ([gain_terms] if plan.ordered else []),
        [
            jax.ShapeDtypeStruct((1, model_width), jnp.float32),
            jax.ShapeDtypeStruct(block_own.shape, low),
        ],
        2,
        [ZoneBlocks(plan, qkv_parts, slots), ZoneBlocks(plan, out_parts, slots, 1)],
        gain_sum,
    )
    if plan.ordered:
        summed_gains, qkv_sent, out_sent = rest
    else:
        qkv_sent, out_sent = rest
        summed_gains = plan.sum_everywhere(
            jnp.concatenate([plan.to_natural(input_gain_grad, 1), gain_terms], 1)
        )
    input_full, summed_gains, qkv_sent, out_sent, total_down, block_side, gate_sums, gate_parts = fence(
        input_full, summed_gains, qkv_sent, out_sent, total_down, block_side, gate_sums, gate_parts
    )

    block_home = jnp.concatenate([block_own, block_side], 0)
    block_row = plan.row_home(block_home)
    summed_both = plan.turn(
        jnp.concatenate([zone_total(qkv_parts, qkv_sent), zone_total(out_parts, out_sent)], 1)
    ).astype(jnp.float32)
    total_gate = zone_total(gate_parts, gate_sums)
    summed_gate = plan.turn(jnp.stack([total_gate[:, :units], total_gate[:, units:]]))
    summed_down = plan.turn(total_down)
    block_full, block_got = plan.share_home(block_home, block_row)
    block_out = jnp.where(plan.home, block_full, block_got)
    summed_qkv = summed_both[:, :mixed_cols].reshape(qkv_weight.shape)
    summed_out = summed_both[:, mixed_cols:]
    summed_gate = summed_gate.astype(jnp.float32)
    summed_down = summed_down.astype(jnp.float32)
    summed_gains = lax.dynamic_slice_in_dim(summed_gains[0], plan.index * gain_count, gain_count, 0)
    input_rows = plan.to_natural(input_full, 1, plan.side).astype(jnp.float32)

    qkv_moment, qkv_square, qkv_updated = adamw(
        qkv_weight, summed_qkv, qkv_first, qkv_second, RATE_QKV, DECAY_RATE
    )
    out_moment, out_square, out_updated = adamw(
        out_weight, summed_out, out_first, out_second, RATE_OUT, DECAY_RATE
    )
    gate_moment, gate_square, gate_updated = adamw(
        gate_up, summed_gate, gate_up_first, gate_up_second, RATE_GATE, DECAY_RATE
    )
    down_moment, down_square, down_updated = adamw(
        down_weight, summed_down, down_first, down_second, RATE_DOWN, DECAY_RATE
    )
    gain_moment, gain_square, gain_updated = adamw(
        gains, summed_gains, gains_first, gains_second, RATE_GAIN, 0.0
    )
    return (
        block_out,
        input_rows,
        qkv_moment,
        qkv_square,
        qkv_updated,
        out_moment,
        out_square,
        out_updated,
        gate_moment,
        gate_square,
        gate_updated,
        down_moment,
        down_square,
        down_updated,
        gain_moment,
        gain_square,
        gain_updated,
    )


def solution(mesh):
    plan = Plan(mesh)
    placed = (
        P("dp", None),
        P("dp"),
        P("dp", None),
        P("dp", "tensor", None, None),
        P("dp", "tensor", None, None),
        P("dp", "tensor", None, None),
        P("dp", "tensor"),
        P("dp", "tensor"),
        P("dp", "tensor"),
        P(None, "dp", "tensor"),
        P(None, "dp", "tensor"),
        P(None, "dp", "tensor"),
        P("dp", "tensor"),
        P("dp", "tensor"),
        P("dp", "tensor"),
        P("dp"),
        P("dp"),
        P("dp"),
    )
    return jax.shard_map(
        functools.partial(shards, plan),
        mesh=mesh,
        in_specs=placed,
        out_specs=(
            P("dp", None),
            P("dp", None),
            P("dp", "tensor", None, None),
            P("dp", "tensor", None, None),
            P("dp", "tensor", None, None),
            P("dp", "tensor"),
            P("dp", "tensor"),
            P("dp", "tensor"),
            P(None, "dp", "tensor"),
            P(None, "dp", "tensor"),
            P(None, "dp", "tensor"),
            P("dp", "tensor"),
            P("dp", "tensor"),
            P("dp", "tensor"),
            P("dp"),
            P("dp"),
            P("dp"),
        ),
        check_vma=False,
    )
```

```python
import functools
import math

import jax
import jax.numpy as jnp
from jax import lax
from jax.experimental import pallas as pl
from jax.experimental.pallas import tpu as pltpu
from jax.sharding import PartitionSpec as P

SEQ = 1024
STEP = 10


EPS_NORM = 1e-06
THETA = 1000000.0
BETA_ONE = 0.9
BETA_TWO = 0.95
ADAM_EPS = 1e-08
DECAY_RATE = 0.1
RATE_QKV = 0.05
RATE_OUT = 0.3
RATE_GATE = 0.05
RATE_DOWN = 0.03
RATE_GAIN = 1.0


def rotary(positions, head_size):
    freq_index = jnp.arange(head_size // 2, dtype=jnp.float32)
    inverse = jnp.exp(freq_index * (-2.0 * math.log(THETA) / head_size))
    angles = positions.astype(jnp.float32)[:, None] * inverse[None, :]
    cosine = jnp.cos(angles)
    sine_table = jnp.sin(angles)
    return (jnp.concatenate([cosine, cosine], -1), jnp.concatenate([sine_table, sine_table], -1))


def rotate(values, cosine, sine_table):
    half_size = values.shape[-1] // 2
    turned = jnp.concatenate([-values[..., half_size:], values[..., :half_size]], -1)
    return values * cosine[:, None, :] + turned * sine_table[:, None, :]


def unrotate(gradient, cosine, sine_table):
    half_size = gradient.shape[-1] // 2
    turned = gradient * sine_table[:, None, :]
    rotated_back = jnp.concatenate([turned[..., half_size:], -turned[..., :half_size]], -1)
    return gradient * cosine[:, None, :] + rotated_back


def norm_back(grad_unit, unit_vals, factor):
    return factor * (grad_unit - unit_vals * jnp.mean(grad_unit * unit_vals, -1, keepdims=True))


def contract_rows(left, right):
    return lax.dot_general(
        left, right, (((0,), (0,)), ((), ())), preferred_element_type=jnp.float32
    )


def contract_cols(left, right):
    return lax.dot_general(
        left, right, (((1,), (1,)), ((), ())), preferred_element_type=jnp.float32
    )


def block_scores(query_part, key_part, first_row, block_rows, last_row):
    scores = jnp.einsum(
        "nqkgd,nskd->nkgqs", query_part, key_part, preferred_element_type=jnp.float32
    )
    causal = (first_row + jnp.arange(block_rows))[:, None] >= jnp.arange(last_row)[None, :]
    return jnp.where(causal, scores, -1000000000.0)


def attention_forward(query, key_rot, values_low, seq_len):
    block_rows = min(512, seq_len)
    outputs = []
    log_sums = []
    for first_row in range(0, seq_len, block_rows):
        last_row = first_row + block_rows
        query_part = query[:, first_row:last_row]
        scores = block_scores(query_part, key_rot[:, :last_row], first_row, block_rows, last_row)
        row_max = jnp.max(scores, -1, keepdims=True)
        exponent = jnp.exp(scores - row_max)
        row_total = jnp.sum(exponent, -1, keepdims=True)
        probs_low = (exponent / row_total).astype(jnp.bfloat16)
        outputs.append(
            jnp.einsum(
                "nkgqs,nskd->nqkgd",
                probs_low,
                values_low[:, :last_row],
                preferred_element_type=jnp.float32,
            )
        )
        log_sums.append(row_max + jnp.log(row_total))
    return (jnp.concatenate(outputs, 1), log_sums)


def attention_backward(query, key_rot, values_low, grad_att, log_sums, seq_len):
    block_rows = min(512, seq_len)
    query_grads = []
    key_grad = jnp.zeros(key_rot.shape, jnp.float32)
    value_grad = jnp.zeros(values_low.shape, jnp.float32)
    for block_index, first_row in enumerate(range(0, seq_len, block_rows)):
        last_row = first_row + block_rows
        query_part = query[:, first_row:last_row]
        grad_part = grad_att[:, first_row:last_row]
        key_part = key_rot[:, :last_row]
        value_part = values_low[:, :last_row]
        scores = block_scores(query_part, key_part, first_row, block_rows, last_row)
        probs = jnp.exp(scores - log_sums[block_index])
        probs_low = probs.astype(jnp.bfloat16)
        grad_probs = jnp.einsum(
            "nqkgd,nskd->nkgqs", grad_part, value_part, preferred_element_type=jnp.float32
        )
        grad_scores = (
            probs * (grad_probs - jnp.sum(probs * grad_probs, -1, keepdims=True))
        ).astype(jnp.bfloat16)
        query_grads.append(
            jnp.einsum(
                "nkgqs,nskd->nqkgd", grad_scores, key_part, preferred_element_type=jnp.float32
            )
        )
        padding = ((0, 0), (0, seq_len - last_row), (0, 0), (0, 0))
        key_grad = key_grad + jnp.pad(
            jnp.einsum(
                "nkgqs,nqkgd->nskd", grad_scores, query_part, preferred_element_type=jnp.float32
            ),
            padding,
        )
        value_grad = value_grad + jnp.pad(
            jnp.einsum(
                "nkgqs,nqkgd->nskd", probs_low, grad_part, preferred_element_type=jnp.float32
            ),
            padding,
        )
    return (jnp.concatenate(query_grads, 1), key_grad, value_grad)


def adamw(weight, gradient, moment, second, step_rate, decay_rate):
    moment = BETA_ONE * moment + (1.0 - BETA_ONE) * gradient
    second = BETA_TWO * second + (1.0 - BETA_TWO) * gradient * gradient
    first_hat = moment / (1.0 - BETA_ONE**STEP)
    second_hat = second / (1.0 - BETA_TWO**STEP)
    weight = weight - step_rate * (
        first_hat / (jnp.sqrt(second_hat) + ADAM_EPS) + decay_rate * weight
    )
    return (moment, second, weight)


def fence(*values):
    return lax.optimization_barrier(values)


MESH = pl.DeviceIdType.MESH
HEAD = 128
AHEAD = 2


def place_here():
    index, place = lax.axis_index("dp"), lax.axis_index("tensor")
    return lax.div(index, 2), lax.rem(index, 2), lax.div(place, 2), lax.rem(place, 2)


def device(zone, side, row, core):
    return (zone * 2 + side, row * 2 + core)


def flipped(zone, flip):
    bit = 1
    while bit <= flip:
        if flip & bit:
            zone = zone + bit - 2 * bit * lax.rem(lax.div(zone, bit), 2)
        bit *= 2
    return zone


def greet(devices, amount=None):
    barrier = pltpu.get_barrier_semaphore()
    for peer in devices:
        pl.semaphore_signal(barrier, inc=1, device_id=peer, device_id_type=MESH)
    pl.semaphore_wait(barrier, len(devices) if amount is None else amount)


def for_rows(count, body):
    step = 32

    def one(block, carry):
        body(pl.multiple_of(block * step, step), step)
        return carry

    lax.fori_loop(0, count // step, one, 0)


class Copies:
    def __init__(self, send_sems, recv_sems):
        self.send_sems, self.recv_sems = send_sems, recv_sems
        self.number = 0

    def make(self, source, target, peer):
        number, self.number = self.number, self.number + 1
        return pltpu.make_async_remote_copy(
            src_ref=source,
            dst_ref=target,
            send_sem=self.send_sems.at[number],
            recv_sem=self.recv_sems.at[number],
            device_id=peer,
            device_id_type=MESH,
        )

    def start(self, source, target, peer):
        copy = self.make(source, target, peer)
        copy.start()
        return copy


class GainSum:
    def __init__(self, plan, rest, width):
        self.plan, self.width = plan, width
        self.total = width + rest
        self.scratch = [
            pltpu.VMEM((8, 1, self.total), jnp.float32),
            pltpu.VMEM((plan.zones, 1, self.total), jnp.float32),
        ]
        self.output = jax.ShapeDtypeStruct((1, self.total), jnp.float32)
        self.count = 7 + plan.zones - 1

    def plane_peers(self, zone, side, row, core):
        steps = [(s, r, c) for s in range(2) for r in range(2) for c in range(2)][1:]
        turn = lambda value, step: 1 - value if step else value
        return [device(zone, turn(side, s), turn(row, r), turn(core, c)) for s, r, c in steps]

    def zone_peers(self, zone, side, row, core):
        return {flip: device(flipped(zone, flip), side, row, core) for flip in self.plan.flips[1:]}

    def start(self, copies, rest, blocks, plane_sums, zone_sums):
        zone, side, row, core = place_here()
        plan = self.plan
        size = self.width // plan.total
        self.copies, self.plane_sums, self.zone_sums, self.zone = copies, plane_sums, zone_sums, zone
        here = side * 4 + row * 2 + core
        plane_sums[here, :, pl.ds(self.width, self.total - self.width)] = rest[...]
        for slot in range(plan.total):
            owner = flipped(zone, plan.flips[slot % plan.zones]) * 2
            owner = owner + (core if slot < plan.zones else 1 - core)
            spot = pl.ds(pl.multiple_of(owner * size, size), size)
            plane_sums[here, :, spot] = blocks[:, pl.ds(slot * size, size)]
        self.plane = [
            copies.start(plane_sums.at[here], plane_sums.at[here], peer)
            for peer in self.plane_peers(zone, side, row, core)
        ]

    def middle(self):
        for copy in self.plane:
            copy.wait_recv()
        total = self.plane_sums[0]
        for place in range(1, 8):
            total = total + self.plane_sums[place]
        self.zone_sums[self.zone] = total
        zone, side, row, core = place_here()
        self.across = [
            self.copies.start(self.zone_sums.at[self.zone], self.zone_sums.at[self.zone], peer)
            for peer in self.zone_peers(zone, side, row, core).values()
        ]

    def finish(self, out):
        for copy in self.across:
            copy.wait_recv()
        total = self.zone_sums[0]
        for place in range(1, self.plan.zones):
            total = total + self.zone_sums[place]
        out[...] = total
        for copy in self.plane + self.across:
            copy.wait_send()


class ZoneBlocks:
    scratch = []

    def __init__(self, plan, source, slots, begin=0):
        self.flips, self.slots, self.sources, self.begin = plan.flips, list(slots), [source], begin
        self.outputs = [
            jax.ShapeDtypeStruct((len(self.slots),) + source.shape[1:], source.dtype)
        ]
        self.count, self.count_local = len(self.slots), 0
        self.in_hbm = False

    def peers(self, zone, side, row, core):
        return {
            self.flips[slot]: device(flipped(zone, self.flips[slot]), side, row, core)
            for slot in self.slots
        }

    def start(self, copies, local_sems, sources, targets, stages):
        zone, side, row, core = place_here()
        self.started = [
            copies.make(
                sources[0].at[slot],
                targets[0].at[number],
                device(flipped(zone, self.flips[slot]), side, row, core),
            )
            for number, slot in enumerate(self.slots)
        ]
        self.waiting = True
        if self.begin == 0:
            self.pump([0])

    def pump(self, steps):
        if self.waiting and self.begin in steps:
            self.waiting = False
            for copy in self.started:
                copy.start()

    def finish(self):
        for copy in self.started:
            copy.wait_send()
        for copy in self.started:
            copy.wait_recv()


def inner_zone(zone):
    return lax.rem(lax.div(zone + 1, 2), 2)


class SideDot:
    count, count_local, scratch, in_hbm = 0, 0, [], False

    def __init__(self, left, right):
        self.sources = [left, right]
        self.outputs = [jax.ShapeDtypeStruct((left.shape[0], right.shape[0]), jnp.bfloat16)]

    def peers(self, zone, side, row, core):
        return {}

    def some(self, first, last):
        left, right = self.refs
        size = 256

        def one(step, carry):
            here = pl.ds(pl.multiple_of(step * size, size), size)
            self.out[:, here] = dot(left[...], right[here, :], 1, 1).astype(jnp.bfloat16)
            return carry

        lax.fori_loop(first, last, one, 0)

    def start(self, copies, local_sems, sources, targets, stages):
        self.refs, self.out = sources, targets[0]
        self.steps = self.out.shape[1] // 256
        self.some(0, self.steps // 2)

    def pump(self, steps):
        if 0 in steps:
            self.some(self.steps // 2, self.steps)

    def finish(self):
        pass


class PairScatter:
    def __init__(self, parts, pieces):
        self.sources, self.pieces = [parts], pieces
        _, rows, columns = parts.shape
        self.size = rows // pieces
        self.outputs = [jax.ShapeDtypeStruct((2, rows, columns), parts.dtype)]
        self.scratch = [pltpu.VMEM((2, rows, columns), parts.dtype)] * 2
        self.count, self.count_local = 4 * pieces, 0
        self.in_hbm = False

    def peers(self, zone, side, row, core):
        return {
            1: device(flipped(zone, 1), side, row, core),
            3: device(flipped(zone, 3), side, row, core),
        }

    def start(self, copies, local_sems, sources, targets, stages):
        zone, side, row, core = place_here()
        self.parts, self.out = sources[0], targets[0]
        self.inward, self.crossed = stages
        inner_peer = device(flipped(zone, 3), side, row, core)
        outer_peer = device(flipped(zone, 1), side, row, core)
        self.inner = inner_zone(zone) == 1
        self.outer = inner_zone(zone) == 0
        self.steps = [
            (slot, pl.ds(piece * self.size, self.size))
            for piece in range(self.pieces)
            for slot in (0, 1)
        ]
        self.to_inner = [
            copies.make(self.parts.at[3 - slot, rows], self.inward.at[slot, rows], outer_peer)
            for slot, rows in self.steps
        ]
        self.across = [
            copies.make(self.inward.at[slot, rows], self.crossed.at[slot, rows], inner_peer)
            for slot, rows in self.steps
        ]

        @pl.when(self.outer)
        def _():
            for copy in self.to_inner[:AHEAD]:
                copy.start()

    def add(self, target, slot, rows, left, right):
        def some(row, count):
            here = pl.ds(rows.start + row, count)
            both = left[here, :].astype(jnp.float32) + right[here, :].astype(jnp.float32)
            target.at[slot][here, :] = both.astype(jnp.bfloat16)

        for_rows(self.size, some)

    def pump(self, steps):
        steps = [step for step in steps if step < len(self.steps)]

        @pl.when(self.inner)
        def _():
            for step in steps:
                slot, rows = self.steps[step]
                self.to_inner[step].wait_recv()
                self.add(self.inward, slot, rows, self.parts.at[2 + slot], self.inward.at[slot])
                self.across[step].start()
                if step >= AHEAD:
                    self.settle(step - AHEAD)

        @pl.when(self.outer)
        def _():
            for step in steps:
                self.to_inner[step].wait_send()
                for copy in self.to_inner[step + AHEAD : step + AHEAD + 1]:
                    copy.start()

    def settle(self, step):
        slot, rows = self.steps[step]
        self.across[step].wait_recv()
        self.add(self.out, slot, rows, self.parts.at[slot], self.crossed.at[slot])

    def finish(self):
        @pl.when(self.inner)
        def _():
            for step in range(len(self.steps) - AHEAD, len(self.steps)):
                self.settle(step)
            for copy in self.across:
                copy.wait_send()

        @pl.when(self.outer)
        def _():
            for slot in (0, 1):

                def some(row, count, slot=slot):
                    here = pl.ds(row, count)
                    self.out.at[slot][here, :] = self.parts.at[slot][here, :]

                for_rows(self.parts.shape[1], some)


class BlockGrad:
    in_hbm = False

    def __init__(self, plan, left, right):
        self.zones, self.flips = plan.zones, plan.flips
        self.sources = [left, right]
        shape = (left.shape[1] // plan.total, right.shape[1])
        low = jnp.bfloat16
        self.outputs = [jax.ShapeDtypeStruct(shape, low)]
        self.scratch = [pltpu.VMEM((plan.zones,) + shape, low)] * 4
        self.count, self.count_local = 2 * plan.zones, 0

    def peers(self, zone, side, row, core):
        return {flip: device(flipped(zone, flip), side, row, core) for flip in self.flips[1:]}

    def product(self, block):
        size = self.out.shape[0]
        return dot(self.left[:, pl.ds(block * size, size)], self.right[...], 0, 0)

    def start(self, copies, local_sems, sources, targets, stages):
        zone, side, row, core = place_here()
        self.left, self.right = sources
        self.out = targets[0]
        self.far, self.got, self.parts, self.arrived = stages
        core_peer = device(zone, side, row, 1 - core)
        self.order = list(range(1, self.zones)) + [0]
        self.over = [
            copies.make(self.far.at[slot], self.got.at[slot], core_peer)
            for slot in range(self.zones)
        ]
        self.along = [
            copies.make(
                self.parts.at[slot],
                self.arrived.at[slot],
                device(flipped(zone, self.flips[slot]), side, row, core),
            )
            for slot in range(1, self.zones)
        ]
        for slot in self.order:
            self.far[slot] = self.product(self.zones + slot).astype(jnp.bfloat16)
            self.over[slot].start()

    def pump(self, steps):
        for slot in self.order if 0 in steps else []:
            near = self.product(slot)
            self.over[slot].wait_recv()
            self.parts[slot] = (near + self.got[slot].astype(jnp.float32)).astype(jnp.bfloat16)
            if slot:
                self.along[slot - 1].start()

    def finish(self):
        total = self.parts[0].astype(jnp.float32)
        for slot in range(1, self.zones):
            self.along[slot - 1].wait_recv()
            total = total + self.arrived[slot].astype(jnp.float32)
        self.out[...] = total.astype(jnp.bfloat16)
        for copy in self.over + self.along:
            copy.wait_send()


class TurnRows:
    count, count_local, scratch, in_hbm = 4, 0, [], False

    def __init__(self, values):
        self.sources = [values]
        self.outputs = [jax.ShapeDtypeStruct(values.shape, values.dtype)]

    def peers(self, zone, side, row, core):
        return {}

    def start(self, copies, local_sems, sources, targets, stages):
        zone, side, row, core = place_here()
        values, target = sources[0], targets[0]
        partner, row_peer = device(zone, core, row, side), device(zone, side, 1 - row, core)
        size = values.shape[0] // 4
        spots = [pl.ds(pl.multiple_of((row * 2 + k) * size, size), size) for k in (0, 1)]
        self.away = side != core
        self.turn = [copies.make(values.at[spot], target.at[spot], partner) for spot in spots]
        self.onward = [copies.make(target.at[spot], target.at[spot], row_peer) for spot in spots]

    def pump(self, steps):
        pass

    def begin(self):
        @pl.when(self.away)
        def _():
            for copy in self.turn:
                copy.start()

    def pass_on(self, piece):
        @pl.when(self.away)
        def _():
            self.turn[piece].wait_recv()
            self.onward[piece].start()

    def finish(self):
        @pl.when(self.away)
        def _():
            for copy in self.onward:
                copy.wait_recv()
            for copy in self.turn + self.onward:
                copy.wait_send()


class PairTree:
    def __init__(self, pairs, pieces):
        self.pairs = [len(pair) for pair in pairs]
        self.sources = [shard for pair in pairs for shard in pair]
        self.pieces = pieces
        self.outputs = [
            jax.ShapeDtypeStruct((8,) + own.shape, own.dtype) for own, *_ in pairs
        ]
        self.count = 6 * sum(pieces) + 2 * len(pairs) + self.pairs.count(1)
        self.count_local = 2 * len(pairs) + 2 * sum(pieces)
        self.scratch = [pltpu.VMEM((2,) + own.shape, own.dtype) for own, *_ in pairs]
        self.scratch += [pltpu.VMEM(p[0].shape, p[0].dtype) for p in pairs if len(p) == 1]
        self.in_hbm = True

    def peers(self, zone, side, row, core):
        return {
            1: device(flipped(zone, 1), side, row, core),
            3: device(flipped(zone, 3), side, row, core),
            "core": device(zone, side, row, 1 - core),
        }

    def start(self, copies, local_sems, sources, targets, stages):
        zone, side, row, core = place_here()
        inner_peer = device(flipped(zone, 3), side, row, core)
        outer_peer = device(flipped(zone, 1), side, row, core)
        core_peer = device(zone, side, row, 1 - core)
        self.inner = inner_zone(zone) == 1
        self.outer = inner_zone(zone) == 0
        self.across, self.onward, self.late, self.place = [], [], [], []
        self.shared, self.kept, self.partners, self.later = [], [], [], []
        sem = 0
        sources, late_stages = list(sources), list(stages[len(targets) :])
        for weight, full in enumerate(targets):
            landing = stages[weight]
            pair = [sources.pop(0) for _ in range(self.pairs[weight])]
            if len(pair) == 1:
                pair.append(late_stages.pop(0))
                self.partners.append(copies.start(pair[0], pair[1], outer_peer))
            size = pair[0].shape[0] // self.pieces[weight]
            for piece in range(self.pieces[weight]):
                rows = pl.ds(piece * size, size)
                for slot in (0, 1):
                    here = landing.at[slot, rows]
                    self.across.append(copies.make(pair[slot].at[rows], here, inner_peer))
                    self.onward.append(copies.make(here, landing.at[1 - slot, rows], outer_peer))
                    self.late.append(copies.make(here, full.at[6 + slot, rows], core_peer))
                    self.place.append(
                        pltpu.make_async_copy(here, full.at[2 + slot, rows], local_sems.at[sem])
                    )
                    sem += 1
            for slot in (0, 1):
                self.shared.append(copies.make(pair[slot], full.at[4 + slot], core_peer))
                self.kept.append(
                    pltpu.make_async_copy(pair[slot], full.at[slot], local_sems.at[sem])
                )
                sem += 1
                if slot >= self.pairs[weight]:
                    self.later += [self.shared[-1], self.kept[-1]]
                else:
                    self.shared[-1].start()
                    self.kept[-1].start()

        @pl.when(self.inner)
        def _():
            for copy in self.across[:AHEAD]:
                copy.start()

    def arrive(self, number):
        self.onward[number].wait_recv()
        swapped = number + 1 - 2 * (number % 2)
        self.late[swapped].start()
        self.place[swapped].start()

    def pump(self, steps):
        steps = [step for step in steps if step < len(self.across)]

        @pl.when(self.inner)
        def _():
            for here in steps:
                self.across[here].wait_recv()
                for copy in self.across[here + AHEAD : here + AHEAD + 1]:
                    copy.start()
                self.onward[here].start()
                self.late[here].start()
                self.place[here].start()

        @pl.when(self.outer)
        def _():
            for step in steps:
                if step > 0:
                    self.arrive(step - 1)

        for copy in self.partners if 1 in steps else []:
            copy.wait_recv()
            copy.wait_send()
        for copy in self.later if 1 in steps else []:
            copy.start()

    def finish(self):
        @pl.when(self.inner)
        def _():
            for copy in self.across + self.onward:
                copy.wait_send()

        @pl.when(self.outer)
        def _():
            self.arrive(len(self.onward) - 1)

        for copy in self.kept + self.place:
            copy.wait()
        for copy in self.shared + self.late:
            copy.wait_send()
        for copy in self.shared + self.late:
            copy.wait_recv()


def sum_eighths(
    copies, row_peer, side_peer, send, keep, forward, first, second, store, begin, pump
):
    size = send.shape[0] // 4
    part = lambda ref, slot: ref.at[pl.ds(slot * size, size)]
    arrivals = [
        copies.start(part(send, 1), part(first, 1), row_peer),
        copies.start(part(send, 3), part(first, 3), side_peer),
        copies.start(part(send, 0), part(first, 0), row_peer),
        copies.start(part(send, 2), part(first, 2), side_peer),
    ]
    begin()
    passed = []
    for number, slot, peer in ((0, 1, side_peer), (1, 3, row_peer)):
        arrivals[number].wait_recv()

        def add(row, count, number=number, slot=slot):
            here = pl.ds(slot * size + row, count)
            both = keep[here, :].astype(jnp.float32) + first[here, :].astype(jnp.float32)
            forward[pl.ds(number * size + row, count), :] = both.astype(jnp.bfloat16)

        for_rows(size, add)
        passed.append(copies.start(part(forward, number), part(second, number), peer))
    pump([0])
    for number, slot in ((0, 0), (1, 2)):
        arrivals[2 + number].wait_recv()
        passed[number].wait_recv()

        def total(row, count, number=number, slot=slot):
            here = pl.ds(slot * size + row, count)
            sums = keep[here, :].astype(jnp.float32) + first[here, :].astype(jnp.float32)
            sums = sums + second[pl.ds(number * size + row, count), :].astype(jnp.float32)
            store(number, row, count, sums)

        for_rows(size, total)
        yield number
    for copy in arrivals + passed:
        copy.wait_send()


def halves(terms):
    rows = terms.shape[0] // 2
    return terms.at[pl.ds(0, rows)], terms.at[pl.ds(rows, rows)]


def split_refs(refs, jobs, extra_count, out_count):
    refs = list(refs)
    take = lambda count: [refs.pop(0) for _ in range(count)]
    extras = take(extra_count)
    sources = [take(len(job.sources)) for job in jobs]
    full = take(1)[0]
    outs = take(out_count)
    targets = [take(len(job.outputs)) for job in jobs]
    return extras, sources, full, outs, targets, refs


def spread_kernel(middle, jobs, extra_count, out_count, gain_sum, terms, *refs):
    keep, send = halves(terms)
    extras, sources, full, outs, targets, scratch = split_refs(refs, jobs, extra_count, out_count)
    forward, first, second, send_sems, recv_sems, local_sems, *stages = scratch
    zone, side, row, core = place_here()
    row_peer, side_peer = device(zone, side, 1 - row, core), device(zone, 1 - side, row, core)
    copies = Copies(send_sems, recv_sems)
    size = send.shape[0] // 4
    part = lambda slot: full.at[pl.ds(slot * size, size)]
    for out in outs:
        if out.shape[0] == 1:
            out[...] = jnp.zeros_like(out)
    peers = {}
    for job in jobs:
        peers.update(job.peers(zone, side, row, core))
    always = [row_peer, side_peer] + list(peers.values())
    turns = [job for job in jobs if isinstance(job, TurnRows)]
    if turns:

        @pl.when(side == core)
        def _():
            greet(always)

        @pl.when(side != core)
        def _():
            greet(always + [device(zone, core, row, side)])

    else:
        greet(always)

    def begin():
        spot = 0
        for job, source, target in zip(jobs, sources, targets):
            own_stages = stages[spot : spot + len(job.scratch)]
            job.start(copies, local_sems, source, target, own_stages)
            spot += len(job.scratch)

    def pump(steps):
        for job in jobs:
            job.pump(steps)

    def store(number, row, count, sums):
        own = pl.ds(number * size + row, count)
        full[pl.ds(2 * number * size + row, count), :] = middle(own, sums, extras, outs)

    firsts, seconds = [], []
    for number in sum_eighths(
        copies, row_peer, side_peer, send, keep, forward, first, second, store, begin, pump
    ):
        near, other = (side_peer, row_peer) if number == 0 else (row_peer, side_peer)
        slot = 2 * number
        firsts.append(copies.start(part(slot), part(slot + 1), near))
        seconds.append(copies.start(part(slot), part(4 + slot), other))
    pump([1])
    firsts[0].wait_recv()
    seconds.append(copies.start(part(1), part(5), row_peer))
    firsts[1].wait_recv()
    seconds.append(copies.start(part(3), part(7), side_peer))
    for job in turns:
        job.begin()
    pump(range(2, 6))
    for job in turns:
        job.pass_on(0)
    pump(range(6, 64))
    for job in turns:
        job.pass_on(1)
    for copy in seconds:
        copy.wait_recv()
    for copy in firsts + seconds:
        copy.wait_send()
    for job in jobs:
        job.finish()


def home_kernel(middle, jobs, extra_count, out_count, gain_sum, terms, *refs):
    keep, send = halves(terms)
    extras, sources, full, outs, targets, scratch = split_refs(refs, jobs, extra_count, out_count)
    forward, first, second, own, send_sems, recv_sems, local_sems, *rest = scratch
    gain_scratch, stages = (rest[:2], rest[2:]) if gain_sum is not None else ([], rest)
    zone, side, row, core = place_here()
    row_peer, side_peer = device(zone, side, 1 - row, core), device(zone, 1 - side, row, core)
    core_peer = device(zone, side, row, 1 - core)
    copies = Copies(send_sems, recv_sems)
    size = send.shape[0] // 4
    at_home = side == core
    away = side != core
    for out in outs:
        if out.shape[0] == 1:
            out[...] = jnp.zeros_like(out)
    peers = {}
    for job in jobs:
        peers.update(job.peers(zone, side, row, core))
    plane = [row_peer, side_peer, core_peer]
    if gain_sum is not None:
        plane = gain_sum.plane_peers(zone, side, row, core)
        peers.update(gain_sum.zone_peers(zone, side, row, core))
    greet(plane + list(peers.values()))

    def begin():
        spot = 0
        for job, source, target in zip(jobs, sources, targets):
            own_stages = stages[spot : spot + len(job.scratch)]
            job.start(copies, local_sems, source, target, own_stages)
            spot += len(job.scratch)

    def pump(steps):
        for job in jobs:
            job.pump(steps)

    def store(number, start, count, sums):
        here = pl.ds(number * size + start, count)
        values = middle(here, sums, extras, outs)
        own[here, :] = values
        eighth = row * 2 + side if number == 0 else 4 + side * 2 + row

        @pl.when(at_home)
        def _():
            full[pl.ds(pl.multiple_of(eighth * size + start, 32), count), :] = values

    for _ in sum_eighths(
        copies, row_peer, side_peer, send, keep, forward, first, second, store, begin, pump
    ):
        pass
    pump([1])

    def piece(number, x, y):
        start = (x * 2 + y) * size if number == 0 else (4 + y * 2 + x) * size
        return full.at[pl.ds(pl.multiple_of(start, size), size)]

    mine = lambda number: own.at[pl.ds(number * size, size)]
    both = (0, 1)
    to_side = [copies.make(mine(k), piece(k, row, side), side_peer) for k in both]
    to_row = [copies.make(mine(k), piece(k, row, side), row_peer) for k in both]
    pass_row = [
        copies.make(piece(k, row, 1 - side), piece(k, row, 1 - side), row_peer) for k in both
    ]
    share = []
    for number, (x, y) in enumerate(
        ((row, side), (row, 1 - side), (1 - row, side), (1 - row, 1 - side))
    ):
        for k in both:
            source = mine(k) if number == 0 else piece(k, x, y)
            share.append(copies.make(source, piece(k, x, y), core_peer))

    if gain_sum is not None:
        gain_sum.start(copies, extras[-1], outs[0], *gain_scratch)

    @pl.when(away)
    def _():
        for copy in to_side:
            copy.start()

    @pl.when(at_home)
    def _():
        for copy in to_row + share[:2]:
            copy.start()

    if gain_sum is not None:
        gain_sum.middle()

    @pl.when(away)
    def _():
        for copy in to_side:
            copy.wait_send()
        for copy in share:
            copy.wait_recv()

    @pl.when(at_home)
    def _():
        for k in both:
            to_side[k].wait_recv()
            pass_row[k].start()
            share[2 + k].start()
        for k, copy in enumerate(to_row + pass_row):
            copy.wait_recv()
            share[4 + k].start()
        for copy in to_row + pass_row + share:
            copy.wait_send()

    if gain_sum is not None:
        gain_sum.finish(outs[-1])
    for job in jobs:
        job.finish()


def sum_rows(kernel, middle, terms, extras, outs, number, jobs=(), gain_sum=None):
    half, width = terms.shape[0] // 2, terms.shape[1]
    eighth = half // 4
    low = jnp.bfloat16
    vmem, hbm = pl.BlockSpec(memory_space=pltpu.VMEM), pl.BlockSpec(memory_space=pl.ANY)
    scratch = [
        pltpu.VMEM((2 * eighth, width), low),
        pltpu.VMEM((half, width), low),
        pltpu.VMEM((2 * eighth, width), low),
    ]
    if kernel is home_kernel:
        scratch.append(pltpu.VMEM((2 * eighth, width), low))
    copies = (12 if kernel is spread_kernel else 20) + sum(job.count for job in jobs)
    local = max([2] + [job.count_local for job in jobs])
    if gain_sum is not None:
        copies += gain_sum.count
        outs = outs + [gain_sum.output]
    scratch += [pltpu.SemaphoreType.DMA((count,)) for count in (copies, copies, local)]
    if gain_sum is not None:
        scratch += gain_sum.scratch
    scratch += [stage for job in jobs for stage in job.scratch]
    sources = [source for job in jobs for source in job.sources]
    targets = [target for job in jobs for target in job.outputs]
    return pl.pallas_call(
        functools.partial(kernel, middle, jobs, len(extras), len(outs), gain_sum),
        out_shape=[jax.ShapeDtypeStruct((2 * half, width), low)] + outs + targets,
        in_specs=[vmem] * (1 + len(extras) + len(sources)),
        out_specs=[vmem] * (1 + len(outs))
        + [hbm if job.in_hbm else vmem for job in jobs for _ in job.outputs],
        scratch_shapes=scratch,
        compiler_params=pltpu.CompilerParams(
            collective_id=number, has_side_effects=True, vmem_limit_bytes=56 * 2**20
        ),
        cost_estimate=pl.CostEstimate(flops=4 * 10**10, bytes_accessed=10**8, transcendentals=0),
        name=middle.__name__,
    )(terms, *extras, *sources)


def block_columns(plan, width):
    if not plan.ordered:
        return [pl.ds(0, width)], [pl.ds(0, width)]
    zone, _, _, core = place_here()
    size, zones = width // plan.total, plan.zones
    owners = [
        flipped(zone, plan.flips[slot % zones]) * 2 + (core if slot < zones else 1 - core)
        for slot in range(plan.total)
    ]
    natural = [pl.ds(pl.multiple_of(owner * size, size), size) for owner in owners]
    return natural, [pl.ds(slot * size, size) for slot in range(plan.total)]


def copy_rows(source, target):
    def some(row, count):
        target[pl.ds(row, count), :] = source[pl.ds(row, count), :]

    if source.shape[0] % 32:
        target[...] = source[...]
    else:
        for_rows(source.shape[0], some)


def cast_rows(source, target):
    def some(row, count):
        here = pl.ds(row, count)
        target[here, :] = source[here, :].astype(target.dtype)

    for_rows(source.shape[0], some)


def opening_kernel(plan, wide_qkv, gains, wide_gate, wide_out, tokens, angles, *refs):
    qkv_full, gains_full, turned_gate, turned_out, turned_tokens, turned_angles = refs[:6]
    partner_gate, send_sems, recv_sems, tokens_stage, qkv, gate, out = refs[6:]
    cast_rows(wide_qkv, qkv)
    zone, side, row, core = place_here()
    partner = device(zone, core, row, side)
    row_peer, core_peer = device(zone, side, 1 - row, core), device(zone, side, row, 1 - core)
    zone_peers = [device(flipped(zone, flip), side, row, core) for flip in plan.flips[1:]]
    at_home, away = side == core, side != core
    always = [row_peer, core_peer] + zone_peers

    @pl.when(at_home)
    def _():
        greet(always)

    @pl.when(away)
    def _():
        greet(always + [partner])

    copies = Copies(send_sems, recv_sems)
    zones = plan.zones
    own = (gains, qkv, angles, gate, out)
    ends = (gains_full.at[0], qkv_full.at[0], turned_angles, turned_gate, turned_out)
    units = wide_gate.shape[2]

    def cast_rest():
        for half in (0, 1):
            cast_rows(wide_gate.at[half], gate.at[:, pl.ds(half * units, units)])
        cast_rows(wide_out, out)

    turn = [copies.make(source, target, partner) for source, target in zip(own, ends)]
    pieces = 2
    size = tokens.shape[0] // (2 * pieces)
    spots = [
        pl.ds(pl.multiple_of((row * pieces + piece) * size, size), size) for piece in range(pieces)
    ]
    turn_rows = [copies.make(tokens.at[s], tokens_stage.at[s], partner) for s in spots]
    pass_rows = [copies.make(tokens_stage.at[s], tokens_stage.at[s], row_peer) for s in spots]
    natural, local = block_columns(plan, tokens.shape[1])

    def lay_down(all_tokens):
        def some(start, count):
            here = pl.ds(start, count)
            for a, b in zip(natural, local):
                turned_tokens[here, b] = all_tokens[here, a]

        for_rows(all_tokens.shape[0], some)

    slots = list(range(1, zones))
    weights = ((gains, gains_full), (qkv, qkv_full))
    swapped = pl.ds(0, gate.shape[0] // 2)
    from_own = [
        [copies.make(source, full.at[slot], zone_peers[slot - 1]) for slot in slots]
        + [copies.make(source, full.at[zones], core_peer)]
        for source, full in weights
    ] + [[copies.make(gate.at[swapped], partner_gate, zone_peers[0])]]
    copies.number -= 2 * zones + 1
    from_turned = [
        [copies.make(full.at[0], full.at[slot], zone_peers[slot - 1]) for slot in slots]
        + [copies.make(full.at[0], full.at[zones], core_peer)]
        for _, full in weights
    ] + [[copies.make(turned_gate.at[swapped], partner_gate, zone_peers[0])]]
    cross = [
        [copies.make(full.at[slot], full.at[zones + slot], core_peer) for slot in slots]
        for _, full in weights
    ]

    def cross_over(k):
        for which in (0, 1):
            from_turned[which][k].wait_recv()
            cross[which][k].start()

    @pl.when(away)
    def _():
        for copy in turn[:3]:
            copy.start()
        cast_rest()
        for which in (0, 1):
            turn[which].wait_recv()
            for copy in from_turned[which]:
                copy.start()
        turn[3].start()
        turn_rows[0].start()
        turn[3].wait_recv()
        from_turned[2][0].start()
        turn_rows[1].start()
        cross_over(0)
        turn_rows[0].wait_recv()
        pass_rows[0].start()
        for copy in turn[4:]:
            copy.start()
        turn_rows[1].wait_recv()
        pass_rows[1].start()

    @pl.when(at_home)
    def _():
        for copy in from_own[0] + from_own[1]:
            copy.start()
        cast_rest()
        for copy in from_own[2]:
            copy.start()
        for source, target in zip(own, ends):
            copy_rows(source, target)
        lay_down(tokens)
        cross_over(0)

    for k in range(1, zones - 1):
        cross_over(k)
    for which in (0, 1):
        from_turned[which][zones - 1].wait_recv()
        for copy in from_turned[which]:
            copy.wait_send()
        for copy in cross[which]:
            copy.wait_recv()
            copy.wait_send()
    from_turned[2][0].wait_recv()
    from_turned[2][0].wait_send()

    @pl.when(away)
    def _():
        for copy in pass_rows + turn[2:3] + turn[4:]:
            copy.wait_recv()
        lay_down(tokens_stage)
        for copy in turn + turn_rows + pass_rows:
            copy.wait_send()


def opening(plan, qkv, gains, gate, out, tokens, angles, number):
    low = jnp.bfloat16
    vmem = pl.BlockSpec(memory_space=pltpu.VMEM)
    like = lambda v: jax.ShapeDtypeStruct(v.shape, v.dtype)
    whole = lambda v: jax.ShapeDtypeStruct((2 * plan.zones,) + v.shape, low)
    operands = (qkv, gains, gate, out, tokens, angles)
    low_gate = jax.ShapeDtypeStruct((gate.shape[1], 2 * gate.shape[2]), low)
    low_out = jax.ShapeDtypeStruct(out.shape, low)
    outputs = [whole(qkv), whole(gains), low_gate, low_out, like(tokens), like(angles)]
    outputs += [jax.ShapeDtypeStruct((gate.shape[1] // 2, 2 * gate.shape[2]), low)]
    copies = 5 + 4 + 2 * plan.zones + 1 + 2 * (plan.zones - 1)
    return pl.pallas_call(
        functools.partial(opening_kernel, plan),
        out_shape=outputs,
        in_specs=[vmem] * len(operands),
        out_specs=[vmem] * len(outputs),
        scratch_shapes=[
            pltpu.SemaphoreType.DMA((copies,)),
            pltpu.SemaphoreType.DMA((copies,)),
            pltpu.VMEM(tokens.shape, tokens.dtype),
            pltpu.VMEM(qkv.shape, low),
            pltpu.VMEM(low_gate.shape, low),
            pltpu.VMEM(out.shape, low),
        ],
        compiler_params=pltpu.CompilerParams(
            collective_id=number, has_side_effects=True, vmem_limit_bytes=56 * 2**20
        ),
        cost_estimate=pl.CostEstimate(flops=4 * 10**10, bytes_accessed=10**8, transcendentals=0),
        name="opening",
    )(*operands)


def inverse_rms(values):
    return lax.rsqrt(jnp.mean(values * values, -1, keepdims=True) + EPS_NORM)


def hidden_rows(own, sums, extras, outs):
    tokens, gain = extras
    hidden = tokens[own, :].astype(jnp.float32) + sums
    outs[0][own, :] = hidden
    return (hidden * inverse_rms(hidden) * gain[...]).astype(jnp.bfloat16)


def grad_hidden_rows(own, sums, extras, outs):
    hidden, out_grad, gain = extras
    values = hidden[own, :]
    factor = inverse_rms(values)
    unit = values * factor
    outs[1][...] += jnp.sum(sums * unit, 0, keepdims=True)
    grad = out_grad[own, :].astype(jnp.float32) + norm_back(sums * gain[...], unit, factor)
    outs[0][own, :] = grad
    return grad.astype(jnp.bfloat16)


def grad_input_rows(own, sums, extras, outs):
    tokens, grad_hidden, gain = extras[:3]
    values = tokens[own, :].astype(jnp.float32)
    factor = inverse_rms(values)
    unit = values * factor
    outs[0][...] += jnp.sum(sums * unit, 0, keepdims=True)
    return (grad_hidden[own, :] + norm_back(sums * gain[...], unit, factor)).astype(jnp.bfloat16)


def dot(left, right, left_dim=1, right_dim=0):
    return lax.dot_general(
        left, right, (((left_dim,), (right_dim,)), ((), ())), preferred_element_type=jnp.float32
    )


def turn_head(values, cosine, signed_sine):
    return values * cosine + pltpu.roll(values, HEAD // 2, 1) * signed_sine


def turn_back(gradient, cosine, signed_sine):
    return gradient * cosine + pltpu.roll(gradient * signed_sine, HEAD // 2, 1)


def softmax_block(query, key, first_row):
    rows, keys = query.shape[0], key.shape[0]
    scores = dot(query, key, 1, 1)
    row_at = lax.broadcasted_iota(jnp.int32, (rows, keys), 0) + first_row
    key_at = lax.broadcasted_iota(jnp.int32, (rows, keys), 1)
    scores = jnp.where(key_at <= row_at, scores, -1000000000.0)
    exponent = jnp.exp(scores - jnp.max(scores, -1, keepdims=True))
    return exponent / jnp.sum(exponent, -1, keepdims=True)


def eighth_owners():
    _, side, row, _ = place_here()
    own, off = (row, side), (1 - row, 1 - side)
    first = lambda x, y: x * 2 + y
    second = lambda x, y: 4 + y * 2 + x
    return [
        first(own[0], own[1]),
        first(own[0], off[1]),
        second(own[0], own[1]),
        second(off[0], own[1]),
        first(off[0], own[1]),
        first(off[0], off[1]),
        second(own[0], off[1]),
        second(off[0], off[1]),
    ]


def reorder_rows(source, target, into_local):
    size = source.shape[0] // 8
    for slot, owner in enumerate(eighth_owners()):
        natural = pl.ds(pl.multiple_of(owner * size, size), size)
        local = pl.ds(slot * size, size)
        if into_local:
            target[local, :] = source[natural, :]
        else:
            target[natural, :] = source[local, :]


def forward_kernel(
    tokens, weights, gain_in, gain_q, gain_k, cosine, sine,
    normed, raw, query, key, value, local, attended,
):
    low = jnp.bfloat16
    total, heads = tokens.shape[0], query.shape[1] // HEAD
    block, wide = 256, 512

    def project(step, carry):
        rows = pl.ds(pl.multiple_of(step * wide, wide), wide)
        values = tokens[rows, :].astype(jnp.float32)
        normed[rows, :] = (values * inverse_rms(values) * gain_in[...]).astype(low)
        raw[rows, :] = dot(normed[rows, :], weights[...])
        turns = (cosine[rows, :], sine[rows, :])
        for head in range(heads):
            column = (head // 2) * 4 * HEAD + (head % 2) * HEAD
            values = raw[rows, pl.ds(column, HEAD)]
            values = turn_head(values * inverse_rms(values) * gain_q[...], *turns)
            query[rows, pl.ds(head * HEAD, HEAD)] = (values * (1.0 / math.sqrt(HEAD))).astype(low)
        for group in range(heads // 2):
            column = group * 4 * HEAD + 2 * HEAD
            here = pl.ds(group * HEAD, HEAD)
            values = raw[rows, pl.ds(column, HEAD)]
            values = turn_head(values * inverse_rms(values) * gain_k[...], *turns)
            key[rows, here] = values.astype(low)
            value[rows, here] = raw[rows, pl.ds(column + HEAD, HEAD)].astype(low)
        return carry

    lax.fori_loop(0, total // wide, project, 0)

    def attend(head, carry):
        mine = pl.ds(pl.multiple_of(head * HEAD, HEAD), HEAD)
        shared = pl.ds(pl.multiple_of(lax.div(head, 2) * HEAD, HEAD), HEAD)
        for start in range(0, total, SEQ):
            for first in range(0, SEQ, block):
                rows, keys = pl.ds(start + first, block), pl.ds(start, first + block)
                probs = softmax_block(query[rows, mine], key[keys, shared], first)
                attended[rows, mine] = dot(probs.astype(low), value[keys, shared]).astype(low)
        return carry

    lax.fori_loop(0, heads, attend, 0)
    reorder_rows(attended, local, True)


def attention(tokens, weights, gain_in, gain_q, gain_k, cosine, sine):
    total = tokens.shape[0]
    columns = weights.shape[1]
    low = jnp.bfloat16
    shape = lambda width, kind=low: jax.ShapeDtypeStruct((total, width), kind)
    vmem = pl.BlockSpec(memory_space=pltpu.VMEM)
    return pl.pallas_call(
        forward_kernel,
        out_shape=[
            shape(tokens.shape[1]),
            shape(columns, jnp.float32),
            shape(columns // 2),
            shape(columns // 4),
            shape(columns // 4),
            shape(columns // 2),
        ],
        in_specs=[vmem] * 7,
        out_specs=[vmem] * 6,
        scratch_shapes=[pltpu.VMEM((total, columns // 2), low)],
        compiler_params=pltpu.CompilerParams(vmem_limit_bytes=48 * 2**20),
        cost_estimate=pl.CostEstimate(flops=10**10, bytes_accessed=2 * 10**7, transcendentals=0),
        name="attention",
    )(tokens, weights, gain_in, gain_q, gain_k, cosine, sine)


def backward_kernel(
    query, key, value, raw, grad_rows, gain_q, gain_k, cosine, sine,
    mixed, mixed_local, query_gain, key_gain, grad, key_sum, value_sum,
):
    low = jnp.bfloat16
    total, heads = query.shape[0], query.shape[1] // HEAD
    block = 256
    reorder_rows(grad_rows, grad, False)
    query_gain[...] = jnp.zeros_like(query_gain)
    key_gain[...] = jnp.zeros_like(key_gain)

    def head_norm_back(rows, column, gradient, gain, gain_grad):
        values = raw[rows, column]
        factor = inverse_rms(values)
        unit = values * factor
        turned = turn_back(gradient, cosine[rows, :], sine[rows, :])
        gain_grad[...] += jnp.sum(turned * unit, 0, keepdims=True)
        mixed[rows, column] = norm_back(turned * gain[...], unit, factor).astype(low)

    def one_group(group, carry):
        at = lambda offset: pl.ds(pl.multiple_of(group * 4 * HEAD + offset * HEAD, HEAD), HEAD)
        shared = pl.ds(pl.multiple_of(group * HEAD, HEAD), HEAD)
        key_sum[...] = jnp.zeros_like(key_sum)
        value_sum[...] = jnp.zeros_like(value_sum)
        for head in (0, 1):
            mine = pl.ds(pl.multiple_of((group * 2 + head) * HEAD, HEAD), HEAD)
            for start in range(0, total, SEQ):
                for first in range(0, SEQ, block):
                    rows, keys = pl.ds(start + first, block), pl.ds(start, first + block)
                    query_part, grad_part = query[rows, mine], grad[rows, mine]
                    probs = softmax_block(query_part, key[keys, shared], first)
                    weighed = probs * dot(grad_part, value[keys, shared], 1, 1)
                    scores = weighed - probs * jnp.sum(weighed, -1, keepdims=True)
                    scores = scores.astype(low)
                    grad_query = dot(scores, key[keys, shared]) * (1.0 / math.sqrt(HEAD))
                    head_norm_back(rows, at(head), grad_query, gain_q, query_gain)
                    key_sum[keys, :] += dot(scores, query_part, 0, 0)
                    value_sum[keys, :] += dot(probs.astype(low), grad_part, 0, 0)
        for first in range(0, total, block):
            rows = pl.ds(first, block)
            head_norm_back(rows, at(2), key_sum[rows, :], gain_k, key_gain)
            mixed[rows, at(3)] = value_sum[rows, :].astype(low)
        return carry

    lax.fori_loop(0, heads // 2, one_group, 0)
    reorder_rows(mixed, mixed_local, True)


def attention_back(query, key, value, raw, grad_rows, gain_q, gain_k, cosine, sine):
    total, columns = raw.shape
    low = jnp.bfloat16
    vmem = pl.BlockSpec(memory_space=pltpu.VMEM)
    return pl.pallas_call(
        backward_kernel,
        out_shape=[
            jax.ShapeDtypeStruct((total, columns), low),
            jax.ShapeDtypeStruct((total, columns), low),
            jax.ShapeDtypeStruct((1, HEAD), jnp.float32),
            jax.ShapeDtypeStruct((1, HEAD), jnp.float32),
        ],
        in_specs=[vmem] * 9,
        out_specs=[vmem] * 4,
        scratch_shapes=[
            pltpu.VMEM(grad_rows.shape, low),
            pltpu.VMEM((total, HEAD), jnp.float32),
            pltpu.VMEM((total, HEAD), jnp.float32),
        ],
        compiler_params=pltpu.CompilerParams(vmem_limit_bytes=48 * 2**20),
        cost_estimate=pl.CostEstimate(flops=10**10, bytes_accessed=2 * 10**7, transcendentals=0),
        name="attention_back",
    )(query, key, value, raw, grad_rows, gain_q, gain_k, cosine, sine)


def feed_kernel(plan, rows, own_grad, got_grad, gate_up, up_part, down, active, grads, out_grad):
    low = jnp.bfloat16
    block = 512
    tile = down.shape[1]
    step = pl.program_id(0)
    gate_at = pl.ds(pl.multiple_of(step * tile, tile), tile)
    up_at = pl.ds(pl.multiple_of(grads.shape[1] // 2 + step * tile, tile), tile)
    _, side, _, core = place_here()

    def lay_down(source):
        natural, blocks = block_columns(plan, source.shape[1])
        eighth = source.shape[0] // 8
        for slot, owner in enumerate(eighth_owners()):

            def some(start, count, slot=slot, owner=owner):
                here = pl.ds(pl.multiple_of(owner * eighth + start, 32), count)
                there = pl.ds(slot * eighth + start, count)
                for a, b in zip(natural, blocks):
                    out_grad[there, b] = source[here, a]

            for_rows(eighth, some)

    @pl.when((step == 0) & (side == core))
    def _():
        lay_down(own_grad)

    @pl.when((step == 0) & (side != core))
    def _():
        lay_down(got_grad)

    def one(block_at, carry):
        here = pl.ds(pl.multiple_of(block_at * block, block), block)
        gate = dot(rows[here, :], gate_up[...])
        up = dot(rows[here, :], up_part[...])
        grad = dot(out_grad[here, :], down[...])
        sigmoid = jax.nn.sigmoid(gate)
        silu = gate * sigmoid
        active[here, :] = (silu * up).astype(low)
        grads[here, gate_at] = (grad * up * sigmoid * (1.0 + gate * (1.0 - sigmoid))).astype(low)
        grads[here, up_at] = (grad * silu).astype(low)
        return carry

    lax.fori_loop(0, rows.shape[0] // block, one, 0)


def feed_forward(plan, rows, own_grad, got_grad, gate_up, down, tile):
    total, width = rows.shape
    units = down.shape[1]
    low = jnp.bfloat16
    tiles = units // tile
    whole = pl.BlockSpec(memory_space=pltpu.VMEM)
    return pl.pallas_call(
        functools.partial(feed_kernel, plan),
        grid=(tiles,),
        out_shape=[
            jax.ShapeDtypeStruct((total, units), low),
            jax.ShapeDtypeStruct((total, 2 * units), low),
            jax.ShapeDtypeStruct((total, width), low),
        ],
        in_specs=[
            whole,
            whole,
            whole,
            pl.BlockSpec((width, tile), lambda step: (0, step)),
            pl.BlockSpec((width, tile), lambda step: (0, step + tiles)),
            pl.BlockSpec((width, tile), lambda step: (0, step)),
        ],
        out_specs=[
            pl.BlockSpec((total, tile), lambda step: (0, step)),
            whole,
            whole,
        ],
        compiler_params=pltpu.CompilerParams(vmem_limit_bytes=56 * 2**20),
        cost_estimate=pl.CostEstimate(
            flops=6 * total * width * units, bytes_accessed=4 * 10**7, transcendentals=total * units
        ),
        name="feed_forward",
    )(rows, own_grad, got_grad, gate_up, gate_up, down)


class Plan:
    def __init__(self, mesh):
        self.total = mesh.shape["dp"]
        self.zones = self.total // 2
        self.tensor = mesh.shape["tensor"]
        self.flips = [k ^ (k >> 1) for k in range(self.zones)]

    def place(self):
        self.index = lax.axis_index("dp")
        self.zone = self.index // 2
        self.side = self.index % 2
        self.row = lax.axis_index("tensor") // 2
        self.core = lax.axis_index("tensor") % 2
        self.home = self.side == self.core

    def move(self, value, target):
        pairs = []
        for d in range(self.total):
            for t in range(self.tensor):
                to = target(d // 2, d % 2, t // 2, t % 2)
                if to is not None:
                    zone, side, row, core = to
                    pairs.append((d * self.tensor + t, (zone * 2 + side) * self.tensor + row * 2 + core))
        return lax.ppermute(value, ("dp", "tensor"), pairs)

    def turn(self, value):
        got = self.move(value, lambda z, y, x, c: (z, c, x, y) if y != c else None)
        return jnp.where(self.home, value, got)

    def zone_flip(self, value, bit):
        return self.move(value, lambda z, y, x, c: (z ^ bit, y, x, c))

    def core_swap(self, value):
        return self.move(value, lambda z, y, x, c: (z, y, x, 1 - c))

    def side_swap(self, value):
        return self.move(value, lambda z, y, x, c: (z, 1 - y, x, c))

    def row_swap(self, value):
        return self.move(value, lambda z, y, x, c: (z, y, 1 - x, c))

    def to_local(self, value, axis):
        width = value.shape[axis] // self.total
        parts = []
        for core in (self.core, 1 - self.core):
            for slot in range(self.zones):
                owner = (self.zone ^ self.flips[slot]) * 2 + core
                parts.append(lax.dynamic_slice_in_dim(value, owner * width, width, axis))
        return jnp.concatenate(parts, axis)

    def to_natural(self, value, axis, core=None):
        core = self.core if core is None else core
        width = value.shape[axis] // self.total
        parts = []
        for block in range(self.total):
            slot = flip = (block // 2) ^ self.zone
            for bits in range(1, self.zones.bit_length()):
                slot = slot ^ (flip >> bits)
            slot = slot + jnp.where(block % 2 == core, 0, self.zones)
            parts.append(lax.dynamic_slice_in_dim(value, slot * width, width, axis))
        return jnp.concatenate(parts, axis)

    def row_owners(self):
        own, off = (self.row, self.side), (1 - self.row, 1 - self.side)
        first = lambda x, y: x * 2 + y
        second = lambda x, y: 4 + y * 2 + x
        return [
            first(own[0], own[1]),
            first(own[0], off[1]),
            second(own[0], own[1]),
            second(off[0], own[1]),
            first(off[0], own[1]),
            first(off[0], off[1]),
            second(own[0], off[1]),
            second(off[0], off[1]),
        ]

    def rows_local(self, value, slots=range(8)):
        size = value.shape[0] // 8
        owners = self.row_owners()
        return jnp.concatenate(
            [lax.dynamic_slice_in_dim(value, owners[slot] * size, size, 0) for slot in slots], 0
        )

    def rows_natural(self, value, order=range(8)):
        size = value.shape[0] // 8
        place = [list(order).index(slot) for slot in range(8)]
        parts = []
        for piece in range(8):
            x, y = (piece // 2, piece % 2) if piece < 4 else (piece % 2, (piece - 4) // 2)
            slots = (0, 1, 4, 5) if piece < 4 else (2, 6, 3, 7)
            same_x, same_y = x == self.row, y == self.side
            slot = jnp.where(
                same_x,
                jnp.where(same_y, place[slots[0]], place[slots[1]]),
                jnp.where(same_y, place[slots[2]], place[slots[3]]),
            )
            parts.append(lax.dynamic_slice_in_dim(value, slot * size, size, 0))
        return jnp.concatenate(parts, 0)

    def from_zones(self, shard):
        return [self.zone_flip(shard, flip) for flip in self.flips[1:]]

    def to_zones(self, parts, slots):
        return [self.zone_flip(parts[slot], self.flips[slot]) for slot in slots]

    def middle_swap(self, pair):
        return self.move(pair, lambda z, y, x, c: (z ^ 3, y, x, c) if z in (1, 2) else None)

    def inward(self, part):
        return self.move(part, lambda z, y, x, c: (z ^ 1, y, x, c) if z in (0, 3) else None)

    def pass_outward(self, pair):
        return self.move(pair, lambda z, y, x, c: (z ^ 1, y, x, c) if z in (1, 2) else None)

    def far_pair(self, middle, passed):
        inner = (self.zone == 1) | (self.zone == 2)
        return jnp.where(inner, middle, passed[::-1])

    def first_swap(self, send):
        half = send.shape[0] // 2
        return self.row_swap(send[:half]), self.side_swap(send[half:])

    def second_swap(self, keep, got):
        quarter = keep.shape[0] // 4
        row_part = keep[: 2 * quarter] + got[0].astype(jnp.float32)
        side_part = keep[2 * quarter :] + got[1].astype(jnp.float32)
        own = jnp.concatenate([row_part[:quarter], side_part[:quarter]], 0)
        return own, (
            self.side_swap(row_part[quarter:].astype(jnp.bfloat16)),
            self.row_swap(side_part[quarter:].astype(jnp.bfloat16)),
        )

    def spread_first(self, own):
        half = own.shape[0] // 2
        return (self.side_swap(own[:half]), self.row_swap(own[half:]))

    def spread_second(self, own, got):
        half = own.shape[0] // 2
        row_part = jnp.concatenate([own[:half], got[0]], 0)
        side_part = jnp.concatenate([own[half:], got[1]], 0)
        return row_part, side_part, self.row_swap(row_part), self.side_swap(side_part)

    def send_home(self, own):
        to_home = lambda z, y, x, c: (z, c, x, c) if y != c else None
        return jnp.concatenate([own, self.move(own, to_home)], 0)

    def row_home(self, part):
        return self.move(part, lambda z, y, x, c: (z, y, 1 - x, c) if y == c else None)

    def share_home(self, part, other):
        full = jnp.concatenate([part, other], 0)
        full = self.to_natural(self.rows_natural(full, (0, 2, 1, 6, 4, 3, 5, 7)), 1)
        got = self.move(full, lambda z, y, x, c: (z, y, x, 1 - c) if y == c else None)
        return full, got

    def turned(self, own, got):
        return jnp.where(self.home, own, got)

    def sum_everywhere(self, value):
        value = value + self.row_swap(value)
        value = value + self.side_swap(value)
        value = value + self.core_swap(value)
        bit = 1
        while bit < self.zones:
            value = value + self.zone_flip(value, bit)
            bit *= 2
        return value


def shards(
    plan,
    tokens,
    positions,
    out_grad,
    qkv_weight,
    qkv_first,
    qkv_second,
    out_weight,
    out_first,
    out_second,
    gate_up,
    gate_up_first,
    gate_up_second,
    down_weight,
    down_first,
    down_second,
    gains,
    gains_first,
    gains_second,
):
    plan.place()
    low = jnp.bfloat16
    tok_rows, model_width = tokens.shape
    groups = qkv_weight.shape[1]
    head_size = qkv_weight.shape[3]
    shard_rows = qkv_weight.shape[0]
    seq_count = tok_rows // SEQ
    mixed_cols = groups * 4 * head_size
    near_cols = model_width // 2
    kept = tok_rows // 2
    gain_count = gains.shape[0]

    tree = plan.zones == 4
    slots = range(1, plan.zones)

    def column_parts(value):
        return value.reshape((plan.zones, -1) + value.shape[1:])

    units = gate_up.shape[2]
    plan.ordered = (model_width // plan.total) % 128 == 0
    gain_rows = 16
    gain_block = jnp.pad(gains.astype(low), (0, gain_rows * 128 - gain_count)).reshape(gain_rows, 128)
    tile = min(units, 256)
    angle_at = positions.astype(jnp.float32).reshape(-1, 128)
    both_qkv, both_gains, turned_gate, turned_out, tokens, angle_at, partner_gate = opening(
        plan,
        qkv_weight.reshape(shard_rows, mixed_cols),
        gain_block,
        gate_up,
        out_weight,
        tokens,
        angle_at,
        3,
    )
    positions = angle_at.reshape(-1)
    turned_out, turned_gate, tokens, positions, both_qkv, both_gains, low_down = fence(
        turned_out,
        turned_gate,
        tokens,
        positions,
        both_qkv,
        both_gains,
        down_weight.astype(low),
    )

    got_down = plan.move(low_down, lambda z, y, x, c: (z, c, x, y) if y != c else None)
    half_rows = shard_rows // 2
    zone_out = plan.from_zones(turned_out)
    if tree:
        partner_rest = plan.zone_flip(turned_gate[half_rows:], 1)
    else:
        partner_rest = partner_gate
        partner_gate = plan.from_zones(turned_gate)
    if not plan.ordered:
        tokens = plan.to_local(tokens, 1)
    cosine, sine_table = rotary(positions, head_size)
    signed_sine = jnp.concatenate(
        [-sine_table[:, : head_size // 2], sine_table[:, head_size // 2 :]], 1
    )
    full_qkv = both_qkv.reshape(model_width, mixed_cols)
    gain_slots = both_gains.reshape(plan.total, -1)[:, :gain_count]
    gain_all = plan.to_natural(gain_slots.reshape(-1), 0).astype(jnp.float32)
    gain_in = plan.to_local(gain_all[:model_width], 0)[None]
    gain_post = plan.to_local(gain_all[model_width : 2 * model_width], 0)[None]
    gain_q = gain_all[2 * model_width : 2 * model_width + head_size][None]
    gain_k = gain_all[2 * model_width + head_size :][None]
    normed, raw, query, key_rot, values_low, attended = attention(
        tokens, full_qkv, gain_in, gain_q, gain_k, cosine, signed_sine
    )
    turned_down = plan.turned(low_down, got_down)
    attended, zone_out, turned_out, turned_down, turned_gate, partner_gate, partner_rest = fence(
        attended, zone_out, turned_out, turned_down, turned_gate, partner_gate, partner_rest
    )

    near_out = jnp.concatenate([turned_out] + zone_out, 0)
    far_out = plan.core_swap(near_out)
    own_tokens = plan.rows_local(tokens, (0, 2))
    near_out, far_out, own_tokens = fence(near_out, far_out, own_tokens)

    full_out = jnp.concatenate([near_out, far_out], 0)
    branch_terms = contract_cols(attended, full_out).astype(low)
    if tree:
        pairs = [(turned_gate, jnp.concatenate([partner_gate, partner_rest], 0)), (turned_down,)]
    else:
        pairs = [(turned_gate, partner_gate), (turned_down, plan.from_zones(turned_down))]
    jobs = [TurnRows(out_grad)] + ([PairTree(pairs, (2, 2))] if tree else [])
    normed_rows, hidden, got_grad, *gathered = sum_rows(
        spread_kernel,
        hidden_rows,
        branch_terms,
        [own_tokens, gain_post],
        [jax.ShapeDtypeStruct((tok_rows // 4, model_width), jnp.float32)],
        0,
        jobs,
    )
    if not tree:
        near = [jnp.concatenate([own] + rest, 0) for own, rest in pairs]
        gathered = [jnp.concatenate([part, plan.core_swap(part)], 0) for part in near]
    full_gate = gathered[0].reshape(model_width, 2 * units)
    full_down = gathered[1].reshape(model_width, units)
    normed_rows, hidden, full_gate, full_down, got_grad = fence(
        normed_rows, hidden, full_gate, full_down, got_grad
    )

    def zone_parts(near, got):
        both = (near + got.astype(jnp.float32)).astype(low)
        return both.reshape((plan.zones, -1) + both.shape[1:])

    def zone_total(parts, *arrived):
        total = parts[0].astype(jnp.float32)
        for part in sum([list(group) for group in arrived], []):
            total = total + part.astype(jnp.float32)
        return total.astype(low)

    active, grad_both, out_grad = feed_forward(
        plan, normed_rows, out_grad, got_grad, full_gate, full_down, tile
    )
    if not plan.ordered:
        out_grad = plan.to_local(out_grad, 1)
    mlp_terms = contract_cols(active, full_down).astype(low)
    mlp_terms, active, grad_both, out_grad = fence(mlp_terms, active, grad_both, out_grad)

    mlp_got = plan.first_swap(mlp_terms[kept:])
    down_far = contract_rows(out_grad[:, near_cols:], active).astype(low)
    down_got = plan.core_swap(down_far)
    gate_far = contract_rows(normed_rows[:, near_cols:], grad_both).astype(low)
    down_parts = zone_parts(contract_rows(out_grad[:, :near_cols], active), down_got)
    down_parts, gate_far, grad_both, mlp_got, mlp_terms = fence(
        down_parts, gate_far, grad_both, mlp_got, mlp_terms
    )

    gate_got = plan.core_swap(gate_far)
    if tree:
        inner_terms = plan.inward(down_parts[3])
    else:
        inner_terms = plan.to_zones(down_parts, slots)
    mlp_own, mlp_last = plan.second_swap(mlp_terms[:kept].astype(jnp.float32), mlp_got)
    post_terms = contract_cols(grad_both, full_gate).astype(low)
    mlp_own, mlp_last, post_terms, gate_got, inner_terms, down_parts, normed_rows, grad_both = fence(
        mlp_own, mlp_last, post_terms, gate_got, inner_terms, down_parts, normed_rows, grad_both
    )

    block_own = (hidden + mlp_own + jnp.concatenate(mlp_last, 0).astype(jnp.float32)).astype(low)
    block_home = plan.send_home(block_own)
    down_sums = jnp.stack([inner_terms, plan.inward(down_parts[2])]) if tree else inner_terms
    gate_parts = zone_parts(contract_rows(normed_rows[:, :near_cols], grad_both), gate_got)
    post_terms, gate_parts, down_parts, down_sums, block_home = fence(
        post_terms, gate_parts, down_parts, down_sums, block_home
    )

    eighth = tok_rows // 8
    own_grad = jnp.concatenate([out_grad[:eighth], out_grad[2 * eighth : 3 * eighth]], 0)
    branch_rows, grad_hidden, post_gain_grad, gate_sums = sum_rows(
        spread_kernel,
        grad_hidden_rows,
        post_terms,
        [hidden, own_grad, gain_post],
        [
            jax.ShapeDtypeStruct((tok_rows // 4, model_width), jnp.float32),
            jax.ShapeDtypeStruct((1, model_width), jnp.float32),
        ],
        1,
        [PairScatter(gate_parts, 2) if tree else ZoneBlocks(plan, gate_parts, slots)],
    )
    if tree:
        down_pair = (down_parts[2:].astype(jnp.float32) + down_sums.astype(jnp.float32)).astype(low)
    else:
        down_pair = down_parts
    branch_rows, grad_hidden, post_gain_grad, gate_sums, block_home, down_parts, down_pair = fence(
        branch_rows, grad_hidden, post_gain_grad, gate_sums, block_home, down_parts, down_pair
    )

    block_row = plan.row_home(block_home)
    if tree:
        gate_last = [plan.zone_flip(gate_sums[1], 1)]
        gate_own = gate_sums
        down_sums = plan.middle_swap(down_pair)
    else:
        gate_last, gate_own = gate_sums, gate_parts
    grad_att = jnp.dot(branch_rows, full_out, preferred_element_type=jnp.float32).astype(low)
    grad_mixed, mixed_rows, query_gain_grad, key_gain_grad = attention_back(
        query, key_rot, values_low, raw, grad_att, gain_q, gain_k, cosine, signed_sine
    )
    gain_terms = jnp.concatenate(
        [plan.to_natural(post_gain_grad, 1), query_gain_grad, key_gain_grad], 1
    )
    if tree:
        down_own = (down_parts[:2].astype(jnp.float32) + down_sums.astype(jnp.float32)).astype(low)
    grad_mixed, mixed_rows, gain_terms, normed, gate_last, branch_rows, block_row, down_sums = fence(
        grad_mixed, mixed_rows, gain_terms, normed, gate_last, branch_rows, block_row, down_sums
    )

    if tree:
        total_down = zone_total(down_own, [plan.zone_flip(down_own[1], 1)])
    else:
        total_down = zone_total(down_parts, down_sums)
    total_gate = zone_total(gate_own, gate_last)
    out_far = contract_rows(branch_rows[:, near_cols:], attended).astype(low)
    out_got = plan.core_swap(out_far)
    normed_terms = contract_cols(mixed_rows, full_qkv).astype(low)
    out_parts = zone_parts(contract_rows(branch_rows[:, :near_cols], attended), out_got)
    out_parts, normed_terms, total_gate, total_down, block_row, normed, grad_mixed = fence(
        out_parts, normed_terms, total_gate, total_down, block_row, normed, grad_mixed
    )

    gain_sum = GainSum(plan, gain_terms.shape[1], model_width) if plan.ordered else None
    input_full, input_gain_grad, *rest = sum_rows(
        home_kernel,
        grad_input_rows,
        normed_terms,
        [own_tokens, grad_hidden, gain_in] + ([gain_terms] if plan.ordered else []),
        [jax.ShapeDtypeStruct((1, model_width), jnp.float32)],
        2,
        [BlockGrad(plan, normed, grad_mixed), ZoneBlocks(plan, out_parts, slots)],
        gain_sum,
    )
    if plan.ordered:
        summed_gains, total_qkv, out_sent = rest
    else:
        total_qkv, out_sent = rest
        summed_gains = plan.sum_everywhere(
            jnp.concatenate([plan.to_natural(input_gain_grad, 1), gain_terms], 1)
        )
    input_full, summed_gains, total_qkv, out_sent, total_gate, total_down, block_row = fence(
        input_full, summed_gains, total_qkv, out_sent, total_gate, total_down, block_row
    )

    summed_down = plan.turn(total_down)
    summed_gate = plan.turn(jnp.stack([total_gate[:, :units], total_gate[:, units:]]))
    block_full, block_got = plan.share_home(block_home, block_row)
    block_out = jnp.where(plan.home, block_full, block_got)
    summed_both = plan.turn(
        jnp.concatenate([total_qkv, zone_total(out_parts, out_sent)], 1)
    ).astype(jnp.float32)
    summed_qkv = summed_both[:, :mixed_cols].reshape(qkv_weight.shape)
    summed_out = summed_both[:, mixed_cols:]
    summed_gate = summed_gate.astype(jnp.float32)
    summed_down = summed_down.astype(jnp.float32)
    summed_gains = lax.dynamic_slice_in_dim(summed_gains[0], plan.index * gain_count, gain_count, 0)
    input_rows = plan.to_natural(input_full, 1, plan.side).astype(jnp.float32)

    qkv_moment, qkv_square, qkv_updated = adamw(
        qkv_weight, summed_qkv, qkv_first, qkv_second, RATE_QKV, DECAY_RATE
    )
    out_moment, out_square, out_updated = adamw(
        out_weight, summed_out, out_first, out_second, RATE_OUT, DECAY_RATE
    )
    gate_moment, gate_square, gate_updated = adamw(
        gate_up, summed_gate, gate_up_first, gate_up_second, RATE_GATE, DECAY_RATE
    )
    down_moment, down_square, down_updated = adamw(
        down_weight, summed_down, down_first, down_second, RATE_DOWN, DECAY_RATE
    )
    gain_moment, gain_square, gain_updated = adamw(
        gains, summed_gains, gains_first, gains_second, RATE_GAIN, 0.0
    )
    return (
        block_out,
        input_rows,
        qkv_moment,
        qkv_square,
        qkv_updated,
        out_moment,
        out_square,
        out_updated,
        gate_moment,
        gate_square,
        gate_updated,
        down_moment,
        down_square,
        down_updated,
        gain_moment,
        gain_square,
        gain_updated,
    )


def solution(mesh):
    plan = Plan(mesh)
    placed = (
        P("dp", None),
        P("dp"),
        P("dp", None),
        P("dp", "tensor", None, None),
        P("dp", "tensor", None, None),
        P("dp", "tensor", None, None),
        P("dp", "tensor"),
        P("dp", "tensor"),
        P("dp", "tensor"),
        P(None, "dp", "tensor"),
        P(None, "dp", "tensor"),
        P(None, "dp", "tensor"),
        P("dp", "tensor"),
        P("dp", "tensor"),
        P("dp", "tensor"),
        P("dp"),
        P("dp"),
        P("dp"),
    )
    return jax.shard_map(
        functools.partial(shards, plan),
        mesh=mesh,
        in_specs=placed,
        out_specs=(
            P("dp", None),
            P("dp", None),
            P("dp", "tensor", None, None),
            P("dp", "tensor", None, None),
            P("dp", "tensor", None, None),
            P("dp", "tensor"),
            P("dp", "tensor"),
            P("dp", "tensor"),
            P(None, "dp", "tensor"),
            P(None, "dp", "tensor"),
            P(None, "dp", "tensor"),
            P("dp", "tensor"),
            P("dp", "tensor"),
            P("dp", "tensor"),
            P("dp"),
            P("dp"),
            P("dp"),
        ),
        check_vma=False,
    )
```

```python
import functools
import math

import jax
import jax.numpy as jnp
from jax import lax
from jax.experimental import pallas as pl
from jax.experimental.pallas import tpu as pltpu
from jax.sharding import PartitionSpec as P

SEQ = 1024
STEP = 10


EPS_NORM = 1e-06
THETA = 1000000.0
BETA_ONE = 0.9
BETA_TWO = 0.95
ADAM_EPS = 1e-08
DECAY_RATE = 0.1
RATE_QKV = 0.05
RATE_OUT = 0.3
RATE_GATE = 0.05
RATE_DOWN = 0.03
RATE_GAIN = 1.0


def rotary(positions, head_size):
    freq_index = jnp.arange(head_size // 2, dtype=jnp.float32)
    inverse = jnp.exp(freq_index * (-2.0 * math.log(THETA) / head_size))
    angles = positions.astype(jnp.float32)[:, None] * inverse[None, :]
    cosine = jnp.cos(angles)
    sine_table = jnp.sin(angles)
    return (jnp.concatenate([cosine, cosine], -1), jnp.concatenate([sine_table, sine_table], -1))


def rotate(values, cosine, sine_table):
    half_size = values.shape[-1] // 2
    turned = jnp.concatenate([-values[..., half_size:], values[..., :half_size]], -1)
    return values * cosine[:, None, :] + turned * sine_table[:, None, :]


def unrotate(gradient, cosine, sine_table):
    half_size = gradient.shape[-1] // 2
    turned = gradient * sine_table[:, None, :]
    rotated_back = jnp.concatenate([turned[..., half_size:], -turned[..., :half_size]], -1)
    return gradient * cosine[:, None, :] + rotated_back


def norm_back(grad_unit, unit_vals, factor):
    return factor * (grad_unit - unit_vals * jnp.mean(grad_unit * unit_vals, -1, keepdims=True))


def contract_rows(left, right):
    return lax.dot_general(
        left, right, (((0,), (0,)), ((), ())), preferred_element_type=jnp.float32
    )


def contract_cols(left, right):
    return lax.dot_general(
        left, right, (((1,), (1,)), ((), ())), preferred_element_type=jnp.float32
    )


def block_scores(query_part, key_part, first_row, block_rows, last_row):
    scores = jnp.einsum(
        "nqkgd,nskd->nkgqs", query_part, key_part, preferred_element_type=jnp.float32
    )
    causal = (first_row + jnp.arange(block_rows))[:, None] >= jnp.arange(last_row)[None, :]
    return jnp.where(causal, scores, -1000000000.0)


def attention_forward(query, key_rot, values_low, seq_len):
    block_rows = min(512, seq_len)
    outputs = []
    log_sums = []
    for first_row in range(0, seq_len, block_rows):
        last_row = first_row + block_rows
        query_part = query[:, first_row:last_row]
        scores = block_scores(query_part, key_rot[:, :last_row], first_row, block_rows, last_row)
        row_max = jnp.max(scores, -1, keepdims=True)
        exponent = jnp.exp(scores - row_max)
        row_total = jnp.sum(exponent, -1, keepdims=True)
        probs_low = (exponent / row_total).astype(jnp.bfloat16)
        outputs.append(
            jnp.einsum(
                "nkgqs,nskd->nqkgd",
                probs_low,
                values_low[:, :last_row],
                preferred_element_type=jnp.float32,
            )
        )
        log_sums.append(row_max + jnp.log(row_total))
    return (jnp.concatenate(outputs, 1), log_sums)


def attention_backward(query, key_rot, values_low, grad_att, log_sums, seq_len):
    block_rows = min(512, seq_len)
    query_grads = []
    key_grad = jnp.zeros(key_rot.shape, jnp.float32)
    value_grad = jnp.zeros(values_low.shape, jnp.float32)
    for block_index, first_row in enumerate(range(0, seq_len, block_rows)):
        last_row = first_row + block_rows
        query_part = query[:, first_row:last_row]
        grad_part = grad_att[:, first_row:last_row]
        key_part = key_rot[:, :last_row]
        value_part = values_low[:, :last_row]
        scores = block_scores(query_part, key_part, first_row, block_rows, last_row)
        probs = jnp.exp(scores - log_sums[block_index])
        probs_low = probs.astype(jnp.bfloat16)
        grad_probs = jnp.einsum(
            "nqkgd,nskd->nkgqs", grad_part, value_part, preferred_element_type=jnp.float32
        )
        grad_scores = (
            probs * (grad_probs - jnp.sum(probs * grad_probs, -1, keepdims=True))
        ).astype(jnp.bfloat16)
        query_grads.append(
            jnp.einsum(
                "nkgqs,nskd->nqkgd", grad_scores, key_part, preferred_element_type=jnp.float32
            )
        )
        padding = ((0, 0), (0, seq_len - last_row), (0, 0), (0, 0))
        key_grad = key_grad + jnp.pad(
            jnp.einsum(
                "nkgqs,nqkgd->nskd", grad_scores, query_part, preferred_element_type=jnp.float32
            ),
            padding,
        )
        value_grad = value_grad + jnp.pad(
            jnp.einsum(
                "nkgqs,nqkgd->nskd", probs_low, grad_part, preferred_element_type=jnp.float32
            ),
            padding,
        )
    return (jnp.concatenate(query_grads, 1), key_grad, value_grad)


def adamw(weight, gradient, moment, second, step_rate, decay_rate):
    moment = BETA_ONE * moment + (1.0 - BETA_ONE) * gradient
    second = BETA_TWO * second + (1.0 - BETA_TWO) * gradient * gradient
    first_hat = moment / (1.0 - BETA_ONE**STEP)
    second_hat = second / (1.0 - BETA_TWO**STEP)
    weight = weight - step_rate * (
        first_hat / (jnp.sqrt(second_hat) + ADAM_EPS) + decay_rate * weight
    )
    return (moment, second, weight)


def fence(*values):
    return lax.optimization_barrier(values)


MESH = pl.DeviceIdType.MESH
HEAD = 128
AHEAD = 2


def place_here():
    index, place = lax.axis_index("dp"), lax.axis_index("tensor")
    return lax.div(index, 2), lax.rem(index, 2), lax.div(place, 2), lax.rem(place, 2)


def device(zone, side, row, core):
    return (zone * 2 + side, row * 2 + core)


def flipped(zone, flip):
    bit = 1
    while bit <= flip:
        if flip & bit:
            zone = zone + bit - 2 * bit * lax.rem(lax.div(zone, bit), 2)
        bit *= 2
    return zone


def greet(devices, amount=None):
    barrier = pltpu.get_barrier_semaphore()
    for peer in devices:
        pl.semaphore_signal(barrier, inc=1, device_id=peer, device_id_type=MESH)
    pl.semaphore_wait(barrier, len(devices) if amount is None else amount)


def for_rows(count, body):
    step = 32

    def one(block, carry):
        body(pl.multiple_of(block * step, step), step)
        return carry

    lax.fori_loop(0, count // step, one, 0)


class Copies:
    def __init__(self, send_sems, recv_sems):
        self.send_sems, self.recv_sems = send_sems, recv_sems
        self.number = 0

    def make(self, source, target, peer):
        number, self.number = self.number, self.number + 1
        return pltpu.make_async_remote_copy(
            src_ref=source,
            dst_ref=target,
            send_sem=self.send_sems.at[number],
            recv_sem=self.recv_sems.at[number],
            device_id=peer,
            device_id_type=MESH,
        )

    def start(self, source, target, peer):
        copy = self.make(source, target, peer)
        copy.start()
        return copy


class GainSum:
    def __init__(self, plan, rest, width):
        self.plan, self.width = plan, width
        self.total = width + rest
        self.scratch = [
            pltpu.VMEM((8, 1, self.total), jnp.float32),
            pltpu.VMEM((plan.zones, 1, self.total), jnp.float32),
        ]
        self.output = jax.ShapeDtypeStruct((1, self.total), jnp.float32)
        self.count = 7 + plan.zones - 1

    def plane_peers(self, zone, side, row, core):
        steps = [(s, r, c) for s in range(2) for r in range(2) for c in range(2)][1:]
        turn = lambda value, step: 1 - value if step else value
        return [device(zone, turn(side, s), turn(row, r), turn(core, c)) for s, r, c in steps]

    def zone_peers(self, zone, side, row, core):
        return {flip: device(flipped(zone, flip), side, row, core) for flip in self.plan.flips[1:]}

    def start(self, copies, rest, blocks, plane_sums, zone_sums):
        zone, side, row, core = place_here()
        plan = self.plan
        size = self.width // plan.total
        self.copies, self.plane_sums, self.zone_sums, self.zone = copies, plane_sums, zone_sums, zone
        here = side * 4 + row * 2 + core
        plane_sums[here, :, pl.ds(self.width, self.total - self.width)] = rest[...]
        for slot in range(plan.total):
            owner = flipped(zone, plan.flips[slot % plan.zones]) * 2
            owner = owner + (core if slot < plan.zones else 1 - core)
            spot = pl.ds(pl.multiple_of(owner * size, size), size)
            plane_sums[here, :, spot] = blocks[:, pl.ds(slot * size, size)]
        self.plane = [
            copies.start(plane_sums.at[here], plane_sums.at[here], peer)
            for peer in self.plane_peers(zone, side, row, core)
        ]

    def middle(self):
        for copy in self.plane:
            copy.wait_recv()
        total = self.plane_sums[0]
        for place in range(1, 8):
            total = total + self.plane_sums[place]
        self.zone_sums[self.zone] = total
        zone, side, row, core = place_here()
        self.across = [
            self.copies.start(self.zone_sums.at[self.zone], self.zone_sums.at[self.zone], peer)
            for peer in self.zone_peers(zone, side, row, core).values()
        ]

    def finish(self, out):
        for copy in self.across:
            copy.wait_recv()
        total = self.zone_sums[0]
        for place in range(1, self.plan.zones):
            total = total + self.zone_sums[place]
        out[...] = total
        for copy in self.plane + self.across:
            copy.wait_send()


class ZoneBlocks:
    scratch = []

    def __init__(self, plan, source, slots, begin=0):
        self.flips, self.slots, self.sources, self.begin = plan.flips, list(slots), [source], begin
        self.outputs = [
            jax.ShapeDtypeStruct((len(self.slots),) + source.shape[1:], source.dtype)
        ]
        self.count, self.count_local = len(self.slots), 0
        self.in_hbm = False

    def peers(self, zone, side, row, core):
        return {
            self.flips[slot]: device(flipped(zone, self.flips[slot]), side, row, core)
            for slot in self.slots
        }

    def start(self, copies, local_sems, sources, targets, stages):
        zone, side, row, core = place_here()
        self.started = [
            copies.make(
                sources[0].at[slot],
                targets[0].at[number],
                device(flipped(zone, self.flips[slot]), side, row, core),
            )
            for number, slot in enumerate(self.slots)
        ]
        self.waiting = True
        if self.begin == 0:
            self.pump([0])

    def pump(self, steps):
        if self.waiting and self.begin in steps:
            self.waiting = False
            for copy in self.started:
                copy.start()

    def finish(self):
        for copy in self.started:
            copy.wait_send()
        for copy in self.started:
            copy.wait_recv()


def inner_zone(zone):
    return lax.rem(lax.div(zone + 1, 2), 2)


class SideDot:
    count, count_local, scratch, in_hbm = 0, 0, [], False

    def __init__(self, left, right):
        self.sources = [left, right]
        self.outputs = [jax.ShapeDtypeStruct((left.shape[0], right.shape[0]), jnp.bfloat16)]

    def peers(self, zone, side, row, core):
        return {}

    def some(self, first, last):
        left, right = self.refs
        size = 256

        def one(step, carry):
            here = pl.ds(pl.multiple_of(step * size, size), size)
            self.out[:, here] = dot(left[...], right[here, :], 1, 1).astype(jnp.bfloat16)
            return carry

        lax.fori_loop(first, last, one, 0)

    def start(self, copies, local_sems, sources, targets, stages):
        self.refs, self.out = sources, targets[0]
        self.steps = self.out.shape[1] // 256
        self.some(0, self.steps // 2)

    def pump(self, steps):
        if 0 in steps:
            self.some(self.steps // 2, self.steps)

    def finish(self):
        pass


class PairScatter:
    def __init__(self, parts, ready, pieces):
        self.sources, self.pieces = [parts, ready], pieces
        _, rows, columns = parts.shape
        self.size = rows // pieces
        self.outputs = [jax.ShapeDtypeStruct((2, rows, columns), parts.dtype)]
        self.scratch = [pltpu.VMEM((2, rows, columns), parts.dtype)] * 2
        self.count, self.count_local = 3 * pieces, 0
        self.in_hbm = False

    def peers(self, zone, side, row, core):
        return {
            1: device(flipped(zone, 1), side, row, core),
            3: device(flipped(zone, 3), side, row, core),
        }

    def start(self, copies, local_sems, sources, targets, stages):
        zone, side, row, core = place_here()
        self.parts, self.ready = sources
        self.out = targets[0]
        self.inward, self.crossed = stages
        inner_peer = device(flipped(zone, 3), side, row, core)
        outer_peer = device(flipped(zone, 1), side, row, core)
        self.inner = inner_zone(zone) == 1
        self.outer = inner_zone(zone) == 0
        pieces = [pl.ds(piece * self.size, self.size) for piece in range(self.pieces)]
        self.steps = [(slot, rows) for slot in (0, 1) for rows in pieces]
        self.to_inner = [
            copies.make(self.parts.at[2, rows], self.inward.at[1, rows], outer_peer)
            for rows in pieces
        ]
        self.across = [
            copies.make(self.inward.at[slot, rows], self.crossed.at[slot, rows], inner_peer)
            for slot, rows in self.steps
        ]

        @pl.when(self.outer)
        def _():
            for copy in self.to_inner[:AHEAD]:
                copy.start()

        @pl.when(self.inner)
        def _():
            for step in range(self.pieces):
                slot, rows = self.steps[step]
                self.add(self.inward, slot, rows, self.parts.at[2], self.ready)
                self.across[step].start()

    def add(self, target, slot, rows, left, right):
        def some(row, count):
            here = pl.ds(rows.start + row, count)
            both = left[here, :].astype(jnp.float32) + right[here, :].astype(jnp.float32)
            target.at[slot][here, :] = both.astype(jnp.bfloat16)

        for_rows(self.size, some)

    def pump(self, steps):
        steps = [step for step in steps if step < self.pieces]

        @pl.when(self.inner)
        def _():
            for step in steps:
                slot, rows = self.steps[self.pieces + step]
                self.to_inner[step].wait_recv()
                self.add(self.inward, slot, rows, self.parts.at[3], self.inward.at[1])
                self.across[self.pieces + step].start()
                self.settle(step)

        @pl.when(self.outer)
        def _():
            for step in steps:
                self.to_inner[step].wait_send()
                for copy in self.to_inner[step + AHEAD : step + AHEAD + 1]:
                    copy.start()

    def settle(self, step):
        slot, rows = self.steps[step]
        self.across[step].wait_recv()
        self.add(self.out, slot, rows, self.parts.at[slot], self.crossed.at[slot])

    def finish(self):
        @pl.when(self.inner)
        def _():
            for step in range(self.pieces, len(self.steps)):
                self.settle(step)
            for copy in self.across:
                copy.wait_send()

        @pl.when(self.outer)
        def _():
            for slot in (0, 1):

                def some(row, count, slot=slot):
                    here = pl.ds(row, count)
                    self.out.at[slot][here, :] = self.parts.at[slot][here, :]

                for_rows(self.parts.shape[1], some)


class BlockGrad:
    in_hbm = False

    def __init__(self, plan, left, right):
        self.zones, self.flips = plan.zones, plan.flips
        self.sources = [left, right]
        shape = (left.shape[1] // plan.total, right.shape[1])
        low = jnp.bfloat16
        self.outputs = [jax.ShapeDtypeStruct(shape, low)]
        self.scratch = [pltpu.VMEM((plan.zones,) + shape, low)] * 4
        self.count, self.count_local = 2 * plan.zones, 0

    def peers(self, zone, side, row, core):
        return {flip: device(flipped(zone, flip), side, row, core) for flip in self.flips[1:]}

    def product(self, block):
        size = self.out.shape[0]
        return dot(self.left[:, pl.ds(block * size, size)], self.right[...], 0, 0)

    def start(self, copies, local_sems, sources, targets, stages):
        zone, side, row, core = place_here()
        self.left, self.right = sources
        self.out = targets[0]
        self.far, self.got, self.parts, self.arrived = stages
        core_peer = device(zone, side, row, 1 - core)
        self.order = list(range(1, self.zones)) + [0]
        self.over = [
            copies.make(self.far.at[slot], self.got.at[slot], core_peer)
            for slot in range(self.zones)
        ]
        self.along = [
            copies.make(
                self.parts.at[slot],
                self.arrived.at[slot],
                device(flipped(zone, self.flips[slot]), side, row, core),
            )
            for slot in range(1, self.zones)
        ]
        for slot in self.order:
            self.far[slot] = self.product(self.zones + slot).astype(jnp.bfloat16)
            self.over[slot].start()

    def pump(self, steps):
        for slot in self.order if 0 in steps else []:
            near = self.product(slot)
            self.over[slot].wait_recv()
            self.parts[slot] = (near + self.got[slot].astype(jnp.float32)).astype(jnp.bfloat16)
            if slot:
                self.along[slot - 1].start()

    def finish(self):
        total = self.parts[0].astype(jnp.float32)
        for slot in range(1, self.zones):
            self.along[slot - 1].wait_recv()
            total = total + self.arrived[slot].astype(jnp.float32)
        self.out[...] = total.astype(jnp.bfloat16)
        for copy in self.over + self.along:
            copy.wait_send()


class PairTree:
    def __init__(self, pairs, pieces):
        self.pairs = [len(pair) for pair in pairs]
        self.sources = [shard for pair in pairs for shard in pair]
        self.pieces = pieces
        self.outputs = [
            jax.ShapeDtypeStruct((8,) + own.shape, own.dtype) for own, *_ in pairs
        ]
        self.count = 6 * sum(pieces) + 2 * len(pairs) + self.pairs.count(1)
        self.count_local = 2 * len(pairs) + 2 * sum(pieces)
        self.scratch = [pltpu.VMEM((2,) + own.shape, own.dtype) for own, *_ in pairs]
        self.scratch += [pltpu.VMEM(p[0].shape, p[0].dtype) for p in pairs if len(p) == 1]
        self.in_hbm = True

    def peers(self, zone, side, row, core):
        return {
            1: device(flipped(zone, 1), side, row, core),
            3: device(flipped(zone, 3), side, row, core),
            "core": device(zone, side, row, 1 - core),
        }

    def start(self, copies, local_sems, sources, targets, stages):
        zone, side, row, core = place_here()
        inner_peer = device(flipped(zone, 3), side, row, core)
        outer_peer = device(flipped(zone, 1), side, row, core)
        core_peer = device(zone, side, row, 1 - core)
        self.inner = inner_zone(zone) == 1
        self.outer = inner_zone(zone) == 0
        self.across, self.onward, self.late, self.place = [], [], [], []
        self.shared, self.kept, self.partners, self.later = [], [], [], []
        sem = 0
        sources, late_stages = list(sources), list(stages[len(targets) :])
        for weight, full in enumerate(targets):
            landing = stages[weight]
            pair = [sources.pop(0) for _ in range(self.pairs[weight])]
            if len(pair) == 1:
                pair.append(late_stages.pop(0))
                self.partners.append(copies.start(pair[0], pair[1], outer_peer))
            size = pair[0].shape[0] // self.pieces[weight]
            for piece in range(self.pieces[weight]):
                rows = pl.ds(piece * size, size)
                for slot in (0, 1):
                    here = landing.at[slot, rows]
                    self.across.append(copies.make(pair[slot].at[rows], here, inner_peer))
                    self.onward.append(copies.make(here, landing.at[1 - slot, rows], outer_peer))
                    self.late.append(copies.make(here, full.at[6 + slot, rows], core_peer))
                    self.place.append(
                        pltpu.make_async_copy(here, full.at[2 + slot, rows], local_sems.at[sem])
                    )
                    sem += 1
            for slot in (0, 1):
                self.shared.append(copies.make(pair[slot], full.at[4 + slot], core_peer))
                self.kept.append(
                    pltpu.make_async_copy(pair[slot], full.at[slot], local_sems.at[sem])
                )
                sem += 1
                if slot >= self.pairs[weight]:
                    self.later += [self.shared[-1], self.kept[-1]]
                else:
                    self.shared[-1].start()
                    self.kept[-1].start()

        @pl.when(self.inner)
        def _():
            for copy in self.across[:AHEAD]:
                copy.start()

    def arrive(self, number):
        self.onward[number].wait_recv()
        swapped = number + 1 - 2 * (number % 2)
        self.late[swapped].start()
        self.place[swapped].start()

    def pump(self, steps):
        steps = [step for step in steps if step < len(self.across)]

        @pl.when(self.inner)
        def _():
            for here in steps:
                self.across[here].wait_recv()
                for copy in self.across[here + AHEAD : here + AHEAD + 1]:
                    copy.start()
                self.onward[here].start()
                self.late[here].start()
                self.place[here].start()

        @pl.when(self.outer)
        def _():
            for step in steps:
                if step > 0:
                    self.arrive(step - 1)

        for copy in self.partners if 1 in steps else []:
            copy.wait_recv()
            copy.wait_send()
        for copy in self.later if 1 in steps else []:
            copy.start()

    def finish(self):
        @pl.when(self.inner)
        def _():
            for copy in self.across + self.onward:
                copy.wait_send()

        @pl.when(self.outer)
        def _():
            self.arrive(len(self.onward) - 1)

        for copy in self.kept + self.place:
            copy.wait()
        for copy in self.shared + self.late:
            copy.wait_send()
        for copy in self.shared + self.late:
            copy.wait_recv()


def sum_eighths(
    copies, row_peer, side_peer, send, keep, forward, first, second, store, begin, pump
):
    size = send.shape[0] // 4
    part = lambda ref, slot: ref.at[pl.ds(slot * size, size)]
    arrivals = [
        copies.start(part(send, 1), part(first, 1), row_peer),
        copies.start(part(send, 3), part(first, 3), side_peer),
        copies.start(part(send, 0), part(first, 0), row_peer),
        copies.start(part(send, 2), part(first, 2), side_peer),
    ]
    begin()
    passed = []
    for number, slot, peer in ((0, 1, side_peer), (1, 3, row_peer)):
        arrivals[number].wait_recv()

        def add(row, count, number=number, slot=slot):
            here = pl.ds(slot * size + row, count)
            both = keep[here, :].astype(jnp.float32) + first[here, :].astype(jnp.float32)
            forward[pl.ds(number * size + row, count), :] = both.astype(jnp.bfloat16)

        for_rows(size, add)
        passed.append(copies.start(part(forward, number), part(second, number), peer))
    pump([0])
    for number, slot in ((0, 0), (1, 2)):
        arrivals[2 + number].wait_recv()
        passed[number].wait_recv()

        def total(row, count, number=number, slot=slot):
            here = pl.ds(slot * size + row, count)
            sums = keep[here, :].astype(jnp.float32) + first[here, :].astype(jnp.float32)
            sums = sums + second[pl.ds(number * size + row, count), :].astype(jnp.float32)
            store(number, row, count, sums)

        for_rows(size, total)
        yield number
    for copy in arrivals + passed:
        copy.wait_send()


def halves(terms):
    rows = terms.shape[0] // 2
    return terms.at[pl.ds(0, rows)], terms.at[pl.ds(rows, rows)]


def split_refs(refs, jobs, extra_count, out_count):
    refs = list(refs)
    take = lambda count: [refs.pop(0) for _ in range(count)]
    extras = take(extra_count)
    sources = [take(len(job.sources)) for job in jobs]
    full = take(1)[0]
    outs = take(out_count)
    targets = [take(len(job.outputs)) for job in jobs]
    return extras, sources, full, outs, targets, refs


def spread_kernel(middle, jobs, extra_count, out_count, gain_sum, terms, *refs):
    keep, send = halves(terms)
    extras, sources, full, outs, targets, scratch = split_refs(refs, jobs, extra_count, out_count)
    forward, first, second, send_sems, recv_sems, local_sems, *stages = scratch
    zone, side, row, core = place_here()
    row_peer, side_peer = device(zone, side, 1 - row, core), device(zone, 1 - side, row, core)
    copies = Copies(send_sems, recv_sems)
    size = send.shape[0] // 4
    part = lambda slot: full.at[pl.ds(slot * size, size)]
    for out in outs:
        if out.shape[0] == 1:
            out[...] = jnp.zeros_like(out)
    peers = {}
    for job in jobs:
        peers.update(job.peers(zone, side, row, core))
    greet([row_peer, side_peer] + list(peers.values()))

    def begin():
        spot = 0
        for job, source, target in zip(jobs, sources, targets):
            own_stages = stages[spot : spot + len(job.scratch)]
            job.start(copies, local_sems, source, target, own_stages)
            spot += len(job.scratch)

    def pump(steps):
        for job in jobs:
            job.pump(steps)

    def store(number, row, count, sums):
        own = pl.ds(number * size + row, count)
        full[pl.ds(2 * number * size + row, count), :] = middle(own, sums, extras, outs)

    firsts, seconds = [], []
    for number in sum_eighths(
        copies, row_peer, side_peer, send, keep, forward, first, second, store, begin, pump
    ):
        near, other = (side_peer, row_peer) if number == 0 else (row_peer, side_peer)
        slot = 2 * number
        firsts.append(copies.start(part(slot), part(slot + 1), near))
        seconds.append(copies.start(part(slot), part(4 + slot), other))
    pump([1])
    firsts[0].wait_recv()
    seconds.append(copies.start(part(1), part(5), row_peer))
    firsts[1].wait_recv()
    seconds.append(copies.start(part(3), part(7), side_peer))
    pump(range(2, 64))
    for copy in seconds:
        copy.wait_recv()
    for copy in firsts + seconds:
        copy.wait_send()
    for job in jobs:
        job.finish()


def home_kernel(middle, jobs, extra_count, out_count, gain_sum, terms, *refs):
    keep, send = halves(terms)
    extras, sources, full, outs, targets, scratch = split_refs(refs, jobs, extra_count, out_count)
    forward, first, second, own, send_sems, recv_sems, local_sems, *rest = scratch
    gain_scratch, stages = (rest[:2], rest[2:]) if gain_sum is not None else ([], rest)
    zone, side, row, core = place_here()
    row_peer, side_peer = device(zone, side, 1 - row, core), device(zone, 1 - side, row, core)
    core_peer = device(zone, side, row, 1 - core)
    copies = Copies(send_sems, recv_sems)
    size = send.shape[0] // 4
    at_home = side == core
    away = side != core
    for out in outs:
        if out.shape[0] == 1:
            out[...] = jnp.zeros_like(out)
    peers = {}
    for job in jobs:
        peers.update(job.peers(zone, side, row, core))
    plane = [row_peer, side_peer, core_peer]
    if gain_sum is not None:
        plane = gain_sum.plane_peers(zone, side, row, core)
        peers.update(gain_sum.zone_peers(zone, side, row, core))
    greet(plane + list(peers.values()))

    def begin():
        spot = 0
        for job, source, target in zip(jobs, sources, targets):
            own_stages = stages[spot : spot + len(job.scratch)]
            job.start(copies, local_sems, source, target, own_stages)
            spot += len(job.scratch)

    def pump(steps):
        for job in jobs:
            job.pump(steps)

    def store(number, start, count, sums):
        here = pl.ds(number * size + start, count)
        values = middle(here, sums, extras, outs)
        own[here, :] = values
        eighth = row * 2 + side if number == 0 else 4 + side * 2 + row

        @pl.when(at_home)
        def _():
            full[pl.ds(pl.multiple_of(eighth * size + start, 32), count), :] = values

    for _ in sum_eighths(
        copies, row_peer, side_peer, send, keep, forward, first, second, store, begin, pump
    ):
        pass
    pump([1])

    def piece(number, x, y):
        start = (x * 2 + y) * size if number == 0 else (4 + y * 2 + x) * size
        return full.at[pl.ds(pl.multiple_of(start, size), size)]

    mine = lambda number: own.at[pl.ds(number * size, size)]
    both = (0, 1)
    to_side = [copies.make(mine(k), piece(k, row, side), side_peer) for k in both]
    to_row = [copies.make(mine(k), piece(k, row, side), row_peer) for k in both]
    pass_row = [
        copies.make(piece(k, row, 1 - side), piece(k, row, 1 - side), row_peer) for k in both
    ]
    share = []
    for number, (x, y) in enumerate(
        ((row, side), (row, 1 - side), (1 - row, side), (1 - row, 1 - side))
    ):
        for k in both:
            source = mine(k) if number == 0 else piece(k, x, y)
            share.append(copies.make(source, piece(k, x, y), core_peer))

    if gain_sum is not None:
        gain_sum.start(copies, extras[-1], outs[0], *gain_scratch)

    @pl.when(away)
    def _():
        for copy in to_side:
            copy.start()

    @pl.when(at_home)
    def _():
        for copy in to_row + share[:2]:
            copy.start()

    if gain_sum is not None:
        gain_sum.middle()

    @pl.when(away)
    def _():
        for copy in to_side:
            copy.wait_send()
        for copy in share:
            copy.wait_recv()

    @pl.when(at_home)
    def _():
        for k in both:
            to_side[k].wait_recv()
            pass_row[k].start()
            share[2 + k].start()
        for k, copy in enumerate(to_row + pass_row):
            copy.wait_recv()
            share[4 + k].start()
        for copy in to_row + pass_row + share:
            copy.wait_send()

    if gain_sum is not None:
        gain_sum.finish(outs[-1])
    for job in jobs:
        job.finish()


def sum_rows(kernel, middle, terms, extras, outs, number, jobs=(), gain_sum=None):
    half, width = terms.shape[0] // 2, terms.shape[1]
    eighth = half // 4
    low = jnp.bfloat16
    vmem, hbm = pl.BlockSpec(memory_space=pltpu.VMEM), pl.BlockSpec(memory_space=pl.ANY)
    scratch = [
        pltpu.VMEM((2 * eighth, width), low),
        pltpu.VMEM((half, width), low),
        pltpu.VMEM((2 * eighth, width), low),
    ]
    if kernel is home_kernel:
        scratch.append(pltpu.VMEM((2 * eighth, width), low))
    copies = (12 if kernel is spread_kernel else 20) + sum(job.count for job in jobs)
    local = max([2] + [job.count_local for job in jobs])
    if gain_sum is not None:
        copies += gain_sum.count
        outs = outs + [gain_sum.output]
    scratch += [pltpu.SemaphoreType.DMA((count,)) for count in (copies, copies, local)]
    if gain_sum is not None:
        scratch += gain_sum.scratch
    scratch += [stage for job in jobs for stage in job.scratch]
    sources = [source for job in jobs for source in job.sources]
    targets = [target for job in jobs for target in job.outputs]
    return pl.pallas_call(
        functools.partial(kernel, middle, jobs, len(extras), len(outs), gain_sum),
        out_shape=[jax.ShapeDtypeStruct((2 * half, width), low)] + outs + targets,
        in_specs=[vmem] * (1 + len(extras) + len(sources)),
        out_specs=[vmem] * (1 + len(outs))
        + [hbm if job.in_hbm else vmem for job in jobs for _ in job.outputs],
        scratch_shapes=scratch,
        compiler_params=pltpu.CompilerParams(
            collective_id=number, has_side_effects=True, vmem_limit_bytes=56 * 2**20
        ),
        cost_estimate=pl.CostEstimate(flops=10**6, bytes_accessed=10**5, transcendentals=0),
        name=middle.__name__,
    )(terms, *extras, *sources)


def block_columns(plan, width):
    if not plan.ordered:
        return [pl.ds(0, width)], [pl.ds(0, width)]
    zone, _, _, core = place_here()
    size, zones = width // plan.total, plan.zones
    owners = [
        flipped(zone, plan.flips[slot % zones]) * 2 + (core if slot < zones else 1 - core)
        for slot in range(plan.total)
    ]
    natural = [pl.ds(pl.multiple_of(owner * size, size), size) for owner in owners]
    return natural, [pl.ds(slot * size, size) for slot in range(plan.total)]


def copy_rows(source, target):
    def some(row, count):
        target[pl.ds(row, count), :] = source[pl.ds(row, count), :]

    if source.shape[0] % 32:
        target[...] = source[...]
    else:
        for_rows(source.shape[0], some)


def cast_rows(source, target):
    def some(row, count):
        here = pl.ds(row, count)
        target[here, :] = source[here, :].astype(target.dtype)

    for_rows(source.shape[0], some)


def opening_kernel(plan, wide_qkv, gains, wide_gate, wide_out, tokens, angles, *refs):
    qkv_full, gains_full, turned_gate, turned_out, turned_tokens, turned_angles = refs[:6]
    partner_gate, send_sems, recv_sems, tokens_stage, qkv, gate, out = refs[6:]
    cast_rows(wide_qkv, qkv)
    zone, side, row, core = place_here()
    partner = device(zone, core, row, side)
    row_peer, core_peer = device(zone, side, 1 - row, core), device(zone, side, row, 1 - core)
    zone_peers = [device(flipped(zone, flip), side, row, core) for flip in plan.flips[1:]]
    at_home, away = side == core, side != core
    always = [row_peer, core_peer] + zone_peers

    @pl.when(at_home)
    def _():
        greet(always)

    @pl.when(away)
    def _():
        greet(always + [partner])

    copies = Copies(send_sems, recv_sems)
    zones = plan.zones
    own = (gains, qkv, angles, gate, out)
    ends = (gains_full.at[0], qkv_full.at[0], turned_angles, turned_gate, turned_out)
    units = wide_gate.shape[2]

    def cast_rest():
        for half in (0, 1):
            cast_rows(wide_gate.at[half], gate.at[:, pl.ds(half * units, units)])
        cast_rows(wide_out, out)

    turn = [copies.make(source, target, partner) for source, target in zip(own, ends)]
    pieces = 2
    size = tokens.shape[0] // (2 * pieces)
    spots = [
        pl.ds(pl.multiple_of((row * pieces + piece) * size, size), size) for piece in range(pieces)
    ]
    turn_rows = [copies.make(tokens.at[s], tokens_stage.at[s], partner) for s in spots]
    pass_rows = [copies.make(tokens_stage.at[s], tokens_stage.at[s], row_peer) for s in spots]
    natural, local = block_columns(plan, tokens.shape[1])

    def lay_down(all_tokens):
        def some(start, count):
            here = pl.ds(start, count)
            for a, b in zip(natural, local):
                turned_tokens[here, b] = all_tokens[here, a]

        for_rows(all_tokens.shape[0], some)

    slots = list(range(1, zones))
    weights = ((gains, gains_full), (qkv, qkv_full))
    swapped = pl.ds(0, gate.shape[0] // 2)
    from_own = [
        [copies.make(source, full.at[slot], zone_peers[slot - 1]) for slot in slots]
        + [copies.make(source, full.at[zones], core_peer)]
        for source, full in weights
    ] + [[copies.make(gate.at[swapped], partner_gate, zone_peers[0])]]
    copies.number -= 2 * zones + 1
    from_turned = [
        [copies.make(full.at[0], full.at[slot], zone_peers[slot - 1]) for slot in slots]
        + [copies.make(full.at[0], full.at[zones], core_peer)]
        for _, full in weights
    ] + [[copies.make(turned_gate.at[swapped], partner_gate, zone_peers[0])]]
    cross = [
        [copies.make(full.at[slot], full.at[zones + slot], core_peer) for slot in slots]
        for _, full in weights
    ]

    def cross_over(k):
        for which in (0, 1):
            from_turned[which][k].wait_recv()
            cross[which][k].start()

    @pl.when(away)
    def _():
        for copy in turn[:3]:
            copy.start()
        cast_rest()
        for which in (0, 1):
            turn[which].wait_recv()
            for copy in from_turned[which]:
                copy.start()
        turn[3].start()
        turn_rows[0].start()
        turn[3].wait_recv()
        from_turned[2][0].start()
        turn_rows[1].start()
        cross_over(0)
        turn_rows[0].wait_recv()
        pass_rows[0].start()
        for copy in turn[4:]:
            copy.start()
        turn_rows[1].wait_recv()
        pass_rows[1].start()

    @pl.when(at_home)
    def _():
        for copy in from_own[0] + from_own[1]:
            copy.start()
        cast_rest()
        for copy in from_own[2]:
            copy.start()
        for source, target in zip(own, ends):
            copy_rows(source, target)
        lay_down(tokens)
        cross_over(0)

    for k in range(1, zones - 1):
        cross_over(k)
    for which in (0, 1):
        from_turned[which][zones - 1].wait_recv()
        for copy in from_turned[which]:
            copy.wait_send()
        for copy in cross[which]:
            copy.wait_recv()
            copy.wait_send()
    from_turned[2][0].wait_recv()
    from_turned[2][0].wait_send()

    @pl.when(away)
    def _():
        for copy in pass_rows + turn[2:3] + turn[4:]:
            copy.wait_recv()
        lay_down(tokens_stage)
        for copy in turn + turn_rows + pass_rows:
            copy.wait_send()


def opening(plan, qkv, gains, gate, out, tokens, angles, number):
    low = jnp.bfloat16
    vmem = pl.BlockSpec(memory_space=pltpu.VMEM)
    like = lambda v: jax.ShapeDtypeStruct(v.shape, v.dtype)
    whole = lambda v: jax.ShapeDtypeStruct((2 * plan.zones,) + v.shape, low)
    operands = (qkv, gains, gate, out, tokens, angles)
    low_gate = jax.ShapeDtypeStruct((gate.shape[1], 2 * gate.shape[2]), low)
    low_out = jax.ShapeDtypeStruct(out.shape, low)
    outputs = [whole(qkv), whole(gains), low_gate, low_out, like(tokens), like(angles)]
    outputs += [jax.ShapeDtypeStruct((gate.shape[1] // 2, 2 * gate.shape[2]), low)]
    copies = 5 + 4 + 2 * plan.zones + 1 + 2 * (plan.zones - 1)
    return pl.pallas_call(
        functools.partial(opening_kernel, plan),
        out_shape=outputs,
        in_specs=[vmem] * len(operands),
        out_specs=[vmem] * len(outputs),
        scratch_shapes=[
            pltpu.SemaphoreType.DMA((copies,)),
            pltpu.SemaphoreType.DMA((copies,)),
            pltpu.VMEM(tokens.shape, tokens.dtype),
            pltpu.VMEM(qkv.shape, low),
            pltpu.VMEM(low_gate.shape, low),
            pltpu.VMEM(out.shape, low),
        ],
        compiler_params=pltpu.CompilerParams(
            collective_id=number, has_side_effects=True, vmem_limit_bytes=56 * 2**20
        ),
        cost_estimate=pl.CostEstimate(flops=10**6, bytes_accessed=10**5, transcendentals=0),
        name="opening",
    )(*operands)


def inverse_rms(values):
    return lax.rsqrt(jnp.mean(values * values, -1, keepdims=True) + EPS_NORM)


def hidden_rows(own, sums, extras, outs):
    tokens, gain = extras
    hidden = tokens[own, :].astype(jnp.float32) + sums
    outs[0][own, :] = hidden
    return (hidden * inverse_rms(hidden) * gain[...]).astype(jnp.bfloat16)


def grad_hidden_rows(own, sums, extras, outs):
    hidden, out_grad, gain = extras
    values = hidden[own, :]
    factor = inverse_rms(values)
    unit = values * factor
    outs[1][...] += jnp.sum(sums * unit, 0, keepdims=True)
    grad = out_grad[own, :].astype(jnp.float32) + norm_back(sums * gain[...], unit, factor)
    outs[0][own, :] = grad
    return grad.astype(jnp.bfloat16)


def grad_input_rows(own, sums, extras, outs):
    tokens, grad_hidden, gain = extras[:3]
    values = tokens[own, :].astype(jnp.float32)
    factor = inverse_rms(values)
    unit = values * factor
    outs[0][...] += jnp.sum(sums * unit, 0, keepdims=True)
    return (grad_hidden[own, :] + norm_back(sums * gain[...], unit, factor)).astype(jnp.bfloat16)


def dot(left, right, left_dim=1, right_dim=0):
    return lax.dot_general(
        left, right, (((left_dim,), (right_dim,)), ((), ())), preferred_element_type=jnp.float32
    )


def turn_head(values, cosine, signed_sine):
    return values * cosine + pltpu.roll(values, HEAD // 2, 1) * signed_sine


def turn_back(gradient, cosine, signed_sine):
    return gradient * cosine + pltpu.roll(gradient * signed_sine, HEAD // 2, 1)


def softmax_block(query, key, first_row):
    rows, keys = query.shape[0], key.shape[0]
    scores = dot(query, key, 1, 1)
    row_at = lax.broadcasted_iota(jnp.int32, (rows, keys), 0) + first_row
    key_at = lax.broadcasted_iota(jnp.int32, (rows, keys), 1)
    scores = jnp.where(key_at <= row_at, scores, -1000000000.0)
    exponent = jnp.exp(scores - jnp.max(scores, -1, keepdims=True))
    return exponent / jnp.sum(exponent, -1, keepdims=True)


def eighth_owners():
    _, side, row, _ = place_here()
    own, off = (row, side), (1 - row, 1 - side)
    first = lambda x, y: x * 2 + y
    second = lambda x, y: 4 + y * 2 + x
    return [
        first(own[0], own[1]),
        first(own[0], off[1]),
        second(own[0], own[1]),
        second(off[0], own[1]),
        first(off[0], own[1]),
        first(off[0], off[1]),
        second(own[0], off[1]),
        second(off[0], off[1]),
    ]


def reorder_rows(source, target, into_local):
    size = source.shape[0] // 8
    for slot, owner in enumerate(eighth_owners()):
        natural = pl.ds(pl.multiple_of(owner * size, size), size)
        local = pl.ds(slot * size, size)
        if into_local:
            target[local, :] = source[natural, :]
        else:
            target[natural, :] = source[local, :]


def forward_kernel(
    tokens, weights, gain_in, gain_q, gain_k, cosine, sine,
    normed, raw, query, key, value, local, attended,
):
    low = jnp.bfloat16
    total, heads = tokens.shape[0], query.shape[1] // HEAD
    block, wide = 256, 512

    def project(step, carry):
        rows = pl.ds(pl.multiple_of(step * wide, wide), wide)
        values = tokens[rows, :].astype(jnp.float32)
        normed[rows, :] = (values * inverse_rms(values) * gain_in[...]).astype(low)
        raw[rows, :] = dot(normed[rows, :], weights[...])
        turns = (cosine[rows, :], sine[rows, :])
        for head in range(heads):
            column = (head // 2) * 4 * HEAD + (head % 2) * HEAD
            values = raw[rows, pl.ds(column, HEAD)]
            values = turn_head(values * inverse_rms(values) * gain_q[...], *turns)
            query[rows, pl.ds(head * HEAD, HEAD)] = (values * (1.0 / math.sqrt(HEAD))).astype(low)
        for group in range(heads // 2):
            column = group * 4 * HEAD + 2 * HEAD
            here = pl.ds(group * HEAD, HEAD)
            values = raw[rows, pl.ds(column, HEAD)]
            values = turn_head(values * inverse_rms(values) * gain_k[...], *turns)
            key[rows, here] = values.astype(low)
            value[rows, here] = raw[rows, pl.ds(column + HEAD, HEAD)].astype(low)
        return carry

    lax.fori_loop(0, total // wide, project, 0)

    def attend(head, carry):
        mine = pl.ds(pl.multiple_of(head * HEAD, HEAD), HEAD)
        shared = pl.ds(pl.multiple_of(lax.div(head, 2) * HEAD, HEAD), HEAD)
        for start in range(0, total, SEQ):
            for first in range(0, SEQ, block):
                rows, keys = pl.ds(start + first, block), pl.ds(start, first + block)
                probs = softmax_block(query[rows, mine], key[keys, shared], first)
                attended[rows, mine] = dot(probs.astype(low), value[keys, shared]).astype(low)
        return carry

    lax.fori_loop(0, heads, attend, 0)
    reorder_rows(attended, local, True)


def attention(tokens, weights, gain_in, gain_q, gain_k, cosine, sine):
    total = tokens.shape[0]
    columns = weights.shape[1]
    low = jnp.bfloat16
    shape = lambda width, kind=low: jax.ShapeDtypeStruct((total, width), kind)
    vmem = pl.BlockSpec(memory_space=pltpu.VMEM)
    return pl.pallas_call(
        forward_kernel,
        out_shape=[
            shape(tokens.shape[1]),
            shape(columns, jnp.float32),
            shape(columns // 2),
            shape(columns // 4),
            shape(columns // 4),
            shape(columns // 2),
        ],
        in_specs=[vmem] * 7,
        out_specs=[vmem] * 6,
        scratch_shapes=[pltpu.VMEM((total, columns // 2), low)],
        compiler_params=pltpu.CompilerParams(vmem_limit_bytes=48 * 2**20),
        cost_estimate=pl.CostEstimate(flops=10**6, bytes_accessed=10**5, transcendentals=0),
        name="attention",
    )(tokens, weights, gain_in, gain_q, gain_k, cosine, sine)


def backward_kernel(
    query, key, value, raw, grad_rows, gain_q, gain_k, cosine, sine,
    mixed, mixed_local, query_gain, key_gain, grad, key_sum, value_sum,
):
    low = jnp.bfloat16
    total, heads = query.shape[0], query.shape[1] // HEAD
    block = 256
    reorder_rows(grad_rows, grad, False)
    query_gain[...] = jnp.zeros_like(query_gain)
    key_gain[...] = jnp.zeros_like(key_gain)

    def head_norm_back(rows, column, gradient, gain, gain_grad):
        values = raw[rows, column]
        factor = inverse_rms(values)
        unit = values * factor
        turned = turn_back(gradient, cosine[rows, :], sine[rows, :])
        gain_grad[...] += jnp.sum(turned * unit, 0, keepdims=True)
        mixed[rows, column] = norm_back(turned * gain[...], unit, factor).astype(low)

    def one_group(group, carry):
        at = lambda offset: pl.ds(pl.multiple_of(group * 4 * HEAD + offset * HEAD, HEAD), HEAD)
        shared = pl.ds(pl.multiple_of(group * HEAD, HEAD), HEAD)
        key_sum[...] = jnp.zeros_like(key_sum)
        value_sum[...] = jnp.zeros_like(value_sum)
        for head in (0, 1):
            mine = pl.ds(pl.multiple_of((group * 2 + head) * HEAD, HEAD), HEAD)
            for start in range(0, total, SEQ):
                for first in range(0, SEQ, block):
                    rows, keys = pl.ds(start + first, block), pl.ds(start, first + block)
                    query_part, grad_part = query[rows, mine], grad[rows, mine]
                    probs = softmax_block(query_part, key[keys, shared], first)
                    weighed = probs * dot(grad_part, value[keys, shared], 1, 1)
                    scores = weighed - probs * jnp.sum(weighed, -1, keepdims=True)
                    scores = scores.astype(low)
                    grad_query = dot(scores, key[keys, shared]) * (1.0 / math.sqrt(HEAD))
                    head_norm_back(rows, at(head), grad_query, gain_q, query_gain)
                    key_sum[keys, :] += dot(scores, query_part, 0, 0)
                    value_sum[keys, :] += dot(probs.astype(low), grad_part, 0, 0)
        for first in range(0, total, block):
            rows = pl.ds(first, block)
            head_norm_back(rows, at(2), key_sum[rows, :], gain_k, key_gain)
            mixed[rows, at(3)] = value_sum[rows, :].astype(low)
        return carry

    lax.fori_loop(0, heads // 2, one_group, 0)
    reorder_rows(mixed, mixed_local, True)


def attention_back(query, key, value, raw, grad_rows, gain_q, gain_k, cosine, sine):
    total, columns = raw.shape
    low = jnp.bfloat16
    vmem = pl.BlockSpec(memory_space=pltpu.VMEM)
    return pl.pallas_call(
        backward_kernel,
        out_shape=[
            jax.ShapeDtypeStruct((total, columns), low),
            jax.ShapeDtypeStruct((total, columns), low),
            jax.ShapeDtypeStruct((1, HEAD), jnp.float32),
            jax.ShapeDtypeStruct((1, HEAD), jnp.float32),
        ],
        in_specs=[vmem] * 9,
        out_specs=[vmem] * 4,
        scratch_shapes=[
            pltpu.VMEM(grad_rows.shape, low),
            pltpu.VMEM((total, HEAD), jnp.float32),
            pltpu.VMEM((total, HEAD), jnp.float32),
        ],
        compiler_params=pltpu.CompilerParams(vmem_limit_bytes=48 * 2**20),
        cost_estimate=pl.CostEstimate(flops=10**6, bytes_accessed=10**5, transcendentals=0),
        name="attention_back",
    )(query, key, value, raw, grad_rows, gain_q, gain_k, cosine, sine)


def feed_kernel(plan, rows, own_grad, got_grad, gate_up, up_part, down, active, grads, out_grad):
    low = jnp.bfloat16
    block = 512
    tile = down.shape[1]
    step = pl.program_id(0)
    gate_at = pl.ds(pl.multiple_of(step * tile, tile), tile)
    up_at = pl.ds(pl.multiple_of(grads.shape[1] // 2 + step * tile, tile), tile)
    _, side, _, core = place_here()

    def lay_down(source):
        natural, blocks = block_columns(plan, source.shape[1])
        eighth = source.shape[0] // 8
        for slot, owner in enumerate(eighth_owners()):

            def some(start, count, slot=slot, owner=owner):
                here = pl.ds(pl.multiple_of(owner * eighth + start, 32), count)
                there = pl.ds(slot * eighth + start, count)
                for a, b in zip(natural, blocks):
                    out_grad[there, b] = source[here, a]

            for_rows(eighth, some)

    @pl.when((step == 0) & (side == core))
    def _():
        lay_down(own_grad)

    @pl.when((step == 0) & (side != core))
    def _():
        lay_down(got_grad)

    def one(block_at, carry):
        here = pl.ds(pl.multiple_of(block_at * block, block), block)
        gate = dot(rows[here, :], gate_up[...])
        up = dot(rows[here, :], up_part[...])
        grad = dot(out_grad[here, :], down[...])
        sigmoid = jax.nn.sigmoid(gate)
        silu = gate * sigmoid
        active[here, :] = (silu * up).astype(low)
        grads[here, gate_at] = (grad * up * sigmoid * (1.0 + gate * (1.0 - sigmoid))).astype(low)
        grads[here, up_at] = (grad * silu).astype(low)
        return carry

    lax.fori_loop(0, rows.shape[0] // block, one, 0)


def feed_forward(plan, rows, own_grad, got_grad, gate_up, down, tile):
    total, width = rows.shape
    units = down.shape[1]
    low = jnp.bfloat16
    tiles = units // tile
    whole = pl.BlockSpec(memory_space=pltpu.VMEM)
    return pl.pallas_call(
        functools.partial(feed_kernel, plan),
        grid=(tiles,),
        out_shape=[
            jax.ShapeDtypeStruct((total, units), low),
            jax.ShapeDtypeStruct((total, 2 * units), low),
            jax.ShapeDtypeStruct((total, width), low),
        ],
        in_specs=[
            whole,
            whole,
            whole,
            pl.BlockSpec((width, tile), lambda step: (0, step)),
            pl.BlockSpec((width, tile), lambda step: (0, step + tiles)),
            pl.BlockSpec((width, tile), lambda step: (0, step)),
        ],
        out_specs=[
            pl.BlockSpec((total, tile), lambda step: (0, step)),
            whole,
            whole,
        ],
        compiler_params=pltpu.CompilerParams(vmem_limit_bytes=56 * 2**20),
        cost_estimate=pl.CostEstimate(
            flops=6 * total * width * units, bytes_accessed=4 * 10**7, transcendentals=total * units
        ),
        name="feed_forward",
    )(rows, own_grad, got_grad, gate_up, gate_up, down)


class Plan:
    def __init__(self, mesh):
        self.total = mesh.shape["dp"]
        self.zones = self.total // 2
        self.tensor = mesh.shape["tensor"]
        self.flips = [k ^ (k >> 1) for k in range(self.zones)]

    def place(self):
        self.index = lax.axis_index("dp")
        self.zone = self.index // 2
        self.side = self.index % 2
        self.row = lax.axis_index("tensor") // 2
        self.core = lax.axis_index("tensor") % 2
        self.home = self.side == self.core

    def move(self, value, target):
        pairs = []
        for d in range(self.total):
            for t in range(self.tensor):
                to = target(d // 2, d % 2, t // 2, t % 2)
                if to is not None:
                    zone, side, row, core = to
                    pairs.append((d * self.tensor + t, (zone * 2 + side) * self.tensor + row * 2 + core))
        return lax.ppermute(value, ("dp", "tensor"), pairs)

    def turn(self, value):
        got = self.move(value, lambda z, y, x, c: (z, c, x, y) if y != c else None)
        return jnp.where(self.home, value, got)

    def zone_flip(self, value, bit):
        return self.move(value, lambda z, y, x, c: (z ^ bit, y, x, c))

    def core_swap(self, value):
        return self.move(value, lambda z, y, x, c: (z, y, x, 1 - c))

    def side_swap(self, value):
        return self.move(value, lambda z, y, x, c: (z, 1 - y, x, c))

    def row_swap(self, value):
        return self.move(value, lambda z, y, x, c: (z, y, 1 - x, c))

    def to_local(self, value, axis):
        width = value.shape[axis] // self.total
        parts = []
        for core in (self.core, 1 - self.core):
            for slot in range(self.zones):
                owner = (self.zone ^ self.flips[slot]) * 2 + core
                parts.append(lax.dynamic_slice_in_dim(value, owner * width, width, axis))
        return jnp.concatenate(parts, axis)

    def to_natural(self, value, axis, core=None):
        core = self.core if core is None else core
        width = value.shape[axis] // self.total
        parts = []
        for block in range(self.total):
            slot = flip = (block // 2) ^ self.zone
            for bits in range(1, self.zones.bit_length()):
                slot = slot ^ (flip >> bits)
            slot = slot + jnp.where(block % 2 == core, 0, self.zones)
            parts.append(lax.dynamic_slice_in_dim(value, slot * width, width, axis))
        return jnp.concatenate(parts, axis)

    def row_owners(self):
        own, off = (self.row, self.side), (1 - self.row, 1 - self.side)
        first = lambda x, y: x * 2 + y
        second = lambda x, y: 4 + y * 2 + x
        return [
            first(own[0], own[1]),
            first(own[0], off[1]),
            second(own[0], own[1]),
            second(off[0], own[1]),
            first(off[0], own[1]),
            first(off[0], off[1]),
            second(own[0], off[1]),
            second(off[0], off[1]),
        ]

    def rows_local(self, value, slots=range(8)):
        size = value.shape[0] // 8
        owners = self.row_owners()
        return jnp.concatenate(
            [lax.dynamic_slice_in_dim(value, owners[slot] * size, size, 0) for slot in slots], 0
        )

    def rows_natural(self, value, order=range(8)):
        size = value.shape[0] // 8
        place = [list(order).index(slot) for slot in range(8)]
        parts = []
        for piece in range(8):
            x, y = (piece // 2, piece % 2) if piece < 4 else (piece % 2, (piece - 4) // 2)
            slots = (0, 1, 4, 5) if piece < 4 else (2, 6, 3, 7)
            same_x, same_y = x == self.row, y == self.side
            slot = jnp.where(
                same_x,
                jnp.where(same_y, place[slots[0]], place[slots[1]]),
                jnp.where(same_y, place[slots[2]], place[slots[3]]),
            )
            parts.append(lax.dynamic_slice_in_dim(value, slot * size, size, 0))
        return jnp.concatenate(parts, 0)

    def from_zones(self, shard):
        return [self.zone_flip(shard, flip) for flip in self.flips[1:]]

    def to_zones(self, parts, slots):
        return [self.zone_flip(parts[slot], self.flips[slot]) for slot in slots]

    def middle_swap(self, pair):
        return self.move(pair, lambda z, y, x, c: (z ^ 3, y, x, c) if z in (1, 2) else None)

    def inward(self, part):
        return self.move(part, lambda z, y, x, c: (z ^ 1, y, x, c) if z in (0, 3) else None)

    def pass_outward(self, pair):
        return self.move(pair, lambda z, y, x, c: (z ^ 1, y, x, c) if z in (1, 2) else None)

    def far_pair(self, middle, passed):
        inner = (self.zone == 1) | (self.zone == 2)
        return jnp.where(inner, middle, passed[::-1])

    def first_swap(self, send):
        half = send.shape[0] // 2
        return self.row_swap(send[:half]), self.side_swap(send[half:])

    def second_swap(self, keep, got):
        quarter = keep.shape[0] // 4
        row_part = keep[: 2 * quarter] + got[0].astype(jnp.float32)
        side_part = keep[2 * quarter :] + got[1].astype(jnp.float32)
        own = jnp.concatenate([row_part[:quarter], side_part[:quarter]], 0)
        return own, (
            self.side_swap(row_part[quarter:].astype(jnp.bfloat16)),
            self.row_swap(side_part[quarter:].astype(jnp.bfloat16)),
        )

    def spread_first(self, own):
        half = own.shape[0] // 2
        return (self.side_swap(own[:half]), self.row_swap(own[half:]))

    def spread_second(self, own, got):
        half = own.shape[0] // 2
        row_part = jnp.concatenate([own[:half], got[0]], 0)
        side_part = jnp.concatenate([own[half:], got[1]], 0)
        return row_part, side_part, self.row_swap(row_part), self.side_swap(side_part)

    def send_home(self, own):
        to_home = lambda z, y, x, c: (z, c, x, c) if y != c else None
        return jnp.concatenate([own, self.move(own, to_home)], 0)

    def row_home(self, part):
        return self.move(part, lambda z, y, x, c: (z, y, 1 - x, c) if y == c else None)

    def share_home(self, part, other):
        full = jnp.concatenate([part, other], 0)
        full = self.to_natural(self.rows_natural(full, (0, 2, 1, 6, 4, 3, 5, 7)), 1)
        got = self.move(full, lambda z, y, x, c: (z, y, x, 1 - c) if y == c else None)
        return full, got

    def turned(self, own, got):
        return jnp.where(self.home, own, got)

    def sum_everywhere(self, value):
        value = value + self.row_swap(value)
        value = value + self.side_swap(value)
        value = value + self.core_swap(value)
        bit = 1
        while bit < self.zones:
            value = value + self.zone_flip(value, bit)
            bit *= 2
        return value


def shards(
    plan,
    tokens,
    positions,
    out_grad,
    qkv_weight,
    qkv_first,
    qkv_second,
    out_weight,
    out_first,
    out_second,
    gate_up,
    gate_up_first,
    gate_up_second,
    down_weight,
    down_first,
    down_second,
    gains,
    gains_first,
    gains_second,
):
    plan.place()
    low = jnp.bfloat16
    tok_rows, model_width = tokens.shape
    groups = qkv_weight.shape[1]
    head_size = qkv_weight.shape[3]
    shard_rows = qkv_weight.shape[0]
    seq_count = tok_rows // SEQ
    mixed_cols = groups * 4 * head_size
    near_cols = model_width // 2
    kept = tok_rows // 2
    gain_count = gains.shape[0]

    tree = plan.zones == 4
    slots = range(1, plan.zones)

    def column_parts(value):
        return value.reshape((plan.zones, -1) + value.shape[1:])

    units = gate_up.shape[2]
    plan.ordered = (model_width // plan.total) % 128 == 0
    gain_rows = 16
    gain_block = jnp.pad(gains.astype(low), (0, gain_rows * 128 - gain_count)).reshape(gain_rows, 128)
    tile = min(units, 256)
    angle_at = positions.astype(jnp.float32).reshape(-1, 128)
    both_qkv, both_gains, turned_gate, turned_out, tokens, angle_at, partner_gate = opening(
        plan,
        qkv_weight.reshape(shard_rows, mixed_cols),
        gain_block,
        gate_up,
        out_weight,
        tokens,
        angle_at,
        3,
    )
    positions = angle_at.reshape(-1)
    turned_out, turned_gate, tokens, positions, both_qkv, both_gains, low_down = fence(
        turned_out,
        turned_gate,
        tokens,
        positions,
        both_qkv,
        both_gains,
        down_weight.astype(low),
    )

    got_down = plan.move(low_down, lambda z, y, x, c: (z, c, x, y) if y != c else None)
    half_rows = shard_rows // 2
    zone_out = plan.from_zones(turned_out)
    if tree:
        partner_rest = plan.zone_flip(turned_gate[half_rows:], 1)
    else:
        partner_rest = partner_gate
        partner_gate = plan.from_zones(turned_gate)
    if not plan.ordered:
        tokens = plan.to_local(tokens, 1)
    cosine, sine_table = rotary(positions, head_size)
    signed_sine = jnp.concatenate(
        [-sine_table[:, : head_size // 2], sine_table[:, head_size // 2 :]], 1
    )
    full_qkv = both_qkv.reshape(model_width, mixed_cols)
    gain_slots = both_gains.reshape(plan.total, -1)[:, :gain_count]
    gain_all = plan.to_natural(gain_slots.reshape(-1), 0).astype(jnp.float32)
    gain_in = plan.to_local(gain_all[:model_width], 0)[None]
    gain_post = plan.to_local(gain_all[model_width : 2 * model_width], 0)[None]
    gain_q = gain_all[2 * model_width : 2 * model_width + head_size][None]
    gain_k = gain_all[2 * model_width + head_size :][None]
    got_down, cosine, signed_sine, gain_in, gain_post, gain_q, gain_k, out_grad, tokens = fence(
        got_down, cosine, signed_sine, gain_in, gain_post, gain_q, gain_k, out_grad, tokens
    )

    got_grad = plan.move(out_grad, lambda z, y, x, c: (z, c, x, y) if y != c else None)
    normed, raw, query, key_rot, values_low, attended = attention(
        tokens, full_qkv, gain_in, gain_q, gain_k, cosine, signed_sine
    )
    turned_down = plan.turned(low_down, got_down)
    attended, zone_out, turned_out, turned_down, turned_gate, partner_gate, partner_rest = fence(
        attended, zone_out, turned_out, turned_down, turned_gate, partner_gate, partner_rest
    )

    near_out = jnp.concatenate([turned_out] + zone_out, 0)
    far_out = plan.core_swap(near_out)
    own_tokens = plan.rows_local(tokens, (0, 2))
    near_out, far_out, own_tokens = fence(near_out, far_out, own_tokens)

    full_out = jnp.concatenate([near_out, far_out], 0)
    branch_terms = contract_cols(attended, full_out).astype(low)
    if tree:
        pairs = [(turned_gate, jnp.concatenate([partner_gate, partner_rest], 0)), (turned_down,)]
    else:
        pairs = [(turned_gate, partner_gate), (turned_down, plan.from_zones(turned_down))]
    jobs = [PairTree(pairs, (2, 2))] if tree else []
    normed_rows, hidden, *gathered = sum_rows(
        spread_kernel,
        hidden_rows,
        branch_terms,
        [own_tokens, gain_post],
        [jax.ShapeDtypeStruct((tok_rows // 4, model_width), jnp.float32)],
        0,
        jobs,
    )
    if not tree:
        near = [jnp.concatenate([own] + rest, 0) for own, rest in pairs]
        gathered = [jnp.concatenate([part, plan.core_swap(part)], 0) for part in near]
    full_gate = gathered[0].reshape(model_width, 2 * units)
    full_down = gathered[1].reshape(model_width, units)
    normed_rows, hidden, full_gate, full_down, got_grad = fence(
        normed_rows, hidden, full_gate, full_down, got_grad
    )

    def zone_parts(near, got):
        both = (near + got.astype(jnp.float32)).astype(low)
        return both.reshape((plan.zones, -1) + both.shape[1:])

    def zone_total(parts, *arrived):
        total = parts[0].astype(jnp.float32)
        for part in sum([list(group) for group in arrived], []):
            total = total + part.astype(jnp.float32)
        return total.astype(low)

    active, grad_both, out_grad = feed_forward(
        plan, normed_rows, out_grad, got_grad, full_gate, full_down, tile
    )
    if not plan.ordered:
        out_grad = plan.to_local(out_grad, 1)
    gate_far = contract_rows(normed_rows[:, near_cols:], grad_both).astype(low)
    gate_far, active, grad_both, out_grad, normed_rows = fence(
        gate_far, active, grad_both, out_grad, normed_rows
    )

    gate_got = plan.core_swap(gate_far)
    mlp_terms = contract_cols(active, full_down).astype(low)
    down_far = contract_rows(out_grad[:, near_cols:], active).astype(low)
    gate_got, mlp_terms, down_far, active, grad_both, normed_rows = fence(
        gate_got, mlp_terms, down_far, active, grad_both, normed_rows
    )

    mlp_got = plan.first_swap(mlp_terms[kept:])
    down_got = plan.core_swap(down_far)
    gate_parts = zone_parts(contract_rows(normed_rows[:, :near_cols], grad_both), gate_got)
    down_parts = zone_parts(contract_rows(out_grad[:, :near_cols], active), down_got)
    gate_parts, down_parts, grad_both, mlp_got, mlp_terms = fence(
        gate_parts, down_parts, grad_both, mlp_got, mlp_terms
    )

    half_rows = shard_rows // 2
    if tree:
        gate_ready = [plan.inward(gate_parts[3, :half_rows])]
    else:
        gate_ready = [gate_parts[0]]
    post_terms = contract_cols(grad_both, full_gate).astype(low)
    mlp_own, mlp_last = plan.second_swap(mlp_terms[:kept].astype(jnp.float32), mlp_got)
    post_terms, gate_parts, gate_ready, mlp_own, mlp_last, down_parts = fence(
        post_terms, gate_parts, gate_ready, mlp_own, mlp_last, down_parts
    )
    if tree:
        gate_ready += [plan.inward(gate_parts[3, half_rows:])]
    block_own = (hidden + mlp_own + jnp.concatenate(mlp_last, 0).astype(jnp.float32)).astype(low)
    block_home = plan.send_home(block_own)
    post_terms, gate_parts, gate_ready, down_parts, block_home = fence(
        post_terms, gate_parts, gate_ready, down_parts, block_home
    )
    gate_ready = jnp.concatenate(gate_ready, 0)

    if tree:
        down_sums = [plan.inward(down_parts[3]), plan.inward(down_parts[2])]
    else:
        down_sums = plan.to_zones(down_parts, slots)
    eighth = tok_rows // 8
    own_grad = jnp.concatenate([out_grad[:eighth], out_grad[2 * eighth : 3 * eighth]], 0)
    branch_rows, grad_hidden, post_gain_grad, gate_sums = sum_rows(
        spread_kernel,
        grad_hidden_rows,
        post_terms,
        [hidden, own_grad, gain_post],
        [
            jax.ShapeDtypeStruct((tok_rows // 4, model_width), jnp.float32),
            jax.ShapeDtypeStruct((1, model_width), jnp.float32),
        ],
        1,
        [PairScatter(gate_parts, gate_ready, 2) if tree else ZoneBlocks(plan, gate_parts, slots)],
    )
    branch_rows, grad_hidden, post_gain_grad, gate_sums, block_home, down_parts, down_sums = fence(
        branch_rows, grad_hidden, post_gain_grad, gate_sums, block_home, down_parts, down_sums
    )

    block_row = plan.row_home(block_home)
    if tree:
        gate_last = [plan.zone_flip(gate_sums[1], 1)]
        gate_own = gate_sums
        down_pair = down_parts[2:].astype(jnp.float32) + jnp.stack(down_sums).astype(jnp.float32)
        down_sums = plan.middle_swap(down_pair.astype(low))
    else:
        gate_last, gate_own = gate_sums, gate_parts
    grad_att = jnp.dot(branch_rows, full_out, preferred_element_type=jnp.float32).astype(low)
    grad_mixed, mixed_rows, query_gain_grad, key_gain_grad = attention_back(
        query, key_rot, values_low, raw, grad_att, gain_q, gain_k, cosine, signed_sine
    )
    gain_terms = jnp.concatenate(
        [plan.to_natural(post_gain_grad, 1), query_gain_grad, key_gain_grad], 1
    )
    if tree:
        down_own = (down_parts[:2].astype(jnp.float32) + down_sums.astype(jnp.float32)).astype(low)
    grad_mixed, mixed_rows, gain_terms, normed, gate_last, branch_rows, block_row, down_sums = fence(
        grad_mixed, mixed_rows, gain_terms, normed, gate_last, branch_rows, block_row, down_sums
    )

    if tree:
        total_down = zone_total(down_own, [plan.zone_flip(down_own[1], 1)])
    else:
        total_down = zone_total(down_parts, down_sums)
    total_gate = zone_total(gate_own, gate_last)
    out_far = contract_rows(branch_rows[:, near_cols:], attended).astype(low)
    out_got = plan.core_swap(out_far)
    block_full, block_got = plan.share_home(block_home, block_row)
    normed_terms = contract_cols(mixed_rows, full_qkv).astype(low)
    out_parts = zone_parts(contract_rows(branch_rows[:, :near_cols], attended), out_got)
    out_parts, normed_terms, total_gate, total_down, block_full, normed, grad_mixed = fence(
        out_parts, normed_terms, total_gate, total_down, block_full, normed, grad_mixed
    )

    gain_sum = GainSum(plan, gain_terms.shape[1], model_width) if plan.ordered else None
    input_full, input_gain_grad, *rest = sum_rows(
        home_kernel,
        grad_input_rows,
        normed_terms,
        [own_tokens, grad_hidden, gain_in] + ([gain_terms] if plan.ordered else []),
        [jax.ShapeDtypeStruct((1, model_width), jnp.float32)],
        2,
        [BlockGrad(plan, normed, grad_mixed), ZoneBlocks(plan, out_parts, slots)],
        gain_sum,
    )
    if plan.ordered:
        summed_gains, total_qkv, out_sent = rest
    else:
        total_qkv, out_sent = rest
        summed_gains = plan.sum_everywhere(
            jnp.concatenate([plan.to_natural(input_gain_grad, 1), gain_terms], 1)
        )
    input_full, summed_gains, total_qkv, out_sent, total_gate, total_down, block_got = fence(
        input_full, summed_gains, total_qkv, out_sent, total_gate, total_down, block_got
    )

    summed_down = plan.turn(total_down)
    summed_gate = plan.turn(jnp.stack([total_gate[:, :units], total_gate[:, units:]]))
    block_out = jnp.where(plan.home, block_full, block_got)
    summed_both = plan.turn(
        jnp.concatenate([total_qkv, zone_total(out_parts, out_sent)], 1)
    ).astype(jnp.float32)
    summed_qkv = summed_both[:, :mixed_cols].reshape(qkv_weight.shape)
    summed_out = summed_both[:, mixed_cols:]
    summed_gate = summed_gate.astype(jnp.float32)
    summed_down = summed_down.astype(jnp.float32)
    summed_gains = lax.dynamic_slice_in_dim(summed_gains[0], plan.index * gain_count, gain_count, 0)
    input_rows = plan.to_natural(input_full, 1, plan.side).astype(jnp.float32)

    qkv_moment, qkv_square, qkv_updated = adamw(
        qkv_weight, summed_qkv, qkv_first, qkv_second, RATE_QKV, DECAY_RATE
    )
    out_moment, out_square, out_updated = adamw(
        out_weight, summed_out, out_first, out_second, RATE_OUT, DECAY_RATE
    )
    gate_moment, gate_square, gate_updated = adamw(
        gate_up, summed_gate, gate_up_first, gate_up_second, RATE_GATE, DECAY_RATE
    )
    down_moment, down_square, down_updated = adamw(
        down_weight, summed_down, down_first, down_second, RATE_DOWN, DECAY_RATE
    )
    gain_moment, gain_square, gain_updated = adamw(
        gains, summed_gains, gains_first, gains_second, RATE_GAIN, 0.0
    )
    return (
        block_out,
        input_rows,
        qkv_moment,
        qkv_square,
        qkv_updated,
        out_moment,
        out_square,
        out_updated,
        gate_moment,
        gate_square,
        gate_updated,
        down_moment,
        down_square,
        down_updated,
        gain_moment,
        gain_square,
        gain_updated,
    )


def solution(mesh):
    plan = Plan(mesh)
    placed = (
        P("dp", None),
        P("dp"),
        P("dp", None),
        P("dp", "tensor", None, None),
        P("dp", "tensor", None, None),
        P("dp", "tensor", None, None),
        P("dp", "tensor"),
        P("dp", "tensor"),
        P("dp", "tensor"),
        P(None, "dp", "tensor"),
        P(None, "dp", "tensor"),
        P(None, "dp", "tensor"),
        P("dp", "tensor"),
        P("dp", "tensor"),
        P("dp", "tensor"),
        P("dp"),
        P("dp"),
        P("dp"),
    )
    return jax.shard_map(
        functools.partial(shards, plan),
        mesh=mesh,
        in_specs=placed,
        out_specs=(
            P("dp", None),
            P("dp", None),
            P("dp", "tensor", None, None),
            P("dp", "tensor", None, None),
            P("dp", "tensor", None, None),
            P("dp", "tensor"),
            P("dp", "tensor"),
            P("dp", "tensor"),
            P(None, "dp", "tensor"),
            P(None, "dp", "tensor"),
            P(None, "dp", "tensor"),
            P("dp", "tensor"),
            P("dp", "tensor"),
            P("dp", "tensor"),
            P("dp"),
            P("dp"),
            P("dp"),
        ),
        check_vma=False,
    )
```

```python
import functools
import math

import jax
import jax.numpy as jnp
from jax import lax
from jax.experimental import pallas as pl
from jax.experimental.pallas import tpu as pltpu
from jax.sharding import PartitionSpec as P

SEQ = 1024
STEP = 10


EPS_NORM = 1e-06
THETA = 1000000.0
BETA_ONE = 0.9
BETA_TWO = 0.95
ADAM_EPS = 1e-08
DECAY_RATE = 0.1
RATE_QKV = 0.05
RATE_OUT = 0.3
RATE_GATE = 0.05
RATE_DOWN = 0.03
RATE_GAIN = 1.0


def rotary(positions, head_size):
    freq_index = jnp.arange(head_size // 2, dtype=jnp.float32)
    inverse = jnp.exp(freq_index * (-2.0 * math.log(THETA) / head_size))
    angles = positions.astype(jnp.float32)[:, None] * inverse[None, :]
    cosine = jnp.cos(angles)
    sine_table = jnp.sin(angles)
    return (jnp.concatenate([cosine, cosine], -1), jnp.concatenate([sine_table, sine_table], -1))


def rotate(values, cosine, sine_table):
    half_size = values.shape[-1] // 2
    turned = jnp.concatenate([-values[..., half_size:], values[..., :half_size]], -1)
    return values * cosine[:, None, :] + turned * sine_table[:, None, :]


def unrotate(gradient, cosine, sine_table):
    half_size = gradient.shape[-1] // 2
    turned = gradient * sine_table[:, None, :]
    rotated_back = jnp.concatenate([turned[..., half_size:], -turned[..., :half_size]], -1)
    return gradient * cosine[:, None, :] + rotated_back


def norm_back(grad_unit, unit_vals, factor):
    return factor * (grad_unit - unit_vals * jnp.mean(grad_unit * unit_vals, -1, keepdims=True))


def contract_rows(left, right):
    return lax.dot_general(
        left, right, (((0,), (0,)), ((), ())), preferred_element_type=jnp.float32
    )


def contract_cols(left, right):
    return lax.dot_general(
        left, right, (((1,), (1,)), ((), ())), preferred_element_type=jnp.float32
    )


def block_scores(query_part, key_part, first_row, block_rows, last_row):
    scores = jnp.einsum(
        "nqkgd,nskd->nkgqs", query_part, key_part, preferred_element_type=jnp.float32
    )
    causal = (first_row + jnp.arange(block_rows))[:, None] >= jnp.arange(last_row)[None, :]
    return jnp.where(causal, scores, -1000000000.0)


def attention_forward(query, key_rot, values_low, seq_len):
    block_rows = min(512, seq_len)
    outputs = []
    log_sums = []
    for first_row in range(0, seq_len, block_rows):
        last_row = first_row + block_rows
        query_part = query[:, first_row:last_row]
        scores = block_scores(query_part, key_rot[:, :last_row], first_row, block_rows, last_row)
        row_max = jnp.max(scores, -1, keepdims=True)
        exponent = jnp.exp(scores - row_max)
        row_total = jnp.sum(exponent, -1, keepdims=True)
        probs_low = (exponent / row_total).astype(jnp.bfloat16)
        outputs.append(
            jnp.einsum(
                "nkgqs,nskd->nqkgd",
                probs_low,
                values_low[:, :last_row],
                preferred_element_type=jnp.float32,
            )
        )
        log_sums.append(row_max + jnp.log(row_total))
    return (jnp.concatenate(outputs, 1), log_sums)


def attention_backward(query, key_rot, values_low, grad_att, log_sums, seq_len):
    block_rows = min(512, seq_len)
    query_grads = []
    key_grad = jnp.zeros(key_rot.shape, jnp.float32)
    value_grad = jnp.zeros(values_low.shape, jnp.float32)
    for block_index, first_row in enumerate(range(0, seq_len, block_rows)):
        last_row = first_row + block_rows
        query_part = query[:, first_row:last_row]
        grad_part = grad_att[:, first_row:last_row]
        key_part = key_rot[:, :last_row]
        value_part = values_low[:, :last_row]
        scores = block_scores(query_part, key_part, first_row, block_rows, last_row)
        probs = jnp.exp(scores - log_sums[block_index])
        probs_low = probs.astype(jnp.bfloat16)
        grad_probs = jnp.einsum(
            "nqkgd,nskd->nkgqs", grad_part, value_part, preferred_element_type=jnp.float32
        )
        grad_scores = (
            probs * (grad_probs - jnp.sum(probs * grad_probs, -1, keepdims=True))
        ).astype(jnp.bfloat16)
        query_grads.append(
            jnp.einsum(
                "nkgqs,nskd->nqkgd", grad_scores, key_part, preferred_element_type=jnp.float32
            )
        )
        padding = ((0, 0), (0, seq_len - last_row), (0, 0), (0, 0))
        key_grad = key_grad + jnp.pad(
            jnp.einsum(
                "nkgqs,nqkgd->nskd", grad_scores, query_part, preferred_element_type=jnp.float32
            ),
            padding,
        )
        value_grad = value_grad + jnp.pad(
            jnp.einsum(
                "nkgqs,nqkgd->nskd", probs_low, grad_part, preferred_element_type=jnp.float32
            ),
            padding,
        )
    return (jnp.concatenate(query_grads, 1), key_grad, value_grad)


def adamw(weight, gradient, moment, second, step_rate, decay_rate):
    moment = BETA_ONE * moment + (1.0 - BETA_ONE) * gradient
    second = BETA_TWO * second + (1.0 - BETA_TWO) * gradient * gradient
    first_hat = moment / (1.0 - BETA_ONE**STEP)
    second_hat = second / (1.0 - BETA_TWO**STEP)
    weight = weight - step_rate * (
        first_hat / (jnp.sqrt(second_hat) + ADAM_EPS) + decay_rate * weight
    )
    return (moment, second, weight)


def fence(*values):
    return lax.optimization_barrier(values)


MESH = pl.DeviceIdType.MESH
HEAD = 128
AHEAD = 2


def place_here():
    index, place = lax.axis_index("dp"), lax.axis_index("tensor")
    return lax.div(index, 2), lax.rem(index, 2), lax.div(place, 2), lax.rem(place, 2)


def device(zone, side, row, core):
    return (zone * 2 + side, row * 2 + core)


def flipped(zone, flip):
    bit = 1
    while bit <= flip:
        if flip & bit:
            zone = zone + bit - 2 * bit * lax.rem(lax.div(zone, bit), 2)
        bit *= 2
    return zone


def greet(devices, amount=None):
    barrier = pltpu.get_barrier_semaphore()
    for peer in devices:
        pl.semaphore_signal(barrier, inc=1, device_id=peer, device_id_type=MESH)
    pl.semaphore_wait(barrier, len(devices) if amount is None else amount)


def for_rows(count, body):
    step = 32

    def one(block, carry):
        body(pl.multiple_of(block * step, step), step)
        return carry

    lax.fori_loop(0, count // step, one, 0)


class Copies:
    def __init__(self, send_sems, recv_sems):
        self.send_sems, self.recv_sems = send_sems, recv_sems
        self.number = 0

    def make(self, source, target, peer):
        number, self.number = self.number, self.number + 1
        return pltpu.make_async_remote_copy(
            src_ref=source,
            dst_ref=target,
            send_sem=self.send_sems.at[number],
            recv_sem=self.recv_sems.at[number],
            device_id=peer,
            device_id_type=MESH,
        )

    def start(self, source, target, peer):
        copy = self.make(source, target, peer)
        copy.start()
        return copy


class GainSum:
    def __init__(self, plan, rest, width):
        self.plan, self.width = plan, width
        self.total = width + rest
        self.scratch = [
            pltpu.VMEM((8, 1, self.total), jnp.float32),
            pltpu.VMEM((plan.zones, 1, self.total), jnp.float32),
        ]
        self.output = jax.ShapeDtypeStruct((1, self.total), jnp.float32)
        self.count = 7 + plan.zones - 1

    def plane_peers(self, zone, side, row, core):
        steps = [(s, r, c) for s in range(2) for r in range(2) for c in range(2)][1:]
        turn = lambda value, step: 1 - value if step else value
        return [device(zone, turn(side, s), turn(row, r), turn(core, c)) for s, r, c in steps]

    def zone_peers(self, zone, side, row, core):
        return {flip: device(flipped(zone, flip), side, row, core) for flip in self.plan.flips[1:]}

    def start(self, copies, rest, blocks, plane_sums, zone_sums):
        zone, side, row, core = place_here()
        plan = self.plan
        size = self.width // plan.total
        self.copies, self.plane_sums, self.zone_sums, self.zone = copies, plane_sums, zone_sums, zone
        here = side * 4 + row * 2 + core
        plane_sums[here, :, pl.ds(self.width, self.total - self.width)] = rest[...]
        for slot in range(plan.total):
            owner = flipped(zone, plan.flips[slot % plan.zones]) * 2
            owner = owner + (core if slot < plan.zones else 1 - core)
            spot = pl.ds(pl.multiple_of(owner * size, size), size)
            plane_sums[here, :, spot] = blocks[:, pl.ds(slot * size, size)]
        self.plane = [
            copies.start(plane_sums.at[here], plane_sums.at[here], peer)
            for peer in self.plane_peers(zone, side, row, core)
        ]

    def middle(self):
        for copy in self.plane:
            copy.wait_recv()
        total = self.plane_sums[0]
        for place in range(1, 8):
            total = total + self.plane_sums[place]
        self.zone_sums[self.zone] = total
        zone, side, row, core = place_here()
        self.across = [
            self.copies.start(self.zone_sums.at[self.zone], self.zone_sums.at[self.zone], peer)
            for peer in self.zone_peers(zone, side, row, core).values()
        ]

    def finish(self, out):
        for copy in self.across:
            copy.wait_recv()
        total = self.zone_sums[0]
        for place in range(1, self.plan.zones):
            total = total + self.zone_sums[place]
        out[...] = total
        for copy in self.plane + self.across:
            copy.wait_send()


class ZoneBlocks:
    scratch = []

    def __init__(self, plan, source, slots, begin=0):
        self.flips, self.slots, self.sources, self.begin = plan.flips, list(slots), [source], begin
        self.outputs = [
            jax.ShapeDtypeStruct((len(self.slots),) + source.shape[1:], source.dtype)
        ]
        self.count, self.count_local = len(self.slots), 0
        self.in_hbm = False

    def peers(self, zone, side, row, core):
        return {
            self.flips[slot]: device(flipped(zone, self.flips[slot]), side, row, core)
            for slot in self.slots
        }

    def start(self, copies, local_sems, sources, targets, stages):
        zone, side, row, core = place_here()
        self.started = [
            copies.make(
                sources[0].at[slot],
                targets[0].at[number],
                device(flipped(zone, self.flips[slot]), side, row, core),
            )
            for number, slot in enumerate(self.slots)
        ]
        self.waiting = True
        if self.begin == 0:
            self.pump([0])

    def pump(self, steps):
        if self.waiting and self.begin in steps:
            self.waiting = False
            for copy in self.started:
                copy.start()

    def finish(self):
        for copy in self.started:
            copy.wait_send()
        for copy in self.started:
            copy.wait_recv()


def inner_zone(zone):
    return lax.rem(lax.div(zone + 1, 2), 2)


class SideDot:
    count, count_local, scratch, in_hbm = 0, 0, [], False

    def __init__(self, left, right):
        self.sources = [left, right]
        self.outputs = [jax.ShapeDtypeStruct((left.shape[0], right.shape[0]), jnp.bfloat16)]

    def peers(self, zone, side, row, core):
        return {}

    def some(self, first, last):
        left, right = self.refs
        size = 256

        def one(step, carry):
            here = pl.ds(pl.multiple_of(step * size, size), size)
            self.out[:, here] = dot(left[...], right[here, :], 1, 1).astype(jnp.bfloat16)
            return carry

        lax.fori_loop(first, last, one, 0)

    def start(self, copies, local_sems, sources, targets, stages):
        self.refs, self.out = sources, targets[0]
        self.steps = self.out.shape[1] // 256
        self.some(0, self.steps // 2)

    def pump(self, steps):
        if 0 in steps:
            self.some(self.steps // 2, self.steps)

    def finish(self):
        pass


class PairScatter:
    def __init__(self, parts, ready, pieces):
        self.sources, self.pieces = [parts, ready], pieces
        _, rows, columns = parts.shape
        self.size = rows // pieces
        self.outputs = [jax.ShapeDtypeStruct((2, rows, columns), parts.dtype)]
        self.scratch = [pltpu.VMEM((2, rows, columns), parts.dtype)] * 2
        self.count, self.count_local = 3 * pieces, 0
        self.in_hbm = False

    def peers(self, zone, side, row, core):
        return {
            1: device(flipped(zone, 1), side, row, core),
            3: device(flipped(zone, 3), side, row, core),
        }

    def start(self, copies, local_sems, sources, targets, stages):
        zone, side, row, core = place_here()
        self.parts, self.ready = sources
        self.out = targets[0]
        self.inward, self.crossed = stages
        inner_peer = device(flipped(zone, 3), side, row, core)
        outer_peer = device(flipped(zone, 1), side, row, core)
        self.inner = inner_zone(zone) == 1
        self.outer = inner_zone(zone) == 0
        pieces = [pl.ds(piece * self.size, self.size) for piece in range(self.pieces)]
        self.steps = [(slot, rows) for slot in (0, 1) for rows in pieces]
        self.to_inner = [
            copies.make(self.parts.at[2, rows], self.inward.at[1, rows], outer_peer)
            for rows in pieces
        ]
        self.across = [
            copies.make(self.inward.at[slot, rows], self.crossed.at[slot, rows], inner_peer)
            for slot, rows in self.steps
        ]

        @pl.when(self.outer)
        def _():
            for copy in self.to_inner[:AHEAD]:
                copy.start()

        @pl.when(self.inner)
        def _():
            for step in range(self.pieces):
                slot, rows = self.steps[step]
                self.add(self.inward, slot, rows, self.parts.at[2], self.ready)
                self.across[step].start()

    def add(self, target, slot, rows, left, right):
        def some(row, count):
            here = pl.ds(rows.start + row, count)
            both = left[here, :].astype(jnp.float32) + right[here, :].astype(jnp.float32)
            target.at[slot][here, :] = both.astype(jnp.bfloat16)

        for_rows(self.size, some)

    def pump(self, steps):
        steps = [step for step in steps if step < self.pieces]

        @pl.when(self.inner)
        def _():
            for step in steps:
                slot, rows = self.steps[self.pieces + step]
                self.to_inner[step].wait_recv()
                self.add(self.inward, slot, rows, self.parts.at[3], self.inward.at[1])
                self.across[self.pieces + step].start()
                self.settle(step)

        @pl.when(self.outer)
        def _():
            for step in steps:
                self.to_inner[step].wait_send()
                for copy in self.to_inner[step + AHEAD : step + AHEAD + 1]:
                    copy.start()

    def settle(self, step):
        slot, rows = self.steps[step]
        self.across[step].wait_recv()
        self.add(self.out, slot, rows, self.parts.at[slot], self.crossed.at[slot])

    def finish(self):
        @pl.when(self.inner)
        def _():
            for step in range(self.pieces, len(self.steps)):
                self.settle(step)
            for copy in self.across:
                copy.wait_send()

        @pl.when(self.outer)
        def _():
            for slot in (0, 1):

                def some(row, count, slot=slot):
                    here = pl.ds(row, count)
                    self.out.at[slot][here, :] = self.parts.at[slot][here, :]

                for_rows(self.parts.shape[1], some)


class BlockGrad:
    in_hbm = False

    def __init__(self, plan, left, right):
        self.zones, self.flips = plan.zones, plan.flips
        self.sources = [left, right]
        shape = (left.shape[1] // plan.total, right.shape[1])
        low = jnp.bfloat16
        self.outputs = [jax.ShapeDtypeStruct(shape, low)]
        self.scratch = [pltpu.VMEM((plan.zones,) + shape, low)] * 4
        self.count, self.count_local = 2 * plan.zones, 0

    def peers(self, zone, side, row, core):
        return {flip: device(flipped(zone, flip), side, row, core) for flip in self.flips[1:]}

    def product(self, block):
        size = self.out.shape[0]
        return dot(self.left[:, pl.ds(block * size, size)], self.right[...], 0, 0)

    def start(self, copies, local_sems, sources, targets, stages):
        zone, side, row, core = place_here()
        self.left, self.right = sources
        self.out = targets[0]
        self.far, self.got, self.parts, self.arrived = stages
        core_peer = device(zone, side, row, 1 - core)
        self.order = list(range(1, self.zones)) + [0]
        self.over = [
            copies.make(self.far.at[slot], self.got.at[slot], core_peer)
            for slot in range(self.zones)
        ]
        self.along = [
            copies.make(
                self.parts.at[slot],
                self.arrived.at[slot],
                device(flipped(zone, self.flips[slot]), side, row, core),
            )
            for slot in range(1, self.zones)
        ]
        for slot in self.order:
            self.far[slot] = self.product(self.zones + slot).astype(jnp.bfloat16)
            self.over[slot].start()

    def pump(self, steps):
        for slot in self.order if 0 in steps else []:
            near = self.product(slot)
            self.over[slot].wait_recv()
            self.parts[slot] = (near + self.got[slot].astype(jnp.float32)).astype(jnp.bfloat16)
            if slot:
                self.along[slot - 1].start()

    def finish(self):
        total = self.parts[0].astype(jnp.float32)
        for slot in range(1, self.zones):
            self.along[slot - 1].wait_recv()
            total = total + self.arrived[slot].astype(jnp.float32)
        self.out[...] = total.astype(jnp.bfloat16)
        for copy in self.over + self.along:
            copy.wait_send()


class PairTree:
    def __init__(self, pairs, pieces):
        self.pairs = [len(pair) for pair in pairs]
        self.sources = [shard for pair in pairs for shard in pair]
        self.pieces = pieces
        self.outputs = [
            jax.ShapeDtypeStruct((8,) + own.shape, own.dtype) for own, *_ in pairs
        ]
        self.count = 6 * sum(pieces) + 2 * len(pairs) + self.pairs.count(1)
        self.count_local = 2 * len(pairs) + 2 * sum(pieces)
        self.scratch = [pltpu.VMEM((2,) + own.shape, own.dtype) for own, *_ in pairs]
        self.scratch += [pltpu.VMEM(p[0].shape, p[0].dtype) for p in pairs if len(p) == 1]
        self.in_hbm = True

    def peers(self, zone, side, row, core):
        return {
            1: device(flipped(zone, 1), side, row, core),
            3: device(flipped(zone, 3), side, row, core),
            "core": device(zone, side, row, 1 - core),
        }

    def start(self, copies, local_sems, sources, targets, stages):
        zone, side, row, core = place_here()
        inner_peer = device(flipped(zone, 3), side, row, core)
        outer_peer = device(flipped(zone, 1), side, row, core)
        core_peer = device(zone, side, row, 1 - core)
        self.inner = inner_zone(zone) == 1
        self.outer = inner_zone(zone) == 0
        self.across, self.onward, self.late, self.place = [], [], [], []
        self.shared, self.kept, self.partners, self.later = [], [], [], []
        sem = 0
        sources, late_stages = list(sources), list(stages[len(targets) :])
        for weight, full in enumerate(targets):
            landing = stages[weight]
            pair = [sources.pop(0) for _ in range(self.pairs[weight])]
            if len(pair) == 1:
                pair.append(late_stages.pop(0))
                self.partners.append(copies.start(pair[0], pair[1], outer_peer))
            size = pair[0].shape[0] // self.pieces[weight]
            for piece in range(self.pieces[weight]):
                rows = pl.ds(piece * size, size)
                for slot in (0, 1):
                    here = landing.at[slot, rows]
                    self.across.append(copies.make(pair[slot].at[rows], here, inner_peer))
                    self.onward.append(copies.make(here, landing.at[1 - slot, rows], outer_peer))
                    self.late.append(copies.make(here, full.at[6 + slot, rows], core_peer))
                    self.place.append(
                        pltpu.make_async_copy(here, full.at[2 + slot, rows], local_sems.at[sem])
                    )
                    sem += 1
            for slot in (0, 1):
                self.shared.append(copies.make(pair[slot], full.at[4 + slot], core_peer))
                self.kept.append(
                    pltpu.make_async_copy(pair[slot], full.at[slot], local_sems.at[sem])
                )
                sem += 1
                if slot >= self.pairs[weight]:
                    self.later += [self.shared[-1], self.kept[-1]]
                else:
                    self.shared[-1].start()
                    self.kept[-1].start()

        @pl.when(self.inner)
        def _():
            for copy in self.across[:AHEAD]:
                copy.start()

    def arrive(self, number):
        self.onward[number].wait_recv()
        swapped = number + 1 - 2 * (number % 2)
        self.late[swapped].start()
        self.place[swapped].start()

    def pump(self, steps):
        steps = [step for step in steps if step < len(self.across)]

        @pl.when(self.inner)
        def _():
            for here in steps:
                self.across[here].wait_recv()
                for copy in self.across[here + AHEAD : here + AHEAD + 1]:
                    copy.start()
                self.onward[here].start()
                self.late[here].start()
                self.place[here].start()

        @pl.when(self.outer)
        def _():
            for step in steps:
                if step > 0:
                    self.arrive(step - 1)

        for copy in self.partners if 1 in steps else []:
            copy.wait_recv()
            copy.wait_send()
        for copy in self.later if 1 in steps else []:
            copy.start()

    def finish(self):
        @pl.when(self.inner)
        def _():
            for copy in self.across + self.onward:
                copy.wait_send()

        @pl.when(self.outer)
        def _():
            self.arrive(len(self.onward) - 1)

        for copy in self.kept + self.place:
            copy.wait()
        for copy in self.shared + self.late:
            copy.wait_send()
        for copy in self.shared + self.late:
            copy.wait_recv()


def sum_eighths(
    copies, row_peer, side_peer, send, keep, forward, first, second, store, begin, pump
):
    size = send.shape[0] // 4
    part = lambda ref, slot: ref.at[pl.ds(slot * size, size)]
    arrivals = [
        copies.start(part(send, 1), part(first, 1), row_peer),
        copies.start(part(send, 3), part(first, 3), side_peer),
        copies.start(part(send, 0), part(first, 0), row_peer),
        copies.start(part(send, 2), part(first, 2), side_peer),
    ]
    begin()
    passed = []
    for number, slot, peer in ((0, 1, side_peer), (1, 3, row_peer)):
        arrivals[number].wait_recv()

        def add(row, count, number=number, slot=slot):
            here = pl.ds(slot * size + row, count)
            both = keep[here, :].astype(jnp.float32) + first[here, :].astype(jnp.float32)
            forward[pl.ds(number * size + row, count), :] = both.astype(jnp.bfloat16)

        for_rows(size, add)
        passed.append(copies.start(part(forward, number), part(second, number), peer))
    pump([0])
    for number, slot in ((0, 0), (1, 2)):
        arrivals[2 + number].wait_recv()
        passed[number].wait_recv()

        def total(row, count, number=number, slot=slot):
            here = pl.ds(slot * size + row, count)
            sums = keep[here, :].astype(jnp.float32) + first[here, :].astype(jnp.float32)
            sums = sums + second[pl.ds(number * size + row, count), :].astype(jnp.float32)
            store(number, row, count, sums)

        for_rows(size, total)
        yield number
    for copy in arrivals + passed:
        copy.wait_send()


def halves(terms):
    rows = terms.shape[0] // 2
    return terms.at[pl.ds(0, rows)], terms.at[pl.ds(rows, rows)]


def split_refs(refs, jobs, extra_count, out_count):
    refs = list(refs)
    take = lambda count: [refs.pop(0) for _ in range(count)]
    extras = take(extra_count)
    sources = [take(len(job.sources)) for job in jobs]
    full = take(1)[0]
    outs = take(out_count)
    targets = [take(len(job.outputs)) for job in jobs]
    return extras, sources, full, outs, targets, refs


def spread_kernel(middle, jobs, extra_count, out_count, gain_sum, plan, terms, *refs):
    keep, send = halves(terms)
    extras, sources, full, outs, targets, scratch = split_refs(refs, jobs, extra_count, out_count)
    forward, first, second, send_sems, recv_sems, local_sems, *stages = scratch
    zone, side, row, core = place_here()
    row_peer, side_peer = device(zone, side, 1 - row, core), device(zone, 1 - side, row, core)
    copies = Copies(send_sems, recv_sems)
    size = send.shape[0] // 4
    part = lambda slot: full.at[pl.ds(slot * size, size)]
    for out in outs:
        if out.shape[0] == 1:
            out[...] = jnp.zeros_like(out)
    peers = {}
    for job in jobs:
        peers.update(job.peers(zone, side, row, core))
    greet([row_peer, side_peer] + list(peers.values()))

    def begin():
        spot = 0
        for job, source, target in zip(jobs, sources, targets):
            own_stages = stages[spot : spot + len(job.scratch)]
            job.start(copies, local_sems, source, target, own_stages)
            spot += len(job.scratch)

    def pump(steps):
        for job in jobs:
            job.pump(steps)

    def store(number, row, count, sums):
        own = pl.ds(number * size + row, count)
        full[pl.ds(2 * number * size + row, count), :] = middle(own, sums, extras, outs)

    firsts, seconds = [], []
    for number in sum_eighths(
        copies, row_peer, side_peer, send, keep, forward, first, second, store, begin, pump
    ):
        near, other = (side_peer, row_peer) if number == 0 else (row_peer, side_peer)
        slot = 2 * number
        firsts.append(copies.start(part(slot), part(slot + 1), near))
        seconds.append(copies.start(part(slot), part(4 + slot), other))
    pump([1])
    firsts[0].wait_recv()
    seconds.append(copies.start(part(1), part(5), row_peer))
    firsts[1].wait_recv()
    seconds.append(copies.start(part(3), part(7), side_peer))
    pump(range(2, 64))
    for copy in seconds:
        copy.wait_recv()
    for copy in firsts + seconds:
        copy.wait_send()
    for job in jobs:
        job.finish()


def home_kernel(middle, jobs, extra_count, out_count, gain_sum, plan, terms, *refs):
    keep, send = halves(terms)
    extras, sources, result, outs, targets, scratch = split_refs(refs, jobs, extra_count, out_count)
    forward, first, second, own, full, send_sems, recv_sems, local_sems, *rest = scratch
    gain_scratch, stages = (rest[:2], rest[2:]) if gain_sum is not None else ([], rest)
    block = extras[3]
    zone, side, row, core = place_here()
    row_peer, side_peer = device(zone, side, 1 - row, core), device(zone, 1 - side, row, core)
    core_peer, other_peer = device(zone, side, row, 1 - core), device(zone, 1 - side, row, 1 - core)
    copies = Copies(send_sems, recv_sems)
    size = send.shape[0] // 4
    at_home = side == core
    away = side != core
    for out in outs:
        if out.shape[0] == 1:
            out[...] = jnp.zeros_like(out)
    peers = {}
    for job in jobs:
        peers.update(job.peers(zone, side, row, core))
    plane = [row_peer, side_peer, core_peer, other_peer]
    if gain_sum is not None:
        plane = gain_sum.plane_peers(zone, side, row, core)
        peers.update(gain_sum.zone_peers(zone, side, row, core))
    greet(plane + list(peers.values()))

    def begin():
        spot = 0
        for job, source, target in zip(jobs, sources, targets):
            own_stages = stages[spot : spot + len(job.scratch)]
            job.start(copies, local_sems, source, target, own_stages)
            spot += len(job.scratch)

    def pump(steps):
        for job in jobs:
            job.pump(steps)

    def store(number, start, count, sums):
        here = pl.ds(number * size + start, count)
        values = middle(here, sums, extras, outs)
        own[here, :] = values
        eighth = row * 2 + side if number == 0 else 4 + side * 2 + row

        @pl.when(at_home)
        def _():
            full[pl.ds(pl.multiple_of(eighth * size + start, 32), count), :] = values

    def piece(number, x, y):
        start = (x * 2 + y) * size if number == 0 else (4 + y * 2 + x) * size
        return full.at[pl.ds(pl.multiple_of(start, size), size)]

    both = (0, 1)
    part = lambda ref, number: ref.at[pl.ds(number * size, size)]
    block_over = [copies.make(part(block, k), piece(k, row, side), core_peer) for k in both]
    block_side = [copies.make(part(block, k), piece(k, row, side), other_peer) for k in both]
    to_side = [copies.make(part(own, k), piece(k, row, side), side_peer) for k in both]
    to_row = [copies.make(piece(k, row, side), piece(k, row, side), row_peer) for k in both]
    pass_row = [
        copies.make(piece(k, row, 1 - side), piece(k, row, 1 - side), row_peer) for k in both
    ]

    @pl.when(at_home)
    def _():
        for copy in block_over:
            copy.start()

    for _ in sum_eighths(
        copies, row_peer, side_peer, send, keep, forward, first, second, store, begin, pump
    ):
        pass
    pump([1])
    if gain_sum is not None:
        gain_sum.start(copies, extras[-1], outs[0], *gain_scratch)

    @pl.when(away)
    def _():
        for copy in to_side + block_side:
            copy.start()
        for copy in block_over:
            copy.wait_recv()

    for copy in to_row:
        copy.start()
    if gain_sum is not None:
        gain_sum.middle()

    @pl.when(at_home)
    def _():
        for copy in to_side:
            copy.wait_recv()
        for copy in block_over:
            copy.wait_send()

    @pl.when(away)
    def _():
        for copy in block_side:
            copy.wait_recv()
        for copy in to_side + block_side:
            copy.wait_send()

    for copy in pass_row:
        copy.start()
    for copy in to_row + pass_row:
        copy.wait_recv()
        copy.wait_send()
    natural, local = block_columns(plan, full.shape[1], side)

    def some(start, count):
        here = pl.ds(start, count)
        for a, b in zip(natural, local):
            result[here, a] = full[here, b]

    for_rows(full.shape[0], some)
    if gain_sum is not None:
        gain_sum.finish(outs[-1])
    for job in jobs:
        job.finish()


def sum_rows(plan, kernel, middle, terms, extras, outs, number, jobs=(), gain_sum=None):
    half, width = terms.shape[0] // 2, terms.shape[1]
    eighth = half // 4
    low = jnp.bfloat16
    vmem, hbm = pl.BlockSpec(memory_space=pltpu.VMEM), pl.BlockSpec(memory_space=pl.ANY)
    scratch = [
        pltpu.VMEM((2 * eighth, width), low),
        pltpu.VMEM((half, width), low),
        pltpu.VMEM((2 * eighth, width), low),
    ]
    if kernel is home_kernel:
        scratch.append(pltpu.VMEM((2 * eighth, width), low))
        scratch.append(pltpu.VMEM((2 * half, width), low))
    copies = (12 if kernel is spread_kernel else 16) + sum(job.count for job in jobs)
    local = max([2] + [job.count_local for job in jobs])
    if gain_sum is not None:
        copies += gain_sum.count
        outs = outs + [gain_sum.output]
    scratch += [pltpu.SemaphoreType.DMA((count,)) for count in (copies, copies, local)]
    if gain_sum is not None:
        scratch += gain_sum.scratch
    scratch += [stage for job in jobs for stage in job.scratch]
    sources = [source for job in jobs for source in job.sources]
    targets = [target for job in jobs for target in job.outputs]
    return pl.pallas_call(
        functools.partial(kernel, middle, jobs, len(extras), len(outs), gain_sum, plan),
        out_shape=[jax.ShapeDtypeStruct((2 * half, width), low)] + outs + targets,
        in_specs=[vmem] * (1 + len(extras) + len(sources)),
        out_specs=[vmem] * (1 + len(outs))
        + [hbm if job.in_hbm else vmem for job in jobs for _ in job.outputs],
        scratch_shapes=scratch,
        compiler_params=pltpu.CompilerParams(
            collective_id=number, has_side_effects=True, vmem_limit_bytes=56 * 2**20
        ),
        cost_estimate=pl.CostEstimate(flops=10**6, bytes_accessed=10**5, transcendentals=0),
        name=middle.__name__,
    )(terms, *extras, *sources)


def block_columns(plan, width, of_core=None):
    if not plan.ordered:
        return [pl.ds(0, width)], [pl.ds(0, width)]
    zone, _, _, core = place_here()
    core = core if of_core is None else of_core
    size, zones = width // plan.total, plan.zones
    owners = [
        flipped(zone, plan.flips[slot % zones]) * 2 + (core if slot < zones else 1 - core)
        for slot in range(plan.total)
    ]
    natural = [pl.ds(pl.multiple_of(owner * size, size), size) for owner in owners]
    return natural, [pl.ds(slot * size, size) for slot in range(plan.total)]


def copy_rows(source, target):
    def some(row, count):
        target[pl.ds(row, count), :] = source[pl.ds(row, count), :]

    if source.shape[0] % 32:
        target[...] = source[...]
    else:
        for_rows(source.shape[0], some)


def cast_rows(source, target):
    def some(row, count):
        here = pl.ds(row, count)
        target[here, :] = source[here, :].astype(target.dtype)

    for_rows(source.shape[0], some)


def opening_kernel(plan, wide_qkv, gains, wide_gate, wide_out, wide_down, tokens, angles, *refs):
    qkv_full, gains_full, turned_gate, turned_out, turned_down, turned_tokens, turned_angles = refs[:7]
    partner_gate, send_sems, recv_sems, tokens_stage, qkv, gate, out, down = refs[7:]
    cast_rows(wide_qkv, qkv)
    zone, side, row, core = place_here()
    partner = device(zone, core, row, side)
    row_peer, core_peer = device(zone, side, 1 - row, core), device(zone, side, row, 1 - core)
    zone_peers = [device(flipped(zone, flip), side, row, core) for flip in plan.flips[1:]]
    at_home, away = side == core, side != core
    always = [row_peer, core_peer] + zone_peers

    @pl.when(at_home)
    def _():
        greet(always)

    @pl.when(away)
    def _():
        greet(always + [partner])

    copies = Copies(send_sems, recv_sems)
    zones = plan.zones
    own = (gains, qkv, angles, gate, out, down)
    ends = (gains_full.at[0], qkv_full.at[0], turned_angles, turned_gate, turned_out, turned_down)
    units = wide_gate.shape[2]

    def cast_rest():
        for half in (0, 1):
            cast_rows(wide_gate.at[half], gate.at[:, pl.ds(half * units, units)])
        cast_rows(wide_out, out)
        cast_rows(wide_down, down)

    turn = [copies.make(source, target, partner) for source, target in zip(own, ends)]
    pieces = 2
    size = tokens.shape[0] // (2 * pieces)
    spots = [
        pl.ds(pl.multiple_of((row * pieces + piece) * size, size), size) for piece in range(pieces)
    ]
    turn_rows = [copies.make(tokens.at[s], tokens_stage.at[s], partner) for s in spots]
    pass_rows = [copies.make(tokens_stage.at[s], tokens_stage.at[s], row_peer) for s in spots]
    natural, local = block_columns(plan, tokens.shape[1])

    def lay_down(all_tokens):
        def some(start, count):
            here = pl.ds(start, count)
            for a, b in zip(natural, local):
                turned_tokens[here, b] = all_tokens[here, a]

        for_rows(all_tokens.shape[0], some)

    slots = list(range(1, zones))
    weights = ((gains, gains_full), (qkv, qkv_full))
    from_own = [
        [copies.make(source, full.at[slot], zone_peers[slot - 1]) for slot in slots]
        + [copies.make(source, full.at[zones], core_peer)]
        for source, full in weights
    ] + [[copies.make(gate, partner_gate, zone_peers[0])]]
    copies.number -= 2 * zones + 1
    from_turned = [
        [copies.make(full.at[0], full.at[slot], zone_peers[slot - 1]) for slot in slots]
        + [copies.make(full.at[0], full.at[zones], core_peer)]
        for _, full in weights
    ] + [[copies.make(turned_gate, partner_gate, zone_peers[0])]]
    cross = [
        [copies.make(full.at[slot], full.at[zones + slot], core_peer) for slot in slots]
        for _, full in weights
    ]

    def cross_over(k):
        for which in (0, 1):
            from_turned[which][k].wait_recv()
            cross[which][k].start()

    @pl.when(away)
    def _():
        for copy in turn[:3]:
            copy.start()
        cast_rest()
        for which in (0, 1):
            turn[which].wait_recv()
            for copy in from_turned[which]:
                copy.start()
        turn[3].start()
        turn_rows[0].start()
        turn[3].wait_recv()
        from_turned[2][0].start()
        turn_rows[1].start()
        cross_over(0)
        turn_rows[0].wait_recv()
        pass_rows[0].start()
        for copy in turn[4:]:
            copy.start()
        turn_rows[1].wait_recv()
        pass_rows[1].start()

    @pl.when(at_home)
    def _():
        for copy in from_own[0] + from_own[1]:
            copy.start()
        cast_rest()
        for copy in from_own[2]:
            copy.start()
        for source, target in zip(own, ends):
            copy_rows(source, target)
        lay_down(tokens)
        cross_over(0)

    for k in range(1, zones - 1):
        cross_over(k)
    for which in (0, 1):
        from_turned[which][zones - 1].wait_recv()
        for copy in from_turned[which]:
            copy.wait_send()
        for copy in cross[which]:
            copy.wait_recv()
            copy.wait_send()
    from_turned[2][0].wait_recv()
    from_turned[2][0].wait_send()

    @pl.when(away)
    def _():
        for copy in pass_rows + turn[2:3] + turn[4:]:
            copy.wait_recv()
        lay_down(tokens_stage)
        for copy in turn + turn_rows + pass_rows:
            copy.wait_send()


def opening(plan, qkv, gains, gate, out, down, tokens, angles, number):
    low = jnp.bfloat16
    vmem = pl.BlockSpec(memory_space=pltpu.VMEM)
    like = lambda v: jax.ShapeDtypeStruct(v.shape, v.dtype)
    whole = lambda v: jax.ShapeDtypeStruct((2 * plan.zones,) + v.shape, low)
    operands = (qkv, gains, gate, out, down, tokens, angles)
    low_gate = jax.ShapeDtypeStruct((gate.shape[1], 2 * gate.shape[2]), low)
    low_out = jax.ShapeDtypeStruct(out.shape, low)
    low_down = jax.ShapeDtypeStruct(down.shape, low)
    outputs = [whole(qkv), whole(gains), low_gate, low_out, low_down, like(tokens), like(angles)]
    outputs += [low_gate]
    copies = 6 + 4 + 2 * plan.zones + 1 + 2 * (plan.zones - 1)
    return pl.pallas_call(
        functools.partial(opening_kernel, plan),
        out_shape=outputs,
        in_specs=[vmem] * len(operands),
        out_specs=[vmem] * len(outputs),
        scratch_shapes=[
            pltpu.SemaphoreType.DMA((copies,)),
            pltpu.SemaphoreType.DMA((copies,)),
            pltpu.VMEM(tokens.shape, tokens.dtype),
            pltpu.VMEM(qkv.shape, low),
            pltpu.VMEM(low_gate.shape, low),
            pltpu.VMEM(out.shape, low),
            pltpu.VMEM(down.shape, low),
        ],
        compiler_params=pltpu.CompilerParams(
            collective_id=number, has_side_effects=True, vmem_limit_bytes=56 * 2**20
        ),
        cost_estimate=pl.CostEstimate(flops=10**6, bytes_accessed=10**5, transcendentals=0),
        name="opening",
    )(*operands)


def inverse_rms(values):
    return lax.rsqrt(jnp.mean(values * values, -1, keepdims=True) + EPS_NORM)


def hidden_rows(own, sums, extras, outs):
    tokens, gain = extras
    hidden = tokens[own, :].astype(jnp.float32) + sums
    outs[0][own, :] = hidden
    return (hidden * inverse_rms(hidden) * gain[...]).astype(jnp.bfloat16)


def grad_hidden_rows(own, sums, extras, outs):
    hidden, out_grad, gain = extras
    values = hidden[own, :]
    factor = inverse_rms(values)
    unit = values * factor
    outs[1][...] += jnp.sum(sums * unit, 0, keepdims=True)
    grad = out_grad[own, :].astype(jnp.float32) + norm_back(sums * gain[...], unit, factor)
    outs[0][own, :] = grad
    return grad.astype(jnp.bfloat16)


def grad_input_rows(own, sums, extras, outs):
    tokens, grad_hidden, gain = extras[:3]
    values = tokens[own, :].astype(jnp.float32)
    factor = inverse_rms(values)
    unit = values * factor
    outs[0][...] += jnp.sum(sums * unit, 0, keepdims=True)
    return (grad_hidden[own, :] + norm_back(sums * gain[...], unit, factor)).astype(jnp.bfloat16)


def dot(left, right, left_dim=1, right_dim=0):
    return lax.dot_general(
        left, right, (((left_dim,), (right_dim,)), ((), ())), preferred_element_type=jnp.float32
    )


def turn_head(values, cosine, signed_sine):
    return values * cosine + pltpu.roll(values, HEAD // 2, 1) * signed_sine


def turn_back(gradient, cosine, signed_sine):
    return gradient * cosine + pltpu.roll(gradient * signed_sine, HEAD // 2, 1)


def softmax_block(query, key, first_row):
    rows, keys = query.shape[0], key.shape[0]
    scores = dot(query, key, 1, 1)
    row_at = lax.broadcasted_iota(jnp.int32, (rows, keys), 0) + first_row
    key_at = lax.broadcasted_iota(jnp.int32, (rows, keys), 1)
    scores = jnp.where(key_at <= row_at, scores, -1000000000.0)
    exponent = jnp.exp(scores - jnp.max(scores, -1, keepdims=True))
    return exponent / jnp.sum(exponent, -1, keepdims=True)


def eighth_owners():
    _, side, row, _ = place_here()
    own, off = (row, side), (1 - row, 1 - side)
    first = lambda x, y: x * 2 + y
    second = lambda x, y: 4 + y * 2 + x
    return [
        first(own[0], own[1]),
        first(own[0], off[1]),
        second(own[0], own[1]),
        second(off[0], own[1]),
        first(off[0], own[1]),
        first(off[0], off[1]),
        second(own[0], off[1]),
        second(off[0], off[1]),
    ]


def reorder_rows(source, target, into_local):
    size = source.shape[0] // 8
    for slot, owner in enumerate(eighth_owners()):
        natural = pl.ds(pl.multiple_of(owner * size, size), size)
        local = pl.ds(slot * size, size)
        if into_local:
            target[local, :] = source[natural, :]
        else:
            target[natural, :] = source[local, :]


def forward_kernel(
    tokens, weights, gain_in, gain_q, gain_k, cosine, sine,
    normed, raw, query, key, value, local, attended,
):
    low = jnp.bfloat16
    total, heads = tokens.shape[0], query.shape[1] // HEAD
    block, wide = 256, 512

    def project(step, carry):
        rows = pl.ds(pl.multiple_of(step * wide, wide), wide)
        values = tokens[rows, :].astype(jnp.float32)
        normed[rows, :] = (values * inverse_rms(values) * gain_in[...]).astype(low)
        raw[rows, :] = dot(normed[rows, :], weights[...])
        turns = (cosine[rows, :], sine[rows, :])
        for head in range(heads):
            column = (head // 2) * 4 * HEAD + (head % 2) * HEAD
            values = raw[rows, pl.ds(column, HEAD)]
            values = turn_head(values * inverse_rms(values) * gain_q[...], *turns)
            query[rows, pl.ds(head * HEAD, HEAD)] = (values * (1.0 / math.sqrt(HEAD))).astype(low)
        for group in range(heads // 2):
            column = group * 4 * HEAD + 2 * HEAD
            here = pl.ds(group * HEAD, HEAD)
            values = raw[rows, pl.ds(column, HEAD)]
            values = turn_head(values * inverse_rms(values) * gain_k[...], *turns)
            key[rows, here] = values.astype(low)
            value[rows, here] = raw[rows, pl.ds(column + HEAD, HEAD)].astype(low)
        return carry

    lax.fori_loop(0, total // wide, project, 0)

    def attend(head, carry):
        mine = pl.ds(pl.multiple_of(head * HEAD, HEAD), HEAD)
        shared = pl.ds(pl.multiple_of(lax.div(head, 2) * HEAD, HEAD), HEAD)
        for start in range(0, total, SEQ):
            for first in range(0, SEQ, block):
                rows, keys = pl.ds(start + first, block), pl.ds(start, first + block)
                probs = softmax_block(query[rows, mine], key[keys, shared], first)
                attended[rows, mine] = dot(probs.astype(low), value[keys, shared]).astype(low)
        return carry

    lax.fori_loop(0, heads, attend, 0)
    reorder_rows(attended, local, True)


def attention(tokens, weights, gain_in, gain_q, gain_k, cosine, sine):
    total = tokens.shape[0]
    columns = weights.shape[1]
    low = jnp.bfloat16
    shape = lambda width, kind=low: jax.ShapeDtypeStruct((total, width), kind)
    vmem = pl.BlockSpec(memory_space=pltpu.VMEM)
    return pl.pallas_call(
        forward_kernel,
        out_shape=[
            shape(tokens.shape[1]),
            shape(columns, jnp.float32),
            shape(columns // 2),
            shape(columns // 4),
            shape(columns // 4),
            shape(columns // 2),
        ],
        in_specs=[vmem] * 7,
        out_specs=[vmem] * 6,
        scratch_shapes=[pltpu.VMEM((total, columns // 2), low)],
        compiler_params=pltpu.CompilerParams(vmem_limit_bytes=48 * 2**20),
        cost_estimate=pl.CostEstimate(flops=10**6, bytes_accessed=10**5, transcendentals=0),
        name="attention",
    )(tokens, weights, gain_in, gain_q, gain_k, cosine, sine)


def backward_kernel(
    query, key, value, raw, grad_rows, gain_q, gain_k, cosine, sine,
    mixed, mixed_local, query_gain, key_gain, grad, key_sum, value_sum,
):
    low = jnp.bfloat16
    total, heads = query.shape[0], query.shape[1] // HEAD
    block = 256
    reorder_rows(grad_rows, grad, False)
    query_gain[...] = jnp.zeros_like(query_gain)
    key_gain[...] = jnp.zeros_like(key_gain)

    def head_norm_back(rows, column, gradient, gain, gain_grad):
        values = raw[rows, column]
        factor = inverse_rms(values)
        unit = values * factor
        turned = turn_back(gradient, cosine[rows, :], sine[rows, :])
        gain_grad[...] += jnp.sum(turned * unit, 0, keepdims=True)
        mixed[rows, column] = norm_back(turned * gain[...], unit, factor).astype(low)

    def one_group(group, carry):
        at = lambda offset: pl.ds(pl.multiple_of(group * 4 * HEAD + offset * HEAD, HEAD), HEAD)
        shared = pl.ds(pl.multiple_of(group * HEAD, HEAD), HEAD)
        key_sum[...] = jnp.zeros_like(key_sum)
        value_sum[...] = jnp.zeros_like(value_sum)
        for head in (0, 1):
            mine = pl.ds(pl.multiple_of((group * 2 + head) * HEAD, HEAD), HEAD)
            for start in range(0, total, SEQ):
                for first in range(0, SEQ, block):
                    rows, keys = pl.ds(start + first, block), pl.ds(start, first + block)
                    query_part, grad_part = query[rows, mine], grad[rows, mine]
                    probs = softmax_block(query_part, key[keys, shared], first)
                    weighed = probs * dot(grad_part, value[keys, shared], 1, 1)
                    scores = weighed - probs * jnp.sum(weighed, -1, keepdims=True)
                    scores = scores.astype(low)
                    grad_query = dot(scores, key[keys, shared]) * (1.0 / math.sqrt(HEAD))
                    head_norm_back(rows, at(head), grad_query, gain_q, query_gain)
                    key_sum[keys, :] += dot(scores, query_part, 0, 0)
                    value_sum[keys, :] += dot(probs.astype(low), grad_part, 0, 0)
        for first in range(0, total, block):
            rows = pl.ds(first, block)
            head_norm_back(rows, at(2), key_sum[rows, :], gain_k, key_gain)
            mixed[rows, at(3)] = value_sum[rows, :].astype(low)
        return carry

    lax.fori_loop(0, heads // 2, one_group, 0)
    reorder_rows(mixed, mixed_local, True)


def attention_back(query, key, value, raw, grad_rows, gain_q, gain_k, cosine, sine):
    total, columns = raw.shape
    low = jnp.bfloat16
    vmem = pl.BlockSpec(memory_space=pltpu.VMEM)
    return pl.pallas_call(
        backward_kernel,
        out_shape=[
            jax.ShapeDtypeStruct((total, columns), low),
            jax.ShapeDtypeStruct((total, columns), low),
            jax.ShapeDtypeStruct((1, HEAD), jnp.float32),
            jax.ShapeDtypeStruct((1, HEAD), jnp.float32),
        ],
        in_specs=[vmem] * 9,
        out_specs=[vmem] * 4,
        scratch_shapes=[
            pltpu.VMEM(grad_rows.shape, low),
            pltpu.VMEM((total, HEAD), jnp.float32),
            pltpu.VMEM((total, HEAD), jnp.float32),
        ],
        compiler_params=pltpu.CompilerParams(vmem_limit_bytes=48 * 2**20),
        cost_estimate=pl.CostEstimate(flops=10**6, bytes_accessed=10**5, transcendentals=0),
        name="attention_back",
    )(query, key, value, raw, grad_rows, gain_q, gain_k, cosine, sine)


def feed_kernel(plan, rows, own_grad, got_grad, gate_up, up_part, down, active, grads, out_grad):
    low = jnp.bfloat16
    block = 512
    tile = down.shape[1]
    step = pl.program_id(0)
    gate_at = pl.ds(pl.multiple_of(step * tile, tile), tile)
    up_at = pl.ds(pl.multiple_of(grads.shape[1] // 2 + step * tile, tile), tile)
    _, side, _, core = place_here()

    def lay_down(source):
        natural, blocks = block_columns(plan, source.shape[1])
        eighth = source.shape[0] // 8
        for slot, owner in enumerate(eighth_owners()):

            def some(start, count, slot=slot, owner=owner):
                here = pl.ds(pl.multiple_of(owner * eighth + start, 32), count)
                there = pl.ds(slot * eighth + start, count)
                for a, b in zip(natural, blocks):
                    out_grad[there, b] = source[here, a]

            for_rows(eighth, some)

    @pl.when((step == 0) & (side == core))
    def _():
        lay_down(own_grad)

    @pl.when((step == 0) & (side != core))
    def _():
        lay_down(got_grad)

    def one(block_at, carry):
        here = pl.ds(pl.multiple_of(block_at * block, block), block)
        gate = dot(rows[here, :], gate_up[...])
        up = dot(rows[here, :], up_part[...])
        grad = dot(out_grad[here, :], down[...])
        sigmoid = jax.nn.sigmoid(gate)
        silu = gate * sigmoid
        active[here, :] = (silu * up).astype(low)
        grads[here, gate_at] = (grad * up * sigmoid * (1.0 + gate * (1.0 - sigmoid))).astype(low)
        grads[here, up_at] = (grad * silu).astype(low)
        return carry

    lax.fori_loop(0, rows.shape[0] // block, one, 0)


def feed_forward(plan, rows, own_grad, got_grad, gate_up, down, tile):
    total, width = rows.shape
    units = down.shape[1]
    low = jnp.bfloat16
    tiles = units // tile
    whole = pl.BlockSpec(memory_space=pltpu.VMEM)
    return pl.pallas_call(
        functools.partial(feed_kernel, plan),
        grid=(tiles,),
        out_shape=[
            jax.ShapeDtypeStruct((total, units), low),
            jax.ShapeDtypeStruct((total, 2 * units), low),
            jax.ShapeDtypeStruct((total, width), low),
        ],
        in_specs=[
            whole,
            whole,
            whole,
            pl.BlockSpec((width, tile), lambda step: (0, step)),
            pl.BlockSpec((width, tile), lambda step: (0, step + tiles)),
            pl.BlockSpec((width, tile), lambda step: (0, step)),
        ],
        out_specs=[
            pl.BlockSpec((total, tile), lambda step: (0, step)),
            whole,
            whole,
        ],
        compiler_params=pltpu.CompilerParams(vmem_limit_bytes=56 * 2**20),
        cost_estimate=pl.CostEstimate(
            flops=6 * total * width * units, bytes_accessed=4 * 10**7, transcendentals=total * units
        ),
        name="feed_forward",
    )(rows, own_grad, got_grad, gate_up, gate_up, down)


class Plan:
    def __init__(self, mesh):
        self.total = mesh.shape["dp"]
        self.zones = self.total // 2
        self.tensor = mesh.shape["tensor"]
        self.flips = [k ^ (k >> 1) for k in range(self.zones)]

    def place(self):
        self.index = lax.axis_index("dp")
        self.zone = self.index // 2
        self.side = self.index % 2
        self.row = lax.axis_index("tensor") // 2
        self.core = lax.axis_index("tensor") % 2
        self.home = self.side == self.core

    def move(self, value, target):
        pairs = []
        for d in range(self.total):
            for t in range(self.tensor):
                to = target(d // 2, d % 2, t // 2, t % 2)
                if to is not None:
                    zone, side, row, core = to
                    pairs.append((d * self.tensor + t, (zone * 2 + side) * self.tensor + row * 2 + core))
        return lax.ppermute(value, ("dp", "tensor"), pairs)

    def turn(self, value):
        got = self.move(value, lambda z, y, x, c: (z, c, x, y) if y != c else None)
        return jnp.where(self.home, value, got)

    def zone_flip(self, value, bit):
        return self.move(value, lambda z, y, x, c: (z ^ bit, y, x, c))

    def core_swap(self, value):
        return self.move(value, lambda z, y, x, c: (z, y, x, 1 - c))

    def side_swap(self, value):
        return self.move(value, lambda z, y, x, c: (z, 1 - y, x, c))

    def row_swap(self, value):
        return self.move(value, lambda z, y, x, c: (z, y, 1 - x, c))

    def to_local(self, value, axis):
        width = value.shape[axis] // self.total
        parts = []
        for core in (self.core, 1 - self.core):
            for slot in range(self.zones):
                owner = (self.zone ^ self.flips[slot]) * 2 + core
                parts.append(lax.dynamic_slice_in_dim(value, owner * width, width, axis))
        return jnp.concatenate(parts, axis)

    def to_natural(self, value, axis, core=None):
        core = self.core if core is None else core
        width = value.shape[axis] // self.total
        parts = []
        for block in range(self.total):
            slot = flip = (block // 2) ^ self.zone
            for bits in range(1, self.zones.bit_length()):
                slot = slot ^ (flip >> bits)
            slot = slot + jnp.where(block % 2 == core, 0, self.zones)
            parts.append(lax.dynamic_slice_in_dim(value, slot * width, width, axis))
        return jnp.concatenate(parts, axis)

    def row_owners(self):
        own, off = (self.row, self.side), (1 - self.row, 1 - self.side)
        first = lambda x, y: x * 2 + y
        second = lambda x, y: 4 + y * 2 + x
        return [
            first(own[0], own[1]),
            first(own[0], off[1]),
            second(own[0], own[1]),
            second(off[0], own[1]),
            first(off[0], own[1]),
            first(off[0], off[1]),
            second(own[0], off[1]),
            second(off[0], off[1]),
        ]

    def rows_local(self, value, slots=range(8)):
        size = value.shape[0] // 8
        owners = self.row_owners()
        return jnp.concatenate(
            [lax.dynamic_slice_in_dim(value, owners[slot] * size, size, 0) for slot in slots], 0
        )

    def rows_natural(self, value, order=range(8)):
        size = value.shape[0] // 8
        place = [list(order).index(slot) for slot in range(8)]
        parts = []
        for piece in range(8):
            x, y = (piece // 2, piece % 2) if piece < 4 else (piece % 2, (piece - 4) // 2)
            slots = (0, 1, 4, 5) if piece < 4 else (2, 6, 3, 7)
            same_x, same_y = x == self.row, y == self.side
            slot = jnp.where(
                same_x,
                jnp.where(same_y, place[slots[0]], place[slots[1]]),
                jnp.where(same_y, place[slots[2]], place[slots[3]]),
            )
            parts.append(lax.dynamic_slice_in_dim(value, slot * size, size, 0))
        return jnp.concatenate(parts, 0)

    def from_zones(self, shard):
        return [self.zone_flip(shard, flip) for flip in self.flips[1:]]

    def to_zones(self, parts, slots):
        return [self.zone_flip(parts[slot], self.flips[slot]) for slot in slots]

    def middle_swap(self, pair):
        return self.move(pair, lambda z, y, x, c: (z ^ 3, y, x, c) if z in (1, 2) else None)

    def inward(self, part):
        return self.move(part, lambda z, y, x, c: (z ^ 1, y, x, c) if z in (0, 3) else None)

    def pass_outward(self, pair):
        return self.move(pair, lambda z, y, x, c: (z ^ 1, y, x, c) if z in (1, 2) else None)

    def far_pair(self, middle, passed):
        inner = (self.zone == 1) | (self.zone == 2)
        return jnp.where(inner, middle, passed[::-1])

    def first_swap(self, send):
        half = send.shape[0] // 2
        return self.row_swap(send[:half]), self.side_swap(send[half:])

    def second_swap(self, keep, got):
        quarter = keep.shape[0] // 4
        row_part = keep[: 2 * quarter] + got[0].astype(jnp.float32)
        side_part = keep[2 * quarter :] + got[1].astype(jnp.float32)
        own = jnp.concatenate([row_part[:quarter], side_part[:quarter]], 0)
        return own, (
            self.side_swap(row_part[quarter:].astype(jnp.bfloat16)),
            self.row_swap(side_part[quarter:].astype(jnp.bfloat16)),
        )

    def spread_first(self, own):
        half = own.shape[0] // 2
        return (self.side_swap(own[:half]), self.row_swap(own[half:]))

    def spread_second(self, own, got):
        half = own.shape[0] // 2
        row_part = jnp.concatenate([own[:half], got[0]], 0)
        side_part = jnp.concatenate([own[half:], got[1]], 0)
        return row_part, side_part, self.row_swap(row_part), self.side_swap(side_part)

    def send_home(self, own):
        to_home = lambda z, y, x, c: (z, c, x, c) if y != c else None
        return jnp.concatenate([own, self.move(own, to_home)], 0)

    def row_home(self, part):
        return self.move(part, lambda z, y, x, c: (z, y, 1 - x, c) if y == c else None)

    def share_home(self, part, other):
        full = jnp.concatenate([part, other], 0)
        full = self.to_natural(self.rows_natural(full, (0, 2, 1, 6, 4, 3, 5, 7)), 1)
        got = self.move(full, lambda z, y, x, c: (z, y, x, 1 - c) if y == c else None)
        return full, got

    def turned(self, own, got):
        return jnp.where(self.home, own, got)

    def sum_everywhere(self, value):
        value = value + self.row_swap(value)
        value = value + self.side_swap(value)
        value = value + self.core_swap(value)
        bit = 1
        while bit < self.zones:
            value = value + self.zone_flip(value, bit)
            bit *= 2
        return value


def shards(
    plan,
    tokens,
    positions,
    out_grad,
    qkv_weight,
    qkv_first,
    qkv_second,
    out_weight,
    out_first,
    out_second,
    gate_up,
    gate_up_first,
    gate_up_second,
    down_weight,
    down_first,
    down_second,
    gains,
    gains_first,
    gains_second,
):
    plan.place()
    low = jnp.bfloat16
    tok_rows, model_width = tokens.shape
    groups = qkv_weight.shape[1]
    head_size = qkv_weight.shape[3]
    shard_rows = qkv_weight.shape[0]
    seq_count = tok_rows // SEQ
    mixed_cols = groups * 4 * head_size
    near_cols = model_width // 2
    kept = tok_rows // 2
    gain_count = gains.shape[0]

    tree = plan.zones == 4
    slots = range(1, plan.zones)

    def column_parts(value):
        return value.reshape((plan.zones, -1) + value.shape[1:])

    units = gate_up.shape[2]
    plan.ordered = (model_width // plan.total) % 128 == 0
    gain_rows = 16
    gain_block = jnp.pad(gains.astype(low), (0, gain_rows * 128 - gain_count)).reshape(gain_rows, 128)
    tile = min(units, 256)
    angle_at = positions.astype(jnp.float32).reshape(-1, 128)
    both_qkv, both_gains, turned_gate, turned_out, turned_down, tokens, angle_at, partner_gate = opening(
        plan,
        qkv_weight.reshape(shard_rows, mixed_cols),
        gain_block,
        gate_up,
        out_weight,
        down_weight,
        tokens,
        angle_at,
        3,
    )
    positions = angle_at.reshape(-1)
    turned_out, turned_gate, turned_down, tokens, positions, both_qkv, both_gains, out_grad = fence(
        turned_out, turned_gate, turned_down, tokens, positions, both_qkv, both_gains, out_grad
    )

    got_grad = plan.move(out_grad, lambda z, y, x, c: (z, c, x, y) if y != c else None)
    zone_out = plan.from_zones(turned_out)
    if tree:
        partner_down = plan.zone_flip(turned_down, 1)
    else:
        partner_down = plan.from_zones(turned_down)
        partner_gate = plan.from_zones(turned_gate)
    if not plan.ordered:
        tokens = plan.to_local(tokens, 1)
    cosine, sine_table = rotary(positions, head_size)
    signed_sine = jnp.concatenate(
        [-sine_table[:, : head_size // 2], sine_table[:, head_size // 2 :]], 1
    )
    full_qkv = both_qkv.reshape(model_width, mixed_cols)
    gain_slots = both_gains.reshape(plan.total, -1)[:, :gain_count]
    gain_all = plan.to_natural(gain_slots.reshape(-1), 0).astype(jnp.float32)
    gain_in = plan.to_local(gain_all[:model_width], 0)[None]
    gain_post = plan.to_local(gain_all[model_width : 2 * model_width], 0)[None]
    gain_q = gain_all[2 * model_width : 2 * model_width + head_size][None]
    gain_k = gain_all[2 * model_width + head_size :][None]
    normed, raw, query, key_rot, values_low, attended = attention(
        tokens, full_qkv, gain_in, gain_q, gain_k, cosine, signed_sine
    )
    attended, zone_out, turned_out, turned_down, turned_gate, partner_gate, partner_down = fence(
        attended, zone_out, turned_out, turned_down, turned_gate, partner_gate, partner_down
    )

    near_out = jnp.concatenate([turned_out] + zone_out, 0)
    far_out = plan.core_swap(near_out)
    own_tokens = plan.rows_local(tokens, (0, 2))
    near_out, far_out, own_tokens = fence(near_out, far_out, own_tokens)

    full_out = jnp.concatenate([near_out, far_out], 0)
    branch_terms = contract_cols(attended, full_out).astype(low)
    pairs = [(turned_gate, partner_gate), (turned_down, partner_down)]
    jobs = [PairTree(pairs, (2, 2))] if tree else []
    normed_rows, hidden, *gathered = sum_rows(
        plan,
        spread_kernel,
        hidden_rows,
        branch_terms,
        [own_tokens, gain_post],
        [jax.ShapeDtypeStruct((tok_rows // 4, model_width), jnp.float32)],
        0,
        jobs,
    )
    if not tree:
        near = [jnp.concatenate([own] + rest, 0) for own, rest in pairs]
        gathered = [jnp.concatenate([part, plan.core_swap(part)], 0) for part in near]
    full_gate = gathered[0].reshape(model_width, 2 * units)
    full_down = gathered[1].reshape(model_width, units)
    normed_rows, hidden, full_gate, full_down, got_grad = fence(
        normed_rows, hidden, full_gate, full_down, got_grad
    )

    def zone_parts(near, got):
        both = (near + got.astype(jnp.float32)).astype(low)
        return both.reshape((plan.zones, -1) + both.shape[1:])

    def zone_total(parts, *arrived):
        total = parts[0].astype(jnp.float32)
        for part in sum([list(group) for group in arrived], []):
            total = total + part.astype(jnp.float32)
        return total.astype(low)

    active, grad_both, out_grad = feed_forward(
        plan, normed_rows, out_grad, got_grad, full_gate, full_down, tile
    )
    if not plan.ordered:
        out_grad = plan.to_local(out_grad, 1)
    gate_far = contract_rows(normed_rows[:, near_cols:], grad_both).astype(low)
    gate_far, active, grad_both, out_grad, normed_rows = fence(
        gate_far, active, grad_both, out_grad, normed_rows
    )

    gate_got = plan.core_swap(gate_far)
    down_far = contract_rows(out_grad[:, near_cols:], active).astype(low)
    gate_got, down_far, active, grad_both, normed_rows = fence(
        gate_got, down_far, active, grad_both, normed_rows
    )

    down_got = plan.core_swap(down_far)
    gate_parts = zone_parts(contract_rows(normed_rows[:, :near_cols], grad_both), gate_got)
    gate_parts, down_got, grad_both, active, out_grad = fence(
        gate_parts, down_got, grad_both, active, out_grad
    )

    half_rows = shard_rows // 2
    if tree:
        gate_ready = [plan.inward(gate_parts[3, :half_rows])]
    else:
        gate_ready = [gate_parts[0]]
    post_terms = contract_cols(grad_both, full_gate).astype(low)
    post_terms, gate_parts, gate_ready, down_got, active, out_grad = fence(
        post_terms, gate_parts, gate_ready, down_got, active, out_grad
    )
    if tree:
        gate_ready += [plan.inward(gate_parts[3, half_rows:])]
    down_parts = zone_parts(contract_rows(out_grad[:, :near_cols], active), down_got)
    post_terms, gate_parts, gate_ready, down_parts = fence(
        post_terms, gate_parts, gate_ready, down_parts
    )
    gate_ready = jnp.concatenate(gate_ready, 0)

    if tree:
        down_sums = [plan.inward(down_parts[3]), plan.inward(down_parts[2])]
    else:
        down_sums = plan.to_zones(down_parts, slots)
    eighth = tok_rows // 8
    own_grad = jnp.concatenate([out_grad[:eighth], out_grad[2 * eighth : 3 * eighth]], 0)
    branch_rows, grad_hidden, post_gain_grad, mlp_terms, gate_sums = sum_rows(
        plan,
        spread_kernel,
        grad_hidden_rows,
        post_terms,
        [hidden, own_grad, gain_post],
        [
            jax.ShapeDtypeStruct((tok_rows // 4, model_width), jnp.float32),
            jax.ShapeDtypeStruct((1, model_width), jnp.float32),
        ],
        1,
        [
            SideDot(active, full_down),
            PairScatter(gate_parts, gate_ready, 2) if tree else ZoneBlocks(plan, gate_parts, slots),
        ],
    )
    branch_rows, grad_hidden, post_gain_grad, gate_sums, mlp_terms, down_parts, down_sums = fence(
        branch_rows, grad_hidden, post_gain_grad, gate_sums, mlp_terms, down_parts, down_sums
    )

    mlp_got = plan.first_swap(mlp_terms[kept:])
    if tree:
        gate_last = [plan.zone_flip(gate_sums[1], 1)]
        gate_own = gate_sums
        down_pair = down_parts[2:].astype(jnp.float32) + jnp.stack(down_sums).astype(jnp.float32)
        down_sums = plan.middle_swap(down_pair.astype(low))
    else:
        gate_last, gate_own = gate_sums, gate_parts
    grad_att = jnp.dot(branch_rows, full_out, preferred_element_type=jnp.float32).astype(low)
    grad_mixed, mixed_rows, query_gain_grad, key_gain_grad = attention_back(
        query, key_rot, values_low, raw, grad_att, gain_q, gain_k, cosine, signed_sine
    )
    gain_terms = jnp.concatenate(
        [plan.to_natural(post_gain_grad, 1), query_gain_grad, key_gain_grad], 1
    )
    if tree:
        down_own = (down_parts[:2].astype(jnp.float32) + down_sums.astype(jnp.float32)).astype(low)
    grad_mixed, mixed_rows, gain_terms, normed, gate_last, branch_rows, mlp_got, down_sums = fence(
        grad_mixed, mixed_rows, gain_terms, normed, gate_last, branch_rows, mlp_got, down_sums
    )

    mlp_own, mlp_last = plan.second_swap(mlp_terms[:kept].astype(jnp.float32), mlp_got)
    if tree:
        total_down = zone_total(down_own, [plan.zone_flip(down_own[1], 1)])
    else:
        total_down = zone_total(down_parts, down_sums)
    total_gate = zone_total(gate_own, gate_last)
    summed_gate = plan.turn(jnp.stack([total_gate[:, :units], total_gate[:, units:]]))
    out_far = contract_rows(branch_rows[:, near_cols:], attended).astype(low)
    out_got = plan.core_swap(out_far)
    normed_terms = contract_cols(mixed_rows, full_qkv).astype(low)
    out_parts = zone_parts(contract_rows(branch_rows[:, :near_cols], attended), out_got)
    block_own = (hidden + mlp_own + jnp.concatenate(mlp_last, 0).astype(jnp.float32)).astype(low)
    out_parts, normed_terms, summed_gate, total_down, block_own, normed, grad_mixed = fence(
        out_parts, normed_terms, summed_gate, total_down, block_own, normed, grad_mixed
    )

    gain_sum = GainSum(plan, gain_terms.shape[1], model_width) if plan.ordered else None
    mine, input_gain_grad, *rest = sum_rows(
        plan,
        home_kernel,
        grad_input_rows,
        normed_terms,
        [own_tokens, grad_hidden, gain_in, block_own] + ([gain_terms] if plan.ordered else []),
        [jax.ShapeDtypeStruct((1, model_width), jnp.float32)],
        2,
        [BlockGrad(plan, normed, grad_mixed), ZoneBlocks(plan, out_parts, slots)],
        gain_sum,
    )
    if plan.ordered:
        summed_gains, total_qkv, out_sent = rest
    else:
        total_qkv, out_sent = rest
        summed_gains = plan.sum_everywhere(
            jnp.concatenate([plan.to_natural(input_gain_grad, 1), gain_terms], 1)
        )
    mine, summed_gains, total_qkv, out_sent, total_down = fence(
        mine, summed_gains, total_qkv, out_sent, total_down
    )

    summed_down = plan.turn(total_down)
    other = plan.core_swap(mine)
    input_full, block_out = jnp.where(plan.home, mine, other), jnp.where(plan.home, other, mine)
    if not plan.ordered:
        input_full = plan.to_natural(input_full, 1, plan.side)
        block_out = plan.to_natural(block_out, 1, plan.side)
    summed_both = plan.turn(
        jnp.concatenate([total_qkv, zone_total(out_parts, out_sent)], 1)
    ).astype(jnp.float32)
    summed_qkv = summed_both[:, :mixed_cols].reshape(qkv_weight.shape)
    summed_out = summed_both[:, mixed_cols:]
    summed_gate = summed_gate.astype(jnp.float32)
    summed_down = summed_down.astype(jnp.float32)
    summed_gains = lax.dynamic_slice_in_dim(summed_gains[0], plan.index * gain_count, gain_count, 0)
    input_rows = input_full.astype(jnp.float32)

    qkv_moment, qkv_square, qkv_updated = adamw(
        qkv_weight, summed_qkv, qkv_first, qkv_second, RATE_QKV, DECAY_RATE
    )
    out_moment, out_square, out_updated = adamw(
        out_weight, summed_out, out_first, out_second, RATE_OUT, DECAY_RATE
    )
    gate_moment, gate_square, gate_updated = adamw(
        gate_up, summed_gate, gate_up_first, gate_up_second, RATE_GATE, DECAY_RATE
    )
    down_moment, down_square, down_updated = adamw(
        down_weight, summed_down, down_first, down_second, RATE_DOWN, DECAY_RATE
    )
    gain_moment, gain_square, gain_updated = adamw(
        gains, summed_gains, gains_first, gains_second, RATE_GAIN, 0.0
    )
    return (
        block_out,
        input_rows,
        qkv_moment,
        qkv_square,
        qkv_updated,
        out_moment,
        out_square,
        out_updated,
        gate_moment,
        gate_square,
        gate_updated,
        down_moment,
        down_square,
        down_updated,
        gain_moment,
        gain_square,
        gain_updated,
    )


def solution(mesh):
    plan = Plan(mesh)
    placed = (
        P("dp", None),
        P("dp"),
        P("dp", None),
        P("dp", "tensor", None, None),
        P("dp", "tensor", None, None),
        P("dp", "tensor", None, None),
        P("dp", "tensor"),
        P("dp", "tensor"),
        P("dp", "tensor"),
        P(None, "dp", "tensor"),
        P(None, "dp", "tensor"),
        P(None, "dp", "tensor"),
        P("dp", "tensor"),
        P("dp", "tensor"),
        P("dp", "tensor"),
        P("dp"),
        P("dp"),
        P("dp"),
    )
    return jax.shard_map(
        functools.partial(shards, plan),
        mesh=mesh,
        in_specs=placed,
        out_specs=(
            P("dp", None),
            P("dp", None),
            P("dp", "tensor", None, None),
            P("dp", "tensor", None, None),
            P("dp", "tensor", None, None),
            P("dp", "tensor"),
            P("dp", "tensor"),
            P("dp", "tensor"),
            P(None, "dp", "tensor"),
            P(None, "dp", "tensor"),
            P(None, "dp", "tensor"),
            P("dp", "tensor"),
            P("dp", "tensor"),
            P("dp", "tensor"),
            P("dp"),
            P("dp"),
            P("dp"),
        ),
        check_vma=False,
    )
```

```python
import functools
import math

import jax
import jax.numpy as jnp
from jax import lax
from jax.experimental import pallas as pl
from jax.experimental.pallas import tpu as pltpu
from jax.sharding import PartitionSpec as P

SEQ = 1024
STEP = 10


EPS_NORM = 1e-06
THETA = 1000000.0
BETA_ONE = 0.9
BETA_TWO = 0.95
ADAM_EPS = 1e-08
DECAY_RATE = 0.1
RATE_QKV = 0.05
RATE_OUT = 0.3
RATE_GATE = 0.05
RATE_DOWN = 0.03
RATE_GAIN = 1.0


def rotary(positions, head_size):
    freq_index = jnp.arange(head_size // 2, dtype=jnp.float32)
    inverse = jnp.exp(freq_index * (-2.0 * math.log(THETA) / head_size))
    angles = positions.astype(jnp.float32)[:, None] * inverse[None, :]
    cosine = jnp.cos(angles)
    sine_table = jnp.sin(angles)
    return (jnp.concatenate([cosine, cosine], -1), jnp.concatenate([sine_table, sine_table], -1))


def rotate(values, cosine, sine_table):
    half_size = values.shape[-1] // 2
    turned = jnp.concatenate([-values[..., half_size:], values[..., :half_size]], -1)
    return values * cosine[:, None, :] + turned * sine_table[:, None, :]


def unrotate(gradient, cosine, sine_table):
    half_size = gradient.shape[-1] // 2
    turned = gradient * sine_table[:, None, :]
    rotated_back = jnp.concatenate([turned[..., half_size:], -turned[..., :half_size]], -1)
    return gradient * cosine[:, None, :] + rotated_back


def norm_back(grad_unit, unit_vals, factor):
    return factor * (grad_unit - unit_vals * jnp.mean(grad_unit * unit_vals, -1, keepdims=True))


def contract_rows(left, right):
    return lax.dot_general(
        left, right, (((0,), (0,)), ((), ())), preferred_element_type=jnp.float32
    )


def contract_cols(left, right):
    return lax.dot_general(
        left, right, (((1,), (1,)), ((), ())), preferred_element_type=jnp.float32
    )


def block_scores(query_part, key_part, first_row, block_rows, last_row):
    scores = jnp.einsum(
        "nqkgd,nskd->nkgqs", query_part, key_part, preferred_element_type=jnp.float32
    )
    causal = (first_row + jnp.arange(block_rows))[:, None] >= jnp.arange(last_row)[None, :]
    return jnp.where(causal, scores, -1000000000.0)


def attention_forward(query, key_rot, values_low, seq_len):
    block_rows = min(512, seq_len)
    outputs = []
    log_sums = []
    for first_row in range(0, seq_len, block_rows):
        last_row = first_row + block_rows
        query_part = query[:, first_row:last_row]
        scores = block_scores(query_part, key_rot[:, :last_row], first_row, block_rows, last_row)
        row_max = jnp.max(scores, -1, keepdims=True)
        exponent = jnp.exp(scores - row_max)
        row_total = jnp.sum(exponent, -1, keepdims=True)
        probs_low = (exponent / row_total).astype(jnp.bfloat16)
        outputs.append(
            jnp.einsum(
                "nkgqs,nskd->nqkgd",
                probs_low,
                values_low[:, :last_row],
                preferred_element_type=jnp.float32,
            )
        )
        log_sums.append(row_max + jnp.log(row_total))
    return (jnp.concatenate(outputs, 1), log_sums)


def attention_backward(query, key_rot, values_low, grad_att, log_sums, seq_len):
    block_rows = min(512, seq_len)
    query_grads = []
    key_grad = jnp.zeros(key_rot.shape, jnp.float32)
    value_grad = jnp.zeros(values_low.shape, jnp.float32)
    for block_index, first_row in enumerate(range(0, seq_len, block_rows)):
        last_row = first_row + block_rows
        query_part = query[:, first_row:last_row]
        grad_part = grad_att[:, first_row:last_row]
        key_part = key_rot[:, :last_row]
        value_part = values_low[:, :last_row]
        scores = block_scores(query_part, key_part, first_row, block_rows, last_row)
        probs = jnp.exp(scores - log_sums[block_index])
        probs_low = probs.astype(jnp.bfloat16)
        grad_probs = jnp.einsum(
            "nqkgd,nskd->nkgqs", grad_part, value_part, preferred_element_type=jnp.float32
        )
        grad_scores = (
            probs * (grad_probs - jnp.sum(probs * grad_probs, -1, keepdims=True))
        ).astype(jnp.bfloat16)
        query_grads.append(
            jnp.einsum(
                "nkgqs,nskd->nqkgd", grad_scores, key_part, preferred_element_type=jnp.float32
            )
        )
        padding = ((0, 0), (0, seq_len - last_row), (0, 0), (0, 0))
        key_grad = key_grad + jnp.pad(
            jnp.einsum(
                "nkgqs,nqkgd->nskd", grad_scores, query_part, preferred_element_type=jnp.float32
            ),
            padding,
        )
        value_grad = value_grad + jnp.pad(
            jnp.einsum(
                "nkgqs,nqkgd->nskd", probs_low, grad_part, preferred_element_type=jnp.float32
            ),
            padding,
        )
    return (jnp.concatenate(query_grads, 1), key_grad, value_grad)


def adamw(weight, gradient, moment, second, step_rate, decay_rate):
    moment = BETA_ONE * moment + (1.0 - BETA_ONE) * gradient
    second = BETA_TWO * second + (1.0 - BETA_TWO) * gradient * gradient
    first_hat = moment / (1.0 - BETA_ONE**STEP)
    second_hat = second / (1.0 - BETA_TWO**STEP)
    weight = weight - step_rate * (
        first_hat / (jnp.sqrt(second_hat) + ADAM_EPS) + decay_rate * weight
    )
    return (moment, second, weight)


def fence(*values):
    return lax.optimization_barrier(values)


MESH = pl.DeviceIdType.MESH
HEAD = 128
AHEAD = 2


def place_here():
    index, place = lax.axis_index("dp"), lax.axis_index("tensor")
    return lax.div(index, 2), lax.rem(index, 2), lax.div(place, 2), lax.rem(place, 2)


def device(zone, side, row, core):
    return (zone * 2 + side, row * 2 + core)


def flipped(zone, flip):
    bit = 1
    while bit <= flip:
        if flip & bit:
            zone = zone + bit - 2 * bit * lax.rem(lax.div(zone, bit), 2)
        bit *= 2
    return zone


def greet(devices, amount=None):
    barrier = pltpu.get_barrier_semaphore()
    for peer in devices:
        pl.semaphore_signal(barrier, inc=1, device_id=peer, device_id_type=MESH)
    pl.semaphore_wait(barrier, len(devices) if amount is None else amount)


def for_rows(count, body):
    step = 32

    def one(block, carry):
        body(pl.multiple_of(block * step, step), step)
        return carry

    lax.fori_loop(0, count // step, one, 0)


class Copies:
    def __init__(self, send_sems, recv_sems):
        self.send_sems, self.recv_sems = send_sems, recv_sems
        self.number = 0

    def make(self, source, target, peer):
        number, self.number = self.number, self.number + 1
        return pltpu.make_async_remote_copy(
            src_ref=source,
            dst_ref=target,
            send_sem=self.send_sems.at[number],
            recv_sem=self.recv_sems.at[number],
            device_id=peer,
            device_id_type=MESH,
        )

    def start(self, source, target, peer):
        copy = self.make(source, target, peer)
        copy.start()
        return copy


class GainSum:
    def __init__(self, plan, rest, width):
        self.plan, self.width = plan, width
        self.total = width + rest
        self.scratch = [
            pltpu.VMEM((8, 1, self.total), jnp.float32),
            pltpu.VMEM((plan.zones, 1, self.total), jnp.float32),
        ]
        self.output = jax.ShapeDtypeStruct((1, self.total), jnp.float32)
        self.count = 7 + plan.zones - 1

    def plane_peers(self, zone, side, row, core):
        steps = [(s, r, c) for s in range(2) for r in range(2) for c in range(2)][1:]
        turn = lambda value, step: 1 - value if step else value
        return [device(zone, turn(side, s), turn(row, r), turn(core, c)) for s, r, c in steps]

    def zone_peers(self, zone, side, row, core):
        return {flip: device(flipped(zone, flip), side, row, core) for flip in self.plan.flips[1:]}

    def start(self, copies, rest, blocks, plane_sums, zone_sums):
        zone, side, row, core = place_here()
        plan = self.plan
        size = self.width // plan.total
        self.copies, self.plane_sums, self.zone_sums, self.zone = copies, plane_sums, zone_sums, zone
        here = side * 4 + row * 2 + core
        plane_sums[here, :, pl.ds(self.width, self.total - self.width)] = rest[...]
        for slot in range(plan.total):
            owner = flipped(zone, plan.flips[slot % plan.zones]) * 2
            owner = owner + (core if slot < plan.zones else 1 - core)
            spot = pl.ds(pl.multiple_of(owner * size, size), size)
            plane_sums[here, :, spot] = blocks[:, pl.ds(slot * size, size)]
        self.plane = [
            copies.start(plane_sums.at[here], plane_sums.at[here], peer)
            for peer in self.plane_peers(zone, side, row, core)
        ]

    def middle(self):
        for copy in self.plane:
            copy.wait_recv()
        total = self.plane_sums[0]
        for place in range(1, 8):
            total = total + self.plane_sums[place]
        self.zone_sums[self.zone] = total
        zone, side, row, core = place_here()
        self.across = [
            self.copies.start(self.zone_sums.at[self.zone], self.zone_sums.at[self.zone], peer)
            for peer in self.zone_peers(zone, side, row, core).values()
        ]

    def finish(self, out):
        for copy in self.across:
            copy.wait_recv()
        total = self.zone_sums[0]
        for place in range(1, self.plan.zones):
            total = total + self.zone_sums[place]
        out[...] = total
        for copy in self.plane + self.across:
            copy.wait_send()


class ZoneBlocks:
    scratch = []

    def __init__(self, plan, source, slots, begin=0):
        self.flips, self.slots, self.sources, self.begin = plan.flips, list(slots), [source], begin
        self.outputs = [
            jax.ShapeDtypeStruct((len(self.slots),) + source.shape[1:], source.dtype)
        ]
        self.count, self.count_local = len(self.slots), 0
        self.in_hbm = False

    def peers(self, zone, side, row, core):
        return {
            self.flips[slot]: device(flipped(zone, self.flips[slot]), side, row, core)
            for slot in self.slots
        }

    def start(self, copies, local_sems, sources, targets, stages):
        zone, side, row, core = place_here()
        self.started = [
            copies.make(
                sources[0].at[slot],
                targets[0].at[number],
                device(flipped(zone, self.flips[slot]), side, row, core),
            )
            for number, slot in enumerate(self.slots)
        ]
        self.waiting = True
        if self.begin == 0:
            self.pump([0])

    def pump(self, steps):
        if self.waiting and self.begin in steps:
            self.waiting = False
            for copy in self.started:
                copy.start()

    def finish(self):
        for copy in self.started:
            copy.wait_send()
        for copy in self.started:
            copy.wait_recv()


def inner_zone(zone):
    return lax.rem(lax.div(zone + 1, 2), 2)


class SideDot:
    count, count_local, scratch, in_hbm = 0, 0, [], False

    def __init__(self, left, right):
        self.sources = [left, right]
        self.outputs = [jax.ShapeDtypeStruct((left.shape[0], right.shape[0]), jnp.bfloat16)]

    def peers(self, zone, side, row, core):
        return {}

    def some(self, first, last):
        left, right = self.refs
        size = 256

        def one(step, carry):
            here = pl.ds(pl.multiple_of(step * size, size), size)
            self.out[:, here] = dot(left[...], right[here, :], 1, 1).astype(jnp.bfloat16)
            return carry

        lax.fori_loop(first, last, one, 0)

    def start(self, copies, local_sems, sources, targets, stages):
        self.refs, self.out = sources, targets[0]
        self.steps = self.out.shape[1] // 256
        self.some(0, self.steps // 2)

    def pump(self, steps):
        if 0 in steps:
            self.some(self.steps // 2, self.steps)

    def finish(self):
        pass


class PairScatter:
    def __init__(self, parts, ready, pieces):
        self.sources, self.pieces = [parts, ready], pieces
        _, rows, columns = parts.shape
        self.size = rows // pieces
        self.outputs = [jax.ShapeDtypeStruct((2, rows, columns), parts.dtype)]
        self.scratch = [pltpu.VMEM((2, rows, columns), parts.dtype)] * 2
        self.count, self.count_local = 4 * pieces - 1, 0
        self.in_hbm = False

    def peers(self, zone, side, row, core):
        return {
            1: device(flipped(zone, 1), side, row, core),
            3: device(flipped(zone, 3), side, row, core),
        }

    def start(self, copies, local_sems, sources, targets, stages):
        zone, side, row, core = place_here()
        self.parts, self.ready = sources
        self.out = targets[0]
        self.inward, self.crossed = stages
        inner_peer = device(flipped(zone, 3), side, row, core)
        outer_peer = device(flipped(zone, 1), side, row, core)
        self.inner = inner_zone(zone) == 1
        self.outer = inner_zone(zone) == 0
        pieces = [pl.ds(piece * self.size, self.size) for piece in range(self.pieces)]
        self.steps = [(slot, rows) for slot in (0, 1) for rows in pieces]
        self.to_inner = [
            copies.make(self.parts.at[3 - slot, rows], self.inward.at[slot, rows], outer_peer)
            for slot, rows in self.steps[1:]
        ]
        self.across = [
            copies.make(self.inward.at[slot, rows], self.crossed.at[slot, rows], inner_peer)
            for slot, rows in self.steps
        ]

        @pl.when(self.outer)
        def _():
            for copy in self.to_inner[:AHEAD]:
                copy.start()

        @pl.when(self.inner)
        def _():
            slot, rows = self.steps[0]
            self.add(self.inward, slot, rows, self.parts.at[2], self.ready)
            self.across[0].start()

    def add(self, target, slot, rows, left, right):
        def some(row, count):
            here = pl.ds(rows.start + row, count)
            both = left[here, :].astype(jnp.float32) + right[here, :].astype(jnp.float32)
            target.at[slot][here, :] = both.astype(jnp.bfloat16)

        for_rows(self.size, some)

    def pump(self, steps):
        steps = [step for step in steps if step < len(self.to_inner)]

        @pl.when(self.inner)
        def _():
            for step in steps:
                slot, rows = self.steps[step + 1]
                self.to_inner[step].wait_recv()
                self.add(self.inward, slot, rows, self.parts.at[2 + slot], self.inward.at[slot])
                self.across[step + 1].start()
                self.settle(step)

        @pl.when(self.outer)
        def _():
            for step in steps:
                self.to_inner[step].wait_send()
                for copy in self.to_inner[step + AHEAD : step + AHEAD + 1]:
                    copy.start()

    def settle(self, step):
        slot, rows = self.steps[step]
        self.across[step].wait_recv()
        self.add(self.out, slot, rows, self.parts.at[slot], self.crossed.at[slot])

    def finish(self):
        @pl.when(self.inner)
        def _():
            self.settle(len(self.steps) - 1)
            for copy in self.across:
                copy.wait_send()

        @pl.when(self.outer)
        def _():
            for slot in (0, 1):

                def some(row, count, slot=slot):
                    here = pl.ds(row, count)
                    self.out.at[slot][here, :] = self.parts.at[slot][here, :]

                for_rows(self.parts.shape[1], some)


class BlockGrad:
    in_hbm = False

    def __init__(self, plan, left, right):
        self.zones, self.flips = plan.zones, plan.flips
        self.sources = [left, right]
        shape = (left.shape[1] // plan.total, right.shape[1])
        low = jnp.bfloat16
        self.outputs = [jax.ShapeDtypeStruct(shape, low)]
        self.scratch = [pltpu.VMEM((plan.zones,) + shape, low)] * 4
        self.count, self.count_local = 2 * plan.zones, 0

    def peers(self, zone, side, row, core):
        return {flip: device(flipped(zone, flip), side, row, core) for flip in self.flips[1:]}

    def product(self, block):
        size = self.out.shape[0]
        return dot(self.left[:, pl.ds(block * size, size)], self.right[...], 0, 0)

    def start(self, copies, local_sems, sources, targets, stages):
        zone, side, row, core = place_here()
        self.left, self.right = sources
        self.out = targets[0]
        self.far, self.got, self.parts, self.arrived = stages
        core_peer = device(zone, side, row, 1 - core)
        self.order = list(range(1, self.zones)) + [0]
        self.over = [
            copies.make(self.far.at[slot], self.got.at[slot], core_peer)
            for slot in range(self.zones)
        ]
        self.along = [
            copies.make(
                self.parts.at[slot],
                self.arrived.at[slot],
                device(flipped(zone, self.flips[slot]), side, row, core),
            )
            for slot in range(1, self.zones)
        ]
        for slot in self.order:
            self.far[slot] = self.product(self.zones + slot).astype(jnp.bfloat16)
            self.over[slot].start()

    def pump(self, steps):
        for slot in self.order if 0 in steps else []:
            near = self.product(slot)
            self.over[slot].wait_recv()
            self.parts[slot] = (near + self.got[slot].astype(jnp.float32)).astype(jnp.bfloat16)
            if slot:
                self.along[slot - 1].start()

    def finish(self):
        total = self.parts[0].astype(jnp.float32)
        for slot in range(1, self.zones):
            self.along[slot - 1].wait_recv()
            total = total + self.arrived[slot].astype(jnp.float32)
        self.out[...] = total.astype(jnp.bfloat16)
        for copy in self.over + self.along:
            copy.wait_send()


class TurnLate:
    count, count_local, scratch, in_hbm = 1, 0, [], False

    def __init__(self, values):
        self.sources = [values]
        self.outputs = [jax.ShapeDtypeStruct(values.shape, values.dtype)]

    def peers(self, zone, side, row, core):
        return {}

    def start(self, copies, local_sems, sources, targets, stages):
        zone, side, row, core = place_here()
        self.away = side != core
        self.copy = copies.make(sources[0], targets[0], device(zone, core, row, side))

    def pump(self, steps):
        pass

    def late(self):
        @pl.when(self.away)
        def _():
            self.copy.start()

    def finish(self):
        @pl.when(self.away)
        def _():
            self.copy.wait_recv()
            self.copy.wait_send()


class PairTree:
    def __init__(self, pairs, pieces):
        self.pairs = [len(pair) for pair in pairs]
        self.sources = [shard for pair in pairs for shard in pair]
        self.pieces = pieces
        self.outputs = [
            jax.ShapeDtypeStruct((8,) + own.shape, own.dtype) for own, *_ in pairs
        ]
        self.count = 6 * sum(pieces) + 2 * len(pairs) + self.pairs.count(1)
        self.count_local = 2 * len(pairs) + 2 * sum(pieces)
        self.scratch = [pltpu.VMEM((2,) + own.shape, own.dtype) for own, *_ in pairs]
        self.scratch += [pltpu.VMEM(p[0].shape, p[0].dtype) for p in pairs if len(p) == 1]
        self.in_hbm = True

    def peers(self, zone, side, row, core):
        return {
            1: device(flipped(zone, 1), side, row, core),
            3: device(flipped(zone, 3), side, row, core),
            "core": device(zone, side, row, 1 - core),
        }

    def start(self, copies, local_sems, sources, targets, stages):
        zone, side, row, core = place_here()
        inner_peer = device(flipped(zone, 3), side, row, core)
        outer_peer = device(flipped(zone, 1), side, row, core)
        core_peer = device(zone, side, row, 1 - core)
        self.inner = inner_zone(zone) == 1
        self.outer = inner_zone(zone) == 0
        self.across, self.onward, self.late, self.place = [], [], [], []
        self.shared, self.kept, self.partners, self.later = [], [], [], []
        sem = 0
        sources, late_stages = list(sources), list(stages[len(targets) :])
        for weight, full in enumerate(targets):
            landing = stages[weight]
            pair = [sources.pop(0) for _ in range(self.pairs[weight])]
            if len(pair) == 1:
                pair.append(late_stages.pop(0))
                self.partners.append(copies.start(pair[0], pair[1], outer_peer))
            size = pair[0].shape[0] // self.pieces[weight]
            for piece in range(self.pieces[weight]):
                rows = pl.ds(piece * size, size)
                for slot in (0, 1):
                    here = landing.at[slot, rows]
                    self.across.append(copies.make(pair[slot].at[rows], here, inner_peer))
                    self.onward.append(copies.make(here, landing.at[1 - slot, rows], outer_peer))
                    self.late.append(copies.make(here, full.at[6 + slot, rows], core_peer))
                    self.place.append(
                        pltpu.make_async_copy(here, full.at[2 + slot, rows], local_sems.at[sem])
                    )
                    sem += 1
            for slot in (0, 1):
                self.shared.append(copies.make(pair[slot], full.at[4 + slot], core_peer))
                self.kept.append(
                    pltpu.make_async_copy(pair[slot], full.at[slot], local_sems.at[sem])
                )
                sem += 1
                if slot >= self.pairs[weight]:
                    self.later += [self.shared[-1], self.kept[-1]]
                else:
                    self.shared[-1].start()
                    self.kept[-1].start()

        @pl.when(self.inner)
        def _():
            for copy in self.across[:AHEAD]:
                copy.start()

    def arrive(self, number):
        self.onward[number].wait_recv()
        swapped = number + 1 - 2 * (number % 2)
        self.late[swapped].start()
        self.place[swapped].start()

    def pump(self, steps):
        steps = [step for step in steps if step < len(self.across)]

        @pl.when(self.inner)
        def _():
            for here in steps:
                self.across[here].wait_recv()
                for copy in self.across[here + AHEAD : here + AHEAD + 1]:
                    copy.start()
                self.onward[here].start()
                self.late[here].start()
                self.place[here].start()

        @pl.when(self.outer)
        def _():
            for step in steps:
                if step > 0:
                    self.arrive(step - 1)

        for copy in self.partners if 1 in steps else []:
            copy.wait_recv()
            copy.wait_send()
        for copy in self.later if 1 in steps else []:
            copy.start()

    def finish(self):
        @pl.when(self.inner)
        def _():
            for copy in self.across + self.onward:
                copy.wait_send()

        @pl.when(self.outer)
        def _():
            self.arrive(len(self.onward) - 1)

        for copy in self.kept + self.place:
            copy.wait()
        for copy in self.shared + self.late:
            copy.wait_send()
        for copy in self.shared + self.late:
            copy.wait_recv()


def sum_eighths(
    copies, row_peer, side_peer, send, keep, forward, first, second, store, begin, pump
):
    size = send.shape[0] // 4
    part = lambda ref, slot: ref.at[pl.ds(slot * size, size)]
    arrivals = [
        copies.start(part(send, 1), part(first, 1), row_peer),
        copies.start(part(send, 3), part(first, 3), side_peer),
        copies.start(part(send, 0), part(first, 0), row_peer),
        copies.start(part(send, 2), part(first, 2), side_peer),
    ]
    begin()
    passed = []
    for number, slot, peer in ((0, 1, side_peer), (1, 3, row_peer)):
        arrivals[number].wait_recv()

        def add(row, count, number=number, slot=slot):
            here = pl.ds(slot * size + row, count)
            both = keep[here, :].astype(jnp.float32) + first[here, :].astype(jnp.float32)
            forward[pl.ds(number * size + row, count), :] = both.astype(jnp.bfloat16)

        for_rows(size, add)
        passed.append(copies.start(part(forward, number), part(second, number), peer))
    pump([0])
    for number, slot in ((0, 0), (1, 2)):
        arrivals[2 + number].wait_recv()
        passed[number].wait_recv()

        def total(row, count, number=number, slot=slot):
            here = pl.ds(slot * size + row, count)
            sums = keep[here, :].astype(jnp.float32) + first[here, :].astype(jnp.float32)
            sums = sums + second[pl.ds(number * size + row, count), :].astype(jnp.float32)
            store(number, row, count, sums)

        for_rows(size, total)
        yield number
    for copy in arrivals + passed:
        copy.wait_send()


def halves(terms):
    rows = terms.shape[0] // 2
    return terms.at[pl.ds(0, rows)], terms.at[pl.ds(rows, rows)]


def split_refs(refs, jobs, extra_count, out_count):
    refs = list(refs)
    take = lambda count: [refs.pop(0) for _ in range(count)]
    extras = take(extra_count)
    sources = [take(len(job.sources)) for job in jobs]
    full = take(1)[0]
    outs = take(out_count)
    targets = [take(len(job.outputs)) for job in jobs]
    return extras, sources, full, outs, targets, refs


def spread_kernel(middle, jobs, extra_count, out_count, gain_sum, plan, terms, *refs):
    keep, send = halves(terms)
    extras, sources, full, outs, targets, scratch = split_refs(refs, jobs, extra_count, out_count)
    forward, first, second, send_sems, recv_sems, local_sems, *stages = scratch
    zone, side, row, core = place_here()
    row_peer, side_peer = device(zone, side, 1 - row, core), device(zone, 1 - side, row, core)
    copies = Copies(send_sems, recv_sems)
    size = send.shape[0] // 4
    part = lambda slot: full.at[pl.ds(slot * size, size)]
    for out in outs:
        if out.shape[0] == 1:
            out[...] = jnp.zeros_like(out)
    peers = {}
    for job in jobs:
        peers.update(job.peers(zone, side, row, core))
    greet([row_peer, side_peer] + list(peers.values()))

    def begin():
        spot = 0
        for job, source, target in zip(jobs, sources, targets):
            own_stages = stages[spot : spot + len(job.scratch)]
            job.start(copies, local_sems, source, target, own_stages)
            spot += len(job.scratch)

    def pump(steps):
        for job in jobs:
            job.pump(steps)

    def store(number, row, count, sums):
        own = pl.ds(number * size + row, count)
        full[pl.ds(2 * number * size + row, count), :] = middle(own, sums, extras, outs)

    firsts, seconds = [], []
    for number in sum_eighths(
        copies, row_peer, side_peer, send, keep, forward, first, second, store, begin, pump
    ):
        near, other = (side_peer, row_peer) if number == 0 else (row_peer, side_peer)
        slot = 2 * number
        firsts.append(copies.start(part(slot), part(slot + 1), near))
        seconds.append(copies.start(part(slot), part(4 + slot), other))
    pump([1])
    firsts[0].wait_recv()
    seconds.append(copies.start(part(1), part(5), row_peer))
    firsts[1].wait_recv()
    seconds.append(copies.start(part(3), part(7), side_peer))
    pump(range(2, 64))
    for copy in seconds:
        copy.wait_recv()
    for copy in firsts + seconds:
        copy.wait_send()
    for job in jobs:
        job.finish()


def home_kernel(middle, jobs, extra_count, out_count, gain_sum, plan, terms, *refs):
    keep, send = halves(terms)
    extras, sources, result, outs, targets, scratch = split_refs(refs, jobs, extra_count, out_count)
    forward, first, second, own, full, send_sems, recv_sems, local_sems, *rest = scratch
    gain_scratch, stages = (rest[:2], rest[2:]) if gain_sum is not None else ([], rest)
    block = extras[3]
    zone, side, row, core = place_here()
    row_peer, side_peer = device(zone, side, 1 - row, core), device(zone, 1 - side, row, core)
    core_peer, other_peer = device(zone, side, row, 1 - core), device(zone, 1 - side, row, 1 - core)
    copies = Copies(send_sems, recv_sems)
    size = send.shape[0] // 4
    at_home = side == core
    away = side != core
    for out in outs:
        if out.shape[0] == 1:
            out[...] = jnp.zeros_like(out)
    peers = {}
    for job in jobs:
        peers.update(job.peers(zone, side, row, core))
    plane = [row_peer, side_peer, core_peer, other_peer]
    if gain_sum is not None:
        plane = gain_sum.plane_peers(zone, side, row, core)
        peers.update(gain_sum.zone_peers(zone, side, row, core))
    greet(plane + list(peers.values()))

    def begin():
        spot = 0
        for job, source, target in zip(jobs, sources, targets):
            own_stages = stages[spot : spot + len(job.scratch)]
            job.start(copies, local_sems, source, target, own_stages)
            spot += len(job.scratch)

    def pump(steps):
        if 0 in steps:

            @pl.when(away)
            def _():
                for copy in block_side:
                    copy.start()

        for job in jobs:
            job.pump(steps)

    def store(number, start, count, sums):
        here = pl.ds(number * size + start, count)
        values = middle(here, sums, extras, outs)
        own[here, :] = values
        eighth = row * 2 + side if number == 0 else 4 + side * 2 + row

        @pl.when(at_home)
        def _():
            full[pl.ds(pl.multiple_of(eighth * size + start, 32), count), :] = values

    def piece(number, x, y):
        start = (x * 2 + y) * size if number == 0 else (4 + y * 2 + x) * size
        return full.at[pl.ds(pl.multiple_of(start, size), size)]

    both = (0, 1)
    part = lambda ref, number: ref.at[pl.ds(number * size, size)]
    block_over = [copies.make(part(block, k), piece(k, row, side), core_peer) for k in both]
    block_side = [copies.make(part(block, k), piece(k, row, side), other_peer) for k in both]
    to_side = [copies.make(part(own, k), piece(k, row, side), side_peer) for k in both]
    to_row = [copies.make(piece(k, row, side), piece(k, row, side), row_peer) for k in both]
    pass_row = [
        copies.make(piece(k, row, 1 - side), piece(k, row, 1 - side), row_peer) for k in both
    ]

    @pl.when(at_home)
    def _():
        for copy in block_over:
            copy.start()

    for _ in sum_eighths(
        copies, row_peer, side_peer, send, keep, forward, first, second, store, begin, pump
    ):
        pass
    pump([1])
    if gain_sum is not None:
        gain_sum.start(copies, extras[-1], outs[0], *gain_scratch)

    @pl.when(away)
    def _():
        for copy in to_side:
            copy.start()
        for copy in block_over:
            copy.wait_recv()

    for copy in to_row:
        copy.start()
    for job in jobs:
        if isinstance(job, TurnLate):
            job.late()
    if gain_sum is not None:
        gain_sum.middle()

    @pl.when(at_home)
    def _():
        for copy in to_side:
            copy.wait_recv()
        for copy in block_over:
            copy.wait_send()

    @pl.when(away)
    def _():
        for copy in block_side:
            copy.wait_recv()
        for copy in to_side + block_side:
            copy.wait_send()

    for copy in pass_row:
        copy.start()
    for copy in to_row + pass_row:
        copy.wait_recv()
        copy.wait_send()
    natural, local = block_columns(plan, full.shape[1], side)

    def some(start, count):
        here = pl.ds(start, count)
        for a, b in zip(natural, local):
            result[here, a] = full[here, b]

    for_rows(full.shape[0], some)
    if gain_sum is not None:
        gain_sum.finish(outs[-1])
    for job in jobs:
        job.finish()


def sum_rows(plan, kernel, middle, terms, extras, outs, number, jobs=(), gain_sum=None):
    half, width = terms.shape[0] // 2, terms.shape[1]
    eighth = half // 4
    low = jnp.bfloat16
    vmem, hbm = pl.BlockSpec(memory_space=pltpu.VMEM), pl.BlockSpec(memory_space=pl.ANY)
    scratch = [
        pltpu.VMEM((2 * eighth, width), low),
        pltpu.VMEM((half, width), low),
        pltpu.VMEM((2 * eighth, width), low),
    ]
    if kernel is home_kernel:
        scratch.append(pltpu.VMEM((2 * eighth, width), low))
        scratch.append(pltpu.VMEM((2 * half, width), low))
    copies = (12 if kernel is spread_kernel else 16) + sum(job.count for job in jobs)
    local = max([2] + [job.count_local for job in jobs])
    if gain_sum is not None:
        copies += gain_sum.count
        outs = outs + [gain_sum.output]
    scratch += [pltpu.SemaphoreType.DMA((count,)) for count in (copies, copies, local)]
    if gain_sum is not None:
        scratch += gain_sum.scratch
    scratch += [stage for job in jobs for stage in job.scratch]
    sources = [source for job in jobs for source in job.sources]
    targets = [target for job in jobs for target in job.outputs]
    return pl.pallas_call(
        functools.partial(kernel, middle, jobs, len(extras), len(outs), gain_sum, plan),
        out_shape=[jax.ShapeDtypeStruct((2 * half, width), low)] + outs + targets,
        in_specs=[vmem] * (1 + len(extras) + len(sources)),
        out_specs=[vmem] * (1 + len(outs))
        + [hbm if job.in_hbm else vmem for job in jobs for _ in job.outputs],
        scratch_shapes=scratch,
        compiler_params=pltpu.CompilerParams(
            collective_id=number, has_side_effects=True, vmem_limit_bytes=56 * 2**20
        ),
        cost_estimate=pl.CostEstimate(flops=10**6, bytes_accessed=10**5, transcendentals=0),
        name=middle.__name__,
    )(terms, *extras, *sources)


def block_columns(plan, width, of_core=None):
    if not plan.ordered:
        return [pl.ds(0, width)], [pl.ds(0, width)]
    zone, _, _, core = place_here()
    core = core if of_core is None else of_core
    size, zones = width // plan.total, plan.zones
    owners = [
        flipped(zone, plan.flips[slot % zones]) * 2 + (core if slot < zones else 1 - core)
        for slot in range(plan.total)
    ]
    natural = [pl.ds(pl.multiple_of(owner * size, size), size) for owner in owners]
    return natural, [pl.ds(slot * size, size) for slot in range(plan.total)]


def copy_rows(source, target):
    def some(row, count):
        target[pl.ds(row, count), :] = source[pl.ds(row, count), :]

    if source.shape[0] % 32:
        target[...] = source[...]
    else:
        for_rows(source.shape[0], some)


def cast_rows(source, target):
    def some(row, count):
        here = pl.ds(row, count)
        target[here, :] = source[here, :].astype(target.dtype)

    for_rows(source.shape[0], some)


def opening_kernel(plan, wide_qkv, gains, wide_gate, wide_out, wide_down, tokens, angles, *refs):
    qkv_full, gains_full, turned_gate, turned_out, turned_down, turned_tokens, turned_angles = refs[:7]
    partner_gate, send_sems, recv_sems, tokens_stage, qkv, gate, out, down = refs[7:]
    cast_rows(wide_qkv, qkv)
    zone, side, row, core = place_here()
    partner = device(zone, core, row, side)
    row_peer, core_peer = device(zone, side, 1 - row, core), device(zone, side, row, 1 - core)
    zone_peers = [device(flipped(zone, flip), side, row, core) for flip in plan.flips[1:]]
    at_home, away = side == core, side != core
    always = [row_peer, core_peer] + zone_peers

    @pl.when(at_home)
    def _():
        greet(always)

    @pl.when(away)
    def _():
        greet(always + [partner])

    copies = Copies(send_sems, recv_sems)
    zones = plan.zones
    own = (gains, qkv, angles, gate, out, down)
    ends = (gains_full.at[0], qkv_full.at[0], turned_angles, turned_gate, turned_out, turned_down)
    units = wide_gate.shape[2]

    def cast_rest():
        for half in (0, 1):
            cast_rows(wide_gate.at[half], gate.at[:, pl.ds(half * units, units)])
        cast_rows(wide_out, out)
        cast_rows(wide_down, down)

    turn = [copies.make(source, target, partner) for source, target in zip(own, ends)]
    pieces = 2
    size = tokens.shape[0] // (2 * pieces)
    spots = [
        pl.ds(pl.multiple_of((row * pieces + piece) * size, size), size) for piece in range(pieces)
    ]
    turn_rows = [copies.make(tokens.at[s], tokens_stage.at[s], partner) for s in spots]
    pass_rows = [copies.make(tokens_stage.at[s], tokens_stage.at[s], row_peer) for s in spots]
    natural, local = block_columns(plan, tokens.shape[1])

    def lay_down(all_tokens):
        def some(start, count):
            here = pl.ds(start, count)
            for a, b in zip(natural, local):
                turned_tokens[here, b] = all_tokens[here, a]

        for_rows(all_tokens.shape[0], some)

    slots = list(range(1, zones))
    weights = ((gains, gains_full), (qkv, qkv_full))
    from_own = [
        [copies.make(source, full.at[slot], zone_peers[slot - 1]) for slot in slots]
        + [copies.make(source, full.at[zones], core_peer)]
        for source, full in weights
    ] + [[copies.make(gate, partner_gate, zone_peers[0])]]
    copies.number -= 2 * zones + 1
    from_turned = [
        [copies.make(full.at[0], full.at[slot], zone_peers[slot - 1]) for slot in slots]
        + [copies.make(full.at[0], full.at[zones], core_peer)]
        for _, full in weights
    ] + [[copies.make(turned_gate, partner_gate, zone_peers[0])]]
    cross = [
        [copies.make(full.at[slot], full.at[zones + slot], core_peer) for slot in slots]
        for _, full in weights
    ]

    def cross_over(k):
        for which in (0, 1):
            from_turned[which][k].wait_recv()
            cross[which][k].start()

    @pl.when(away)
    def _():
        for copy in turn[:3]:
            copy.start()
        cast_rest()
        for which in (0, 1):
            turn[which].wait_recv()
            for copy in from_turned[which]:
                copy.start()
        turn[3].start()
        turn_rows[0].start()
        turn[3].wait_recv()
        from_turned[2][0].start()
        turn_rows[1].start()
        cross_over(0)
        turn_rows[0].wait_recv()
        pass_rows[0].start()
        for copy in turn[4:]:
            copy.start()
        turn_rows[1].wait_recv()
        pass_rows[1].start()

    @pl.when(at_home)
    def _():
        for copy in from_own[0] + from_own[1]:
            copy.start()
        cast_rest()
        for copy in from_own[2]:
            copy.start()
        for source, target in zip(own, ends):
            copy_rows(source, target)
        lay_down(tokens)
        cross_over(0)

    for k in range(1, zones - 1):
        cross_over(k)
    for which in (0, 1):
        from_turned[which][zones - 1].wait_recv()
        for copy in from_turned[which]:
            copy.wait_send()
        for copy in cross[which]:
            copy.wait_recv()
            copy.wait_send()
    from_turned[2][0].wait_recv()
    from_turned[2][0].wait_send()

    @pl.when(away)
    def _():
        for copy in pass_rows + turn[2:3] + turn[4:]:
            copy.wait_recv()
        lay_down(tokens_stage)
        for copy in turn + turn_rows + pass_rows:
            copy.wait_send()


def opening(plan, qkv, gains, gate, out, down, tokens, angles, number):
    low = jnp.bfloat16
    vmem = pl.BlockSpec(memory_space=pltpu.VMEM)
    like = lambda v: jax.ShapeDtypeStruct(v.shape, v.dtype)
    whole = lambda v: jax.ShapeDtypeStruct((2 * plan.zones,) + v.shape, low)
    operands = (qkv, gains, gate, out, down, tokens, angles)
    low_gate = jax.ShapeDtypeStruct((gate.shape[1], 2 * gate.shape[2]), low)
    low_out = jax.ShapeDtypeStruct(out.shape, low)
    low_down = jax.ShapeDtypeStruct(down.shape, low)
    outputs = [whole(qkv), whole(gains), low_gate, low_out, low_down, like(tokens), like(angles)]
    outputs += [low_gate]
    copies = 6 + 4 + 2 * plan.zones + 1 + 2 * (plan.zones - 1)
    return pl.pallas_call(
        functools.partial(opening_kernel, plan),
        out_shape=outputs,
        in_specs=[vmem] * len(operands),
        out_specs=[vmem] * len(outputs),
        scratch_shapes=[
            pltpu.SemaphoreType.DMA((copies,)),
            pltpu.SemaphoreType.DMA((copies,)),
            pltpu.VMEM(tokens.shape, tokens.dtype),
            pltpu.VMEM(qkv.shape, low),
            pltpu.VMEM(low_gate.shape, low),
            pltpu.VMEM(out.shape, low),
            pltpu.VMEM(down.shape, low),
        ],
        compiler_params=pltpu.CompilerParams(
            collective_id=number, has_side_effects=True, vmem_limit_bytes=56 * 2**20
        ),
        cost_estimate=pl.CostEstimate(flops=10**6, bytes_accessed=10**5, transcendentals=0),
        name="opening",
    )(*operands)


def inverse_rms(values):
    return lax.rsqrt(jnp.mean(values * values, -1, keepdims=True) + EPS_NORM)


def hidden_rows(own, sums, extras, outs):
    tokens, gain = extras
    hidden = tokens[own, :].astype(jnp.float32) + sums
    outs[0][own, :] = hidden
    return (hidden * inverse_rms(hidden) * gain[...]).astype(jnp.bfloat16)


def grad_hidden_rows(own, sums, extras, outs):
    hidden, out_grad, gain = extras
    values = hidden[own, :]
    factor = inverse_rms(values)
    unit = values * factor
    outs[1][...] += jnp.sum(sums * unit, 0, keepdims=True)
    grad = out_grad[own, :].astype(jnp.float32) + norm_back(sums * gain[...], unit, factor)
    outs[0][own, :] = grad
    return grad.astype(jnp.bfloat16)


def grad_input_rows(own, sums, extras, outs):
    tokens, grad_hidden, gain = extras[:3]
    values = tokens[own, :].astype(jnp.float32)
    factor = inverse_rms(values)
    unit = values * factor
    outs[0][...] += jnp.sum(sums * unit, 0, keepdims=True)
    return (grad_hidden[own, :] + norm_back(sums * gain[...], unit, factor)).astype(jnp.bfloat16)


def dot(left, right, left_dim=1, right_dim=0):
    return lax.dot_general(
        left, right, (((left_dim,), (right_dim,)), ((), ())), preferred_element_type=jnp.float32
    )


def turn_head(values, cosine, signed_sine):
    return values * cosine + pltpu.roll(values, HEAD // 2, 1) * signed_sine


def turn_back(gradient, cosine, signed_sine):
    return gradient * cosine + pltpu.roll(gradient * signed_sine, HEAD // 2, 1)


def softmax_block(query, key, first_row):
    rows, keys = query.shape[0], key.shape[0]
    scores = dot(query, key, 1, 1)
    row_at = lax.broadcasted_iota(jnp.int32, (rows, keys), 0) + first_row
    key_at = lax.broadcasted_iota(jnp.int32, (rows, keys), 1)
    scores = jnp.where(key_at <= row_at, scores, -1000000000.0)
    exponent = jnp.exp(scores - jnp.max(scores, -1, keepdims=True))
    return exponent / jnp.sum(exponent, -1, keepdims=True)


def eighth_owners():
    _, side, row, _ = place_here()
    own, off = (row, side), (1 - row, 1 - side)
    first = lambda x, y: x * 2 + y
    second = lambda x, y: 4 + y * 2 + x
    return [
        first(own[0], own[1]),
        first(own[0], off[1]),
        second(own[0], own[1]),
        second(off[0], own[1]),
        first(off[0], own[1]),
        first(off[0], off[1]),
        second(own[0], off[1]),
        second(off[0], off[1]),
    ]


def reorder_rows(source, target, into_local):
    size = source.shape[0] // 8
    for slot, owner in enumerate(eighth_owners()):
        natural = pl.ds(pl.multiple_of(owner * size, size), size)
        local = pl.ds(slot * size, size)
        if into_local:
            target[local, :] = source[natural, :]
        else:
            target[natural, :] = source[local, :]


def forward_kernel(
    tokens, weights, gain_in, gain_q, gain_k, cosine, sine,
    normed, raw, query, key, value, local, attended,
):
    low = jnp.bfloat16
    total, heads = tokens.shape[0], query.shape[1] // HEAD
    block, wide = 256, 512

    def project(step, carry):
        rows = pl.ds(pl.multiple_of(step * wide, wide), wide)
        values = tokens[rows, :].astype(jnp.float32)
        normed[rows, :] = (values * inverse_rms(values) * gain_in[...]).astype(low)
        raw[rows, :] = dot(normed[rows, :], weights[...])
        turns = (cosine[rows, :], sine[rows, :])
        for head in range(heads):
            column = (head // 2) * 4 * HEAD + (head % 2) * HEAD
            values = raw[rows, pl.ds(column, HEAD)]
            values = turn_head(values * inverse_rms(values) * gain_q[...], *turns)
            query[rows, pl.ds(head * HEAD, HEAD)] = (values * (1.0 / math.sqrt(HEAD))).astype(low)
        for group in range(heads // 2):
            column = group * 4 * HEAD + 2 * HEAD
            here = pl.ds(group * HEAD, HEAD)
            values = raw[rows, pl.ds(column, HEAD)]
            values = turn_head(values * inverse_rms(values) * gain_k[...], *turns)
            key[rows, here] = values.astype(low)
            value[rows, here] = raw[rows, pl.ds(column + HEAD, HEAD)].astype(low)
        return carry

    lax.fori_loop(0, total // wide, project, 0)

    def attend(head, carry):
        mine = pl.ds(pl.multiple_of(head * HEAD, HEAD), HEAD)
        shared = pl.ds(pl.multiple_of(lax.div(head, 2) * HEAD, HEAD), HEAD)
        for start in range(0, total, SEQ):
            for first in range(0, SEQ, block):
                rows, keys = pl.ds(start + first, block), pl.ds(start, first + block)
                probs = softmax_block(query[rows, mine], key[keys, shared], first)
                attended[rows, mine] = dot(probs.astype(low), value[keys, shared]).astype(low)
        return carry

    lax.fori_loop(0, heads, attend, 0)
    reorder_rows(attended, local, True)


def attention(tokens, weights, gain_in, gain_q, gain_k, cosine, sine):
    total = tokens.shape[0]
    columns = weights.shape[1]
    low = jnp.bfloat16
    shape = lambda width, kind=low: jax.ShapeDtypeStruct((total, width), kind)
    vmem = pl.BlockSpec(memory_space=pltpu.VMEM)
    return pl.pallas_call(
        forward_kernel,
        out_shape=[
            shape(tokens.shape[1]),
            shape(columns, jnp.float32),
            shape(columns // 2),
            shape(columns // 4),
            shape(columns // 4),
            shape(columns // 2),
        ],
        in_specs=[vmem] * 7,
        out_specs=[vmem] * 6,
        scratch_shapes=[pltpu.VMEM((total, columns // 2), low)],
        compiler_params=pltpu.CompilerParams(vmem_limit_bytes=48 * 2**20),
        cost_estimate=pl.CostEstimate(flops=10**6, bytes_accessed=10**5, transcendentals=0),
        name="attention",
    )(tokens, weights, gain_in, gain_q, gain_k, cosine, sine)


def backward_kernel(
    query, key, value, raw, grad_rows, gain_q, gain_k, cosine, sine,
    mixed, mixed_local, query_gain, key_gain, grad, key_sum, value_sum,
):
    low = jnp.bfloat16
    total, heads = query.shape[0], query.shape[1] // HEAD
    block = 256
    reorder_rows(grad_rows, grad, False)
    query_gain[...] = jnp.zeros_like(query_gain)
    key_gain[...] = jnp.zeros_like(key_gain)

    def head_norm_back(rows, column, gradient, gain, gain_grad):
        values = raw[rows, column]
        factor = inverse_rms(values)
        unit = values * factor
        turned = turn_back(gradient, cosine[rows, :], sine[rows, :])
        gain_grad[...] += jnp.sum(turned * unit, 0, keepdims=True)
        mixed[rows, column] = norm_back(turned * gain[...], unit, factor).astype(low)

    def one_group(group, carry):
        at = lambda offset: pl.ds(pl.multiple_of(group * 4 * HEAD + offset * HEAD, HEAD), HEAD)
        shared = pl.ds(pl.multiple_of(group * HEAD, HEAD), HEAD)
        key_sum[...] = jnp.zeros_like(key_sum)
        value_sum[...] = jnp.zeros_like(value_sum)
        for head in (0, 1):
            mine = pl.ds(pl.multiple_of((group * 2 + head) * HEAD, HEAD), HEAD)
            for start in range(0, total, SEQ):
                for first in range(0, SEQ, block):
                    rows, keys = pl.ds(start + first, block), pl.ds(start, first + block)
                    query_part, grad_part = query[rows, mine], grad[rows, mine]
                    probs = softmax_block(query_part, key[keys, shared], first)
                    weighed = probs * dot(grad_part, value[keys, shared], 1, 1)
                    scores = weighed - probs * jnp.sum(weighed, -1, keepdims=True)
                    scores = scores.astype(low)
                    grad_query = dot(scores, key[keys, shared]) * (1.0 / math.sqrt(HEAD))
                    head_norm_back(rows, at(head), grad_query, gain_q, query_gain)
                    key_sum[keys, :] += dot(scores, query_part, 0, 0)
                    value_sum[keys, :] += dot(probs.astype(low), grad_part, 0, 0)
        for first in range(0, total, block):
            rows = pl.ds(first, block)
            head_norm_back(rows, at(2), key_sum[rows, :], gain_k, key_gain)
            mixed[rows, at(3)] = value_sum[rows, :].astype(low)
        return carry

    lax.fori_loop(0, heads // 2, one_group, 0)
    reorder_rows(mixed, mixed_local, True)


def attention_back(query, key, value, raw, grad_rows, gain_q, gain_k, cosine, sine):
    total, columns = raw.shape
    low = jnp.bfloat16
    vmem = pl.BlockSpec(memory_space=pltpu.VMEM)
    return pl.pallas_call(
        backward_kernel,
        out_shape=[
            jax.ShapeDtypeStruct((total, columns), low),
            jax.ShapeDtypeStruct((total, columns), low),
            jax.ShapeDtypeStruct((1, HEAD), jnp.float32),
            jax.ShapeDtypeStruct((1, HEAD), jnp.float32),
        ],
        in_specs=[vmem] * 9,
        out_specs=[vmem] * 4,
        scratch_shapes=[
            pltpu.VMEM(grad_rows.shape, low),
            pltpu.VMEM((total, HEAD), jnp.float32),
            pltpu.VMEM((total, HEAD), jnp.float32),
        ],
        compiler_params=pltpu.CompilerParams(vmem_limit_bytes=48 * 2**20),
        cost_estimate=pl.CostEstimate(flops=10**6, bytes_accessed=10**5, transcendentals=0),
        name="attention_back",
    )(query, key, value, raw, grad_rows, gain_q, gain_k, cosine, sine)


def feed_kernel(plan, rows, own_grad, got_grad, gate_up, up_part, down, active, grads, out_grad):
    low = jnp.bfloat16
    block = 512
    tile = down.shape[1]
    step = pl.program_id(0)
    gate_at = pl.ds(pl.multiple_of(step * tile, tile), tile)
    up_at = pl.ds(pl.multiple_of(grads.shape[1] // 2 + step * tile, tile), tile)
    _, side, _, core = place_here()

    def lay_down(source):
        natural, blocks = block_columns(plan, source.shape[1])
        eighth = source.shape[0] // 8
        for slot, owner in enumerate(eighth_owners()):

            def some(start, count, slot=slot, owner=owner):
                here = pl.ds(pl.multiple_of(owner * eighth + start, 32), count)
                there = pl.ds(slot * eighth + start, count)
                for a, b in zip(natural, blocks):
                    out_grad[there, b] = source[here, a]

            for_rows(eighth, some)

    @pl.when((step == 0) & (side == core))
    def _():
        lay_down(own_grad)

    @pl.when((step == 0) & (side != core))
    def _():
        lay_down(got_grad)

    def one(block_at, carry):
        here = pl.ds(pl.multiple_of(block_at * block, block), block)
        gate = dot(rows[here, :], gate_up[...])
        up = dot(rows[here, :], up_part[...])
        grad = dot(out_grad[here, :], down[...])
        sigmoid = jax.nn.sigmoid(gate)
        silu = gate * sigmoid
        active[here, :] = (silu * up).astype(low)
        grads[here, gate_at] = (grad * up * sigmoid * (1.0 + gate * (1.0 - sigmoid))).astype(low)
        grads[here, up_at] = (grad * silu).astype(low)
        return carry

    lax.fori_loop(0, rows.shape[0] // block, one, 0)


def feed_forward(plan, rows, own_grad, got_grad, gate_up, down, tile):
    total, width = rows.shape
    units = down.shape[1]
    low = jnp.bfloat16
    tiles = units // tile
    whole = pl.BlockSpec(memory_space=pltpu.VMEM)
    return pl.pallas_call(
        functools.partial(feed_kernel, plan),
        grid=(tiles,),
        out_shape=[
            jax.ShapeDtypeStruct((total, units), low),
            jax.ShapeDtypeStruct((total, 2 * units), low),
            jax.ShapeDtypeStruct((total, width), low),
        ],
        in_specs=[
            whole,
            whole,
            whole,
            pl.BlockSpec((width, tile), lambda step: (0, step)),
            pl.BlockSpec((width, tile), lambda step: (0, step + tiles)),
            pl.BlockSpec((width, tile), lambda step: (0, step)),
        ],
        out_specs=[
            pl.BlockSpec((total, tile), lambda step: (0, step)),
            whole,
            whole,
        ],
        compiler_params=pltpu.CompilerParams(vmem_limit_bytes=56 * 2**20),
        cost_estimate=pl.CostEstimate(
            flops=6 * total * width * units, bytes_accessed=4 * 10**7, transcendentals=total * units
        ),
        name="feed_forward",
    )(rows, own_grad, got_grad, gate_up, gate_up, down)


class Plan:
    def __init__(self, mesh):
        self.total = mesh.shape["dp"]
        self.zones = self.total // 2
        self.tensor = mesh.shape["tensor"]
        self.flips = [k ^ (k >> 1) for k in range(self.zones)]

    def place(self):
        self.index = lax.axis_index("dp")
        self.zone = self.index // 2
        self.side = self.index % 2
        self.row = lax.axis_index("tensor") // 2
        self.core = lax.axis_index("tensor") % 2
        self.home = self.side == self.core

    def move(self, value, target):
        pairs = []
        for d in range(self.total):
            for t in range(self.tensor):
                to = target(d // 2, d % 2, t // 2, t % 2)
                if to is not None:
                    zone, side, row, core = to
                    pairs.append((d * self.tensor + t, (zone * 2 + side) * self.tensor + row * 2 + core))
        return lax.ppermute(value, ("dp", "tensor"), pairs)

    def turn(self, value):
        got = self.move(value, lambda z, y, x, c: (z, c, x, y) if y != c else None)
        return jnp.where(self.home, value, got)

    def zone_flip(self, value, bit):
        return self.move(value, lambda z, y, x, c: (z ^ bit, y, x, c))

    def core_swap(self, value):
        return self.move(value, lambda z, y, x, c: (z, y, x, 1 - c))

    def side_swap(self, value):
        return self.move(value, lambda z, y, x, c: (z, 1 - y, x, c))

    def row_swap(self, value):
        return self.move(value, lambda z, y, x, c: (z, y, 1 - x, c))

    def to_local(self, value, axis):
        width = value.shape[axis] // self.total
        parts = []
        for core in (self.core, 1 - self.core):
            for slot in range(self.zones):
                owner = (self.zone ^ self.flips[slot]) * 2 + core
                parts.append(lax.dynamic_slice_in_dim(value, owner * width, width, axis))
        return jnp.concatenate(parts, axis)

    def to_natural(self, value, axis, core=None):
        core = self.core if core is None else core
        width = value.shape[axis] // self.total
        parts = []
        for block in range(self.total):
            slot = flip = (block // 2) ^ self.zone
            for bits in range(1, self.zones.bit_length()):
                slot = slot ^ (flip >> bits)
            slot = slot + jnp.where(block % 2 == core, 0, self.zones)
            parts.append(lax.dynamic_slice_in_dim(value, slot * width, width, axis))
        return jnp.concatenate(parts, axis)

    def row_owners(self):
        own, off = (self.row, self.side), (1 - self.row, 1 - self.side)
        first = lambda x, y: x * 2 + y
        second = lambda x, y: 4 + y * 2 + x
        return [
            first(own[0], own[1]),
            first(own[0], off[1]),
            second(own[0], own[1]),
            second(off[0], own[1]),
            first(off[0], own[1]),
            first(off[0], off[1]),
            second(own[0], off[1]),
            second(off[0], off[1]),
        ]

    def rows_local(self, value, slots=range(8)):
        size = value.shape[0] // 8
        owners = self.row_owners()
        return jnp.concatenate(
            [lax.dynamic_slice_in_dim(value, owners[slot] * size, size, 0) for slot in slots], 0
        )

    def rows_natural(self, value, order=range(8)):
        size = value.shape[0] // 8
        place = [list(order).index(slot) for slot in range(8)]
        parts = []
        for piece in range(8):
            x, y = (piece // 2, piece % 2) if piece < 4 else (piece % 2, (piece - 4) // 2)
            slots = (0, 1, 4, 5) if piece < 4 else (2, 6, 3, 7)
            same_x, same_y = x == self.row, y == self.side
            slot = jnp.where(
                same_x,
                jnp.where(same_y, place[slots[0]], place[slots[1]]),
                jnp.where(same_y, place[slots[2]], place[slots[3]]),
            )
            parts.append(lax.dynamic_slice_in_dim(value, slot * size, size, 0))
        return jnp.concatenate(parts, 0)

    def from_zones(self, shard):
        return [self.zone_flip(shard, flip) for flip in self.flips[1:]]

    def to_zones(self, parts, slots):
        return [self.zone_flip(parts[slot], self.flips[slot]) for slot in slots]

    def middle_swap(self, pair):
        return self.move(pair, lambda z, y, x, c: (z ^ 3, y, x, c) if z in (1, 2) else None)

    def inward(self, part):
        return self.move(part, lambda z, y, x, c: (z ^ 1, y, x, c) if z in (0, 3) else None)

    def pass_outward(self, pair):
        return self.move(pair, lambda z, y, x, c: (z ^ 1, y, x, c) if z in (1, 2) else None)

    def far_pair(self, middle, passed):
        inner = (self.zone == 1) | (self.zone == 2)
        return jnp.where(inner, middle, passed[::-1])

    def first_swap(self, send):
        half = send.shape[0] // 2
        return self.row_swap(send[:half]), self.side_swap(send[half:])

    def second_swap(self, keep, got):
        quarter = keep.shape[0] // 4
        row_part = keep[: 2 * quarter] + got[0].astype(jnp.float32)
        side_part = keep[2 * quarter :] + got[1].astype(jnp.float32)
        own = jnp.concatenate([row_part[:quarter], side_part[:quarter]], 0)
        return own, (
            self.side_swap(row_part[quarter:].astype(jnp.bfloat16)),
            self.row_swap(side_part[quarter:].astype(jnp.bfloat16)),
        )

    def spread_first(self, own):
        half = own.shape[0] // 2
        return (self.side_swap(own[:half]), self.row_swap(own[half:]))

    def spread_second(self, own, got):
        half = own.shape[0] // 2
        row_part = jnp.concatenate([own[:half], got[0]], 0)
        side_part = jnp.concatenate([own[half:], got[1]], 0)
        return row_part, side_part, self.row_swap(row_part), self.side_swap(side_part)

    def send_home(self, own):
        to_home = lambda z, y, x, c: (z, c, x, c) if y != c else None
        return jnp.concatenate([own, self.move(own, to_home)], 0)

    def row_home(self, part):
        return self.move(part, lambda z, y, x, c: (z, y, 1 - x, c) if y == c else None)

    def share_home(self, part, other):
        full = jnp.concatenate([part, other], 0)
        full = self.to_natural(self.rows_natural(full, (0, 2, 1, 6, 4, 3, 5, 7)), 1)
        got = self.move(full, lambda z, y, x, c: (z, y, x, 1 - c) if y == c else None)
        return full, got

    def turned(self, own, got):
        return jnp.where(self.home, own, got)

    def sum_everywhere(self, value):
        value = value + self.row_swap(value)
        value = value + self.side_swap(value)
        value = value + self.core_swap(value)
        bit = 1
        while bit < self.zones:
            value = value + self.zone_flip(value, bit)
            bit *= 2
        return value


def shards(
    plan,
    tokens,
    positions,
    out_grad,
    qkv_weight,
    qkv_first,
    qkv_second,
    out_weight,
    out_first,
    out_second,
    gate_up,
    gate_up_first,
    gate_up_second,
    down_weight,
    down_first,
    down_second,
    gains,
    gains_first,
    gains_second,
):
    plan.place()
    low = jnp.bfloat16
    tok_rows, model_width = tokens.shape
    groups = qkv_weight.shape[1]
    head_size = qkv_weight.shape[3]
    shard_rows = qkv_weight.shape[0]
    seq_count = tok_rows // SEQ
    mixed_cols = groups * 4 * head_size
    near_cols = model_width // 2
    kept = tok_rows // 2
    gain_count = gains.shape[0]

    tree = plan.zones == 4
    slots = range(1, plan.zones)

    def column_parts(value):
        return value.reshape((plan.zones, -1) + value.shape[1:])

    units = gate_up.shape[2]
    plan.ordered = (model_width // plan.total) % 128 == 0
    gain_rows = 16
    gain_block = jnp.pad(gains.astype(low), (0, gain_rows * 128 - gain_count)).reshape(gain_rows, 128)
    tile = min(units, 256)
    angle_at = positions.astype(jnp.float32).reshape(-1, 128)
    both_qkv, both_gains, turned_gate, turned_out, turned_down, tokens, angle_at, partner_gate = opening(
        plan,
        qkv_weight.reshape(shard_rows, mixed_cols),
        gain_block,
        gate_up,
        out_weight,
        down_weight,
        tokens,
        angle_at,
        3,
    )
    positions = angle_at.reshape(-1)
    turned_out, turned_gate, turned_down, tokens, positions, both_qkv, both_gains, out_grad = fence(
        turned_out, turned_gate, turned_down, tokens, positions, both_qkv, both_gains, out_grad
    )

    got_grad = plan.move(out_grad, lambda z, y, x, c: (z, c, x, y) if y != c else None)
    zone_out = plan.from_zones(turned_out)
    if tree:
        partner_down = plan.zone_flip(turned_down, 1)
    else:
        partner_down = plan.from_zones(turned_down)
        partner_gate = plan.from_zones(turned_gate)
    if not plan.ordered:
        tokens = plan.to_local(tokens, 1)
    cosine, sine_table = rotary(positions, head_size)
    signed_sine = jnp.concatenate(
        [-sine_table[:, : head_size // 2], sine_table[:, head_size // 2 :]], 1
    )
    full_qkv = both_qkv.reshape(model_width, mixed_cols)
    gain_slots = both_gains.reshape(plan.total, -1)[:, :gain_count]
    gain_all = plan.to_natural(gain_slots.reshape(-1), 0).astype(jnp.float32)
    gain_in = plan.to_local(gain_all[:model_width], 0)[None]
    gain_post = plan.to_local(gain_all[model_width : 2 * model_width], 0)[None]
    gain_q = gain_all[2 * model_width : 2 * model_width + head_size][None]
    gain_k = gain_all[2 * model_width + head_size :][None]
    normed, raw, query, key_rot, values_low, attended = attention(
        tokens, full_qkv, gain_in, gain_q, gain_k, cosine, signed_sine
    )
    attended, zone_out, turned_out, turned_down, turned_gate, partner_gate, partner_down = fence(
        attended, zone_out, turned_out, turned_down, turned_gate, partner_gate, partner_down
    )

    near_out = jnp.concatenate([turned_out] + zone_out, 0)
    far_out = plan.core_swap(near_out)
    own_tokens = plan.rows_local(tokens, (0, 2))
    near_out, far_out, own_tokens = fence(near_out, far_out, own_tokens)

    full_out = jnp.concatenate([near_out, far_out], 0)
    branch_terms = contract_cols(attended, full_out).astype(low)
    pairs = [(turned_gate, partner_gate), (turned_down, partner_down)]
    jobs = [PairTree(pairs, (2, 2))] if tree else []
    normed_rows, hidden, *gathered = sum_rows(
        plan,
        spread_kernel,
        hidden_rows,
        branch_terms,
        [own_tokens, gain_post],
        [jax.ShapeDtypeStruct((tok_rows // 4, model_width), jnp.float32)],
        0,
        jobs,
    )
    if not tree:
        near = [jnp.concatenate([own] + rest, 0) for own, rest in pairs]
        gathered = [jnp.concatenate([part, plan.core_swap(part)], 0) for part in near]
    full_gate = gathered[0].reshape(model_width, 2 * units)
    full_down = gathered[1].reshape(model_width, units)
    normed_rows, hidden, full_gate, full_down, got_grad = fence(
        normed_rows, hidden, full_gate, full_down, got_grad
    )

    def zone_parts(near, got):
        both = (near + got.astype(jnp.float32)).astype(low)
        return both.reshape((plan.zones, -1) + both.shape[1:])

    def zone_total(parts, *arrived):
        total = parts[0].astype(jnp.float32)
        for part in sum([list(group) for group in arrived], []):
            total = total + part.astype(jnp.float32)
        return total.astype(low)

    active, grad_both, out_grad = feed_forward(
        plan, normed_rows, out_grad, got_grad, full_gate, full_down, tile
    )
    if not plan.ordered:
        out_grad = plan.to_local(out_grad, 1)
    gate_far = contract_rows(normed_rows[:, near_cols:], grad_both).astype(low)
    gate_far, active, grad_both, out_grad, normed_rows = fence(
        gate_far, active, grad_both, out_grad, normed_rows
    )

    gate_got = plan.core_swap(gate_far)
    down_far = contract_rows(out_grad[:, near_cols:], active).astype(low)
    gate_got, down_far, active, grad_both, normed_rows = fence(
        gate_got, down_far, active, grad_both, normed_rows
    )

    down_got = plan.core_swap(down_far)
    gate_parts = zone_parts(contract_rows(normed_rows[:, :near_cols], grad_both), gate_got)
    down_parts = zone_parts(contract_rows(out_grad[:, :near_cols], active), down_got)
    gate_parts, down_parts, grad_both = fence(gate_parts, down_parts, grad_both)

    if tree:
        gate_ready = plan.inward(gate_parts[3, : shard_rows // 2])
    else:
        gate_ready = gate_parts[0]
    post_terms = contract_cols(grad_both, full_gate).astype(low)
    post_terms, gate_parts, gate_ready, down_parts = fence(
        post_terms, gate_parts, gate_ready, down_parts
    )

    if tree:
        down_sums = [plan.inward(down_parts[3]), plan.inward(down_parts[2])]
    else:
        down_sums = plan.to_zones(down_parts, slots)
    eighth = tok_rows // 8
    own_grad = jnp.concatenate([out_grad[:eighth], out_grad[2 * eighth : 3 * eighth]], 0)
    branch_rows, grad_hidden, post_gain_grad, mlp_terms, gate_sums = sum_rows(
        plan,
        spread_kernel,
        grad_hidden_rows,
        post_terms,
        [hidden, own_grad, gain_post],
        [
            jax.ShapeDtypeStruct((tok_rows // 4, model_width), jnp.float32),
            jax.ShapeDtypeStruct((1, model_width), jnp.float32),
        ],
        1,
        [
            SideDot(active, full_down),
            PairScatter(gate_parts, gate_ready, 2) if tree else ZoneBlocks(plan, gate_parts, slots),
        ],
    )
    branch_rows, grad_hidden, post_gain_grad, gate_sums, mlp_terms, down_parts, down_sums = fence(
        branch_rows, grad_hidden, post_gain_grad, gate_sums, mlp_terms, down_parts, down_sums
    )

    mlp_got = plan.first_swap(mlp_terms[kept:])
    if tree:
        gate_last = [plan.zone_flip(gate_sums[1], 1)]
        gate_own = gate_sums
        down_pair = down_parts[2:].astype(jnp.float32) + jnp.stack(down_sums).astype(jnp.float32)
        down_sums = plan.middle_swap(down_pair.astype(low))
    else:
        gate_last, gate_own = gate_sums, gate_parts
    grad_att = jnp.dot(branch_rows, full_out, preferred_element_type=jnp.float32).astype(low)
    grad_mixed, mixed_rows, query_gain_grad, key_gain_grad = attention_back(
        query, key_rot, values_low, raw, grad_att, gain_q, gain_k, cosine, signed_sine
    )
    gain_terms = jnp.concatenate(
        [plan.to_natural(post_gain_grad, 1), query_gain_grad, key_gain_grad], 1
    )
    if tree:
        down_own = (down_parts[:2].astype(jnp.float32) + down_sums.astype(jnp.float32)).astype(low)
    grad_mixed, mixed_rows, gain_terms, normed, gate_last, branch_rows, mlp_got, down_sums = fence(
        grad_mixed, mixed_rows, gain_terms, normed, gate_last, branch_rows, mlp_got, down_sums
    )

    mlp_own, mlp_last = plan.second_swap(mlp_terms[:kept].astype(jnp.float32), mlp_got)
    if tree:
        total_down = zone_total(down_own, [plan.zone_flip(down_own[1], 1)])
    else:
        total_down = zone_total(down_parts, down_sums)
    total_gate = zone_total(gate_own, gate_last)
    total_gate = jnp.concatenate([total_gate[:, :units], total_gate[:, units:]], 0)
    out_far = contract_rows(branch_rows[:, near_cols:], attended).astype(low)
    out_got = plan.core_swap(out_far)
    normed_terms = contract_cols(mixed_rows, full_qkv).astype(low)
    out_parts = zone_parts(contract_rows(branch_rows[:, :near_cols], attended), out_got)
    block_own = (hidden + mlp_own + jnp.concatenate(mlp_last, 0).astype(jnp.float32)).astype(low)
    out_parts, normed_terms, total_gate, total_down, block_own, normed, grad_mixed = fence(
        out_parts, normed_terms, total_gate, total_down, block_own, normed, grad_mixed
    )

    gain_sum = GainSum(plan, gain_terms.shape[1], model_width) if plan.ordered else None
    mine, input_gain_grad, *rest = sum_rows(
        plan,
        home_kernel,
        grad_input_rows,
        normed_terms,
        [own_tokens, grad_hidden, gain_in, block_own] + ([gain_terms] if plan.ordered else []),
        [jax.ShapeDtypeStruct((1, model_width), jnp.float32)],
        2,
        [
            BlockGrad(plan, normed, grad_mixed),
            ZoneBlocks(plan, out_parts, slots),
            TurnLate(total_gate),
            TurnLate(total_down),
        ],
        gain_sum,
    )
    if plan.ordered:
        summed_gains, total_qkv, out_sent, got_gate, got_down = rest
    else:
        total_qkv, out_sent, got_gate, got_down = rest
        summed_gains = plan.sum_everywhere(
            jnp.concatenate([plan.to_natural(input_gain_grad, 1), gain_terms], 1)
        )
    mine, summed_gains, total_qkv, out_sent, got_gate, got_down = fence(
        mine, summed_gains, total_qkv, out_sent, got_gate, got_down
    )

    summed_gate = plan.turned(total_gate, got_gate).reshape(gate_up.shape)
    summed_down = plan.turned(total_down, got_down)
    other = plan.core_swap(mine)
    input_full, block_out = jnp.where(plan.home, mine, other), jnp.where(plan.home, other, mine)
    if not plan.ordered:
        input_full = plan.to_natural(input_full, 1, plan.side)
        block_out = plan.to_natural(block_out, 1, plan.side)
    summed_both = plan.turn(
        jnp.concatenate([total_qkv, zone_total(out_parts, out_sent)], 1)
    ).astype(jnp.float32)
    summed_qkv = summed_both[:, :mixed_cols].reshape(qkv_weight.shape)
    summed_out = summed_both[:, mixed_cols:]
    summed_gate = summed_gate.astype(jnp.float32)
    summed_down = summed_down.astype(jnp.float32)
    summed_gains = lax.dynamic_slice_in_dim(summed_gains[0], plan.index * gain_count, gain_count, 0)
    input_rows = input_full.astype(jnp.float32)

    qkv_moment, qkv_square, qkv_updated = adamw(
        qkv_weight, summed_qkv, qkv_first, qkv_second, RATE_QKV, DECAY_RATE
    )
    out_moment, out_square, out_updated = adamw(
        out_weight, summed_out, out_first, out_second, RATE_OUT, DECAY_RATE
    )
    gate_moment, gate_square, gate_updated = adamw(
        gate_up, summed_gate, gate_up_first, gate_up_second, RATE_GATE, DECAY_RATE
    )
    down_moment, down_square, down_updated = adamw(
        down_weight, summed_down, down_first, down_second, RATE_DOWN, DECAY_RATE
    )
    gain_moment, gain_square, gain_updated = adamw(
        gains, summed_gains, gains_first, gains_second, RATE_GAIN, 0.0
    )
    return (
        block_out,
        input_rows,
        qkv_moment,
        qkv_square,
        qkv_updated,
        out_moment,
        out_square,
        out_updated,
        gate_moment,
        gate_square,
        gate_updated,
        down_moment,
        down_square,
        down_updated,
        gain_moment,
        gain_square,
        gain_updated,
    )


def solution(mesh):
    plan = Plan(mesh)
    placed = (
        P("dp", None),
        P("dp"),
        P("dp", None),
        P("dp", "tensor", None, None),
        P("dp", "tensor", None, None),
        P("dp", "tensor", None, None),
        P("dp", "tensor"),
        P("dp", "tensor"),
        P("dp", "tensor"),
        P(None, "dp", "tensor"),
        P(None, "dp", "tensor"),
        P(None, "dp", "tensor"),
        P("dp", "tensor"),
        P("dp", "tensor"),
        P("dp", "tensor"),
        P("dp"),
        P("dp"),
        P("dp"),
    )
    return jax.shard_map(
        functools.partial(shards, plan),
        mesh=mesh,
        in_specs=placed,
        out_specs=(
            P("dp", None),
            P("dp", None),
            P("dp", "tensor", None, None),
            P("dp", "tensor", None, None),
            P("dp", "tensor", None, None),
            P("dp", "tensor"),
            P("dp", "tensor"),
            P("dp", "tensor"),
            P(None, "dp", "tensor"),
            P(None, "dp", "tensor"),
            P(None, "dp", "tensor"),
            P("dp", "tensor"),
            P("dp", "tensor"),
            P("dp", "tensor"),
            P("dp"),
            P("dp"),
            P("dp"),
        ),
        check_vma=False,
    )
```

```python
import functools
import math

import jax
import jax.numpy as jnp
from jax import lax
from jax.experimental import pallas as pl
from jax.experimental.pallas import tpu as pltpu
from jax.sharding import PartitionSpec as P

SEQ = 1024
STEP = 10


EPS_NORM = 1e-06
THETA = 1000000.0
BETA_ONE = 0.9
BETA_TWO = 0.95
ADAM_EPS = 1e-08
DECAY_RATE = 0.1
RATE_QKV = 0.05
RATE_OUT = 0.3
RATE_GATE = 0.05
RATE_DOWN = 0.03
RATE_GAIN = 1.0


def rotary(positions, head_size):
    freq_index = jnp.arange(head_size // 2, dtype=jnp.float32)
    inverse = jnp.exp(freq_index * (-2.0 * math.log(THETA) / head_size))
    angles = positions.astype(jnp.float32)[:, None] * inverse[None, :]
    cosine = jnp.cos(angles)
    sine_table = jnp.sin(angles)
    return (jnp.concatenate([cosine, cosine], -1), jnp.concatenate([sine_table, sine_table], -1))


def rotate(values, cosine, sine_table):
    half_size = values.shape[-1] // 2
    turned = jnp.concatenate([-values[..., half_size:], values[..., :half_size]], -1)
    return values * cosine[:, None, :] + turned * sine_table[:, None, :]


def unrotate(gradient, cosine, sine_table):
    half_size = gradient.shape[-1] // 2
    turned = gradient * sine_table[:, None, :]
    rotated_back = jnp.concatenate([turned[..., half_size:], -turned[..., :half_size]], -1)
    return gradient * cosine[:, None, :] + rotated_back


def norm_back(grad_unit, unit_vals, factor):
    return factor * (grad_unit - unit_vals * jnp.mean(grad_unit * unit_vals, -1, keepdims=True))


def contract_rows(left, right):
    return lax.dot_general(
        left, right, (((0,), (0,)), ((), ())), preferred_element_type=jnp.float32
    )


def contract_cols(left, right):
    return lax.dot_general(
        left, right, (((1,), (1,)), ((), ())), preferred_element_type=jnp.float32
    )


def block_scores(query_part, key_part, first_row, block_rows, last_row):
    scores = jnp.einsum(
        "nqkgd,nskd->nkgqs", query_part, key_part, preferred_element_type=jnp.float32
    )
    causal = (first_row + jnp.arange(block_rows))[:, None] >= jnp.arange(last_row)[None, :]
    return jnp.where(causal, scores, -1000000000.0)


def attention_forward(query, key_rot, values_low, seq_len):
    block_rows = min(512, seq_len)
    outputs = []
    log_sums = []
    for first_row in range(0, seq_len, block_rows):
        last_row = first_row + block_rows
        query_part = query[:, first_row:last_row]
        scores = block_scores(query_part, key_rot[:, :last_row], first_row, block_rows, last_row)
        row_max = jnp.max(scores, -1, keepdims=True)
        exponent = jnp.exp(scores - row_max)
        row_total = jnp.sum(exponent, -1, keepdims=True)
        probs_low = (exponent / row_total).astype(jnp.bfloat16)
        outputs.append(
            jnp.einsum(
                "nkgqs,nskd->nqkgd",
                probs_low,
                values_low[:, :last_row],
                preferred_element_type=jnp.float32,
            )
        )
        log_sums.append(row_max + jnp.log(row_total))
    return (jnp.concatenate(outputs, 1), log_sums)


def attention_backward(query, key_rot, values_low, grad_att, log_sums, seq_len):
    block_rows = min(512, seq_len)
    query_grads = []
    key_grad = jnp.zeros(key_rot.shape, jnp.float32)
    value_grad = jnp.zeros(values_low.shape, jnp.float32)
    for block_index, first_row in enumerate(range(0, seq_len, block_rows)):
        last_row = first_row + block_rows
        query_part = query[:, first_row:last_row]
        grad_part = grad_att[:, first_row:last_row]
        key_part = key_rot[:, :last_row]
        value_part = values_low[:, :last_row]
        scores = block_scores(query_part, key_part, first_row, block_rows, last_row)
        probs = jnp.exp(scores - log_sums[block_index])
        probs_low = probs.astype(jnp.bfloat16)
        grad_probs = jnp.einsum(
            "nqkgd,nskd->nkgqs", grad_part, value_part, preferred_element_type=jnp.float32
        )
        grad_scores = (
            probs * (grad_probs - jnp.sum(probs * grad_probs, -1, keepdims=True))
        ).astype(jnp.bfloat16)
        query_grads.append(
            jnp.einsum(
                "nkgqs,nskd->nqkgd", grad_scores, key_part, preferred_element_type=jnp.float32
            )
        )
        padding = ((0, 0), (0, seq_len - last_row), (0, 0), (0, 0))
        key_grad = key_grad + jnp.pad(
            jnp.einsum(
                "nkgqs,nqkgd->nskd", grad_scores, query_part, preferred_element_type=jnp.float32
            ),
            padding,
        )
        value_grad = value_grad + jnp.pad(
            jnp.einsum(
                "nkgqs,nqkgd->nskd", probs_low, grad_part, preferred_element_type=jnp.float32
            ),
            padding,
        )
    return (jnp.concatenate(query_grads, 1), key_grad, value_grad)


def adamw(weight, gradient, moment, second, step_rate, decay_rate):
    moment = BETA_ONE * moment + (1.0 - BETA_ONE) * gradient
    second = BETA_TWO * second + (1.0 - BETA_TWO) * gradient * gradient
    first_hat = moment / (1.0 - BETA_ONE**STEP)
    second_hat = second / (1.0 - BETA_TWO**STEP)
    weight = weight - step_rate * (
        first_hat / (jnp.sqrt(second_hat) + ADAM_EPS) + decay_rate * weight
    )
    return (moment, second, weight)


def fence(*values):
    return lax.optimization_barrier(values)


MESH = pl.DeviceIdType.MESH
HEAD = 128
AHEAD = 2


def place_here():
    index, place = lax.axis_index("dp"), lax.axis_index("tensor")
    return lax.div(index, 2), lax.rem(index, 2), lax.div(place, 2), lax.rem(place, 2)


def device(zone, side, row, core):
    return (zone * 2 + side, row * 2 + core)


def flipped(zone, flip):
    bit = 1
    while bit <= flip:
        if flip & bit:
            zone = zone + bit - 2 * bit * lax.rem(lax.div(zone, bit), 2)
        bit *= 2
    return zone


def greet(devices, amount=None):
    barrier = pltpu.get_barrier_semaphore()
    for peer in devices:
        pl.semaphore_signal(barrier, inc=1, device_id=peer, device_id_type=MESH)
    pl.semaphore_wait(barrier, len(devices) if amount is None else amount)


def for_rows(count, body):
    step = 32

    def one(block, carry):
        body(pl.multiple_of(block * step, step), step)
        return carry

    lax.fori_loop(0, count // step, one, 0)


class Copies:
    def __init__(self, send_sems, recv_sems):
        self.send_sems, self.recv_sems = send_sems, recv_sems
        self.number = 0

    def make(self, source, target, peer):
        number, self.number = self.number, self.number + 1
        return pltpu.make_async_remote_copy(
            src_ref=source,
            dst_ref=target,
            send_sem=self.send_sems.at[number],
            recv_sem=self.recv_sems.at[number],
            device_id=peer,
            device_id_type=MESH,
        )

    def start(self, source, target, peer):
        copy = self.make(source, target, peer)
        copy.start()
        return copy


class GainSum:
    def __init__(self, plan, rest, width):
        self.plan, self.width = plan, width
        self.total = width + rest
        self.scratch = [
            pltpu.VMEM((8, 1, self.total), jnp.float32),
            pltpu.VMEM((plan.zones, 1, self.total), jnp.float32),
        ]
        self.output = jax.ShapeDtypeStruct((1, self.total), jnp.float32)
        self.count = 7 + plan.zones - 1

    def plane_peers(self, zone, side, row, core):
        steps = [(s, r, c) for s in range(2) for r in range(2) for c in range(2)][1:]
        turn = lambda value, step: 1 - value if step else value
        return [device(zone, turn(side, s), turn(row, r), turn(core, c)) for s, r, c in steps]

    def zone_peers(self, zone, side, row, core):
        return {flip: device(flipped(zone, flip), side, row, core) for flip in self.plan.flips[1:]}

    def start(self, copies, rest, blocks, plane_sums, zone_sums):
        zone, side, row, core = place_here()
        plan = self.plan
        size = self.width // plan.total
        self.copies, self.plane_sums, self.zone_sums, self.zone = copies, plane_sums, zone_sums, zone
        here = side * 4 + row * 2 + core
        plane_sums[here, :, pl.ds(self.width, self.total - self.width)] = rest[...]
        for slot in range(plan.total):
            owner = flipped(zone, plan.flips[slot % plan.zones]) * 2
            owner = owner + (core if slot < plan.zones else 1 - core)
            spot = pl.ds(pl.multiple_of(owner * size, size), size)
            plane_sums[here, :, spot] = blocks[:, pl.ds(slot * size, size)]
        self.plane = [
            copies.start(plane_sums.at[here], plane_sums.at[here], peer)
            for peer in self.plane_peers(zone, side, row, core)
        ]

    def middle(self):
        for copy in self.plane:
            copy.wait_recv()
        total = self.plane_sums[0]
        for place in range(1, 8):
            total = total + self.plane_sums[place]
        self.zone_sums[self.zone] = total
        zone, side, row, core = place_here()
        self.across = [
            self.copies.start(self.zone_sums.at[self.zone], self.zone_sums.at[self.zone], peer)
            for peer in self.zone_peers(zone, side, row, core).values()
        ]

    def finish(self, out):
        for copy in self.across:
            copy.wait_recv()
        total = self.zone_sums[0]
        for place in range(1, self.plan.zones):
            total = total + self.zone_sums[place]
        out[...] = total
        for copy in self.plane + self.across:
            copy.wait_send()


class ZoneBlocks:
    scratch = []

    def __init__(self, plan, source, slots, begin=0):
        self.flips, self.slots, self.sources, self.begin = plan.flips, list(slots), [source], begin
        self.outputs = [
            jax.ShapeDtypeStruct((len(self.slots),) + source.shape[1:], source.dtype)
        ]
        self.count, self.count_local = len(self.slots), 0
        self.in_hbm = False

    def peers(self, zone, side, row, core):
        return {
            self.flips[slot]: device(flipped(zone, self.flips[slot]), side, row, core)
            for slot in self.slots
        }

    def start(self, copies, local_sems, sources, targets, stages):
        zone, side, row, core = place_here()
        self.started = [
            copies.make(
                sources[0].at[slot],
                targets[0].at[number],
                device(flipped(zone, self.flips[slot]), side, row, core),
            )
            for number, slot in enumerate(self.slots)
        ]
        self.waiting = True
        if self.begin == 0:
            self.pump([0])

    def pump(self, steps):
        if self.waiting and self.begin in steps:
            self.waiting = False
            for copy in self.started:
                copy.start()

    def finish(self):
        for copy in self.started:
            copy.wait_send()
        for copy in self.started:
            copy.wait_recv()


def inner_zone(zone):
    return lax.rem(lax.div(zone + 1, 2), 2)


class SideDot:
    count, count_local, scratch, in_hbm = 0, 0, [], False

    def __init__(self, left, right):
        self.sources = [left, right]
        self.outputs = [jax.ShapeDtypeStruct((left.shape[0], right.shape[0]), jnp.bfloat16)]

    def peers(self, zone, side, row, core):
        return {}

    def some(self, first, last):
        left, right = self.refs
        size = 256

        def one(step, carry):
            here = pl.ds(pl.multiple_of(step * size, size), size)
            self.out[:, here] = dot(left[...], right[here, :], 1, 1).astype(jnp.bfloat16)
            return carry

        lax.fori_loop(first, last, one, 0)

    def start(self, copies, local_sems, sources, targets, stages):
        self.refs, self.out = sources, targets[0]
        self.steps = self.out.shape[1] // 256
        self.some(0, self.steps // 2)

    def pump(self, steps):
        if 0 in steps:
            self.some(self.steps // 2, self.steps)

    def finish(self):
        pass


class PairScatter:
    def __init__(self, parts, ready, pieces):
        self.sources, self.pieces = [parts, ready], pieces
        _, rows, columns = parts.shape
        self.size = rows // pieces
        self.outputs = [jax.ShapeDtypeStruct((2, rows, columns), parts.dtype)]
        self.scratch = [pltpu.VMEM((2, rows, columns), parts.dtype)] * 2
        self.count, self.count_local = 4 * pieces - 1, 0
        self.in_hbm = False

    def peers(self, zone, side, row, core):
        return {
            1: device(flipped(zone, 1), side, row, core),
            3: device(flipped(zone, 3), side, row, core),
        }

    def start(self, copies, local_sems, sources, targets, stages):
        zone, side, row, core = place_here()
        self.parts, self.ready = sources
        self.out = targets[0]
        self.inward, self.crossed = stages
        inner_peer = device(flipped(zone, 3), side, row, core)
        outer_peer = device(flipped(zone, 1), side, row, core)
        self.inner = inner_zone(zone) == 1
        self.outer = inner_zone(zone) == 0
        pieces = [pl.ds(piece * self.size, self.size) for piece in range(self.pieces)]
        self.steps = [(slot, rows) for slot in (0, 1) for rows in pieces]
        self.to_inner = [
            copies.make(self.parts.at[3 - slot, rows], self.inward.at[slot, rows], outer_peer)
            for slot, rows in self.steps[1:]
        ]
        self.across = [
            copies.make(self.inward.at[slot, rows], self.crossed.at[slot, rows], inner_peer)
            for slot, rows in self.steps
        ]

        @pl.when(self.outer)
        def _():
            for copy in self.to_inner[:AHEAD]:
                copy.start()

        @pl.when(self.inner)
        def _():
            slot, rows = self.steps[0]
            self.add(self.inward, slot, rows, self.parts.at[2], self.ready)
            self.across[0].start()

    def add(self, target, slot, rows, left, right):
        def some(row, count):
            here = pl.ds(rows.start + row, count)
            both = left[here, :].astype(jnp.float32) + right[here, :].astype(jnp.float32)
            target.at[slot][here, :] = both.astype(jnp.bfloat16)

        for_rows(self.size, some)

    def pump(self, steps):
        steps = [step for step in steps if step < len(self.to_inner)]

        @pl.when(self.inner)
        def _():
            for step in steps:
                slot, rows = self.steps[step + 1]
                self.to_inner[step].wait_recv()
                self.add(self.inward, slot, rows, self.parts.at[2 + slot], self.inward.at[slot])
                self.across[step + 1].start()
                self.settle(step)

        @pl.when(self.outer)
        def _():
            for step in steps:
                self.to_inner[step].wait_send()
                for copy in self.to_inner[step + AHEAD : step + AHEAD + 1]:
                    copy.start()

    def settle(self, step):
        slot, rows = self.steps[step]
        self.across[step].wait_recv()
        self.add(self.out, slot, rows, self.parts.at[slot], self.crossed.at[slot])

    def finish(self):
        @pl.when(self.inner)
        def _():
            self.settle(len(self.steps) - 1)
            for copy in self.across:
                copy.wait_send()

        @pl.when(self.outer)
        def _():
            for slot in (0, 1):

                def some(row, count, slot=slot):
                    here = pl.ds(row, count)
                    self.out.at[slot][here, :] = self.parts.at[slot][here, :]

                for_rows(self.parts.shape[1], some)


class BlockGrad:
    in_hbm = False

    def __init__(self, plan, left, right):
        self.zones, self.flips = plan.zones, plan.flips
        self.sources = [left, right]
        shape = (left.shape[1] // plan.total, right.shape[1])
        low = jnp.bfloat16
        self.outputs = [jax.ShapeDtypeStruct(shape, low)]
        self.scratch = [pltpu.VMEM((plan.zones,) + shape, low)] * 4
        self.count, self.count_local = 2 * plan.zones, 0

    def peers(self, zone, side, row, core):
        return {flip: device(flipped(zone, flip), side, row, core) for flip in self.flips[1:]}

    def product(self, block):
        size = self.out.shape[0]
        return dot(self.left[:, pl.ds(block * size, size)], self.right[...], 0, 0)

    def start(self, copies, local_sems, sources, targets, stages):
        zone, side, row, core = place_here()
        self.left, self.right = sources
        self.out = targets[0]
        self.far, self.got, self.parts, self.arrived = stages
        core_peer = device(zone, side, row, 1 - core)
        self.order = list(range(1, self.zones)) + [0]
        self.over = [
            copies.make(self.far.at[slot], self.got.at[slot], core_peer)
            for slot in range(self.zones)
        ]
        self.along = [
            copies.make(
                self.parts.at[slot],
                self.arrived.at[slot],
                device(flipped(zone, self.flips[slot]), side, row, core),
            )
            for slot in range(1, self.zones)
        ]
        for slot in self.order:
            self.far[slot] = self.product(self.zones + slot).astype(jnp.bfloat16)
            self.over[slot].start()

    def pump(self, steps):
        for slot in self.order if 0 in steps else []:
            near = self.product(slot)
            self.over[slot].wait_recv()
            self.parts[slot] = (near + self.got[slot].astype(jnp.float32)).astype(jnp.bfloat16)
            if slot:
                self.along[slot - 1].start()

    def finish(self):
        total = self.parts[0].astype(jnp.float32)
        for slot in range(1, self.zones):
            self.along[slot - 1].wait_recv()
            total = total + self.arrived[slot].astype(jnp.float32)
        self.out[...] = total.astype(jnp.bfloat16)
        for copy in self.over + self.along:
            copy.wait_send()


class TurnLate:
    count, count_local, scratch, in_hbm = 1, 0, [], False

    def __init__(self, values):
        self.sources = [values]
        self.outputs = [jax.ShapeDtypeStruct(values.shape, values.dtype)]

    def peers(self, zone, side, row, core):
        return {}

    def start(self, copies, local_sems, sources, targets, stages):
        zone, side, row, core = place_here()
        self.away = side != core
        self.copy = copies.make(sources[0], targets[0], device(zone, core, row, side))

    def pump(self, steps):
        pass

    def late(self):
        @pl.when(self.away)
        def _():
            self.copy.start()

    def finish(self):
        @pl.when(self.away)
        def _():
            self.copy.wait_recv()
            self.copy.wait_send()


class PairTree:
    def __init__(self, pairs, pieces):
        self.pairs = [len(pair) for pair in pairs]
        self.sources = [shard for pair in pairs for shard in pair]
        self.pieces = pieces
        self.outputs = [
            jax.ShapeDtypeStruct((8,) + own.shape, own.dtype) for own, *_ in pairs
        ]
        self.count = 6 * sum(pieces) + 2 * len(pairs) + self.pairs.count(1)
        self.count_local = 2 * len(pairs) + 2 * sum(pieces)
        self.scratch = [pltpu.VMEM((2,) + own.shape, own.dtype) for own, *_ in pairs]
        self.scratch += [pltpu.VMEM(p[0].shape, p[0].dtype) for p in pairs if len(p) == 1]
        self.in_hbm = True

    def peers(self, zone, side, row, core):
        return {
            1: device(flipped(zone, 1), side, row, core),
            3: device(flipped(zone, 3), side, row, core),
            "core": device(zone, side, row, 1 - core),
        }

    def start(self, copies, local_sems, sources, targets, stages):
        zone, side, row, core = place_here()
        inner_peer = device(flipped(zone, 3), side, row, core)
        outer_peer = device(flipped(zone, 1), side, row, core)
        core_peer = device(zone, side, row, 1 - core)
        self.inner = inner_zone(zone) == 1
        self.outer = inner_zone(zone) == 0
        self.across, self.onward, self.late, self.place = [], [], [], []
        self.shared, self.kept, self.partners, self.later = [], [], [], []
        sem = 0
        sources, late_stages = list(sources), list(stages[len(targets) :])
        for weight, full in enumerate(targets):
            landing = stages[weight]
            pair = [sources.pop(0) for _ in range(self.pairs[weight])]
            if len(pair) == 1:
                pair.append(late_stages.pop(0))
                self.partners.append(copies.start(pair[0], pair[1], outer_peer))
            size = pair[0].shape[0] // self.pieces[weight]
            for piece in range(self.pieces[weight]):
                rows = pl.ds(piece * size, size)
                for slot in (0, 1):
                    here = landing.at[slot, rows]
                    self.across.append(copies.make(pair[slot].at[rows], here, inner_peer))
                    self.onward.append(copies.make(here, landing.at[1 - slot, rows], outer_peer))
                    self.late.append(copies.make(here, full.at[6 + slot, rows], core_peer))
                    self.place.append(
                        pltpu.make_async_copy(here, full.at[2 + slot, rows], local_sems.at[sem])
                    )
                    sem += 1
            for slot in (0, 1):
                self.shared.append(copies.make(pair[slot], full.at[4 + slot], core_peer))
                self.kept.append(
                    pltpu.make_async_copy(pair[slot], full.at[slot], local_sems.at[sem])
                )
                sem += 1
                if slot >= self.pairs[weight]:
                    self.later += [self.shared[-1], self.kept[-1]]
                else:
                    self.shared[-1].start()
                    self.kept[-1].start()

        @pl.when(self.inner)
        def _():
            for copy in self.across[:AHEAD]:
                copy.start()

    def arrive(self, number):
        self.onward[number].wait_recv()
        swapped = number + 1 - 2 * (number % 2)
        self.late[swapped].start()
        self.place[swapped].start()

    def pump(self, steps):
        steps = [step for step in steps if step < len(self.across)]

        @pl.when(self.inner)
        def _():
            for here in steps:
                self.across[here].wait_recv()
                for copy in self.across[here + AHEAD : here + AHEAD + 1]:
                    copy.start()
                self.onward[here].start()
                self.late[here].start()
                self.place[here].start()

        @pl.when(self.outer)
        def _():
            for step in steps:
                if step > 0:
                    self.arrive(step - 1)

        for copy in self.partners if 1 in steps else []:
            copy.wait_recv()
            copy.wait_send()
        for copy in self.later if 1 in steps else []:
            copy.start()

    def finish(self):
        @pl.when(self.inner)
        def _():
            for copy in self.across + self.onward:
                copy.wait_send()

        @pl.when(self.outer)
        def _():
            self.arrive(len(self.onward) - 1)

        for copy in self.kept + self.place:
            copy.wait()
        for copy in self.shared + self.late:
            copy.wait_send()
        for copy in self.shared + self.late:
            copy.wait_recv()


def sum_eighths(
    copies, row_peer, side_peer, send, keep, forward, first, second, store, begin, pump
):
    size = send.shape[0] // 4
    part = lambda ref, slot: ref.at[pl.ds(slot * size, size)]
    arrivals = [
        copies.start(part(send, 1), part(first, 1), row_peer),
        copies.start(part(send, 3), part(first, 3), side_peer),
        copies.start(part(send, 0), part(first, 0), row_peer),
        copies.start(part(send, 2), part(first, 2), side_peer),
    ]
    begin()
    passed = []
    for number, slot, peer in ((0, 1, side_peer), (1, 3, row_peer)):
        arrivals[number].wait_recv()

        def add(row, count, number=number, slot=slot):
            here = pl.ds(slot * size + row, count)
            both = keep[here, :].astype(jnp.float32) + first[here, :].astype(jnp.float32)
            forward[pl.ds(number * size + row, count), :] = both.astype(jnp.bfloat16)

        for_rows(size, add)
        passed.append(copies.start(part(forward, number), part(second, number), peer))
    pump([0])
    for number, slot in ((0, 0), (1, 2)):
        arrivals[2 + number].wait_recv()
        passed[number].wait_recv()

        def total(row, count, number=number, slot=slot):
            here = pl.ds(slot * size + row, count)
            sums = keep[here, :].astype(jnp.float32) + first[here, :].astype(jnp.float32)
            sums = sums + second[pl.ds(number * size + row, count), :].astype(jnp.float32)
            store(number, row, count, sums)

        for_rows(size, total)
        yield number
    for copy in arrivals + passed:
        copy.wait_send()


def halves(terms):
    rows = terms.shape[0] // 2
    return terms.at[pl.ds(0, rows)], terms.at[pl.ds(rows, rows)]


def split_refs(refs, jobs, extra_count, out_count):
    refs = list(refs)
    take = lambda count: [refs.pop(0) for _ in range(count)]
    extras = take(extra_count)
    sources = [take(len(job.sources)) for job in jobs]
    full = take(1)[0]
    outs = take(out_count)
    targets = [take(len(job.outputs)) for job in jobs]
    return extras, sources, full, outs, targets, refs


def spread_kernel(middle, jobs, extra_count, out_count, gain_sum, plan, terms, *refs):
    keep, send = halves(terms)
    extras, sources, full, outs, targets, scratch = split_refs(refs, jobs, extra_count, out_count)
    forward, first, second, send_sems, recv_sems, local_sems, *stages = scratch
    zone, side, row, core = place_here()
    row_peer, side_peer = device(zone, side, 1 - row, core), device(zone, 1 - side, row, core)
    copies = Copies(send_sems, recv_sems)
    size = send.shape[0] // 4
    part = lambda slot: full.at[pl.ds(slot * size, size)]
    for out in outs:
        if out.shape[0] == 1:
            out[...] = jnp.zeros_like(out)
    peers = {}
    for job in jobs:
        peers.update(job.peers(zone, side, row, core))
    greet([row_peer, side_peer] + list(peers.values()))

    def begin():
        spot = 0
        for job, source, target in zip(jobs, sources, targets):
            own_stages = stages[spot : spot + len(job.scratch)]
            job.start(copies, local_sems, source, target, own_stages)
            spot += len(job.scratch)

    def pump(steps):
        for job in jobs:
            job.pump(steps)

    def store(number, row, count, sums):
        own = pl.ds(number * size + row, count)
        full[pl.ds(2 * number * size + row, count), :] = middle(own, sums, extras, outs)

    firsts, seconds = [], []
    for number in sum_eighths(
        copies, row_peer, side_peer, send, keep, forward, first, second, store, begin, pump
    ):
        near, other = (side_peer, row_peer) if number == 0 else (row_peer, side_peer)
        slot = 2 * number
        firsts.append(copies.start(part(slot), part(slot + 1), near))
        seconds.append(copies.start(part(slot), part(4 + slot), other))
    pump([1])
    firsts[0].wait_recv()
    seconds.append(copies.start(part(1), part(5), row_peer))
    firsts[1].wait_recv()
    seconds.append(copies.start(part(3), part(7), side_peer))
    pump(range(2, 64))
    for copy in seconds:
        copy.wait_recv()
    for copy in firsts + seconds:
        copy.wait_send()
    for job in jobs:
        job.finish()


def home_kernel(middle, jobs, extra_count, out_count, gain_sum, plan, terms, *refs):
    keep, send = halves(terms)
    extras, sources, result, outs, targets, scratch = split_refs(refs, jobs, extra_count, out_count)
    forward, first, second, own, full, send_sems, recv_sems, local_sems, *rest = scratch
    gain_scratch, stages = (rest[:2], rest[2:]) if gain_sum is not None else ([], rest)
    block = extras[3]
    zone, side, row, core = place_here()
    row_peer, side_peer = device(zone, side, 1 - row, core), device(zone, 1 - side, row, core)
    core_peer, other_peer = device(zone, side, row, 1 - core), device(zone, 1 - side, row, 1 - core)
    copies = Copies(send_sems, recv_sems)
    size = send.shape[0] // 4
    at_home = side == core
    away = side != core
    for out in outs:
        if out.shape[0] == 1:
            out[...] = jnp.zeros_like(out)
    peers = {}
    for job in jobs:
        peers.update(job.peers(zone, side, row, core))
    plane = [row_peer, side_peer, core_peer, other_peer]
    if gain_sum is not None:
        plane = gain_sum.plane_peers(zone, side, row, core)
        peers.update(gain_sum.zone_peers(zone, side, row, core))
    greet(plane + list(peers.values()))

    def begin():
        spot = 0
        for job, source, target in zip(jobs, sources, targets):
            own_stages = stages[spot : spot + len(job.scratch)]
            job.start(copies, local_sems, source, target, own_stages)
            spot += len(job.scratch)

    def pump(steps):
        if 0 in steps:

            @pl.when(away)
            def _():
                for copy in block_side:
                    copy.start()

        for job in jobs:
            job.pump(steps)

    def store(number, start, count, sums):
        here = pl.ds(number * size + start, count)
        values = middle(here, sums, extras, outs)
        own[here, :] = values
        eighth = row * 2 + side if number == 0 else 4 + side * 2 + row

        @pl.when(at_home)
        def _():
            full[pl.ds(pl.multiple_of(eighth * size + start, 32), count), :] = values

    def piece(number, x, y):
        start = (x * 2 + y) * size if number == 0 else (4 + y * 2 + x) * size
        return full.at[pl.ds(pl.multiple_of(start, size), size)]

    both = (0, 1)
    part = lambda ref, number: ref.at[pl.ds(number * size, size)]
    block_over = [copies.make(part(block, k), piece(k, row, side), core_peer) for k in both]
    block_side = [copies.make(part(block, k), piece(k, row, side), other_peer) for k in both]
    to_side = [copies.make(part(own, k), piece(k, row, side), side_peer) for k in both]
    to_row = [copies.make(piece(k, row, side), piece(k, row, side), row_peer) for k in both]
    pass_row = [
        copies.make(piece(k, row, 1 - side), piece(k, row, 1 - side), row_peer) for k in both
    ]

    @pl.when(at_home)
    def _():
        for copy in block_over:
            copy.start()

    for _ in sum_eighths(
        copies, row_peer, side_peer, send, keep, forward, first, second, store, begin, pump
    ):
        pass
    pump([1])
    if gain_sum is not None:
        gain_sum.start(copies, extras[-1], outs[0], *gain_scratch)

    @pl.when(away)
    def _():
        for copy in to_side:
            copy.start()
        for copy in block_over:
            copy.wait_recv()

    for copy in to_row:
        copy.start()
    for job in jobs:
        if isinstance(job, TurnLate):
            job.late()
    if gain_sum is not None:
        gain_sum.middle()

    @pl.when(at_home)
    def _():
        for copy in to_side:
            copy.wait_recv()
        for copy in block_over:
            copy.wait_send()

    @pl.when(away)
    def _():
        for copy in block_side:
            copy.wait_recv()
        for copy in to_side + block_side:
            copy.wait_send()

    for copy in pass_row:
        copy.start()
    for copy in to_row + pass_row:
        copy.wait_recv()
        copy.wait_send()
    natural, local = block_columns(plan, full.shape[1], side)

    def some(start, count):
        here = pl.ds(start, count)
        for a, b in zip(natural, local):
            result[here, a] = full[here, b]

    for_rows(full.shape[0], some)
    if gain_sum is not None:
        gain_sum.finish(outs[-1])
    for job in jobs:
        job.finish()


def sum_rows(plan, kernel, middle, terms, extras, outs, number, jobs=(), gain_sum=None):
    half, width = terms.shape[0] // 2, terms.shape[1]
    eighth = half // 4
    low = jnp.bfloat16
    vmem, hbm = pl.BlockSpec(memory_space=pltpu.VMEM), pl.BlockSpec(memory_space=pl.ANY)
    scratch = [
        pltpu.VMEM((2 * eighth, width), low),
        pltpu.VMEM((half, width), low),
        pltpu.VMEM((2 * eighth, width), low),
    ]
    if kernel is home_kernel:
        scratch.append(pltpu.VMEM((2 * eighth, width), low))
        scratch.append(pltpu.VMEM((2 * half, width), low))
    copies = (12 if kernel is spread_kernel else 16) + sum(job.count for job in jobs)
    local = max([2] + [job.count_local for job in jobs])
    if gain_sum is not None:
        copies += gain_sum.count
        outs = outs + [gain_sum.output]
    scratch += [pltpu.SemaphoreType.DMA((count,)) for count in (copies, copies, local)]
    if gain_sum is not None:
        scratch += gain_sum.scratch
    scratch += [stage for job in jobs for stage in job.scratch]
    sources = [source for job in jobs for source in job.sources]
    targets = [target for job in jobs for target in job.outputs]
    return pl.pallas_call(
        functools.partial(kernel, middle, jobs, len(extras), len(outs), gain_sum, plan),
        out_shape=[jax.ShapeDtypeStruct((2 * half, width), low)] + outs + targets,
        in_specs=[vmem] * (1 + len(extras) + len(sources)),
        out_specs=[vmem] * (1 + len(outs))
        + [hbm if job.in_hbm else vmem for job in jobs for _ in job.outputs],
        scratch_shapes=scratch,
        compiler_params=pltpu.CompilerParams(
            collective_id=number, has_side_effects=True, vmem_limit_bytes=56 * 2**20
        ),
        cost_estimate=pl.CostEstimate(flops=10**6, bytes_accessed=10**5, transcendentals=0),
        name=middle.__name__,
    )(terms, *extras, *sources)


def block_columns(plan, width, of_core=None):
    if not plan.ordered:
        return [pl.ds(0, width)], [pl.ds(0, width)]
    zone, _, _, core = place_here()
    core = core if of_core is None else of_core
    size, zones = width // plan.total, plan.zones
    owners = [
        flipped(zone, plan.flips[slot % zones]) * 2 + (core if slot < zones else 1 - core)
        for slot in range(plan.total)
    ]
    natural = [pl.ds(pl.multiple_of(owner * size, size), size) for owner in owners]
    return natural, [pl.ds(slot * size, size) for slot in range(plan.total)]


def copy_rows(source, target):
    def some(row, count):
        target[pl.ds(row, count), :] = source[pl.ds(row, count), :]

    if source.shape[0] % 32:
        target[...] = source[...]
    else:
        for_rows(source.shape[0], some)


def cast_rows(source, target):
    def some(row, count):
        here = pl.ds(row, count)
        target[here, :] = source[here, :].astype(target.dtype)

    for_rows(source.shape[0], some)


def opening_kernel(plan, wide_qkv, gains, wide_gate, wide_out, wide_down, tokens, angles, *refs):
    qkv_full, gains_full, turned_gate, turned_out, turned_down, turned_tokens, turned_angles = refs[:7]
    partner_gate, send_sems, recv_sems, tokens_stage, qkv, gate, out, down = refs[7:]
    cast_rows(wide_qkv, qkv)
    zone, side, row, core = place_here()
    partner = device(zone, core, row, side)
    row_peer, core_peer = device(zone, side, 1 - row, core), device(zone, side, row, 1 - core)
    zone_peers = [device(flipped(zone, flip), side, row, core) for flip in plan.flips[1:]]
    at_home, away = side == core, side != core
    always = [row_peer, core_peer] + zone_peers

    @pl.when(at_home)
    def _():
        greet(always)

    @pl.when(away)
    def _():
        greet(always + [partner])

    copies = Copies(send_sems, recv_sems)
    zones = plan.zones
    own = (gains, qkv, angles, gate, out, down)
    ends = (gains_full.at[0], qkv_full.at[0], turned_angles, turned_gate, turned_out, turned_down)
    units = wide_gate.shape[2]

    def cast_rest():
        for half in (0, 1):
            cast_rows(wide_gate.at[half], gate.at[:, pl.ds(half * units, units)])
        cast_rows(wide_out, out)
        cast_rows(wide_down, down)

    turn = [copies.make(source, target, partner) for source, target in zip(own, ends)]
    pieces = 2
    size = tokens.shape[0] // (2 * pieces)
    spots = [
        pl.ds(pl.multiple_of((row * pieces + piece) * size, size), size) for piece in range(pieces)
    ]
    turn_rows = [copies.make(tokens.at[s], tokens_stage.at[s], partner) for s in spots]
    pass_rows = [copies.make(tokens_stage.at[s], tokens_stage.at[s], row_peer) for s in spots]
    natural, local = block_columns(plan, tokens.shape[1])

    def lay_down(all_tokens):
        def some(start, count):
            here = pl.ds(start, count)
            for a, b in zip(natural, local):
                turned_tokens[here, b] = all_tokens[here, a]

        for_rows(all_tokens.shape[0], some)

    slots = list(range(1, zones))
    weights = ((gains, gains_full), (qkv, qkv_full))
    from_own = [
        [copies.make(source, full.at[slot], zone_peers[slot - 1]) for slot in slots]
        + [copies.make(source, full.at[zones], core_peer)]
        for source, full in weights
    ] + [[copies.make(gate, partner_gate, zone_peers[0])]]
    copies.number -= 2 * zones + 1
    from_turned = [
        [copies.make(full.at[0], full.at[slot], zone_peers[slot - 1]) for slot in slots]
        + [copies.make(full.at[0], full.at[zones], core_peer)]
        for _, full in weights
    ] + [[copies.make(turned_gate, partner_gate, zone_peers[0])]]
    cross = [
        [copies.make(full.at[slot], full.at[zones + slot], core_peer) for slot in slots]
        for _, full in weights
    ]

    def cross_over(k):
        for which in (0, 1):
            from_turned[which][k].wait_recv()
            cross[which][k].start()

    @pl.when(away)
    def _():
        for copy in turn[:3]:
            copy.start()
        cast_rest()
        for which in (0, 1):
            turn[which].wait_recv()
            for copy in from_turned[which]:
                copy.start()
        turn[3].start()
        turn_rows[0].start()
        turn[3].wait_recv()
        from_turned[2][0].start()
        turn_rows[1].start()
        cross_over(0)
        turn_rows[0].wait_recv()
        pass_rows[0].start()
        for copy in turn[4:]:
            copy.start()
        turn_rows[1].wait_recv()
        pass_rows[1].start()

    @pl.when(at_home)
    def _():
        for copy in from_own[0] + from_own[1]:
            copy.start()
        cast_rest()
        for copy in from_own[2]:
            copy.start()
        for source, target in zip(own, ends):
            copy_rows(source, target)
        lay_down(tokens)
        cross_over(0)

    for k in range(1, zones - 1):
        cross_over(k)
    for which in (0, 1):
        from_turned[which][zones - 1].wait_recv()
        for copy in from_turned[which]:
            copy.wait_send()
        for copy in cross[which]:
            copy.wait_recv()
            copy.wait_send()
    from_turned[2][0].wait_recv()
    from_turned[2][0].wait_send()

    @pl.when(away)
    def _():
        for copy in pass_rows + turn[2:3] + turn[4:]:
            copy.wait_recv()
        lay_down(tokens_stage)
        for copy in turn + turn_rows + pass_rows:
            copy.wait_send()


def opening(plan, qkv, gains, gate, out, down, tokens, angles, number):
    low = jnp.bfloat16
    vmem = pl.BlockSpec(memory_space=pltpu.VMEM)
    like = lambda v: jax.ShapeDtypeStruct(v.shape, v.dtype)
    whole = lambda v: jax.ShapeDtypeStruct((2 * plan.zones,) + v.shape, low)
    operands = (qkv, gains, gate, out, down, tokens, angles)
    low_gate = jax.ShapeDtypeStruct((gate.shape[1], 2 * gate.shape[2]), low)
    low_out = jax.ShapeDtypeStruct(out.shape, low)
    low_down = jax.ShapeDtypeStruct(down.shape, low)
    outputs = [whole(qkv), whole(gains), low_gate, low_out, low_down, like(tokens), like(angles)]
    outputs += [low_gate]
    copies = 6 + 4 + 2 * plan.zones + 1 + 2 * (plan.zones - 1)
    return pl.pallas_call(
        functools.partial(opening_kernel, plan),
        out_shape=outputs,
        in_specs=[vmem] * len(operands),
        out_specs=[vmem] * len(outputs),
        scratch_shapes=[
            pltpu.SemaphoreType.DMA((copies,)),
            pltpu.SemaphoreType.DMA((copies,)),
            pltpu.VMEM(tokens.shape, tokens.dtype),
            pltpu.VMEM(qkv.shape, low),
            pltpu.VMEM(low_gate.shape, low),
            pltpu.VMEM(out.shape, low),
            pltpu.VMEM(down.shape, low),
        ],
        compiler_params=pltpu.CompilerParams(
            collective_id=number, has_side_effects=True, vmem_limit_bytes=56 * 2**20
        ),
        cost_estimate=pl.CostEstimate(flops=10**6, bytes_accessed=10**5, transcendentals=0),
        name="opening",
    )(*operands)


def inverse_rms(values):
    return lax.rsqrt(jnp.mean(values * values, -1, keepdims=True) + EPS_NORM)


def hidden_rows(own, sums, extras, outs):
    tokens, gain = extras
    hidden = tokens[own, :].astype(jnp.float32) + sums
    outs[0][own, :] = hidden
    return (hidden * inverse_rms(hidden) * gain[...]).astype(jnp.bfloat16)


def grad_hidden_rows(own, sums, extras, outs):
    hidden, out_grad, gain = extras
    values = hidden[own, :]
    factor = inverse_rms(values)
    unit = values * factor
    outs[1][...] += jnp.sum(sums * unit, 0, keepdims=True)
    grad = out_grad[own, :].astype(jnp.float32) + norm_back(sums * gain[...], unit, factor)
    outs[0][own, :] = grad
    return grad.astype(jnp.bfloat16)


def grad_input_rows(own, sums, extras, outs):
    tokens, grad_hidden, gain = extras[:3]
    values = tokens[own, :].astype(jnp.float32)
    factor = inverse_rms(values)
    unit = values * factor
    outs[0][...] += jnp.sum(sums * unit, 0, keepdims=True)
    return (grad_hidden[own, :] + norm_back(sums * gain[...], unit, factor)).astype(jnp.bfloat16)


def dot(left, right, left_dim=1, right_dim=0):
    return lax.dot_general(
        left, right, (((left_dim,), (right_dim,)), ((), ())), preferred_element_type=jnp.float32
    )


def turn_head(values, cosine, signed_sine):
    return values * cosine + pltpu.roll(values, HEAD // 2, 1) * signed_sine


def turn_back(gradient, cosine, signed_sine):
    return gradient * cosine + pltpu.roll(gradient * signed_sine, HEAD // 2, 1)


def softmax_block(query, key, first_row):
    rows, keys = query.shape[0], key.shape[0]
    scores = dot(query, key, 1, 1)
    row_at = lax.broadcasted_iota(jnp.int32, (rows, keys), 0) + first_row
    key_at = lax.broadcasted_iota(jnp.int32, (rows, keys), 1)
    scores = jnp.where(key_at <= row_at, scores, -1000000000.0)
    exponent = jnp.exp(scores - jnp.max(scores, -1, keepdims=True))
    return exponent / jnp.sum(exponent, -1, keepdims=True)


def eighth_owners():
    _, side, row, _ = place_here()
    own, off = (row, side), (1 - row, 1 - side)
    first = lambda x, y: x * 2 + y
    second = lambda x, y: 4 + y * 2 + x
    return [
        first(own[0], own[1]),
        first(own[0], off[1]),
        second(own[0], own[1]),
        second(off[0], own[1]),
        first(off[0], own[1]),
        first(off[0], off[1]),
        second(own[0], off[1]),
        second(off[0], off[1]),
    ]


def reorder_rows(source, target, into_local):
    size = source.shape[0] // 8
    for slot, owner in enumerate(eighth_owners()):
        natural = pl.ds(pl.multiple_of(owner * size, size), size)
        local = pl.ds(slot * size, size)
        if into_local:
            target[local, :] = source[natural, :]
        else:
            target[natural, :] = source[local, :]


def forward_kernel(
    tokens, weights, gain_in, gain_q, gain_k, cosine, sine,
    normed, raw, query, key, value, local, attended,
):
    low = jnp.bfloat16
    total, heads = tokens.shape[0], query.shape[1] // HEAD
    block, wide = 256, 512

    def project(step, carry):
        rows = pl.ds(pl.multiple_of(step * wide, wide), wide)
        values = tokens[rows, :].astype(jnp.float32)
        normed[rows, :] = (values * inverse_rms(values) * gain_in[...]).astype(low)
        raw[rows, :] = dot(normed[rows, :], weights[...])
        turns = (cosine[rows, :], sine[rows, :])
        for head in range(heads):
            column = (head // 2) * 4 * HEAD + (head % 2) * HEAD
            values = raw[rows, pl.ds(column, HEAD)]
            values = turn_head(values * inverse_rms(values) * gain_q[...], *turns)
            query[rows, pl.ds(head * HEAD, HEAD)] = (values * (1.0 / math.sqrt(HEAD))).astype(low)
        for group in range(heads // 2):
            column = group * 4 * HEAD + 2 * HEAD
            here = pl.ds(group * HEAD, HEAD)
            values = raw[rows, pl.ds(column, HEAD)]
            values = turn_head(values * inverse_rms(values) * gain_k[...], *turns)
            key[rows, here] = values.astype(low)
            value[rows, here] = raw[rows, pl.ds(column + HEAD, HEAD)].astype(low)
        return carry

    lax.fori_loop(0, total // wide, project, 0)

    def attend(head, carry):
        mine = pl.ds(pl.multiple_of(head * HEAD, HEAD), HEAD)
        shared = pl.ds(pl.multiple_of(lax.div(head, 2) * HEAD, HEAD), HEAD)
        for start in range(0, total, SEQ):
            for first in range(0, SEQ, block):
                rows, keys = pl.ds(start + first, block), pl.ds(start, first + block)
                probs = softmax_block(query[rows, mine], key[keys, shared], first)
                attended[rows, mine] = dot(probs.astype(low), value[keys, shared]).astype(low)
        return carry

    lax.fori_loop(0, heads, attend, 0)
    reorder_rows(attended, local, True)


def attention(tokens, weights, gain_in, gain_q, gain_k, cosine, sine):
    total = tokens.shape[0]
    columns = weights.shape[1]
    low = jnp.bfloat16
    shape = lambda width, kind=low: jax.ShapeDtypeStruct((total, width), kind)
    vmem = pl.BlockSpec(memory_space=pltpu.VMEM)
    return pl.pallas_call(
        forward_kernel,
        out_shape=[
            shape(tokens.shape[1]),
            shape(columns, jnp.float32),
            shape(columns // 2),
            shape(columns // 4),
            shape(columns // 4),
            shape(columns // 2),
        ],
        in_specs=[vmem] * 7,
        out_specs=[vmem] * 6,
        scratch_shapes=[pltpu.VMEM((total, columns // 2), low)],
        compiler_params=pltpu.CompilerParams(vmem_limit_bytes=48 * 2**20),
        cost_estimate=pl.CostEstimate(flops=10**6, bytes_accessed=10**5, transcendentals=0),
        name="attention",
    )(tokens, weights, gain_in, gain_q, gain_k, cosine, sine)


def backward_kernel(
    query, key, value, raw, grad_rows, gain_q, gain_k, cosine, sine,
    mixed, mixed_local, query_gain, key_gain, grad, key_sum, value_sum,
):
    low = jnp.bfloat16
    total, heads = query.shape[0], query.shape[1] // HEAD
    block = 256
    reorder_rows(grad_rows, grad, False)
    query_gain[...] = jnp.zeros_like(query_gain)
    key_gain[...] = jnp.zeros_like(key_gain)

    def head_norm_back(rows, column, gradient, gain, gain_grad):
        values = raw[rows, column]
        factor = inverse_rms(values)
        unit = values * factor
        turned = turn_back(gradient, cosine[rows, :], sine[rows, :])
        gain_grad[...] += jnp.sum(turned * unit, 0, keepdims=True)
        mixed[rows, column] = norm_back(turned * gain[...], unit, factor).astype(low)

    def one_group(group, carry):
        at = lambda offset: pl.ds(pl.multiple_of(group * 4 * HEAD + offset * HEAD, HEAD), HEAD)
        shared = pl.ds(pl.multiple_of(group * HEAD, HEAD), HEAD)
        key_sum[...] = jnp.zeros_like(key_sum)
        value_sum[...] = jnp.zeros_like(value_sum)
        for head in (0, 1):
            mine = pl.ds(pl.multiple_of((group * 2 + head) * HEAD, HEAD), HEAD)
            for start in range(0, total, SEQ):
                for first in range(0, SEQ, block):
                    rows, keys = pl.ds(start + first, block), pl.ds(start, first + block)
                    query_part, grad_part = query[rows, mine], grad[rows, mine]
                    probs = softmax_block(query_part, key[keys, shared], first)
                    weighed = probs * dot(grad_part, value[keys, shared], 1, 1)
                    scores = weighed - probs * jnp.sum(weighed, -1, keepdims=True)
                    scores = scores.astype(low)
                    grad_query = dot(scores, key[keys, shared]) * (1.0 / math.sqrt(HEAD))
                    head_norm_back(rows, at(head), grad_query, gain_q, query_gain)
                    key_sum[keys, :] += dot(scores, query_part, 0, 0)
                    value_sum[keys, :] += dot(probs.astype(low), grad_part, 0, 0)
        for first in range(0, total, block):
            rows = pl.ds(first, block)
            head_norm_back(rows, at(2), key_sum[rows, :], gain_k, key_gain)
            mixed[rows, at(3)] = value_sum[rows, :].astype(low)
        return carry

    lax.fori_loop(0, heads // 2, one_group, 0)
    reorder_rows(mixed, mixed_local, True)


def attention_back(query, key, value, raw, grad_rows, gain_q, gain_k, cosine, sine):
    total, columns = raw.shape
    low = jnp.bfloat16
    vmem = pl.BlockSpec(memory_space=pltpu.VMEM)
    return pl.pallas_call(
        backward_kernel,
        out_shape=[
            jax.ShapeDtypeStruct((total, columns), low),
            jax.ShapeDtypeStruct((total, columns), low),
            jax.ShapeDtypeStruct((1, HEAD), jnp.float32),
            jax.ShapeDtypeStruct((1, HEAD), jnp.float32),
        ],
        in_specs=[vmem] * 9,
        out_specs=[vmem] * 4,
        scratch_shapes=[
            pltpu.VMEM(grad_rows.shape, low),
            pltpu.VMEM((total, HEAD), jnp.float32),
            pltpu.VMEM((total, HEAD), jnp.float32),
        ],
        compiler_params=pltpu.CompilerParams(vmem_limit_bytes=48 * 2**20),
        cost_estimate=pl.CostEstimate(flops=10**6, bytes_accessed=10**5, transcendentals=0),
        name="attention_back",
    )(query, key, value, raw, grad_rows, gain_q, gain_k, cosine, sine)


def feed_kernel(plan, rows, own_grad, got_grad, gate_up, up_part, down, active, grads, out_grad):
    low = jnp.bfloat16
    block = 512
    tile = down.shape[1]
    step = pl.program_id(0)
    gate_at = pl.ds(pl.multiple_of(step * tile, tile), tile)
    up_at = pl.ds(pl.multiple_of(grads.shape[1] // 2 + step * tile, tile), tile)
    _, side, _, core = place_here()

    def lay_down(source):
        natural, blocks = block_columns(plan, source.shape[1])
        eighth = source.shape[0] // 8
        for slot, owner in enumerate(eighth_owners()):

            def some(start, count, slot=slot, owner=owner):
                here = pl.ds(pl.multiple_of(owner * eighth + start, 32), count)
                there = pl.ds(slot * eighth + start, count)
                for a, b in zip(natural, blocks):
                    out_grad[there, b] = source[here, a]

            for_rows(eighth, some)

    @pl.when((step == 0) & (side == core))
    def _():
        lay_down(own_grad)

    @pl.when((step == 0) & (side != core))
    def _():
        lay_down(got_grad)

    def one(block_at, carry):
        here = pl.ds(pl.multiple_of(block_at * block, block), block)
        gate = dot(rows[here, :], gate_up[...])
        up = dot(rows[here, :], up_part[...])
        grad = dot(out_grad[here, :], down[...])
        sigmoid = jax.nn.sigmoid(gate)
        silu = gate * sigmoid
        active[here, :] = (silu * up).astype(low)
        grads[here, gate_at] = (grad * up * sigmoid * (1.0 + gate * (1.0 - sigmoid))).astype(low)
        grads[here, up_at] = (grad * silu).astype(low)
        return carry

    lax.fori_loop(0, rows.shape[0] // block, one, 0)


def feed_forward(plan, rows, own_grad, got_grad, gate_up, down, tile):
    total, width = rows.shape
    units = down.shape[1]
    low = jnp.bfloat16
    tiles = units // tile
    whole = pl.BlockSpec(memory_space=pltpu.VMEM)
    return pl.pallas_call(
        functools.partial(feed_kernel, plan),
        grid=(tiles,),
        out_shape=[
            jax.ShapeDtypeStruct((total, units), low),
            jax.ShapeDtypeStruct((total, 2 * units), low),
            jax.ShapeDtypeStruct((total, width), low),
        ],
        in_specs=[
            whole,
            whole,
            whole,
            pl.BlockSpec((width, tile), lambda step: (0, step)),
            pl.BlockSpec((width, tile), lambda step: (0, step + tiles)),
            pl.BlockSpec((width, tile), lambda step: (0, step)),
        ],
        out_specs=[
            pl.BlockSpec((total, tile), lambda step: (0, step)),
            whole,
            whole,
        ],
        compiler_params=pltpu.CompilerParams(vmem_limit_bytes=56 * 2**20),
        cost_estimate=pl.CostEstimate(
            flops=6 * total * width * units, bytes_accessed=4 * 10**7, transcendentals=total * units
        ),
        name="feed_forward",
    )(rows, own_grad, got_grad, gate_up, gate_up, down)


class Plan:
    def __init__(self, mesh):
        self.total = mesh.shape["dp"]
        self.zones = self.total // 2
        self.tensor = mesh.shape["tensor"]
        self.flips = [k ^ (k >> 1) for k in range(self.zones)]

    def place(self):
        self.index = lax.axis_index("dp")
        self.zone = self.index // 2
        self.side = self.index % 2
        self.row = lax.axis_index("tensor") // 2
        self.core = lax.axis_index("tensor") % 2
        self.home = self.side == self.core

    def move(self, value, target):
        pairs = []
        for d in range(self.total):
            for t in range(self.tensor):
                to = target(d // 2, d % 2, t // 2, t % 2)
                if to is not None:
                    zone, side, row, core = to
                    pairs.append((d * self.tensor + t, (zone * 2 + side) * self.tensor + row * 2 + core))
        return lax.ppermute(value, ("dp", "tensor"), pairs)

    def turn(self, value):
        got = self.move(value, lambda z, y, x, c: (z, c, x, y) if y != c else None)
        return jnp.where(self.home, value, got)

    def zone_flip(self, value, bit):
        return self.move(value, lambda z, y, x, c: (z ^ bit, y, x, c))

    def core_swap(self, value):
        return self.move(value, lambda z, y, x, c: (z, y, x, 1 - c))

    def side_swap(self, value):
        return self.move(value, lambda z, y, x, c: (z, 1 - y, x, c))

    def row_swap(self, value):
        return self.move(value, lambda z, y, x, c: (z, y, 1 - x, c))

    def to_local(self, value, axis):
        width = value.shape[axis] // self.total
        parts = []
        for core in (self.core, 1 - self.core):
            for slot in range(self.zones):
                owner = (self.zone ^ self.flips[slot]) * 2 + core
                parts.append(lax.dynamic_slice_in_dim(value, owner * width, width, axis))
        return jnp.concatenate(parts, axis)

    def to_natural(self, value, axis, core=None):
        core = self.core if core is None else core
        width = value.shape[axis] // self.total
        parts = []
        for block in range(self.total):
            slot = flip = (block // 2) ^ self.zone
            for bits in range(1, self.zones.bit_length()):
                slot = slot ^ (flip >> bits)
            slot = slot + jnp.where(block % 2 == core, 0, self.zones)
            parts.append(lax.dynamic_slice_in_dim(value, slot * width, width, axis))
        return jnp.concatenate(parts, axis)

    def row_owners(self):
        own, off = (self.row, self.side), (1 - self.row, 1 - self.side)
        first = lambda x, y: x * 2 + y
        second = lambda x, y: 4 + y * 2 + x
        return [
            first(own[0], own[1]),
            first(own[0], off[1]),
            second(own[0], own[1]),
            second(off[0], own[1]),
            first(off[0], own[1]),
            first(off[0], off[1]),
            second(own[0], off[1]),
            second(off[0], off[1]),
        ]

    def rows_local(self, value, slots=range(8)):
        size = value.shape[0] // 8
        owners = self.row_owners()
        return jnp.concatenate(
            [lax.dynamic_slice_in_dim(value, owners[slot] * size, size, 0) for slot in slots], 0
        )

    def rows_natural(self, value, order=range(8)):
        size = value.shape[0] // 8
        place = [list(order).index(slot) for slot in range(8)]
        parts = []
        for piece in range(8):
            x, y = (piece // 2, piece % 2) if piece < 4 else (piece % 2, (piece - 4) // 2)
            slots = (0, 1, 4, 5) if piece < 4 else (2, 6, 3, 7)
            same_x, same_y = x == self.row, y == self.side
            slot = jnp.where(
                same_x,
                jnp.where(same_y, place[slots[0]], place[slots[1]]),
                jnp.where(same_y, place[slots[2]], place[slots[3]]),
            )
            parts.append(lax.dynamic_slice_in_dim(value, slot * size, size, 0))
        return jnp.concatenate(parts, 0)

    def from_zones(self, shard):
        return [self.zone_flip(shard, flip) for flip in self.flips[1:]]

    def to_zones(self, parts, slots):
        return [self.zone_flip(parts[slot], self.flips[slot]) for slot in slots]

    def middle_swap(self, pair):
        return self.move(pair, lambda z, y, x, c: (z ^ 3, y, x, c) if z in (1, 2) else None)

    def inward(self, part):
        return self.move(part, lambda z, y, x, c: (z ^ 1, y, x, c) if z in (0, 3) else None)

    def pass_outward(self, pair):
        return self.move(pair, lambda z, y, x, c: (z ^ 1, y, x, c) if z in (1, 2) else None)

    def far_pair(self, middle, passed):
        inner = (self.zone == 1) | (self.zone == 2)
        return jnp.where(inner, middle, passed[::-1])

    def first_swap(self, send):
        half = send.shape[0] // 2
        return self.row_swap(send[:half]), self.side_swap(send[half:])

    def second_swap(self, keep, got):
        quarter = keep.shape[0] // 4
        row_part = keep[: 2 * quarter] + got[0].astype(jnp.float32)
        side_part = keep[2 * quarter :] + got[1].astype(jnp.float32)
        own = jnp.concatenate([row_part[:quarter], side_part[:quarter]], 0)
        return own, (
            self.side_swap(row_part[quarter:].astype(jnp.bfloat16)),
            self.row_swap(side_part[quarter:].astype(jnp.bfloat16)),
        )

    def spread_first(self, own):
        half = own.shape[0] // 2
        return (self.side_swap(own[:half]), self.row_swap(own[half:]))

    def spread_second(self, own, got):
        half = own.shape[0] // 2
        row_part = jnp.concatenate([own[:half], got[0]], 0)
        side_part = jnp.concatenate([own[half:], got[1]], 0)
        return row_part, side_part, self.row_swap(row_part), self.side_swap(side_part)

    def send_home(self, own):
        to_home = lambda z, y, x, c: (z, c, x, c) if y != c else None
        return jnp.concatenate([own, self.move(own, to_home)], 0)

    def row_home(self, part):
        return self.move(part, lambda z, y, x, c: (z, y, 1 - x, c) if y == c else None)

    def share_home(self, part, other):
        full = jnp.concatenate([part, other], 0)
        full = self.to_natural(self.rows_natural(full, (0, 2, 1, 6, 4, 3, 5, 7)), 1)
        got = self.move(full, lambda z, y, x, c: (z, y, x, 1 - c) if y == c else None)
        return full, got

    def turned(self, own, got):
        return jnp.where(self.home, own, got)

    def sum_everywhere(self, value):
        value = value + self.row_swap(value)
        value = value + self.side_swap(value)
        value = value + self.core_swap(value)
        bit = 1
        while bit < self.zones:
            value = value + self.zone_flip(value, bit)
            bit *= 2
        return value


def shards(
    plan,
    tokens,
    positions,
    out_grad,
    qkv_weight,
    qkv_first,
    qkv_second,
    out_weight,
    out_first,
    out_second,
    gate_up,
    gate_up_first,
    gate_up_second,
    down_weight,
    down_first,
    down_second,
    gains,
    gains_first,
    gains_second,
):
    plan.place()
    low = jnp.bfloat16
    tok_rows, model_width = tokens.shape
    groups = qkv_weight.shape[1]
    head_size = qkv_weight.shape[3]
    shard_rows = qkv_weight.shape[0]
    seq_count = tok_rows // SEQ
    mixed_cols = groups * 4 * head_size
    near_cols = model_width // 2
    kept = tok_rows // 2
    gain_count = gains.shape[0]

    tree = plan.zones == 4
    slots = range(1, plan.zones)

    def column_parts(value):
        return value.reshape((plan.zones, -1) + value.shape[1:])

    units = gate_up.shape[2]
    plan.ordered = (model_width // plan.total) % 128 == 0
    gain_rows = 16
    gain_block = jnp.pad(gains.astype(low), (0, gain_rows * 128 - gain_count)).reshape(gain_rows, 128)
    tile = min(units, 256)
    angle_at = positions.astype(jnp.float32).reshape(-1, 128)
    both_qkv, both_gains, turned_gate, turned_out, turned_down, tokens, angle_at, partner_gate = opening(
        plan,
        qkv_weight.reshape(shard_rows, mixed_cols),
        gain_block,
        gate_up,
        out_weight,
        down_weight,
        tokens,
        angle_at,
        3,
    )
    positions = angle_at.reshape(-1)
    turned_out, turned_gate, turned_down, tokens, positions, both_qkv, both_gains, out_grad = fence(
        turned_out, turned_gate, turned_down, tokens, positions, both_qkv, both_gains, out_grad
    )

    got_grad = plan.move(out_grad, lambda z, y, x, c: (z, c, x, y) if y != c else None)
    zone_out = plan.from_zones(turned_out)
    if tree:
        partner_down = plan.zone_flip(turned_down, 1)
    else:
        partner_down = plan.from_zones(turned_down)
        partner_gate = plan.from_zones(turned_gate)
    if not plan.ordered:
        tokens = plan.to_local(tokens, 1)
    cosine, sine_table = rotary(positions, head_size)
    signed_sine = jnp.concatenate(
        [-sine_table[:, : head_size // 2], sine_table[:, head_size // 2 :]], 1
    )
    full_qkv = both_qkv.reshape(model_width, mixed_cols)
    gain_slots = both_gains.reshape(plan.total, -1)[:, :gain_count]
    gain_all = plan.to_natural(gain_slots.reshape(-1), 0).astype(jnp.float32)
    gain_in = plan.to_local(gain_all[:model_width], 0)[None]
    gain_post = plan.to_local(gain_all[model_width : 2 * model_width], 0)[None]
    gain_q = gain_all[2 * model_width : 2 * model_width + head_size][None]
    gain_k = gain_all[2 * model_width + head_size :][None]
    normed, raw, query, key_rot, values_low, attended = attention(
        tokens, full_qkv, gain_in, gain_q, gain_k, cosine, signed_sine
    )
    attended, zone_out, turned_out, turned_down, turned_gate, partner_gate, partner_down = fence(
        attended, zone_out, turned_out, turned_down, turned_gate, partner_gate, partner_down
    )

    near_out = jnp.concatenate([turned_out] + zone_out, 0)
    far_out = plan.core_swap(near_out)
    own_tokens = plan.rows_local(tokens, (0, 2))
    near_out, far_out, own_tokens = fence(near_out, far_out, own_tokens)

    full_out = jnp.concatenate([near_out, far_out], 0)
    branch_terms = contract_cols(attended, full_out).astype(low)
    pairs = [(turned_gate, partner_gate), (turned_down, partner_down)]
    jobs = [PairTree(pairs, (2, 2))] if tree else []
    normed_rows, hidden, *gathered = sum_rows(
        plan,
        spread_kernel,
        hidden_rows,
        branch_terms,
        [own_tokens, gain_post],
        [jax.ShapeDtypeStruct((tok_rows // 4, model_width), jnp.float32)],
        0,
        jobs,
    )
    if not tree:
        near = [jnp.concatenate([own] + rest, 0) for own, rest in pairs]
        gathered = [jnp.concatenate([part, plan.core_swap(part)], 0) for part in near]
    full_gate = gathered[0].reshape(model_width, 2 * units)
    full_down = gathered[1].reshape(model_width, units)
    normed_rows, hidden, full_gate, full_down, got_grad = fence(
        normed_rows, hidden, full_gate, full_down, got_grad
    )

    def zone_parts(near, got):
        both = (near + got.astype(jnp.float32)).astype(low)
        return both.reshape((plan.zones, -1) + both.shape[1:])

    def zone_total(parts, *arrived):
        total = parts[0].astype(jnp.float32)
        for part in sum([list(group) for group in arrived], []):
            total = total + part.astype(jnp.float32)
        return total.astype(low)

    active, grad_both, out_grad = feed_forward(
        plan, normed_rows, out_grad, got_grad, full_gate, full_down, tile
    )
    if not plan.ordered:
        out_grad = plan.to_local(out_grad, 1)
    gate_far = contract_rows(normed_rows[:, near_cols:], grad_both).astype(low)
    gate_far, active, grad_both, out_grad, normed_rows = fence(
        gate_far, active, grad_both, out_grad, normed_rows
    )

    gate_got = plan.core_swap(gate_far)
    down_far = contract_rows(out_grad[:, near_cols:], active).astype(low)
    gate_got, down_far, active, grad_both, normed_rows = fence(
        gate_got, down_far, active, grad_both, normed_rows
    )

    down_got = plan.core_swap(down_far)
    gate_parts = zone_parts(contract_rows(normed_rows[:, :near_cols], grad_both), gate_got)
    down_parts = zone_parts(contract_rows(out_grad[:, :near_cols], active), down_got)
    gate_parts, down_parts, grad_both = fence(gate_parts, down_parts, grad_both)

    if tree:
        gate_ready = plan.inward(gate_parts[3, : shard_rows // 2])
    else:
        gate_ready = gate_parts[0]
    post_terms = contract_cols(grad_both, full_gate).astype(low)
    post_terms, gate_parts, gate_ready, down_parts = fence(
        post_terms, gate_parts, gate_ready, down_parts
    )

    eighth = tok_rows // 8
    own_grad = jnp.concatenate([out_grad[:eighth], out_grad[2 * eighth : 3 * eighth]], 0)
    branch_rows, grad_hidden, post_gain_grad, mlp_terms, gate_sums = sum_rows(
        plan,
        spread_kernel,
        grad_hidden_rows,
        post_terms,
        [hidden, own_grad, gain_post],
        [
            jax.ShapeDtypeStruct((tok_rows // 4, model_width), jnp.float32),
            jax.ShapeDtypeStruct((1, model_width), jnp.float32),
        ],
        1,
        [
            SideDot(active, full_down),
            PairScatter(gate_parts, gate_ready, 2) if tree else ZoneBlocks(plan, gate_parts, slots),
        ],
    )
    branch_rows, grad_hidden, post_gain_grad, gate_sums, mlp_terms, down_parts = fence(
        branch_rows, grad_hidden, post_gain_grad, gate_sums, mlp_terms, down_parts
    )

    mlp_got = plan.first_swap(mlp_terms[kept:])
    if tree:
        down_sums = [plan.inward(down_parts[3]), plan.inward(down_parts[2])]
    else:
        down_sums = plan.to_zones(down_parts, slots)
    grad_att = jnp.dot(branch_rows, full_out, preferred_element_type=jnp.float32).astype(low)
    grad_mixed, mixed_rows, query_gain_grad, key_gain_grad = attention_back(
        query, key_rot, values_low, raw, grad_att, gain_q, gain_k, cosine, signed_sine
    )
    gain_terms = jnp.concatenate(
        [plan.to_natural(post_gain_grad, 1), query_gain_grad, key_gain_grad], 1
    )
    grad_mixed, mixed_rows, gain_terms, normed, branch_rows, mlp_got, down_sums, gate_sums = fence(
        grad_mixed, mixed_rows, gain_terms, normed, branch_rows, mlp_got, down_sums, gate_sums
    )

    def plus(left, right):
        return (left.astype(jnp.float32) + right.astype(jnp.float32)).astype(low)

    if tree:
        down_sums = plan.middle_swap(plus(down_parts[2:], jnp.stack(down_sums)))
        gate_last = [plan.zone_flip(gate_sums[1], 1)]
        gate_own = gate_sums
    else:
        gate_own, gate_last = gate_parts, gate_sums
    mlp_own, mlp_last = plan.second_swap(mlp_terms[:kept].astype(jnp.float32), mlp_got)
    out_far = contract_rows(branch_rows[:, near_cols:], attended).astype(low)
    out_got = plan.core_swap(out_far)
    normed_terms = contract_cols(mixed_rows, full_qkv).astype(low)
    out_parts = zone_parts(contract_rows(branch_rows[:, :near_cols], attended), out_got)
    out_parts, normed_terms, gate_last, down_sums, mlp_own, mlp_last, normed, grad_mixed = fence(
        out_parts, normed_terms, gate_last, down_sums, mlp_own, mlp_last, normed, grad_mixed
    )
    block_own = (hidden + mlp_own + jnp.concatenate(mlp_last, 0).astype(jnp.float32)).astype(low)
    total_gate = zone_total(gate_own, gate_last)
    total_gate = jnp.concatenate([total_gate[:, :units], total_gate[:, units:]], 0)
    if tree:
        down_own = [plus(down_parts[slot], down_sums[slot]) for slot in (0, 1)]
    else:
        down_own = [zone_total(down_parts, down_sums)]

    gain_sum = GainSum(plan, gain_terms.shape[1], model_width) if plan.ordered else None
    mine, input_gain_grad, *rest = sum_rows(
        plan,
        home_kernel,
        grad_input_rows,
        normed_terms,
        [own_tokens, grad_hidden, gain_in, block_own] + ([gain_terms] if plan.ordered else []),
        [jax.ShapeDtypeStruct((1, model_width), jnp.float32)],
        2,
        [
            BlockGrad(plan, normed, grad_mixed),
            ZoneBlocks(plan, out_parts, slots),
            TurnLate(total_gate),
        ],
        gain_sum,
    )
    if plan.ordered:
        summed_gains, total_qkv, out_sent, got_gate = rest
    else:
        total_qkv, out_sent, got_gate = rest
        summed_gains = plan.sum_everywhere(
            jnp.concatenate([plan.to_natural(input_gain_grad, 1), gain_terms], 1)
        )
    mine, summed_gains, total_qkv, out_sent, got_gate, down_own = fence(
        mine, summed_gains, total_qkv, out_sent, got_gate, down_own
    )

    summed_gate = plan.turned(total_gate, got_gate).reshape(gate_up.shape)
    summed_down = plan.turn(down_own[0]).astype(jnp.float32)
    for part in down_own[1:]:
        part = plan.move(part, lambda z, y, x, c: (z ^ 1, c, x, y))
        summed_down = summed_down + part.astype(jnp.float32)
    other = plan.core_swap(mine)
    input_full, block_out = jnp.where(plan.home, mine, other), jnp.where(plan.home, other, mine)
    if not plan.ordered:
        input_full = plan.to_natural(input_full, 1, plan.side)
        block_out = plan.to_natural(block_out, 1, plan.side)
    summed_both = plan.turn(
        jnp.concatenate([total_qkv, zone_total(out_parts, out_sent)], 1)
    ).astype(jnp.float32)
    summed_qkv = summed_both[:, :mixed_cols].reshape(qkv_weight.shape)
    summed_out = summed_both[:, mixed_cols:]
    summed_gate = summed_gate.astype(jnp.float32)
    summed_gains = lax.dynamic_slice_in_dim(summed_gains[0], plan.index * gain_count, gain_count, 0)
    input_rows = input_full.astype(jnp.float32)

    qkv_moment, qkv_square, qkv_updated = adamw(
        qkv_weight, summed_qkv, qkv_first, qkv_second, RATE_QKV, DECAY_RATE
    )
    out_moment, out_square, out_updated = adamw(
        out_weight, summed_out, out_first, out_second, RATE_OUT, DECAY_RATE
    )
    gate_moment, gate_square, gate_updated = adamw(
        gate_up, summed_gate, gate_up_first, gate_up_second, RATE_GATE, DECAY_RATE
    )
    down_moment, down_square, down_updated = adamw(
        down_weight, summed_down, down_first, down_second, RATE_DOWN, DECAY_RATE
    )
    gain_moment, gain_square, gain_updated = adamw(
        gains, summed_gains, gains_first, gains_second, RATE_GAIN, 0.0
    )
    return (
        block_out,
        input_rows,
        qkv_moment,
        qkv_square,
        qkv_updated,
        out_moment,
        out_square,
        out_updated,
        gate_moment,
        gate_square,
        gate_updated,
        down_moment,
        down_square,
        down_updated,
        gain_moment,
        gain_square,
        gain_updated,
    )


def solution(mesh):
    plan = Plan(mesh)
    placed = (
        P("dp", None),
        P("dp"),
        P("dp", None),
        P("dp", "tensor", None, None),
        P("dp", "tensor", None, None),
        P("dp", "tensor", None, None),
        P("dp", "tensor"),
        P("dp", "tensor"),
        P("dp", "tensor"),
        P(None, "dp", "tensor"),
        P(None, "dp", "tensor"),
        P(None, "dp", "tensor"),
        P("dp", "tensor"),
        P("dp", "tensor"),
        P("dp", "tensor"),
        P("dp"),
        P("dp"),
        P("dp"),
    )
    return jax.shard_map(
        functools.partial(shards, plan),
        mesh=mesh,
        in_specs=placed,
        out_specs=(
            P("dp", None),
            P("dp", None),
            P("dp", "tensor", None, None),
            P("dp", "tensor", None, None),
            P("dp", "tensor", None, None),
            P("dp", "tensor"),
            P("dp", "tensor"),
            P("dp", "tensor"),
            P(None, "dp", "tensor"),
            P(None, "dp", "tensor"),
            P(None, "dp", "tensor"),
            P("dp", "tensor"),
            P("dp", "tensor"),
            P("dp", "tensor"),
            P("dp"),
            P("dp"),
            P("dp"),
        ),
        check_vma=False,
    )
```

```python
import functools
import math

import jax
import jax.numpy as jnp
from jax import lax
from jax.experimental import pallas as pl
from jax.experimental.pallas import tpu as pltpu
from jax.sharding import PartitionSpec as P

SEQ = 1024
STEP = 10


EPS_NORM = 1e-06
THETA = 1000000.0
BETA_ONE = 0.9
BETA_TWO = 0.95
ADAM_EPS = 1e-08
DECAY_RATE = 0.1
RATE_QKV = 0.05
RATE_OUT = 0.3
RATE_GATE = 0.05
RATE_DOWN = 0.03
RATE_GAIN = 1.0


def rotary(positions, head_size):
    freq_index = jnp.arange(head_size // 2, dtype=jnp.float32)
    inverse = jnp.exp(freq_index * (-2.0 * math.log(THETA) / head_size))
    angles = positions.astype(jnp.float32)[:, None] * inverse[None, :]
    cosine = jnp.cos(angles)
    sine_table = jnp.sin(angles)
    return (jnp.concatenate([cosine, cosine], -1), jnp.concatenate([sine_table, sine_table], -1))


def rotate(values, cosine, sine_table):
    half_size = values.shape[-1] // 2
    turned = jnp.concatenate([-values[..., half_size:], values[..., :half_size]], -1)
    return values * cosine[:, None, :] + turned * sine_table[:, None, :]


def unrotate(gradient, cosine, sine_table):
    half_size = gradient.shape[-1] // 2
    turned = gradient * sine_table[:, None, :]
    rotated_back = jnp.concatenate([turned[..., half_size:], -turned[..., :half_size]], -1)
    return gradient * cosine[:, None, :] + rotated_back


def norm_back(grad_unit, unit_vals, factor):
    return factor * (grad_unit - unit_vals * jnp.mean(grad_unit * unit_vals, -1, keepdims=True))


def contract_rows(left, right):
    return lax.dot_general(
        left, right, (((0,), (0,)), ((), ())), preferred_element_type=jnp.float32
    )


def contract_cols(left, right):
    return lax.dot_general(
        left, right, (((1,), (1,)), ((), ())), preferred_element_type=jnp.float32
    )


def block_scores(query_part, key_part, first_row, block_rows, last_row):
    scores = jnp.einsum(
        "nqkgd,nskd->nkgqs", query_part, key_part, preferred_element_type=jnp.float32
    )
    causal = (first_row + jnp.arange(block_rows))[:, None] >= jnp.arange(last_row)[None, :]
    return jnp.where(causal, scores, -1000000000.0)


def attention_forward(query, key_rot, values_low, seq_len):
    block_rows = min(512, seq_len)
    outputs = []
    log_sums = []
    for first_row in range(0, seq_len, block_rows):
        last_row = first_row + block_rows
        query_part = query[:, first_row:last_row]
        scores = block_scores(query_part, key_rot[:, :last_row], first_row, block_rows, last_row)
        row_max = jnp.max(scores, -1, keepdims=True)
        exponent = jnp.exp(scores - row_max)
        row_total = jnp.sum(exponent, -1, keepdims=True)
        probs_low = (exponent / row_total).astype(jnp.bfloat16)
        outputs.append(
            jnp.einsum(
                "nkgqs,nskd->nqkgd",
                probs_low,
                values_low[:, :last_row],
                preferred_element_type=jnp.float32,
            )
        )
        log_sums.append(row_max + jnp.log(row_total))
    return (jnp.concatenate(outputs, 1), log_sums)


def attention_backward(query, key_rot, values_low, grad_att, log_sums, seq_len):
    block_rows = min(512, seq_len)
    query_grads = []
    key_grad = jnp.zeros(key_rot.shape, jnp.float32)
    value_grad = jnp.zeros(values_low.shape, jnp.float32)
    for block_index, first_row in enumerate(range(0, seq_len, block_rows)):
        last_row = first_row + block_rows
        query_part = query[:, first_row:last_row]
        grad_part = grad_att[:, first_row:last_row]
        key_part = key_rot[:, :last_row]
        value_part = values_low[:, :last_row]
        scores = block_scores(query_part, key_part, first_row, block_rows, last_row)
        probs = jnp.exp(scores - log_sums[block_index])
        probs_low = probs.astype(jnp.bfloat16)
        grad_probs = jnp.einsum(
            "nqkgd,nskd->nkgqs", grad_part, value_part, preferred_element_type=jnp.float32
        )
        grad_scores = (
            probs * (grad_probs - jnp.sum(probs * grad_probs, -1, keepdims=True))
        ).astype(jnp.bfloat16)
        query_grads.append(
            jnp.einsum(
                "nkgqs,nskd->nqkgd", grad_scores, key_part, preferred_element_type=jnp.float32
            )
        )
        padding = ((0, 0), (0, seq_len - last_row), (0, 0), (0, 0))
        key_grad = key_grad + jnp.pad(
            jnp.einsum(
                "nkgqs,nqkgd->nskd", grad_scores, query_part, preferred_element_type=jnp.float32
            ),
            padding,
        )
        value_grad = value_grad + jnp.pad(
            jnp.einsum(
                "nkgqs,nqkgd->nskd", probs_low, grad_part, preferred_element_type=jnp.float32
            ),
            padding,
        )
    return (jnp.concatenate(query_grads, 1), key_grad, value_grad)


def adamw(weight, gradient, moment, second, step_rate, decay_rate):
    moment = BETA_ONE * moment + (1.0 - BETA_ONE) * gradient
    second = BETA_TWO * second + (1.0 - BETA_TWO) * gradient * gradient
    first_hat = moment / (1.0 - BETA_ONE**STEP)
    second_hat = second / (1.0 - BETA_TWO**STEP)
    weight = weight - step_rate * (
        first_hat / (jnp.sqrt(second_hat) + ADAM_EPS) + decay_rate * weight
    )
    return (moment, second, weight)


def fence(*values):
    return lax.optimization_barrier(values)


MESH = pl.DeviceIdType.MESH
HEAD = 128
AHEAD = 2


def place_here():
    index, place = lax.axis_index("dp"), lax.axis_index("tensor")
    return lax.div(index, 2), lax.rem(index, 2), lax.div(place, 2), lax.rem(place, 2)


def device(zone, side, row, core):
    return (zone * 2 + side, row * 2 + core)


def flipped(zone, flip):
    bit = 1
    while bit <= flip:
        if flip & bit:
            zone = zone + bit - 2 * bit * lax.rem(lax.div(zone, bit), 2)
        bit *= 2
    return zone


def greet(devices, amount=None):
    barrier = pltpu.get_barrier_semaphore()
    for peer in devices:
        pl.semaphore_signal(barrier, inc=1, device_id=peer, device_id_type=MESH)
    pl.semaphore_wait(barrier, len(devices) if amount is None else amount)


def for_rows(count, body):
    step = 32

    def one(block, carry):
        body(pl.multiple_of(block * step, step), step)
        return carry

    lax.fori_loop(0, count // step, one, 0)


class Copies:
    def __init__(self, send_sems, recv_sems):
        self.send_sems, self.recv_sems = send_sems, recv_sems
        self.number = 0

    def make(self, source, target, peer):
        number, self.number = self.number, self.number + 1
        return pltpu.make_async_remote_copy(
            src_ref=source,
            dst_ref=target,
            send_sem=self.send_sems.at[number],
            recv_sem=self.recv_sems.at[number],
            device_id=peer,
            device_id_type=MESH,
        )

    def start(self, source, target, peer):
        copy = self.make(source, target, peer)
        copy.start()
        return copy


class GainSum:
    def __init__(self, plan, rest, width):
        self.plan, self.width = plan, width
        self.total = width + rest
        self.scratch = [
            pltpu.VMEM((8, 1, self.total), jnp.float32),
            pltpu.VMEM((plan.zones, 1, self.total), jnp.float32),
        ]
        self.output = jax.ShapeDtypeStruct((1, self.total), jnp.float32)
        self.count = 7 + plan.zones - 1

    def plane_peers(self, zone, side, row, core):
        steps = [(s, r, c) for s in range(2) for r in range(2) for c in range(2)][1:]
        turn = lambda value, step: 1 - value if step else value
        return [device(zone, turn(side, s), turn(row, r), turn(core, c)) for s, r, c in steps]

    def zone_peers(self, zone, side, row, core):
        return {flip: device(flipped(zone, flip), side, row, core) for flip in self.plan.flips[1:]}

    def start(self, copies, rest, blocks, plane_sums, zone_sums):
        zone, side, row, core = place_here()
        plan = self.plan
        size = self.width // plan.total
        self.copies, self.plane_sums, self.zone_sums, self.zone = copies, plane_sums, zone_sums, zone
        here = side * 4 + row * 2 + core
        plane_sums[here, :, pl.ds(self.width, self.total - self.width)] = rest[...]
        for slot in range(plan.total):
            owner = flipped(zone, plan.flips[slot % plan.zones]) * 2
            owner = owner + (core if slot < plan.zones else 1 - core)
            spot = pl.ds(pl.multiple_of(owner * size, size), size)
            plane_sums[here, :, spot] = blocks[:, pl.ds(slot * size, size)]
        self.plane = [
            copies.start(plane_sums.at[here], plane_sums.at[here], peer)
            for peer in self.plane_peers(zone, side, row, core)
        ]

    def middle(self):
        for copy in self.plane:
            copy.wait_recv()
        total = self.plane_sums[0]
        for place in range(1, 8):
            total = total + self.plane_sums[place]
        self.zone_sums[self.zone] = total
        zone, side, row, core = place_here()
        self.across = [
            self.copies.start(self.zone_sums.at[self.zone], self.zone_sums.at[self.zone], peer)
            for peer in self.zone_peers(zone, side, row, core).values()
        ]

    def finish(self, out):
        for copy in self.across:
            copy.wait_recv()
        total = self.zone_sums[0]
        for place in range(1, self.plan.zones):
            total = total + self.zone_sums[place]
        out[...] = total
        for copy in self.plane + self.across:
            copy.wait_send()


class ZoneBlocks:
    scratch = []

    def __init__(self, plan, source, slots, begin=0):
        self.flips, self.slots, self.sources, self.begin = plan.flips, list(slots), [source], begin
        self.outputs = [
            jax.ShapeDtypeStruct((len(self.slots),) + source.shape[1:], source.dtype)
        ]
        self.count, self.count_local = len(self.slots), 0
        self.in_hbm = False

    def peers(self, zone, side, row, core):
        return {
            self.flips[slot]: device(flipped(zone, self.flips[slot]), side, row, core)
            for slot in self.slots
        }

    def start(self, copies, local_sems, sources, targets, stages):
        zone, side, row, core = place_here()
        self.started = [
            copies.make(
                sources[0].at[slot],
                targets[0].at[number],
                device(flipped(zone, self.flips[slot]), side, row, core),
            )
            for number, slot in enumerate(self.slots)
        ]
        self.waiting = True
        if self.begin == 0:
            self.pump([0])

    def pump(self, steps):
        if self.waiting and self.begin in steps:
            self.waiting = False
            for copy in self.started:
                copy.start()

    def finish(self):
        for copy in self.started:
            copy.wait_send()
        for copy in self.started:
            copy.wait_recv()


def inner_zone(zone):
    return lax.rem(lax.div(zone + 1, 2), 2)


class SideDot:
    count, count_local, scratch, in_hbm = 0, 0, [], False

    def __init__(self, left, right):
        self.sources = [left, right]
        self.outputs = [jax.ShapeDtypeStruct((left.shape[0], right.shape[0]), jnp.bfloat16)]

    def peers(self, zone, side, row, core):
        return {}

    def some(self, first, last):
        left, right = self.refs
        size = 256

        def one(step, carry):
            here = pl.ds(pl.multiple_of(step * size, size), size)
            self.out[:, here] = dot(left[...], right[here, :], 1, 1).astype(jnp.bfloat16)
            return carry

        lax.fori_loop(first, last, one, 0)

    def start(self, copies, local_sems, sources, targets, stages):
        self.refs, self.out = sources, targets[0]
        self.steps = self.out.shape[1] // 256
        self.some(0, self.steps // 2)

    def pump(self, steps):
        if 0 in steps:
            self.some(self.steps // 2, self.steps)

    def finish(self):
        pass


class PairScatter:
    def __init__(self, parts, pieces):
        self.sources, self.pieces = [parts], pieces
        _, rows, columns = parts.shape
        self.size = rows // pieces
        self.outputs = [jax.ShapeDtypeStruct((2, rows, columns), parts.dtype)]
        self.scratch = [pltpu.VMEM((2, rows, columns), parts.dtype)] * 2
        self.count, self.count_local = 4 * pieces, 0
        self.in_hbm = False

    def peers(self, zone, side, row, core):
        return {
            1: device(flipped(zone, 1), side, row, core),
            3: device(flipped(zone, 3), side, row, core),
        }

    def start(self, copies, local_sems, sources, targets, stages):
        zone, side, row, core = place_here()
        self.parts, self.out = sources[0], targets[0]
        self.inward, self.crossed = stages
        inner_peer = device(flipped(zone, 3), side, row, core)
        outer_peer = device(flipped(zone, 1), side, row, core)
        self.inner = inner_zone(zone) == 1
        self.outer = inner_zone(zone) == 0
        self.steps = [
            (slot, pl.ds(piece * self.size, self.size))
            for piece in range(self.pieces)
            for slot in (0, 1)
        ]
        self.to_inner = [
            copies.make(self.parts.at[3 - slot, rows], self.inward.at[slot, rows], outer_peer)
            for slot, rows in self.steps
        ]
        self.across = [
            copies.make(self.inward.at[slot, rows], self.crossed.at[slot, rows], inner_peer)
            for slot, rows in self.steps
        ]

        @pl.when(self.outer)
        def _():
            for copy in self.to_inner[:AHEAD]:
                copy.start()

    def add(self, target, slot, rows, left, right):
        def some(row, count):
            here = pl.ds(rows.start + row, count)
            both = left[here, :].astype(jnp.float32) + right[here, :].astype(jnp.float32)
            target.at[slot][here, :] = both.astype(jnp.bfloat16)

        for_rows(self.size, some)

    def pump(self, steps):
        steps = [step for step in steps if step < len(self.steps)]

        @pl.when(self.inner)
        def _():
            for step in steps:
                slot, rows = self.steps[step]
                self.to_inner[step].wait_recv()
                self.add(self.inward, slot, rows, self.parts.at[2 + slot], self.inward.at[slot])
                self.across[step].start()
                if step >= AHEAD:
                    self.settle(step - AHEAD)

        @pl.when(self.outer)
        def _():
            for step in steps:
                self.to_inner[step].wait_send()
                for copy in self.to_inner[step + AHEAD : step + AHEAD + 1]:
                    copy.start()

    def settle(self, step):
        slot, rows = self.steps[step]
        self.across[step].wait_recv()
        self.add(self.out, slot, rows, self.parts.at[slot], self.crossed.at[slot])

    def finish(self):
        @pl.when(self.inner)
        def _():
            for step in range(len(self.steps) - AHEAD, len(self.steps)):
                self.settle(step)
            for copy in self.across:
                copy.wait_send()

        @pl.when(self.outer)
        def _():
            for slot in (0, 1):

                def some(row, count, slot=slot):
                    here = pl.ds(row, count)
                    self.out.at[slot][here, :] = self.parts.at[slot][here, :]

                for_rows(self.parts.shape[1], some)


class BlockGrad:
    in_hbm = False

    def __init__(self, plan, left, right):
        self.zones, self.flips = plan.zones, plan.flips
        self.sources = [left, right]
        shape = (left.shape[1] // plan.total, right.shape[1])
        low = jnp.bfloat16
        self.outputs = [jax.ShapeDtypeStruct(shape, low)]
        self.scratch = [pltpu.VMEM((plan.zones,) + shape, low)] * 4
        self.count, self.count_local = 2 * plan.zones, 0

    def peers(self, zone, side, row, core):
        return {flip: device(flipped(zone, flip), side, row, core) for flip in self.flips[1:]}

    def product(self, block):
        size = self.out.shape[0]
        return dot(self.left[:, pl.ds(block * size, size)], self.right[...], 0, 0)

    def start(self, copies, local_sems, sources, targets, stages):
        zone, side, row, core = place_here()
        self.left, self.right = sources
        self.out = targets[0]
        self.far, self.got, self.parts, self.arrived = stages
        core_peer = device(zone, side, row, 1 - core)
        self.order = list(range(1, self.zones)) + [0]
        self.over = [
            copies.make(self.far.at[slot], self.got.at[slot], core_peer)
            for slot in range(self.zones)
        ]
        self.along = [
            copies.make(
                self.parts.at[slot],
                self.arrived.at[slot],
                device(flipped(zone, self.flips[slot]), side, row, core),
            )
            for slot in range(1, self.zones)
        ]
        for slot in self.order:
            self.far[slot] = self.product(self.zones + slot).astype(jnp.bfloat16)
            self.over[slot].start()

    def pump(self, steps):
        for slot in self.order if 0 in steps else []:
            near = self.product(slot)
            self.over[slot].wait_recv()
            self.parts[slot] = (near + self.got[slot].astype(jnp.float32)).astype(jnp.bfloat16)
            if slot:
                self.along[slot - 1].start()

    def finish(self):
        total = self.parts[0].astype(jnp.float32)
        for slot in range(1, self.zones):
            self.along[slot - 1].wait_recv()
            total = total + self.arrived[slot].astype(jnp.float32)
        self.out[...] = total.astype(jnp.bfloat16)
        for copy in self.over + self.along:
            copy.wait_send()


class TurnLate:
    count, count_local, scratch, in_hbm = 1, 0, [], False

    def __init__(self, values):
        self.sources = [values]
        self.outputs = [jax.ShapeDtypeStruct(values.shape, values.dtype)]

    def peers(self, zone, side, row, core):
        return {}

    def start(self, copies, local_sems, sources, targets, stages):
        zone, side, row, core = place_here()
        self.away = side != core
        self.copy = copies.make(sources[0], targets[0], device(zone, core, row, side))

    def pump(self, steps):
        pass

    def late(self):
        @pl.when(self.away)
        def _():
            self.copy.start()

    def finish(self):
        @pl.when(self.away)
        def _():
            self.copy.wait_recv()
            self.copy.wait_send()


class PairTree:
    def __init__(self, pairs, pieces):
        self.pairs = [len(pair) for pair in pairs]
        self.sources = [shard for pair in pairs for shard in pair]
        self.pieces = pieces
        self.outputs = [
            jax.ShapeDtypeStruct((8,) + own.shape, own.dtype) for own, *_ in pairs
        ]
        self.count = 6 * sum(pieces) + 2 * len(pairs) + self.pairs.count(1)
        self.count_local = 2 * len(pairs) + 2 * sum(pieces)
        self.scratch = [pltpu.VMEM((2,) + own.shape, own.dtype) for own, *_ in pairs]
        self.scratch += [pltpu.VMEM(p[0].shape, p[0].dtype) for p in pairs if len(p) == 1]
        self.in_hbm = True

    def peers(self, zone, side, row, core):
        return {
            1: device(flipped(zone, 1), side, row, core),
            3: device(flipped(zone, 3), side, row, core),
            "core": device(zone, side, row, 1 - core),
        }

    def start(self, copies, local_sems, sources, targets, stages):
        zone, side, row, core = place_here()
        inner_peer = device(flipped(zone, 3), side, row, core)
        outer_peer = device(flipped(zone, 1), side, row, core)
        core_peer = device(zone, side, row, 1 - core)
        self.inner = inner_zone(zone) == 1
        self.outer = inner_zone(zone) == 0
        self.across, self.onward, self.late, self.place = [], [], [], []
        self.shared, self.kept, self.partners, self.later = [], [], [], []
        sem = 0
        sources, late_stages = list(sources), list(stages[len(targets) :])
        for weight, full in enumerate(targets):
            landing = stages[weight]
            pair = [sources.pop(0) for _ in range(self.pairs[weight])]
            if len(pair) == 1:
                pair.append(late_stages.pop(0))
                self.partners.append(copies.start(pair[0], pair[1], outer_peer))
            size = pair[0].shape[0] // self.pieces[weight]
            for piece in range(self.pieces[weight]):
                rows = pl.ds(piece * size, size)
                for slot in (0, 1):
                    here = landing.at[slot, rows]
                    self.across.append(copies.make(pair[slot].at[rows], here, inner_peer))
                    self.onward.append(copies.make(here, landing.at[1 - slot, rows], outer_peer))
                    self.late.append(copies.make(here, full.at[6 + slot, rows], core_peer))
                    self.place.append(
                        pltpu.make_async_copy(here, full.at[2 + slot, rows], local_sems.at[sem])
                    )
                    sem += 1
            for slot in (0, 1):
                self.shared.append(copies.make(pair[slot], full.at[4 + slot], core_peer))
                self.kept.append(
                    pltpu.make_async_copy(pair[slot], full.at[slot], local_sems.at[sem])
                )
                sem += 1
                if slot >= self.pairs[weight]:
                    self.later += [self.shared[-1], self.kept[-1]]
                else:
                    self.shared[-1].start()
                    self.kept[-1].start()

        @pl.when(self.inner)
        def _():
            for copy in self.across[:AHEAD]:
                copy.start()

    def arrive(self, number):
        self.onward[number].wait_recv()
        swapped = number + 1 - 2 * (number % 2)
        self.late[swapped].start()
        self.place[swapped].start()

    def pump(self, steps):
        steps = [step for step in steps if step < len(self.across)]

        @pl.when(self.inner)
        def _():
            for here in steps:
                self.across[here].wait_recv()
                for copy in self.across[here + AHEAD : here + AHEAD + 1]:
                    copy.start()
                self.onward[here].start()
                self.late[here].start()
                self.place[here].start()

        @pl.when(self.outer)
        def _():
            for step in steps:
                if step > 0:
                    self.arrive(step - 1)

        for copy in self.partners if 1 in steps else []:
            copy.wait_recv()
            copy.wait_send()
        for copy in self.later if 1 in steps else []:
            copy.start()

    def finish(self):
        @pl.when(self.inner)
        def _():
            for copy in self.across + self.onward:
                copy.wait_send()

        @pl.when(self.outer)
        def _():
            self.arrive(len(self.onward) - 1)

        for copy in self.kept + self.place:
            copy.wait()
        for copy in self.shared + self.late:
            copy.wait_send()
        for copy in self.shared + self.late:
            copy.wait_recv()


def sum_eighths(
    copies, row_peer, side_peer, send, keep, forward, first, second, store, begin, pump
):
    size = send.shape[0] // 4
    part = lambda ref, slot: ref.at[pl.ds(slot * size, size)]
    arrivals = [
        copies.start(part(send, 1), part(first, 1), row_peer),
        copies.start(part(send, 3), part(first, 3), side_peer),
        copies.start(part(send, 0), part(first, 0), row_peer),
        copies.start(part(send, 2), part(first, 2), side_peer),
    ]
    begin()
    passed = []
    for number, slot, peer in ((0, 1, side_peer), (1, 3, row_peer)):
        arrivals[number].wait_recv()

        def add(row, count, number=number, slot=slot):
            here = pl.ds(slot * size + row, count)
            both = keep[here, :].astype(jnp.float32) + first[here, :].astype(jnp.float32)
            forward[pl.ds(number * size + row, count), :] = both.astype(jnp.bfloat16)

        for_rows(size, add)
        passed.append(copies.start(part(forward, number), part(second, number), peer))
    pump([0])
    for number, slot in ((0, 0), (1, 2)):
        arrivals[2 + number].wait_recv()
        passed[number].wait_recv()

        def total(row, count, number=number, slot=slot):
            here = pl.ds(slot * size + row, count)
            sums = keep[here, :].astype(jnp.float32) + first[here, :].astype(jnp.float32)
            sums = sums + second[pl.ds(number * size + row, count), :].astype(jnp.float32)
            store(number, row, count, sums)

        for_rows(size, total)
        yield number
    for copy in arrivals + passed:
        copy.wait_send()


def halves(terms):
    rows = terms.shape[0] // 2
    return terms.at[pl.ds(0, rows)], terms.at[pl.ds(rows, rows)]


def split_refs(refs, jobs, extra_count, out_count):
    refs = list(refs)
    take = lambda count: [refs.pop(0) for _ in range(count)]
    extras = take(extra_count)
    sources = [take(len(job.sources)) for job in jobs]
    full = take(1)[0]
    outs = take(out_count)
    targets = [take(len(job.outputs)) for job in jobs]
    return extras, sources, full, outs, targets, refs


def spread_kernel(middle, jobs, extra_count, out_count, gain_sum, plan, terms, *refs):
    keep, send = halves(terms)
    extras, sources, full, outs, targets, scratch = split_refs(refs, jobs, extra_count, out_count)
    forward, first, second, send_sems, recv_sems, local_sems, *stages = scratch
    zone, side, row, core = place_here()
    row_peer, side_peer = device(zone, side, 1 - row, core), device(zone, 1 - side, row, core)
    copies = Copies(send_sems, recv_sems)
    size = send.shape[0] // 4
    part = lambda slot: full.at[pl.ds(slot * size, size)]
    for out in outs:
        if out.shape[0] == 1:
            out[...] = jnp.zeros_like(out)
    peers = {}
    for job in jobs:
        peers.update(job.peers(zone, side, row, core))
    greet([row_peer, side_peer] + list(peers.values()))

    def begin():
        spot = 0
        for job, source, target in zip(jobs, sources, targets):
            own_stages = stages[spot : spot + len(job.scratch)]
            job.start(copies, local_sems, source, target, own_stages)
            spot += len(job.scratch)

    def pump(steps):
        for job in jobs:
            job.pump(steps)

    def store(number, row, count, sums):
        own = pl.ds(number * size + row, count)
        full[pl.ds(2 * number * size + row, count), :] = middle(own, sums, extras, outs)

    firsts, seconds = [], []
    for number in sum_eighths(
        copies, row_peer, side_peer, send, keep, forward, first, second, store, begin, pump
    ):
        near, other = (side_peer, row_peer) if number == 0 else (row_peer, side_peer)
        slot = 2 * number
        firsts.append(copies.start(part(slot), part(slot + 1), near))
        seconds.append(copies.start(part(slot), part(4 + slot), other))
    pump([1])
    firsts[0].wait_recv()
    seconds.append(copies.start(part(1), part(5), row_peer))
    firsts[1].wait_recv()
    seconds.append(copies.start(part(3), part(7), side_peer))
    pump(range(2, 64))
    for copy in seconds:
        copy.wait_recv()
    for copy in firsts + seconds:
        copy.wait_send()
    for job in jobs:
        job.finish()


def home_kernel(middle, jobs, extra_count, out_count, gain_sum, plan, terms, *refs):
    keep, send = halves(terms)
    extras, sources, result, outs, targets, scratch = split_refs(refs, jobs, extra_count, out_count)
    forward, first, second, own, full, send_sems, recv_sems, local_sems, *rest = scratch
    gain_scratch, stages = (rest[:2], rest[2:]) if gain_sum is not None else ([], rest)
    block = extras[3]
    zone, side, row, core = place_here()
    row_peer, side_peer = device(zone, side, 1 - row, core), device(zone, 1 - side, row, core)
    core_peer, other_peer = device(zone, side, row, 1 - core), device(zone, 1 - side, row, 1 - core)
    copies = Copies(send_sems, recv_sems)
    size = send.shape[0] // 4
    at_home = side == core
    away = side != core
    for out in outs:
        if out.shape[0] == 1:
            out[...] = jnp.zeros_like(out)
    peers = {}
    for job in jobs:
        peers.update(job.peers(zone, side, row, core))
    plane = [row_peer, side_peer, core_peer, other_peer]
    if gain_sum is not None:
        plane = gain_sum.plane_peers(zone, side, row, core)
        peers.update(gain_sum.zone_peers(zone, side, row, core))
    greet(plane + list(peers.values()))

    def begin():
        spot = 0
        for job, source, target in zip(jobs, sources, targets):
            own_stages = stages[spot : spot + len(job.scratch)]
            job.start(copies, local_sems, source, target, own_stages)
            spot += len(job.scratch)

    def pump(steps):
        if 0 in steps:

            @pl.when(away)
            def _():
                for copy in block_side:
                    copy.start()

        for job in jobs:
            job.pump(steps)

    def store(number, start, count, sums):
        here = pl.ds(number * size + start, count)
        values = middle(here, sums, extras, outs)
        own[here, :] = values
        eighth = row * 2 + side if number == 0 else 4 + side * 2 + row

        @pl.when(at_home)
        def _():
            full[pl.ds(pl.multiple_of(eighth * size + start, 32), count), :] = values

    def piece(number, x, y):
        start = (x * 2 + y) * size if number == 0 else (4 + y * 2 + x) * size
        return full.at[pl.ds(pl.multiple_of(start, size), size)]

    both = (0, 1)
    part = lambda ref, number: ref.at[pl.ds(number * size, size)]
    block_over = [copies.make(part(block, k), piece(k, row, side), core_peer) for k in both]
    block_side = [copies.make(part(block, k), piece(k, row, side), other_peer) for k in both]
    to_side = [copies.make(part(own, k), piece(k, row, side), side_peer) for k in both]
    to_row = [copies.make(piece(k, row, side), piece(k, row, side), row_peer) for k in both]
    pass_row = [
        copies.make(piece(k, row, 1 - side), piece(k, row, 1 - side), row_peer) for k in both
    ]

    @pl.when(at_home)
    def _():
        for copy in block_over:
            copy.start()

    for _ in sum_eighths(
        copies, row_peer, side_peer, send, keep, forward, first, second, store, begin, pump
    ):
        pass
    pump([1])
    if gain_sum is not None:
        gain_sum.start(copies, extras[-1], outs[0], *gain_scratch)

    @pl.when(away)
    def _():
        for copy in to_side:
            copy.start()
        for copy in block_over:
            copy.wait_recv()

    for copy in to_row:
        copy.start()
    for job in jobs:
        if isinstance(job, TurnLate):
            job.late()
    if gain_sum is not None:
        gain_sum.middle()

    @pl.when(at_home)
    def _():
        for copy in to_side:
            copy.wait_recv()
        for copy in block_over:
            copy.wait_send()

    @pl.when(away)
    def _():
        for copy in block_side:
            copy.wait_recv()
        for copy in to_side + block_side:
            copy.wait_send()

    for copy in pass_row:
        copy.start()
    for copy in to_row + pass_row:
        copy.wait_recv()
        copy.wait_send()
    natural, local = block_columns(plan, full.shape[1], side)

    def some(start, count):
        here = pl.ds(start, count)
        for a, b in zip(natural, local):
            result[here, a] = full[here, b]

    for_rows(full.shape[0], some)
    if gain_sum is not None:
        gain_sum.finish(outs[-1])
    for job in jobs:
        job.finish()


def sum_rows(plan, kernel, middle, terms, extras, outs, number, jobs=(), gain_sum=None):
    half, width = terms.shape[0] // 2, terms.shape[1]
    eighth = half // 4
    low = jnp.bfloat16
    vmem, hbm = pl.BlockSpec(memory_space=pltpu.VMEM), pl.BlockSpec(memory_space=pl.ANY)
    scratch = [
        pltpu.VMEM((2 * eighth, width), low),
        pltpu.VMEM((half, width), low),
        pltpu.VMEM((2 * eighth, width), low),
    ]
    if kernel is home_kernel:
        scratch.append(pltpu.VMEM((2 * eighth, width), low))
        scratch.append(pltpu.VMEM((2 * half, width), low))
    copies = (12 if kernel is spread_kernel else 16) + sum(job.count for job in jobs)
    local = max([2] + [job.count_local for job in jobs])
    if gain_sum is not None:
        copies += gain_sum.count
        outs = outs + [gain_sum.output]
    scratch += [pltpu.SemaphoreType.DMA((count,)) for count in (copies, copies, local)]
    if gain_sum is not None:
        scratch += gain_sum.scratch
    scratch += [stage for job in jobs for stage in job.scratch]
    sources = [source for job in jobs for source in job.sources]
    targets = [target for job in jobs for target in job.outputs]
    return pl.pallas_call(
        functools.partial(kernel, middle, jobs, len(extras), len(outs), gain_sum, plan),
        out_shape=[jax.ShapeDtypeStruct((2 * half, width), low)] + outs + targets,
        in_specs=[vmem] * (1 + len(extras) + len(sources)),
        out_specs=[vmem] * (1 + len(outs))
        + [hbm if job.in_hbm else vmem for job in jobs for _ in job.outputs],
        scratch_shapes=scratch,
        compiler_params=pltpu.CompilerParams(
            collective_id=number, has_side_effects=True, vmem_limit_bytes=56 * 2**20
        ),
        cost_estimate=pl.CostEstimate(flops=10**6, bytes_accessed=10**5, transcendentals=0),
        name=middle.__name__,
    )(terms, *extras, *sources)


def block_columns(plan, width, of_core=None):
    if not plan.ordered:
        return [pl.ds(0, width)], [pl.ds(0, width)]
    zone, _, _, core = place_here()
    core = core if of_core is None else of_core
    size, zones = width // plan.total, plan.zones
    owners = [
        flipped(zone, plan.flips[slot % zones]) * 2 + (core if slot < zones else 1 - core)
        for slot in range(plan.total)
    ]
    natural = [pl.ds(pl.multiple_of(owner * size, size), size) for owner in owners]
    return natural, [pl.ds(slot * size, size) for slot in range(plan.total)]


def copy_rows(source, target):
    def some(row, count):
        target[pl.ds(row, count), :] = source[pl.ds(row, count), :]

    if source.shape[0] % 32:
        target[...] = source[...]
    else:
        for_rows(source.shape[0], some)


def cast_rows(source, target):
    def some(row, count):
        here = pl.ds(row, count)
        target[here, :] = source[here, :].astype(target.dtype)

    for_rows(source.shape[0], some)


def opening_kernel(plan, wide_qkv, gains, wide_gate, wide_out, wide_down, tokens, angles, *refs):
    qkv_full, gains_full, turned_gate, turned_out, turned_down, turned_tokens, turned_angles = refs[:7]
    partner_gate, send_sems, recv_sems, tokens_stage, qkv, gate, out, down = refs[7:]
    cast_rows(wide_qkv, qkv)
    zone, side, row, core = place_here()
    partner = device(zone, core, row, side)
    row_peer, core_peer = device(zone, side, 1 - row, core), device(zone, side, row, 1 - core)
    zone_peers = [device(flipped(zone, flip), side, row, core) for flip in plan.flips[1:]]
    at_home, away = side == core, side != core
    always = [row_peer, core_peer] + zone_peers

    @pl.when(at_home)
    def _():
        greet(always)

    @pl.when(away)
    def _():
        greet(always + [partner])

    copies = Copies(send_sems, recv_sems)
    zones = plan.zones
    own = (gains, qkv, angles, gate, out, down)
    ends = (gains_full.at[0], qkv_full.at[0], turned_angles, turned_gate, turned_out, turned_down)
    units = wide_gate.shape[2]

    def cast_rest():
        for half in (0, 1):
            cast_rows(wide_gate.at[half], gate.at[:, pl.ds(half * units, units)])
        cast_rows(wide_out, out)
        cast_rows(wide_down, down)

    turn = [copies.make(source, target, partner) for source, target in zip(own, ends)]
    pieces = 2
    size = tokens.shape[0] // (2 * pieces)
    spots = [
        pl.ds(pl.multiple_of((row * pieces + piece) * size, size), size) for piece in range(pieces)
    ]
    turn_rows = [copies.make(tokens.at[s], tokens_stage.at[s], partner) for s in spots]
    pass_rows = [copies.make(tokens_stage.at[s], tokens_stage.at[s], row_peer) for s in spots]
    natural, local = block_columns(plan, tokens.shape[1])

    def lay_down(all_tokens):
        def some(start, count):
            here = pl.ds(start, count)
            for a, b in zip(natural, local):
                turned_tokens[here, b] = all_tokens[here, a]

        for_rows(all_tokens.shape[0], some)

    slots = list(range(1, zones))
    weights = ((gains, gains_full), (qkv, qkv_full))
    from_own = [
        [copies.make(source, full.at[slot], zone_peers[slot - 1]) for slot in slots]
        + [copies.make(source, full.at[zones], core_peer)]
        for source, full in weights
    ] + [[copies.make(gate, partner_gate, zone_peers[0])]]
    copies.number -= 2 * zones + 1
    from_turned = [
        [copies.make(full.at[0], full.at[slot], zone_peers[slot - 1]) for slot in slots]
        + [copies.make(full.at[0], full.at[zones], core_peer)]
        for _, full in weights
    ] + [[copies.make(turned_gate, partner_gate, zone_peers[0])]]
    cross = [
        [copies.make(full.at[slot], full.at[zones + slot], core_peer) for slot in slots]
        for _, full in weights
    ]

    def cross_over(k):
        for which in (0, 1):
            from_turned[which][k].wait_recv()
            cross[which][k].start()

    @pl.when(away)
    def _():
        for copy in turn[:3]:
            copy.start()
        cast_rest()
        for which in (0, 1):
            turn[which].wait_recv()
            for copy in from_turned[which]:
                copy.start()
        turn[3].start()
        turn_rows[0].start()
        turn[3].wait_recv()
        from_turned[2][0].start()
        turn_rows[1].start()
        cross_over(0)
        turn_rows[0].wait_recv()
        pass_rows[0].start()
        for copy in turn[4:]:
            copy.start()
        turn_rows[1].wait_recv()
        pass_rows[1].start()

    @pl.when(at_home)
    def _():
        for copy in from_own[0] + from_own[1]:
            copy.start()
        cast_rest()
        for copy in from_own[2]:
            copy.start()
        for source, target in zip(own, ends):
            copy_rows(source, target)
        lay_down(tokens)
        cross_over(0)

    for k in range(1, zones - 1):
        cross_over(k)
    for which in (0, 1):
        from_turned[which][zones - 1].wait_recv()
        for copy in from_turned[which]:
            copy.wait_send()
        for copy in cross[which]:
            copy.wait_recv()
            copy.wait_send()
    from_turned[2][0].wait_recv()
    from_turned[2][0].wait_send()

    @pl.when(away)
    def _():
        for copy in pass_rows + turn[2:3] + turn[4:]:
            copy.wait_recv()
        lay_down(tokens_stage)
        for copy in turn + turn_rows + pass_rows:
            copy.wait_send()


def opening(plan, qkv, gains, gate, out, down, tokens, angles, number):
    low = jnp.bfloat16
    vmem = pl.BlockSpec(memory_space=pltpu.VMEM)
    like = lambda v: jax.ShapeDtypeStruct(v.shape, v.dtype)
    whole = lambda v: jax.ShapeDtypeStruct((2 * plan.zones,) + v.shape, low)
    operands = (qkv, gains, gate, out, down, tokens, angles)
    low_gate = jax.ShapeDtypeStruct((gate.shape[1], 2 * gate.shape[2]), low)
    low_out = jax.ShapeDtypeStruct(out.shape, low)
    low_down = jax.ShapeDtypeStruct(down.shape, low)
    outputs = [whole(qkv), whole(gains), low_gate, low_out, low_down, like(tokens), like(angles)]
    outputs += [low_gate]
    copies = 6 + 4 + 2 * plan.zones + 1 + 2 * (plan.zones - 1)
    return pl.pallas_call(
        functools.partial(opening_kernel, plan),
        out_shape=outputs,
        in_specs=[vmem] * len(operands),
        out_specs=[vmem] * len(outputs),
        scratch_shapes=[
            pltpu.SemaphoreType.DMA((copies,)),
            pltpu.SemaphoreType.DMA((copies,)),
            pltpu.VMEM(tokens.shape, tokens.dtype),
            pltpu.VMEM(qkv.shape, low),
            pltpu.VMEM(low_gate.shape, low),
            pltpu.VMEM(out.shape, low),
            pltpu.VMEM(down.shape, low),
        ],
        compiler_params=pltpu.CompilerParams(
            collective_id=number, has_side_effects=True, vmem_limit_bytes=56 * 2**20
        ),
        cost_estimate=pl.CostEstimate(flops=10**6, bytes_accessed=10**5, transcendentals=0),
        name="opening",
    )(*operands)


def inverse_rms(values):
    return lax.rsqrt(jnp.mean(values * values, -1, keepdims=True) + EPS_NORM)


def hidden_rows(own, sums, extras, outs):
    tokens, gain = extras
    hidden = tokens[own, :].astype(jnp.float32) + sums
    outs[0][own, :] = hidden
    return (hidden * inverse_rms(hidden) * gain[...]).astype(jnp.bfloat16)


def grad_hidden_rows(own, sums, extras, outs):
    hidden, out_grad, gain = extras
    values = hidden[own, :]
    factor = inverse_rms(values)
    unit = values * factor
    outs[1][...] += jnp.sum(sums * unit, 0, keepdims=True)
    grad = out_grad[own, :].astype(jnp.float32) + norm_back(sums * gain[...], unit, factor)
    outs[0][own, :] = grad
    return grad.astype(jnp.bfloat16)


def grad_input_rows(own, sums, extras, outs):
    tokens, grad_hidden, gain = extras[:3]
    values = tokens[own, :].astype(jnp.float32)
    factor = inverse_rms(values)
    unit = values * factor
    outs[0][...] += jnp.sum(sums * unit, 0, keepdims=True)
    return (grad_hidden[own, :] + norm_back(sums * gain[...], unit, factor)).astype(jnp.bfloat16)


def dot(left, right, left_dim=1, right_dim=0):
    return lax.dot_general(
        left, right, (((left_dim,), (right_dim,)), ((), ())), preferred_element_type=jnp.float32
    )


def turn_head(values, cosine, signed_sine):
    return values * cosine + pltpu.roll(values, HEAD // 2, 1) * signed_sine


def turn_back(gradient, cosine, signed_sine):
    return gradient * cosine + pltpu.roll(gradient * signed_sine, HEAD // 2, 1)


def softmax_block(query, key, first_row):
    rows, keys = query.shape[0], key.shape[0]
    scores = dot(query, key, 1, 1)
    row_at = lax.broadcasted_iota(jnp.int32, (rows, keys), 0) + first_row
    key_at = lax.broadcasted_iota(jnp.int32, (rows, keys), 1)
    scores = jnp.where(key_at <= row_at, scores, -1000000000.0)
    exponent = jnp.exp(scores - jnp.max(scores, -1, keepdims=True))
    return exponent / jnp.sum(exponent, -1, keepdims=True)


def eighth_owners():
    _, side, row, _ = place_here()
    own, off = (row, side), (1 - row, 1 - side)
    first = lambda x, y: x * 2 + y
    second = lambda x, y: 4 + y * 2 + x
    return [
        first(own[0], own[1]),
        first(own[0], off[1]),
        second(own[0], own[1]),
        second(off[0], own[1]),
        first(off[0], own[1]),
        first(off[0], off[1]),
        second(own[0], off[1]),
        second(off[0], off[1]),
    ]


def reorder_rows(source, target, into_local):
    size = source.shape[0] // 8
    for slot, owner in enumerate(eighth_owners()):
        natural = pl.ds(pl.multiple_of(owner * size, size), size)
        local = pl.ds(slot * size, size)
        if into_local:
            target[local, :] = source[natural, :]
        else:
            target[natural, :] = source[local, :]


def forward_kernel(
    tokens, weights, gain_in, gain_q, gain_k, cosine, sine,
    normed, raw, query, key, value, local, attended,
):
    low = jnp.bfloat16
    total, heads = tokens.shape[0], query.shape[1] // HEAD
    block, wide = 256, 512

    def project(step, carry):
        rows = pl.ds(pl.multiple_of(step * wide, wide), wide)
        values = tokens[rows, :].astype(jnp.float32)
        normed[rows, :] = (values * inverse_rms(values) * gain_in[...]).astype(low)
        raw[rows, :] = dot(normed[rows, :], weights[...])
        turns = (cosine[rows, :], sine[rows, :])
        for head in range(heads):
            column = (head // 2) * 4 * HEAD + (head % 2) * HEAD
            values = raw[rows, pl.ds(column, HEAD)]
            values = turn_head(values * inverse_rms(values) * gain_q[...], *turns)
            query[rows, pl.ds(head * HEAD, HEAD)] = (values * (1.0 / math.sqrt(HEAD))).astype(low)
        for group in range(heads // 2):
            column = group * 4 * HEAD + 2 * HEAD
            here = pl.ds(group * HEAD, HEAD)
            values = raw[rows, pl.ds(column, HEAD)]
            values = turn_head(values * inverse_rms(values) * gain_k[...], *turns)
            key[rows, here] = values.astype(low)
            value[rows, here] = raw[rows, pl.ds(column + HEAD, HEAD)].astype(low)
        return carry

    lax.fori_loop(0, total // wide, project, 0)

    def attend(head, carry):
        mine = pl.ds(pl.multiple_of(head * HEAD, HEAD), HEAD)
        shared = pl.ds(pl.multiple_of(lax.div(head, 2) * HEAD, HEAD), HEAD)
        for start in range(0, total, SEQ):
            for first in range(0, SEQ, block):
                rows, keys = pl.ds(start + first, block), pl.ds(start, first + block)
                probs = softmax_block(query[rows, mine], key[keys, shared], first)
                attended[rows, mine] = dot(probs.astype(low), value[keys, shared]).astype(low)
        return carry

    lax.fori_loop(0, heads, attend, 0)
    reorder_rows(attended, local, True)


def attention(tokens, weights, gain_in, gain_q, gain_k, cosine, sine):
    total = tokens.shape[0]
    columns = weights.shape[1]
    low = jnp.bfloat16
    shape = lambda width, kind=low: jax.ShapeDtypeStruct((total, width), kind)
    vmem = pl.BlockSpec(memory_space=pltpu.VMEM)
    return pl.pallas_call(
        forward_kernel,
        out_shape=[
            shape(tokens.shape[1]),
            shape(columns, jnp.float32),
            shape(columns // 2),
            shape(columns // 4),
            shape(columns // 4),
            shape(columns // 2),
        ],
        in_specs=[vmem] * 7,
        out_specs=[vmem] * 6,
        scratch_shapes=[pltpu.VMEM((total, columns // 2), low)],
        compiler_params=pltpu.CompilerParams(vmem_limit_bytes=48 * 2**20),
        cost_estimate=pl.CostEstimate(flops=10**6, bytes_accessed=10**5, transcendentals=0),
        name="attention",
    )(tokens, weights, gain_in, gain_q, gain_k, cosine, sine)


def backward_kernel(
    query, key, value, raw, grad_rows, gain_q, gain_k, cosine, sine,
    mixed, mixed_local, query_gain, key_gain, grad, key_sum, value_sum,
):
    low = jnp.bfloat16
    total, heads = query.shape[0], query.shape[1] // HEAD
    block = 256
    reorder_rows(grad_rows, grad, False)
    query_gain[...] = jnp.zeros_like(query_gain)
    key_gain[...] = jnp.zeros_like(key_gain)

    def head_norm_back(rows, column, gradient, gain, gain_grad):
        values = raw[rows, column]
        factor = inverse_rms(values)
        unit = values * factor
        turned = turn_back(gradient, cosine[rows, :], sine[rows, :])
        gain_grad[...] += jnp.sum(turned * unit, 0, keepdims=True)
        mixed[rows, column] = norm_back(turned * gain[...], unit, factor).astype(low)

    def one_group(group, carry):
        at = lambda offset: pl.ds(pl.multiple_of(group * 4 * HEAD + offset * HEAD, HEAD), HEAD)
        shared = pl.ds(pl.multiple_of(group * HEAD, HEAD), HEAD)
        key_sum[...] = jnp.zeros_like(key_sum)
        value_sum[...] = jnp.zeros_like(value_sum)
        for head in (0, 1):
            mine = pl.ds(pl.multiple_of((group * 2 + head) * HEAD, HEAD), HEAD)
            for start in range(0, total, SEQ):
                for first in range(0, SEQ, block):
                    rows, keys = pl.ds(start + first, block), pl.ds(start, first + block)
                    query_part, grad_part = query[rows, mine], grad[rows, mine]
                    probs = softmax_block(query_part, key[keys, shared], first)
                    weighed = probs * dot(grad_part, value[keys, shared], 1, 1)
                    scores = weighed - probs * jnp.sum(weighed, -1, keepdims=True)
                    scores = scores.astype(low)
                    grad_query = dot(scores, key[keys, shared]) * (1.0 / math.sqrt(HEAD))
                    head_norm_back(rows, at(head), grad_query, gain_q, query_gain)
                    key_sum[keys, :] += dot(scores, query_part, 0, 0)
                    value_sum[keys, :] += dot(probs.astype(low), grad_part, 0, 0)
        for first in range(0, total, block):
            rows = pl.ds(first, block)
            head_norm_back(rows, at(2), key_sum[rows, :], gain_k, key_gain)
            mixed[rows, at(3)] = value_sum[rows, :].astype(low)
        return carry

    lax.fori_loop(0, heads // 2, one_group, 0)
    reorder_rows(mixed, mixed_local, True)


def attention_back(query, key, value, raw, grad_rows, gain_q, gain_k, cosine, sine):
    total, columns = raw.shape
    low = jnp.bfloat16
    vmem = pl.BlockSpec(memory_space=pltpu.VMEM)
    return pl.pallas_call(
        backward_kernel,
        out_shape=[
            jax.ShapeDtypeStruct((total, columns), low),
            jax.ShapeDtypeStruct((total, columns), low),
            jax.ShapeDtypeStruct((1, HEAD), jnp.float32),
            jax.ShapeDtypeStruct((1, HEAD), jnp.float32),
        ],
        in_specs=[vmem] * 9,
        out_specs=[vmem] * 4,
        scratch_shapes=[
            pltpu.VMEM(grad_rows.shape, low),
            pltpu.VMEM((total, HEAD), jnp.float32),
            pltpu.VMEM((total, HEAD), jnp.float32),
        ],
        compiler_params=pltpu.CompilerParams(vmem_limit_bytes=48 * 2**20),
        cost_estimate=pl.CostEstimate(flops=10**6, bytes_accessed=10**5, transcendentals=0),
        name="attention_back",
    )(query, key, value, raw, grad_rows, gain_q, gain_k, cosine, sine)


def feed_kernel(plan, rows, own_grad, got_grad, gate_up, up_part, down, active, grads, out_grad):
    low = jnp.bfloat16
    block = 512
    tile = down.shape[1]
    step = pl.program_id(0)
    gate_at = pl.ds(pl.multiple_of(step * tile, tile), tile)
    up_at = pl.ds(pl.multiple_of(grads.shape[1] // 2 + step * tile, tile), tile)
    _, side, _, core = place_here()

    def lay_down(source):
        natural, blocks = block_columns(plan, source.shape[1])
        eighth = source.shape[0] // 8
        for slot, owner in enumerate(eighth_owners()):

            def some(start, count, slot=slot, owner=owner):
                here = pl.ds(pl.multiple_of(owner * eighth + start, 32), count)
                there = pl.ds(slot * eighth + start, count)
                for a, b in zip(natural, blocks):
                    out_grad[there, b] = source[here, a]

            for_rows(eighth, some)

    @pl.when((step == 0) & (side == core))
    def _():
        lay_down(own_grad)

    @pl.when((step == 0) & (side != core))
    def _():
        lay_down(got_grad)

    def one(block_at, carry):
        here = pl.ds(pl.multiple_of(block_at * block, block), block)
        gate = dot(rows[here, :], gate_up[...])
        up = dot(rows[here, :], up_part[...])
        grad = dot(out_grad[here, :], down[...])
        sigmoid = jax.nn.sigmoid(gate)
        silu = gate * sigmoid
        active[here, :] = (silu * up).astype(low)
        grads[here, gate_at] = (grad * up * sigmoid * (1.0 + gate * (1.0 - sigmoid))).astype(low)
        grads[here, up_at] = (grad * silu).astype(low)
        return carry

    lax.fori_loop(0, rows.shape[0] // block, one, 0)


def feed_forward(plan, rows, own_grad, got_grad, gate_up, down, tile):
    total, width = rows.shape
    units = down.shape[1]
    low = jnp.bfloat16
    tiles = units // tile
    whole = pl.BlockSpec(memory_space=pltpu.VMEM)
    return pl.pallas_call(
        functools.partial(feed_kernel, plan),
        grid=(tiles,),
        out_shape=[
            jax.ShapeDtypeStruct((total, units), low),
            jax.ShapeDtypeStruct((total, 2 * units), low),
            jax.ShapeDtypeStruct((total, width), low),
        ],
        in_specs=[
            whole,
            whole,
            whole,
            pl.BlockSpec((width, tile), lambda step: (0, step)),
            pl.BlockSpec((width, tile), lambda step: (0, step + tiles)),
            pl.BlockSpec((width, tile), lambda step: (0, step)),
        ],
        out_specs=[
            pl.BlockSpec((total, tile), lambda step: (0, step)),
            whole,
            whole,
        ],
        compiler_params=pltpu.CompilerParams(vmem_limit_bytes=56 * 2**20),
        cost_estimate=pl.CostEstimate(
            flops=6 * total * width * units, bytes_accessed=4 * 10**7, transcendentals=total * units
        ),
        name="feed_forward",
    )(rows, own_grad, got_grad, gate_up, gate_up, down)


class Plan:
    def __init__(self, mesh):
        self.total = mesh.shape["dp"]
        self.zones = self.total // 2
        self.tensor = mesh.shape["tensor"]
        self.flips = [k ^ (k >> 1) for k in range(self.zones)]

    def place(self):
        self.index = lax.axis_index("dp")
        self.zone = self.index // 2
        self.side = self.index % 2
        self.row = lax.axis_index("tensor") // 2
        self.core = lax.axis_index("tensor") % 2
        self.home = self.side == self.core

    def move(self, value, target):
        pairs = []
        for d in range(self.total):
            for t in range(self.tensor):
                to = target(d // 2, d % 2, t // 2, t % 2)
                if to is not None:
                    zone, side, row, core = to
                    pairs.append((d * self.tensor + t, (zone * 2 + side) * self.tensor + row * 2 + core))
        return lax.ppermute(value, ("dp", "tensor"), pairs)

    def turn(self, value):
        got = self.move(value, lambda z, y, x, c: (z, c, x, y) if y != c else None)
        return jnp.where(self.home, value, got)

    def zone_flip(self, value, bit):
        return self.move(value, lambda z, y, x, c: (z ^ bit, y, x, c))

    def core_swap(self, value):
        return self.move(value, lambda z, y, x, c: (z, y, x, 1 - c))

    def side_swap(self, value):
        return self.move(value, lambda z, y, x, c: (z, 1 - y, x, c))

    def row_swap(self, value):
        return self.move(value, lambda z, y, x, c: (z, y, 1 - x, c))

    def to_local(self, value, axis):
        width = value.shape[axis] // self.total
        parts = []
        for core in (self.core, 1 - self.core):
            for slot in range(self.zones):
                owner = (self.zone ^ self.flips[slot]) * 2 + core
                parts.append(lax.dynamic_slice_in_dim(value, owner * width, width, axis))
        return jnp.concatenate(parts, axis)

    def to_natural(self, value, axis, core=None):
        core = self.core if core is None else core
        width = value.shape[axis] // self.total
        parts = []
        for block in range(self.total):
            slot = flip = (block // 2) ^ self.zone
            for bits in range(1, self.zones.bit_length()):
                slot = slot ^ (flip >> bits)
            slot = slot + jnp.where(block % 2 == core, 0, self.zones)
            parts.append(lax.dynamic_slice_in_dim(value, slot * width, width, axis))
        return jnp.concatenate(parts, axis)

    def row_owners(self):
        own, off = (self.row, self.side), (1 - self.row, 1 - self.side)
        first = lambda x, y: x * 2 + y
        second = lambda x, y: 4 + y * 2 + x
        return [
            first(own[0], own[1]),
            first(own[0], off[1]),
            second(own[0], own[1]),
            second(off[0], own[1]),
            first(off[0], own[1]),
            first(off[0], off[1]),
            second(own[0], off[1]),
            second(off[0], off[1]),
        ]

    def rows_local(self, value, slots=range(8)):
        size = value.shape[0] // 8
        owners = self.row_owners()
        return jnp.concatenate(
            [lax.dynamic_slice_in_dim(value, owners[slot] * size, size, 0) for slot in slots], 0
        )

    def rows_natural(self, value, order=range(8)):
        size = value.shape[0] // 8
        place = [list(order).index(slot) for slot in range(8)]
        parts = []
        for piece in range(8):
            x, y = (piece // 2, piece % 2) if piece < 4 else (piece % 2, (piece - 4) // 2)
            slots = (0, 1, 4, 5) if piece < 4 else (2, 6, 3, 7)
            same_x, same_y = x == self.row, y == self.side
            slot = jnp.where(
                same_x,
                jnp.where(same_y, place[slots[0]], place[slots[1]]),
                jnp.where(same_y, place[slots[2]], place[slots[3]]),
            )
            parts.append(lax.dynamic_slice_in_dim(value, slot * size, size, 0))
        return jnp.concatenate(parts, 0)

    def from_zones(self, shard):
        return [self.zone_flip(shard, flip) for flip in self.flips[1:]]

    def to_zones(self, parts, slots):
        return [self.zone_flip(parts[slot], self.flips[slot]) for slot in slots]

    def middle_swap(self, pair):
        return self.move(pair, lambda z, y, x, c: (z ^ 3, y, x, c) if z in (1, 2) else None)

    def inward(self, part):
        return self.move(part, lambda z, y, x, c: (z ^ 1, y, x, c) if z in (0, 3) else None)

    def pass_outward(self, pair):
        return self.move(pair, lambda z, y, x, c: (z ^ 1, y, x, c) if z in (1, 2) else None)

    def far_pair(self, middle, passed):
        inner = (self.zone == 1) | (self.zone == 2)
        return jnp.where(inner, middle, passed[::-1])

    def first_swap(self, send):
        half = send.shape[0] // 2
        return self.row_swap(send[:half]), self.side_swap(send[half:])

    def second_swap(self, keep, got):
        quarter = keep.shape[0] // 4
        row_part = keep[: 2 * quarter] + got[0].astype(jnp.float32)
        side_part = keep[2 * quarter :] + got[1].astype(jnp.float32)
        own = jnp.concatenate([row_part[:quarter], side_part[:quarter]], 0)
        return own, (
            self.side_swap(row_part[quarter:].astype(jnp.bfloat16)),
            self.row_swap(side_part[quarter:].astype(jnp.bfloat16)),
        )

    def spread_first(self, own):
        half = own.shape[0] // 2
        return (self.side_swap(own[:half]), self.row_swap(own[half:]))

    def spread_second(self, own, got):
        half = own.shape[0] // 2
        row_part = jnp.concatenate([own[:half], got[0]], 0)
        side_part = jnp.concatenate([own[half:], got[1]], 0)
        return row_part, side_part, self.row_swap(row_part), self.side_swap(side_part)

    def send_home(self, own):
        to_home = lambda z, y, x, c: (z, c, x, c) if y != c else None
        return jnp.concatenate([own, self.move(own, to_home)], 0)

    def row_home(self, part):
        return self.move(part, lambda z, y, x, c: (z, y, 1 - x, c) if y == c else None)

    def share_home(self, part, other):
        full = jnp.concatenate([part, other], 0)
        full = self.to_natural(self.rows_natural(full, (0, 2, 1, 6, 4, 3, 5, 7)), 1)
        got = self.move(full, lambda z, y, x, c: (z, y, x, 1 - c) if y == c else None)
        return full, got

    def turned(self, own, got):
        return jnp.where(self.home, own, got)

    def sum_everywhere(self, value):
        value = value + self.row_swap(value)
        value = value + self.side_swap(value)
        value = value + self.core_swap(value)
        bit = 1
        while bit < self.zones:
            value = value + self.zone_flip(value, bit)
            bit *= 2
        return value


def shards(
    plan,
    tokens,
    positions,
    out_grad,
    qkv_weight,
    qkv_first,
    qkv_second,
    out_weight,
    out_first,
    out_second,
    gate_up,
    gate_up_first,
    gate_up_second,
    down_weight,
    down_first,
    down_second,
    gains,
    gains_first,
    gains_second,
):
    plan.place()
    low = jnp.bfloat16
    tok_rows, model_width = tokens.shape
    groups = qkv_weight.shape[1]
    head_size = qkv_weight.shape[3]
    shard_rows = qkv_weight.shape[0]
    seq_count = tok_rows // SEQ
    mixed_cols = groups * 4 * head_size
    near_cols = model_width // 2
    kept = tok_rows // 2
    gain_count = gains.shape[0]

    tree = plan.zones == 4
    slots = range(1, plan.zones)

    def column_parts(value):
        return value.reshape((plan.zones, -1) + value.shape[1:])

    units = gate_up.shape[2]
    plan.ordered = (model_width // plan.total) % 128 == 0
    gain_rows = 16
    gain_block = jnp.pad(gains.astype(low), (0, gain_rows * 128 - gain_count)).reshape(gain_rows, 128)
    tile = min(units, 256)
    angle_at = positions.astype(jnp.float32).reshape(-1, 128)
    both_qkv, both_gains, turned_gate, turned_out, turned_down, tokens, angle_at, partner_gate = opening(
        plan,
        qkv_weight.reshape(shard_rows, mixed_cols),
        gain_block,
        gate_up,
        out_weight,
        down_weight,
        tokens,
        angle_at,
        3,
    )
    positions = angle_at.reshape(-1)
    turned_out, turned_gate, turned_down, tokens, positions, both_qkv, both_gains, out_grad = fence(
        turned_out, turned_gate, turned_down, tokens, positions, both_qkv, both_gains, out_grad
    )

    got_grad = plan.move(out_grad, lambda z, y, x, c: (z, c, x, y) if y != c else None)
    zone_out = plan.from_zones(turned_out)
    if tree:
        partner_down = plan.zone_flip(turned_down, 1)
    else:
        partner_down = plan.from_zones(turned_down)
        partner_gate = plan.from_zones(turned_gate)
    if not plan.ordered:
        tokens = plan.to_local(tokens, 1)
    cosine, sine_table = rotary(positions, head_size)
    signed_sine = jnp.concatenate(
        [-sine_table[:, : head_size // 2], sine_table[:, head_size // 2 :]], 1
    )
    full_qkv = both_qkv.reshape(model_width, mixed_cols)
    gain_slots = both_gains.reshape(plan.total, -1)[:, :gain_count]
    gain_all = plan.to_natural(gain_slots.reshape(-1), 0).astype(jnp.float32)
    gain_in = plan.to_local(gain_all[:model_width], 0)[None]
    gain_post = plan.to_local(gain_all[model_width : 2 * model_width], 0)[None]
    gain_q = gain_all[2 * model_width : 2 * model_width + head_size][None]
    gain_k = gain_all[2 * model_width + head_size :][None]
    normed, raw, query, key_rot, values_low, attended = attention(
        tokens, full_qkv, gain_in, gain_q, gain_k, cosine, signed_sine
    )
    attended, zone_out, turned_out, turned_down, turned_gate, partner_gate, partner_down = fence(
        attended, zone_out, turned_out, turned_down, turned_gate, partner_gate, partner_down
    )

    near_out = jnp.concatenate([turned_out] + zone_out, 0)
    far_out = plan.core_swap(near_out)
    own_tokens = plan.rows_local(tokens, (0, 2))
    near_out, far_out, own_tokens = fence(near_out, far_out, own_tokens)

    full_out = jnp.concatenate([near_out, far_out], 0)
    branch_terms = contract_cols(attended, full_out).astype(low)
    pairs = [(turned_gate, partner_gate), (turned_down, partner_down)]
    jobs = [PairTree(pairs, (2, 2))] if tree else []
    normed_rows, hidden, *gathered = sum_rows(
        plan,
        spread_kernel,
        hidden_rows,
        branch_terms,
        [own_tokens, gain_post],
        [jax.ShapeDtypeStruct((tok_rows // 4, model_width), jnp.float32)],
        0,
        jobs,
    )
    if not tree:
        near = [jnp.concatenate([own] + rest, 0) for own, rest in pairs]
        gathered = [jnp.concatenate([part, plan.core_swap(part)], 0) for part in near]
    full_gate = gathered[0].reshape(model_width, 2 * units)
    full_down = gathered[1].reshape(model_width, units)
    normed_rows, hidden, full_gate, full_down, got_grad = fence(
        normed_rows, hidden, full_gate, full_down, got_grad
    )

    def zone_parts(near, got):
        both = (near + got.astype(jnp.float32)).astype(low)
        return both.reshape((plan.zones, -1) + both.shape[1:])

    def zone_total(parts, *arrived):
        total = parts[0].astype(jnp.float32)
        for part in sum([list(group) for group in arrived], []):
            total = total + part.astype(jnp.float32)
        return total.astype(low)

    active, grad_both, out_grad = feed_forward(
        plan, normed_rows, out_grad, got_grad, full_gate, full_down, tile
    )
    if not plan.ordered:
        out_grad = plan.to_local(out_grad, 1)
    down_far = contract_rows(out_grad[:, near_cols:], active).astype(low)
    down_far, active, grad_both, out_grad, normed_rows = fence(
        down_far, active, grad_both, out_grad, normed_rows
    )

    down_got = plan.core_swap(down_far)
    gate_far = contract_rows(normed_rows[:, near_cols:], grad_both).astype(low)
    down_parts = zone_parts(contract_rows(out_grad[:, :near_cols], active), down_got)
    gate_far, down_parts, grad_both, normed_rows = fence(
        gate_far, down_parts, grad_both, normed_rows
    )

    gate_got = plan.core_swap(gate_far)
    if tree:
        down_sums = [plan.inward(down_parts[3])]
    else:
        down_sums = plan.to_zones(down_parts, slots)
    post_terms = contract_cols(grad_both, full_gate).astype(low)
    post_terms, gate_got, down_parts, down_sums, grad_both, normed_rows = fence(
        post_terms, gate_got, down_parts, down_sums, grad_both, normed_rows
    )

    if tree:
        down_sums += [plan.inward(down_parts[2])]
    gate_parts = zone_parts(contract_rows(normed_rows[:, :near_cols], grad_both), gate_got)
    post_terms, gate_parts, down_parts, down_sums = fence(
        post_terms, gate_parts, down_parts, down_sums
    )

    eighth = tok_rows // 8
    own_grad = jnp.concatenate([out_grad[:eighth], out_grad[2 * eighth : 3 * eighth]], 0)
    branch_rows, grad_hidden, post_gain_grad, mlp_terms, gate_sums = sum_rows(
        plan,
        spread_kernel,
        grad_hidden_rows,
        post_terms,
        [hidden, own_grad, gain_post],
        [
            jax.ShapeDtypeStruct((tok_rows // 4, model_width), jnp.float32),
            jax.ShapeDtypeStruct((1, model_width), jnp.float32),
        ],
        1,
        [
            SideDot(active, full_down),
            PairScatter(gate_parts, 2) if tree else ZoneBlocks(plan, gate_parts, slots),
        ],
    )
    branch_rows, grad_hidden, post_gain_grad, gate_sums, mlp_terms, down_parts, down_sums = fence(
        branch_rows, grad_hidden, post_gain_grad, gate_sums, mlp_terms, down_parts, down_sums
    )

    mlp_got = plan.first_swap(mlp_terms[kept:])
    if tree:
        gate_last = [plan.zone_flip(gate_sums[1], 1)]
        gate_own = gate_sums
        down_pair = down_parts[2:].astype(jnp.float32) + jnp.stack(down_sums).astype(jnp.float32)
        down_sums = plan.middle_swap(down_pair.astype(low))
    else:
        gate_last, gate_own = gate_sums, gate_parts
    grad_att = jnp.dot(branch_rows, full_out, preferred_element_type=jnp.float32).astype(low)
    grad_mixed, mixed_rows, query_gain_grad, key_gain_grad = attention_back(
        query, key_rot, values_low, raw, grad_att, gain_q, gain_k, cosine, signed_sine
    )
    gain_terms = jnp.concatenate(
        [plan.to_natural(post_gain_grad, 1), query_gain_grad, key_gain_grad], 1
    )
    if tree:
        down_own = (down_parts[:2].astype(jnp.float32) + down_sums.astype(jnp.float32)).astype(low)
    grad_mixed, mixed_rows, gain_terms, normed, gate_last, branch_rows, mlp_got, down_sums = fence(
        grad_mixed, mixed_rows, gain_terms, normed, gate_last, branch_rows, mlp_got, down_sums
    )

    mlp_own, mlp_last = plan.second_swap(mlp_terms[:kept].astype(jnp.float32), mlp_got)
    if tree:
        total_down = zone_total(down_own, [plan.zone_flip(down_own[1], 1)])
    else:
        total_down = zone_total(down_parts, down_sums)
    total_gate = zone_total(gate_own, gate_last)
    total_gate = jnp.stack([total_gate[:, :units], total_gate[:, units:]])
    out_far = contract_rows(branch_rows[:, near_cols:], attended).astype(low)
    out_got = plan.core_swap(out_far)
    normed_terms = contract_cols(mixed_rows, full_qkv).astype(low)
    out_parts = zone_parts(contract_rows(branch_rows[:, :near_cols], attended), out_got)
    block_own = (hidden + mlp_own + jnp.concatenate(mlp_last, 0).astype(jnp.float32)).astype(low)
    out_parts, normed_terms, total_gate, total_down, block_own, normed, grad_mixed = fence(
        out_parts, normed_terms, total_gate, total_down, block_own, normed, grad_mixed
    )

    gain_sum = GainSum(plan, gain_terms.shape[1], model_width) if plan.ordered else None
    mine, input_gain_grad, *rest = sum_rows(
        plan,
        home_kernel,
        grad_input_rows,
        normed_terms,
        [own_tokens, grad_hidden, gain_in, block_own] + ([gain_terms] if plan.ordered else []),
        [jax.ShapeDtypeStruct((1, model_width), jnp.float32)],
        2,
        [
            BlockGrad(plan, normed, grad_mixed),
            ZoneBlocks(plan, out_parts, slots),
            TurnLate(total_down),
        ],
        gain_sum,
    )
    if plan.ordered:
        summed_gains, total_qkv, out_sent, got_down = rest
    else:
        total_qkv, out_sent, got_down = rest
        summed_gains = plan.sum_everywhere(
            jnp.concatenate([plan.to_natural(input_gain_grad, 1), gain_terms], 1)
        )
    mine, summed_gains, total_qkv, out_sent, total_gate, got_down = fence(
        mine, summed_gains, total_qkv, out_sent, total_gate, got_down
    )

    summed_gate = plan.turn(total_gate)
    summed_down = plan.turned(total_down, got_down)
    other = plan.core_swap(mine)
    input_full, block_out = jnp.where(plan.home, mine, other), jnp.where(plan.home, other, mine)
    if not plan.ordered:
        input_full = plan.to_natural(input_full, 1, plan.side)
        block_out = plan.to_natural(block_out, 1, plan.side)
    summed_both = plan.turn(
        jnp.concatenate([total_qkv, zone_total(out_parts, out_sent)], 1)
    ).astype(jnp.float32)
    summed_qkv = summed_both[:, :mixed_cols].reshape(qkv_weight.shape)
    summed_out = summed_both[:, mixed_cols:]
    summed_gate = summed_gate.astype(jnp.float32)
    summed_down = summed_down.astype(jnp.float32)
    summed_gains = lax.dynamic_slice_in_dim(summed_gains[0], plan.index * gain_count, gain_count, 0)
    input_rows = input_full.astype(jnp.float32)

    qkv_moment, qkv_square, qkv_updated = adamw(
        qkv_weight, summed_qkv, qkv_first, qkv_second, RATE_QKV, DECAY_RATE
    )
    out_moment, out_square, out_updated = adamw(
        out_weight, summed_out, out_first, out_second, RATE_OUT, DECAY_RATE
    )
    gate_moment, gate_square, gate_updated = adamw(
        gate_up, summed_gate, gate_up_first, gate_up_second, RATE_GATE, DECAY_RATE
    )
    down_moment, down_square, down_updated = adamw(
        down_weight, summed_down, down_first, down_second, RATE_DOWN, DECAY_RATE
    )
    gain_moment, gain_square, gain_updated = adamw(
        gains, summed_gains, gains_first, gains_second, RATE_GAIN, 0.0
    )
    return (
        block_out,
        input_rows,
        qkv_moment,
        qkv_square,
        qkv_updated,
        out_moment,
        out_square,
        out_updated,
        gate_moment,
        gate_square,
        gate_updated,
        down_moment,
        down_square,
        down_updated,
        gain_moment,
        gain_square,
        gain_updated,
    )


def solution(mesh):
    plan = Plan(mesh)
    placed = (
        P("dp", None),
        P("dp"),
        P("dp", None),
        P("dp", "tensor", None, None),
        P("dp", "tensor", None, None),
        P("dp", "tensor", None, None),
        P("dp", "tensor"),
        P("dp", "tensor"),
        P("dp", "tensor"),
        P(None, "dp", "tensor"),
        P(None, "dp", "tensor"),
        P(None, "dp", "tensor"),
        P("dp", "tensor"),
        P("dp", "tensor"),
        P("dp", "tensor"),
        P("dp"),
        P("dp"),
        P("dp"),
    )
    return jax.shard_map(
        functools.partial(shards, plan),
        mesh=mesh,
        in_specs=placed,
        out_specs=(
            P("dp", None),
            P("dp", None),
            P("dp", "tensor", None, None),
            P("dp", "tensor", None, None),
            P("dp", "tensor", None, None),
            P("dp", "tensor"),
            P("dp", "tensor"),
            P("dp", "tensor"),
            P(None, "dp", "tensor"),
            P(None, "dp", "tensor"),
            P(None, "dp", "tensor"),
            P("dp", "tensor"),
            P("dp", "tensor"),
            P("dp", "tensor"),
            P("dp"),
            P("dp"),
            P("dp"),
        ),
        check_vma=False,
    )
```

```python
import functools
import math

import jax
import jax.numpy as jnp
from jax import lax
from jax.experimental import pallas as pl
from jax.experimental.pallas import tpu as pltpu
from jax.sharding import PartitionSpec as P

SEQ = 1024
STEP = 10


EPS_NORM = 1e-06
THETA = 1000000.0
BETA_ONE = 0.9
BETA_TWO = 0.95
ADAM_EPS = 1e-08
DECAY_RATE = 0.1
RATE_QKV = 0.05
RATE_OUT = 0.3
RATE_GATE = 0.05
RATE_DOWN = 0.03
RATE_GAIN = 1.0


def rotary(positions, head_size):
    freq_index = jnp.arange(head_size // 2, dtype=jnp.float32)
    inverse = jnp.exp(freq_index * (-2.0 * math.log(THETA) / head_size))
    angles = positions.astype(jnp.float32)[:, None] * inverse[None, :]
    cosine = jnp.cos(angles)
    sine_table = jnp.sin(angles)
    return (jnp.concatenate([cosine, cosine], -1), jnp.concatenate([sine_table, sine_table], -1))


def rotate(values, cosine, sine_table):
    half_size = values.shape[-1] // 2
    turned = jnp.concatenate([-values[..., half_size:], values[..., :half_size]], -1)
    return values * cosine[:, None, :] + turned * sine_table[:, None, :]


def unrotate(gradient, cosine, sine_table):
    half_size = gradient.shape[-1] // 2
    turned = gradient * sine_table[:, None, :]
    rotated_back = jnp.concatenate([turned[..., half_size:], -turned[..., :half_size]], -1)
    return gradient * cosine[:, None, :] + rotated_back


def norm_back(grad_unit, unit_vals, factor):
    return factor * (grad_unit - unit_vals * jnp.mean(grad_unit * unit_vals, -1, keepdims=True))


def contract_rows(left, right):
    return lax.dot_general(
        left, right, (((0,), (0,)), ((), ())), preferred_element_type=jnp.float32
    )


def contract_cols(left, right):
    return lax.dot_general(
        left, right, (((1,), (1,)), ((), ())), preferred_element_type=jnp.float32
    )


def block_scores(query_part, key_part, first_row, block_rows, last_row):
    scores = jnp.einsum(
        "nqkgd,nskd->nkgqs", query_part, key_part, preferred_element_type=jnp.float32
    )
    causal = (first_row + jnp.arange(block_rows))[:, None] >= jnp.arange(last_row)[None, :]
    return jnp.where(causal, scores, -1000000000.0)


def attention_forward(query, key_rot, values_low, seq_len):
    block_rows = min(512, seq_len)
    outputs = []
    log_sums = []
    for first_row in range(0, seq_len, block_rows):
        last_row = first_row + block_rows
        query_part = query[:, first_row:last_row]
        scores = block_scores(query_part, key_rot[:, :last_row], first_row, block_rows, last_row)
        row_max = jnp.max(scores, -1, keepdims=True)
        exponent = jnp.exp(scores - row_max)
        row_total = jnp.sum(exponent, -1, keepdims=True)
        probs_low = (exponent / row_total).astype(jnp.bfloat16)
        outputs.append(
            jnp.einsum(
                "nkgqs,nskd->nqkgd",
                probs_low,
                values_low[:, :last_row],
                preferred_element_type=jnp.float32,
            )
        )
        log_sums.append(row_max + jnp.log(row_total))
    return (jnp.concatenate(outputs, 1), log_sums)


def attention_backward(query, key_rot, values_low, grad_att, log_sums, seq_len):
    block_rows = min(512, seq_len)
    query_grads = []
    key_grad = jnp.zeros(key_rot.shape, jnp.float32)
    value_grad = jnp.zeros(values_low.shape, jnp.float32)
    for block_index, first_row in enumerate(range(0, seq_len, block_rows)):
        last_row = first_row + block_rows
        query_part = query[:, first_row:last_row]
        grad_part = grad_att[:, first_row:last_row]
        key_part = key_rot[:, :last_row]
        value_part = values_low[:, :last_row]
        scores = block_scores(query_part, key_part, first_row, block_rows, last_row)
        probs = jnp.exp(scores - log_sums[block_index])
        probs_low = probs.astype(jnp.bfloat16)
        grad_probs = jnp.einsum(
            "nqkgd,nskd->nkgqs", grad_part, value_part, preferred_element_type=jnp.float32
        )
        grad_scores = (
            probs * (grad_probs - jnp.sum(probs * grad_probs, -1, keepdims=True))
        ).astype(jnp.bfloat16)
        query_grads.append(
            jnp.einsum(
                "nkgqs,nskd->nqkgd", grad_scores, key_part, preferred_element_type=jnp.float32
            )
        )
        padding = ((0, 0), (0, seq_len - last_row), (0, 0), (0, 0))
        key_grad = key_grad + jnp.pad(
            jnp.einsum(
                "nkgqs,nqkgd->nskd", grad_scores, query_part, preferred_element_type=jnp.float32
            ),
            padding,
        )
        value_grad = value_grad + jnp.pad(
            jnp.einsum(
                "nkgqs,nqkgd->nskd", probs_low, grad_part, preferred_element_type=jnp.float32
            ),
            padding,
        )
    return (jnp.concatenate(query_grads, 1), key_grad, value_grad)


def adamw(weight, gradient, moment, second, step_rate, decay_rate):
    moment = BETA_ONE * moment + (1.0 - BETA_ONE) * gradient
    second = BETA_TWO * second + (1.0 - BETA_TWO) * gradient * gradient
    first_hat = moment / (1.0 - BETA_ONE**STEP)
    second_hat = second / (1.0 - BETA_TWO**STEP)
    weight = weight - step_rate * (
        first_hat / (jnp.sqrt(second_hat) + ADAM_EPS) + decay_rate * weight
    )
    return (moment, second, weight)


def fence(*values):
    return lax.optimization_barrier(values)


MESH = pl.DeviceIdType.MESH
HEAD = 128
AHEAD = 2


def place_here():
    index, place = lax.axis_index("dp"), lax.axis_index("tensor")
    return lax.div(index, 2), lax.rem(index, 2), lax.div(place, 2), lax.rem(place, 2)


def device(zone, side, row, core):
    return (zone * 2 + side, row * 2 + core)


def flipped(zone, flip):
    bit = 1
    while bit <= flip:
        if flip & bit:
            zone = zone + bit - 2 * bit * lax.rem(lax.div(zone, bit), 2)
        bit *= 2
    return zone


def greet(devices, amount=None):
    barrier = pltpu.get_barrier_semaphore()
    for peer in devices:
        pl.semaphore_signal(barrier, inc=1, device_id=peer, device_id_type=MESH)
    pl.semaphore_wait(barrier, len(devices) if amount is None else amount)


def for_rows(count, body):
    step = 32

    def one(block, carry):
        body(pl.multiple_of(block * step, step), step)
        return carry

    lax.fori_loop(0, count // step, one, 0)


class Copies:
    def __init__(self, send_sems, recv_sems):
        self.send_sems, self.recv_sems = send_sems, recv_sems
        self.number = 0

    def make(self, source, target, peer):
        number, self.number = self.number, self.number + 1
        return pltpu.make_async_remote_copy(
            src_ref=source,
            dst_ref=target,
            send_sem=self.send_sems.at[number],
            recv_sem=self.recv_sems.at[number],
            device_id=peer,
            device_id_type=MESH,
        )

    def start(self, source, target, peer):
        copy = self.make(source, target, peer)
        copy.start()
        return copy


class GainSum:
    def __init__(self, plan, rest, width):
        self.plan, self.width = plan, width
        self.total = width + rest
        self.scratch = [
            pltpu.VMEM((8, 1, self.total), jnp.float32),
            pltpu.VMEM((plan.zones, 1, self.total), jnp.float32),
        ]
        self.output = jax.ShapeDtypeStruct((1, self.total), jnp.float32)
        self.count = 7 + plan.zones - 1

    def plane_peers(self, zone, side, row, core):
        steps = [(s, r, c) for s in range(2) for r in range(2) for c in range(2)][1:]
        turn = lambda value, step: 1 - value if step else value
        return [device(zone, turn(side, s), turn(row, r), turn(core, c)) for s, r, c in steps]

    def zone_peers(self, zone, side, row, core):
        return {flip: device(flipped(zone, flip), side, row, core) for flip in self.plan.flips[1:]}

    def start(self, copies, rest, blocks, plane_sums, zone_sums):
        zone, side, row, core = place_here()
        plan = self.plan
        size = self.width // plan.total
        self.copies, self.plane_sums, self.zone_sums, self.zone = copies, plane_sums, zone_sums, zone
        here = side * 4 + row * 2 + core
        plane_sums[here, :, pl.ds(self.width, self.total - self.width)] = rest[...]
        for slot in range(plan.total):
            owner = flipped(zone, plan.flips[slot % plan.zones]) * 2
            owner = owner + (core if slot < plan.zones else 1 - core)
            spot = pl.ds(pl.multiple_of(owner * size, size), size)
            plane_sums[here, :, spot] = blocks[:, pl.ds(slot * size, size)]
        self.plane = [
            copies.start(plane_sums.at[here], plane_sums.at[here], peer)
            for peer in self.plane_peers(zone, side, row, core)
        ]

    def middle(self):
        for copy in self.plane:
            copy.wait_recv()
        total = self.plane_sums[0]
        for place in range(1, 8):
            total = total + self.plane_sums[place]
        self.zone_sums[self.zone] = total
        zone, side, row, core = place_here()
        self.across = [
            self.copies.start(self.zone_sums.at[self.zone], self.zone_sums.at[self.zone], peer)
            for peer in self.zone_peers(zone, side, row, core).values()
        ]

    def finish(self, out):
        for copy in self.across:
            copy.wait_recv()
        total = self.zone_sums[0]
        for place in range(1, self.plan.zones):
            total = total + self.zone_sums[place]
        out[...] = total
        for copy in self.plane + self.across:
            copy.wait_send()


class ZoneBlocks:
    scratch = []

    def __init__(self, plan, source, slots, begin=0):
        self.flips, self.slots, self.sources, self.begin = plan.flips, list(slots), [source], begin
        self.outputs = [
            jax.ShapeDtypeStruct((len(self.slots),) + source.shape[1:], source.dtype)
        ]
        self.count, self.count_local = len(self.slots), 0
        self.in_hbm = False

    def peers(self, zone, side, row, core):
        return {
            self.flips[slot]: device(flipped(zone, self.flips[slot]), side, row, core)
            for slot in self.slots
        }

    def start(self, copies, local_sems, sources, targets, stages):
        zone, side, row, core = place_here()
        self.started = [
            copies.make(
                sources[0].at[slot],
                targets[0].at[number],
                device(flipped(zone, self.flips[slot]), side, row, core),
            )
            for number, slot in enumerate(self.slots)
        ]
        self.waiting = True
        if self.begin == 0:
            self.pump([0])

    def pump(self, steps):
        if self.waiting and self.begin in steps:
            self.waiting = False
            for copy in self.started:
                copy.start()

    def finish(self):
        for copy in self.started:
            copy.wait_send()
        for copy in self.started:
            copy.wait_recv()


def inner_zone(zone):
    return lax.rem(lax.div(zone + 1, 2), 2)


class SideDot:
    count, count_local, scratch, in_hbm = 0, 0, [], False

    def __init__(self, left, right):
        self.sources = [left, right]
        self.outputs = [jax.ShapeDtypeStruct((left.shape[0], right.shape[0]), jnp.bfloat16)]

    def peers(self, zone, side, row, core):
        return {}

    def some(self, first, last):
        left, right = self.refs
        size = 256

        def one(step, carry):
            here = pl.ds(pl.multiple_of(step * size, size), size)
            self.out[:, here] = dot(left[...], right[here, :], 1, 1).astype(jnp.bfloat16)
            return carry

        lax.fori_loop(first, last, one, 0)

    def start(self, copies, local_sems, sources, targets, stages):
        self.refs, self.out = sources, targets[0]
        self.steps = self.out.shape[1] // 256
        self.some(0, self.steps // 2)

    def pump(self, steps):
        if 0 in steps:
            self.some(self.steps // 2, self.steps)

    def finish(self):
        pass


class PairScatter:
    def __init__(self, parts, pieces):
        self.sources, self.pieces = [parts], pieces
        _, rows, columns = parts.shape
        self.size = rows // pieces
        self.outputs = [jax.ShapeDtypeStruct((2, rows, columns), parts.dtype)]
        self.scratch = [pltpu.VMEM((2, rows, columns), parts.dtype)] * 2
        self.count, self.count_local = 6 * pieces, 0
        self.in_hbm = False

    def peers(self, zone, side, row, core):
        return {
            1: device(flipped(zone, 1), side, row, core),
            3: device(flipped(zone, 3), side, row, core),
        }

    def start(self, copies, local_sems, sources, targets, stages):
        zone, side, row, core = place_here()
        self.parts, self.out = sources[0], targets[0]
        self.inward, self.crossed = stages
        inner_peer = device(flipped(zone, 3), side, row, core)
        outer_peer = device(flipped(zone, 1), side, row, core)
        self.inner = inner_zone(zone) == 1
        self.outer = inner_zone(zone) == 0
        self.steps = [
            (slot, pl.ds(piece * size, size))
            for slot, size in ((0, self.size), (1, self.size // 2))
            for piece in range(self.parts.shape[1] // size)
        ]
        self.to_inner = [
            copies.make(self.parts.at[3 - slot, rows], self.inward.at[slot, rows], outer_peer)
            for slot, rows in self.steps
        ]
        self.across = [
            copies.make(self.inward.at[slot, rows], self.crossed.at[slot, rows], inner_peer)
            for slot, rows in self.steps
        ]

        @pl.when(self.outer)
        def _():
            for copy in self.to_inner[:AHEAD]:
                copy.start()

    def add(self, target, slot, rows, left, right):
        def some(row, count):
            here = pl.ds(rows.start + row, count)
            both = left[here, :].astype(jnp.float32) + right[here, :].astype(jnp.float32)
            target.at[slot][here, :] = both.astype(jnp.bfloat16)

        for_rows(rows.size, some)

    def pump(self, steps):
        steps = [step for step in steps if step < len(self.steps)]

        @pl.when(self.inner)
        def _():
            for step in steps:
                slot, rows = self.steps[step]
                self.to_inner[step].wait_recv()
                self.add(self.inward, slot, rows, self.parts.at[2 + slot], self.inward.at[slot])
                self.across[step].start()
                if step >= AHEAD:
                    self.settle(step - AHEAD)

        @pl.when(self.outer)
        def _():
            for step in steps:
                self.to_inner[step].wait_send()
                for copy in self.to_inner[step + AHEAD : step + AHEAD + 1]:
                    copy.start()

    def settle(self, step):
        slot, rows = self.steps[step]
        self.across[step].wait_recv()
        self.add(self.out, slot, rows, self.parts.at[slot], self.crossed.at[slot])

    def finish(self):
        @pl.when(self.inner)
        def _():
            for step in range(len(self.steps) - AHEAD, len(self.steps)):
                self.settle(step)
            for copy in self.across:
                copy.wait_send()

        @pl.when(self.outer)
        def _():
            for slot in (0, 1):

                def some(row, count, slot=slot):
                    here = pl.ds(row, count)
                    self.out.at[slot][here, :] = self.parts.at[slot][here, :]

                for_rows(self.parts.shape[1], some)


class BlockGrad:
    in_hbm = False

    def __init__(self, plan, left, right):
        self.zones, self.flips = plan.zones, plan.flips
        self.sources = [left, right]
        shape = (left.shape[1] // plan.total, right.shape[1])
        low = jnp.bfloat16
        self.outputs = [jax.ShapeDtypeStruct(shape, low)]
        self.scratch = [pltpu.VMEM((plan.zones,) + shape, low)] * 4
        self.count, self.count_local = 2 * plan.zones, 0

    def peers(self, zone, side, row, core):
        return {flip: device(flipped(zone, flip), side, row, core) for flip in self.flips[1:]}

    def product(self, block):
        size = self.out.shape[0]
        return dot(self.left[:, pl.ds(block * size, size)], self.right[...], 0, 0)

    def start(self, copies, local_sems, sources, targets, stages):
        zone, side, row, core = place_here()
        self.left, self.right = sources
        self.out = targets[0]
        self.far, self.got, self.parts, self.arrived = stages
        core_peer = device(zone, side, row, 1 - core)
        self.order = list(range(2, self.zones)) + [1, 0]
        self.over = [
            copies.make(self.far.at[slot], self.got.at[slot], core_peer)
            for slot in range(self.zones)
        ]
        self.along = [
            copies.make(
                self.parts.at[slot],
                self.arrived.at[slot],
                device(flipped(zone, self.flips[slot]), side, row, core),
            )
            for slot in range(1, self.zones)
        ]
        for slot in self.order:
            self.far[slot] = self.product(self.zones + slot).astype(jnp.bfloat16)
            self.over[slot].start()

    def pump(self, steps):
        for slot in self.order if 0 in steps else []:
            near = self.product(slot)
            self.over[slot].wait_recv()
            self.parts[slot] = (near + self.got[slot].astype(jnp.float32)).astype(jnp.bfloat16)
            if slot:
                self.along[slot - 1].start()

    def finish(self):
        total = self.parts[0].astype(jnp.float32)
        for slot in range(1, self.zones):
            self.along[slot - 1].wait_recv()
            total = total + self.arrived[slot].astype(jnp.float32)
        self.out[...] = total.astype(jnp.bfloat16)
        for copy in self.over + self.along:
            copy.wait_send()


class TurnLate:
    count, count_local, scratch, in_hbm = 1, 0, [], False

    def __init__(self, values):
        self.sources = [values]
        self.outputs = [jax.ShapeDtypeStruct(values.shape, values.dtype)]

    def peers(self, zone, side, row, core):
        return {}

    def start(self, copies, local_sems, sources, targets, stages):
        zone, side, row, core = place_here()
        self.away = side != core
        self.copy = copies.make(sources[0], targets[0], device(zone, core, row, side))

    def pump(self, steps):
        pass

    def late(self):
        @pl.when(self.away)
        def _():
            self.copy.start()

    def finish(self):
        @pl.when(self.away)
        def _():
            self.copy.wait_recv()
            self.copy.wait_send()


class PairTree:
    def __init__(self, pairs, pieces):
        self.pairs = [len(pair) for pair in pairs]
        self.sources = [shard for pair in pairs for shard in pair]
        self.pieces = pieces
        self.outputs = [
            jax.ShapeDtypeStruct((8,) + own.shape, own.dtype) for own, *_ in pairs
        ]
        self.count = 6 * sum(pieces) + 2 * len(pairs) + self.pairs.count(1)
        self.count_local = 2 * len(pairs) + 2 * sum(pieces)
        self.scratch = [pltpu.VMEM((2,) + own.shape, own.dtype) for own, *_ in pairs]
        self.scratch += [pltpu.VMEM(p[0].shape, p[0].dtype) for p in pairs if len(p) == 1]
        self.in_hbm = True

    def peers(self, zone, side, row, core):
        return {
            1: device(flipped(zone, 1), side, row, core),
            3: device(flipped(zone, 3), side, row, core),
            "core": device(zone, side, row, 1 - core),
        }

    def start(self, copies, local_sems, sources, targets, stages):
        zone, side, row, core = place_here()
        inner_peer = device(flipped(zone, 3), side, row, core)
        outer_peer = device(flipped(zone, 1), side, row, core)
        core_peer = device(zone, side, row, 1 - core)
        self.inner = inner_zone(zone) == 1
        self.outer = inner_zone(zone) == 0
        self.across, self.onward, self.late, self.place = [], [], [], []
        self.shared, self.kept, self.partners, self.later = [], [], [], []
        sem = 0
        sources, late_stages = list(sources), list(stages[len(targets) :])
        for weight, full in enumerate(targets):
            landing = stages[weight]
            pair = [sources.pop(0) for _ in range(self.pairs[weight])]
            if len(pair) == 1:
                pair.append(late_stages.pop(0))
                self.partners.append(copies.start(pair[0], pair[1], outer_peer))
            size = pair[0].shape[0] // self.pieces[weight]
            for piece in range(self.pieces[weight]):
                rows = pl.ds(piece * size, size)
                for slot in (0, 1):
                    here = landing.at[slot, rows]
                    self.across.append(copies.make(pair[slot].at[rows], here, inner_peer))
                    self.onward.append(copies.make(here, landing.at[1 - slot, rows], outer_peer))
                    self.late.append(copies.make(here, full.at[6 + slot, rows], core_peer))
                    self.place.append(
                        pltpu.make_async_copy(here, full.at[2 + slot, rows], local_sems.at[sem])
                    )
                    sem += 1
            for slot in (0, 1):
                self.shared.append(copies.make(pair[slot], full.at[4 + slot], core_peer))
                self.kept.append(
                    pltpu.make_async_copy(pair[slot], full.at[slot], local_sems.at[sem])
                )
                sem += 1
                if slot >= self.pairs[weight]:
                    self.later += [self.shared[-1], self.kept[-1]]
                else:
                    self.shared[-1].start()
                    self.kept[-1].start()

        @pl.when(self.inner)
        def _():
            for copy in self.across[:AHEAD]:
                copy.start()

    def arrive(self, number):
        self.onward[number].wait_recv()
        swapped = number + 1 - 2 * (number % 2)
        self.late[swapped].start()
        self.place[swapped].start()

    def pump(self, steps):
        steps = [step for step in steps if step < len(self.across)]

        @pl.when(self.inner)
        def _():
            for here in steps:
                self.across[here].wait_recv()
                for copy in self.across[here + AHEAD : here + AHEAD + 1]:
                    copy.start()
                self.onward[here].start()
                self.late[here].start()
                self.place[here].start()

        @pl.when(self.outer)
        def _():
            for step in steps:
                if step > 0:
                    self.arrive(step - 1)

        for copy in self.partners if 1 in steps else []:
            copy.wait_recv()
            copy.wait_send()
        for copy in self.later if 1 in steps else []:
            copy.start()

    def finish(self):
        @pl.when(self.inner)
        def _():
            for copy in self.across + self.onward:
                copy.wait_send()

        @pl.when(self.outer)
        def _():
            self.arrive(len(self.onward) - 1)

        for copy in self.kept + self.place:
            copy.wait()
        for copy in self.shared + self.late:
            copy.wait_send()
        for copy in self.shared + self.late:
            copy.wait_recv()


def sum_eighths(
    copies, row_peer, side_peer, send, keep, forward, first, second, store, begin, pump
):
    size = send.shape[0] // 4
    part = lambda ref, slot: ref.at[pl.ds(slot * size, size)]
    arrivals = [
        copies.start(part(send, 1), part(first, 1), row_peer),
        copies.start(part(send, 3), part(first, 3), side_peer),
        copies.start(part(send, 0), part(first, 0), row_peer),
        copies.start(part(send, 2), part(first, 2), side_peer),
    ]
    begin()
    passed = []
    for number, slot, peer in ((0, 1, side_peer), (1, 3, row_peer)):
        arrivals[number].wait_recv()

        def add(row, count, number=number, slot=slot):
            here = pl.ds(slot * size + row, count)
            both = keep[here, :].astype(jnp.float32) + first[here, :].astype(jnp.float32)
            forward[pl.ds(number * size + row, count), :] = both.astype(jnp.bfloat16)

        for_rows(size, add)
        passed.append(copies.start(part(forward, number), part(second, number), peer))
    pump([0])
    for number, slot in ((0, 0), (1, 2)):
        arrivals[2 + number].wait_recv()
        passed[number].wait_recv()

        def total(row, count, number=number, slot=slot):
            here = pl.ds(slot * size + row, count)
            sums = keep[here, :].astype(jnp.float32) + first[here, :].astype(jnp.float32)
            sums = sums + second[pl.ds(number * size + row, count), :].astype(jnp.float32)
            store(number, row, count, sums)

        for_rows(size, total)
        yield number
    for copy in arrivals + passed:
        copy.wait_send()


def halves(terms):
    rows = terms.shape[0] // 2
    return terms.at[pl.ds(0, rows)], terms.at[pl.ds(rows, rows)]


def split_refs(refs, jobs, extra_count, out_count):
    refs = list(refs)
    take = lambda count: [refs.pop(0) for _ in range(count)]
    extras = take(extra_count)
    sources = [take(len(job.sources)) for job in jobs]
    full = take(1)[0]
    outs = take(out_count)
    targets = [take(len(job.outputs)) for job in jobs]
    return extras, sources, full, outs, targets, refs


def spread_kernel(middle, jobs, extra_count, out_count, gain_sum, plan, terms, *refs):
    keep, send = halves(terms)
    extras, sources, full, outs, targets, scratch = split_refs(refs, jobs, extra_count, out_count)
    forward, first, second, send_sems, recv_sems, local_sems, *stages = scratch
    zone, side, row, core = place_here()
    row_peer, side_peer = device(zone, side, 1 - row, core), device(zone, 1 - side, row, core)
    copies = Copies(send_sems, recv_sems)
    size = send.shape[0] // 4
    part = lambda slot: full.at[pl.ds(slot * size, size)]
    for out in outs:
        if out.shape[0] == 1:
            out[...] = jnp.zeros_like(out)
    peers = {}
    for job in jobs:
        peers.update(job.peers(zone, side, row, core))
    greet([row_peer, side_peer] + list(peers.values()))

    def begin():
        spot = 0
        for job, source, target in zip(jobs, sources, targets):
            own_stages = stages[spot : spot + len(job.scratch)]
            job.start(copies, local_sems, source, target, own_stages)
            spot += len(job.scratch)

    def pump(steps):
        for job in jobs:
            job.pump(steps)

    def store(number, row, count, sums):
        own = pl.ds(number * size + row, count)
        full[pl.ds(2 * number * size + row, count), :] = middle(own, sums, extras, outs)

    firsts, seconds = [], []
    for number in sum_eighths(
        copies, row_peer, side_peer, send, keep, forward, first, second, store, begin, pump
    ):
        near, other = (side_peer, row_peer) if number == 0 else (row_peer, side_peer)
        slot = 2 * number
        firsts.append(copies.start(part(slot), part(slot + 1), near))
        seconds.append(copies.start(part(slot), part(4 + slot), other))
    pump([1])
    firsts[0].wait_recv()
    seconds.append(copies.start(part(1), part(5), row_peer))
    firsts[1].wait_recv()
    seconds.append(copies.start(part(3), part(7), side_peer))
    pump(range(2, 64))
    for copy in seconds:
        copy.wait_recv()
    for copy in firsts + seconds:
        copy.wait_send()
    for job in jobs:
        job.finish()


def home_kernel(middle, jobs, extra_count, out_count, gain_sum, plan, terms, *refs):
    keep, send = halves(terms)
    extras, sources, result, outs, targets, scratch = split_refs(refs, jobs, extra_count, out_count)
    forward, first, second, own, full, send_sems, recv_sems, local_sems, *rest = scratch
    gain_scratch, stages = (rest[:2], rest[2:]) if gain_sum is not None else ([], rest)
    block = extras[3]
    zone, side, row, core = place_here()
    row_peer, side_peer = device(zone, side, 1 - row, core), device(zone, 1 - side, row, core)
    core_peer, other_peer = device(zone, side, row, 1 - core), device(zone, 1 - side, row, 1 - core)
    copies = Copies(send_sems, recv_sems)
    size = send.shape[0] // 4
    at_home = side == core
    away = side != core
    for out in outs:
        if out.shape[0] == 1:
            out[...] = jnp.zeros_like(out)
    peers = {}
    for job in jobs:
        peers.update(job.peers(zone, side, row, core))
    plane = [row_peer, side_peer, core_peer, other_peer]
    if gain_sum is not None:
        plane = gain_sum.plane_peers(zone, side, row, core)
        peers.update(gain_sum.zone_peers(zone, side, row, core))
    greet(plane + list(peers.values()))

    def begin():
        spot = 0
        for job, source, target in zip(jobs, sources, targets):
            own_stages = stages[spot : spot + len(job.scratch)]
            job.start(copies, local_sems, source, target, own_stages)
            spot += len(job.scratch)

    def pump(steps):
        if 0 in steps:

            @pl.when(away)
            def _():
                for copy in block_side:
                    copy.start()

        for job in jobs:
            job.pump(steps)

    def store(number, start, count, sums):
        here = pl.ds(number * size + start, count)
        values = middle(here, sums, extras, outs)
        own[here, :] = values
        eighth = row * 2 + side if number == 0 else 4 + side * 2 + row

        @pl.when(at_home)
        def _():
            full[pl.ds(pl.multiple_of(eighth * size + start, 32), count), :] = values

    def piece(number, x, y):
        start = (x * 2 + y) * size if number == 0 else (4 + y * 2 + x) * size
        return full.at[pl.ds(pl.multiple_of(start, size), size)]

    both = (0, 1)
    part = lambda ref, number: ref.at[pl.ds(number * size, size)]
    block_over = [copies.make(part(block, k), piece(k, row, side), core_peer) for k in both]
    block_side = [copies.make(part(block, k), piece(k, row, side), other_peer) for k in both]
    to_side = [copies.make(part(own, k), piece(k, row, side), side_peer) for k in both]
    to_row = [copies.make(piece(k, row, side), piece(k, row, side), row_peer) for k in both]
    pass_row = [
        copies.make(piece(k, row, 1 - side), piece(k, row, 1 - side), row_peer) for k in both
    ]

    @pl.when(at_home)
    def _():
        for copy in block_over:
            copy.start()

    for _ in sum_eighths(
        copies, row_peer, side_peer, send, keep, forward, first, second, store, begin, pump
    ):
        pass
    pump([1])
    if gain_sum is not None:
        gain_sum.start(copies, extras[-1], outs[0], *gain_scratch)

    @pl.when(away)
    def _():
        for copy in to_side:
            copy.start()
        for copy in block_over:
            copy.wait_recv()

    for copy in to_row:
        copy.start()
    for job in jobs:
        if isinstance(job, TurnLate):
            job.late()
    if gain_sum is not None:
        gain_sum.middle()

    @pl.when(at_home)
    def _():
        for copy in to_side:
            copy.wait_recv()
        for copy in block_over:
            copy.wait_send()

    @pl.when(away)
    def _():
        for copy in block_side:
            copy.wait_recv()

    for copy in pass_row:
        copy.start()
    for copy in to_row + pass_row:
        copy.wait_recv()
        copy.wait_send()
    @pl.when(away)
    def _():
        for copy in to_side + block_side:
            copy.wait_send()

    natural, local = block_columns(plan, full.shape[1], side)

    def some(start, count):
        here = pl.ds(start, count)
        for a, b in zip(natural, local):
            result[here, a] = full[here, b]

    for_rows(full.shape[0], some)
    if gain_sum is not None:
        gain_sum.finish(outs[-1])
    for job in jobs:
        job.finish()


def sum_rows(plan, kernel, middle, terms, extras, outs, number, jobs=(), gain_sum=None):
    half, width = terms.shape[0] // 2, terms.shape[1]
    eighth = half // 4
    low = jnp.bfloat16
    vmem, hbm = pl.BlockSpec(memory_space=pltpu.VMEM), pl.BlockSpec(memory_space=pl.ANY)
    scratch = [
        pltpu.VMEM((2 * eighth, width), low),
        pltpu.VMEM((half, width), low),
        pltpu.VMEM((2 * eighth, width), low),
    ]
    if kernel is home_kernel:
        scratch.append(pltpu.VMEM((2 * eighth, width), low))
        scratch.append(pltpu.VMEM((2 * half, width), low))
    copies = (12 if kernel is spread_kernel else 16) + sum(job.count for job in jobs)
    local = max([2] + [job.count_local for job in jobs])
    if gain_sum is not None:
        copies += gain_sum.count
        outs = outs + [gain_sum.output]
    scratch += [pltpu.SemaphoreType.DMA((count,)) for count in (copies, copies, local)]
    if gain_sum is not None:
        scratch += gain_sum.scratch
    scratch += [stage for job in jobs for stage in job.scratch]
    sources = [source for job in jobs for source in job.sources]
    targets = [target for job in jobs for target in job.outputs]
    return pl.pallas_call(
        functools.partial(kernel, middle, jobs, len(extras), len(outs), gain_sum, plan),
        out_shape=[jax.ShapeDtypeStruct((2 * half, width), low)] + outs + targets,
        in_specs=[vmem] * (1 + len(extras) + len(sources)),
        out_specs=[vmem] * (1 + len(outs))
        + [hbm if job.in_hbm else vmem for job in jobs for _ in job.outputs],
        scratch_shapes=scratch,
        compiler_params=pltpu.CompilerParams(
            collective_id=number, has_side_effects=True, vmem_limit_bytes=56 * 2**20
        ),
        cost_estimate=pl.CostEstimate(flops=10**6, bytes_accessed=10**5, transcendentals=0),
        name=middle.__name__,
    )(terms, *extras, *sources)


def block_columns(plan, width, of_core=None):
    if not plan.ordered:
        return [pl.ds(0, width)], [pl.ds(0, width)]
    zone, _, _, core = place_here()
    core = core if of_core is None else of_core
    size, zones = width // plan.total, plan.zones
    owners = [
        flipped(zone, plan.flips[slot % zones]) * 2 + (core if slot < zones else 1 - core)
        for slot in range(plan.total)
    ]
    natural = [pl.ds(pl.multiple_of(owner * size, size), size) for owner in owners]
    return natural, [pl.ds(slot * size, size) for slot in range(plan.total)]


def copy_rows(source, target):
    def some(row, count):
        target[pl.ds(row, count), :] = source[pl.ds(row, count), :]

    if source.shape[0] % 32:
        target[...] = source[...]
    else:
        for_rows(source.shape[0], some)


def cast_rows(source, target):
    def some(row, count):
        here = pl.ds(row, count)
        target[here, :] = source[here, :].astype(target.dtype)

    for_rows(source.shape[0], some)


def opening_kernel(plan, wide_qkv, gains, wide_gate, wide_out, wide_down, tokens, angles, *refs):
    qkv_full, gains_full, turned_gate, turned_out, turned_down, turned_tokens, turned_angles = refs[:7]
    partner_gate, send_sems, recv_sems, tokens_stage, qkv, gate, out, down = refs[7:]
    cast_rows(wide_qkv, qkv)
    zone, side, row, core = place_here()
    partner = device(zone, core, row, side)
    row_peer, core_peer = device(zone, side, 1 - row, core), device(zone, side, row, 1 - core)
    zone_peers = [device(flipped(zone, flip), side, row, core) for flip in plan.flips[1:]]
    at_home, away = side == core, side != core
    always = [row_peer, core_peer] + zone_peers

    @pl.when(at_home)
    def _():
        greet(always)

    @pl.when(away)
    def _():
        greet(always + [partner])

    copies = Copies(send_sems, recv_sems)
    zones = plan.zones
    own = (gains, qkv, angles, gate, out, down)
    ends = (gains_full.at[0], qkv_full.at[0], turned_angles, turned_gate, turned_out, turned_down)
    units = wide_gate.shape[2]

    def cast_rest():
        for half in (0, 1):
            cast_rows(wide_gate.at[half], gate.at[:, pl.ds(half * units, units)])
        cast_rows(wide_out, out)
        cast_rows(wide_down, down)

    turn = [copies.make(source, target, partner) for source, target in zip(own, ends)]
    pieces = 2
    size = tokens.shape[0] // (2 * pieces)
    spots = [
        pl.ds(pl.multiple_of((row * pieces + piece) * size, size), size) for piece in range(pieces)
    ]
    turn_rows = [copies.make(tokens.at[s], tokens_stage.at[s], partner) for s in spots]
    pass_rows = [copies.make(tokens_stage.at[s], tokens_stage.at[s], row_peer) for s in spots]
    natural, local = block_columns(plan, tokens.shape[1])

    def lay_down(all_tokens):
        def some(start, count):
            here = pl.ds(start, count)
            for a, b in zip(natural, local):
                turned_tokens[here, b] = all_tokens[here, a]

        for_rows(all_tokens.shape[0], some)

    slots = list(range(1, zones))
    weights = ((gains, gains_full), (qkv, qkv_full))
    from_own = [
        [copies.make(source, full.at[slot], zone_peers[slot - 1]) for slot in slots]
        + [copies.make(source, full.at[zones], core_peer)]
        for source, full in weights
    ] + [[copies.make(gate, partner_gate, zone_peers[0])]]
    copies.number -= 2 * zones + 1
    from_turned = [
        [copies.make(full.at[0], full.at[slot], zone_peers[slot - 1]) for slot in slots]
        + [copies.make(full.at[0], full.at[zones], core_peer)]
        for _, full in weights
    ] + [[copies.make(turned_gate, partner_gate, zone_peers[0])]]
    cross = [
        [copies.make(full.at[slot], full.at[zones + slot], core_peer) for slot in slots]
        for _, full in weights
    ]

    def cross_over(k):
        for which in (0, 1):
            from_turned[which][k].wait_recv()
            cross[which][k].start()

    @pl.when(away)
    def _():
        for copy in turn[:3]:
            copy.start()
        cast_rest()
        for which in (0, 1):
            turn[which].wait_recv()
            for copy in from_turned[which]:
                copy.start()
        turn[3].start()
        turn_rows[0].start()
        turn[3].wait_recv()
        from_turned[2][0].start()
        turn_rows[1].start()
        cross_over(0)
        turn_rows[0].wait_recv()
        pass_rows[0].start()
        for copy in turn[4:]:
            copy.start()
        turn_rows[1].wait_recv()
        pass_rows[1].start()

    @pl.when(at_home)
    def _():
        for copy in from_own[0] + from_own[1]:
            copy.start()
        cast_rest()
        for copy in from_own[2]:
            copy.start()
        for source, target in zip(own, ends):
            copy_rows(source, target)
        lay_down(tokens)
        cross_over(0)

    for k in range(1, zones - 1):
        cross_over(k)
    for which in (0, 1):
        from_turned[which][zones - 1].wait_recv()
        for copy in from_turned[which]:
            copy.wait_send()
        for copy in cross[which]:
            copy.wait_recv()
            copy.wait_send()
    from_turned[2][0].wait_recv()
    from_turned[2][0].wait_send()

    @pl.when(away)
    def _():
        for copy in pass_rows + turn[2:3] + turn[4:]:
            copy.wait_recv()
        lay_down(tokens_stage)
        for copy in turn + turn_rows + pass_rows:
            copy.wait_send()


def opening(plan, qkv, gains, gate, out, down, tokens, angles, number):
    low = jnp.bfloat16
    vmem = pl.BlockSpec(memory_space=pltpu.VMEM)
    like = lambda v: jax.ShapeDtypeStruct(v.shape, v.dtype)
    whole = lambda v: jax.ShapeDtypeStruct((2 * plan.zones,) + v.shape, low)
    operands = (qkv, gains, gate, out, down, tokens, angles)
    low_gate = jax.ShapeDtypeStruct((gate.shape[1], 2 * gate.shape[2]), low)
    low_out = jax.ShapeDtypeStruct(out.shape, low)
    low_down = jax.ShapeDtypeStruct(down.shape, low)
    outputs = [whole(qkv), whole(gains), low_gate, low_out, low_down, like(tokens), like(angles)]
    outputs += [low_gate]
    copies = 6 + 4 + 2 * plan.zones + 1 + 2 * (plan.zones - 1)
    return pl.pallas_call(
        functools.partial(opening_kernel, plan),
        out_shape=outputs,
        in_specs=[vmem] * len(operands),
        out_specs=[vmem] * len(outputs),
        scratch_shapes=[
            pltpu.SemaphoreType.DMA((copies,)),
            pltpu.SemaphoreType.DMA((copies,)),
            pltpu.VMEM(tokens.shape, tokens.dtype),
            pltpu.VMEM(qkv.shape, low),
            pltpu.VMEM(low_gate.shape, low),
            pltpu.VMEM(out.shape, low),
            pltpu.VMEM(down.shape, low),
        ],
        compiler_params=pltpu.CompilerParams(
            collective_id=number, has_side_effects=True, vmem_limit_bytes=56 * 2**20
        ),
        cost_estimate=pl.CostEstimate(flops=10**6, bytes_accessed=10**5, transcendentals=0),
        name="opening",
    )(*operands)


def inverse_rms(values):
    return lax.rsqrt(jnp.mean(values * values, -1, keepdims=True) + EPS_NORM)


def hidden_rows(own, sums, extras, outs):
    tokens, gain = extras
    hidden = tokens[own, :].astype(jnp.float32) + sums
    outs[0][own, :] = hidden
    return (hidden * inverse_rms(hidden) * gain[...]).astype(jnp.bfloat16)


def grad_hidden_rows(own, sums, extras, outs):
    hidden, out_grad, gain = extras
    values = hidden[own, :]
    factor = inverse_rms(values)
    unit = values * factor
    outs[1][...] += jnp.sum(sums * unit, 0, keepdims=True)
    grad = out_grad[own, :].astype(jnp.float32) + norm_back(sums * gain[...], unit, factor)
    outs[0][own, :] = grad
    return grad.astype(jnp.bfloat16)


def grad_input_rows(own, sums, extras, outs):
    tokens, grad_hidden, gain = extras[:3]
    values = tokens[own, :].astype(jnp.float32)
    factor = inverse_rms(values)
    unit = values * factor
    outs[0][...] += jnp.sum(sums * unit, 0, keepdims=True)
    return (grad_hidden[own, :] + norm_back(sums * gain[...], unit, factor)).astype(jnp.bfloat16)


def dot(left, right, left_dim=1, right_dim=0):
    return lax.dot_general(
        left, right, (((left_dim,), (right_dim,)), ((), ())), preferred_element_type=jnp.float32
    )


def turn_head(values, cosine, signed_sine):
    return values * cosine + pltpu.roll(values, HEAD // 2, 1) * signed_sine


def turn_back(gradient, cosine, signed_sine):
    return gradient * cosine + pltpu.roll(gradient * signed_sine, HEAD // 2, 1)


def softmax_block(query, key, first_row):
    rows, keys = query.shape[0], key.shape[0]
    scores = dot(query, key, 1, 1)
    row_at = lax.broadcasted_iota(jnp.int32, (rows, keys), 0) + first_row
    key_at = lax.broadcasted_iota(jnp.int32, (rows, keys), 1)
    scores = jnp.where(key_at <= row_at, scores, -1000000000.0)
    exponent = jnp.exp(scores - jnp.max(scores, -1, keepdims=True))
    return exponent / jnp.sum(exponent, -1, keepdims=True)


def eighth_owners():
    _, side, row, _ = place_here()
    own, off = (row, side), (1 - row, 1 - side)
    first = lambda x, y: x * 2 + y
    second = lambda x, y: 4 + y * 2 + x
    return [
        first(own[0], own[1]),
        first(own[0], off[1]),
        second(own[0], own[1]),
        second(off[0], own[1]),
        first(off[0], own[1]),
        first(off[0], off[1]),
        second(own[0], off[1]),
        second(off[0], off[1]),
    ]


def reorder_rows(source, target, into_local):
    size = source.shape[0] // 8
    for slot, owner in enumerate(eighth_owners()):
        natural = pl.ds(pl.multiple_of(owner * size, size), size)
        local = pl.ds(slot * size, size)
        if into_local:
            target[local, :] = source[natural, :]
        else:
            target[natural, :] = source[local, :]


def forward_kernel(
    tokens, weights, gain_in, gain_q, gain_k, cosine, sine,
    normed, raw, query, key, value, local, attended,
):
    low = jnp.bfloat16
    total, heads = tokens.shape[0], query.shape[1] // HEAD
    block, wide = 256, 512

    def project(step, carry):
        rows = pl.ds(pl.multiple_of(step * wide, wide), wide)
        values = tokens[rows, :].astype(jnp.float32)
        normed[rows, :] = (values * inverse_rms(values) * gain_in[...]).astype(low)
        raw[rows, :] = dot(normed[rows, :], weights[...])
        turns = (cosine[rows, :], sine[rows, :])
        for head in range(heads):
            column = (head // 2) * 4 * HEAD + (head % 2) * HEAD
            values = raw[rows, pl.ds(column, HEAD)]
            values = turn_head(values * inverse_rms(values) * gain_q[...], *turns)
            query[rows, pl.ds(head * HEAD, HEAD)] = (values * (1.0 / math.sqrt(HEAD))).astype(low)
        for group in range(heads // 2):
            column = group * 4 * HEAD + 2 * HEAD
            here = pl.ds(group * HEAD, HEAD)
            values = raw[rows, pl.ds(column, HEAD)]
            values = turn_head(values * inverse_rms(values) * gain_k[...], *turns)
            key[rows, here] = values.astype(low)
            value[rows, here] = raw[rows, pl.ds(column + HEAD, HEAD)].astype(low)
        return carry

    lax.fori_loop(0, total // wide, project, 0)

    def attend(head, carry):
        mine = pl.ds(pl.multiple_of(head * HEAD, HEAD), HEAD)
        shared = pl.ds(pl.multiple_of(lax.div(head, 2) * HEAD, HEAD), HEAD)
        for start in range(0, total, SEQ):
            for first in range(0, SEQ, block):
                rows, keys = pl.ds(start + first, block), pl.ds(start, first + block)
                probs = softmax_block(query[rows, mine], key[keys, shared], first)
                attended[rows, mine] = dot(probs.astype(low), value[keys, shared]).astype(low)
        return carry

    lax.fori_loop(0, heads, attend, 0)
    reorder_rows(attended, local, True)


def attention(tokens, weights, gain_in, gain_q, gain_k, cosine, sine):
    total = tokens.shape[0]
    columns = weights.shape[1]
    low = jnp.bfloat16
    shape = lambda width, kind=low: jax.ShapeDtypeStruct((total, width), kind)
    vmem = pl.BlockSpec(memory_space=pltpu.VMEM)
    return pl.pallas_call(
        forward_kernel,
        out_shape=[
            shape(tokens.shape[1]),
            shape(columns, jnp.float32),
            shape(columns // 2),
            shape(columns // 4),
            shape(columns // 4),
            shape(columns // 2),
        ],
        in_specs=[vmem] * 7,
        out_specs=[vmem] * 6,
        scratch_shapes=[pltpu.VMEM((total, columns // 2), low)],
        compiler_params=pltpu.CompilerParams(vmem_limit_bytes=48 * 2**20),
        cost_estimate=pl.CostEstimate(flops=10**6, bytes_accessed=10**5, transcendentals=0),
        name="attention",
    )(tokens, weights, gain_in, gain_q, gain_k, cosine, sine)


def backward_kernel(
    query, key, value, raw, grad_rows, gain_q, gain_k, cosine, sine,
    mixed, mixed_local, query_gain, key_gain, grad, key_sum, value_sum,
):
    low = jnp.bfloat16
    total, heads = query.shape[0], query.shape[1] // HEAD
    block = 256
    reorder_rows(grad_rows, grad, False)
    query_gain[...] = jnp.zeros_like(query_gain)
    key_gain[...] = jnp.zeros_like(key_gain)

    def head_norm_back(rows, column, gradient, gain, gain_grad):
        values = raw[rows, column]
        factor = inverse_rms(values)
        unit = values * factor
        turned = turn_back(gradient, cosine[rows, :], sine[rows, :])
        gain_grad[...] += jnp.sum(turned * unit, 0, keepdims=True)
        mixed[rows, column] = norm_back(turned * gain[...], unit, factor).astype(low)

    def one_group(group, carry):
        at = lambda offset: pl.ds(pl.multiple_of(group * 4 * HEAD + offset * HEAD, HEAD), HEAD)
        shared = pl.ds(pl.multiple_of(group * HEAD, HEAD), HEAD)
        key_sum[...] = jnp.zeros_like(key_sum)
        value_sum[...] = jnp.zeros_like(value_sum)
        for head in (0, 1):
            mine = pl.ds(pl.multiple_of((group * 2 + head) * HEAD, HEAD), HEAD)
            for start in range(0, total, SEQ):
                for first in range(0, SEQ, block):
                    rows, keys = pl.ds(start + first, block), pl.ds(start, first + block)
                    query_part, grad_part = query[rows, mine], grad[rows, mine]
                    probs = softmax_block(query_part, key[keys, shared], first)
                    weighed = probs * dot(grad_part, value[keys, shared], 1, 1)
                    scores = weighed - probs * jnp.sum(weighed, -1, keepdims=True)
                    scores = scores.astype(low)
                    grad_query = dot(scores, key[keys, shared]) * (1.0 / math.sqrt(HEAD))
                    head_norm_back(rows, at(head), grad_query, gain_q, query_gain)
                    key_sum[keys, :] += dot(scores, query_part, 0, 0)
                    value_sum[keys, :] += dot(probs.astype(low), grad_part, 0, 0)
        for first in range(0, total, block):
            rows = pl.ds(first, block)
            head_norm_back(rows, at(2), key_sum[rows, :], gain_k, key_gain)
            mixed[rows, at(3)] = value_sum[rows, :].astype(low)
        return carry

    lax.fori_loop(0, heads // 2, one_group, 0)
    reorder_rows(mixed, mixed_local, True)


def attention_back(query, key, value, raw, grad_rows, gain_q, gain_k, cosine, sine):
    total, columns = raw.shape
    low = jnp.bfloat16
    vmem = pl.BlockSpec(memory_space=pltpu.VMEM)
    return pl.pallas_call(
        backward_kernel,
        out_shape=[
            jax.ShapeDtypeStruct((total, columns), low),
            jax.ShapeDtypeStruct((total, columns), low),
            jax.ShapeDtypeStruct((1, HEAD), jnp.float32),
            jax.ShapeDtypeStruct((1, HEAD), jnp.float32),
        ],
        in_specs=[vmem] * 9,
        out_specs=[vmem] * 4,
        scratch_shapes=[
            pltpu.VMEM(grad_rows.shape, low),
            pltpu.VMEM((total, HEAD), jnp.float32),
            pltpu.VMEM((total, HEAD), jnp.float32),
        ],
        compiler_params=pltpu.CompilerParams(vmem_limit_bytes=48 * 2**20),
        cost_estimate=pl.CostEstimate(flops=10**6, bytes_accessed=10**5, transcendentals=0),
        name="attention_back",
    )(query, key, value, raw, grad_rows, gain_q, gain_k, cosine, sine)


def feed_kernel(plan, rows, own_grad, got_grad, gate_up, up_part, down, active, grads, out_grad):
    low = jnp.bfloat16
    block = 512
    tile = down.shape[1]
    step = pl.program_id(0)
    gate_at = pl.ds(pl.multiple_of(step * tile, tile), tile)
    up_at = pl.ds(pl.multiple_of(grads.shape[1] // 2 + step * tile, tile), tile)
    _, side, _, core = place_here()

    def lay_down(source):
        natural, blocks = block_columns(plan, source.shape[1])
        eighth = source.shape[0] // 8
        for slot, owner in enumerate(eighth_owners()):

            def some(start, count, slot=slot, owner=owner):
                here = pl.ds(pl.multiple_of(owner * eighth + start, 32), count)
                there = pl.ds(slot * eighth + start, count)
                for a, b in zip(natural, blocks):
                    out_grad[there, b] = source[here, a]

            for_rows(eighth, some)

    @pl.when((step == 0) & (side == core))
    def _():
        lay_down(own_grad)

    @pl.when((step == 0) & (side != core))
    def _():
        lay_down(got_grad)

    def one(block_at, carry):
        here = pl.ds(pl.multiple_of(block_at * block, block), block)
        gate = dot(rows[here, :], gate_up[...])
        up = dot(rows[here, :], up_part[...])
        grad = dot(out_grad[here, :], down[...])
        sigmoid = jax.nn.sigmoid(gate)
        silu = gate * sigmoid
        active[here, :] = (silu * up).astype(low)
        grads[here, gate_at] = (grad * up * sigmoid * (1.0 + gate * (1.0 - sigmoid))).astype(low)
        grads[here, up_at] = (grad * silu).astype(low)
        return carry

    lax.fori_loop(0, rows.shape[0] // block, one, 0)


def feed_forward(plan, rows, own_grad, got_grad, gate_up, down, tile):
    total, width = rows.shape
    units = down.shape[1]
    low = jnp.bfloat16
    tiles = units // tile
    whole = pl.BlockSpec(memory_space=pltpu.VMEM)
    return pl.pallas_call(
        functools.partial(feed_kernel, plan),
        grid=(tiles,),
        out_shape=[
            jax.ShapeDtypeStruct((total, units), low),
            jax.ShapeDtypeStruct((total, 2 * units), low),
            jax.ShapeDtypeStruct((total, width), low),
        ],
        in_specs=[
            whole,
            whole,
            whole,
            pl.BlockSpec((width, tile), lambda step: (0, step)),
            pl.BlockSpec((width, tile), lambda step: (0, step + tiles)),
            pl.BlockSpec((width, tile), lambda step: (0, step)),
        ],
        out_specs=[
            pl.BlockSpec((total, tile), lambda step: (0, step)),
            whole,
            whole,
        ],
        compiler_params=pltpu.CompilerParams(vmem_limit_bytes=56 * 2**20),
        cost_estimate=pl.CostEstimate(
            flops=6 * total * width * units, bytes_accessed=4 * 10**7, transcendentals=total * units
        ),
        name="feed_forward",
    )(rows, own_grad, got_grad, gate_up, gate_up, down)


class Plan:
    def __init__(self, mesh):
        self.total = mesh.shape["dp"]
        self.zones = self.total // 2
        self.tensor = mesh.shape["tensor"]
        self.flips = [k ^ (k >> 1) for k in range(self.zones)]

    def place(self):
        self.index = lax.axis_index("dp")
        self.zone = self.index // 2
        self.side = self.index % 2
        self.row = lax.axis_index("tensor") // 2
        self.core = lax.axis_index("tensor") % 2
        self.home = self.side == self.core

    def move(self, value, target):
        pairs = []
        for d in range(self.total):
            for t in range(self.tensor):
                to = target(d // 2, d % 2, t // 2, t % 2)
                if to is not None:
                    zone, side, row, core = to
                    pairs.append((d * self.tensor + t, (zone * 2 + side) * self.tensor + row * 2 + core))
        return lax.ppermute(value, ("dp", "tensor"), pairs)

    def turn(self, value):
        got = self.move(value, lambda z, y, x, c: (z, c, x, y) if y != c else None)
        return jnp.where(self.home, value, got)

    def zone_flip(self, value, bit):
        return self.move(value, lambda z, y, x, c: (z ^ bit, y, x, c))

    def core_swap(self, value):
        return self.move(value, lambda z, y, x, c: (z, y, x, 1 - c))

    def side_swap(self, value):
        return self.move(value, lambda z, y, x, c: (z, 1 - y, x, c))

    def row_swap(self, value):
        return self.move(value, lambda z, y, x, c: (z, y, 1 - x, c))

    def to_local(self, value, axis):
        width = value.shape[axis] // self.total
        parts = []
        for core in (self.core, 1 - self.core):
            for slot in range(self.zones):
                owner = (self.zone ^ self.flips[slot]) * 2 + core
                parts.append(lax.dynamic_slice_in_dim(value, owner * width, width, axis))
        return jnp.concatenate(parts, axis)

    def to_natural(self, value, axis, core=None):
        core = self.core if core is None else core
        width = value.shape[axis] // self.total
        parts = []
        for block in range(self.total):
            slot = flip = (block // 2) ^ self.zone
            for bits in range(1, self.zones.bit_length()):
                slot = slot ^ (flip >> bits)
            slot = slot + jnp.where(block % 2 == core, 0, self.zones)
            parts.append(lax.dynamic_slice_in_dim(value, slot * width, width, axis))
        return jnp.concatenate(parts, axis)

    def row_owners(self):
        own, off = (self.row, self.side), (1 - self.row, 1 - self.side)
        first = lambda x, y: x * 2 + y
        second = lambda x, y: 4 + y * 2 + x
        return [
            first(own[0], own[1]),
            first(own[0], off[1]),
            second(own[0], own[1]),
            second(off[0], own[1]),
            first(off[0], own[1]),
            first(off[0], off[1]),
            second(own[0], off[1]),
            second(off[0], off[1]),
        ]

    def rows_local(self, value, slots=range(8)):
        size = value.shape[0] // 8
        owners = self.row_owners()
        return jnp.concatenate(
            [lax.dynamic_slice_in_dim(value, owners[slot] * size, size, 0) for slot in slots], 0
        )

    def rows_natural(self, value, order=range(8)):
        size = value.shape[0] // 8
        place = [list(order).index(slot) for slot in range(8)]
        parts = []
        for piece in range(8):
            x, y = (piece // 2, piece % 2) if piece < 4 else (piece % 2, (piece - 4) // 2)
            slots = (0, 1, 4, 5) if piece < 4 else (2, 6, 3, 7)
            same_x, same_y = x == self.row, y == self.side
            slot = jnp.where(
                same_x,
                jnp.where(same_y, place[slots[0]], place[slots[1]]),
                jnp.where(same_y, place[slots[2]], place[slots[3]]),
            )
            parts.append(lax.dynamic_slice_in_dim(value, slot * size, size, 0))
        return jnp.concatenate(parts, 0)

    def from_zones(self, shard):
        return [self.zone_flip(shard, flip) for flip in self.flips[1:]]

    def to_zones(self, parts, slots):
        return [self.zone_flip(parts[slot], self.flips[slot]) for slot in slots]

    def middle_swap(self, pair):
        return self.move(pair, lambda z, y, x, c: (z ^ 3, y, x, c) if z in (1, 2) else None)

    def inward(self, part):
        return self.move(part, lambda z, y, x, c: (z ^ 1, y, x, c) if z in (0, 3) else None)

    def pass_outward(self, pair):
        return self.move(pair, lambda z, y, x, c: (z ^ 1, y, x, c) if z in (1, 2) else None)

    def far_pair(self, middle, passed):
        inner = (self.zone == 1) | (self.zone == 2)
        return jnp.where(inner, middle, passed[::-1])

    def first_swap(self, send):
        half = send.shape[0] // 2
        return self.row_swap(send[:half]), self.side_swap(send[half:])

    def second_swap(self, keep, got):
        quarter = keep.shape[0] // 4
        row_part = keep[: 2 * quarter] + got[0].astype(jnp.float32)
        side_part = keep[2 * quarter :] + got[1].astype(jnp.float32)
        own = jnp.concatenate([row_part[:quarter], side_part[:quarter]], 0)
        return own, (
            self.side_swap(row_part[quarter:].astype(jnp.bfloat16)),
            self.row_swap(side_part[quarter:].astype(jnp.bfloat16)),
        )

    def spread_first(self, own):
        half = own.shape[0] // 2
        return (self.side_swap(own[:half]), self.row_swap(own[half:]))

    def spread_second(self, own, got):
        half = own.shape[0] // 2
        row_part = jnp.concatenate([own[:half], got[0]], 0)
        side_part = jnp.concatenate([own[half:], got[1]], 0)
        return row_part, side_part, self.row_swap(row_part), self.side_swap(side_part)

    def send_home(self, own):
        to_home = lambda z, y, x, c: (z, c, x, c) if y != c else None
        return jnp.concatenate([own, self.move(own, to_home)], 0)

    def row_home(self, part):
        return self.move(part, lambda z, y, x, c: (z, y, 1 - x, c) if y == c else None)

    def share_home(self, part, other):
        full = jnp.concatenate([part, other], 0)
        full = self.to_natural(self.rows_natural(full, (0, 2, 1, 6, 4, 3, 5, 7)), 1)
        got = self.move(full, lambda z, y, x, c: (z, y, x, 1 - c) if y == c else None)
        return full, got

    def turned(self, own, got):
        return jnp.where(self.home, own, got)

    def sum_everywhere(self, value):
        value = value + self.row_swap(value)
        value = value + self.side_swap(value)
        value = value + self.core_swap(value)
        bit = 1
        while bit < self.zones:
            value = value + self.zone_flip(value, bit)
            bit *= 2
        return value


def shards(
    plan,
    tokens,
    positions,
    out_grad,
    qkv_weight,
    qkv_first,
    qkv_second,
    out_weight,
    out_first,
    out_second,
    gate_up,
    gate_up_first,
    gate_up_second,
    down_weight,
    down_first,
    down_second,
    gains,
    gains_first,
    gains_second,
):
    plan.place()
    low = jnp.bfloat16
    tok_rows, model_width = tokens.shape
    groups = qkv_weight.shape[1]
    head_size = qkv_weight.shape[3]
    shard_rows = qkv_weight.shape[0]
    seq_count = tok_rows // SEQ
    mixed_cols = groups * 4 * head_size
    near_cols = model_width // 2
    kept = tok_rows // 2
    gain_count = gains.shape[0]

    tree = plan.zones == 4
    slots = range(1, plan.zones)

    def column_parts(value):
        return value.reshape((plan.zones, -1) + value.shape[1:])

    units = gate_up.shape[2]
    plan.ordered = (model_width // plan.total) % 128 == 0
    gain_rows = 16
    gain_block = jnp.pad(gains.astype(low), (0, gain_rows * 128 - gain_count)).reshape(gain_rows, 128)
    tile = min(units, 256)
    angle_at = positions.astype(jnp.float32).reshape(-1, 128)
    both_qkv, both_gains, turned_gate, turned_out, turned_down, tokens, angle_at, partner_gate = opening(
        plan,
        qkv_weight.reshape(shard_rows, mixed_cols),
        gain_block,
        gate_up,
        out_weight,
        down_weight,
        tokens,
        angle_at,
        3,
    )
    positions = angle_at.reshape(-1)
    turned_out, turned_gate, turned_down, tokens, positions, both_qkv, both_gains, out_grad = fence(
        turned_out, turned_gate, turned_down, tokens, positions, both_qkv, both_gains, out_grad
    )

    got_grad = plan.move(out_grad, lambda z, y, x, c: (z, c, x, y) if y != c else None)
    zone_out = plan.from_zones(turned_out)
    if tree:
        partner_down = plan.zone_flip(turned_down, 1)
    else:
        partner_down = plan.from_zones(turned_down)
        partner_gate = plan.from_zones(turned_gate)
    if not plan.ordered:
        tokens = plan.to_local(tokens, 1)
    cosine, sine_table = rotary(positions, head_size)
    signed_sine = jnp.concatenate(
        [-sine_table[:, : head_size // 2], sine_table[:, head_size // 2 :]], 1
    )
    full_qkv = both_qkv.reshape(model_width, mixed_cols)
    gain_slots = both_gains.reshape(plan.total, -1)[:, :gain_count]
    gain_all = plan.to_natural(gain_slots.reshape(-1), 0).astype(jnp.float32)
    gain_in = plan.to_local(gain_all[:model_width], 0)[None]
    gain_post = plan.to_local(gain_all[model_width : 2 * model_width], 0)[None]
    gain_q = gain_all[2 * model_width : 2 * model_width + head_size][None]
    gain_k = gain_all[2 * model_width + head_size :][None]
    normed, raw, query, key_rot, values_low, attended = attention(
        tokens, full_qkv, gain_in, gain_q, gain_k, cosine, signed_sine
    )
    attended, zone_out, turned_out, turned_down, turned_gate, partner_gate, partner_down = fence(
        attended, zone_out, turned_out, turned_down, turned_gate, partner_gate, partner_down
    )

    near_out = jnp.concatenate([turned_out] + zone_out, 0)
    far_out = plan.core_swap(near_out)
    own_tokens = plan.rows_local(tokens, (0, 2))
    near_out, far_out, own_tokens = fence(near_out, far_out, own_tokens)

    full_out = jnp.concatenate([near_out, far_out], 0)
    branch_terms = contract_cols(attended, full_out).astype(low)
    pairs = [(turned_gate, partner_gate), (turned_down, partner_down)]
    jobs = [PairTree(pairs, (2, 2))] if tree else []
    normed_rows, hidden, *gathered = sum_rows(
        plan,
        spread_kernel,
        hidden_rows,
        branch_terms,
        [own_tokens, gain_post],
        [jax.ShapeDtypeStruct((tok_rows // 4, model_width), jnp.float32)],
        0,
        jobs,
    )
    if not tree:
        near = [jnp.concatenate([own] + rest, 0) for own, rest in pairs]
        gathered = [jnp.concatenate([part, plan.core_swap(part)], 0) for part in near]
    full_gate = gathered[0].reshape(model_width, 2 * units)
    full_down = gathered[1].reshape(model_width, units)
    normed_rows, hidden, full_gate, full_down, got_grad = fence(
        normed_rows, hidden, full_gate, full_down, got_grad
    )

    def zone_parts(near, got):
        both = (near + got.astype(jnp.float32)).astype(low)
        return both.reshape((plan.zones, -1) + both.shape[1:])

    def zone_total(parts, *arrived):
        total = parts[0].astype(jnp.float32)
        for part in sum([list(group) for group in arrived], []):
            total = total + part.astype(jnp.float32)
        return total.astype(low)

    active, grad_both, out_grad = feed_forward(
        plan, normed_rows, out_grad, got_grad, full_gate, full_down, tile
    )
    if not plan.ordered:
        out_grad = plan.to_local(out_grad, 1)
    down_far = contract_rows(out_grad[:, near_cols:], active).astype(low)
    down_far, active, grad_both, out_grad, normed_rows = fence(
        down_far, active, grad_both, out_grad, normed_rows
    )

    down_got = plan.core_swap(down_far)
    gate_far = contract_rows(normed_rows[:, near_cols:], grad_both).astype(low)
    down_parts = zone_parts(contract_rows(out_grad[:, :near_cols], active), down_got)
    gate_far, down_parts, grad_both, normed_rows = fence(
        gate_far, down_parts, grad_both, normed_rows
    )

    gate_got = plan.core_swap(gate_far)
    if tree:
        down_sums = [plan.inward(down_parts[3])]
    else:
        down_sums = plan.to_zones(down_parts, slots)
    post_terms = contract_cols(grad_both, full_gate).astype(low)
    post_terms, gate_got, down_parts, down_sums, grad_both, normed_rows = fence(
        post_terms, gate_got, down_parts, down_sums, grad_both, normed_rows
    )

    if tree:
        down_sums += [plan.inward(down_parts[2])]
    gate_parts = zone_parts(contract_rows(normed_rows[:, :near_cols], grad_both), gate_got)
    post_terms, gate_parts, down_parts, down_sums = fence(
        post_terms, gate_parts, down_parts, down_sums
    )

    eighth = tok_rows // 8
    own_grad = jnp.concatenate([out_grad[:eighth], out_grad[2 * eighth : 3 * eighth]], 0)
    branch_rows, grad_hidden, post_gain_grad, mlp_terms, gate_sums = sum_rows(
        plan,
        spread_kernel,
        grad_hidden_rows,
        post_terms,
        [hidden, own_grad, gain_post],
        [
            jax.ShapeDtypeStruct((tok_rows // 4, model_width), jnp.float32),
            jax.ShapeDtypeStruct((1, model_width), jnp.float32),
        ],
        1,
        [
            SideDot(active, full_down),
            PairScatter(gate_parts, 2) if tree else ZoneBlocks(plan, gate_parts, slots),
        ],
    )
    branch_rows, grad_hidden, post_gain_grad, gate_sums, mlp_terms, down_parts, down_sums = fence(
        branch_rows, grad_hidden, post_gain_grad, gate_sums, mlp_terms, down_parts, down_sums
    )

    mlp_got = plan.first_swap(mlp_terms[kept:])
    if tree:
        gate_last = [plan.zone_flip(gate_sums[1], 1)]
        gate_own = gate_sums
        down_pair = down_parts[2:].astype(jnp.float32) + jnp.stack(down_sums).astype(jnp.float32)
        down_sums = plan.middle_swap(down_pair.astype(low))
    else:
        gate_last, gate_own = gate_sums, gate_parts
    grad_att = jnp.dot(branch_rows, full_out, preferred_element_type=jnp.float32).astype(low)
    grad_mixed, mixed_rows, query_gain_grad, key_gain_grad = attention_back(
        query, key_rot, values_low, raw, grad_att, gain_q, gain_k, cosine, signed_sine
    )
    gain_terms = jnp.concatenate(
        [plan.to_natural(post_gain_grad, 1), query_gain_grad, key_gain_grad], 1
    )
    if tree:
        down_own = (down_parts[:2].astype(jnp.float32) + down_sums.astype(jnp.float32)).astype(low)
    grad_mixed, mixed_rows, gain_terms, normed, gate_last, branch_rows, mlp_got, down_sums = fence(
        grad_mixed, mixed_rows, gain_terms, normed, gate_last, branch_rows, mlp_got, down_sums
    )

    mlp_own, mlp_last = plan.second_swap(mlp_terms[:kept].astype(jnp.float32), mlp_got)
    if tree:
        total_down = zone_total(down_own, [plan.zone_flip(down_own[1], 1)])
    else:
        total_down = zone_total(down_parts, down_sums)
    total_gate = zone_total(gate_own, gate_last)
    total_gate = jnp.concatenate([total_gate[:, :units], total_gate[:, units:]], 0)
    out_far = contract_rows(branch_rows[:, near_cols:], attended).astype(low)
    out_got = plan.core_swap(out_far)
    normed_terms = contract_cols(mixed_rows, full_qkv).astype(low)
    out_parts = zone_parts(contract_rows(branch_rows[:, :near_cols], attended), out_got)
    block_own = (hidden + mlp_own + jnp.concatenate(mlp_last, 0).astype(jnp.float32)).astype(low)
    out_parts, normed_terms, total_gate, total_down, block_own, normed, grad_mixed = fence(
        out_parts, normed_terms, total_gate, total_down, block_own, normed, grad_mixed
    )

    gain_sum = GainSum(plan, gain_terms.shape[1], model_width) if plan.ordered else None
    mine, input_gain_grad, *rest = sum_rows(
        plan,
        home_kernel,
        grad_input_rows,
        normed_terms,
        [own_tokens, grad_hidden, gain_in, block_own] + ([gain_terms] if plan.ordered else []),
        [jax.ShapeDtypeStruct((1, model_width), jnp.float32)],
        2,
        [
            BlockGrad(plan, normed, grad_mixed),
            ZoneBlocks(plan, out_parts, slots),
            TurnLate(total_gate),
            TurnLate(total_down),
        ],
        gain_sum,
    )
    if plan.ordered:
        summed_gains, total_qkv, out_sent, got_gate, got_down = rest
    else:
        total_qkv, out_sent, got_gate, got_down = rest
        summed_gains = plan.sum_everywhere(
            jnp.concatenate([plan.to_natural(input_gain_grad, 1), gain_terms], 1)
        )
    mine, summed_gains, total_qkv, out_sent, got_gate, got_down = fence(
        mine, summed_gains, total_qkv, out_sent, got_gate, got_down
    )

    summed_gate = plan.turned(total_gate, got_gate).reshape(gate_up.shape)
    summed_down = plan.turned(total_down, got_down)
    other = plan.core_swap(mine)
    input_full, block_out = jnp.where(plan.home, mine, other), jnp.where(plan.home, other, mine)
    if not plan.ordered:
        input_full = plan.to_natural(input_full, 1, plan.side)
        block_out = plan.to_natural(block_out, 1, plan.side)
    summed_both = plan.turn(
        jnp.concatenate([total_qkv, zone_total(out_parts, out_sent)], 1)
    ).astype(jnp.float32)
    summed_qkv = summed_both[:, :mixed_cols].reshape(qkv_weight.shape)
    summed_out = summed_both[:, mixed_cols:]
    summed_gate = summed_gate.astype(jnp.float32)
    summed_down = summed_down.astype(jnp.float32)
    summed_gains = lax.dynamic_slice_in_dim(summed_gains[0], plan.index * gain_count, gain_count, 0)
    input_rows = input_full.astype(jnp.float32)

    qkv_moment, qkv_square, qkv_updated = adamw(
        qkv_weight, summed_qkv, qkv_first, qkv_second, RATE_QKV, DECAY_RATE
    )
    out_moment, out_square, out_updated = adamw(
        out_weight, summed_out, out_first, out_second, RATE_OUT, DECAY_RATE
    )
    gate_moment, gate_square, gate_updated = adamw(
        gate_up, summed_gate, gate_up_first, gate_up_second, RATE_GATE, DECAY_RATE
    )
    down_moment, down_square, down_updated = adamw(
        down_weight, summed_down, down_first, down_second, RATE_DOWN, DECAY_RATE
    )
    gain_moment, gain_square, gain_updated = adamw(
        gains, summed_gains, gains_first, gains_second, RATE_GAIN, 0.0
    )
    return (
        block_out,
        input_rows,
        qkv_moment,
        qkv_square,
        qkv_updated,
        out_moment,
        out_square,
        out_updated,
        gate_moment,
        gate_square,
        gate_updated,
        down_moment,
        down_square,
        down_updated,
        gain_moment,
        gain_square,
        gain_updated,
    )


def solution(mesh):
    plan = Plan(mesh)
    placed = (
        P("dp", None),
        P("dp"),
        P("dp", None),
        P("dp", "tensor", None, None),
        P("dp", "tensor", None, None),
        P("dp", "tensor", None, None),
        P("dp", "tensor"),
        P("dp", "tensor"),
        P("dp", "tensor"),
        P(None, "dp", "tensor"),
        P(None, "dp", "tensor"),
        P(None, "dp", "tensor"),
        P("dp", "tensor"),
        P("dp", "tensor"),
        P("dp", "tensor"),
        P("dp"),
        P("dp"),
        P("dp"),
    )
    return jax.shard_map(
        functools.partial(shards, plan),
        mesh=mesh,
        in_specs=placed,
        out_specs=(
            P("dp", None),
            P("dp", None),
            P("dp", "tensor", None, None),
            P("dp", "tensor", None, None),
            P("dp", "tensor", None, None),
            P("dp", "tensor"),
            P("dp", "tensor"),
            P("dp", "tensor"),
            P(None, "dp", "tensor"),
            P(None, "dp", "tensor"),
            P(None, "dp", "tensor"),
            P("dp", "tensor"),
            P("dp", "tensor"),
            P("dp", "tensor"),
            P("dp"),
            P("dp"),
            P("dp"),
        ),
        check_vma=False,
    )
```

```python
import functools
import math

import jax
import jax.numpy as jnp
from jax import lax
from jax.experimental import pallas as pl
from jax.experimental.pallas import tpu as pltpu
from jax.sharding import PartitionSpec as P

SEQ = 1024
STEP = 10


EPS_NORM = 1e-06
THETA = 1000000.0
BETA_ONE = 0.9
BETA_TWO = 0.95
ADAM_EPS = 1e-08
DECAY_RATE = 0.1
RATE_QKV = 0.05
RATE_OUT = 0.3
RATE_GATE = 0.05
RATE_DOWN = 0.03
RATE_GAIN = 1.0


def rotary(positions, head_size):
    freq_index = jnp.arange(head_size // 2, dtype=jnp.float32)
    inverse = jnp.exp(freq_index * (-2.0 * math.log(THETA) / head_size))
    angles = positions.astype(jnp.float32)[:, None] * inverse[None, :]
    cosine = jnp.cos(angles)
    sine_table = jnp.sin(angles)
    return (jnp.concatenate([cosine, cosine], -1), jnp.concatenate([sine_table, sine_table], -1))


def rotate(values, cosine, sine_table):
    half_size = values.shape[-1] // 2
    turned = jnp.concatenate([-values[..., half_size:], values[..., :half_size]], -1)
    return values * cosine[:, None, :] + turned * sine_table[:, None, :]


def unrotate(gradient, cosine, sine_table):
    half_size = gradient.shape[-1] // 2
    turned = gradient * sine_table[:, None, :]
    rotated_back = jnp.concatenate([turned[..., half_size:], -turned[..., :half_size]], -1)
    return gradient * cosine[:, None, :] + rotated_back


def norm_back(grad_unit, unit_vals, factor):
    return factor * (grad_unit - unit_vals * jnp.mean(grad_unit * unit_vals, -1, keepdims=True))


def contract_rows(left, right):
    return lax.dot_general(
        left, right, (((0,), (0,)), ((), ())), preferred_element_type=jnp.float32
    )


def contract_cols(left, right):
    return lax.dot_general(
        left, right, (((1,), (1,)), ((), ())), preferred_element_type=jnp.float32
    )


def block_scores(query_part, key_part, first_row, block_rows, last_row):
    scores = jnp.einsum(
        "nqkgd,nskd->nkgqs", query_part, key_part, preferred_element_type=jnp.float32
    )
    causal = (first_row + jnp.arange(block_rows))[:, None] >= jnp.arange(last_row)[None, :]
    return jnp.where(causal, scores, -1000000000.0)


def attention_forward(query, key_rot, values_low, seq_len):
    block_rows = min(512, seq_len)
    outputs = []
    log_sums = []
    for first_row in range(0, seq_len, block_rows):
        last_row = first_row + block_rows
        query_part = query[:, first_row:last_row]
        scores = block_scores(query_part, key_rot[:, :last_row], first_row, block_rows, last_row)
        row_max = jnp.max(scores, -1, keepdims=True)
        exponent = jnp.exp(scores - row_max)
        row_total = jnp.sum(exponent, -1, keepdims=True)
        probs_low = (exponent / row_total).astype(jnp.bfloat16)
        outputs.append(
            jnp.einsum(
                "nkgqs,nskd->nqkgd",
                probs_low,
                values_low[:, :last_row],
                preferred_element_type=jnp.float32,
            )
        )
        log_sums.append(row_max + jnp.log(row_total))
    return (jnp.concatenate(outputs, 1), log_sums)


def attention_backward(query, key_rot, values_low, grad_att, log_sums, seq_len):
    block_rows = min(512, seq_len)
    query_grads = []
    key_grad = jnp.zeros(key_rot.shape, jnp.float32)
    value_grad = jnp.zeros(values_low.shape, jnp.float32)
    for block_index, first_row in enumerate(range(0, seq_len, block_rows)):
        last_row = first_row + block_rows
        query_part = query[:, first_row:last_row]
        grad_part = grad_att[:, first_row:last_row]
        key_part = key_rot[:, :last_row]
        value_part = values_low[:, :last_row]
        scores = block_scores(query_part, key_part, first_row, block_rows, last_row)
        probs = jnp.exp(scores - log_sums[block_index])
        probs_low = probs.astype(jnp.bfloat16)
        grad_probs = jnp.einsum(
            "nqkgd,nskd->nkgqs", grad_part, value_part, preferred_element_type=jnp.float32
        )
        grad_scores = (
            probs * (grad_probs - jnp.sum(probs * grad_probs, -1, keepdims=True))
        ).astype(jnp.bfloat16)
        query_grads.append(
            jnp.einsum(
                "nkgqs,nskd->nqkgd", grad_scores, key_part, preferred_element_type=jnp.float32
            )
        )
        padding = ((0, 0), (0, seq_len - last_row), (0, 0), (0, 0))
        key_grad = key_grad + jnp.pad(
            jnp.einsum(
                "nkgqs,nqkgd->nskd", grad_scores, query_part, preferred_element_type=jnp.float32
            ),
            padding,
        )
        value_grad = value_grad + jnp.pad(
            jnp.einsum(
                "nkgqs,nqkgd->nskd", probs_low, grad_part, preferred_element_type=jnp.float32
            ),
            padding,
        )
    return (jnp.concatenate(query_grads, 1), key_grad, value_grad)


def adamw(weight, gradient, moment, second, step_rate, decay_rate):
    moment = BETA_ONE * moment + (1.0 - BETA_ONE) * gradient
    second = BETA_TWO * second + (1.0 - BETA_TWO) * gradient * gradient
    first_hat = moment / (1.0 - BETA_ONE**STEP)
    second_hat = second / (1.0 - BETA_TWO**STEP)
    weight = weight - step_rate * (
        first_hat / (jnp.sqrt(second_hat) + ADAM_EPS) + decay_rate * weight
    )
    return (moment, second, weight)


def fence(*values):
    return lax.optimization_barrier(values)


MESH = pl.DeviceIdType.MESH
HEAD = 128
AHEAD = 2


def place_here():
    index, place = lax.axis_index("dp"), lax.axis_index("tensor")
    return lax.div(index, 2), lax.rem(index, 2), lax.div(place, 2), lax.rem(place, 2)


def device(zone, side, row, core):
    return (zone * 2 + side, row * 2 + core)


def flipped(zone, flip):
    bit = 1
    while bit <= flip:
        if flip & bit:
            zone = zone + bit - 2 * bit * lax.rem(lax.div(zone, bit), 2)
        bit *= 2
    return zone


def greet(devices, amount=None):
    barrier = pltpu.get_barrier_semaphore()
    for peer in devices:
        pl.semaphore_signal(barrier, inc=1, device_id=peer, device_id_type=MESH)
    pl.semaphore_wait(barrier, len(devices) if amount is None else amount)


def for_rows(count, body):
    step = 32

    def one(block, carry):
        body(pl.multiple_of(block * step, step), step)
        return carry

    lax.fori_loop(0, count // step, one, 0)


class Copies:
    def __init__(self, send_sems, recv_sems):
        self.send_sems, self.recv_sems = send_sems, recv_sems
        self.number = 0

    def make(self, source, target, peer):
        number, self.number = self.number, self.number + 1
        return pltpu.make_async_remote_copy(
            src_ref=source,
            dst_ref=target,
            send_sem=self.send_sems.at[number],
            recv_sem=self.recv_sems.at[number],
            device_id=peer,
            device_id_type=MESH,
        )

    def start(self, source, target, peer):
        copy = self.make(source, target, peer)
        copy.start()
        return copy


class GainSum:
    def __init__(self, plan, rest, width):
        self.plan, self.width = plan, width
        self.total = width + rest
        self.scratch = [
            pltpu.VMEM((8, 1, self.total), jnp.float32),
            pltpu.VMEM((plan.zones, 1, self.total), jnp.float32),
        ]
        self.output = jax.ShapeDtypeStruct((1, self.total), jnp.float32)
        self.count = 7 + plan.zones - 1

    def plane_peers(self, zone, side, row, core):
        steps = [(s, r, c) for s in range(2) for r in range(2) for c in range(2)][1:]
        turn = lambda value, step: 1 - value if step else value
        return [device(zone, turn(side, s), turn(row, r), turn(core, c)) for s, r, c in steps]

    def zone_peers(self, zone, side, row, core):
        return {flip: device(flipped(zone, flip), side, row, core) for flip in self.plan.flips[1:]}

    def start(self, copies, rest, blocks, plane_sums, zone_sums):
        zone, side, row, core = place_here()
        plan = self.plan
        size = self.width // plan.total
        self.copies, self.plane_sums, self.zone_sums, self.zone = copies, plane_sums, zone_sums, zone
        here = side * 4 + row * 2 + core
        plane_sums[here, :, pl.ds(self.width, self.total - self.width)] = rest[...]
        for slot in range(plan.total):
            owner = flipped(zone, plan.flips[slot % plan.zones]) * 2
            owner = owner + (core if slot < plan.zones else 1 - core)
            spot = pl.ds(pl.multiple_of(owner * size, size), size)
            plane_sums[here, :, spot] = blocks[:, pl.ds(slot * size, size)]
        self.plane = [
            copies.start(plane_sums.at[here], plane_sums.at[here], peer)
            for peer in self.plane_peers(zone, side, row, core)
        ]

    def middle(self):
        for copy in self.plane:
            copy.wait_recv()
        total = self.plane_sums[0]
        for place in range(1, 8):
            total = total + self.plane_sums[place]
        self.zone_sums[self.zone] = total
        zone, side, row, core = place_here()
        self.across = [
            self.copies.start(self.zone_sums.at[self.zone], self.zone_sums.at[self.zone], peer)
            for peer in self.zone_peers(zone, side, row, core).values()
        ]

    def finish(self, out):
        for copy in self.across:
            copy.wait_recv()
        total = self.zone_sums[0]
        for place in range(1, self.plan.zones):
            total = total + self.zone_sums[place]
        out[...] = total
        for copy in self.plane + self.across:
            copy.wait_send()


class ZoneBlocks:
    scratch = []

    def __init__(self, plan, source, slots, begin=0):
        self.flips, self.slots, self.sources, self.begin = plan.flips, list(slots), [source], begin
        self.outputs = [
            jax.ShapeDtypeStruct((len(self.slots),) + source.shape[1:], source.dtype)
        ]
        self.count, self.count_local = len(self.slots), 0
        self.in_hbm = False

    def peers(self, zone, side, row, core):
        return {
            self.flips[slot]: device(flipped(zone, self.flips[slot]), side, row, core)
            for slot in self.slots
        }

    def start(self, copies, local_sems, sources, targets, stages):
        zone, side, row, core = place_here()
        self.started = [
            copies.make(
                sources[0].at[slot],
                targets[0].at[number],
                device(flipped(zone, self.flips[slot]), side, row, core),
            )
            for number, slot in enumerate(self.slots)
        ]
        self.waiting = True
        if self.begin == 0:
            self.pump([0])

    def pump(self, steps):
        if self.waiting and self.begin in steps:
            self.waiting = False
            for copy in self.started:
                copy.start()

    def finish(self):
        for copy in self.started:
            copy.wait_send()
        for copy in self.started:
            copy.wait_recv()


def due(point, early, total):
    if 0 in point:
        return range(early)
    return range(early, early + 1) if 1 in point else range(early + 1, total)


def inner_zone(zone):
    return lax.rem(lax.div(zone + 1, 2), 2)


class SideDot:
    count, count_local, scratch, in_hbm = 0, 0, [], False

    def __init__(self, left, right):
        self.sources = [left, right]
        self.outputs = [jax.ShapeDtypeStruct((left.shape[0], right.shape[0]), jnp.bfloat16)]

    def peers(self, zone, side, row, core):
        return {}

    def some(self, first, last):
        left, right = self.refs
        size = 256

        def one(step, carry):
            here = pl.ds(pl.multiple_of(step * size, size), size)
            self.out[:, here] = dot(left[...], right[here, :], 1, 1).astype(jnp.bfloat16)
            return carry

        lax.fori_loop(first, last, one, 0)

    def start(self, copies, local_sems, sources, targets, stages):
        self.refs, self.out = sources, targets[0]
        self.steps = self.out.shape[1] // 256
        self.some(0, self.steps // 2)

    def pump(self, steps):
        if 0 in steps:
            self.some(self.steps // 2, self.steps)

    def finish(self):
        pass


class PairScatter:
    def __init__(self, parts):
        self.sources = [parts]
        _, rows, columns = parts.shape
        self.outputs = [jax.ShapeDtypeStruct((2, rows, columns), parts.dtype)]
        self.scratch = [pltpu.VMEM((2, rows, columns), parts.dtype)] * 2
        self.count, self.count_local = 14, 0
        self.in_hbm = False

    def peers(self, zone, side, row, core):
        return {
            1: device(flipped(zone, 1), side, row, core),
            3: device(flipped(zone, 3), side, row, core),
        }

    def start(self, copies, local_sems, sources, targets, stages):
        zone, side, row, core = place_here()
        self.parts, self.out = sources[0], targets[0]
        self.inward, self.crossed = stages
        inner_peer = device(flipped(zone, 3), side, row, core)
        outer_peer = device(flipped(zone, 1), side, row, core)
        self.inner = inner_zone(zone) == 1
        self.outer = inner_zone(zone) == 0
        rows = self.parts.shape[1]
        cuts = ((0, (rows // 4, rows // 4, rows // 2)), (1, (rows // 4,) * 4))
        self.steps = [
            (slot, pl.ds(sum(sizes[:place]), size))
            for slot, sizes in cuts
            for place, size in enumerate(sizes)
        ]
        self.to_inner = [
            copies.make(self.parts.at[3 - slot, rows], self.inward.at[slot, rows], outer_peer)
            for slot, rows in self.steps
        ]
        self.across = [
            copies.make(self.inward.at[slot, rows], self.crossed.at[slot, rows], inner_peer)
            for slot, rows in self.steps
        ]

        @pl.when(self.outer)
        def _():
            for copy in self.to_inner[:AHEAD]:
                copy.start()

    def add(self, target, slot, rows, left, right):
        def some(row, count):
            here = pl.ds(rows.start + row, count)
            both = left[here, :].astype(jnp.float32) + right[here, :].astype(jnp.float32)
            target.at[slot][here, :] = both.astype(jnp.bfloat16)

        for_rows(rows.size, some)

    def pump(self, steps):
        steps = due(steps, 2, len(self.steps))

        @pl.when(self.inner)
        def _():
            for step in steps:
                slot, rows = self.steps[step]
                self.to_inner[step].wait_recv()
                self.add(self.inward, slot, rows, self.parts.at[2 + slot], self.inward.at[slot])
                self.across[step].start()
                if step >= AHEAD:
                    self.settle(step - AHEAD)

        @pl.when(self.outer)
        def _():
            for step in steps:
                self.to_inner[step].wait_send()
                for copy in self.to_inner[step + AHEAD : step + AHEAD + 1]:
                    copy.start()

    def settle(self, step):
        slot, rows = self.steps[step]
        self.across[step].wait_recv()
        self.add(self.out, slot, rows, self.parts.at[slot], self.crossed.at[slot])

    def finish(self):
        @pl.when(self.inner)
        def _():
            for step in range(len(self.steps) - AHEAD, len(self.steps)):
                self.settle(step)
            for copy in self.across:
                copy.wait_send()

        @pl.when(self.outer)
        def _():
            for slot in (0, 1):

                def some(row, count, slot=slot):
                    here = pl.ds(row, count)
                    self.out.at[slot][here, :] = self.parts.at[slot][here, :]

                for_rows(self.parts.shape[1], some)


class BlockGrad:
    in_hbm = False

    def __init__(self, plan, left, right):
        self.zones, self.flips = plan.zones, plan.flips
        self.sources = [left, right]
        shape = (left.shape[1] // plan.total, right.shape[1])
        low = jnp.bfloat16
        self.outputs = [jax.ShapeDtypeStruct(shape, low)]
        self.scratch = [pltpu.VMEM((plan.zones,) + shape, low)] * 4
        self.count, self.count_local = 2 * plan.zones, 0

    def peers(self, zone, side, row, core):
        return {flip: device(flipped(zone, flip), side, row, core) for flip in self.flips[1:]}

    def product(self, block):
        size = self.out.shape[0]
        return dot(self.left[:, pl.ds(block * size, size)], self.right[...], 0, 0)

    def start(self, copies, local_sems, sources, targets, stages):
        zone, side, row, core = place_here()
        self.left, self.right = sources
        self.out = targets[0]
        self.far, self.got, self.parts, self.arrived = stages
        core_peer = device(zone, side, row, 1 - core)
        self.order = list(range(2, self.zones)) + [1, 0]
        self.over = [
            copies.make(self.far.at[slot], self.got.at[slot], core_peer)
            for slot in range(self.zones)
        ]
        self.along = [
            copies.make(
                self.parts.at[slot],
                self.arrived.at[slot],
                device(flipped(zone, self.flips[slot]), side, row, core),
            )
            for slot in range(1, self.zones)
        ]
        for slot in self.order:
            self.far[slot] = self.product(self.zones + slot).astype(jnp.bfloat16)
            self.over[slot].start()

    def pump(self, steps):
        for slot in self.order if 0 in steps else []:
            near = self.product(slot)
            self.over[slot].wait_recv()
            self.parts[slot] = (near + self.got[slot].astype(jnp.float32)).astype(jnp.bfloat16)
            if slot:
                self.along[slot - 1].start()

    def finish(self):
        total = self.parts[0].astype(jnp.float32)
        for slot in range(1, self.zones):
            self.along[slot - 1].wait_recv()
            total = total + self.arrived[slot].astype(jnp.float32)
        self.out[...] = total.astype(jnp.bfloat16)
        for copy in self.over + self.along:
            copy.wait_send()


class TurnLate:
    count, count_local, scratch, in_hbm = 1, 0, [], False

    def __init__(self, values):
        self.sources = [values]
        self.outputs = [jax.ShapeDtypeStruct(values.shape, values.dtype)]

    def peers(self, zone, side, row, core):
        return {}

    def start(self, copies, local_sems, sources, targets, stages):
        zone, side, row, core = place_here()
        self.away = side != core
        self.copy = copies.make(sources[0], targets[0], device(zone, core, row, side))

    def pump(self, steps):
        pass

    def late(self):
        @pl.when(self.away)
        def _():
            self.copy.start()

    def finish(self):
        @pl.when(self.away)
        def _():
            self.copy.wait_recv()
            self.copy.wait_send()


class PairTree:
    def __init__(self, pairs):
        halves_of = [own.shape[0] // 2 for own, *_ in pairs]
        self.cuts = [
            (size // 2, size // 2, size) if weight == 0 else (size, size)
            for weight, size in enumerate(halves_of)
        ]
        pieces = [len(cut) for cut in self.cuts]
        self.pairs = [len(pair) for pair in pairs]
        self.sources = [shard for pair in pairs for shard in pair]
        self.outputs = [
            jax.ShapeDtypeStruct((8,) + own.shape, own.dtype) for own, *_ in pairs
        ]
        self.count = 6 * sum(pieces) + 2 * len(pairs) + self.pairs.count(1)
        self.count_local = 2 * len(pairs) + 2 * sum(pieces)
        self.scratch = [pltpu.VMEM((2,) + own.shape, own.dtype) for own, *_ in pairs]
        self.scratch += [pltpu.VMEM(p[0].shape, p[0].dtype) for p in pairs if len(p) == 1]
        self.in_hbm = True

    def peers(self, zone, side, row, core):
        return {
            1: device(flipped(zone, 1), side, row, core),
            3: device(flipped(zone, 3), side, row, core),
            "core": device(zone, side, row, 1 - core),
        }

    def start(self, copies, local_sems, sources, targets, stages):
        zone, side, row, core = place_here()
        inner_peer = device(flipped(zone, 3), side, row, core)
        outer_peer = device(flipped(zone, 1), side, row, core)
        core_peer = device(zone, side, row, 1 - core)
        self.inner = inner_zone(zone) == 1
        self.outer = inner_zone(zone) == 0
        self.across, self.onward, self.late, self.place = [], [], [], []
        self.shared, self.kept, self.partners, self.later = [], [], [], []
        sem = 0
        sources, late_stages = list(sources), list(stages[len(targets) :])
        for weight, full in enumerate(targets):
            landing = stages[weight]
            pair = [sources.pop(0) for _ in range(self.pairs[weight])]
            if len(pair) == 1:
                pair.append(late_stages.pop(0))
                self.partners.append(copies.start(pair[0], pair[1], outer_peer))
            for place, size in enumerate(self.cuts[weight]):
                rows = pl.ds(sum(self.cuts[weight][:place]), size)
                for slot in (0, 1):
                    here = landing.at[slot, rows]
                    self.across.append(copies.make(pair[slot].at[rows], here, inner_peer))
                    self.onward.append(copies.make(here, landing.at[1 - slot, rows], outer_peer))
                    self.late.append(copies.make(here, full.at[6 + slot, rows], core_peer))
                    self.place.append(
                        pltpu.make_async_copy(here, full.at[2 + slot, rows], local_sems.at[sem])
                    )
                    sem += 1
            for slot in (0, 1):
                self.shared.append(copies.make(pair[slot], full.at[4 + slot], core_peer))
                self.kept.append(
                    pltpu.make_async_copy(pair[slot], full.at[slot], local_sems.at[sem])
                )
                sem += 1
                if slot >= self.pairs[weight]:
                    self.later += [self.shared[-1], self.kept[-1]]
                else:
                    self.shared[-1].start()
                    self.kept[-1].start()

        @pl.when(self.inner)
        def _():
            for copy in self.across[:AHEAD]:
                copy.start()

    def arrive(self, number):
        self.onward[number].wait_recv()
        swapped = number + 1 - 2 * (number % 2)
        self.late[swapped].start()
        self.place[swapped].start()

    def pump(self, steps):
        middle = 1 in steps
        steps = due(steps, 3, len(self.across))

        @pl.when(self.inner)
        def _():
            for here in steps:
                self.across[here].wait_recv()
                for copy in self.across[here + AHEAD : here + AHEAD + 1]:
                    copy.start()
                self.onward[here].start()
                self.late[here].start()
                self.place[here].start()

        @pl.when(self.outer)
        def _():
            for step in steps:
                if step > 0:
                    self.arrive(step - 1)

        for copy in self.partners if middle else []:
            copy.wait_recv()
            copy.wait_send()
        for copy in self.later if middle else []:
            copy.start()

    def finish(self):
        @pl.when(self.inner)
        def _():
            for copy in self.across + self.onward:
                copy.wait_send()

        @pl.when(self.outer)
        def _():
            self.arrive(len(self.onward) - 1)

        for copy in self.kept + self.place:
            copy.wait()
        for copy in self.shared + self.late:
            copy.wait_send()
        for copy in self.shared + self.late:
            copy.wait_recv()


def sum_eighths(
    copies, row_peer, side_peer, send, keep, forward, first, second, store, begin, pump
):
    size = send.shape[0] // 4
    part = lambda ref, slot: ref.at[pl.ds(slot * size, size)]
    arrivals = [
        copies.start(part(send, 1), part(first, 1), row_peer),
        copies.start(part(send, 3), part(first, 3), side_peer),
        copies.start(part(send, 0), part(first, 0), row_peer),
        copies.start(part(send, 2), part(first, 2), side_peer),
    ]
    begin()
    passed = []
    for number, slot, peer in ((0, 1, side_peer), (1, 3, row_peer)):
        arrivals[number].wait_recv()

        def add(row, count, number=number, slot=slot):
            here = pl.ds(slot * size + row, count)
            both = keep[here, :].astype(jnp.float32) + first[here, :].astype(jnp.float32)
            forward[pl.ds(number * size + row, count), :] = both.astype(jnp.bfloat16)

        for_rows(size, add)
        passed.append(copies.start(part(forward, number), part(second, number), peer))
    pump([0])
    for number, slot in ((0, 0), (1, 2)):
        arrivals[2 + number].wait_recv()
        passed[number].wait_recv()

        def total(row, count, number=number, slot=slot):
            here = pl.ds(slot * size + row, count)
            sums = keep[here, :].astype(jnp.float32) + first[here, :].astype(jnp.float32)
            sums = sums + second[pl.ds(number * size + row, count), :].astype(jnp.float32)
            store(number, row, count, sums)

        for_rows(size, total)
        yield number
    for copy in arrivals + passed:
        copy.wait_send()


def halves(terms):
    rows = terms.shape[0] // 2
    return terms.at[pl.ds(0, rows)], terms.at[pl.ds(rows, rows)]


def split_refs(refs, jobs, extra_count, out_count):
    refs = list(refs)
    take = lambda count: [refs.pop(0) for _ in range(count)]
    extras = take(extra_count)
    sources = [take(len(job.sources)) for job in jobs]
    full = take(1)[0]
    outs = take(out_count)
    targets = [take(len(job.outputs)) for job in jobs]
    return extras, sources, full, outs, targets, refs


def spread_kernel(middle, jobs, extra_count, out_count, gain_sum, plan, terms, *refs):
    keep, send = halves(terms)
    extras, sources, full, outs, targets, scratch = split_refs(refs, jobs, extra_count, out_count)
    forward, first, second, send_sems, recv_sems, local_sems, *stages = scratch
    zone, side, row, core = place_here()
    row_peer, side_peer = device(zone, side, 1 - row, core), device(zone, 1 - side, row, core)
    copies = Copies(send_sems, recv_sems)
    size = send.shape[0] // 4
    part = lambda slot: full.at[pl.ds(slot * size, size)]
    for out in outs:
        if out.shape[0] == 1:
            out[...] = jnp.zeros_like(out)
    peers = {}
    for job in jobs:
        peers.update(job.peers(zone, side, row, core))
    greet([row_peer, side_peer] + list(peers.values()))

    def begin():
        spot = 0
        for job, source, target in zip(jobs, sources, targets):
            own_stages = stages[spot : spot + len(job.scratch)]
            job.start(copies, local_sems, source, target, own_stages)
            spot += len(job.scratch)

    def pump(steps):
        for job in jobs:
            job.pump(steps)

    def store(number, row, count, sums):
        own = pl.ds(number * size + row, count)
        full[pl.ds(2 * number * size + row, count), :] = middle(own, sums, extras, outs)

    firsts, seconds = [], []
    for number in sum_eighths(
        copies, row_peer, side_peer, send, keep, forward, first, second, store, begin, pump
    ):
        near, other = (side_peer, row_peer) if number == 0 else (row_peer, side_peer)
        slot = 2 * number
        firsts.append(copies.start(part(slot), part(slot + 1), near))
        seconds.append(copies.start(part(slot), part(4 + slot), other))
    pump([1])
    firsts[0].wait_recv()
    seconds.append(copies.start(part(1), part(5), row_peer))
    firsts[1].wait_recv()
    seconds.append(copies.start(part(3), part(7), side_peer))
    pump(range(2, 64))
    for copy in seconds:
        copy.wait_recv()
    for copy in firsts + seconds:
        copy.wait_send()
    for job in jobs:
        job.finish()


def home_kernel(middle, jobs, extra_count, out_count, gain_sum, plan, terms, *refs):
    keep, send = halves(terms)
    extras, sources, result, outs, targets, scratch = split_refs(refs, jobs, extra_count, out_count)
    forward, first, second, own, full, send_sems, recv_sems, local_sems, *rest = scratch
    gain_scratch, stages = (rest[:2], rest[2:]) if gain_sum is not None else ([], rest)
    block = extras[3]
    zone, side, row, core = place_here()
    row_peer, side_peer = device(zone, side, 1 - row, core), device(zone, 1 - side, row, core)
    core_peer, other_peer = device(zone, side, row, 1 - core), device(zone, 1 - side, row, 1 - core)
    copies = Copies(send_sems, recv_sems)
    size = send.shape[0] // 4
    at_home = side == core
    away = side != core
    for out in outs:
        if out.shape[0] == 1:
            out[...] = jnp.zeros_like(out)
    peers = {}
    for job in jobs:
        peers.update(job.peers(zone, side, row, core))
    plane = [row_peer, side_peer, core_peer, other_peer]
    if gain_sum is not None:
        plane = gain_sum.plane_peers(zone, side, row, core)
        peers.update(gain_sum.zone_peers(zone, side, row, core))
    greet(plane + list(peers.values()))

    def begin():
        spot = 0
        for job, source, target in zip(jobs, sources, targets):
            own_stages = stages[spot : spot + len(job.scratch)]
            job.start(copies, local_sems, source, target, own_stages)
            spot += len(job.scratch)

    def pump(steps):
        if 0 in steps:

            @pl.when(away)
            def _():
                for copy in block_side:
                    copy.start()

        for job in jobs:
            job.pump(steps)

    def store(number, start, count, sums):
        here = pl.ds(number * size + start, count)
        values = middle(here, sums, extras, outs)
        own[here, :] = values
        eighth = row * 2 + side if number == 0 else 4 + side * 2 + row

        @pl.when(at_home)
        def _():
            full[pl.ds(pl.multiple_of(eighth * size + start, 32), count), :] = values

    def piece(number, x, y):
        start = (x * 2 + y) * size if number == 0 else (4 + y * 2 + x) * size
        return full.at[pl.ds(pl.multiple_of(start, size), size)]

    both = (0, 1)
    part = lambda ref, number: ref.at[pl.ds(number * size, size)]
    block_over = [copies.make(part(block, k), piece(k, row, side), core_peer) for k in both]
    block_side = [copies.make(part(block, k), piece(k, row, side), other_peer) for k in both]
    to_side = [copies.make(part(own, k), piece(k, row, side), side_peer) for k in both]
    to_row = [copies.make(piece(k, row, side), piece(k, row, side), row_peer) for k in both]
    pass_row = [
        copies.make(piece(k, row, 1 - side), piece(k, row, 1 - side), row_peer) for k in both
    ]

    @pl.when(at_home)
    def _():
        for copy in block_over:
            copy.start()

    for _ in sum_eighths(
        copies, row_peer, side_peer, send, keep, forward, first, second, store, begin, pump
    ):
        pass
    pump([1])
    if gain_sum is not None:
        gain_sum.start(copies, extras[-1], outs[0], *gain_scratch)

    @pl.when(away)
    def _():
        for copy in to_side:
            copy.start()
        for copy in block_over:
            copy.wait_recv()

    for copy in to_row:
        copy.start()
    for job in jobs:
        if isinstance(job, TurnLate):
            job.late()
    if gain_sum is not None:
        gain_sum.middle()

    @pl.when(at_home)
    def _():
        for copy in to_side:
            copy.wait_recv()
        for copy in block_over:
            copy.wait_send()

    @pl.when(away)
    def _():
        for copy in block_side:
            copy.wait_recv()

    for copy in pass_row:
        copy.start()
    for copy in to_row + pass_row:
        copy.wait_recv()
        copy.wait_send()
    @pl.when(away)
    def _():
        for copy in to_side + block_side:
            copy.wait_send()

    natural, local = block_columns(plan, full.shape[1], side)

    def some(start, count):
        here = pl.ds(start, count)
        for a, b in zip(natural, local):
            result[here, a] = full[here, b]

    for_rows(full.shape[0], some)
    if gain_sum is not None:
        gain_sum.finish(outs[-1])
    for job in jobs:
        job.finish()


def sum_rows(plan, kernel, middle, terms, extras, outs, number, jobs=(), gain_sum=None):
    half, width = terms.shape[0] // 2, terms.shape[1]
    eighth = half // 4
    low = jnp.bfloat16
    vmem, hbm = pl.BlockSpec(memory_space=pltpu.VMEM), pl.BlockSpec(memory_space=pl.ANY)
    scratch = [
        pltpu.VMEM((2 * eighth, width), low),
        pltpu.VMEM((half, width), low),
        pltpu.VMEM((2 * eighth, width), low),
    ]
    if kernel is home_kernel:
        scratch.append(pltpu.VMEM((2 * eighth, width), low))
        scratch.append(pltpu.VMEM((2 * half, width), low))
    copies = (12 if kernel is spread_kernel else 16) + sum(job.count for job in jobs)
    local = max([2] + [job.count_local for job in jobs])
    if gain_sum is not None:
        copies += gain_sum.count
        outs = outs + [gain_sum.output]
    scratch += [pltpu.SemaphoreType.DMA((count,)) for count in (copies, copies, local)]
    if gain_sum is not None:
        scratch += gain_sum.scratch
    scratch += [stage for job in jobs for stage in job.scratch]
    sources = [source for job in jobs for source in job.sources]
    targets = [target for job in jobs for target in job.outputs]
    return pl.pallas_call(
        functools.partial(kernel, middle, jobs, len(extras), len(outs), gain_sum, plan),
        out_shape=[jax.ShapeDtypeStruct((2 * half, width), low)] + outs + targets,
        in_specs=[vmem] * (1 + len(extras) + len(sources)),
        out_specs=[vmem] * (1 + len(outs))
        + [hbm if job.in_hbm else vmem for job in jobs for _ in job.outputs],
        scratch_shapes=scratch,
        compiler_params=pltpu.CompilerParams(
            collective_id=number, has_side_effects=True, vmem_limit_bytes=56 * 2**20
        ),
        cost_estimate=pl.CostEstimate(flops=10**6, bytes_accessed=10**5, transcendentals=0),
        name=middle.__name__,
    )(terms, *extras, *sources)


def block_columns(plan, width, of_core=None):
    if not plan.ordered:
        return [pl.ds(0, width)], [pl.ds(0, width)]
    zone, _, _, core = place_here()
    core = core if of_core is None else of_core
    size, zones = width // plan.total, plan.zones
    owners = [
        flipped(zone, plan.flips[slot % zones]) * 2 + (core if slot < zones else 1 - core)
        for slot in range(plan.total)
    ]
    natural = [pl.ds(pl.multiple_of(owner * size, size), size) for owner in owners]
    return natural, [pl.ds(slot * size, size) for slot in range(plan.total)]


def copy_rows(source, target):
    def some(row, count):
        target[pl.ds(row, count), :] = source[pl.ds(row, count), :]

    if source.shape[0] % 32:
        target[...] = source[...]
    else:
        for_rows(source.shape[0], some)


def cast_rows(source, target):
    def some(row, count):
        here = pl.ds(row, count)
        target[here, :] = source[here, :].astype(target.dtype)

    for_rows(source.shape[0], some)


def opening_kernel(plan, wide_qkv, gains, wide_gate, wide_out, wide_down, tokens, angles, *refs):
    qkv_full, gains_full, turned_gate, turned_out, turned_down, turned_tokens, turned_angles = refs[:7]
    partner_gate, send_sems, recv_sems, tokens_stage, qkv, gate, out, down = refs[7:]
    cast_rows(wide_qkv, qkv)
    zone, side, row, core = place_here()
    partner = device(zone, core, row, side)
    row_peer, core_peer = device(zone, side, 1 - row, core), device(zone, side, row, 1 - core)
    zone_peers = [device(flipped(zone, flip), side, row, core) for flip in plan.flips[1:]]
    at_home, away = side == core, side != core
    always = [row_peer, core_peer] + zone_peers

    @pl.when(at_home)
    def _():
        greet(always)

    @pl.when(away)
    def _():
        greet(always + [partner])

    copies = Copies(send_sems, recv_sems)
    zones = plan.zones
    own = (gains, qkv, angles, gate, out, down)
    ends = (gains_full.at[0], qkv_full.at[0], turned_angles, turned_gate, turned_out, turned_down)
    units = wide_gate.shape[2]

    def cast_rest():
        for half in (0, 1):
            cast_rows(wide_gate.at[half], gate.at[:, pl.ds(half * units, units)])
        cast_rows(wide_out, out)
        cast_rows(wide_down, down)

    turn = [copies.make(source, target, partner) for source, target in zip(own, ends)]
    pieces = 2
    size = tokens.shape[0] // (2 * pieces)
    spots = [
        pl.ds(pl.multiple_of((row * pieces + piece) * size, size), size) for piece in range(pieces)
    ]
    turn_rows = [copies.make(tokens.at[s], tokens_stage.at[s], partner) for s in spots]
    pass_rows = [copies.make(tokens_stage.at[s], tokens_stage.at[s], row_peer) for s in spots]
    natural, local = block_columns(plan, tokens.shape[1])

    def lay_down(all_tokens):
        def some(start, count):
            here = pl.ds(start, count)
            for a, b in zip(natural, local):
                turned_tokens[here, b] = all_tokens[here, a]

        for_rows(all_tokens.shape[0], some)

    slots = list(range(1, zones))
    weights = ((gains, gains_full), (qkv, qkv_full))
    from_own = [
        [copies.make(source, full.at[slot], zone_peers[slot - 1]) for slot in slots]
        + [copies.make(source, full.at[zones], core_peer)]
        for source, full in weights
    ] + [[copies.make(gate, partner_gate, zone_peers[0])]]
    copies.number -= 2 * zones + 1
    from_turned = [
        [copies.make(full.at[0], full.at[slot], zone_peers[slot - 1]) for slot in slots]
        + [copies.make(full.at[0], full.at[zones], core_peer)]
        for _, full in weights
    ] + [[copies.make(turned_gate, partner_gate, zone_peers[0])]]
    cross = [
        [copies.make(full.at[slot], full.at[zones + slot], core_peer) for slot in slots]
        for _, full in weights
    ]

    def cross_over(k):
        for which in (0, 1):
            from_turned[which][k].wait_recv()
            cross[which][k].start()

    @pl.when(away)
    def _():
        for copy in turn[:3]:
            copy.start()
        cast_rest()
        for which in (0, 1):
            turn[which].wait_recv()
            for copy in from_turned[which]:
                copy.start()
        turn[3].start()
        turn_rows[0].start()
        turn[3].wait_recv()
        from_turned[2][0].start()
        turn_rows[1].start()
        cross_over(0)
        turn_rows[0].wait_recv()
        pass_rows[0].start()
        for copy in turn[4:]:
            copy.start()
        turn_rows[1].wait_recv()
        pass_rows[1].start()

    @pl.when(at_home)
    def _():
        for copy in from_own[0] + from_own[1]:
            copy.start()
        cast_rest()
        for copy in from_own[2]:
            copy.start()
        for source, target in zip(own, ends):
            copy_rows(source, target)
        lay_down(tokens)
        cross_over(0)

    for k in range(1, zones - 1):
        cross_over(k)
    for which in (0, 1):
        from_turned[which][zones - 1].wait_recv()
        for copy in from_turned[which]:
            copy.wait_send()
        for copy in cross[which]:
            copy.wait_recv()
            copy.wait_send()
    from_turned[2][0].wait_recv()
    from_turned[2][0].wait_send()

    @pl.when(away)
    def _():
        for copy in pass_rows + turn[2:3] + turn[4:]:
            copy.wait_recv()
        lay_down(tokens_stage)
        for copy in turn + turn_rows + pass_rows:
            copy.wait_send()


def opening(plan, qkv, gains, gate, out, down, tokens, angles, number):
    low = jnp.bfloat16
    vmem = pl.BlockSpec(memory_space=pltpu.VMEM)
    like = lambda v: jax.ShapeDtypeStruct(v.shape, v.dtype)
    whole = lambda v: jax.ShapeDtypeStruct((2 * plan.zones,) + v.shape, low)
    operands = (qkv, gains, gate, out, down, tokens, angles)
    low_gate = jax.ShapeDtypeStruct((gate.shape[1], 2 * gate.shape[2]), low)
    low_out = jax.ShapeDtypeStruct(out.shape, low)
    low_down = jax.ShapeDtypeStruct(down.shape, low)
    outputs = [whole(qkv), whole(gains), low_gate, low_out, low_down, like(tokens), like(angles)]
    outputs += [low_gate]
    copies = 6 + 4 + 2 * plan.zones + 1 + 2 * (plan.zones - 1)
    return pl.pallas_call(
        functools.partial(opening_kernel, plan),
        out_shape=outputs,
        in_specs=[vmem] * len(operands),
        out_specs=[vmem] * len(outputs),
        scratch_shapes=[
            pltpu.SemaphoreType.DMA((copies,)),
            pltpu.SemaphoreType.DMA((copies,)),
            pltpu.VMEM(tokens.shape, tokens.dtype),
            pltpu.VMEM(qkv.shape, low),
            pltpu.VMEM(low_gate.shape, low),
            pltpu.VMEM(out.shape, low),
            pltpu.VMEM(down.shape, low),
        ],
        compiler_params=pltpu.CompilerParams(
            collective_id=number, has_side_effects=True, vmem_limit_bytes=56 * 2**20
        ),
        cost_estimate=pl.CostEstimate(flops=10**6, bytes_accessed=10**5, transcendentals=0),
        name="opening",
    )(*operands)


def inverse_rms(values):
    return lax.rsqrt(jnp.mean(values * values, -1, keepdims=True) + EPS_NORM)


def hidden_rows(own, sums, extras, outs):
    tokens, gain = extras
    hidden = tokens[own, :].astype(jnp.float32) + sums
    outs[0][own, :] = hidden
    return (hidden * inverse_rms(hidden) * gain[...]).astype(jnp.bfloat16)


def grad_hidden_rows(own, sums, extras, outs):
    hidden, out_grad, gain = extras
    values = hidden[own, :]
    factor = inverse_rms(values)
    unit = values * factor
    outs[1][...] += jnp.sum(sums * unit, 0, keepdims=True)
    grad = out_grad[own, :].astype(jnp.float32) + norm_back(sums * gain[...], unit, factor)
    outs[0][own, :] = grad
    return grad.astype(jnp.bfloat16)


def grad_input_rows(own, sums, extras, outs):
    tokens, grad_hidden, gain = extras[:3]
    values = tokens[own, :].astype(jnp.float32)
    factor = inverse_rms(values)
    unit = values * factor
    outs[0][...] += jnp.sum(sums * unit, 0, keepdims=True)
    return (grad_hidden[own, :] + norm_back(sums * gain[...], unit, factor)).astype(jnp.bfloat16)


def dot(left, right, left_dim=1, right_dim=0):
    return lax.dot_general(
        left, right, (((left_dim,), (right_dim,)), ((), ())), preferred_element_type=jnp.float32
    )


def turn_head(values, cosine, signed_sine):
    return values * cosine + pltpu.roll(values, HEAD // 2, 1) * signed_sine


def turn_back(gradient, cosine, signed_sine):
    return gradient * cosine + pltpu.roll(gradient * signed_sine, HEAD // 2, 1)


def softmax_block(query, key, first_row):
    rows, keys = query.shape[0], key.shape[0]
    scores = dot(query, key, 1, 1)
    row_at = lax.broadcasted_iota(jnp.int32, (rows, keys), 0) + first_row
    key_at = lax.broadcasted_iota(jnp.int32, (rows, keys), 1)
    scores = jnp.where(key_at <= row_at, scores, -1000000000.0)
    exponent = jnp.exp(scores - jnp.max(scores, -1, keepdims=True))
    return exponent / jnp.sum(exponent, -1, keepdims=True)


def eighth_owners():
    _, side, row, _ = place_here()
    own, off = (row, side), (1 - row, 1 - side)
    first = lambda x, y: x * 2 + y
    second = lambda x, y: 4 + y * 2 + x
    return [
        first(own[0], own[1]),
        first(own[0], off[1]),
        second(own[0], own[1]),
        second(off[0], own[1]),
        first(off[0], own[1]),
        first(off[0], off[1]),
        second(own[0], off[1]),
        second(off[0], off[1]),
    ]


def reorder_rows(source, target, into_local):
    size = source.shape[0] // 8
    for slot, owner in enumerate(eighth_owners()):
        natural = pl.ds(pl.multiple_of(owner * size, size), size)
        local = pl.ds(slot * size, size)
        if into_local:
            target[local, :] = source[natural, :]
        else:
            target[natural, :] = source[local, :]


def forward_kernel(
    tokens, weights, gain_in, gain_q, gain_k, cosine, sine,
    normed, raw, query, key, value, local, attended,
):
    low = jnp.bfloat16
    total, heads = tokens.shape[0], query.shape[1] // HEAD
    block, wide = 256, 512

    def project(step, carry):
        rows = pl.ds(pl.multiple_of(step * wide, wide), wide)
        values = tokens[rows, :].astype(jnp.float32)
        normed[rows, :] = (values * inverse_rms(values) * gain_in[...]).astype(low)
        raw[rows, :] = dot(normed[rows, :], weights[...])
        turns = (cosine[rows, :], sine[rows, :])
        for head in range(heads):
            column = (head // 2) * 4 * HEAD + (head % 2) * HEAD
            values = raw[rows, pl.ds(column, HEAD)]
            values = turn_head(values * inverse_rms(values) * gain_q[...], *turns)
            query[rows, pl.ds(head * HEAD, HEAD)] = (values * (1.0 / math.sqrt(HEAD))).astype(low)
        for group in range(heads // 2):
            column = group * 4 * HEAD + 2 * HEAD
            here = pl.ds(group * HEAD, HEAD)
            values = raw[rows, pl.ds(column, HEAD)]
            values = turn_head(values * inverse_rms(values) * gain_k[...], *turns)
            key[rows, here] = values.astype(low)
            value[rows, here] = raw[rows, pl.ds(column + HEAD, HEAD)].astype(low)
        return carry

    lax.fori_loop(0, total // wide, project, 0)

    def attend(head, carry):
        mine = pl.ds(pl.multiple_of(head * HEAD, HEAD), HEAD)
        shared = pl.ds(pl.multiple_of(lax.div(head, 2) * HEAD, HEAD), HEAD)
        for start in range(0, total, SEQ):
            for first in range(0, SEQ, block):
                rows, keys = pl.ds(start + first, block), pl.ds(start, first + block)
                probs = softmax_block(query[rows, mine], key[keys, shared], first)
                attended[rows, mine] = dot(probs.astype(low), value[keys, shared]).astype(low)
        return carry

    lax.fori_loop(0, heads, attend, 0)
    reorder_rows(attended, local, True)


def attention(tokens, weights, gain_in, gain_q, gain_k, cosine, sine):
    total = tokens.shape[0]
    columns = weights.shape[1]
    low = jnp.bfloat16
    shape = lambda width, kind=low: jax.ShapeDtypeStruct((total, width), kind)
    vmem = pl.BlockSpec(memory_space=pltpu.VMEM)
    return pl.pallas_call(
        forward_kernel,
        out_shape=[
            shape(tokens.shape[1]),
            shape(columns, jnp.float32),
            shape(columns // 2),
            shape(columns // 4),
            shape(columns // 4),
            shape(columns // 2),
        ],
        in_specs=[vmem] * 7,
        out_specs=[vmem] * 6,
        scratch_shapes=[pltpu.VMEM((total, columns // 2), low)],
        compiler_params=pltpu.CompilerParams(vmem_limit_bytes=48 * 2**20),
        cost_estimate=pl.CostEstimate(flops=10**6, bytes_accessed=10**5, transcendentals=0),
        name="attention",
    )(tokens, weights, gain_in, gain_q, gain_k, cosine, sine)


def backward_kernel(
    query, key, value, raw, grad_rows, gain_q, gain_k, cosine, sine,
    mixed, mixed_local, query_gain, key_gain, grad, key_sum, value_sum,
):
    low = jnp.bfloat16
    total, heads = query.shape[0], query.shape[1] // HEAD
    block = 256
    reorder_rows(grad_rows, grad, False)
    query_gain[...] = jnp.zeros_like(query_gain)
    key_gain[...] = jnp.zeros_like(key_gain)

    def head_norm_back(rows, column, gradient, gain, gain_grad):
        values = raw[rows, column]
        factor = inverse_rms(values)
        unit = values * factor
        turned = turn_back(gradient, cosine[rows, :], sine[rows, :])
        gain_grad[...] += jnp.sum(turned * unit, 0, keepdims=True)
        mixed[rows, column] = norm_back(turned * gain[...], unit, factor).astype(low)

    def one_group(group, carry):
        at = lambda offset: pl.ds(pl.multiple_of(group * 4 * HEAD + offset * HEAD, HEAD), HEAD)
        shared = pl.ds(pl.multiple_of(group * HEAD, HEAD), HEAD)
        key_sum[...] = jnp.zeros_like(key_sum)
        value_sum[...] = jnp.zeros_like(value_sum)
        for head in (0, 1):
            mine = pl.ds(pl.multiple_of((group * 2 + head) * HEAD, HEAD), HEAD)
            for start in range(0, total, SEQ):
                for first in range(0, SEQ, block):
                    rows, keys = pl.ds(start + first, block), pl.ds(start, first + block)
                    query_part, grad_part = query[rows, mine], grad[rows, mine]
                    probs = softmax_block(query_part, key[keys, shared], first)
                    weighed = probs * dot(grad_part, value[keys, shared], 1, 1)
                    scores = weighed - probs * jnp.sum(weighed, -1, keepdims=True)
                    scores = scores.astype(low)
                    grad_query = dot(scores, key[keys, shared]) * (1.0 / math.sqrt(HEAD))
                    head_norm_back(rows, at(head), grad_query, gain_q, query_gain)
                    key_sum[keys, :] += dot(scores, query_part, 0, 0)
                    value_sum[keys, :] += dot(probs.astype(low), grad_part, 0, 0)
        for first in range(0, total, block):
            rows = pl.ds(first, block)
            head_norm_back(rows, at(2), key_sum[rows, :], gain_k, key_gain)
            mixed[rows, at(3)] = value_sum[rows, :].astype(low)
        return carry

    lax.fori_loop(0, heads // 2, one_group, 0)
    reorder_rows(mixed, mixed_local, True)


def attention_back(query, key, value, raw, grad_rows, gain_q, gain_k, cosine, sine):
    total, columns = raw.shape
    low = jnp.bfloat16
    vmem = pl.BlockSpec(memory_space=pltpu.VMEM)
    return pl.pallas_call(
        backward_kernel,
        out_shape=[
            jax.ShapeDtypeStruct((total, columns), low),
            jax.ShapeDtypeStruct((total, columns), low),
            jax.ShapeDtypeStruct((1, HEAD), jnp.float32),
            jax.ShapeDtypeStruct((1, HEAD), jnp.float32),
        ],
        in_specs=[vmem] * 9,
        out_specs=[vmem] * 4,
        scratch_shapes=[
            pltpu.VMEM(grad_rows.shape, low),
            pltpu.VMEM((total, HEAD), jnp.float32),
            pltpu.VMEM((total, HEAD), jnp.float32),
        ],
        compiler_params=pltpu.CompilerParams(vmem_limit_bytes=48 * 2**20),
        cost_estimate=pl.CostEstimate(flops=10**6, bytes_accessed=10**5, transcendentals=0),
        name="attention_back",
    )(query, key, value, raw, grad_rows, gain_q, gain_k, cosine, sine)


def feed_kernel(plan, rows, own_grad, got_grad, gate_up, up_part, down, active, grads, out_grad):
    low = jnp.bfloat16
    block = 512
    tile = down.shape[1]
    step = pl.program_id(0)
    gate_at = pl.ds(pl.multiple_of(step * tile, tile), tile)
    up_at = pl.ds(pl.multiple_of(grads.shape[1] // 2 + step * tile, tile), tile)
    _, side, _, core = place_here()

    def lay_down(source):
        natural, blocks = block_columns(plan, source.shape[1])
        eighth = source.shape[0] // 8
        for slot, owner in enumerate(eighth_owners()):

            def some(start, count, slot=slot, owner=owner):
                here = pl.ds(pl.multiple_of(owner * eighth + start, 32), count)
                there = pl.ds(slot * eighth + start, count)
                for a, b in zip(natural, blocks):
                    out_grad[there, b] = source[here, a]

            for_rows(eighth, some)

    @pl.when((step == 0) & (side == core))
    def _():
        lay_down(own_grad)

    @pl.when((step == 0) & (side != core))
    def _():
        lay_down(got_grad)

    def one(block_at, carry):
        here = pl.ds(pl.multiple_of(block_at * block, block), block)
        gate = dot(rows[here, :], gate_up[...])
        up = dot(rows[here, :], up_part[...])
        grad = dot(out_grad[here, :], down[...])
        sigmoid = jax.nn.sigmoid(gate)
        silu = gate * sigmoid
        active[here, :] = (silu * up).astype(low)
        grads[here, gate_at] = (grad * up * sigmoid * (1.0 + gate * (1.0 - sigmoid))).astype(low)
        grads[here, up_at] = (grad * silu).astype(low)
        return carry

    lax.fori_loop(0, rows.shape[0] // block, one, 0)


def feed_forward(plan, rows, own_grad, got_grad, gate_up, down, tile):
    total, width = rows.shape
    units = down.shape[1]
    low = jnp.bfloat16
    tiles = units // tile
    whole = pl.BlockSpec(memory_space=pltpu.VMEM)
    return pl.pallas_call(
        functools.partial(feed_kernel, plan),
        grid=(tiles,),
        out_shape=[
            jax.ShapeDtypeStruct((total, units), low),
            jax.ShapeDtypeStruct((total, 2 * units), low),
            jax.ShapeDtypeStruct((total, width), low),
        ],
        in_specs=[
            whole,
            whole,
            whole,
            pl.BlockSpec((width, tile), lambda step: (0, step)),
            pl.BlockSpec((width, tile), lambda step: (0, step + tiles)),
            pl.BlockSpec((width, tile), lambda step: (0, step)),
        ],
        out_specs=[
            pl.BlockSpec((total, tile), lambda step: (0, step)),
            whole,
            whole,
        ],
        compiler_params=pltpu.CompilerParams(vmem_limit_bytes=56 * 2**20),
        cost_estimate=pl.CostEstimate(
            flops=6 * total * width * units, bytes_accessed=4 * 10**7, transcendentals=total * units
        ),
        name="feed_forward",
    )(rows, own_grad, got_grad, gate_up, gate_up, down)


class Plan:
    def __init__(self, mesh):
        self.total = mesh.shape["dp"]
        self.zones = self.total // 2
        self.tensor = mesh.shape["tensor"]
        self.flips = [k ^ (k >> 1) for k in range(self.zones)]

    def place(self):
        self.index = lax.axis_index("dp")
        self.zone = self.index // 2
        self.side = self.index % 2
        self.row = lax.axis_index("tensor") // 2
        self.core = lax.axis_index("tensor") % 2
        self.home = self.side == self.core

    def move(self, value, target):
        pairs = []
        for d in range(self.total):
            for t in range(self.tensor):
                to = target(d // 2, d % 2, t // 2, t % 2)
                if to is not None:
                    zone, side, row, core = to
                    pairs.append((d * self.tensor + t, (zone * 2 + side) * self.tensor + row * 2 + core))
        return lax.ppermute(value, ("dp", "tensor"), pairs)

    def turn(self, value):
        got = self.move(value, lambda z, y, x, c: (z, c, x, y) if y != c else None)
        return jnp.where(self.home, value, got)

    def zone_flip(self, value, bit):
        return self.move(value, lambda z, y, x, c: (z ^ bit, y, x, c))

    def core_swap(self, value):
        return self.move(value, lambda z, y, x, c: (z, y, x, 1 - c))

    def side_swap(self, value):
        return self.move(value, lambda z, y, x, c: (z, 1 - y, x, c))

    def row_swap(self, value):
        return self.move(value, lambda z, y, x, c: (z, y, 1 - x, c))

    def to_local(self, value, axis):
        width = value.shape[axis] // self.total
        parts = []
        for core in (self.core, 1 - self.core):
            for slot in range(self.zones):
                owner = (self.zone ^ self.flips[slot]) * 2 + core
                parts.append(lax.dynamic_slice_in_dim(value, owner * width, width, axis))
        return jnp.concatenate(parts, axis)

    def to_natural(self, value, axis, core=None):
        core = self.core if core is None else core
        width = value.shape[axis] // self.total
        parts = []
        for block in range(self.total):
            slot = flip = (block // 2) ^ self.zone
            for bits in range(1, self.zones.bit_length()):
                slot = slot ^ (flip >> bits)
            slot = slot + jnp.where(block % 2 == core, 0, self.zones)
            parts.append(lax.dynamic_slice_in_dim(value, slot * width, width, axis))
        return jnp.concatenate(parts, axis)

    def row_owners(self):
        own, off = (self.row, self.side), (1 - self.row, 1 - self.side)
        first = lambda x, y: x * 2 + y
        second = lambda x, y: 4 + y * 2 + x
        return [
            first(own[0], own[1]),
            first(own[0], off[1]),
            second(own[0], own[1]),
            second(off[0], own[1]),
            first(off[0], own[1]),
            first(off[0], off[1]),
            second(own[0], off[1]),
            second(off[0], off[1]),
        ]

    def rows_local(self, value, slots=range(8)):
        size = value.shape[0] // 8
        owners = self.row_owners()
        return jnp.concatenate(
            [lax.dynamic_slice_in_dim(value, owners[slot] * size, size, 0) for slot in slots], 0
        )

    def rows_natural(self, value, order=range(8)):
        size = value.shape[0] // 8
        place = [list(order).index(slot) for slot in range(8)]
        parts = []
        for piece in range(8):
            x, y = (piece // 2, piece % 2) if piece < 4 else (piece % 2, (piece - 4) // 2)
            slots = (0, 1, 4, 5) if piece < 4 else (2, 6, 3, 7)
            same_x, same_y = x == self.row, y == self.side
            slot = jnp.where(
                same_x,
                jnp.where(same_y, place[slots[0]], place[slots[1]]),
                jnp.where(same_y, place[slots[2]], place[slots[3]]),
            )
            parts.append(lax.dynamic_slice_in_dim(value, slot * size, size, 0))
        return jnp.concatenate(parts, 0)

    def from_zones(self, shard):
        return [self.zone_flip(shard, flip) for flip in self.flips[1:]]

    def to_zones(self, parts, slots):
        return [self.zone_flip(parts[slot], self.flips[slot]) for slot in slots]

    def middle_swap(self, pair):
        return self.move(pair, lambda z, y, x, c: (z ^ 3, y, x, c) if z in (1, 2) else None)

    def inward(self, part):
        return self.move(part, lambda z, y, x, c: (z ^ 1, y, x, c) if z in (0, 3) else None)

    def pass_outward(self, pair):
        return self.move(pair, lambda z, y, x, c: (z ^ 1, y, x, c) if z in (1, 2) else None)

    def far_pair(self, middle, passed):
        inner = (self.zone == 1) | (self.zone == 2)
        return jnp.where(inner, middle, passed[::-1])

    def first_swap(self, send):
        half = send.shape[0] // 2
        return self.row_swap(send[:half]), self.side_swap(send[half:])

    def second_swap(self, keep, got):
        quarter = keep.shape[0] // 4
        row_part = keep[: 2 * quarter] + got[0].astype(jnp.float32)
        side_part = keep[2 * quarter :] + got[1].astype(jnp.float32)
        own = jnp.concatenate([row_part[:quarter], side_part[:quarter]], 0)
        return own, (
            self.side_swap(row_part[quarter:].astype(jnp.bfloat16)),
            self.row_swap(side_part[quarter:].astype(jnp.bfloat16)),
        )

    def spread_first(self, own):
        half = own.shape[0] // 2
        return (self.side_swap(own[:half]), self.row_swap(own[half:]))

    def spread_second(self, own, got):
        half = own.shape[0] // 2
        row_part = jnp.concatenate([own[:half], got[0]], 0)
        side_part = jnp.concatenate([own[half:], got[1]], 0)
        return row_part, side_part, self.row_swap(row_part), self.side_swap(side_part)

    def send_home(self, own):
        to_home = lambda z, y, x, c: (z, c, x, c) if y != c else None
        return jnp.concatenate([own, self.move(own, to_home)], 0)

    def row_home(self, part):
        return self.move(part, lambda z, y, x, c: (z, y, 1 - x, c) if y == c else None)

    def share_home(self, part, other):
        full = jnp.concatenate([part, other], 0)
        full = self.to_natural(self.rows_natural(full, (0, 2, 1, 6, 4, 3, 5, 7)), 1)
        got = self.move(full, lambda z, y, x, c: (z, y, x, 1 - c) if y == c else None)
        return full, got

    def turned(self, own, got):
        return jnp.where(self.home, own, got)

    def sum_everywhere(self, value):
        value = value + self.row_swap(value)
        value = value + self.side_swap(value)
        value = value + self.core_swap(value)
        bit = 1
        while bit < self.zones:
            value = value + self.zone_flip(value, bit)
            bit *= 2
        return value


def shards(
    plan,
    tokens,
    positions,
    out_grad,
    qkv_weight,
    qkv_first,
    qkv_second,
    out_weight,
    out_first,
    out_second,
    gate_up,
    gate_up_first,
    gate_up_second,
    down_weight,
    down_first,
    down_second,
    gains,
    gains_first,
    gains_second,
):
    plan.place()
    low = jnp.bfloat16
    tok_rows, model_width = tokens.shape
    groups = qkv_weight.shape[1]
    head_size = qkv_weight.shape[3]
    shard_rows = qkv_weight.shape[0]
    seq_count = tok_rows // SEQ
    mixed_cols = groups * 4 * head_size
    near_cols = model_width // 2
    kept = tok_rows // 2
    gain_count = gains.shape[0]

    tree = plan.zones == 4
    slots = range(1, plan.zones)

    def column_parts(value):
        return value.reshape((plan.zones, -1) + value.shape[1:])

    units = gate_up.shape[2]
    plan.ordered = (model_width // plan.total) % 128 == 0
    gain_rows = 16
    gain_block = jnp.pad(gains.astype(low), (0, gain_rows * 128 - gain_count)).reshape(gain_rows, 128)
    tile = min(units, 256)
    angle_at = positions.astype(jnp.float32).reshape(-1, 128)
    both_qkv, both_gains, turned_gate, turned_out, turned_down, tokens, angle_at, partner_gate = opening(
        plan,
        qkv_weight.reshape(shard_rows, mixed_cols),
        gain_block,
        gate_up,
        out_weight,
        down_weight,
        tokens,
        angle_at,
        3,
    )
    positions = angle_at.reshape(-1)
    turned_out, turned_gate, turned_down, tokens, positions, both_qkv, both_gains, out_grad = fence(
        turned_out, turned_gate, turned_down, tokens, positions, both_qkv, both_gains, out_grad
    )

    got_grad = plan.move(out_grad, lambda z, y, x, c: (z, c, x, y) if y != c else None)
    zone_out = plan.from_zones(turned_out)
    if tree:
        partner_down = plan.zone_flip(turned_down, 1)
    else:
        partner_down = plan.from_zones(turned_down)
        partner_gate = plan.from_zones(turned_gate)
    if not plan.ordered:
        tokens = plan.to_local(tokens, 1)
    cosine, sine_table = rotary(positions, head_size)
    signed_sine = jnp.concatenate(
        [-sine_table[:, : head_size // 2], sine_table[:, head_size // 2 :]], 1
    )
    full_qkv = both_qkv.reshape(model_width, mixed_cols)
    gain_slots = both_gains.reshape(plan.total, -1)[:, :gain_count]
    gain_all = plan.to_natural(gain_slots.reshape(-1), 0).astype(jnp.float32)
    gain_in = plan.to_local(gain_all[:model_width], 0)[None]
    gain_post = plan.to_local(gain_all[model_width : 2 * model_width], 0)[None]
    gain_q = gain_all[2 * model_width : 2 * model_width + head_size][None]
    gain_k = gain_all[2 * model_width + head_size :][None]
    normed, raw, query, key_rot, values_low, attended = attention(
        tokens, full_qkv, gain_in, gain_q, gain_k, cosine, signed_sine
    )
    attended, zone_out, turned_out, turned_down, turned_gate, partner_gate, partner_down = fence(
        attended, zone_out, turned_out, turned_down, turned_gate, partner_gate, partner_down
    )

    near_out = jnp.concatenate([turned_out] + zone_out, 0)
    far_out = plan.core_swap(near_out)
    own_tokens = plan.rows_local(tokens, (0, 2))
    near_out, far_out, own_tokens = fence(near_out, far_out, own_tokens)

    full_out = jnp.concatenate([near_out, far_out], 0)
    branch_terms = contract_cols(attended, full_out).astype(low)
    pairs = [(turned_gate, partner_gate), (turned_down, partner_down)]
    jobs = [PairTree(pairs)] if tree else []
    normed_rows, hidden, *gathered = sum_rows(
        plan,
        spread_kernel,
        hidden_rows,
        branch_terms,
        [own_tokens, gain_post],
        [jax.ShapeDtypeStruct((tok_rows // 4, model_width), jnp.float32)],
        0,
        jobs,
    )
    if not tree:
        near = [jnp.concatenate([own] + rest, 0) for own, rest in pairs]
        gathered = [jnp.concatenate([part, plan.core_swap(part)], 0) for part in near]
    full_gate = gathered[0].reshape(model_width, 2 * units)
    full_down = gathered[1].reshape(model_width, units)
    normed_rows, hidden, full_gate, full_down, got_grad = fence(
        normed_rows, hidden, full_gate, full_down, got_grad
    )

    def zone_parts(near, got):
        both = (near + got.astype(jnp.float32)).astype(low)
        return both.reshape((plan.zones, -1) + both.shape[1:])

    def zone_total(parts, *arrived):
        total = parts[0].astype(jnp.float32)
        for part in sum([list(group) for group in arrived], []):
            total = total + part.astype(jnp.float32)
        return total.astype(low)

    active, grad_both, out_grad = feed_forward(
        plan, normed_rows, out_grad, got_grad, full_gate, full_down, tile
    )
    if not plan.ordered:
        out_grad = plan.to_local(out_grad, 1)
    down_far = contract_rows(out_grad[:, near_cols:], active).astype(low)
    down_far, active, grad_both, out_grad, normed_rows = fence(
        down_far, active, grad_both, out_grad, normed_rows
    )

    down_got = plan.core_swap(down_far)
    gate_far = contract_rows(normed_rows[:, near_cols:], grad_both).astype(low)
    down_parts = zone_parts(contract_rows(out_grad[:, :near_cols], active), down_got)
    gate_far, down_parts, grad_both, normed_rows = fence(
        gate_far, down_parts, grad_both, normed_rows
    )

    gate_got = plan.core_swap(gate_far)
    if tree:
        down_sums = [plan.inward(down_parts[3])]
    else:
        down_sums = plan.to_zones(down_parts, slots)
    post_terms = contract_cols(grad_both, full_gate).astype(low)
    post_terms, gate_got, down_parts, down_sums, grad_both, normed_rows = fence(
        post_terms, gate_got, down_parts, down_sums, grad_both, normed_rows
    )

    if tree:
        down_sums += [plan.inward(down_parts[2])]
    gate_parts = zone_parts(contract_rows(normed_rows[:, :near_cols], grad_both), gate_got)
    post_terms, gate_parts, down_parts, down_sums = fence(
        post_terms, gate_parts, down_parts, down_sums
    )

    eighth = tok_rows // 8
    own_grad = jnp.concatenate([out_grad[:eighth], out_grad[2 * eighth : 3 * eighth]], 0)
    branch_rows, grad_hidden, post_gain_grad, mlp_terms, gate_sums = sum_rows(
        plan,
        spread_kernel,
        grad_hidden_rows,
        post_terms,
        [hidden, own_grad, gain_post],
        [
            jax.ShapeDtypeStruct((tok_rows // 4, model_width), jnp.float32),
            jax.ShapeDtypeStruct((1, model_width), jnp.float32),
        ],
        1,
        [
            SideDot(active, full_down),
            PairScatter(gate_parts) if tree else ZoneBlocks(plan, gate_parts, slots),
        ],
    )
    branch_rows, grad_hidden, post_gain_grad, gate_sums, mlp_terms, down_parts, down_sums = fence(
        branch_rows, grad_hidden, post_gain_grad, gate_sums, mlp_terms, down_parts, down_sums
    )

    mlp_got = plan.first_swap(mlp_terms[kept:])
    if tree:
        gate_last = [plan.zone_flip(gate_sums[1], 1)]
        gate_own = gate_sums
        down_pair = down_parts[2:].astype(jnp.float32) + jnp.stack(down_sums).astype(jnp.float32)
        down_sums = plan.middle_swap(down_pair.astype(low))
    else:
        gate_last, gate_own = gate_sums, gate_parts
    grad_att = jnp.dot(branch_rows, full_out, preferred_element_type=jnp.float32).astype(low)
    grad_mixed, mixed_rows, query_gain_grad, key_gain_grad = attention_back(
        query, key_rot, values_low, raw, grad_att, gain_q, gain_k, cosine, signed_sine
    )
    gain_terms = jnp.concatenate(
        [plan.to_natural(post_gain_grad, 1), query_gain_grad, key_gain_grad], 1
    )
    if tree:
        down_own = (down_parts[:2].astype(jnp.float32) + down_sums.astype(jnp.float32)).astype(low)
    grad_mixed, mixed_rows, gain_terms, normed, gate_last, branch_rows, mlp_got, down_sums = fence(
        grad_mixed, mixed_rows, gain_terms, normed, gate_last, branch_rows, mlp_got, down_sums
    )

    mlp_own, mlp_last = plan.second_swap(mlp_terms[:kept].astype(jnp.float32), mlp_got)
    if tree:
        total_down = zone_total(down_own, [plan.zone_flip(down_own[1], 1)])
    else:
        total_down = zone_total(down_parts, down_sums)
    total_gate = zone_total(gate_own, gate_last)
    total_gate = jnp.concatenate([total_gate[:, :units], total_gate[:, units:]], 0)
    out_far = contract_rows(branch_rows[:, near_cols:], attended).astype(low)
    out_got = plan.core_swap(out_far)
    normed_terms = contract_cols(mixed_rows, full_qkv).astype(low)
    out_parts = zone_parts(contract_rows(branch_rows[:, :near_cols], attended), out_got)
    block_own = (hidden + mlp_own + jnp.concatenate(mlp_last, 0).astype(jnp.float32)).astype(low)
    out_parts, normed_terms, total_gate, total_down, block_own, normed, grad_mixed = fence(
        out_parts, normed_terms, total_gate, total_down, block_own, normed, grad_mixed
    )

    gain_sum = GainSum(plan, gain_terms.shape[1], model_width) if plan.ordered else None
    mine, input_gain_grad, *rest = sum_rows(
        plan,
        home_kernel,
        grad_input_rows,
        normed_terms,
        [own_tokens, grad_hidden, gain_in, block_own] + ([gain_terms] if plan.ordered else []),
        [jax.ShapeDtypeStruct((1, model_width), jnp.float32)],
        2,
        [
            BlockGrad(plan, normed, grad_mixed),
            ZoneBlocks(plan, out_parts, slots),
            TurnLate(total_gate),
            TurnLate(total_down),
        ],
        gain_sum,
    )
    if plan.ordered:
        summed_gains, total_qkv, out_sent, got_gate, got_down = rest
    else:
        total_qkv, out_sent, got_gate, got_down = rest
        summed_gains = plan.sum_everywhere(
            jnp.concatenate([plan.to_natural(input_gain_grad, 1), gain_terms], 1)
        )
    mine, summed_gains, total_qkv, out_sent, got_gate, got_down = fence(
        mine, summed_gains, total_qkv, out_sent, got_gate, got_down
    )

    summed_gate = plan.turned(total_gate, got_gate).reshape(gate_up.shape)
    summed_down = plan.turned(total_down, got_down)
    other = plan.core_swap(mine)
    input_full, block_out = jnp.where(plan.home, mine, other), jnp.where(plan.home, other, mine)
    if not plan.ordered:
        input_full = plan.to_natural(input_full, 1, plan.side)
        block_out = plan.to_natural(block_out, 1, plan.side)
    summed_both = plan.turn(
        jnp.concatenate([total_qkv, zone_total(out_parts, out_sent)], 1)
    ).astype(jnp.float32)
    summed_qkv = summed_both[:, :mixed_cols].reshape(qkv_weight.shape)
    summed_out = summed_both[:, mixed_cols:]
    summed_gate = summed_gate.astype(jnp.float32)
    summed_down = summed_down.astype(jnp.float32)
    summed_gains = lax.dynamic_slice_in_dim(summed_gains[0], plan.index * gain_count, gain_count, 0)
    input_rows = input_full.astype(jnp.float32)

    qkv_moment, qkv_square, qkv_updated = adamw(
        qkv_weight, summed_qkv, qkv_first, qkv_second, RATE_QKV, DECAY_RATE
    )
    out_moment, out_square, out_updated = adamw(
        out_weight, summed_out, out_first, out_second, RATE_OUT, DECAY_RATE
    )
    gate_moment, gate_square, gate_updated = adamw(
        gate_up, summed_gate, gate_up_first, gate_up_second, RATE_GATE, DECAY_RATE
    )
    down_moment, down_square, down_updated = adamw(
        down_weight, summed_down, down_first, down_second, RATE_DOWN, DECAY_RATE
    )
    gain_moment, gain_square, gain_updated = adamw(
        gains, summed_gains, gains_first, gains_second, RATE_GAIN, 0.0
    )
    return (
        block_out,
        input_rows,
        qkv_moment,
        qkv_square,
        qkv_updated,
        out_moment,
        out_square,
        out_updated,
        gate_moment,
        gate_square,
        gate_updated,
        down_moment,
        down_square,
        down_updated,
        gain_moment,
        gain_square,
        gain_updated,
    )


def solution(mesh):
    plan = Plan(mesh)
    placed = (
        P("dp", None),
        P("dp"),
        P("dp", None),
        P("dp", "tensor", None, None),
        P("dp", "tensor", None, None),
        P("dp", "tensor", None, None),
        P("dp", "tensor"),
        P("dp", "tensor"),
        P("dp", "tensor"),
        P(None, "dp", "tensor"),
        P(None, "dp", "tensor"),
        P(None, "dp", "tensor"),
        P("dp", "tensor"),
        P("dp", "tensor"),
        P("dp", "tensor"),
        P("dp"),
        P("dp"),
        P("dp"),
    )
    return jax.shard_map(
        functools.partial(shards, plan),
        mesh=mesh,
        in_specs=placed,
        out_specs=(
            P("dp", None),
            P("dp", None),
            P("dp", "tensor", None, None),
            P("dp", "tensor", None, None),
            P("dp", "tensor", None, None),
            P("dp", "tensor"),
            P("dp", "tensor"),
            P("dp", "tensor"),
            P(None, "dp", "tensor"),
            P(None, "dp", "tensor"),
            P(None, "dp", "tensor"),
            P("dp", "tensor"),
            P("dp", "tensor"),
            P("dp", "tensor"),
            P("dp"),
            P("dp"),
            P("dp"),
        ),
        check_vma=False,
    )
```

```python
import functools
import math

import jax
import jax.numpy as jnp
from jax import lax
from jax.experimental import pallas as pl
from jax.experimental.pallas import tpu as pltpu
from jax.sharding import PartitionSpec as P

SEQ = 1024
STEP = 10


EPS_NORM = 1e-06
THETA = 1000000.0
BETA_ONE = 0.9
BETA_TWO = 0.95
ADAM_EPS = 1e-08
DECAY_RATE = 0.1
RATE_QKV = 0.05
RATE_OUT = 0.3
RATE_GATE = 0.05
RATE_DOWN = 0.03
RATE_GAIN = 1.0


def rotary(positions, head_size):
    freq_index = jnp.arange(head_size // 2, dtype=jnp.float32)
    inverse = jnp.exp(freq_index * (-2.0 * math.log(THETA) / head_size))
    angles = positions.astype(jnp.float32)[:, None] * inverse[None, :]
    cosine = jnp.cos(angles)
    sine_table = jnp.sin(angles)
    return (jnp.concatenate([cosine, cosine], -1), jnp.concatenate([sine_table, sine_table], -1))


def rotate(values, cosine, sine_table):
    half_size = values.shape[-1] // 2
    turned = jnp.concatenate([-values[..., half_size:], values[..., :half_size]], -1)
    return values * cosine[:, None, :] + turned * sine_table[:, None, :]


def unrotate(gradient, cosine, sine_table):
    half_size = gradient.shape[-1] // 2
    turned = gradient * sine_table[:, None, :]
    rotated_back = jnp.concatenate([turned[..., half_size:], -turned[..., :half_size]], -1)
    return gradient * cosine[:, None, :] + rotated_back


def norm_back(grad_unit, unit_vals, factor):
    return factor * (grad_unit - unit_vals * jnp.mean(grad_unit * unit_vals, -1, keepdims=True))


def contract_rows(left, right):
    return lax.dot_general(
        left, right, (((0,), (0,)), ((), ())), preferred_element_type=jnp.float32
    )


def contract_cols(left, right):
    return lax.dot_general(
        left, right, (((1,), (1,)), ((), ())), preferred_element_type=jnp.float32
    )


def block_scores(query_part, key_part, first_row, block_rows, last_row):
    scores = jnp.einsum(
        "nqkgd,nskd->nkgqs", query_part, key_part, preferred_element_type=jnp.float32
    )
    causal = (first_row + jnp.arange(block_rows))[:, None] >= jnp.arange(last_row)[None, :]
    return jnp.where(causal, scores, -1000000000.0)


def attention_forward(query, key_rot, values_low, seq_len):
    block_rows = min(512, seq_len)
    outputs = []
    log_sums = []
    for first_row in range(0, seq_len, block_rows):
        last_row = first_row + block_rows
        query_part = query[:, first_row:last_row]
        scores = block_scores(query_part, key_rot[:, :last_row], first_row, block_rows, last_row)
        row_max = jnp.max(scores, -1, keepdims=True)
        exponent = jnp.exp(scores - row_max)
        row_total = jnp.sum(exponent, -1, keepdims=True)
        probs_low = (exponent / row_total).astype(jnp.bfloat16)
        outputs.append(
            jnp.einsum(
                "nkgqs,nskd->nqkgd",
                probs_low,
                values_low[:, :last_row],
                preferred_element_type=jnp.float32,
            )
        )
        log_sums.append(row_max + jnp.log(row_total))
    return (jnp.concatenate(outputs, 1), log_sums)


def attention_backward(query, key_rot, values_low, grad_att, log_sums, seq_len):
    block_rows = min(512, seq_len)
    query_grads = []
    key_grad = jnp.zeros(key_rot.shape, jnp.float32)
    value_grad = jnp.zeros(values_low.shape, jnp.float32)
    for block_index, first_row in enumerate(range(0, seq_len, block_rows)):
        last_row = first_row + block_rows
        query_part = query[:, first_row:last_row]
        grad_part = grad_att[:, first_row:last_row]
        key_part = key_rot[:, :last_row]
        value_part = values_low[:, :last_row]
        scores = block_scores(query_part, key_part, first_row, block_rows, last_row)
        probs = jnp.exp(scores - log_sums[block_index])
        probs_low = probs.astype(jnp.bfloat16)
        grad_probs = jnp.einsum(
            "nqkgd,nskd->nkgqs", grad_part, value_part, preferred_element_type=jnp.float32
        )
        grad_scores = (
            probs * (grad_probs - jnp.sum(probs * grad_probs, -1, keepdims=True))
        ).astype(jnp.bfloat16)
        query_grads.append(
            jnp.einsum(
                "nkgqs,nskd->nqkgd", grad_scores, key_part, preferred_element_type=jnp.float32
            )
        )
        padding = ((0, 0), (0, seq_len - last_row), (0, 0), (0, 0))
        key_grad = key_grad + jnp.pad(
            jnp.einsum(
                "nkgqs,nqkgd->nskd", grad_scores, query_part, preferred_element_type=jnp.float32
            ),
            padding,
        )
        value_grad = value_grad + jnp.pad(
            jnp.einsum(
                "nkgqs,nqkgd->nskd", probs_low, grad_part, preferred_element_type=jnp.float32
            ),
            padding,
        )
    return (jnp.concatenate(query_grads, 1), key_grad, value_grad)


def adamw(weight, gradient, moment, second, step_rate, decay_rate):
    moment = BETA_ONE * moment + (1.0 - BETA_ONE) * gradient
    second = BETA_TWO * second + (1.0 - BETA_TWO) * gradient * gradient
    first_hat = moment / (1.0 - BETA_ONE**STEP)
    second_hat = second / (1.0 - BETA_TWO**STEP)
    weight = weight - step_rate * (
        first_hat / (jnp.sqrt(second_hat) + ADAM_EPS) + decay_rate * weight
    )
    return (moment, second, weight)


def fence(*values):
    return lax.optimization_barrier(values)


MESH = pl.DeviceIdType.MESH
HEAD = 128
AHEAD = 2


def place_here():
    index, place = lax.axis_index("dp"), lax.axis_index("tensor")
    return lax.div(index, 2), lax.rem(index, 2), lax.div(place, 2), lax.rem(place, 2)


def device(zone, side, row, core):
    return (zone * 2 + side, row * 2 + core)


def flipped(zone, flip):
    bit = 1
    while bit <= flip:
        if flip & bit:
            zone = zone + bit - 2 * bit * lax.rem(lax.div(zone, bit), 2)
        bit *= 2
    return zone


def greet(devices, amount=None):
    barrier = pltpu.get_barrier_semaphore()
    for peer in devices:
        pl.semaphore_signal(barrier, inc=1, device_id=peer, device_id_type=MESH)
    pl.semaphore_wait(barrier, len(devices) if amount is None else amount)


def for_rows(count, body):
    step = 32

    def one(block, carry):
        body(pl.multiple_of(block * step, step), step)
        return carry

    lax.fori_loop(0, count // step, one, 0)


class Copies:
    def __init__(self, send_sems, recv_sems):
        self.send_sems, self.recv_sems = send_sems, recv_sems
        self.number = 0

    def make(self, source, target, peer):
        number, self.number = self.number, self.number + 1
        return pltpu.make_async_remote_copy(
            src_ref=source,
            dst_ref=target,
            send_sem=self.send_sems.at[number],
            recv_sem=self.recv_sems.at[number],
            device_id=peer,
            device_id_type=MESH,
        )

    def start(self, source, target, peer):
        copy = self.make(source, target, peer)
        copy.start()
        return copy


class GainSum:
    def __init__(self, plan, rest, width):
        self.plan, self.width = plan, width
        self.total = width + rest
        self.scratch = [
            pltpu.VMEM((8, 1, self.total), jnp.float32),
            pltpu.VMEM((plan.zones, 1, self.total), jnp.float32),
        ]
        self.output = jax.ShapeDtypeStruct((1, self.total), jnp.float32)
        self.count = 7 + plan.zones - 1

    def plane_peers(self, zone, side, row, core):
        steps = [(s, r, c) for s in range(2) for r in range(2) for c in range(2)][1:]
        turn = lambda value, step: 1 - value if step else value
        return [device(zone, turn(side, s), turn(row, r), turn(core, c)) for s, r, c in steps]

    def zone_peers(self, zone, side, row, core):
        return {flip: device(flipped(zone, flip), side, row, core) for flip in self.plan.flips[1:]}

    def start(self, copies, rest, blocks, plane_sums, zone_sums):
        zone, side, row, core = place_here()
        plan = self.plan
        size = self.width // plan.total
        self.copies, self.plane_sums, self.zone_sums, self.zone = copies, plane_sums, zone_sums, zone
        here = side * 4 + row * 2 + core
        plane_sums[here, :, pl.ds(self.width, self.total - self.width)] = rest[...]
        for slot in range(plan.total):
            owner = flipped(zone, plan.flips[slot % plan.zones]) * 2
            owner = owner + (core if slot < plan.zones else 1 - core)
            spot = pl.ds(pl.multiple_of(owner * size, size), size)
            plane_sums[here, :, spot] = blocks[:, pl.ds(slot * size, size)]
        self.plane = [
            copies.start(plane_sums.at[here], plane_sums.at[here], peer)
            for peer in self.plane_peers(zone, side, row, core)
        ]

    def middle(self):
        for copy in self.plane:
            copy.wait_recv()
        total = self.plane_sums[0]
        for place in range(1, 8):
            total = total + self.plane_sums[place]
        self.zone_sums[self.zone] = total
        zone, side, row, core = place_here()
        self.across = [
            self.copies.start(self.zone_sums.at[self.zone], self.zone_sums.at[self.zone], peer)
            for peer in self.zone_peers(zone, side, row, core).values()
        ]

    def finish(self, out):
        for copy in self.across:
            copy.wait_recv()
        total = self.zone_sums[0]
        for place in range(1, self.plan.zones):
            total = total + self.zone_sums[place]
        out[...] = total
        for copy in self.plane + self.across:
            copy.wait_send()


class ZoneBlocks:
    scratch = []

    def __init__(self, plan, source, slots, begin=0):
        self.flips, self.slots, self.sources, self.begin = plan.flips, list(slots), [source], begin
        self.outputs = [
            jax.ShapeDtypeStruct((len(self.slots),) + source.shape[1:], source.dtype)
        ]
        self.count, self.count_local = len(self.slots), 0
        self.in_hbm = False

    def peers(self, zone, side, row, core):
        return {
            self.flips[slot]: device(flipped(zone, self.flips[slot]), side, row, core)
            for slot in self.slots
        }

    def start(self, copies, local_sems, sources, targets, stages):
        zone, side, row, core = place_here()
        self.started = [
            copies.make(
                sources[0].at[slot],
                targets[0].at[number],
                device(flipped(zone, self.flips[slot]), side, row, core),
            )
            for number, slot in enumerate(self.slots)
        ]
        self.waiting = True
        if self.begin == 0:
            self.pump([0])

    def pump(self, steps):
        if self.waiting and self.begin in steps:
            self.waiting = False
            for copy in self.started:
                copy.start()

    def finish(self):
        for copy in self.started:
            copy.wait_send()
        for copy in self.started:
            copy.wait_recv()


def due(point, early, total):
    if 0 in point:
        return range(early)
    return range(early, early + 1) if 1 in point else range(early + 1, total)


def inner_zone(zone):
    return lax.rem(lax.div(zone + 1, 2), 2)


class SideDot:
    count, count_local, scratch, in_hbm = 0, 0, [], False

    def __init__(self, left, right):
        self.sources = [left, right]
        self.outputs = [jax.ShapeDtypeStruct((left.shape[0], right.shape[0]), jnp.bfloat16)]

    def peers(self, zone, side, row, core):
        return {}

    def some(self, first, last):
        left, right = self.refs
        size = 256

        def one(step, carry):
            here = pl.ds(pl.multiple_of(step * size, size), size)
            self.out[:, here] = dot(left[...], right[here, :], 1, 1).astype(jnp.bfloat16)
            return carry

        lax.fori_loop(first, last, one, 0)

    def start(self, copies, local_sems, sources, targets, stages):
        self.refs, self.out = sources, targets[0]
        self.steps = self.out.shape[1] // 256
        self.some(0, self.steps // 2)

    def pump(self, steps):
        if 0 in steps:
            self.some(self.steps // 2, self.steps)

    def finish(self):
        pass


class PairScatter:
    def __init__(self, parts):
        self.sources = [parts]
        _, rows, columns = parts.shape
        self.outputs = [jax.ShapeDtypeStruct((2, rows, columns), parts.dtype)]
        self.scratch = [pltpu.VMEM((2, rows, columns), parts.dtype)] * 2
        self.count, self.count_local = 14, 0
        self.in_hbm = False

    def peers(self, zone, side, row, core):
        return {
            1: device(flipped(zone, 1), side, row, core),
            3: device(flipped(zone, 3), side, row, core),
        }

    def start(self, copies, local_sems, sources, targets, stages):
        zone, side, row, core = place_here()
        self.parts, self.out = sources[0], targets[0]
        self.inward, self.crossed = stages
        inner_peer = device(flipped(zone, 3), side, row, core)
        outer_peer = device(flipped(zone, 1), side, row, core)
        self.inner = inner_zone(zone) == 1
        self.outer = inner_zone(zone) == 0
        rows = self.parts.shape[1]
        cuts = ((0, (rows // 4, rows // 4, rows // 2)), (1, (rows // 4,) * 4))
        self.steps = [
            (slot, pl.ds(sum(sizes[:place]), size))
            for slot, sizes in cuts
            for place, size in enumerate(sizes)
        ]
        self.to_inner = [
            copies.make(self.parts.at[3 - slot, rows], self.inward.at[slot, rows], outer_peer)
            for slot, rows in self.steps
        ]
        self.across = [
            copies.make(self.inward.at[slot, rows], self.crossed.at[slot, rows], inner_peer)
            for slot, rows in self.steps
        ]

        @pl.when(self.outer)
        def _():
            for copy in self.to_inner[:AHEAD]:
                copy.start()

    def add(self, target, slot, rows, left, right):
        def some(row, count):
            here = pl.ds(rows.start + row, count)
            both = left[here, :].astype(jnp.float32) + right[here, :].astype(jnp.float32)
            target.at[slot][here, :] = both.astype(jnp.bfloat16)

        for_rows(rows.size, some)

    def pump(self, steps):
        steps = due(steps, 2, len(self.steps))

        @pl.when(self.inner)
        def _():
            for step in steps:
                slot, rows = self.steps[step]
                self.to_inner[step].wait_recv()
                self.add(self.inward, slot, rows, self.parts.at[2 + slot], self.inward.at[slot])
                self.across[step].start()
                if step >= AHEAD:
                    self.settle(step - AHEAD)

        @pl.when(self.outer)
        def _():
            for step in steps:
                self.to_inner[step].wait_send()
                for copy in self.to_inner[step + AHEAD : step + AHEAD + 1]:
                    copy.start()

    def settle(self, step):
        slot, rows = self.steps[step]
        self.across[step].wait_recv()
        self.add(self.out, slot, rows, self.parts.at[slot], self.crossed.at[slot])

    def finish(self):
        @pl.when(self.inner)
        def _():
            for step in range(len(self.steps) - AHEAD, len(self.steps)):
                self.settle(step)
            for copy in self.across:
                copy.wait_send()

        @pl.when(self.outer)
        def _():
            for slot in (0, 1):

                def some(row, count, slot=slot):
                    here = pl.ds(row, count)
                    self.out.at[slot][here, :] = self.parts.at[slot][here, :]

                for_rows(self.parts.shape[1], some)


class BlockGrad:
    in_hbm = False

    def __init__(self, plan, left, right):
        self.zones, self.flips = plan.zones, plan.flips
        self.sources = [left, right]
        shape = (left.shape[1] // plan.total, right.shape[1])
        low = jnp.bfloat16
        self.outputs = [jax.ShapeDtypeStruct(shape, low)]
        self.scratch = [pltpu.VMEM((plan.zones,) + shape, low)] * 4
        self.count, self.count_local = 2 * plan.zones, 0

    def peers(self, zone, side, row, core):
        return {flip: device(flipped(zone, flip), side, row, core) for flip in self.flips[1:]}

    def product(self, block):
        size = self.out.shape[0]
        return dot(self.left[:, pl.ds(block * size, size)], self.right[...], 0, 0)

    def start(self, copies, local_sems, sources, targets, stages):
        zone, side, row, core = place_here()
        self.left, self.right = sources
        self.out = targets[0]
        self.far, self.got, self.parts, self.arrived = stages
        core_peer = device(zone, side, row, 1 - core)
        self.order = list(range(2, self.zones)) + [1, 0]
        self.over = [
            copies.make(self.far.at[slot], self.got.at[slot], core_peer)
            for slot in range(self.zones)
        ]
        self.along = [
            copies.make(
                self.parts.at[slot],
                self.arrived.at[slot],
                device(flipped(zone, self.flips[slot]), side, row, core),
            )
            for slot in range(1, self.zones)
        ]
        for slot in self.order:
            self.far[slot] = self.product(self.zones + slot).astype(jnp.bfloat16)
            self.over[slot].start()

    def pump(self, steps):
        for slot in self.order if 0 in steps else []:
            near = self.product(slot)
            self.over[slot].wait_recv()
            self.parts[slot] = (near + self.got[slot].astype(jnp.float32)).astype(jnp.bfloat16)
            if slot:
                self.along[slot - 1].start()

    def finish(self):
        total = self.parts[0].astype(jnp.float32)
        for slot in range(1, self.zones):
            self.along[slot - 1].wait_recv()
            total = total + self.arrived[slot].astype(jnp.float32)
        self.out[...] = total.astype(jnp.bfloat16)
        for copy in self.over + self.along:
            copy.wait_send()


class TurnLate:
    count, count_local, scratch, in_hbm = 1, 0, [], False

    def __init__(self, values):
        self.sources = [values]
        self.outputs = [jax.ShapeDtypeStruct(values.shape, values.dtype)]

    def peers(self, zone, side, row, core):
        return {}

    def start(self, copies, local_sems, sources, targets, stages):
        zone, side, row, core = place_here()
        self.away = side != core
        self.copy = copies.make(sources[0], targets[0], device(zone, core, row, side))

    def pump(self, steps):
        pass

    def late(self):
        @pl.when(self.away)
        def _():
            self.copy.start()

    def finish(self):
        @pl.when(self.away)
        def _():
            self.copy.wait_recv()
            self.copy.wait_send()


class PairTree:
    def __init__(self, pairs):
        halves_of = [own.shape[0] // 2 for own, *_ in pairs]
        self.cuts = [
            (size // 2, size // 2, size) if weight == 0 else (size, size)
            for weight, size in enumerate(halves_of)
        ]
        pieces = [len(cut) for cut in self.cuts]
        self.pairs = [len(pair) for pair in pairs]
        self.sources = [shard for pair in pairs for shard in pair]
        self.outputs = [
            jax.ShapeDtypeStruct((8,) + own.shape, own.dtype) for own, *_ in pairs
        ]
        self.count = 6 * sum(pieces) + 2 * len(pairs) + self.pairs.count(1)
        self.count_local = 2 * len(pairs) + 2 * sum(pieces)
        self.scratch = [pltpu.VMEM((2,) + own.shape, own.dtype) for own, *_ in pairs]
        self.scratch += [pltpu.VMEM(p[0].shape, p[0].dtype) for p in pairs if len(p) == 1]
        self.in_hbm = True

    def peers(self, zone, side, row, core):
        return {
            1: device(flipped(zone, 1), side, row, core),
            3: device(flipped(zone, 3), side, row, core),
            "core": device(zone, side, row, 1 - core),
        }

    def start(self, copies, local_sems, sources, targets, stages):
        zone, side, row, core = place_here()
        inner_peer = device(flipped(zone, 3), side, row, core)
        outer_peer = device(flipped(zone, 1), side, row, core)
        core_peer = device(zone, side, row, 1 - core)
        self.inner = inner_zone(zone) == 1
        self.outer = inner_zone(zone) == 0
        self.across, self.onward, self.late, self.place = [], [], [], []
        self.shared, self.kept, self.partners, self.later = [], [], [], []
        sem = 0
        sources, late_stages = list(sources), list(stages[len(targets) :])
        for weight, full in enumerate(targets):
            landing = stages[weight]
            pair = [sources.pop(0) for _ in range(self.pairs[weight])]
            if len(pair) == 1:
                pair.append(late_stages.pop(0))
                self.partners.append(copies.start(pair[0], pair[1], outer_peer))
            for place, size in enumerate(self.cuts[weight]):
                rows = pl.ds(sum(self.cuts[weight][:place]), size)
                for slot in (0, 1):
                    here = landing.at[slot, rows]
                    self.across.append(copies.make(pair[slot].at[rows], here, inner_peer))
                    self.onward.append(copies.make(here, landing.at[1 - slot, rows], outer_peer))
                    self.late.append(copies.make(here, full.at[6 + slot, rows], core_peer))
                    self.place.append(
                        pltpu.make_async_copy(here, full.at[2 + slot, rows], local_sems.at[sem])
                    )
                    sem += 1
            for slot in (0, 1):
                self.shared.append(copies.make(pair[slot], full.at[4 + slot], core_peer))
                self.kept.append(
                    pltpu.make_async_copy(pair[slot], full.at[slot], local_sems.at[sem])
                )
                sem += 1
                if slot >= self.pairs[weight]:
                    self.later += [self.shared[-1], self.kept[-1]]
                else:
                    self.shared[-1].start()
                    self.kept[-1].start()

        @pl.when(self.inner)
        def _():
            for copy in self.across[:AHEAD]:
                copy.start()

    def arrive(self, number):
        self.onward[number].wait_recv()
        swapped = number + 1 - 2 * (number % 2)
        self.late[swapped].start()
        self.place[swapped].start()

    def pump(self, steps):
        middle = 1 in steps
        steps = due(steps, 3, len(self.across))

        @pl.when(self.inner)
        def _():
            for here in steps:
                self.across[here].wait_recv()
                for copy in self.across[here + AHEAD : here + AHEAD + 1]:
                    copy.start()
                self.onward[here].start()
                self.late[here].start()
                self.place[here].start()

        @pl.when(self.outer)
        def _():
            for step in steps:
                if step > 0:
                    self.arrive(step - 1)

        for copy in self.partners if middle else []:
            copy.wait_recv()
            copy.wait_send()
        for copy in self.later if middle else []:
            copy.start()

    def finish(self):
        @pl.when(self.inner)
        def _():
            for copy in self.across + self.onward:
                copy.wait_send()

        @pl.when(self.outer)
        def _():
            self.arrive(len(self.onward) - 1)

        for copy in self.kept + self.place:
            copy.wait()
        for copy in self.shared + self.late:
            copy.wait_send()
        for copy in self.shared + self.late:
            copy.wait_recv()


def sum_eighths(
    copies, row_peer, side_peer, send, keep, forward, first, second, store, begin, pump
):
    size = send.shape[0] // 4
    part = lambda ref, slot: ref.at[pl.ds(slot * size, size)]
    arrivals = [
        copies.start(part(send, 1), part(first, 1), row_peer),
        copies.start(part(send, 3), part(first, 3), side_peer),
        copies.start(part(send, 0), part(first, 0), row_peer),
        copies.start(part(send, 2), part(first, 2), side_peer),
    ]
    begin()
    passed = []
    for number, slot, peer in ((0, 1, side_peer), (1, 3, row_peer)):
        arrivals[number].wait_recv()

        def add(row, count, number=number, slot=slot):
            here = pl.ds(slot * size + row, count)
            both = keep[here, :].astype(jnp.float32) + first[here, :].astype(jnp.float32)
            forward[pl.ds(number * size + row, count), :] = both.astype(jnp.bfloat16)

        for_rows(size, add)
        passed.append(copies.start(part(forward, number), part(second, number), peer))
    pump([0])
    for number, slot in ((0, 0), (1, 2)):
        arrivals[2 + number].wait_recv()
        passed[number].wait_recv()

        def total(row, count, number=number, slot=slot):
            here = pl.ds(slot * size + row, count)
            sums = keep[here, :].astype(jnp.float32) + first[here, :].astype(jnp.float32)
            sums = sums + second[pl.ds(number * size + row, count), :].astype(jnp.float32)
            store(number, row, count, sums)

        for_rows(size, total)
        yield number
    for copy in arrivals + passed:
        copy.wait_send()


def halves(terms):
    rows = terms.shape[0] // 2
    return terms.at[pl.ds(0, rows)], terms.at[pl.ds(rows, rows)]


def split_refs(refs, jobs, extra_count, out_count):
    refs = list(refs)
    take = lambda count: [refs.pop(0) for _ in range(count)]
    extras = take(extra_count)
    sources = [take(len(job.sources)) for job in jobs]
    full = take(1)[0]
    outs = take(out_count)
    targets = [take(len(job.outputs)) for job in jobs]
    return extras, sources, full, outs, targets, refs


def spread_kernel(middle, jobs, extra_count, out_count, gain_sum, plan, terms, *refs):
    keep, send = halves(terms)
    extras, sources, full, outs, targets, scratch = split_refs(refs, jobs, extra_count, out_count)
    forward, first, second, send_sems, recv_sems, local_sems, *stages = scratch
    zone, side, row, core = place_here()
    row_peer, side_peer = device(zone, side, 1 - row, core), device(zone, 1 - side, row, core)
    copies = Copies(send_sems, recv_sems)
    size = send.shape[0] // 4
    part = lambda slot: full.at[pl.ds(slot * size, size)]
    for out in outs:
        if out.shape[0] == 1:
            out[...] = jnp.zeros_like(out)
    peers = {}
    for job in jobs:
        peers.update(job.peers(zone, side, row, core))
    greet([row_peer, side_peer] + list(peers.values()))

    def begin():
        spot = 0
        for job, source, target in zip(jobs, sources, targets):
            own_stages = stages[spot : spot + len(job.scratch)]
            job.start(copies, local_sems, source, target, own_stages)
            spot += len(job.scratch)

    def pump(steps):
        for job in jobs:
            job.pump(steps)

    def store(number, row, count, sums):
        own = pl.ds(number * size + row, count)
        full[pl.ds(2 * number * size + row, count), :] = middle(own, sums, extras, outs)

    firsts, seconds = [], []
    for number in sum_eighths(
        copies, row_peer, side_peer, send, keep, forward, first, second, store, begin, pump
    ):
        near, other = (side_peer, row_peer) if number == 0 else (row_peer, side_peer)
        slot = 2 * number
        firsts.append(copies.start(part(slot), part(slot + 1), near))
        seconds.append(copies.start(part(slot), part(4 + slot), other))
    pump([1])
    firsts[0].wait_recv()
    seconds.append(copies.start(part(1), part(5), row_peer))
    firsts[1].wait_recv()
    seconds.append(copies.start(part(3), part(7), side_peer))
    pump(range(2, 64))
    for copy in seconds:
        copy.wait_recv()
    for copy in firsts + seconds:
        copy.wait_send()
    for job in jobs:
        job.finish()


def home_kernel(middle, jobs, extra_count, out_count, gain_sum, plan, terms, *refs):
    keep, send = halves(terms)
    extras, sources, result, outs, targets, scratch = split_refs(refs, jobs, extra_count, out_count)
    forward, first, second, own, full, send_sems, recv_sems, local_sems, *rest = scratch
    gain_scratch, stages = (rest[:2], rest[2:]) if gain_sum is not None else ([], rest)
    block = extras[3]
    zone, side, row, core = place_here()
    row_peer, side_peer = device(zone, side, 1 - row, core), device(zone, 1 - side, row, core)
    core_peer, other_peer = device(zone, side, row, 1 - core), device(zone, 1 - side, row, 1 - core)
    copies = Copies(send_sems, recv_sems)
    size = send.shape[0] // 4
    at_home = side == core
    away = side != core
    for out in outs:
        if out.shape[0] == 1:
            out[...] = jnp.zeros_like(out)
    peers = {}
    for job in jobs:
        peers.update(job.peers(zone, side, row, core))
    plane = [row_peer, side_peer, core_peer, other_peer]
    if gain_sum is not None:
        plane = gain_sum.plane_peers(zone, side, row, core)
        peers.update(gain_sum.zone_peers(zone, side, row, core))
    greet(plane + list(peers.values()))

    def begin():
        spot = 0
        for job, source, target in zip(jobs, sources, targets):
            own_stages = stages[spot : spot + len(job.scratch)]
            job.start(copies, local_sems, source, target, own_stages)
            spot += len(job.scratch)

    def pump(steps):
        if 0 in steps:

            @pl.when(away)
            def _():
                for copy in block_side:
                    copy.start()

        for job in jobs:
            job.pump(steps)

    def store(number, start, count, sums):
        here = pl.ds(number * size + start, count)
        values = middle(here, sums, extras, outs)
        own[here, :] = values
        eighth = row * 2 + side if number == 0 else 4 + side * 2 + row

        @pl.when(at_home)
        def _():
            full[pl.ds(pl.multiple_of(eighth * size + start, 32), count), :] = values

    def piece(number, x, y):
        start = (x * 2 + y) * size if number == 0 else (4 + y * 2 + x) * size
        return full.at[pl.ds(pl.multiple_of(start, size), size)]

    both = (0, 1)
    part = lambda ref, number: ref.at[pl.ds(number * size, size)]
    block_over = [copies.make(part(block, k), piece(k, row, side), core_peer) for k in both]
    block_side = [copies.make(part(block, k), piece(k, row, side), other_peer) for k in both]
    to_side = [copies.make(part(own, k), piece(k, row, side), side_peer) for k in both]
    to_row = [copies.make(piece(k, row, side), piece(k, row, side), row_peer) for k in both]
    pass_row = [
        copies.make(piece(k, row, 1 - side), piece(k, row, 1 - side), row_peer) for k in both
    ]

    @pl.when(at_home)
    def _():
        for copy in block_over:
            copy.start()

    for _ in sum_eighths(
        copies, row_peer, side_peer, send, keep, forward, first, second, store, begin, pump
    ):
        pass
    pump([1])
    if gain_sum is not None:
        gain_sum.start(copies, extras[-1], outs[0], *gain_scratch)

    @pl.when(away)
    def _():
        for copy in to_side:
            copy.start()
        for copy in block_over:
            copy.wait_recv()

    for copy in to_row:
        copy.start()
    for job in jobs:
        if isinstance(job, TurnLate):
            job.late()
    if gain_sum is not None:
        gain_sum.middle()

    @pl.when(at_home)
    def _():
        for copy in to_side:
            copy.wait_recv()
        for copy in block_over:
            copy.wait_send()

    @pl.when(away)
    def _():
        for copy in block_side:
            copy.wait_recv()

    for copy in pass_row:
        copy.start()
    for copy in to_row + pass_row:
        copy.wait_recv()
        copy.wait_send()
    @pl.when(away)
    def _():
        for copy in to_side + block_side:
            copy.wait_send()

    natural, local = block_columns(plan, full.shape[1], side)

    def some(start, count):
        here = pl.ds(start, count)
        for a, b in zip(natural, local):
            result[here, a] = full[here, b]

    for_rows(full.shape[0], some)
    if gain_sum is not None:
        gain_sum.finish(outs[-1])
    for job in jobs:
        job.finish()


def sum_rows(plan, kernel, middle, terms, extras, outs, number, jobs=(), gain_sum=None):
    half, width = terms.shape[0] // 2, terms.shape[1]
    eighth = half // 4
    low = jnp.bfloat16
    vmem, hbm = pl.BlockSpec(memory_space=pltpu.VMEM), pl.BlockSpec(memory_space=pl.ANY)
    scratch = [
        pltpu.VMEM((2 * eighth, width), low),
        pltpu.VMEM((half, width), low),
        pltpu.VMEM((2 * eighth, width), low),
    ]
    if kernel is home_kernel:
        scratch.append(pltpu.VMEM((2 * eighth, width), low))
        scratch.append(pltpu.VMEM((2 * half, width), low))
    copies = (12 if kernel is spread_kernel else 16) + sum(job.count for job in jobs)
    local = max([2] + [job.count_local for job in jobs])
    if gain_sum is not None:
        copies += gain_sum.count
        outs = outs + [gain_sum.output]
    scratch += [pltpu.SemaphoreType.DMA((count,)) for count in (copies, copies, local)]
    if gain_sum is not None:
        scratch += gain_sum.scratch
    scratch += [stage for job in jobs for stage in job.scratch]
    sources = [source for job in jobs for source in job.sources]
    targets = [target for job in jobs for target in job.outputs]
    return pl.pallas_call(
        functools.partial(kernel, middle, jobs, len(extras), len(outs), gain_sum, plan),
        out_shape=[jax.ShapeDtypeStruct((2 * half, width), low)] + outs + targets,
        in_specs=[vmem] * (1 + len(extras) + len(sources)),
        out_specs=[vmem] * (1 + len(outs))
        + [hbm if job.in_hbm else vmem for job in jobs for _ in job.outputs],
        scratch_shapes=scratch,
        compiler_params=pltpu.CompilerParams(
            collective_id=number, has_side_effects=True, vmem_limit_bytes=56 * 2**20
        ),
        cost_estimate=pl.CostEstimate(flops=10**6, bytes_accessed=10**5, transcendentals=0),
        name=middle.__name__,
    )(terms, *extras, *sources)


def block_columns(plan, width, of_core=None):
    if not plan.ordered:
        return [pl.ds(0, width)], [pl.ds(0, width)]
    zone, _, _, core = place_here()
    core = core if of_core is None else of_core
    size, zones = width // plan.total, plan.zones
    owners = [
        flipped(zone, plan.flips[slot % zones]) * 2 + (core if slot < zones else 1 - core)
        for slot in range(plan.total)
    ]
    natural = [pl.ds(pl.multiple_of(owner * size, size), size) for owner in owners]
    return natural, [pl.ds(slot * size, size) for slot in range(plan.total)]


def copy_rows(source, target):
    def some(row, count):
        target[pl.ds(row, count), :] = source[pl.ds(row, count), :]

    if source.shape[0] % 32:
        target[...] = source[...]
    else:
        for_rows(source.shape[0], some)


def cast_rows(source, target):
    def some(row, count):
        here = pl.ds(row, count)
        target[here, :] = source[here, :].astype(target.dtype)

    for_rows(source.shape[0], some)


def opening_kernel(plan, wide_qkv, gains, wide_gate, wide_out, wide_down, tokens, angles, *refs):
    qkv_full, gains_full, turned_gate, turned_out, turned_down, turned_tokens, turned_angles = refs[:7]
    partner_gate, send_sems, recv_sems, tokens_stage, qkv, gate, out, down = refs[7:]
    cast_rows(wide_qkv, qkv)
    zone, side, row, core = place_here()
    partner = device(zone, core, row, side)
    row_peer, core_peer = device(zone, side, 1 - row, core), device(zone, side, row, 1 - core)
    zone_peers = [device(flipped(zone, flip), side, row, core) for flip in plan.flips[1:]]
    at_home, away = side == core, side != core
    always = [row_peer, core_peer] + zone_peers

    @pl.when(at_home)
    def _():
        greet(always)

    @pl.when(away)
    def _():
        greet(always + [partner])

    copies = Copies(send_sems, recv_sems)
    zones = plan.zones
    own = (gains, qkv, angles, gate, out, down)
    ends = (gains_full.at[0], qkv_full.at[0], turned_angles, turned_gate, turned_out, turned_down)
    units = wide_gate.shape[2]

    def cast_rest():
        for half in (0, 1):
            cast_rows(wide_gate.at[half], gate.at[:, pl.ds(half * units, units)])
        cast_rows(wide_out, out)
        cast_rows(wide_down, down)

    turn = [copies.make(source, target, partner) for source, target in zip(own, ends)]
    pieces = 2
    size = tokens.shape[0] // (2 * pieces)
    spots = [
        pl.ds(pl.multiple_of((row * pieces + piece) * size, size), size) for piece in range(pieces)
    ]
    turn_rows = [copies.make(tokens.at[s], tokens_stage.at[s], partner) for s in spots]
    pass_rows = [copies.make(tokens_stage.at[s], tokens_stage.at[s], row_peer) for s in spots]
    natural, local = block_columns(plan, tokens.shape[1])

    def lay_down(all_tokens):
        def some(start, count):
            here = pl.ds(start, count)
            for a, b in zip(natural, local):
                turned_tokens[here, b] = all_tokens[here, a]

        for_rows(all_tokens.shape[0], some)

    slots = list(range(1, zones))
    weights = ((gains, gains_full), (qkv, qkv_full))
    from_own = [
        [copies.make(source, full.at[slot], zone_peers[slot - 1]) for slot in slots]
        + [copies.make(source, full.at[zones], core_peer)]
        for source, full in weights
    ] + [[copies.make(gate, partner_gate, zone_peers[0])]]
    copies.number -= 2 * zones + 1
    from_turned = [
        [copies.make(full.at[0], full.at[slot], zone_peers[slot - 1]) for slot in slots]
        + [copies.make(full.at[0], full.at[zones], core_peer)]
        for _, full in weights
    ] + [[copies.make(turned_gate, partner_gate, zone_peers[0])]]
    cross = [
        [copies.make(full.at[slot], full.at[zones + slot], core_peer) for slot in slots]
        for _, full in weights
    ]

    def cross_over(k):
        for which in (0, 1):
            from_turned[which][k].wait_recv()
            cross[which][k].start()

    @pl.when(away)
    def _():
        for copy in turn[:3]:
            copy.start()
        cast_rest()
        for which in (0, 1):
            turn[which].wait_recv()
            for copy in from_turned[which]:
                copy.start()
        turn[3].start()
        turn_rows[0].start()
        turn[3].wait_recv()
        from_turned[2][0].start()
        turn_rows[1].start()
        cross_over(0)
        turn_rows[0].wait_recv()
        pass_rows[0].start()
        for copy in turn[4:]:
            copy.start()
        turn_rows[1].wait_recv()
        pass_rows[1].start()

    @pl.when(at_home)
    def _():
        for copy in from_own[0] + from_own[1]:
            copy.start()
        cast_rest()
        for copy in from_own[2]:
            copy.start()
        for source, target in zip(own, ends):
            copy_rows(source, target)
        lay_down(tokens)
        cross_over(0)

    for k in range(1, zones - 1):
        cross_over(k)
    for which in (0, 1):
        from_turned[which][zones - 1].wait_recv()
        for copy in from_turned[which]:
            copy.wait_send()
        for copy in cross[which]:
            copy.wait_recv()
            copy.wait_send()
    from_turned[2][0].wait_recv()
    from_turned[2][0].wait_send()

    @pl.when(away)
    def _():
        for copy in pass_rows + turn[2:3] + turn[4:]:
            copy.wait_recv()
        lay_down(tokens_stage)
        for copy in turn + turn_rows + pass_rows:
            copy.wait_send()


def opening(plan, qkv, gains, gate, out, down, tokens, angles, number):
    low = jnp.bfloat16
    vmem = pl.BlockSpec(memory_space=pltpu.VMEM)
    like = lambda v: jax.ShapeDtypeStruct(v.shape, v.dtype)
    whole = lambda v: jax.ShapeDtypeStruct((2 * plan.zones,) + v.shape, low)
    operands = (qkv, gains, gate, out, down, tokens, angles)
    low_gate = jax.ShapeDtypeStruct((gate.shape[1], 2 * gate.shape[2]), low)
    low_out = jax.ShapeDtypeStruct(out.shape, low)
    low_down = jax.ShapeDtypeStruct(down.shape, low)
    outputs = [whole(qkv), whole(gains), low_gate, low_out, low_down, like(tokens), like(angles)]
    outputs += [low_gate]
    copies = 6 + 4 + 2 * plan.zones + 1 + 2 * (plan.zones - 1)
    return pl.pallas_call(
        functools.partial(opening_kernel, plan),
        out_shape=outputs,
        in_specs=[vmem] * len(operands),
        out_specs=[vmem] * len(outputs),
        scratch_shapes=[
            pltpu.SemaphoreType.DMA((copies,)),
            pltpu.SemaphoreType.DMA((copies,)),
            pltpu.VMEM(tokens.shape, tokens.dtype),
            pltpu.VMEM(qkv.shape, low),
            pltpu.VMEM(low_gate.shape, low),
            pltpu.VMEM(out.shape, low),
            pltpu.VMEM(down.shape, low),
        ],
        compiler_params=pltpu.CompilerParams(
            collective_id=number, has_side_effects=True, vmem_limit_bytes=56 * 2**20
        ),
        cost_estimate=pl.CostEstimate(flops=10**6, bytes_accessed=10**5, transcendentals=0),
        name="opening",
    )(*operands)


def inverse_rms(values):
    return lax.rsqrt(jnp.mean(values * values, -1, keepdims=True) + EPS_NORM)


def hidden_rows(own, sums, extras, outs):
    tokens, gain = extras
    hidden = tokens[own, :].astype(jnp.float32) + sums
    outs[0][own, :] = hidden
    return (hidden * inverse_rms(hidden) * gain[...]).astype(jnp.bfloat16)


def grad_hidden_rows(own, sums, extras, outs):
    hidden, out_grad, gain = extras
    values = hidden[own, :]
    factor = inverse_rms(values)
    unit = values * factor
    outs[1][...] += jnp.sum(sums * unit, 0, keepdims=True)
    grad = out_grad[own, :].astype(jnp.float32) + norm_back(sums * gain[...], unit, factor)
    outs[0][own, :] = grad
    return grad.astype(jnp.bfloat16)


def grad_input_rows(own, sums, extras, outs):
    tokens, grad_hidden, gain = extras[:3]
    values = tokens[own, :].astype(jnp.float32)
    factor = inverse_rms(values)
    unit = values * factor
    outs[0][...] += jnp.sum(sums * unit, 0, keepdims=True)
    return (grad_hidden[own, :] + norm_back(sums * gain[...], unit, factor)).astype(jnp.bfloat16)


def dot(left, right, left_dim=1, right_dim=0):
    return lax.dot_general(
        left, right, (((left_dim,), (right_dim,)), ((), ())), preferred_element_type=jnp.float32
    )


def turn_head(values, cosine, signed_sine):
    return values * cosine + pltpu.roll(values, HEAD // 2, 1) * signed_sine


def turn_back(gradient, cosine, signed_sine):
    return gradient * cosine + pltpu.roll(gradient * signed_sine, HEAD // 2, 1)


def softmax_block(query, key, first_row):
    rows, keys = query.shape[0], key.shape[0]
    scores = dot(query, key, 1, 1)
    row_at = lax.broadcasted_iota(jnp.int32, (rows, keys), 0) + first_row
    key_at = lax.broadcasted_iota(jnp.int32, (rows, keys), 1)
    scores = jnp.where(key_at <= row_at, scores, -1000000000.0)
    exponent = jnp.exp(scores - jnp.max(scores, -1, keepdims=True))
    return exponent / jnp.sum(exponent, -1, keepdims=True)


def eighth_owners():
    _, side, row, _ = place_here()
    own, off = (row, side), (1 - row, 1 - side)
    first = lambda x, y: x * 2 + y
    second = lambda x, y: 4 + y * 2 + x
    return [
        first(own[0], own[1]),
        first(own[0], off[1]),
        second(own[0], own[1]),
        second(off[0], own[1]),
        first(off[0], own[1]),
        first(off[0], off[1]),
        second(own[0], off[1]),
        second(off[0], off[1]),
    ]


def reorder_rows(source, target, into_local):
    size = source.shape[0] // 8
    for slot, owner in enumerate(eighth_owners()):
        natural = pl.ds(pl.multiple_of(owner * size, size), size)
        local = pl.ds(slot * size, size)
        if into_local:
            target[local, :] = source[natural, :]
        else:
            target[natural, :] = source[local, :]


def forward_kernel(
    tokens, weights, gain_in, gain_q, gain_k, cosine, sine,
    normed, raw, query, key, value, local, attended,
):
    low = jnp.bfloat16
    total, heads = tokens.shape[0], query.shape[1] // HEAD
    block, wide = 256, 512

    def project(step, carry):
        rows = pl.ds(pl.multiple_of(step * wide, wide), wide)
        values = tokens[rows, :].astype(jnp.float32)
        normed[rows, :] = (values * inverse_rms(values) * gain_in[...]).astype(low)
        raw[rows, :] = dot(normed[rows, :], weights[...])
        turns = (cosine[rows, :], sine[rows, :])
        for head in range(heads):
            column = (head // 2) * 4 * HEAD + (head % 2) * HEAD
            values = raw[rows, pl.ds(column, HEAD)]
            values = turn_head(values * inverse_rms(values) * gain_q[...], *turns)
            query[rows, pl.ds(head * HEAD, HEAD)] = (values * (1.0 / math.sqrt(HEAD))).astype(low)
        for group in range(heads // 2):
            column = group * 4 * HEAD + 2 * HEAD
            here = pl.ds(group * HEAD, HEAD)
            values = raw[rows, pl.ds(column, HEAD)]
            values = turn_head(values * inverse_rms(values) * gain_k[...], *turns)
            key[rows, here] = values.astype(low)
            value[rows, here] = raw[rows, pl.ds(column + HEAD, HEAD)].astype(low)
        return carry

    lax.fori_loop(0, total // wide, project, 0)

    def attend(head, carry):
        mine = pl.ds(pl.multiple_of(head * HEAD, HEAD), HEAD)
        shared = pl.ds(pl.multiple_of(lax.div(head, 2) * HEAD, HEAD), HEAD)
        for start in range(0, total, SEQ):
            for first in range(0, SEQ, block):
                rows, keys = pl.ds(start + first, block), pl.ds(start, first + block)
                probs = softmax_block(query[rows, mine], key[keys, shared], first)
                attended[rows, mine] = dot(probs.astype(low), value[keys, shared]).astype(low)
        return carry

    lax.fori_loop(0, heads, attend, 0)
    reorder_rows(attended, local, True)


def attention(tokens, weights, gain_in, gain_q, gain_k, cosine, sine):
    total = tokens.shape[0]
    columns = weights.shape[1]
    low = jnp.bfloat16
    shape = lambda width, kind=low: jax.ShapeDtypeStruct((total, width), kind)
    vmem = pl.BlockSpec(memory_space=pltpu.VMEM)
    return pl.pallas_call(
        forward_kernel,
        out_shape=[
            shape(tokens.shape[1]),
            shape(columns, jnp.float32),
            shape(columns // 2),
            shape(columns // 4),
            shape(columns // 4),
            shape(columns // 2),
        ],
        in_specs=[vmem] * 7,
        out_specs=[vmem] * 6,
        scratch_shapes=[pltpu.VMEM((total, columns // 2), low)],
        compiler_params=pltpu.CompilerParams(vmem_limit_bytes=48 * 2**20),
        cost_estimate=pl.CostEstimate(flops=10**6, bytes_accessed=10**5, transcendentals=0),
        name="attention",
    )(tokens, weights, gain_in, gain_q, gain_k, cosine, sine)


def backward_kernel(
    query, key, value, raw, grad_rows, gain_q, gain_k, cosine, sine,
    mixed, mixed_local, query_gain, key_gain, grad, key_sum, value_sum,
):
    low = jnp.bfloat16
    total, heads = query.shape[0], query.shape[1] // HEAD
    block = 256
    reorder_rows(grad_rows, grad, False)
    query_gain[...] = jnp.zeros_like(query_gain)
    key_gain[...] = jnp.zeros_like(key_gain)

    def head_norm_back(rows, column, gradient, gain, gain_grad):
        values = raw[rows, column]
        factor = inverse_rms(values)
        unit = values * factor
        turned = turn_back(gradient, cosine[rows, :], sine[rows, :])
        gain_grad[...] += jnp.sum(turned * unit, 0, keepdims=True)
        mixed[rows, column] = norm_back(turned * gain[...], unit, factor).astype(low)

    def one_group(group, carry):
        at = lambda offset: pl.ds(pl.multiple_of(group * 4 * HEAD + offset * HEAD, HEAD), HEAD)
        shared = pl.ds(pl.multiple_of(group * HEAD, HEAD), HEAD)
        key_sum[...] = jnp.zeros_like(key_sum)
        value_sum[...] = jnp.zeros_like(value_sum)
        for head in (0, 1):
            mine = pl.ds(pl.multiple_of((group * 2 + head) * HEAD, HEAD), HEAD)
            for start in range(0, total, SEQ):
                for first in range(0, SEQ, block):
                    rows, keys = pl.ds(start + first, block), pl.ds(start, first + block)
                    query_part, grad_part = query[rows, mine], grad[rows, mine]
                    probs = softmax_block(query_part, key[keys, shared], first)
                    weighed = probs * dot(grad_part, value[keys, shared], 1, 1)
                    scores = weighed - probs * jnp.sum(weighed, -1, keepdims=True)
                    scores = scores.astype(low)
                    grad_query = dot(scores, key[keys, shared]) * (1.0 / math.sqrt(HEAD))
                    head_norm_back(rows, at(head), grad_query, gain_q, query_gain)
                    key_sum[keys, :] += dot(scores, query_part, 0, 0)
                    value_sum[keys, :] += dot(probs.astype(low), grad_part, 0, 0)
        for first in range(0, total, block):
            rows = pl.ds(first, block)
            head_norm_back(rows, at(2), key_sum[rows, :], gain_k, key_gain)
            mixed[rows, at(3)] = value_sum[rows, :].astype(low)
        return carry

    lax.fori_loop(0, heads // 2, one_group, 0)
    reorder_rows(mixed, mixed_local, True)


def attention_back(query, key, value, raw, grad_rows, gain_q, gain_k, cosine, sine):
    total, columns = raw.shape
    low = jnp.bfloat16
    vmem = pl.BlockSpec(memory_space=pltpu.VMEM)
    return pl.pallas_call(
        backward_kernel,
        out_shape=[
            jax.ShapeDtypeStruct((total, columns), low),
            jax.ShapeDtypeStruct((total, columns), low),
            jax.ShapeDtypeStruct((1, HEAD), jnp.float32),
            jax.ShapeDtypeStruct((1, HEAD), jnp.float32),
        ],
        in_specs=[vmem] * 9,
        out_specs=[vmem] * 4,
        scratch_shapes=[
            pltpu.VMEM(grad_rows.shape, low),
            pltpu.VMEM((total, HEAD), jnp.float32),
            pltpu.VMEM((total, HEAD), jnp.float32),
        ],
        compiler_params=pltpu.CompilerParams(vmem_limit_bytes=48 * 2**20),
        cost_estimate=pl.CostEstimate(flops=10**6, bytes_accessed=10**5, transcendentals=0),
        name="attention_back",
    )(query, key, value, raw, grad_rows, gain_q, gain_k, cosine, sine)


def feed_kernel(plan, rows, own_grad, got_grad, gate_up, up_part, down, active, grads, out_grad):
    low = jnp.bfloat16
    block = 512
    tile = down.shape[1]
    step = pl.program_id(0)
    gate_at = pl.ds(pl.multiple_of(step * tile, tile), tile)
    up_at = pl.ds(pl.multiple_of(grads.shape[1] // 2 + step * tile, tile), tile)
    _, side, _, core = place_here()

    def lay_down(source):
        natural, blocks = block_columns(plan, source.shape[1])
        eighth = source.shape[0] // 8
        for slot, owner in enumerate(eighth_owners()):

            def some(start, count, slot=slot, owner=owner):
                here = pl.ds(pl.multiple_of(owner * eighth + start, 32), count)
                there = pl.ds(slot * eighth + start, count)
                for a, b in zip(natural, blocks):
                    out_grad[there, b] = source[here, a]

            for_rows(eighth, some)

    @pl.when((step == 0) & (side == core))
    def _():
        lay_down(own_grad)

    @pl.when((step == 0) & (side != core))
    def _():
        lay_down(got_grad)

    def one(block_at, carry):
        here = pl.ds(pl.multiple_of(block_at * block, block), block)
        gate = dot(rows[here, :], gate_up[...])
        up = dot(rows[here, :], up_part[...])
        grad = dot(out_grad[here, :], down[...])
        sigmoid = jax.nn.sigmoid(gate)
        silu = gate * sigmoid
        active[here, :] = (silu * up).astype(low)
        grads[here, gate_at] = (grad * up * sigmoid * (1.0 + gate * (1.0 - sigmoid))).astype(low)
        grads[here, up_at] = (grad * silu).astype(low)
        return carry

    lax.fori_loop(0, rows.shape[0] // block, one, 0)


def feed_forward(plan, rows, own_grad, got_grad, gate_up, down, tile):
    total, width = rows.shape
    units = down.shape[1]
    low = jnp.bfloat16
    tiles = units // tile
    whole = pl.BlockSpec(memory_space=pltpu.VMEM)
    return pl.pallas_call(
        functools.partial(feed_kernel, plan),
        grid=(tiles,),
        out_shape=[
            jax.ShapeDtypeStruct((total, units), low),
            jax.ShapeDtypeStruct((total, 2 * units), low),
            jax.ShapeDtypeStruct((total, width), low),
        ],
        in_specs=[
            whole,
            whole,
            whole,
            pl.BlockSpec((width, tile), lambda step: (0, step)),
            pl.BlockSpec((width, tile), lambda step: (0, step + tiles)),
            pl.BlockSpec((width, tile), lambda step: (0, step)),
        ],
        out_specs=[
            pl.BlockSpec((total, tile), lambda step: (0, step)),
            whole,
            whole,
        ],
        compiler_params=pltpu.CompilerParams(vmem_limit_bytes=56 * 2**20),
        cost_estimate=pl.CostEstimate(
            flops=6 * total * width * units, bytes_accessed=4 * 10**7, transcendentals=total * units
        ),
        name="feed_forward",
    )(rows, own_grad, got_grad, gate_up, gate_up, down)


class Plan:
    def __init__(self, mesh):
        self.total = mesh.shape["dp"]
        self.zones = self.total // 2
        self.tensor = mesh.shape["tensor"]
        self.flips = [k ^ (k >> 1) for k in range(self.zones)]

    def place(self):
        self.index = lax.axis_index("dp")
        self.zone = self.index // 2
        self.side = self.index % 2
        self.row = lax.axis_index("tensor") // 2
        self.core = lax.axis_index("tensor") % 2
        self.home = self.side == self.core

    def move(self, value, target):
        pairs = []
        for d in range(self.total):
            for t in range(self.tensor):
                to = target(d // 2, d % 2, t // 2, t % 2)
                if to is not None:
                    zone, side, row, core = to
                    pairs.append((d * self.tensor + t, (zone * 2 + side) * self.tensor + row * 2 + core))
        return lax.ppermute(value, ("dp", "tensor"), pairs)

    def turn(self, value):
        got = self.move(value, lambda z, y, x, c: (z, c, x, y) if y != c else None)
        return jnp.where(self.home, value, got)

    def zone_flip(self, value, bit):
        return self.move(value, lambda z, y, x, c: (z ^ bit, y, x, c))

    def core_swap(self, value):
        return self.move(value, lambda z, y, x, c: (z, y, x, 1 - c))

    def side_swap(self, value):
        return self.move(value, lambda z, y, x, c: (z, 1 - y, x, c))

    def row_swap(self, value):
        return self.move(value, lambda z, y, x, c: (z, y, 1 - x, c))

    def to_local(self, value, axis):
        width = value.shape[axis] // self.total
        parts = []
        for core in (self.core, 1 - self.core):
            for slot in range(self.zones):
                owner = (self.zone ^ self.flips[slot]) * 2 + core
                parts.append(lax.dynamic_slice_in_dim(value, owner * width, width, axis))
        return jnp.concatenate(parts, axis)

    def to_natural(self, value, axis, core=None):
        core = self.core if core is None else core
        width = value.shape[axis] // self.total
        parts = []
        for block in range(self.total):
            slot = flip = (block // 2) ^ self.zone
            for bits in range(1, self.zones.bit_length()):
                slot = slot ^ (flip >> bits)
            slot = slot + jnp.where(block % 2 == core, 0, self.zones)
            parts.append(lax.dynamic_slice_in_dim(value, slot * width, width, axis))
        return jnp.concatenate(parts, axis)

    def row_owners(self):
        own, off = (self.row, self.side), (1 - self.row, 1 - self.side)
        first = lambda x, y: x * 2 + y
        second = lambda x, y: 4 + y * 2 + x
        return [
            first(own[0], own[1]),
            first(own[0], off[1]),
            second(own[0], own[1]),
            second(off[0], own[1]),
            first(off[0], own[1]),
            first(off[0], off[1]),
            second(own[0], off[1]),
            second(off[0], off[1]),
        ]

    def rows_local(self, value, slots=range(8)):
        size = value.shape[0] // 8
        owners = self.row_owners()
        return jnp.concatenate(
            [lax.dynamic_slice_in_dim(value, owners[slot] * size, size, 0) for slot in slots], 0
        )

    def rows_natural(self, value, order=range(8)):
        size = value.shape[0] // 8
        place = [list(order).index(slot) for slot in range(8)]
        parts = []
        for piece in range(8):
            x, y = (piece // 2, piece % 2) if piece < 4 else (piece % 2, (piece - 4) // 2)
            slots = (0, 1, 4, 5) if piece < 4 else (2, 6, 3, 7)
            same_x, same_y = x == self.row, y == self.side
            slot = jnp.where(
                same_x,
                jnp.where(same_y, place[slots[0]], place[slots[1]]),
                jnp.where(same_y, place[slots[2]], place[slots[3]]),
            )
            parts.append(lax.dynamic_slice_in_dim(value, slot * size, size, 0))
        return jnp.concatenate(parts, 0)

    def from_zones(self, shard):
        return [self.zone_flip(shard, flip) for flip in self.flips[1:]]

    def to_zones(self, parts, slots):
        return [self.zone_flip(parts[slot], self.flips[slot]) for slot in slots]

    def middle_swap(self, pair):
        return self.move(pair, lambda z, y, x, c: (z ^ 3, y, x, c) if z in (1, 2) else None)

    def inward(self, part):
        return self.move(part, lambda z, y, x, c: (z ^ 1, y, x, c) if z in (0, 3) else None)

    def pass_outward(self, pair):
        return self.move(pair, lambda z, y, x, c: (z ^ 1, y, x, c) if z in (1, 2) else None)

    def far_pair(self, middle, passed):
        inner = (self.zone == 1) | (self.zone == 2)
        return jnp.where(inner, middle, passed[::-1])

    def first_swap(self, send):
        half = send.shape[0] // 2
        return self.row_swap(send[:half]), self.side_swap(send[half:])

    def second_swap(self, keep, got):
        quarter = keep.shape[0] // 4
        row_part = keep[: 2 * quarter] + got[0].astype(jnp.float32)
        side_part = keep[2 * quarter :] + got[1].astype(jnp.float32)
        own = jnp.concatenate([row_part[:quarter], side_part[:quarter]], 0)
        return own, (
            self.side_swap(row_part[quarter:].astype(jnp.bfloat16)),
            self.row_swap(side_part[quarter:].astype(jnp.bfloat16)),
        )

    def spread_first(self, own):
        half = own.shape[0] // 2
        return (self.side_swap(own[:half]), self.row_swap(own[half:]))

    def spread_second(self, own, got):
        half = own.shape[0] // 2
        row_part = jnp.concatenate([own[:half], got[0]], 0)
        side_part = jnp.concatenate([own[half:], got[1]], 0)
        return row_part, side_part, self.row_swap(row_part), self.side_swap(side_part)

    def send_home(self, own):
        to_home = lambda z, y, x, c: (z, c, x, c) if y != c else None
        return jnp.concatenate([own, self.move(own, to_home)], 0)

    def row_home(self, part):
        return self.move(part, lambda z, y, x, c: (z, y, 1 - x, c) if y == c else None)

    def share_home(self, part, other):
        full = jnp.concatenate([part, other], 0)
        full = self.to_natural(self.rows_natural(full, (0, 2, 1, 6, 4, 3, 5, 7)), 1)
        got = self.move(full, lambda z, y, x, c: (z, y, x, 1 - c) if y == c else None)
        return full, got

    def turned(self, own, got):
        return jnp.where(self.home, own, got)

    def sum_everywhere(self, value):
        value = value + self.row_swap(value)
        value = value + self.side_swap(value)
        value = value + self.core_swap(value)
        bit = 1
        while bit < self.zones:
            value = value + self.zone_flip(value, bit)
            bit *= 2
        return value


def shards(
    plan,
    tokens,
    positions,
    out_grad,
    qkv_weight,
    qkv_first,
    qkv_second,
    out_weight,
    out_first,
    out_second,
    gate_up,
    gate_up_first,
    gate_up_second,
    down_weight,
    down_first,
    down_second,
    gains,
    gains_first,
    gains_second,
):
    plan.place()
    low = jnp.bfloat16
    tok_rows, model_width = tokens.shape
    groups = qkv_weight.shape[1]
    head_size = qkv_weight.shape[3]
    shard_rows = qkv_weight.shape[0]
    seq_count = tok_rows // SEQ
    mixed_cols = groups * 4 * head_size
    near_cols = model_width // 2
    kept = tok_rows // 2
    gain_count = gains.shape[0]

    tree = plan.zones == 4
    slots = range(1, plan.zones)

    def column_parts(value):
        return value.reshape((plan.zones, -1) + value.shape[1:])

    units = gate_up.shape[2]
    plan.ordered = (model_width // plan.total) % 128 == 0
    gain_rows = 16
    gain_block = jnp.pad(gains.astype(low), (0, gain_rows * 128 - gain_count)).reshape(gain_rows, 128)
    tile = min(units, 256)
    angle_at = positions.astype(jnp.float32).reshape(-1, 128)
    both_qkv, both_gains, turned_gate, turned_out, turned_down, tokens, angle_at, partner_gate = opening(
        plan,
        qkv_weight.reshape(shard_rows, mixed_cols),
        gain_block,
        gate_up,
        out_weight,
        down_weight,
        tokens,
        angle_at,
        3,
    )
    positions = angle_at.reshape(-1)
    turned_out, turned_gate, turned_down, tokens, positions, both_qkv, both_gains, out_grad = fence(
        turned_out, turned_gate, turned_down, tokens, positions, both_qkv, both_gains, out_grad
    )

    got_grad = plan.move(out_grad, lambda z, y, x, c: (z, c, x, y) if y != c else None)
    zone_out = plan.from_zones(turned_out)
    if tree:
        partner_down = plan.zone_flip(turned_down, 1)
    else:
        partner_down = plan.from_zones(turned_down)
        partner_gate = plan.from_zones(turned_gate)
    if not plan.ordered:
        tokens = plan.to_local(tokens, 1)
    cosine, sine_table = rotary(positions, head_size)
    signed_sine = jnp.concatenate(
        [-sine_table[:, : head_size // 2], sine_table[:, head_size // 2 :]], 1
    )
    full_qkv = both_qkv.reshape(model_width, mixed_cols)
    gain_slots = both_gains.reshape(plan.total, -1)[:, :gain_count]
    gain_all = plan.to_natural(gain_slots.reshape(-1), 0).astype(jnp.float32)
    gain_in = plan.to_local(gain_all[:model_width], 0)[None]
    gain_post = plan.to_local(gain_all[model_width : 2 * model_width], 0)[None]
    gain_q = gain_all[2 * model_width : 2 * model_width + head_size][None]
    gain_k = gain_all[2 * model_width + head_size :][None]
    normed, raw, query, key_rot, values_low, attended = attention(
        tokens, full_qkv, gain_in, gain_q, gain_k, cosine, signed_sine
    )
    attended, zone_out, turned_out, turned_down, turned_gate, partner_gate, partner_down = fence(
        attended, zone_out, turned_out, turned_down, turned_gate, partner_gate, partner_down
    )

    near_out = jnp.concatenate([turned_out] + zone_out, 0)
    far_out = plan.core_swap(near_out)
    own_tokens = plan.rows_local(tokens, (0, 2))
    near_out, far_out, own_tokens = fence(near_out, far_out, own_tokens)

    full_out = jnp.concatenate([near_out, far_out], 0)
    branch_terms = contract_cols(attended, full_out).astype(low)
    pairs = [(turned_gate, partner_gate), (turned_down, partner_down)]
    jobs = [PairTree(pairs)] if tree else []
    normed_rows, hidden, *gathered = sum_rows(
        plan,
        spread_kernel,
        hidden_rows,
        branch_terms,
        [own_tokens, gain_post],
        [jax.ShapeDtypeStruct((tok_rows // 4, model_width), jnp.float32)],
        0,
        jobs,
    )
    if not tree:
        near = [jnp.concatenate([own] + rest, 0) for own, rest in pairs]
        gathered = [jnp.concatenate([part, plan.core_swap(part)], 0) for part in near]
    full_gate = gathered[0].reshape(model_width, 2 * units)
    full_down = gathered[1].reshape(model_width, units)
    normed_rows, hidden, full_gate, full_down, got_grad = fence(
        normed_rows, hidden, full_gate, full_down, got_grad
    )

    def zone_parts(near, got):
        both = (near + got.astype(jnp.float32)).astype(low)
        return both.reshape((plan.zones, -1) + both.shape[1:])

    def zone_total(parts, *arrived):
        total = parts[0].astype(jnp.float32)
        for part in sum([list(group) for group in arrived], []):
            total = total + part.astype(jnp.float32)
        return total.astype(low)

    active, grad_both, out_grad = feed_forward(
        plan, normed_rows, out_grad, got_grad, full_gate, full_down, tile
    )
    if not plan.ordered:
        out_grad = plan.to_local(out_grad, 1)
    down_far = contract_rows(out_grad[:, near_cols:], active).astype(low)
    down_far, active, grad_both, out_grad, normed_rows = fence(
        down_far, active, grad_both, out_grad, normed_rows
    )

    down_got = plan.core_swap(down_far)
    gate_far = contract_rows(normed_rows[:, near_cols:], grad_both).astype(low)
    down_parts = zone_parts(contract_rows(out_grad[:, :near_cols], active), down_got)
    gate_far, down_parts, grad_both, normed_rows = fence(
        gate_far, down_parts, grad_both, normed_rows
    )

    gate_got = plan.core_swap(gate_far)
    if tree:
        down_sums = [plan.inward(down_parts[3])]
    else:
        down_sums = plan.to_zones(down_parts, slots)
    post_terms = contract_cols(grad_both, full_gate).astype(low)
    post_terms, gate_got, down_parts, down_sums, grad_both, normed_rows = fence(
        post_terms, gate_got, down_parts, down_sums, grad_both, normed_rows
    )

    if tree:
        down_sums += [plan.inward(down_parts[2])]
    gate_parts = zone_parts(contract_rows(normed_rows[:, :near_cols], grad_both), gate_got)
    post_terms, gate_parts, down_parts, down_sums = fence(
        post_terms, gate_parts, down_parts, down_sums
    )

    eighth = tok_rows // 8
    own_grad = jnp.concatenate([out_grad[:eighth], out_grad[2 * eighth : 3 * eighth]], 0)
    branch_rows, grad_hidden, post_gain_grad, gate_sums, mlp_terms = sum_rows(
        plan,
        spread_kernel,
        grad_hidden_rows,
        post_terms,
        [hidden, own_grad, gain_post],
        [
            jax.ShapeDtypeStruct((tok_rows // 4, model_width), jnp.float32),
            jax.ShapeDtypeStruct((1, model_width), jnp.float32),
        ],
        1,
        [
            PairScatter(gate_parts) if tree else ZoneBlocks(plan, gate_parts, slots),
            SideDot(active, full_down),
        ],
    )
    branch_rows, grad_hidden, post_gain_grad, gate_sums, mlp_terms, down_parts, down_sums = fence(
        branch_rows, grad_hidden, post_gain_grad, gate_sums, mlp_terms, down_parts, down_sums
    )

    mlp_got = plan.first_swap(mlp_terms[kept:])
    if tree:
        gate_last = [plan.zone_flip(gate_sums[1], 1)]
        gate_own = gate_sums
        down_pair = down_parts[2:].astype(jnp.float32) + jnp.stack(down_sums).astype(jnp.float32)
        down_sums = plan.middle_swap(down_pair.astype(low))
    else:
        gate_last, gate_own = gate_sums, gate_parts
    grad_att = jnp.dot(branch_rows, full_out, preferred_element_type=jnp.float32).astype(low)
    grad_mixed, mixed_rows, query_gain_grad, key_gain_grad = attention_back(
        query, key_rot, values_low, raw, grad_att, gain_q, gain_k, cosine, signed_sine
    )
    gain_terms = jnp.concatenate(
        [plan.to_natural(post_gain_grad, 1), query_gain_grad, key_gain_grad], 1
    )
    if tree:
        down_own = (down_parts[:2].astype(jnp.float32) + down_sums.astype(jnp.float32)).astype(low)
    grad_mixed, mixed_rows, gain_terms, normed, gate_last, branch_rows, mlp_got, down_sums = fence(
        grad_mixed, mixed_rows, gain_terms, normed, gate_last, branch_rows, mlp_got, down_sums
    )

    mlp_own, mlp_last = plan.second_swap(mlp_terms[:kept].astype(jnp.float32), mlp_got)
    if tree:
        total_down = zone_total(down_own, [plan.zone_flip(down_own[1], 1)])
    else:
        total_down = zone_total(down_parts, down_sums)
    total_gate = zone_total(gate_own, gate_last)
    total_gate = jnp.concatenate([total_gate[:, :units], total_gate[:, units:]], 0)
    out_far = contract_rows(branch_rows[:, near_cols:], attended).astype(low)
    out_got = plan.core_swap(out_far)
    normed_terms = contract_cols(mixed_rows, full_qkv).astype(low)
    out_parts = zone_parts(contract_rows(branch_rows[:, :near_cols], attended), out_got)
    block_own = (hidden + mlp_own + jnp.concatenate(mlp_last, 0).astype(jnp.float32)).astype(low)
    out_parts, normed_terms, total_gate, total_down, block_own, normed, grad_mixed = fence(
        out_parts, normed_terms, total_gate, total_down, block_own, normed, grad_mixed
    )

    gain_sum = GainSum(plan, gain_terms.shape[1], model_width) if plan.ordered else None
    mine, input_gain_grad, *rest = sum_rows(
        plan,
        home_kernel,
        grad_input_rows,
        normed_terms,
        [own_tokens, grad_hidden, gain_in, block_own] + ([gain_terms] if plan.ordered else []),
        [jax.ShapeDtypeStruct((1, model_width), jnp.float32)],
        2,
        [
            ZoneBlocks(plan, out_parts, slots),
            BlockGrad(plan, normed, grad_mixed),
            TurnLate(total_gate),
            TurnLate(total_down),
        ],
        gain_sum,
    )
    if plan.ordered:
        summed_gains, out_sent, total_qkv, got_gate, got_down = rest
    else:
        out_sent, total_qkv, got_gate, got_down = rest
        summed_gains = plan.sum_everywhere(
            jnp.concatenate([plan.to_natural(input_gain_grad, 1), gain_terms], 1)
        )
    mine, summed_gains, total_qkv, out_sent, got_gate, got_down = fence(
        mine, summed_gains, total_qkv, out_sent, got_gate, got_down
    )

    summed_gate = plan.turned(total_gate, got_gate).reshape(gate_up.shape)
    summed_down = plan.turned(total_down, got_down)
    other = plan.core_swap(mine)
    input_full, block_out = jnp.where(plan.home, mine, other), jnp.where(plan.home, other, mine)
    if not plan.ordered:
        input_full = plan.to_natural(input_full, 1, plan.side)
        block_out = plan.to_natural(block_out, 1, plan.side)
    summed_both = plan.turn(
        jnp.concatenate([total_qkv, zone_total(out_parts, out_sent)], 1)
    ).astype(jnp.float32)
    summed_qkv = summed_both[:, :mixed_cols].reshape(qkv_weight.shape)
    summed_out = summed_both[:, mixed_cols:]
    summed_gate = summed_gate.astype(jnp.float32)
    summed_down = summed_down.astype(jnp.float32)
    summed_gains = lax.dynamic_slice_in_dim(summed_gains[0], plan.index * gain_count, gain_count, 0)
    input_rows = input_full.astype(jnp.float32)

    qkv_moment, qkv_square, qkv_updated = adamw(
        qkv_weight, summed_qkv, qkv_first, qkv_second, RATE_QKV, DECAY_RATE
    )
    out_moment, out_square, out_updated = adamw(
        out_weight, summed_out, out_first, out_second, RATE_OUT, DECAY_RATE
    )
    gate_moment, gate_square, gate_updated = adamw(
        gate_up, summed_gate, gate_up_first, gate_up_second, RATE_GATE, DECAY_RATE
    )
    down_moment, down_square, down_updated = adamw(
        down_weight, summed_down, down_first, down_second, RATE_DOWN, DECAY_RATE
    )
    gain_moment, gain_square, gain_updated = adamw(
        gains, summed_gains, gains_first, gains_second, RATE_GAIN, 0.0
    )
    return (
        block_out,
        input_rows,
        qkv_moment,
        qkv_square,
        qkv_updated,
        out_moment,
        out_square,
        out_updated,
        gate_moment,
        gate_square,
        gate_updated,
        down_moment,
        down_square,
        down_updated,
        gain_moment,
        gain_square,
        gain_updated,
    )


def solution(mesh):
    plan = Plan(mesh)
    placed = (
        P("dp", None),
        P("dp"),
        P("dp", None),
        P("dp", "tensor", None, None),
        P("dp", "tensor", None, None),
        P("dp", "tensor", None, None),
        P("dp", "tensor"),
        P("dp", "tensor"),
        P("dp", "tensor"),
        P(None, "dp", "tensor"),
        P(None, "dp", "tensor"),
        P(None, "dp", "tensor"),
        P("dp", "tensor"),
        P("dp", "tensor"),
        P("dp", "tensor"),
        P("dp"),
        P("dp"),
        P("dp"),
    )
    return jax.shard_map(
        functools.partial(shards, plan),
        mesh=mesh,
        in_specs=placed,
        out_specs=(
            P("dp", None),
            P("dp", None),
            P("dp", "tensor", None, None),
            P("dp", "tensor", None, None),
            P("dp", "tensor", None, None),
            P("dp", "tensor"),
            P("dp", "tensor"),
            P("dp", "tensor"),
            P(None, "dp", "tensor"),
            P(None, "dp", "tensor"),
            P(None, "dp", "tensor"),
            P("dp", "tensor"),
            P("dp", "tensor"),
            P("dp", "tensor"),
            P("dp"),
            P("dp"),
            P("dp"),
        ),
        check_vma=False,
    )
```
